32 devices in a mesh: parts: 2 (over y), snp: 4 (over x, core), hap: 4 (over z).
Axes of the slice: x: 2, y: 2, z: 4, core: 2. Of those that a mesh axis runs over, the one named last changes fastest.
Arguments:
- haplotypes: int32 [8192, 3072], P('hap', ('parts', 'snp')), parts along dimension 1, may hold values from 0 to 1
- labels: int32 [16384], P(('parts', 'hap')), parts along dimension 0, may hold values from 0 to 1
- annotations: int32 [50, 3072], P(None, ('parts', 'snp')), parts along dimension 1, may hold values 0 or 1
- reach: int32 [8], P('parts'), parts along dimension 0, may hold values from 96 to 384, as said below
Outputs:
- ld_scores: float32 [50, 3072], P(None, ('parts', 'snp', 'hap')), parts along dimension 1
The draws below stay inside these ranges and needn't reach their ends.
There are 2 independent parts, one for each index of `parts`. The reference program is written for one: setup_inputs(seed, part) draws one part's arguments, and reference() takes and returns one part's arrays. A program takes and returns all parts, laid end to end along the dimension named above; each array names one. Nothing has to cross between parts.
Inputs may be any that keep to these rules, and one draw needn't show every extreme that they name: `reach`: the largest value is 384 in every window.
All inputs are finite; a program needn't handle non-finite values. No bound on the sum of `annotations` on one device may be relied on, other than what follows from the above.
Results may differ from the reference program's by a relative error of at most 0.0041.
Values may be sent and summed in bfloat16 or wider, within the bound.
No kernel may reach another device: no remote copies, remote signals or barrier semaphores. Data moves between devices by JAX's collectives and lax.ppermute only.
A program may use at most 64 MiB of HBM per device.

```python
import jax
import jax.numpy as jnp
from jax import lax

SB = 384
HAP_DEV = 2048
ANNOT = 50
NBLK = 4
M = 1536
NHAP = 8192


def population_labels(key):
    share_key, roll_key = jax.random.split(key)
    group_count = NHAP // HAP_DEV
    shares = jax.random.randint(share_key, (group_count, 1), 550, 950)
    rolled = jax.random.randint(roll_key, (group_count, HAP_DEV), 0, 1000)
    return (rolled >= shares).astype(jnp.int32).reshape(NHAP)


def draw_labels(key, part):
    return population_labels(key)


def draw_haplotypes(key, part):
    labels = population_labels(key)
    key = jax.random.fold_in(key, 7)
    subkeys = jax.random.split(key, 6)
    group_count = NHAP // HAP_DEV
    permille = jax.random.randint(subkeys[0], (1, M), 5, 500)
    founders = (jax.random.randint(subkeys[1], (60, M), 0, 1000) < permille).astype(jnp.int32)
    powers = jax.random.randint(subkeys[2], (NHAP, 1), 0, 4)
    lengths = SB // 2 * jnp.left_shift(jnp.ones_like(powers), powers)
    phases = jax.random.randint(subkeys[3], (NHAP, 1), 0, 4 * SB) % lengths
    segment = (jnp.arange(M, dtype=jnp.int32)[None, :] + phases) // lengths
    founder_table = jax.random.randint(subkeys[4], (NHAP, 2 * NBLK + 2), 0, 24)
    group_of = jnp.arange(NHAP, dtype=jnp.int32) // HAP_DEV
    drift = group_of * 24 // group_count
    picked = jnp.take_along_axis(founder_table, segment, axis=1) + 12 * labels[:, None] + drift[:, None]
    alleles = jnp.take_along_axis(founders, picked, axis=0)
    mutations = (jax.random.randint(subkeys[5], (NHAP, M), 0, 1000) < 6).astype(jnp.int32)
    return jnp.abs(alleles - mutations).astype(jnp.int32)


def draw_reach(key, part):
    key = jax.random.fold_in(key, 13)
    value_key, widest_key = jax.random.split(key)
    values = jax.random.randint(value_key, (NBLK,), SB // 4, SB + 1)
    widest = jax.random.randint(widest_key, (), 0, NBLK)
    return jnp.where(jnp.arange(NBLK) == widest, SB, values).astype(jnp.int32)


def with_ends(entries, own_key, smallest, largest):
    longest = entries.shape.index(max(entries.shape))
    spots = []
    for shift in (0, 1):
        where = [jax.random.randint(jax.random.fold_in(own_key, axis), (), 0, length) for axis, length in enumerate(entries.shape)]
        where[longest] = (where[longest] + shift) % entries.shape[longest]
        spots.append(tuple(where))
    return entries.at[spots[0]].set(smallest).at[spots[1]].set(largest)


def setup_inputs(seed: int = 0, part: int = 0) -> dict:
    streams_of = jax.random.split(jax.random.key(seed), 5)
    part_keys = jax.random.split(jax.random.fold_in(streams_of[4], part), 5)
    return {
        "haplotypes": draw_haplotypes(jax.random.fold_in(jax.random.fold_in(streams_of[4], part), 71), part),
        "labels": draw_labels(jax.random.fold_in(jax.random.fold_in(streams_of[4], part), 71), part),
        "annotations": with_ends((jax.random.randint(part_keys[2], (ANNOT, M), 0, 3) < 1).astype(jnp.int32), jax.random.fold_in(part_keys[2], 1), 0, 1),
        "reach": draw_reach(jax.random.fold_in(jax.random.fold_in(streams_of[4], part), 71), part),
    }


PRECISE = lax.Precision.HIGHEST
VARIANCE_FLOOR = 0.01

def standardize(alleles, second, totals, counts):
    pop_sizes = jnp.maximum(counts, 1.0)
    frequency = totals / pop_sizes[:, None]
    variance = jnp.maximum(frequency * (1.0 - frequency), VARIANCE_FLOOR)
    inverse = 1.0 / jnp.sqrt(pop_sizes[:, None] * variance)
    centred_first = (alleles - frequency[0]) * inverse[0]
    centred_second = (alleles - frequency[1]) * inverse[1]
    return jnp.where(second[:, None] > 0.5, centred_second, centred_first).astype(jnp.bfloat16)

def reference(haplotypes, labels, annotations, reach):
    alleles = haplotypes.astype(jnp.float32)
    second = labels.astype(jnp.float32)
    weights = jnp.stack([1.0 - second, second])
    totals = jnp.dot(weights, alleles, precision=PRECISE)
    counts = lax.optimization_barrier(jnp.sum(weights, axis=1))
    scaled = standardize(alleles, second, totals, counts)
    zero_block = jnp.zeros_like(scaled)
    first_pop = jnp.where(second[:, None] > 0.5, zero_block, scaled)
    second_pop = jnp.where(second[:, None] > 0.5, scaled, zero_block)
    padded = jnp.pad(scaled, ((0, 0), (SB, SB)))
    annot_padded = jnp.pad(annotations.astype(jnp.float32), ((0, 0), (SB, SB)))

    def one_block(number):
        start = number * SB
        nearby = lax.dynamic_slice_in_dim(padded, start, 3 * SB, 1).astype(jnp.float32)
        left_first = lax.dynamic_slice_in_dim(first_pop, start, SB, 1).astype(jnp.float32)
        left_second = lax.dynamic_slice_in_dim(second_pop, start, SB, 1).astype(jnp.float32)
        corr_first = jnp.dot(left_first.T, nearby, precision=PRECISE)
        corr_second = jnp.dot(left_second.T, nearby, precision=PRECISE)
        product = corr_first * corr_second
        row_index = jnp.arange(SB, dtype=jnp.int32)
        col_index = jnp.arange(3 * SB, dtype=jnp.int32) - SB
        limit = reach[number]
        inside = jnp.abs(row_index[:, None] - col_index[None, :]) <= limit
        kept_terms = jnp.where(inside, product, jnp.float32(0.0))
        nearby_annot = lax.dynamic_slice_in_dim(annot_padded, start, 3 * SB, 1)
        return jnp.dot(nearby_annot, kept_terms.T, precision=PRECISE)
    blocks = lax.map(one_block, jnp.arange(NBLK, dtype=jnp.int32))
    return jnp.transpose(blocks, (1, 0, 2)).reshape(ANNOT, M)
```

```python
import jax
import jax.numpy as jnp
from jax import lax
from jax.sharding import PartitionSpec as P

PRECISE = lax.Precision.HIGHEST
VARIANCE_FLOOR = 0.01
BASE_BITS = 12
BASE = 1 << BASE_BITS
FIELD_BITS = 16


def shifted(value, axis, steps):
    count = lax.axis_size(axis)
    leading, last = (max(0, -steps), min(count, count - steps))
    return lax.ppermute(value, axis, [(source, source + steps) for source in range(leading, last)])


def to_fields(values):
    whole = values.astype(jnp.int32)
    return whole + (whole >> BASE_BITS) * ((1 << FIELD_BITS) - BASE)


def from_fields(packed):
    first = packed & ((1 << FIELD_BITS) - 1)
    second = lax.shift_right_logical(packed, FIELD_BITS)
    return first.astype(jnp.float32), second.astype(jnp.float32)


def column_stats(totals, count):
    size = jnp.maximum(count, 1.0)
    frequency = totals / size
    variance = jnp.maximum(frequency * (1.0 - frequency), VARIANCE_FLOOR)
    inverse = 1.0 / jnp.sqrt(size * variance)
    low = ((0.0 - frequency) * inverse).astype(jnp.bfloat16).astype(jnp.float32)
    high = ((1.0 - frequency) * inverse).astype(jnp.bfloat16).astype(jnp.float32)
    step = high - low
    root = lax.rsqrt(size)
    carried = step * totals * root
    whole = (low * count + step * totals) * root
    return step, carried, whole


def count_dot(left, right):
    return lax.dot_general(
        left, right, (((0,), (0,)), ((), ())), preferred_element_type=jnp.float32
    )


def lookup(table, position):
    places = jnp.arange(table.shape[0], dtype=jnp.int32)
    return jnp.sum(jnp.where(places == position, table, 0))


def per_device(haplotypes, labels, annotations, reach):
    rows, snps = haplotypes.shape
    half = snps // 2
    groups = lax.axis_size("hap")
    blocks = lax.axis_size("snp")
    share = snps // groups
    hap_index = lax.axis_index("hap")
    snp_index = lax.axis_index("snp")

    alleles = haplotypes.astype(jnp.bfloat16)
    weight = jnp.where(labels > 0, BASE, 1).astype(jnp.bfloat16)
    weighted = alleles * weight[:, None]
    annots = annotations.astype(jnp.bfloat16)
    payload = jnp.concatenate([alleles, annots], axis=0)
    upper = shifted(payload[:, :half], "snp", -1)
    lower = shifted(payload[:, half:], "snp", 1)

    row = jnp.arange(snps, dtype=jnp.int32)[:, None]
    col = jnp.arange(snps, dtype=jnp.int32)[None, :]
    own_tile = count_dot(weighted, alleles)
    upper_tile = count_dot(weighted, upper[:rows])
    lower_tile = count_dot(lower[:rows], weighted[:, half:])
    weight_row = weight[None, :]
    nearby = jnp.concatenate([upper[:rows], lower[:rows]], axis=1)
    own_totals = jnp.dot(weight_row, alleles, preferred_element_type=jnp.float32)
    near_totals = jnp.dot(weight_row, nearby, preferred_element_type=jnp.float32)
    other = jnp.concatenate(
        [upper_tile, jnp.concatenate([jnp.zeros_like(lower_tile), lower_tile], axis=0)], axis=1
    )
    square = jnp.where(col >= row, own_tile, other)
    far = jnp.sum(jnp.where(col == row, other, 0.0), axis=0, keepdims=True)
    sizes = jnp.broadcast_to(jnp.sum(weight.astype(jnp.float32)), (1, snps))
    extras = jnp.concatenate([own_totals, near_totals, far, sizes, jnp.zeros((4, snps))], axis=0)
    square, extras = to_fields(square), to_fields(extras)

    def for_group(group):
        part = lax.dynamic_slice_in_dim(square, group * share, share, 0)
        return jnp.concatenate([part, extras], axis=0)

    summed = for_group(hap_index)
    received = []
    for step in range(1, groups):
        received.append(
            lax.ppermute(
                for_group((hap_index + step) % groups),
                "hap",
                [(source, (source + step) % groups) for source in range(groups)],
            )
        )
    for piece in received:
        summed = summed + piece

    counts = from_fields(summed[:share])
    extra = from_fields(summed[share:])
    col = jnp.arange(snps, dtype=jnp.int32)[None, :]
    row = hap_index * share + jnp.arange(share, dtype=jnp.int32)[:, None]
    in_own = col >= row
    in_upper = (col < row) & (col < half)
    in_lower = (col < row) & (col >= half)
    distance = jnp.where(in_own, col - row, snps + col - row)

    product = 1.0
    far_product = 1.0
    for pop in range(2):
        count = extra[pop][3, 0]
        own = column_stats(extra[pop][0], count)
        near = column_stats(extra[pop][1], count)
        own_rows = [lax.dynamic_slice_in_dim(v, hap_index * share, share, 0) for v in own]
        near_rows = [lax.dynamic_slice_in_dim(v, hap_index * share, share, 0) for v in near]
        at_row = [jnp.where(in_lower, n[:, None], o[:, None]) for o, n in zip(own_rows, near_rows)]
        at_col = [jnp.where(in_upper, n[None, :], o[None, :]) for o, n in zip(own, near)]
        corr = (
            at_row[0] * at_col[0] * counts[pop]
            - at_row[1] * at_col[1]
            + at_row[2] * at_col[2]
        )
        product = product * corr
        far_count = lax.dynamic_slice_in_dim(extra[pop][2], hap_index * share, share, 0)
        far_product = far_product * (
            own_rows[0] * near_rows[0] * far_count
            - own_rows[1] * near_rows[1]
            + own_rows[2] * near_rows[2]
        )

    reach_here = lookup(reach, snp_index)
    reach_up = lookup(reach, snp_index + 1)
    reach_down = lookup(reach, snp_index - 1)
    near_annots = jnp.concatenate([upper[rows:], lower[rows:]], axis=1).astype(jnp.float32)
    annots = annots.astype(jnp.float32)
    annots_rows = lax.dynamic_slice_in_dim(annots, hap_index * share, share, 1)
    near_rows = lax.dynamic_slice_in_dim(near_annots, hap_index * share, share, 1)
    is_upper = hap_index < groups // 2

    def kept(where, limit):
        return jnp.where(where & (distance <= limit), product, 0.0)

    def dot(left, right):
        return jnp.dot(left, right, precision=PRECISE)

    direct_own = dot(annots, kept(in_own, reach_here).T) + dot(
        near_annots[:, :half], kept(in_upper, reach_here)[:, :half].T
    )
    direct_down = dot(annots[:, half:], kept(in_lower, reach_down)[:, half:].T)
    mirrored_own = dot(annots_rows, kept(in_own & (col > row), reach_here)) + dot(
        near_rows, kept(in_lower, reach_here)
    )
    mirrored_up = dot(annots_rows, kept(in_upper, reach_up)[:, :half])
    mirrored_up = jnp.concatenate([mirrored_up, jnp.zeros_like(mirrored_up)], axis=1)
    far_own = near_rows * jnp.where(snps <= reach_here, far_product, 0.0)[None, :]
    reach_far = jnp.where(is_upper, reach_up, reach_down)
    far_near = annots_rows * jnp.where(snps <= reach_far, far_product, 0.0)[None, :]

    mirrored = jnp.stack([mirrored_own, mirrored_up])

    def scores_for(group):
        return lax.dynamic_slice_in_dim(mirrored, group * share, share, 2)

    scores = scores_for(hap_index)
    received = []
    for step in range(1, groups):
        received.append(
            lax.ppermute(
                scores_for((hap_index + step) % groups),
                "hap",
                [(source, (source + step) % groups) for source in range(groups)],
            )
        )
    for piece in received:
        scores = scores + piece
    own_scores = scores[0] + direct_own + far_own
    near_scores = scores[1] + direct_down + far_near
    pairs = []
    for block in range(blocks):
        for group in range(groups):
            target = block + 1 if group < groups // 2 else block - 1
            if 0 <= target < blocks:
                pairs.append((block * groups + group, target * groups + group))
    return own_scores + lax.ppermute(near_scores, ("snp", "hap"), pairs)


def solution(mesh):
    in_specs = (
        P("hap", ("parts", "snp")),
        P(("parts", "hap")),
        P(None, ("parts", "snp")),
        P("parts"),
    )
    out_specs = P(None, ("parts", "snp", "hap"))
    return jax.shard_map(
        per_device, mesh=mesh, in_specs=in_specs, out_specs=out_specs, check_vma=False
    )
```

```python
import functools

import jax
import jax.numpy as jnp
from jax import lax
from jax.experimental import pallas as pl
from jax.experimental.pallas import tpu as pltpu
from jax.sharding import PartitionSpec as P

VARIANCE_FLOOR = 0.01
BASE_BITS = 12
BASE = 1 << BASE_BITS
FIELD_BITS = 16
LANES = 128
HALF_LANES = LANES // 2
CHUNKS = 4
VMEM = pl.BlockSpec(memory_space=pltpu.VMEM)
SMEM = pl.BlockSpec(memory_space=pltpu.SMEM)
ANY = pl.BlockSpec(memory_space=pl.ANY)
VMEM_LIMIT = 24 * 1024 * 1024


def iota(shape, axis):
    return lax.broadcasted_iota(jnp.int32, shape, axis)


def round_up(value, step):
    return -(-value // step) * step


def to_fields(values):
    whole = values.astype(jnp.int32)
    return whole + (whole >> BASE_BITS) * ((1 << FIELD_BITS) - BASE)


def from_fields(packed):
    first = packed & ((1 << FIELD_BITS) - 1)
    second = lax.shift_right_logical(packed, FIELD_BITS)
    return first.astype(jnp.float32), second.astype(jnp.float32)


def call(kernel, out_shape, in_specs, scratch_shapes=(), flops=0, moved=0):
    several = isinstance(out_shape, (list, tuple))
    return pl.pallas_call(
        kernel,
        out_shape=out_shape,
        in_specs=in_specs,
        out_specs=[VMEM] * len(out_shape) if several else VMEM,
        scratch_shapes=list(scratch_shapes),
        compiler_params=pltpu.CompilerParams(vmem_limit_bytes=VMEM_LIMIT),
        cost_estimate=pl.CostEstimate(flops=flops, bytes_accessed=moved, transcendentals=0),
    )


def store_packed(up_ref, down_ref, where, first, second):
    left = iota((first.shape[0], LANES), 1) < HALF_LANES
    middle = first[:, LANES : 2 * LANES]
    turned = pltpu.roll(second[:, LANES : 2 * LANES], HALF_LANES, 1)
    for ref, side, mixed in (
        (up_ref, slice(0, LANES), jnp.where(left, middle, turned)),
        (down_ref, slice(2 * LANES, 3 * LANES), jnp.where(left, turned, middle)),
    ):
        ref[where, 0:LANES] = first[:, side].astype(jnp.bfloat16)
        ref[where, LANES : 2 * LANES] = second[:, side].astype(jnp.bfloat16)
        ref[where, 2 * LANES : 3 * LANES] = mixed.astype(jnp.bfloat16)


def load_packed(up, down):
    left = iota((up.shape[0], LANES), 1) < HALF_LANES
    up_mixed, down_mixed = up[:, 2 * LANES :], down[:, 2 * LANES :]
    first = jnp.where(left, up_mixed, down_mixed)
    second = jnp.where(left, down_mixed, up_mixed).astype(jnp.float32)
    second = pltpu.roll(second, HALF_LANES, 1).astype(jnp.bfloat16)
    return (
        (up[:, :LANES], first, down[:, :LANES]),
        (up[:, LANES : 2 * LANES], second, down[:, LANES : 2 * LANES]),
    )


def prepare_kernel(hap_ref, annot_ref, alleles_ref, up_ref, down_ref, held, sems):
    rows = hap_ref.shape[0]
    size = rows // (2 * CHUNKS)
    starts = [side * (rows // 2) + chunk * size for chunk in range(CHUNKS) for side in range(2)]
    copies = [
        pltpu.make_async_copy(
            hap_ref.at[pl.ds(start, size)], held.at[pl.ds(start, size)], sems.at[number]
        )
        for number, start in enumerate(starts)
    ]
    for copy in copies:
        copy.start()
    annots = annot_ref[...].astype(jnp.float32)
    part = (up_ref.shape[0] - rows // 2)
    annots = jnp.concatenate(
        [annots, jnp.zeros((2 * part - annots.shape[0], annots.shape[1]), jnp.float32)], axis=0
    )
    store_packed(up_ref, down_ref, slice(rows // 2, rows // 2 + part), annots[:part], annots[part:])
    for chunk in range(CHUNKS):
        pair = []
        for side in range(2):
            number = 2 * chunk + side
            copies[number].wait()
            where = slice(starts[number], starts[number] + size)
            values = held[where, :].astype(jnp.float32)
            alleles_ref[where, :] = values.astype(jnp.bfloat16)
            pair.append(values)
        store_packed(up_ref, down_ref, slice(chunk * size, (chunk + 1) * size), *pair)


def send_shares(groups, source, share, targets):
    me = lax.axis_index("hap")
    for step, target in enumerate(targets):
        group = lax.rem(me + step, groups)
        target[0:share, :] = source[pl.ds(pl.multiple_of(group * share, 8), share), :]


def own_kernel(groups, share, alleles_ref, label_ref, *refs):
    weighted_ref, totals_ref, *targets = refs[: 2 + groups]
    tile, folded = refs[2 + groups :]
    rows, snps = alleles_ref.shape
    half = snps // 2
    weight = jnp.where(label_ref[...] > 0, float(BASE), 1.0)
    weighted_ref[0:snps, :] = alleles_ref[...].T * weight.astype(jnp.bfloat16)
    extra = weighted_ref.shape[0] - snps
    weighted_ref[snps:, :] = jnp.broadcast_to(weight, (extra, rows)).astype(jnp.bfloat16)
    tile[...] = jnp.dot(weighted_ref[...], alleles_ref[...], preferred_element_type=jnp.float32)
    count = jnp.sum(weight, axis=1, keepdims=True)
    totals_ref[...] = jnp.concatenate(
        [tile[snps : snps + 1, :], jnp.broadcast_to(count, (1, snps)), jnp.zeros((6, snps))], axis=0
    )
    row, col = iota((half, snps), 0), iota((half, snps), 1)
    moved = (col < half) | (col - half > row)
    turned = pltpu.roll(tile[0:half, :], half, 1)
    folded[0:half, :] = to_fields(jnp.where(moved, turned, tile[half:snps, :]))
    if folded.shape[0] > half:
        folded[half:, :] = jnp.zeros((folded.shape[0] - half, snps), jnp.int32)
    send_shares(groups, folded, share, targets)


def near_kernel(groups, share, weighted_ref, up_ref, down_ref, totals_ref, *refs):
    targets, (near, tile, folded) = refs[:groups], refs[groups:]
    rows, snps = near.shape
    half = snps // 2
    pieces = load_packed(up_ref[0 : rows // 2, :], down_ref[0 : rows // 2, :])
    for side in range(2):
        for number in range(3):
            near[side * (rows // 2) : (side + 1) * (rows // 2), number * LANES : (number + 1) * LANES] = pieces[side][number]
    tile[...] = jnp.dot(weighted_ref[...], near[...], preferred_element_type=jnp.float32)
    row, col = iota((half, snps), 0), iota((half, snps), 1)
    moved = (col >= half) & (col - half < row)
    turned = pltpu.roll(tile[0:half, :], half, 1)
    folded[0:half, :] = to_fields(jnp.where(moved, turned, tile[half:snps, :]))
    if folded.shape[0] > half:
        folded[half:, :] = jnp.zeros((folded.shape[0] - half, snps), jnp.int32)
    square = (snps, snps)
    far = jnp.sum(
        jnp.where(iota(square, 0) == iota(square, 1), tile[0:snps, :], 0.0), axis=0, keepdims=True
    )
    extras = to_fields(
        jnp.concatenate(
            [totals_ref[0:2, :], tile[snps : snps + 1, :], far, jnp.zeros((4, snps))], axis=0
        )
    )
    send_shares(groups, folded, share, targets)
    for target in targets:
        target[share:, :] = extras


def annots_kernel(annot_ref, up_ref, down_ref, own_ref, near_ref):
    snps = annot_ref.shape[1]
    part = up_ref.shape[0]
    wide = 2 * part
    own = annot_ref[...].astype(jnp.float32)
    own = jnp.concatenate([own, jnp.zeros((LANES - own.shape[0], snps), jnp.float32)], axis=0)
    own_ref[...] = own.T
    first, second = load_packed(up_ref[...], down_ref[...])
    near = jnp.concatenate(
        [
            jnp.concatenate([piece.astype(jnp.float32) for piece in first], axis=1),
            jnp.concatenate([piece.astype(jnp.float32) for piece in second], axis=1),
            jnp.zeros((LANES - wide, snps), jnp.float32),
        ],
        axis=0,
    )
    near_ref[...] = near.T


def column_stats(totals, count):
    size = jnp.maximum(count, 1.0)
    frequency = totals / size
    variance = jnp.maximum(frequency * (1.0 - frequency), VARIANCE_FLOOR)
    inverse = 1.0 / jnp.sqrt(size * variance)
    low = ((0.0 - frequency) * inverse).astype(jnp.bfloat16).astype(jnp.float32)
    high = ((1.0 - frequency) * inverse).astype(jnp.bfloat16).astype(jnp.float32)
    step = high - low
    root = 1.0 / jnp.sqrt(size)
    return step, step * totals * root, (low * count + step * totals) * root


def correlation(row, col, count):
    return row[0] * col[0] * count - row[1] * col[1] + row[2] * col[2]


def split(values):
    high = values.astype(jnp.bfloat16)
    return high, (values - high.astype(jnp.float32)).astype(jnp.bfloat16)


def dot_split(values, right, axis):
    dims = (((axis,), (0,)), ((), ()))
    return sum(
        lax.dot_general(part, right, dims, preferred_element_type=jnp.float32)
        for part in split(values)
    )


def score_kernel(groups, share, reach_ref, *refs):
    own_parts, near_parts = refs[:groups], refs[groups : 2 * groups]
    annot_ref, near_annot_ref = refs[2 * groups : 2 * groups + 2]
    targets = refs[2 * groups + 2 : 3 * groups + 2]
    table, annots, near_annots, scores = refs[3 * groups + 2 :]
    snps = annot_ref.shape[0]
    half = snps // 2
    out_share = snps // groups
    me = lax.axis_index("hap")
    block = lax.axis_index("snp")
    last = reach_ref.shape[0] - 1
    reach_here = reach_ref[block]
    reach_up = reach_ref[jnp.minimum(block + 1, last)]
    reach_down = reach_ref[jnp.maximum(block - 1, 0)]

    own_counts = sum((part[...] for part in own_parts[1:]), own_parts[0][...])
    near_sums = sum((part[...] for part in near_parts[1:]), near_parts[0][...])
    extras = from_fields(near_sums[share:, :])
    near_counts = near_sums[0:share, :]

    own_stats, near_stats, lines = [], [], []
    for pop in range(2):
        count = extras[pop][1:2, :]
        own_stats.append(column_stats(extras[pop][0:1, :], count))
        near_stats.append(column_stats(extras[pop][2:3, :], count))
        lines += [*own_stats[pop], *near_stats[pop], extras[pop][0:1, :], extras[pop][3:4, :]]
    by_row = jnp.concatenate(lines, axis=0).T
    table[0:snps, 0:16] = by_row
    if table.shape[0] > snps:
        table[snps:, 0:16] = jnp.zeros((table.shape[0] - snps, 16), jnp.float32)
    annots[0:snps, :] = annot_ref[...]
    near_annots[0:snps, :] = near_annot_ref[...]
    if annots.shape[0] > snps:
        annots[snps:, :] = jnp.zeros((annots.shape[0] - snps, LANES), jnp.float32)

    low_rows = pl.multiple_of(me * share, 8)
    high_rows = pl.multiple_of(half + me * share, 8)

    def both(ref):
        return jnp.concatenate([ref[pl.ds(low_rows, share), :], ref[pl.ds(high_rows, share), :]], axis=0)

    here = both(table)
    own_count = jnp.concatenate([pltpu.roll(own_counts, half, 1), own_counts], axis=0)
    near_count = jnp.concatenate([pltpu.roll(near_counts, half, 1), near_counts], axis=0)
    shape = (2 * share, snps)
    local, col = iota(shape, 0), iota(shape, 1)
    low = local < share
    place = jnp.where(low, local, local - share) + me * share
    row = jnp.where(low, place, place + half)
    own_fields, near_fields = from_fields(own_count), from_fields(near_count)
    own_product, near_product = 1.0, 1.0
    for pop in range(2):
        row_stats = [here[:, 8 * pop + k : 8 * pop + k + 1] for k in range(3)]
        own_product *= correlation(row_stats, own_stats[pop], own_fields[pop])
        near_product *= correlation(row_stats, near_stats[pop], near_fields[pop])
    real = place < half
    own_inside = real & ((low & (col > row)) | (~low & (col >= half) & (col < row)))
    own_inside &= jnp.abs(col - row) <= reach_here
    own_kept = jnp.where(own_inside, own_product, 0.0)
    in_upper = col < half
    near_inside = real & ((low & (col < row)) | (~low & (in_upper | (col > row))))
    distance = jnp.where(in_upper, snps + col - row, snps + row - col)
    near_here = jnp.where(near_inside & (distance <= reach_here), near_product, 0.0)
    reach_there = jnp.where(in_upper, reach_up, reach_down)
    near_there = jnp.where(near_inside & (distance <= reach_there), near_product, 0.0)

    rows_here = both(annots)
    rows_there = pltpu.roll(rows_here, HALF_LANES, 1)
    scores[0:snps, :] = dot_split(
        jnp.concatenate([own_kept, near_there], axis=0),
        jnp.concatenate([rows_here, rows_there], axis=0).astype(jnp.bfloat16),
        0,
    )
    direct = dot_split(
        jnp.concatenate([own_kept, near_here], axis=1),
        jnp.concatenate([annot_ref[...], near_annot_ref[...]], axis=0).astype(jnp.bfloat16),
        1,
    )
    scores[pl.ds(low_rows, share), :] += direct[0:share, :]
    scores[pl.ds(high_rows, share), :] += direct[share:, :]

    out_rows = pl.ds(pl.multiple_of(me * out_share, 8), out_share)
    mine = table[out_rows, :]
    self_product, far_product = 1.0, 1.0
    for pop in range(2):
        k = 8 * pop
        own_row = [mine[:, k + s : k + s + 1] for s in range(3)]
        near_row = [mine[:, k + 3 + s : k + 4 + s] for s in range(3)]
        self_product *= correlation(own_row, own_row, mine[:, k + 6 : k + 7])
        far_product *= correlation(own_row, near_row, mine[:, k + 7 : k + 8])
    mine_annots = annots[out_rows, :]
    far_reach = jnp.where(me < groups // 2, reach_up, reach_down)
    scores[out_rows, :] += (
        mine_annots * self_product
        + near_annots[out_rows, :] * jnp.where(reach_here >= snps, far_product, 0.0)
        + pltpu.roll(mine_annots, HALF_LANES, 1) * jnp.where(far_reach >= snps, far_product, 0.0)
    )
    for step, target in enumerate(targets):
        group = lax.rem(me + step, groups)
        target[...] = scores[pl.ds(pl.multiple_of(group * out_share, 8), out_share), :]


def sum_kernel(*refs):
    *parts, out_ref = refs
    out_ref[...] = sum((part[...] for part in parts[1:]), parts[0][...])


def finish_kernel(own_ref, there_ref, out_ref):
    annots = out_ref.shape[0]
    there = pltpu.roll(there_ref[...], HALF_LANES, 1)
    out_ref[...] = (own_ref[...] + there).T[0:annots, :]


def around(value, groups, step):
    return lax.ppermute(
        value, "hap", [(source, (source + step) % groups) for source in range(groups)]
    )


def shifted(value, axis, steps):
    count = lax.axis_size(axis)
    leading, last = (max(0, -steps), min(count, count - steps))
    return lax.ppermute(value, axis, [(source, source + steps) for source in range(leading, last)])


def per_device(haplotypes, labels, annotations, reach):
    rows, snps = haplotypes.shape
    half = snps // 2
    groups = lax.axis_size("hap")
    blocks = lax.axis_size("snp")
    share = round_up(-(-half // groups), 16)
    folded_rows = share * groups
    out_share = snps // groups
    padded = half + folded_rows
    annot_part = 32
    bf16, f32, i32 = jnp.bfloat16, jnp.float32, jnp.int32
    shape = jax.ShapeDtypeStruct

    packed = shape((rows // 2 + annot_part, snps), bf16)
    alleles, up, down = call(
        prepare_kernel,
        [shape((rows, snps), bf16), packed, packed],
        [ANY, VMEM],
        [pltpu.VMEM((rows, snps), i32), pltpu.SemaphoreType.DMA((2 * CHUNKS,))],
        moved=rows * snps * 8,
    )(haplotypes, annotations)
    from_up = shifted(up, "snp", -1)
    from_down = shifted(down, "snp", 1)

    tile = pltpu.VMEM((snps + 16, snps), f32)
    folded = pltpu.VMEM((folded_rows, snps), i32)
    weighted, totals, *own_parts = call(
        functools.partial(own_kernel, groups, share),
        [shape((snps + 16, rows), bf16), shape((8, snps), f32)] + [shape((share, snps), i32)] * groups,
        [VMEM, VMEM],
        [tile, folded],
        flops=2 * rows * snps * snps,
        moved=rows * snps * 4,
    )(alleles, labels.reshape(1, rows))
    own_parts = [own_parts[0]] + [around(own_parts[k], groups, k) for k in range(1, groups)]

    near_parts = call(
        functools.partial(near_kernel, groups, share),
        [shape((share + 8, snps), i32)] * groups,
        [VMEM] * 4,
        [pltpu.VMEM((rows, snps), bf16), tile, folded],
        flops=2 * rows * snps * snps,
        moved=rows * snps * 4,
    )(weighted, from_up, from_down, totals)
    near_parts = [near_parts[0]] + [around(near_parts[k], groups, k) for k in range(1, groups)]

    by_snp = shape((snps, LANES), f32)
    own_annots, near_annots = call(annots_kernel, [by_snp, by_snp], [VMEM] * 3, moved=1 << 20)(
        annotations, from_up[rows // 2 :], from_down[rows // 2 :]
    )
    tall = pltpu.VMEM((padded, LANES), f32)
    scores = call(
        functools.partial(score_kernel, groups, share),
        [shape((out_share, LANES), f32)] * groups,
        [SMEM] + [VMEM] * (2 * groups + 2),
        [tall, tall, tall, tall],
        flops=1 << 26,
        moved=1 << 21,
    )(reach, *own_parts, *near_parts, own_annots, near_annots)
    scores = [scores[0]] + [around(scores[k], groups, k) for k in range(1, groups)]
    summed = call(sum_kernel, shape((out_share, LANES), f32), [VMEM] * groups)(*scores)
    pairs = []
    for block in range(blocks):
        for group in range(groups):
            target = block + 1 if group < groups // 2 else block - 1
            if 0 <= target < blocks:
                pairs.append((block * groups + group, target * groups + group))
    there = lax.ppermute(summed, ("snp", "hap"), pairs)
    return call(finish_kernel, shape((annotations.shape[0], out_share), f32), [VMEM] * 2)(summed, there)


def solution(mesh):
    in_specs = (
        P("hap", ("parts", "snp")),
        P(("parts", "hap")),
        P(None, ("parts", "snp")),
        P("parts"),
    )
    out_specs = P(None, ("parts", "snp", "hap"))
    return jax.shard_map(
        per_device, mesh=mesh, in_specs=in_specs, out_specs=out_specs, check_vma=False
    )
```

```python
import functools

import jax
import jax.numpy as jnp
from jax import lax
from jax.experimental import pallas as pl
from jax.experimental.pallas import tpu as pltpu
from jax.sharding import PartitionSpec as P

VARIANCE_FLOOR = 0.01
BASE_BITS = 12
BASE = 1 << BASE_BITS
FIELD_BITS = 16
LANES = 128
HALF_LANES = LANES // 2
CHUNKS = 4
VMEM = pl.BlockSpec(memory_space=pltpu.VMEM)
SMEM = pl.BlockSpec(memory_space=pltpu.SMEM)
HBM = pl.BlockSpec(memory_space=pltpu.HBM)
VMEM_LIMIT = 24 * 1024 * 1024


def iota(shape, axis):
    return lax.broadcasted_iota(jnp.int32, shape, axis)


def round_up(value, step):
    return -(-value // step) * step


def to_fields(values):
    whole = values.astype(jnp.int32)
    return whole + (whole >> BASE_BITS) * ((1 << FIELD_BITS) - BASE)


def from_fields(packed):
    first = packed & ((1 << FIELD_BITS) - 1)
    second = lax.shift_right_logical(packed, FIELD_BITS)
    return first.astype(jnp.float32), second.astype(jnp.float32)


def call(kernel, out_shape, in_specs, scratch_shapes=(), flops=0, moved=0):
    several = isinstance(out_shape, (list, tuple))
    return pl.pallas_call(
        kernel,
        out_shape=out_shape,
        in_specs=in_specs,
        out_specs=[VMEM] * len(out_shape) if several else VMEM,
        scratch_shapes=list(scratch_shapes),
        compiler_params=pltpu.CompilerParams(vmem_limit_bytes=VMEM_LIMIT),
        cost_estimate=pl.CostEstimate(flops=flops, bytes_accessed=moved, transcendentals=0),
    )


def odd_block():
    return lax.rem(lax.axis_index("snp"), 2) == 1


def store_packed(up_ref, down_ref, where, first, second):
    left = iota((first.shape[0], LANES), 1) < HALF_LANES
    middle = first[:, LANES : 2 * LANES]
    turned = pltpu.roll(second[:, LANES : 2 * LANES], HALF_LANES, 1)
    for ref, side, mixed in (
        (up_ref, slice(0, LANES), jnp.where(left, middle, turned)),
        (down_ref, slice(2 * LANES, 3 * LANES), jnp.where(left, turned, middle)),
    ):
        ref[where, 0:LANES] = first[:, side].astype(jnp.bfloat16)
        ref[where, LANES : 2 * LANES] = second[:, side].astype(jnp.bfloat16)
        ref[where, 2 * LANES : 3 * LANES] = mixed.astype(jnp.bfloat16)


def load_packed(up, down):
    left = iota((up.shape[0], LANES), 1) < HALF_LANES
    up_mixed, down_mixed = up[:, 2 * LANES :], down[:, 2 * LANES :]
    first = jnp.where(left, up_mixed, down_mixed)
    second = jnp.where(left, down_mixed, up_mixed)
    second = pltpu.roll(second.astype(jnp.float32), HALF_LANES, 1).astype(second.dtype)
    return (
        (up[:, :LANES], first, down[:, :LANES]),
        (up[:, LANES : 2 * LANES], second, down[:, LANES : 2 * LANES]),
    )


def prepare_kernel(hap_ref, annot_ref, alleles_ref, far_ref, close_ref, held, held_annots, sems):
    rows = hap_ref.shape[0]
    annot_rows = annot_ref.shape[0]
    size = rows // (2 * CHUNKS)
    starts = [side * (rows // 2) + chunk * size for chunk in range(CHUNKS) for side in range(2)]
    copies = [
        pltpu.make_async_copy(
            hap_ref.at[pl.ds(start, size)], held.at[pl.ds(start, size)], sems.at[number]
        )
        for number, start in enumerate(starts)
    ]
    copies.append(pltpu.make_async_copy(annot_ref, held_annots, sems.at[2 * CHUNKS]))
    for copy in copies:
        copy.start()
    part = far_ref.shape[0] - rows // 2
    odd = odd_block()

    def store(where, first, second):
        @pl.when(odd)
        def _():
            store_packed(close_ref, far_ref, where, first, second)

        @pl.when(jnp.logical_not(odd))
        def _():
            store_packed(far_ref, close_ref, where, first, second)

    for chunk in range(CHUNKS):
        pair = []
        for side in range(2):
            number = 2 * chunk + side
            copies[number].wait()
            where = slice(starts[number], starts[number] + size)
            values = held[where, :].astype(jnp.float32)
            alleles_ref[where, :] = values.astype(jnp.bfloat16)
            pair.append(values)
        store(slice(chunk * size, (chunk + 1) * size), *pair)
    copies[-1].wait()
    annots = jnp.concatenate(
        [
            held_annots[...].astype(jnp.float32),
            jnp.zeros((2 * part - annot_rows, annot_ref.shape[1]), jnp.float32),
        ],
        axis=0,
    )
    store(slice(rows // 2, rows // 2 + part), annots[:part], annots[part:])


def send_shares(groups, source, share, targets):
    me = lax.axis_index("hap")
    for step, target in enumerate(targets):
        group = lax.rem(me + step, groups)
        target[0:share, :] = source[pl.ds(pl.multiple_of(group * share, 8), share), :]


def own_kernel(groups, share, alleles_ref, label_ref, *refs):
    weighted_ref, totals_ref, *targets = refs[: 2 + groups]
    tile, folded = refs[2 + groups :]
    rows, snps = alleles_ref.shape
    half = snps // 2
    weight = jnp.where(label_ref[...] > 0, float(BASE), 1.0)
    weighted_ref[0:snps, :] = alleles_ref[...].T * weight.astype(jnp.bfloat16)
    extra = weighted_ref.shape[0] - snps
    weighted_ref[snps:, :] = jnp.broadcast_to(weight, (extra, rows)).astype(jnp.bfloat16)
    tile[...] = jnp.dot(weighted_ref[...], alleles_ref[...], preferred_element_type=jnp.float32)
    count = jnp.sum(weight, axis=1, keepdims=True)
    totals_ref[...] = jnp.concatenate(
        [tile[snps : snps + 1, :], jnp.broadcast_to(count, (1, snps)), jnp.zeros((6, snps))], axis=0
    )
    row, col = iota((half, snps), 0), iota((half, snps), 1)
    moved = (col < half) | (col - half > row)
    turned = pltpu.roll(tile[0:half, :], half, 1)
    folded[0:half, :] = to_fields(jnp.where(moved, turned, tile[half:snps, :]))
    if folded.shape[0] > half:
        folded[half:, :] = jnp.zeros((folded.shape[0] - half, snps), jnp.int32)
    send_shares(groups, folded, share, targets)


def near_kernel(groups, share, weighted_ref, far_ref, close_ref, totals_ref, *refs):
    own_parts, own_sum_ref = refs[:groups], refs[groups]
    targets, (near, tile, folded) = refs[groups + 1 : 2 * groups + 1], refs[2 * groups + 1 :]
    rows, snps = near.shape
    half = snps // 2
    odd = odd_block()

    def unpack(up_ref, down_ref):
        pieces = load_packed(up_ref[0 : rows // 2, :], down_ref[0 : rows // 2, :])
        for side in range(2):
            where = slice(side * (rows // 2), (side + 1) * (rows // 2))
            for number in range(3):
                near[where, number * LANES : (number + 1) * LANES] = pieces[side][number]

    @pl.when(odd)
    def _():
        unpack(far_ref, close_ref)

    @pl.when(jnp.logical_not(odd))
    def _():
        unpack(close_ref, far_ref)

    tile[...] = jnp.dot(weighted_ref[...], near[...], preferred_element_type=jnp.float32)
    row, col = iota((half, snps), 0), iota((half, snps), 1)
    moved = (col >= half) & (col - half < row)
    turned = pltpu.roll(tile[0:half, :], half, 1)
    folded[0:half, :] = to_fields(jnp.where(moved, turned, tile[half:snps, :]))
    if folded.shape[0] > half:
        folded[half:, :] = jnp.zeros((folded.shape[0] - half, snps), jnp.int32)
    square = (snps, snps)
    far = jnp.sum(
        jnp.where(iota(square, 0) == iota(square, 1), tile[0:snps, :], 0.0), axis=0, keepdims=True
    )
    extras = to_fields(
        jnp.concatenate(
            [totals_ref[0:2, :], tile[snps : snps + 1, :], far, jnp.zeros((4, snps))], axis=0
        )
    )
    send_shares(groups, folded, share, targets)
    for target in targets:
        target[share:, :] = extras
    own_sum_ref[...] = sum((part[...] for part in own_parts[1:]), own_parts[0][...])


def annots_kernel(annot_ref, far_ref, close_ref, own_ref, near_ref):
    snps = annot_ref.shape[1]
    part = far_ref.shape[0]
    wide = 2 * part
    own = annot_ref[...].astype(jnp.float32)
    own = jnp.concatenate([own, jnp.zeros((LANES - own.shape[0], snps), jnp.float32)], axis=0)
    own_ref[...] = own.T
    odd = odd_block()
    far, close = far_ref[...].astype(jnp.float32), close_ref[...].astype(jnp.float32)
    first, second = load_packed(jnp.where(odd, far, close), jnp.where(odd, close, far))
    near = jnp.concatenate(
        [
            jnp.concatenate([piece.astype(jnp.float32) for piece in first], axis=1),
            jnp.concatenate([piece.astype(jnp.float32) for piece in second], axis=1),
            jnp.zeros((LANES - wide, snps), jnp.float32),
        ],
        axis=0,
    )
    near_ref[...] = near.T


def column_stats(totals, count):
    size = jnp.maximum(count, 1.0)
    frequency = totals / size
    variance = jnp.maximum(frequency * (1.0 - frequency), VARIANCE_FLOOR)
    inverse = 1.0 / jnp.sqrt(size * variance)
    low = ((0.0 - frequency) * inverse).astype(jnp.bfloat16).astype(jnp.float32)
    high = ((1.0 - frequency) * inverse).astype(jnp.bfloat16).astype(jnp.float32)
    step = high - low
    root = 1.0 / jnp.sqrt(size)
    return step, step * totals * root, (low * count + step * totals) * root


def correlation(row, col, count):
    return row[0] * col[0] * count - row[1] * col[1] + row[2] * col[2]


def split(values):
    high = values.astype(jnp.bfloat16)
    return high, (values - high.astype(jnp.float32)).astype(jnp.bfloat16)


def dot_split(values, right, axis):
    dims = (((axis,), (0,)), ((), ()))
    return sum(
        lax.dot_general(part, right, dims, preferred_element_type=jnp.float32)
        for part in split(values)
    )


def score_kernel(groups, share, reach_ref, *refs):
    own_sum_ref, near_parts = refs[0], refs[1 : groups + 1]
    annot_ref, near_annot_ref = refs[groups + 1 : groups + 3]
    targets = refs[groups + 3 : 2 * groups + 3]
    table, annots, near_annots, scores = refs[2 * groups + 3 :]
    snps = annot_ref.shape[0]
    half = snps // 2
    out_share = snps // groups
    me = lax.axis_index("hap")
    block = lax.axis_index("snp")
    last = reach_ref.shape[0] - 1
    reach_here = reach_ref[block]
    reach_up = reach_ref[jnp.minimum(block + 1, last)]
    reach_down = reach_ref[jnp.maximum(block - 1, 0)]

    own_counts = own_sum_ref[...]
    near_sums = sum((part[...] for part in near_parts[1:]), near_parts[0][...])
    extras = from_fields(near_sums[share:, :])
    near_counts = near_sums[0:share, :]

    own_stats, near_stats, lines = [], [], []
    for pop in range(2):
        count = extras[pop][1:2, :]
        own_stats.append(column_stats(extras[pop][0:1, :], count))
        near_stats.append(column_stats(extras[pop][2:3, :], count))
        lines += [*own_stats[pop], *near_stats[pop], extras[pop][0:1, :], extras[pop][3:4, :]]
    by_row = jnp.concatenate(lines, axis=0).T
    table[0:snps, 0:16] = by_row
    if table.shape[0] > snps:
        table[snps:, 0:16] = jnp.zeros((table.shape[0] - snps, 16), jnp.float32)
    annots[0:snps, :] = annot_ref[...]
    near_annots[0:snps, :] = near_annot_ref[...]
    if annots.shape[0] > snps:
        annots[snps:, :] = jnp.zeros((annots.shape[0] - snps, LANES), jnp.float32)

    low_rows = pl.multiple_of(me * share, 8)
    high_rows = pl.multiple_of(half + me * share, 8)

    def both(ref):
        return jnp.concatenate([ref[pl.ds(low_rows, share), :], ref[pl.ds(high_rows, share), :]], axis=0)

    here = both(table)
    own_count = jnp.concatenate([pltpu.roll(own_counts, half, 1), own_counts], axis=0)
    near_count = jnp.concatenate([pltpu.roll(near_counts, half, 1), near_counts], axis=0)
    shape = (2 * share, snps)
    local, col = iota(shape, 0), iota(shape, 1)
    low = local < share
    place = jnp.where(low, local, local - share) + me * share
    row = jnp.where(low, place, place + half)
    own_fields, near_fields = from_fields(own_count), from_fields(near_count)
    own_product, near_product = 1.0, 1.0
    for pop in range(2):
        row_stats = [here[:, 8 * pop + k : 8 * pop + k + 1] for k in range(3)]
        own_product *= correlation(row_stats, own_stats[pop], own_fields[pop])
        near_product *= correlation(row_stats, near_stats[pop], near_fields[pop])
    real = place < half
    own_inside = real & ((low & (col > row)) | (~low & (col >= half) & (col < row)))
    own_inside &= jnp.abs(col - row) <= reach_here
    own_kept = jnp.where(own_inside, own_product, 0.0)
    in_upper = col < half
    near_inside = real & ((low & (col < row)) | (~low & (in_upper | (col > row))))
    distance = jnp.where(in_upper, snps + col - row, snps + row - col)
    near_here = jnp.where(near_inside & (distance <= reach_here), near_product, 0.0)
    reach_there = jnp.where(in_upper, reach_up, reach_down)
    near_there = jnp.where(near_inside & (distance <= reach_there), near_product, 0.0)

    rows_here = both(annots)
    rows_there = pltpu.roll(rows_here, HALF_LANES, 1)
    scores[0:snps, :] = dot_split(
        jnp.concatenate([own_kept, near_there], axis=0),
        jnp.concatenate([rows_here, rows_there], axis=0).astype(jnp.bfloat16),
        0,
    )
    direct = dot_split(
        jnp.concatenate([own_kept, near_here], axis=1),
        jnp.concatenate([annot_ref[...], near_annot_ref[...]], axis=0).astype(jnp.bfloat16),
        1,
    )
    scores[pl.ds(low_rows, share), :] += direct[0:share, :]
    scores[pl.ds(high_rows, share), :] += direct[share:, :]

    out_rows = pl.ds(pl.multiple_of(me * out_share, 8), out_share)
    mine = table[out_rows, :]
    self_product, far_product = 1.0, 1.0
    for pop in range(2):
        k = 8 * pop
        own_row = [mine[:, k + s : k + s + 1] for s in range(3)]
        near_row = [mine[:, k + 3 + s : k + 4 + s] for s in range(3)]
        self_product *= correlation(own_row, own_row, mine[:, k + 6 : k + 7])
        far_product *= correlation(own_row, near_row, mine[:, k + 7 : k + 8])
    mine_annots = annots[out_rows, :]
    far_reach = jnp.where(me < groups // 2, reach_up, reach_down)
    scores[out_rows, :] += (
        mine_annots * self_product
        + near_annots[out_rows, :] * jnp.where(reach_here >= snps, far_product, 0.0)
        + pltpu.roll(mine_annots, HALF_LANES, 1) * jnp.where(far_reach >= snps, far_product, 0.0)
    )
    for step, target in enumerate(targets):
        group = lax.rem(me + step, groups)
        target[...] = scores[pl.ds(pl.multiple_of(group * out_share, 8), out_share), :]


def sum_kernel(*refs):
    *parts, out_ref = refs
    out_ref[...] = sum((part[...] for part in parts[1:]), parts[0][...])


def finish_kernel(own_ref, there_ref, out_ref):
    annots = out_ref.shape[0]
    there = pltpu.roll(there_ref[...], HALF_LANES, 1)
    out_ref[...] = (own_ref[...] + there).T[0:annots, :]


def around(value, groups, step):
    return lax.ppermute(
        value, "hap", [(source, (source + step) % groups) for source in range(groups)]
    )


def swapped(value, first):
    pairs = []
    for block in range(first, lax.axis_size("snp") - 1, 2):
        pairs += [(block, block + 1), (block + 1, block)]
    return lax.ppermute(value, "snp", pairs)


def per_device(haplotypes, labels, annotations, reach):
    rows, snps = haplotypes.shape
    half = snps // 2
    groups = lax.axis_size("hap")
    blocks = lax.axis_size("snp")
    share = round_up(-(-half // groups), 16)
    folded_rows = share * groups
    out_share = snps // groups
    padded = half + folded_rows
    annot_part = 32
    bf16, f32, i32 = jnp.bfloat16, jnp.float32, jnp.int32
    shape = jax.ShapeDtypeStruct

    packed = shape((rows // 2 + annot_part, snps), bf16)
    haplotypes = pltpu.with_memory_space_constraint(haplotypes, pltpu.HBM)
    annots_in = pltpu.with_memory_space_constraint(annotations, pltpu.HBM)
    alleles, far, close = call(
        prepare_kernel,
        [shape((rows, snps), bf16), packed, packed],
        [HBM, HBM],
        [
            pltpu.VMEM((rows, snps), i32),
            pltpu.VMEM(annotations.shape, i32),
            pltpu.SemaphoreType.DMA((2 * CHUNKS + 1,)),
        ],
        moved=rows * snps * 8,
    )(haplotypes, annots_in)
    from_far = swapped(far, 1)
    from_close = swapped(close, 0)

    tile = pltpu.VMEM((snps + 16, snps), f32)
    folded = pltpu.VMEM((folded_rows, snps), i32)
    weighted, totals, *own_parts = call(
        functools.partial(own_kernel, groups, share),
        [shape((snps + 16, rows), bf16), shape((8, snps), f32)] + [shape((share, snps), i32)] * groups,
        [VMEM, VMEM],
        [tile, folded],
        flops=2 * rows * snps * snps,
        moved=rows * snps * 4,
    )(alleles, labels.reshape(1, rows))
    own_parts = [own_parts[0]] + [around(own_parts[k], groups, k) for k in range(1, groups)]

    own_sum, *near_parts = call(
        functools.partial(near_kernel, groups, share),
        [shape((share, snps), i32)] + [shape((share + 8, snps), i32)] * groups,
        [VMEM] * (4 + groups),
        [pltpu.VMEM((rows, snps), bf16), tile, folded],
        flops=2 * rows * snps * snps,
        moved=rows * snps * 4,
    )(weighted, from_far, from_close, totals, *own_parts)
    near_parts = [near_parts[0]] + [around(near_parts[k], groups, k) for k in range(1, groups)]

    by_snp = shape((snps, LANES), f32)
    own_annots, near_annots = call(annots_kernel, [by_snp, by_snp], [VMEM] * 3, moved=1 << 20)(
        annotations, from_far[rows // 2 :], from_close[rows // 2 :]
    )
    tall = pltpu.VMEM((padded, LANES), f32)
    scores = call(
        functools.partial(score_kernel, groups, share),
        [shape((out_share, LANES), f32)] * groups,
        [SMEM] + [VMEM] * (groups + 3),
        [tall, tall, tall, tall],
        flops=1 << 26,
        moved=1 << 21,
    )(reach, own_sum, *near_parts, own_annots, near_annots)
    scores = [scores[0]] + [around(scores[k], groups, k) for k in range(1, groups)]
    summed = call(sum_kernel, shape((out_share, LANES), f32), [VMEM] * groups)(*scores)
    pairs = []
    for block in range(blocks):
        for group in range(groups):
            target = block + 1 if group < groups // 2 else block - 1
            if 0 <= target < blocks:
                pairs.append((block * groups + group, target * groups + group))
    there = lax.ppermute(summed, ("snp", "hap"), pairs)
    return call(finish_kernel, shape((annotations.shape[0], out_share), f32), [VMEM] * 2)(summed, there)


def solution(mesh):
    in_specs = (
        P("hap", ("parts", "snp")),
        P(("parts", "hap")),
        P(None, ("parts", "snp")),
        P("parts"),
    )
    out_specs = P(None, ("parts", "snp", "hap"))
    return jax.shard_map(
        per_device, mesh=mesh, in_specs=in_specs, out_specs=out_specs, check_vma=False
    )
```

```python
import functools

import jax
import jax.numpy as jnp
from jax import lax
from jax.experimental import pallas as pl
from jax.experimental.pallas import tpu as pltpu
from jax.sharding import PartitionSpec as P

VARIANCE_FLOOR = 0.01
BASE_BITS = 12
BASE = 1 << BASE_BITS
FIELD_BITS = 16
LANES = 128
HALF_LANES = LANES // 2
CHUNKS = 4
VMEM = pl.BlockSpec(memory_space=pltpu.VMEM)
SMEM = pl.BlockSpec(memory_space=pltpu.SMEM)
HBM = pl.BlockSpec(memory_space=pltpu.HBM)
VMEM_LIMIT = 24 * 1024 * 1024


def iota(shape, axis):
    return lax.broadcasted_iota(jnp.int32, shape, axis)


def round_up(value, step):
    return -(-value // step) * step


def to_fields(values):
    whole = values.astype(jnp.int32)
    return whole + (whole >> BASE_BITS) * ((1 << FIELD_BITS) - BASE)


def from_fields(packed):
    first = packed & ((1 << FIELD_BITS) - 1)
    second = lax.shift_right_logical(packed, FIELD_BITS)
    return first.astype(jnp.float32), second.astype(jnp.float32)


def call(kernel, out_shape, in_specs, scratch_shapes=(), flops=0, moved=0):
    several = isinstance(out_shape, (list, tuple))
    return pl.pallas_call(
        kernel,
        out_shape=out_shape,
        in_specs=in_specs,
        out_specs=[VMEM] * len(out_shape) if several else VMEM,
        scratch_shapes=list(scratch_shapes),
        compiler_params=pltpu.CompilerParams(vmem_limit_bytes=VMEM_LIMIT),
        cost_estimate=pl.CostEstimate(flops=flops, bytes_accessed=moved, transcendentals=0),
    )


def odd_block():
    return lax.rem(lax.axis_index("snp"), 2) == 1


def store_packed(up_ref, down_ref, where, first, second):
    left = iota((first.shape[0], LANES), 1) < HALF_LANES
    middle = first[:, LANES : 2 * LANES]
    turned = pltpu.roll(second[:, LANES : 2 * LANES], HALF_LANES, 1)
    for ref, side, mixed in (
        (up_ref, slice(0, LANES), jnp.where(left, middle, turned)),
        (down_ref, slice(2 * LANES, 3 * LANES), jnp.where(left, turned, middle)),
    ):
        ref[where, 0:LANES] = first[:, side].astype(jnp.bfloat16)
        ref[where, LANES : 2 * LANES] = second[:, side].astype(jnp.bfloat16)
        ref[where, 2 * LANES : 3 * LANES] = mixed.astype(jnp.bfloat16)


def load_packed(up, down):
    left = iota((up.shape[0], LANES), 1) < HALF_LANES
    up_mixed, down_mixed = up[:, 2 * LANES :], down[:, 2 * LANES :]
    first = jnp.where(left, up_mixed, down_mixed)
    second = jnp.where(left, down_mixed, up_mixed)
    second = pltpu.roll(second.astype(jnp.float32), HALF_LANES, 1).astype(second.dtype)
    return (
        (up[:, :LANES], first, down[:, :LANES]),
        (up[:, LANES : 2 * LANES], second, down[:, LANES : 2 * LANES]),
    )


def prepare_kernel(hap_ref, annot_ref, alleles_ref, far_ref, close_ref, held, held_annots, sems):
    rows = hap_ref.shape[0]
    annot_rows = annot_ref.shape[0]
    size = rows // (2 * CHUNKS)
    starts = [side * (rows // 2) + chunk * size for chunk in range(CHUNKS) for side in range(2)]
    copies = [
        pltpu.make_async_copy(
            hap_ref.at[pl.ds(start, size)], held.at[pl.ds(start, size)], sems.at[number]
        )
        for number, start in enumerate(starts)
    ]
    copies.append(pltpu.make_async_copy(annot_ref, held_annots, sems.at[2 * CHUNKS]))
    for copy in copies:
        copy.start()
    part = far_ref.shape[0] - rows // 2
    odd = odd_block()

    def store(where, first, second):
        @pl.when(odd)
        def _():
            store_packed(close_ref, far_ref, where, first, second)

        @pl.when(jnp.logical_not(odd))
        def _():
            store_packed(far_ref, close_ref, where, first, second)

    for chunk in range(CHUNKS):
        pair = []
        for side in range(2):
            number = 2 * chunk + side
            copies[number].wait()
            where = slice(starts[number], starts[number] + size)
            values = held[where, :].astype(jnp.float32)
            alleles_ref[where, :] = values.astype(jnp.bfloat16)
            pair.append(values)
        store(slice(chunk * size, (chunk + 1) * size), *pair)
    copies[-1].wait()
    annots = jnp.concatenate(
        [
            held_annots[...].astype(jnp.float32),
            jnp.zeros((2 * part - annot_rows, annot_ref.shape[1]), jnp.float32),
        ],
        axis=0,
    )
    store(slice(rows // 2, rows // 2 + part), annots[:part], annots[part:])


def pad_rows(ref, done):
    if ref.shape[0] > done:
        ref[done:, :] = jnp.zeros((ref.shape[0] - done, ref.shape[1]), ref.dtype)


def sum_of_parts(ref, groups):
    size = ref.shape[0] // groups
    return sum((ref[k * size : (k + 1) * size, :] for k in range(1, groups)), ref[0:size, :])


def own_kernel(alleles_ref, label_ref, weighted_ref, totals_ref, folded, tile):
    rows, snps = alleles_ref.shape
    half = snps // 2
    weight = jnp.where(label_ref[...] > 0, float(BASE), 1.0)
    weighted_ref[0:snps, :] = alleles_ref[...].T * weight.astype(jnp.bfloat16)
    extra = weighted_ref.shape[0] - snps
    weighted_ref[snps:, :] = jnp.broadcast_to(weight, (extra, rows)).astype(jnp.bfloat16)
    tile[...] = jnp.dot(weighted_ref[...], alleles_ref[...], preferred_element_type=jnp.float32)
    count = jnp.sum(weight, axis=1, keepdims=True)
    totals_ref[...] = jnp.concatenate(
        [tile[snps : snps + 1, :], jnp.broadcast_to(count, (1, snps)), jnp.zeros((6, snps))], axis=0
    )
    row, col = iota((half, snps), 0), iota((half, snps), 1)
    moved = (col < half) | (col - half > row)
    turned = pltpu.roll(tile[0:half, :], half, 1)
    folded[0:half, :] = to_fields(jnp.where(moved, turned, tile[half:snps, :]))
    pad_rows(folded, half)


def near_kernel(
    groups, weighted_ref, far_ref, close_ref, totals_ref, own_parts_ref, own_sum_ref, out_ref, near, tile
):
    rows, snps = near.shape
    half = snps // 2
    odd = odd_block()

    def unpack(up_ref, down_ref):
        pieces = load_packed(up_ref[0 : rows // 2, :], down_ref[0 : rows // 2, :])
        for side in range(2):
            where = slice(side * (rows // 2), (side + 1) * (rows // 2))
            for number in range(3):
                near[where, number * LANES : (number + 1) * LANES] = pieces[side][number]

    @pl.when(odd)
    def _():
        unpack(far_ref, close_ref)

    @pl.when(jnp.logical_not(odd))
    def _():
        unpack(close_ref, far_ref)

    tile[...] = jnp.dot(weighted_ref[...], near[...], preferred_element_type=jnp.float32)
    row, col = iota((half, snps), 0), iota((half, snps), 1)
    moved = (col >= half) & (col - half < row)
    turned = pltpu.roll(tile[0:half, :], half, 1)
    folded = to_fields(jnp.where(moved, turned, tile[half:snps, :]))
    square = (snps, snps)
    far = jnp.sum(
        jnp.where(iota(square, 0) == iota(square, 1), tile[0:snps, :], 0.0), axis=0, keepdims=True
    )
    extras = to_fields(
        jnp.concatenate(
            [totals_ref[0:2, :], tile[snps : snps + 1, :], far, jnp.zeros((4, snps))], axis=0
        )
    )
    size = out_ref.shape[0] // groups
    share = size - extras.shape[0]
    for group in range(groups):
        start = group * size
        real = min(max(half - group * share, 0), share)
        if real:
            out_ref[start : start + real, :] = folded[group * share : group * share + real, :]
        if real < share:
            out_ref[start + real : start + share, :] = jnp.zeros((share - real, snps), jnp.int32)
        out_ref[start + share : start + size, :] = extras
    own_sum_ref[...] = sum_of_parts(own_parts_ref, groups)


def annots_kernel(annot_ref, far_ref, close_ref, own_ref, near_ref):
    snps = annot_ref.shape[1]
    part = far_ref.shape[0]
    wide = 2 * part
    own = annot_ref[...].astype(jnp.float32)
    own = jnp.concatenate([own, jnp.zeros((LANES - own.shape[0], snps), jnp.float32)], axis=0)
    own_ref[...] = own.T
    odd = odd_block()
    far, close = far_ref[...].astype(jnp.float32), close_ref[...].astype(jnp.float32)
    first, second = load_packed(jnp.where(odd, far, close), jnp.where(odd, close, far))
    near = jnp.concatenate(
        [
            jnp.concatenate([piece.astype(jnp.float32) for piece in first], axis=1),
            jnp.concatenate([piece.astype(jnp.float32) for piece in second], axis=1),
            jnp.zeros((LANES - wide, snps), jnp.float32),
        ],
        axis=0,
    )
    near_ref[...] = near.T


def column_stats(totals, count):
    size = jnp.maximum(count, 1.0)
    frequency = totals / size
    variance = jnp.maximum(frequency * (1.0 - frequency), VARIANCE_FLOOR)
    inverse = 1.0 / jnp.sqrt(size * variance)
    low = ((0.0 - frequency) * inverse).astype(jnp.bfloat16).astype(jnp.float32)
    high = ((1.0 - frequency) * inverse).astype(jnp.bfloat16).astype(jnp.float32)
    step = high - low
    root = 1.0 / jnp.sqrt(size)
    return step, step * totals * root, (low * count + step * totals) * root


def correlation(row, col, count):
    return row[0] * col[0] * count - row[1] * col[1] + row[2] * col[2]


def split(values):
    high = values.astype(jnp.bfloat16)
    return high, (values - high.astype(jnp.float32)).astype(jnp.bfloat16)


def dot_split(values, right, axis):
    dims = (((axis,), (0,)), ((), ()))
    return sum(
        lax.dot_general(part, right, dims, preferred_element_type=jnp.float32)
        for part in split(values)
    )


def score_kernel(
    groups, reach_ref, own_sum_ref, near_parts_ref, annot_ref, near_annot_ref, out_ref, table, annots, near_annots, *more
):
    scores = more[0] if more else out_ref
    share = own_sum_ref.shape[0]
    snps = annot_ref.shape[0]
    half = snps // 2
    out_share = snps // groups
    me = lax.axis_index("hap")
    block = lax.axis_index("snp")
    last = reach_ref.shape[0] - 1
    reach_here = reach_ref[block]
    reach_up = reach_ref[jnp.minimum(block + 1, last)]
    reach_down = reach_ref[jnp.maximum(block - 1, 0)]

    own_counts = own_sum_ref[...]
    near_sums = sum_of_parts(near_parts_ref, groups)
    extras = from_fields(near_sums[share:, :])
    near_counts = near_sums[0:share, :]

    own_stats, near_stats, lines = [], [], []
    for pop in range(2):
        count = extras[pop][1:2, :]
        own_stats.append(column_stats(extras[pop][0:1, :], count))
        near_stats.append(column_stats(extras[pop][2:3, :], count))
        lines += [*own_stats[pop], *near_stats[pop], extras[pop][0:1, :], extras[pop][3:4, :]]
    by_row = jnp.concatenate(lines, axis=0).T
    table[0:snps, 0:16] = by_row
    if table.shape[0] > snps:
        table[snps:, 0:16] = jnp.zeros((table.shape[0] - snps, 16), jnp.float32)
    annots[0:snps, :] = annot_ref[...]
    near_annots[0:snps, :] = near_annot_ref[...]
    if annots.shape[0] > snps:
        annots[snps:, :] = jnp.zeros((annots.shape[0] - snps, LANES), jnp.float32)

    low_rows = pl.multiple_of(me * share, 8)
    high_rows = pl.multiple_of(half + me * share, 8)

    def both(ref):
        return jnp.concatenate([ref[pl.ds(low_rows, share), :], ref[pl.ds(high_rows, share), :]], axis=0)

    here = both(table)
    own_count = jnp.concatenate([pltpu.roll(own_counts, half, 1), own_counts], axis=0)
    near_count = jnp.concatenate([pltpu.roll(near_counts, half, 1), near_counts], axis=0)
    shape = (2 * share, snps)
    local, col = iota(shape, 0), iota(shape, 1)
    low = local < share
    place = jnp.where(low, local, local - share) + me * share
    row = jnp.where(low, place, place + half)
    own_fields, near_fields = from_fields(own_count), from_fields(near_count)
    own_product, near_product = 1.0, 1.0
    for pop in range(2):
        row_stats = [here[:, 8 * pop + k : 8 * pop + k + 1] for k in range(3)]
        own_product *= correlation(row_stats, own_stats[pop], own_fields[pop])
        near_product *= correlation(row_stats, near_stats[pop], near_fields[pop])
    real = place < half
    own_inside = real & ((low & (col > row)) | (~low & (col >= half) & (col < row)))
    own_inside &= jnp.abs(col - row) <= reach_here
    own_kept = jnp.where(own_inside, own_product, 0.0)
    in_upper = col < half
    near_inside = real & ((low & (col < row)) | (~low & (in_upper | (col > row))))
    distance = jnp.where(in_upper, snps + col - row, snps + row - col)
    near_here = jnp.where(near_inside & (distance <= reach_here), near_product, 0.0)
    reach_there = jnp.where(in_upper, reach_up, reach_down)
    near_there = jnp.where(near_inside & (distance <= reach_there), near_product, 0.0)

    rows_here = both(annots)
    rows_there = pltpu.roll(rows_here, HALF_LANES, 1)
    scores[0:snps, :] = dot_split(
        jnp.concatenate([own_kept, near_there], axis=0),
        jnp.concatenate([rows_here, rows_there], axis=0).astype(jnp.bfloat16),
        0,
    )
    direct = dot_split(
        jnp.concatenate([own_kept, near_here], axis=1),
        jnp.concatenate([annot_ref[...], near_annot_ref[...]], axis=0).astype(jnp.bfloat16),
        1,
    )
    scores[pl.ds(low_rows, share), :] += direct[0:share, :]
    scores[pl.ds(high_rows, share), :] += direct[share:, :]

    out_rows = pl.ds(pl.multiple_of(me * out_share, 8), out_share)
    mine = table[out_rows, :]
    self_product, far_product = 1.0, 1.0
    for pop in range(2):
        k = 8 * pop
        own_row = [mine[:, k + s : k + s + 1] for s in range(3)]
        near_row = [mine[:, k + 3 + s : k + 4 + s] for s in range(3)]
        self_product *= correlation(own_row, own_row, mine[:, k + 6 : k + 7])
        far_product *= correlation(own_row, near_row, mine[:, k + 7 : k + 8])
    mine_annots = annots[out_rows, :]
    far_reach = jnp.where(me < groups // 2, reach_up, reach_down)
    scores[out_rows, :] += (
        mine_annots * self_product
        + near_annots[out_rows, :] * jnp.where(reach_here >= snps, far_product, 0.0)
        + pltpu.roll(mine_annots, HALF_LANES, 1) * jnp.where(far_reach >= snps, far_product, 0.0)
    )
    if more:
        out_ref[...] = scores[0:snps, :]


def sum_kernel(groups, parts_ref, out_ref):
    out_ref[...] = sum_of_parts(parts_ref, groups)


def finish_kernel(own_ref, there_ref, out_ref):
    annots = out_ref.shape[0]
    there = pltpu.roll(there_ref[...], HALF_LANES, 1)
    out_ref[...] = (own_ref[...] + there).T[0:annots, :]


def exchanged(value):
    return lax.all_to_all(value, "hap", 0, 0, tiled=True)


def swapped(value, first):
    pairs = []
    for block in range(first, lax.axis_size("snp") - 1, 2):
        pairs += [(block, block + 1), (block + 1, block)]
    return lax.ppermute(value, "snp", pairs)


def per_device(haplotypes, labels, annotations, reach):
    rows, snps = haplotypes.shape
    half = snps // 2
    groups = lax.axis_size("hap")
    blocks = lax.axis_size("snp")
    share = round_up(-(-half // groups), 16)
    folded_rows = share * groups
    out_share = snps // groups
    padded = half + folded_rows
    annot_part = 32
    bf16, f32, i32 = jnp.bfloat16, jnp.float32, jnp.int32
    shape = jax.ShapeDtypeStruct

    packed = shape((rows // 2 + annot_part, snps), bf16)
    haplotypes = pltpu.with_memory_space_constraint(haplotypes, pltpu.HBM)
    annots_in = pltpu.with_memory_space_constraint(annotations, pltpu.HBM)
    alleles, far, close = call(
        prepare_kernel,
        [shape((rows, snps), bf16), packed, packed],
        [HBM, HBM],
        [
            pltpu.VMEM((rows, snps), i32),
            pltpu.VMEM(annotations.shape, i32),
            pltpu.SemaphoreType.DMA((2 * CHUNKS + 1,)),
        ],
        moved=rows * snps * 8,
    )(haplotypes, annots_in)
    from_far = swapped(far, 1)
    from_close = swapped(close, 0)

    tile = pltpu.VMEM((snps + 16, snps), f32)
    weighted, totals, own_parts = call(
        own_kernel,
        [shape((snps + 16, rows), bf16), shape((8, snps), f32), shape((folded_rows, snps), i32)],
        [VMEM, VMEM],
        [tile],
        flops=2 * rows * snps * snps,
        moved=rows * snps * 4,
    )(alleles, labels.reshape(1, rows))
    own_parts = exchanged(own_parts)

    own_sum, near_parts = call(
        functools.partial(near_kernel, groups),
        [shape((share, snps), i32), shape(((share + 8) * groups, snps), i32)],
        [VMEM] * 5,
        [pltpu.VMEM((rows, snps), bf16), tile],
        flops=2 * rows * snps * snps,
        moved=rows * snps * 4,
    )(weighted, from_far, from_close, totals, own_parts)
    near_parts = exchanged(near_parts)

    by_snp = shape((snps, LANES), f32)
    own_annots, near_annots = call(annots_kernel, [by_snp, by_snp], [VMEM] * 3, moved=1 << 20)(
        annotations, from_far[rows // 2 :], from_close[rows // 2 :]
    )
    tall = pltpu.VMEM((padded, LANES), f32)
    scores = call(
        functools.partial(score_kernel, groups),
        by_snp,
        [SMEM] + [VMEM] * 4,
        [tall] * (3 if padded == snps else 4),
        flops=1 << 26,
        moved=1 << 21,
    )(reach, own_sum, near_parts, own_annots, near_annots)
    summed = call(functools.partial(sum_kernel, groups), shape((out_share, LANES), f32), [VMEM])(
        exchanged(scores)
    )
    pairs = []
    for block in range(blocks):
        for group in range(groups):
            target = block + 1 if group < groups // 2 else block - 1
            if 0 <= target < blocks:
                pairs.append((block * groups + group, target * groups + group))
    there = lax.ppermute(summed, ("snp", "hap"), pairs)
    return call(finish_kernel, shape((annotations.shape[0], out_share), f32), [VMEM] * 2)(summed, there)


def solution(mesh):
    in_specs = (
        P("hap", ("parts", "snp")),
        P(("parts", "hap")),
        P(None, ("parts", "snp")),
        P("parts"),
    )
    out_specs = P(None, ("parts", "snp", "hap"))
    return jax.shard_map(
        per_device, mesh=mesh, in_specs=in_specs, out_specs=out_specs, check_vma=False
    )
```

```python
import functools

import jax
import jax.numpy as jnp
from jax import lax
from jax.experimental import pallas as pl
from jax.experimental.pallas import tpu as pltpu
from jax.sharding import PartitionSpec as P

VARIANCE_FLOOR = 0.01
BASE_BITS = 12
BASE = 1 << BASE_BITS
FIELD_BITS = 16
LANES = 128
HALF_LANES = LANES // 2
CHUNKS = 4
VMEM = pl.BlockSpec(memory_space=pltpu.VMEM)
SMEM = pl.BlockSpec(memory_space=pltpu.SMEM)
HBM = pl.BlockSpec(memory_space=pltpu.HBM)
VMEM_LIMIT = 24 * 1024 * 1024


def iota(shape, axis):
    return lax.broadcasted_iota(jnp.int32, shape, axis)


def round_up(value, step):
    return -(-value // step) * step


def to_fields(values):
    whole = values.astype(jnp.int32)
    return whole + (whole >> BASE_BITS) * ((1 << FIELD_BITS) - BASE)


def from_fields(packed):
    first = packed & ((1 << FIELD_BITS) - 1)
    second = lax.shift_right_logical(packed, FIELD_BITS)
    return first.astype(jnp.float32), second.astype(jnp.float32)


def call(kernel, out_shape, in_specs, scratch_shapes=(), flops=0, moved=0):
    several = isinstance(out_shape, (list, tuple))
    return pl.pallas_call(
        kernel,
        out_shape=out_shape,
        in_specs=in_specs,
        out_specs=[VMEM] * len(out_shape) if several else VMEM,
        scratch_shapes=list(scratch_shapes),
        compiler_params=pltpu.CompilerParams(vmem_limit_bytes=VMEM_LIMIT),
        cost_estimate=pl.CostEstimate(flops=flops, bytes_accessed=moved, transcendentals=0),
    )


def odd_block():
    return lax.rem(lax.axis_index("snp"), 2) == 1


def store_packed(up_ref, down_ref, where, first, second):
    left = iota((first.shape[0], LANES), 1) < HALF_LANES
    middle = first[:, LANES : 2 * LANES]
    turned = pltpu.roll(second[:, LANES : 2 * LANES], HALF_LANES, 1)
    for ref, side, mixed in (
        (up_ref, slice(0, LANES), jnp.where(left, middle, turned)),
        (down_ref, slice(2 * LANES, 3 * LANES), jnp.where(left, turned, middle)),
    ):
        ref[where, 0:LANES] = first[:, side].astype(jnp.bfloat16)
        ref[where, LANES : 2 * LANES] = second[:, side].astype(jnp.bfloat16)
        ref[where, 2 * LANES : 3 * LANES] = mixed.astype(jnp.bfloat16)


def load_packed(up, down):
    left = iota((up.shape[0], LANES), 1) < HALF_LANES
    up_mixed, down_mixed = up[:, 2 * LANES :], down[:, 2 * LANES :]
    first = jnp.where(left, up_mixed, down_mixed)
    second = jnp.where(left, down_mixed, up_mixed)
    second = pltpu.roll(second.astype(jnp.float32), HALF_LANES, 1).astype(second.dtype)
    return (
        (up[:, :LANES], first, down[:, :LANES]),
        (up[:, LANES : 2 * LANES], second, down[:, LANES : 2 * LANES]),
    )


def prepare_kernel(hap_ref, annot_ref, alleles_ref, far_ref, close_ref, held, held_annots, sems):
    rows = hap_ref.shape[0]
    annot_rows = annot_ref.shape[0]
    size = rows // (2 * CHUNKS)
    starts = [side * (rows // 2) + chunk * size for chunk in range(CHUNKS) for side in range(2)]
    copies = [
        pltpu.make_async_copy(
            hap_ref.at[pl.ds(start, size)], held.at[pl.ds(start, size)], sems.at[number]
        )
        for number, start in enumerate(starts)
    ]
    copies.append(pltpu.make_async_copy(annot_ref, held_annots, sems.at[2 * CHUNKS]))
    for copy in copies:
        copy.start()
    part = far_ref.shape[0] - rows // 2
    odd = odd_block()

    def store(where, first, second):
        @pl.when(odd)
        def _():
            store_packed(close_ref, far_ref, where, first, second)

        @pl.when(jnp.logical_not(odd))
        def _():
            store_packed(far_ref, close_ref, where, first, second)

    for chunk in range(CHUNKS):
        pair = []
        for side in range(2):
            number = 2 * chunk + side
            copies[number].wait()
            where = slice(starts[number], starts[number] + size)
            values = held[where, :].astype(jnp.float32)
            alleles_ref[where, :] = values.astype(jnp.bfloat16)
            pair.append(values)
        store(slice(chunk * size, (chunk + 1) * size), *pair)
    copies[-1].wait()
    annots = jnp.concatenate(
        [
            held_annots[...].astype(jnp.float32),
            jnp.zeros((2 * part - annot_rows, annot_ref.shape[1]), jnp.float32),
        ],
        axis=0,
    )
    store(slice(rows // 2, rows // 2 + part), annots[:part], annots[part:])


def partner(group, step, groups):
    if groups & (groups - 1) == 0:
        return group ^ step
    return (group + step) % groups


def send_shares(groups, source, share, targets):
    me = lax.axis_index("hap")
    for step, target in enumerate(targets):
        group = partner(me, step, groups)
        rows = source[pl.ds(pl.multiple_of(group * share, 8), share), :]
        target[0:share, :] = rows.astype(target.dtype)


def own_kernel(groups, share, alleles_ref, label_ref, *refs):
    weighted_ref, totals_ref, *targets = refs[: 2 + groups]
    tile, folded = refs[2 + groups :]
    rows, snps = alleles_ref.shape
    half = snps // 2
    weight = jnp.where(label_ref[...] > 0, float(BASE), 1.0)
    weighted_ref[0:snps, :] = alleles_ref[...].T * weight.astype(jnp.bfloat16)
    extra = weighted_ref.shape[0] - snps
    weighted_ref[snps:, :] = jnp.broadcast_to(weight, (extra, rows)).astype(jnp.bfloat16)
    tile[...] = jnp.dot(weighted_ref[...], alleles_ref[...], preferred_element_type=jnp.float32)
    count = jnp.sum(weight, axis=1, keepdims=True)
    totals_ref[...] = jnp.concatenate(
        [tile[snps : snps + 1, :], jnp.broadcast_to(count, (1, snps)), jnp.zeros((6, snps))], axis=0
    )
    row, col = iota((half, snps), 0), iota((half, snps), 1)
    moved = (col < half) | (col - half > row)
    turned = pltpu.roll(tile[0:half, :], half, 1)
    folded[0:half, :] = to_fields(jnp.where(moved, turned, tile[half:snps, :]))
    if folded.shape[0] > half:
        folded[half:, :] = jnp.zeros((folded.shape[0] - half, snps), jnp.int32)
    send_shares(groups, folded, share, targets)


def near_kernel(groups, share, weighted_ref, far_ref, close_ref, totals_ref, *refs):
    own_parts, own_sum_ref = refs[:groups], refs[groups]
    targets, (near, tile, folded) = refs[groups + 1 : 2 * groups + 1], refs[2 * groups + 1 :]
    rows, snps = near.shape
    half = snps // 2
    odd = odd_block()

    def unpack(up_ref, down_ref):
        pieces = load_packed(up_ref[0 : rows // 2, :], down_ref[0 : rows // 2, :])
        for side in range(2):
            where = slice(side * (rows // 2), (side + 1) * (rows // 2))
            for number in range(3):
                near[where, number * LANES : (number + 1) * LANES] = pieces[side][number]

    @pl.when(odd)
    def _():
        unpack(far_ref, close_ref)

    @pl.when(jnp.logical_not(odd))
    def _():
        unpack(close_ref, far_ref)

    tile[...] = jnp.dot(weighted_ref[...], near[...], preferred_element_type=jnp.float32)
    row, col = iota((half, snps), 0), iota((half, snps), 1)
    moved = (col >= half) & (col - half < row)
    turned = pltpu.roll(tile[0:half, :], half, 1)
    folded[0:half, :] = to_fields(jnp.where(moved, turned, tile[half:snps, :]))
    if folded.shape[0] > half:
        folded[half:, :] = jnp.zeros((folded.shape[0] - half, snps), jnp.int32)
    square = (snps, snps)
    far = jnp.sum(
        jnp.where(iota(square, 0) == iota(square, 1), tile[0:snps, :], 0.0), axis=0, keepdims=True
    )
    extras = to_fields(
        jnp.concatenate(
            [totals_ref[0:2, :], tile[snps : snps + 1, :], far, jnp.zeros((4, snps))], axis=0
        )
    )
    send_shares(groups, folded, share, targets)
    for target in targets:
        target[share:, :] = extras
    own_sum_ref[...] = sum((part[...] for part in own_parts[1:]), own_parts[0][...])


def annots_kernel(annot_ref, far_ref, close_ref, own_ref, near_ref):
    snps = annot_ref.shape[1]
    part = far_ref.shape[0]
    wide = 2 * part
    own = annot_ref[...].astype(jnp.float32)
    own = jnp.concatenate([own, jnp.zeros((LANES - own.shape[0], snps), jnp.float32)], axis=0)
    own_ref[...] = own.T
    odd = odd_block()
    far, close = far_ref[...].astype(jnp.float32), close_ref[...].astype(jnp.float32)
    first, second = load_packed(jnp.where(odd, far, close), jnp.where(odd, close, far))
    near = jnp.concatenate(
        [
            jnp.concatenate([piece.astype(jnp.float32) for piece in first], axis=1),
            jnp.concatenate([piece.astype(jnp.float32) for piece in second], axis=1),
            jnp.zeros((LANES - wide, snps), jnp.float32),
        ],
        axis=0,
    )
    near_ref[...] = near.T


def column_stats(totals, count):
    size = jnp.maximum(count, 1.0)
    frequency = totals / size
    variance = jnp.maximum(frequency * (1.0 - frequency), VARIANCE_FLOOR)
    inverse = 1.0 / jnp.sqrt(size * variance)
    low = ((0.0 - frequency) * inverse).astype(jnp.bfloat16).astype(jnp.float32)
    high = ((1.0 - frequency) * inverse).astype(jnp.bfloat16).astype(jnp.float32)
    step = high - low
    root = 1.0 / jnp.sqrt(size)
    return step, step * totals * root, (low * count + step * totals) * root


def correlation(row, col, count):
    return row[0] * col[0] * count - row[1] * col[1] + row[2] * col[2]


def split(values):
    high = values.astype(jnp.bfloat16)
    return high, (values - high.astype(jnp.float32)).astype(jnp.bfloat16)


def dot_split(values, right, axis):
    dims = (((axis,), (0,)), ((), ()))
    return sum(
        lax.dot_general(part, right, dims, preferred_element_type=jnp.float32)
        for part in split(values)
    )


def score_kernel(groups, share, reach_ref, *refs):
    own_sum_ref, near_parts = refs[0], refs[1 : groups + 1]
    annot_ref, near_annot_ref = refs[groups + 1 : groups + 3]
    targets = refs[groups + 3 : 2 * groups + 3]
    table, annots, near_annots, scores = refs[2 * groups + 3 :]
    snps = annot_ref.shape[0]
    half = snps // 2
    out_share = snps // groups
    me = lax.axis_index("hap")
    block = lax.axis_index("snp")
    last = reach_ref.shape[0] - 1
    reach_here = reach_ref[block]
    reach_up = reach_ref[jnp.minimum(block + 1, last)]
    reach_down = reach_ref[jnp.maximum(block - 1, 0)]

    own_counts = own_sum_ref[...]
    near_sums = sum((part[...] for part in near_parts[1:]), near_parts[0][...])
    extras = from_fields(near_sums[share:, :])
    near_counts = near_sums[0:share, :]

    own_stats, near_stats, lines = [], [], []
    for pop in range(2):
        count = extras[pop][1:2, :]
        own_stats.append(column_stats(extras[pop][0:1, :], count))
        near_stats.append(column_stats(extras[pop][2:3, :], count))
        lines += [*own_stats[pop], *near_stats[pop], extras[pop][0:1, :], extras[pop][3:4, :]]
    by_row = jnp.concatenate(lines, axis=0).T
    table[0:snps, 0:16] = by_row
    if table.shape[0] > snps:
        table[snps:, 0:16] = jnp.zeros((table.shape[0] - snps, 16), jnp.float32)
    annots[0:snps, :] = annot_ref[...]
    near_annots[0:snps, :] = near_annot_ref[...]
    if annots.shape[0] > snps:
        annots[snps:, :] = jnp.zeros((annots.shape[0] - snps, LANES), jnp.float32)

    low_rows = pl.multiple_of(me * share, 8)
    high_rows = pl.multiple_of(half + me * share, 8)

    def both(ref):
        return jnp.concatenate([ref[pl.ds(low_rows, share), :], ref[pl.ds(high_rows, share), :]], axis=0)

    here = both(table)
    own_count = jnp.concatenate([pltpu.roll(own_counts, half, 1), own_counts], axis=0)
    near_count = jnp.concatenate([pltpu.roll(near_counts, half, 1), near_counts], axis=0)
    shape = (2 * share, snps)
    local, col = iota(shape, 0), iota(shape, 1)
    low = local < share
    place = jnp.where(low, local, local - share) + me * share
    row = jnp.where(low, place, place + half)
    own_fields, near_fields = from_fields(own_count), from_fields(near_count)
    own_product, near_product = 1.0, 1.0
    for pop in range(2):
        row_stats = [here[:, 8 * pop + k : 8 * pop + k + 1] for k in range(3)]
        own_product *= correlation(row_stats, own_stats[pop], own_fields[pop])
        near_product *= correlation(row_stats, near_stats[pop], near_fields[pop])
    real = place < half
    own_inside = real & ((low & (col > row)) | (~low & (col >= half) & (col < row)))
    own_inside &= jnp.abs(col - row) <= reach_here
    own_kept = jnp.where(own_inside, own_product, 0.0)
    in_upper = col < half
    near_inside = real & ((low & (col < row)) | (~low & (in_upper | (col > row))))
    distance = jnp.where(in_upper, snps + col - row, snps + row - col)
    near_here = jnp.where(near_inside & (distance <= reach_here), near_product, 0.0)
    reach_there = jnp.where(in_upper, reach_up, reach_down)
    near_there = jnp.where(near_inside & (distance <= reach_there), near_product, 0.0)

    rows_here = both(annots)
    rows_there = pltpu.roll(rows_here, HALF_LANES, 1)
    scores[0:snps, :] = dot_split(
        jnp.concatenate([own_kept, near_there], axis=0),
        jnp.concatenate([rows_here, rows_there], axis=0).astype(jnp.bfloat16),
        0,
    )
    direct = dot_split(
        jnp.concatenate([own_kept, near_here], axis=1),
        jnp.concatenate([annot_ref[...], near_annot_ref[...]], axis=0).astype(jnp.bfloat16),
        1,
    )
    scores[pl.ds(low_rows, share), :] += direct[0:share, :]
    scores[pl.ds(high_rows, share), :] += direct[share:, :]

    out_rows = pl.ds(pl.multiple_of(me * out_share, 8), out_share)
    mine = table[out_rows, :]
    self_product, far_product = 1.0, 1.0
    for pop in range(2):
        k = 8 * pop
        own_row = [mine[:, k + s : k + s + 1] for s in range(3)]
        near_row = [mine[:, k + 3 + s : k + 4 + s] for s in range(3)]
        self_product *= correlation(own_row, own_row, mine[:, k + 6 : k + 7])
        far_product *= correlation(own_row, near_row, mine[:, k + 7 : k + 8])
    mine_annots = annots[out_rows, :]
    far_reach = jnp.where(me < groups // 2, reach_up, reach_down)
    scores[out_rows, :] += (
        mine_annots * self_product
        + near_annots[out_rows, :] * jnp.where(reach_here >= snps, far_product, 0.0)
        + pltpu.roll(mine_annots, HALF_LANES, 1) * jnp.where(far_reach >= snps, far_product, 0.0)
    )
    send_shares(groups, scores, out_share, targets)


def sum_kernel(*refs):
    *parts, own_ref, there_ref = refs
    total = sum((part[...].astype(jnp.float32) for part in parts[1:]), parts[0][...])
    own_ref[...] = total
    half = there_ref.shape[0]
    left = iota((half, LANES), 1) < HALF_LANES
    second = total[half:]
    if second.shape[0] < half:
        second = jnp.concatenate([second, jnp.zeros((half - second.shape[0], LANES))], axis=0)
    there_ref[...] = jnp.where(left, pltpu.roll(total[0:half], HALF_LANES, 1), second)


def finish_kernel(own_ref, there_ref, out_ref):
    annots, rows = out_ref.shape
    there = there_ref[...]
    there = jnp.concatenate([there, pltpu.roll(there, HALF_LANES, 1)], axis=0)
    out_ref[...] = (own_ref[...] + there[0:rows]).T[0:annots, :]


def around(value, groups, step):
    return lax.ppermute(
        value, "hap", [(source, partner(source, step, groups)) for source in range(groups)]
    )


def swapped(value, first):
    pairs = []
    for block in range(first, lax.axis_size("snp") - 1, 2):
        pairs += [(block, block + 1), (block + 1, block)]
    return lax.ppermute(value, "snp", pairs)


def per_device(haplotypes, labels, annotations, reach):
    rows, snps = haplotypes.shape
    half = snps // 2
    groups = lax.axis_size("hap")
    blocks = lax.axis_size("snp")
    share = round_up(-(-half // groups), 16)
    folded_rows = share * groups
    out_share = snps // groups
    padded = half + folded_rows
    annot_part = 32
    bf16, f32, i32 = jnp.bfloat16, jnp.float32, jnp.int32
    shape = jax.ShapeDtypeStruct

    packed = shape((rows // 2 + annot_part, snps), bf16)
    haplotypes = pltpu.with_memory_space_constraint(haplotypes, pltpu.HBM)
    annots_in = pltpu.with_memory_space_constraint(annotations, pltpu.HBM)
    alleles, far, close = call(
        prepare_kernel,
        [shape((rows, snps), bf16), packed, packed],
        [HBM, HBM],
        [
            pltpu.VMEM((rows, snps), i32),
            pltpu.VMEM(annotations.shape, i32),
            pltpu.SemaphoreType.DMA((2 * CHUNKS + 1,)),
        ],
        moved=rows * snps * 8,
    )(haplotypes, annots_in)
    from_far = swapped(far, 1)
    from_close = swapped(close, 0)

    tile = pltpu.VMEM((snps + 16, snps), f32)
    folded = pltpu.VMEM((folded_rows, snps), i32)
    weighted, totals, *own_parts = call(
        functools.partial(own_kernel, groups, share),
        [shape((snps + 16, rows), bf16), shape((8, snps), f32)] + [shape((share, snps), i32)] * groups,
        [VMEM, VMEM],
        [tile, folded],
        flops=2 * rows * snps * snps,
        moved=rows * snps * 4,
    )(alleles, labels.reshape(1, rows))
    own_parts = [own_parts[0]] + [around(own_parts[k], groups, k) for k in range(groups - 1, 0, -1)]

    own_sum, *near_parts = call(
        functools.partial(near_kernel, groups, share),
        [shape((share, snps), i32)] + [shape((share + 8, snps), i32)] * groups,
        [VMEM] * (4 + groups),
        [pltpu.VMEM((rows, snps), bf16), tile, folded],
        flops=2 * rows * snps * snps,
        moved=rows * snps * 4,
    )(weighted, from_far, from_close, totals, *own_parts)
    near_parts = [near_parts[0]] + [around(near_parts[k], groups, k) for k in range(groups - 1, 0, -1)]

    by_snp = shape((snps, LANES), f32)
    own_annots, near_annots = call(annots_kernel, [by_snp, by_snp], [VMEM] * 3, moved=1 << 20)(
        annotations, from_far[rows // 2 :], from_close[rows // 2 :]
    )
    tall = pltpu.VMEM((padded, LANES), f32)
    scores = call(
        functools.partial(score_kernel, groups, share),
        [shape((out_share, LANES), f32)] + [shape((out_share, LANES), bf16)] * (groups - 1),
        [SMEM] + [VMEM] * (groups + 3),
        [tall, tall, tall, tall],
        flops=1 << 26,
        moved=1 << 21,
    )(reach, own_sum, *near_parts, own_annots, near_annots)
    scores = [scores[0]] + [around(scores[k], groups, k) for k in range(groups - 1, 0, -1)]
    half_share = round_up(-(-out_share // 2), 8)
    own_scores, near_scores = call(
        sum_kernel,
        [shape((out_share, LANES), f32), shape((half_share, LANES), f32)],
        [VMEM] * groups,
    )(*scores)
    pairs = []
    for block in range(blocks):
        for group in range(groups):
            target = block + 1 if group < groups // 2 else block - 1
            if 0 <= target < blocks:
                pairs.append((block * groups + group, target * groups + group))
    there = lax.ppermute(near_scores, ("snp", "hap"), pairs)
    return call(finish_kernel, shape((annotations.shape[0], out_share), f32), [VMEM] * 2)(own_scores, there)


def solution(mesh):
    in_specs = (
        P("hap", ("parts", "snp")),
        P(("parts", "hap")),
        P(None, ("parts", "snp")),
        P("parts"),
    )
    out_specs = P(None, ("parts", "snp", "hap"))
    return jax.shard_map(
        per_device, mesh=mesh, in_specs=in_specs, out_specs=out_specs, check_vma=False
    )
```

```python
import functools

import jax
import jax.numpy as jnp
from jax import lax
from jax.experimental import pallas as pl
from jax.experimental.pallas import tpu as pltpu
from jax.sharding import PartitionSpec as P

VARIANCE_FLOOR = 0.01
BASE_BITS = 12
BASE = 1 << BASE_BITS
FIELD_BITS = 16
LANES = 128
HALF_LANES = LANES // 2
CHUNKS = 4
VMEM = pl.BlockSpec(memory_space=pltpu.VMEM)
SMEM = pl.BlockSpec(memory_space=pltpu.SMEM)
HBM = pl.BlockSpec(memory_space=pltpu.HBM)
VMEM_LIMIT = 24 * 1024 * 1024


def iota(shape, axis):
    return lax.broadcasted_iota(jnp.int32, shape, axis)


def round_up(value, step):
    return -(-value // step) * step


def to_fields(values):
    whole = values.astype(jnp.int32)
    return whole + (whole >> BASE_BITS) * ((1 << FIELD_BITS) - BASE)


def from_fields(packed):
    first = packed & ((1 << FIELD_BITS) - 1)
    second = lax.shift_right_logical(packed, FIELD_BITS)
    return first.astype(jnp.float32), second.astype(jnp.float32)


def call(kernel, out_shape, in_specs, scratch_shapes=(), flops=0, moved=0):
    several = isinstance(out_shape, (list, tuple))
    return pl.pallas_call(
        kernel,
        out_shape=out_shape,
        in_specs=in_specs,
        out_specs=[VMEM] * len(out_shape) if several else VMEM,
        scratch_shapes=list(scratch_shapes),
        compiler_params=pltpu.CompilerParams(vmem_limit_bytes=VMEM_LIMIT),
        cost_estimate=pl.CostEstimate(flops=flops, bytes_accessed=moved, transcendentals=0),
    )


def odd_block():
    return lax.rem(lax.axis_index("snp"), 2) == 1


def store_packed(up_ref, down_ref, where, first, second):
    left = iota((first.shape[0], LANES), 1) < HALF_LANES
    middle = first[:, LANES : 2 * LANES]
    turned = pltpu.roll(second[:, LANES : 2 * LANES], HALF_LANES, 1)
    for ref, side, mixed in (
        (up_ref, slice(0, LANES), jnp.where(left, middle, turned)),
        (down_ref, slice(2 * LANES, 3 * LANES), jnp.where(left, turned, middle)),
    ):
        ref[where, 0:LANES] = first[:, side].astype(jnp.bfloat16)
        ref[where, LANES : 2 * LANES] = second[:, side].astype(jnp.bfloat16)
        ref[where, 2 * LANES : 3 * LANES] = mixed.astype(jnp.bfloat16)


def load_packed(up, down):
    left = iota((up.shape[0], LANES), 1) < HALF_LANES
    up_mixed, down_mixed = up[:, 2 * LANES :], down[:, 2 * LANES :]
    first = jnp.where(left, up_mixed, down_mixed)
    second = jnp.where(left, down_mixed, up_mixed)
    second = pltpu.roll(second.astype(jnp.float32), HALF_LANES, 1).astype(second.dtype)
    return (
        (up[:, :LANES], first, down[:, :LANES]),
        (up[:, LANES : 2 * LANES], second, down[:, LANES : 2 * LANES]),
    )


def prepare_kernel(hap_ref, annot_ref, alleles_ref, far_ref, close_ref, held, held_annots, sems):
    rows = hap_ref.shape[0]
    annot_rows = annot_ref.shape[0]
    size = rows // (2 * CHUNKS)
    starts = [side * (rows // 2) + chunk * size for chunk in range(CHUNKS) for side in range(2)]
    copies = [
        pltpu.make_async_copy(
            hap_ref.at[pl.ds(start, size)], held.at[pl.ds(start, size)], sems.at[number]
        )
        for number, start in enumerate(starts)
    ]
    copies.append(pltpu.make_async_copy(annot_ref, held_annots, sems.at[2 * CHUNKS]))
    for copy in copies:
        copy.start()
    part = far_ref.shape[0] - rows // 2
    odd = odd_block()

    def store(where, first, second):
        @pl.when(odd)
        def _():
            store_packed(close_ref, far_ref, where, first, second)

        @pl.when(jnp.logical_not(odd))
        def _():
            store_packed(far_ref, close_ref, where, first, second)

    for chunk in range(CHUNKS):
        pair = []
        for side in range(2):
            number = 2 * chunk + side
            copies[number].wait()
            where = slice(starts[number], starts[number] + size)
            values = held[where, :].astype(jnp.float32)
            alleles_ref[where, :] = values.astype(jnp.bfloat16)
            pair.append(values)
        store(slice(chunk * size, (chunk + 1) * size), *pair)
    copies[-1].wait()
    annots = jnp.concatenate(
        [
            held_annots[...].astype(jnp.float32),
            jnp.zeros((2 * part - annot_rows, annot_ref.shape[1]), jnp.float32),
        ],
        axis=0,
    )
    store(slice(rows // 2, rows // 2 + part), annots[:part], annots[part:])


def partner(group, step, groups):
    if groups & (groups - 1) == 0:
        return group ^ step
    return (group + step) % groups


def send_shares(groups, source, share, targets):
    me = lax.axis_index("hap")
    for step, target in enumerate(targets):
        group = partner(me, step, groups)
        rows = source[pl.ds(pl.multiple_of(group * share, 8), share), :]
        target[0:share, :] = rows.astype(target.dtype)


def own_kernel(groups, share, alleles_ref, label_ref, *refs):
    weighted_ref, totals_ref, *targets = refs[: 2 + groups]
    tile, folded = refs[2 + groups :]
    rows, snps = alleles_ref.shape
    half = snps // 2
    weight = jnp.where(label_ref[...] > 0, float(BASE), 1.0)
    weighted_ref[0:snps, :] = alleles_ref[...].T * weight.astype(jnp.bfloat16)
    extra = weighted_ref.shape[0] - snps
    weighted_ref[snps:, :] = jnp.broadcast_to(weight, (extra, rows)).astype(jnp.bfloat16)
    tile[...] = jnp.dot(weighted_ref[...], alleles_ref[...], preferred_element_type=jnp.float32)
    count = jnp.sum(weight, axis=1, keepdims=True)
    totals_ref[...] = jnp.concatenate(
        [tile[snps : snps + 1, :], jnp.broadcast_to(count, (1, snps)), jnp.zeros((6, snps))], axis=0
    )
    row, col = iota((half, snps), 0), iota((half, snps), 1)
    moved = (col < half) | (col - half > row)
    turned = pltpu.roll(tile[0:half, :], half, 1)
    folded[0:half, :] = to_fields(jnp.where(moved, turned, tile[half:snps, :]))
    if folded.shape[0] > half:
        folded[half:, :] = jnp.zeros((folded.shape[0] - half, snps), jnp.int32)
    send_shares(groups, folded, share, targets)


LEFT_BLOCKS = ((0, 1, 2, 3), (2, 3, 6, 7), (4, 0, 1, 2), (6, 0, 4, 5))
RIGHT_BLOCKS = ((2, 3, 6, 7), (4, 5, 6, 7), (0, 1, 2, 4), (0, 4, 5, 6))


def fold_by_column(tile, flipped, folded):
    owners = len(LEFT_BLOCKS)
    snps = folded.shape[1]
    wide = snps // owners
    size = wide // 2
    shape = (size, snps)
    row, lane = iota(shape, 0), iota(shape, 1)

    def block(number):
        return tile[number * size : (number + 1) * size, :]

    diagonal = block(0)
    for number in range(1, 2 * owners):
        diagonal = jnp.where(lane >= number * size, block(number), diagonal)
    flipped[:, 0:size] = diagonal.T
    corner = diagonal
    for owner in range(owners):
        start = (2 * owner + 1) * size
        turned = jnp.concatenate(
            [flipped[start : start + size, :], jnp.zeros((size, snps - LANES), jnp.float32)], axis=1
        )
        if owner:
            turned = pltpu.roll(turned, owner * wide, 1)
        inside = lane - owner * wide
        other = (row <= inside) if owner < owners // 2 else (row >= inside)
        corner = jnp.where((inside >= 0) & (inside < size) & other, turned, corner)
    rolled = []
    for shift in range(owners):
        mixed = None
        for owner in range(owners):
            slot = (owner + shift) % owners
            left = block(LEFT_BLOCKS[owner][slot]) if slot else corner
            start = owner * wide
            mixed = left if mixed is None else jnp.where(lane >= start, left, mixed)
            mixed = jnp.where(lane >= start + size, block(RIGHT_BLOCKS[owner][slot]), mixed)
        rolled.append(pltpu.roll(mixed, shift * wide, 1) if shift else mixed)
    for owner in range(owners):
        mixed = rolled[(0 - owner) % owners]
        for slot in range(1, owners):
            mixed = jnp.where(lane >= slot * wide, rolled[(slot - owner) % owners], mixed)
        folded[owner * size : (owner + 1) * size, :] = to_fields(mixed)


def near_kernel(groups, share, weighted_ref, far_ref, close_ref, totals_ref, *refs):
    own_parts, own_sum_ref = refs[:groups], refs[groups]
    targets, (near, tile, folded, flipped) = refs[groups + 1 : 2 * groups + 1], refs[2 * groups + 1 :]
    rows, snps = near.shape
    half = snps // 2
    odd = odd_block()

    def unpack(up_ref, down_ref):
        pieces = load_packed(up_ref[0 : rows // 2, :], down_ref[0 : rows // 2, :])
        for side in range(2):
            where = slice(side * (rows // 2), (side + 1) * (rows // 2))
            for number in range(3):
                near[where, number * LANES : (number + 1) * LANES] = pieces[side][number]

    @pl.when(odd)
    def _():
        unpack(far_ref, close_ref)

    @pl.when(jnp.logical_not(odd))
    def _():
        unpack(close_ref, far_ref)

    tile[...] = jnp.dot(weighted_ref[...], near[...], preferred_element_type=jnp.float32)
    if groups == len(LEFT_BLOCKS):
        fold_by_column(tile, flipped, folded)
    else:
        row, col = iota((half, snps), 0), iota((half, snps), 1)
        moved = (col >= half) & (col - half < row)
        turned = pltpu.roll(tile[0:half, :], half, 1)
        folded[0:half, :] = to_fields(jnp.where(moved, turned, tile[half:snps, :]))
        if folded.shape[0] > half:
            folded[half:, :] = jnp.zeros((folded.shape[0] - half, snps), jnp.int32)
    square = (snps, snps)
    far = jnp.sum(
        jnp.where(iota(square, 0) == iota(square, 1), tile[0:snps, :], 0.0), axis=0, keepdims=True
    )
    extras = to_fields(
        jnp.concatenate(
            [totals_ref[0:2, :], tile[snps : snps + 1, :], far, jnp.zeros((4, snps))], axis=0
        )
    )
    send_shares(groups, folded, share, targets)
    for target in targets:
        target[share:, :] = extras
    own_sum_ref[...] = sum((part[...] for part in own_parts[1:]), own_parts[0][...])


def annots_kernel(annot_ref, far_ref, close_ref, own_ref, near_ref):
    snps = annot_ref.shape[1]
    part = far_ref.shape[0]
    wide = 2 * part
    own = annot_ref[...].astype(jnp.float32)
    own = jnp.concatenate([own, jnp.zeros((LANES - own.shape[0], snps), jnp.float32)], axis=0)
    own_ref[...] = own.T
    odd = odd_block()
    far, close = far_ref[...].astype(jnp.float32), close_ref[...].astype(jnp.float32)
    first, second = load_packed(jnp.where(odd, far, close), jnp.where(odd, close, far))
    near = jnp.concatenate(
        [
            jnp.concatenate([piece.astype(jnp.float32) for piece in first], axis=1),
            jnp.concatenate([piece.astype(jnp.float32) for piece in second], axis=1),
            jnp.zeros((LANES - wide, snps), jnp.float32),
        ],
        axis=0,
    )
    near_ref[...] = near.T


def column_stats(totals, count):
    size = jnp.maximum(count, 1.0)
    frequency = totals / size
    variance = jnp.maximum(frequency * (1.0 - frequency), VARIANCE_FLOOR)
    inverse = 1.0 / jnp.sqrt(size * variance)
    low = ((0.0 - frequency) * inverse).astype(jnp.bfloat16).astype(jnp.float32)
    high = ((1.0 - frequency) * inverse).astype(jnp.bfloat16).astype(jnp.float32)
    step = high - low
    root = 1.0 / jnp.sqrt(size)
    return step, step * totals * root, (low * count + step * totals) * root


def correlation(row, col, count):
    return row[0] * col[0] * count - row[1] * col[1] + row[2] * col[2]


def split(values):
    high = values.astype(jnp.bfloat16)
    return high, (values - high.astype(jnp.float32)).astype(jnp.bfloat16)


def dot_split(values, right, axis):
    dims = (((axis,), (0,)), ((), ()))
    return sum(
        lax.dot_general(part, right, dims, preferred_element_type=jnp.float32)
        for part in split(values)
    )


def score_kernel(groups, share, reach_ref, *refs):
    own_sum_ref, near_parts = refs[0], refs[1 : groups + 1]
    annot_ref, near_annot_ref = refs[groups + 1 : groups + 3]
    targets = refs[groups + 3 : 2 * groups + 3]
    table, annots, near_annots, scores = refs[2 * groups + 3 :]
    snps = annot_ref.shape[0]
    half = snps // 2
    out_share = snps // groups
    me = lax.axis_index("hap")
    block = lax.axis_index("snp")
    last = reach_ref.shape[0] - 1
    reach_here = reach_ref[block]
    reach_up = reach_ref[jnp.minimum(block + 1, last)]
    reach_down = reach_ref[jnp.maximum(block - 1, 0)]

    own_counts = own_sum_ref[...]
    near_sums = sum((part[...] for part in near_parts[1:]), near_parts[0][...])
    extras = from_fields(near_sums[share:, :])
    near_counts = near_sums[0:share, :]

    own_stats, near_stats, lines = [], [], []
    for pop in range(2):
        count = extras[pop][1:2, :]
        own_stats.append(column_stats(extras[pop][0:1, :], count))
        near_stats.append(column_stats(extras[pop][2:3, :], count))
        lines += [*own_stats[pop], *near_stats[pop], extras[pop][0:1, :], extras[pop][3:4, :]]
    by_row = jnp.concatenate(lines, axis=0).T
    table[0:snps, 0:16] = by_row
    if table.shape[0] > snps:
        table[snps:, 0:16] = jnp.zeros((table.shape[0] - snps, 16), jnp.float32)
    annots[0:snps, :] = annot_ref[...]
    near_annots[0:snps, :] = near_annot_ref[...]
    if annots.shape[0] > snps:
        annots[snps:, :] = jnp.zeros((annots.shape[0] - snps, LANES), jnp.float32)

    low_rows = pl.multiple_of(me * share, 8)
    high_rows = pl.multiple_of(half + me * share, 8)

    def both(ref):
        return jnp.concatenate([ref[pl.ds(low_rows, share), :], ref[pl.ds(high_rows, share), :]], axis=0)

    here = both(table)
    own_count = jnp.concatenate([pltpu.roll(own_counts, half, 1), own_counts], axis=0)
    near_count = jnp.concatenate([pltpu.roll(near_counts, half, 1), near_counts], axis=0)
    shape = (2 * share, snps)
    local, col = iota(shape, 0), iota(shape, 1)
    low = local < share
    place = jnp.where(low, local, local - share) + me * share
    row = jnp.where(low, place, place + half)
    own_fields, near_fields = from_fields(own_count), from_fields(near_count)
    own_product, near_product = 1.0, 1.0
    for pop in range(2):
        row_stats = [here[:, 8 * pop + k : 8 * pop + k + 1] for k in range(3)]
        own_product *= correlation(row_stats, own_stats[pop], own_fields[pop])
        near_product *= correlation(row_stats, near_stats[pop], near_fields[pop])
    real = place < half
    own_inside = real & ((low & (col > row)) | (~low & (col >= half) & (col < row)))
    own_inside &= jnp.abs(col - row) <= reach_here
    own_kept = jnp.where(own_inside, own_product, 0.0)
    in_upper = col < half
    near_inside = real & ((low & (col < row)) | (~low & (in_upper | (col > row))))
    distance = jnp.where(in_upper, snps + col - row, snps + row - col)
    near_here = jnp.where(near_inside & (distance <= reach_here), near_product, 0.0)
    reach_there = jnp.where(in_upper, reach_up, reach_down)
    near_there = jnp.where(near_inside & (distance <= reach_there), near_product, 0.0)

    rows_here = both(annots)
    rows_there = pltpu.roll(rows_here, HALF_LANES, 1)
    scores[0:snps, :] = dot_split(
        jnp.concatenate([own_kept, near_there], axis=0),
        jnp.concatenate([rows_here, rows_there], axis=0).astype(jnp.bfloat16),
        0,
    )
    direct = dot_split(
        jnp.concatenate([own_kept, near_here], axis=1),
        jnp.concatenate([annot_ref[...], near_annot_ref[...]], axis=0).astype(jnp.bfloat16),
        1,
    )
    scores[pl.ds(low_rows, share), :] += direct[0:share, :]
    scores[pl.ds(high_rows, share), :] += direct[share:, :]

    out_rows = pl.ds(pl.multiple_of(me * out_share, 8), out_share)
    mine = table[out_rows, :]
    self_product, far_product = 1.0, 1.0
    for pop in range(2):
        k = 8 * pop
        own_row = [mine[:, k + s : k + s + 1] for s in range(3)]
        near_row = [mine[:, k + 3 + s : k + 4 + s] for s in range(3)]
        self_product *= correlation(own_row, own_row, mine[:, k + 6 : k + 7])
        far_product *= correlation(own_row, near_row, mine[:, k + 7 : k + 8])
    mine_annots = annots[out_rows, :]
    far_reach = jnp.where(me < groups // 2, reach_up, reach_down)
    scores[out_rows, :] += (
        mine_annots * self_product
        + near_annots[out_rows, :] * jnp.where(reach_here >= snps, far_product, 0.0)
        + pltpu.roll(mine_annots, HALF_LANES, 1) * jnp.where(far_reach >= snps, far_product, 0.0)
    )
    send_shares(groups, scores, out_share, targets)


def pack_halves(values):
    half = values.shape[0] // 2
    left = iota((half, LANES), 1) < HALF_LANES
    return jnp.where(left, values[0:half], pltpu.roll(values[half:], HALF_LANES, 1))


def unpack_halves(packed):
    return jnp.concatenate([packed, pltpu.roll(packed, HALF_LANES, 1)], axis=0)


def column_score_kernel(groups, share, reach_ref, *refs):
    own_sum_ref, near_parts = refs[0], refs[1 : groups + 1]
    annot_ref, near_annot_ref = refs[groups + 1 : groups + 3]
    out_ref, *targets = refs[groups + 3 : 2 * groups + 3]
    near_out_ref, table, flipped, scores = refs[2 * groups + 3 :]
    snps = annot_ref.shape[0]
    half = snps // 2
    wide = snps // groups
    size = wide // 2
    me = lax.axis_index("hap")
    block = lax.axis_index("snp")
    last = reach_ref.shape[0] - 1
    upper = me < groups // 2
    reach_here = reach_ref[block]
    reach_there = jnp.where(
        upper, reach_ref[jnp.minimum(block + 1, last)], reach_ref[jnp.maximum(block - 1, 0)]
    )

    def mine(choices):
        value = choices[0]
        for group in range(1, groups):
            value = jnp.where(me == group, choices[group], value)
        return value

    own_counts = own_sum_ref[...]
    near_sums = sum((part[...] for part in near_parts[1:]), near_parts[0][...])
    extras = from_fields(near_sums[share:, :])
    near_counts = near_sums[0:share, :]

    own_stats, near_stats, lines = [], [], []
    for pop in range(2):
        count = extras[pop][1:2, :]
        own_stats.append(column_stats(extras[pop][0:1, :], count))
        near_stats.append(column_stats(extras[pop][2:3, :], count))
        lines += [*own_stats[pop], *near_stats[pop], extras[pop][0:1, :], extras[pop][3:4, :]]
    table[:, 0:16] = jnp.concatenate(lines, axis=0).T

    low_rows = pl.multiple_of(me * share, 8)
    high_rows = pl.multiple_of(half + me * share, 8)

    def both(ref):
        return jnp.concatenate([ref[pl.ds(low_rows, share), :], ref[pl.ds(high_rows, share), :]], axis=0)

    here = both(table)
    own_fields = from_fields(
        jnp.concatenate([pltpu.roll(own_counts, half, 1), own_counts], axis=0)
    )
    shape = (2 * share, snps)
    local, col = iota(shape, 0), iota(shape, 1)
    low = local < share
    row = jnp.where(low, local, local + half - share) + me * share
    product = 1.0
    for pop in range(2):
        row_stats = [here[:, 8 * pop + k : 8 * pop + k + 1] for k in range(3)]
        product *= correlation(row_stats, own_stats[pop], own_fields[pop])
    inside = (low & (col > row)) | (~low & (col >= half) & (col < row))
    own_kept = jnp.where(inside & (jnp.abs(col - row) <= reach_here), product, 0.0)
    rows_here = both(annot_ref).astype(jnp.bfloat16)
    scores[...] = dot_split(own_kept, rows_here, 0)
    direct = dot_split(own_kept, annot_ref[...].astype(jnp.bfloat16), 1)
    scores[pl.ds(low_rows, share), :] += direct[0:share, :]
    scores[pl.ds(high_rows, share), :] += direct[share:, :]

    slots = [near_counts[:, 0:LANES]]
    for slot in range(1, groups):
        slots.append(pltpu.roll(near_counts, snps - slot * wide, 1)[:, 0:LANES])
    flipped[:, 0:size] = slots[0].T
    slots.append(pltpu.roll(flipped[0:size, :], size, 1))
    left_places = [mine([LEFT_BLOCKS[g][slot] for g in range(groups)]) * size for slot in range(groups)]
    right_places = [mine([RIGHT_BLOCKS[g][slot] for g in range(groups)]) * size for slot in range(groups)]
    left_places.append(left_places[0])
    right_places.append((2 * me + 1) * size)

    def rows_of(ref, places):
        return [ref[pl.ds(pl.multiple_of(place, 8), size), :] for place in places]

    near_fields = from_fields(jnp.concatenate(slots, axis=0))
    left_table = jnp.concatenate(rows_of(table, left_places), axis=0)
    right_table = jnp.concatenate(rows_of(table, right_places), axis=0)
    local, lane = iota((size, LANES), 0), iota((size, LANES), 1)
    is_left = lane < size
    own_row = jnp.concatenate(
        [local + jnp.where(is_left, a, b) for a, b in zip(left_places, right_places)], axis=0
    )
    shape = own_row.shape
    lane = iota(shape, 1)
    is_left = lane < size
    apart = jnp.abs(own_row - (lane + me * wide))
    ahead = (own_row - (lane + me * wide)) * jnp.where(upper, 1, -1) > 0
    real = ahead & (lane < wide) & ((lane >= size) | (iota(shape, 0) < groups * size))
    near_lines = jnp.concatenate([*near_stats[0], *near_stats[1], *near_stats[0][0:2]], axis=0)
    near_lines = mine(
        [near_lines[:, 0:LANES]]
        + [pltpu.roll(near_lines, snps - group * wide, 1)[:, 0:LANES] for group in range(1, groups)]
    )
    product = 1.0
    for pop in range(2):
        row_stats = [
            jnp.where(
                is_left,
                left_table[:, 8 * pop + k : 8 * pop + k + 1],
                right_table[:, 8 * pop + k : 8 * pop + k + 1],
            )
            for k in range(3)
        ]
        col_stats = [near_lines[3 * pop + k : 3 * pop + k + 1, :] for k in range(3)]
        product *= correlation(row_stats, col_stats, near_fields[pop])
    near_here = jnp.where(real & (snps - apart <= reach_here), product, 0.0)
    near_there = jnp.where(real & (snps - apart <= reach_there), product, 0.0)

    def sides(values):
        return jnp.concatenate(
            [jnp.where(is_left, values, 0.0), jnp.where(is_left, 0.0, values)], axis=0
        )

    slice_rows = pl.ds(pl.multiple_of(me * wide, 8), wide)
    their_annots = near_annot_ref[slice_rows, :]
    columns = jnp.concatenate([their_annots, jnp.zeros((LANES - wide, LANES), jnp.float32)], axis=0)
    direct = dot_split(sides(near_here), columns.astype(jnp.bfloat16), 1)
    places = left_places + right_places
    for number, place in enumerate(places):
        scores[pl.ds(pl.multiple_of(place, 8), size), :] += direct[number * size : (number + 1) * size, :]
    own_rows = jnp.concatenate(rows_of(annot_ref, places), axis=0).astype(jnp.bfloat16)
    near_scores = dot_split(sides(near_there), own_rows, 0)[0:wide, :]

    mine_table = table[slice_rows, :]
    self_product, far_product = 1.0, 1.0
    for pop in range(2):
        k = 8 * pop
        own_row = [mine_table[:, k + s : k + s + 1] for s in range(3)]
        near_row = [mine_table[:, k + 3 + s : k + 4 + s] for s in range(3)]
        self_product *= correlation(own_row, own_row, mine_table[:, k + 6 : k + 7])
        far_product *= correlation(own_row, near_row, mine_table[:, k + 7 : k + 8])
    my_annots = annot_ref[slice_rows, :]
    out_ref[...] = (
        scores[slice_rows, :]
        + my_annots * self_product
        + their_annots * jnp.where(reach_here >= snps, far_product, 0.0)
    )
    near_scores += my_annots * jnp.where(reach_there >= snps, far_product, 0.0)
    near_out_ref[...] = pack_halves(near_scores)
    for step, target in enumerate(targets, 1):
        group = partner(me, step, groups)
        rows = scores[pl.ds(pl.multiple_of(group * wide, 8), wide), :]
        target[...] = pack_halves(rows).astype(target.dtype)


def column_finish_kernel(own_ref, there_ref, *refs):
    *parts, out_ref = refs
    packed = sum((part[...].astype(jnp.float32) for part in parts), there_ref[...])
    out_ref[...] = (own_ref[...] + unpack_halves(packed)).T[0 : out_ref.shape[0], :]


def sum_kernel(*refs):
    *parts, own_ref, there_ref = refs
    total = sum((part[...].astype(jnp.float32) for part in parts[1:]), parts[0][...])
    own_ref[...] = total
    half = there_ref.shape[0]
    left = iota((half, LANES), 1) < HALF_LANES
    second = total[half:]
    if second.shape[0] < half:
        second = jnp.concatenate([second, jnp.zeros((half - second.shape[0], LANES))], axis=0)
    there_ref[...] = jnp.where(left, pltpu.roll(total[0:half], HALF_LANES, 1), second)


def finish_kernel(own_ref, there_ref, out_ref):
    annots, rows = out_ref.shape
    there = there_ref[...]
    there = jnp.concatenate([there, pltpu.roll(there, HALF_LANES, 1)], axis=0)
    out_ref[...] = (own_ref[...] + there[0:rows]).T[0:annots, :]


def around(value, groups, step):
    return lax.ppermute(
        value, "hap", [(source, partner(source, step, groups)) for source in range(groups)]
    )


def swapped(value, first):
    pairs = []
    for block in range(first, lax.axis_size("snp") - 1, 2):
        pairs += [(block, block + 1), (block + 1, block)]
    return lax.ppermute(value, "snp", pairs)


def per_device(haplotypes, labels, annotations, reach):
    rows, snps = haplotypes.shape
    half = snps // 2
    groups = lax.axis_size("hap")
    blocks = lax.axis_size("snp")
    share = round_up(-(-half // groups), 16)
    folded_rows = share * groups
    out_share = snps // groups
    padded = half + folded_rows
    annot_part = 32
    bf16, f32, i32 = jnp.bfloat16, jnp.float32, jnp.int32
    shape = jax.ShapeDtypeStruct

    packed = shape((rows // 2 + annot_part, snps), bf16)
    haplotypes = pltpu.with_memory_space_constraint(haplotypes, pltpu.HBM)
    annots_in = pltpu.with_memory_space_constraint(annotations, pltpu.HBM)
    alleles, far, close = call(
        prepare_kernel,
        [shape((rows, snps), bf16), packed, packed],
        [HBM, HBM],
        [
            pltpu.VMEM((rows, snps), i32),
            pltpu.VMEM(annotations.shape, i32),
            pltpu.SemaphoreType.DMA((2 * CHUNKS + 1,)),
        ],
        moved=rows * snps * 8,
    )(haplotypes, annots_in)
    from_far = swapped(far, 1)
    from_close = swapped(close, 0)

    tile = pltpu.VMEM((snps + 16, snps), f32)
    folded = pltpu.VMEM((folded_rows, snps), i32)
    weighted, totals, *own_parts = call(
        functools.partial(own_kernel, groups, share),
        [shape((snps + 16, rows), bf16), shape((8, snps), f32)] + [shape((share, snps), i32)] * groups,
        [VMEM, VMEM],
        [tile, folded],
        flops=2 * rows * snps * snps,
        moved=rows * snps * 4,
    )(alleles, labels.reshape(1, rows))
    own_parts = [own_parts[0]] + [around(own_parts[k], groups, k) for k in range(groups - 1, 0, -1)]

    own_sum, *near_parts = call(
        functools.partial(near_kernel, groups, share),
        [shape((share, snps), i32)] + [shape((share + 8, snps), i32)] * groups,
        [VMEM] * (4 + groups),
        [pltpu.VMEM((rows, snps), bf16), tile, folded, pltpu.VMEM((snps, LANES), f32)],
        flops=2 * rows * snps * snps,
        moved=rows * snps * 4,
    )(weighted, from_far, from_close, totals, *own_parts)
    near_parts = [near_parts[0]] + [around(near_parts[k], groups, k) for k in range(groups - 1, 0, -1)]

    by_snp = shape((snps, LANES), f32)
    own_annots, near_annots = call(annots_kernel, [by_snp, by_snp], [VMEM] * 3, moved=1 << 20)(
        annotations, from_far[rows // 2 :], from_close[rows // 2 :]
    )
    pairs = []
    for block in range(blocks):
        for group in range(groups):
            target = block + 1 if group < groups // 2 else block - 1
            if 0 <= target < blocks:
                pairs.append((block * groups + group, target * groups + group))

    def to_neighbour(value):
        return lax.ppermute(value, ("snp", "hap"), pairs)

    result = shape((annotations.shape[0], out_share), f32)
    half_share = round_up(-(-out_share // 2), 8)
    own_share = shape((out_share, LANES), f32)
    packed_share = shape((half_share, LANES), f32)
    if groups == len(LEFT_BLOCKS):
        own_scores, *scores, near_scores = call(
            functools.partial(column_score_kernel, groups, share),
            [own_share] + [shape((half_share, LANES), bf16)] * (groups - 1) + [packed_share],
            [SMEM] + [VMEM] * (groups + 3),
            [pltpu.VMEM((snps, LANES), f32), pltpu.VMEM((LANES, LANES), i32), pltpu.VMEM((snps, LANES), f32)],
            flops=1 << 26,
            moved=1 << 21,
        )(reach, own_sum, *near_parts, own_annots, near_annots)
        scores = [around(scores[k - 1], groups, k) for k in range(groups - 1, 0, -1)]
        there = to_neighbour(near_scores)
        return call(column_finish_kernel, result, [VMEM] * (groups + 1))(own_scores, there, *scores)

    tall = pltpu.VMEM((padded, LANES), f32)
    scores = call(
        functools.partial(score_kernel, groups, share),
        [own_share] + [shape((out_share, LANES), bf16)] * (groups - 1),
        [SMEM] + [VMEM] * (groups + 3),
        [tall, tall, tall, tall],
        flops=1 << 26,
        moved=1 << 21,
    )(reach, own_sum, *near_parts, own_annots, near_annots)
    scores = [scores[0]] + [around(scores[k], groups, k) for k in range(groups - 1, 0, -1)]
    own_scores, near_scores = call(sum_kernel, [own_share, packed_share], [VMEM] * groups)(*scores)
    return call(finish_kernel, result, [VMEM] * 2)(own_scores, to_neighbour(near_scores))


def solution(mesh):
    in_specs = (
        P("hap", ("parts", "snp")),
        P(("parts", "hap")),
        P(None, ("parts", "snp")),
        P("parts"),
    )
    out_specs = P(None, ("parts", "snp", "hap"))
    return jax.shard_map(
        per_device, mesh=mesh, in_specs=in_specs, out_specs=out_specs, check_vma=False
    )
```

```python
import functools

import jax
import jax.numpy as jnp
from jax import lax
from jax.experimental import pallas as pl
from jax.experimental.pallas import tpu as pltpu
from jax.sharding import PartitionSpec as P

VARIANCE_FLOOR = 0.01
BASE_BITS = 12
BASE = 1 << BASE_BITS
FIELD_BITS = 16
LANES = 128
HALF_LANES = LANES // 2
CHUNKS = 4
VMEM = pl.BlockSpec(memory_space=pltpu.VMEM)
SMEM = pl.BlockSpec(memory_space=pltpu.SMEM)
HBM = pl.BlockSpec(memory_space=pltpu.HBM)
VMEM_LIMIT = 24 * 1024 * 1024


def iota(shape, axis):
    return lax.broadcasted_iota(jnp.int32, shape, axis)


def round_up(value, step):
    return -(-value // step) * step


def to_fields(values):
    whole = values.astype(jnp.int32)
    return whole + (whole >> BASE_BITS) * ((1 << FIELD_BITS) - BASE)


def from_fields(packed):
    first = packed & ((1 << FIELD_BITS) - 1)
    second = lax.shift_right_logical(packed, FIELD_BITS)
    return first.astype(jnp.float32), second.astype(jnp.float32)


def call(kernel, out_shape, in_specs, scratch_shapes=(), flops=0, moved=0):
    several = isinstance(out_shape, (list, tuple))
    return pl.pallas_call(
        kernel,
        out_shape=out_shape,
        in_specs=in_specs,
        out_specs=[VMEM] * len(out_shape) if several else VMEM,
        scratch_shapes=list(scratch_shapes),
        compiler_params=pltpu.CompilerParams(vmem_limit_bytes=VMEM_LIMIT),
        cost_estimate=pl.CostEstimate(flops=flops, bytes_accessed=moved, transcendentals=0),
    )


def odd_block():
    return lax.rem(lax.axis_index("snp"), 2) == 1


def store_packed(up_ref, down_ref, where, first, second):
    left = iota((first.shape[0], LANES), 1) < HALF_LANES
    middle = first[:, LANES : 2 * LANES]
    turned = pltpu.roll(second[:, LANES : 2 * LANES], HALF_LANES, 1)
    for ref, side, mixed in (
        (up_ref, slice(0, LANES), jnp.where(left, middle, turned)),
        (down_ref, slice(2 * LANES, 3 * LANES), jnp.where(left, turned, middle)),
    ):
        ref[where, 0:LANES] = first[:, side].astype(jnp.bfloat16)
        ref[where, LANES : 2 * LANES] = second[:, side].astype(jnp.bfloat16)
        ref[where, 2 * LANES : 3 * LANES] = mixed.astype(jnp.bfloat16)


def load_packed(up, down):
    left = iota((up.shape[0], LANES), 1) < HALF_LANES
    up_mixed, down_mixed = up[:, 2 * LANES :], down[:, 2 * LANES :]
    first = jnp.where(left, up_mixed, down_mixed)
    second = jnp.where(left, down_mixed, up_mixed)
    second = pltpu.roll(second.astype(jnp.float32), HALF_LANES, 1).astype(second.dtype)
    return (
        (up[:, :LANES], first, down[:, :LANES]),
        (up[:, LANES : 2 * LANES], second, down[:, LANES : 2 * LANES]),
    )


def prepare_kernel(hap_ref, annot_ref, alleles_ref, far_ref, close_ref, held, held_annots, sems):
    rows = hap_ref.shape[0]
    annot_rows = annot_ref.shape[0]
    size = rows // (2 * CHUNKS)
    starts = [side * (rows // 2) + chunk * size for chunk in range(CHUNKS) for side in range(2)]
    copies = [
        pltpu.make_async_copy(
            hap_ref.at[pl.ds(start, size)], held.at[pl.ds(start, size)], sems.at[number]
        )
        for number, start in enumerate(starts)
    ]
    copies.append(pltpu.make_async_copy(annot_ref, held_annots, sems.at[2 * CHUNKS]))
    for copy in copies:
        copy.start()
    part = far_ref.shape[0] - rows // 2
    odd = odd_block()

    def store(where, first, second):
        @pl.when(odd)
        def _():
            store_packed(close_ref, far_ref, where, first, second)

        @pl.when(jnp.logical_not(odd))
        def _():
            store_packed(far_ref, close_ref, where, first, second)

    for chunk in range(CHUNKS):
        pair = []
        for side in range(2):
            number = 2 * chunk + side
            copies[number].wait()
            where = slice(starts[number], starts[number] + size)
            values = held[where, :].astype(jnp.float32)
            alleles_ref[where, :] = values.astype(jnp.bfloat16)
            pair.append(values)
        store(slice(chunk * size, (chunk + 1) * size), *pair)
    copies[-1].wait()
    annots = jnp.concatenate(
        [
            held_annots[...].astype(jnp.float32),
            jnp.zeros((2 * part - annot_rows, annot_ref.shape[1]), jnp.float32),
        ],
        axis=0,
    )
    store(slice(rows // 2, rows // 2 + part), annots[:part], annots[part:])


def partner(group, step, groups):
    if groups & (groups - 1) == 0:
        return group ^ step
    return (group + step) % groups


def send_shares(groups, source, share, targets):
    me = lax.axis_index("hap")
    for step, target in enumerate(targets):
        group = partner(me, step, groups)
        rows = source[pl.ds(pl.multiple_of(group * share, 8), share), :]
        target[0:share, :] = rows.astype(target.dtype)


def own_kernel(groups, share, alleles_ref, label_ref, *refs):
    weighted_ref, totals_ref, *targets = refs[: 2 + groups]
    tile, folded = refs[2 + groups :]
    rows, snps = alleles_ref.shape
    half = snps // 2
    weight = jnp.where(label_ref[...] > 0, float(BASE), 1.0)
    weighted_ref[0:snps, :] = alleles_ref[...].T * weight.astype(jnp.bfloat16)
    extra = weighted_ref.shape[0] - snps
    weighted_ref[snps:, :] = jnp.broadcast_to(weight, (extra, rows)).astype(jnp.bfloat16)
    tile[...] = jnp.dot(weighted_ref[...], alleles_ref[...], preferred_element_type=jnp.float32)
    count = jnp.sum(weight, axis=1, keepdims=True)
    totals_ref[...] = jnp.concatenate(
        [tile[snps : snps + 1, :], jnp.broadcast_to(count, (1, snps)), jnp.zeros((6, snps))], axis=0
    )
    row, col = iota((half, snps), 0), iota((half, snps), 1)
    moved = (col < half) | (col - half > row)
    turned = pltpu.roll(tile[0:half, :], half, 1)
    folded[0:half, :] = to_fields(jnp.where(moved, turned, tile[half:snps, :]))
    if folded.shape[0] > half:
        folded[half:, :] = jnp.zeros((folded.shape[0] - half, snps), jnp.int32)
    send_shares(groups, folded, share, targets)


LEFT_BLOCKS = ((0, 1, 2, 3), (2, 3, 6, 7), (4, 0, 1, 2), (6, 0, 4, 5))
RIGHT_BLOCKS = ((2, 3, 6, 7), (4, 5, 6, 7), (0, 1, 2, 4), (0, 4, 5, 6))


def fold_by_column(tile, flipped, folded, first):
    groups = len(LEFT_BLOCKS)
    owners = range(first, first + groups // 2)
    snps = folded.shape[1]
    wide = snps // groups
    size = wide // 2
    shape = (size, snps)
    row, lane = iota(shape, 0), iota(shape, 1)

    def block(number):
        return tile[number * size : (number + 1) * size, :]

    diagonal = block(2 * first)
    for number in range(2 * first + 1, 2 * first + groups):
        diagonal = jnp.where(lane >= number * size, block(number), diagonal)
    flipped[:, 0:size] = diagonal.T
    corner = diagonal
    for owner in owners:
        start = (2 * owner + 1) * size
        turned = jnp.concatenate(
            [flipped[start : start + size, :], jnp.zeros((size, snps - LANES), jnp.float32)], axis=1
        )
        if owner:
            turned = pltpu.roll(turned, owner * wide, 1)
        inside = lane - owner * wide
        other = (row <= inside) if first == 0 else (row >= inside)
        corner = jnp.where((inside >= 0) & (inside < size) & other, turned, corner)
    rolled = []
    for shift in range(groups):
        mixed = None
        for owner in owners:
            slot = (owner + shift) % groups
            left = block(LEFT_BLOCKS[owner][slot]) if slot else corner
            start = owner * wide
            mixed = left if mixed is None else jnp.where(lane >= start, left, mixed)
            mixed = jnp.where(lane >= start + size, block(RIGHT_BLOCKS[owner][slot]), mixed)
        rolled.append(pltpu.roll(mixed, shift * wide, 1) if shift else mixed)
    for owner in owners:
        mixed = rolled[(0 - owner) % groups]
        for slot in range(1, groups):
            mixed = jnp.where(lane >= slot * wide, rolled[(slot - owner) % groups], mixed)
        where = slice((owner - first) * size, (owner - first + 1) * size)
        folded[where, :] = to_fields(mixed)


def side_kernel(far, share, weighted_ref, side_ref, totals_ref, *refs):
    groups = len(LEFT_BLOCKS)
    if far:
        own_parts, refs = refs[:groups], refs[groups + 1 :]
        own_sum_ref, refs = refs[0], refs[1:]
        own_sum_ref[...] = sum((part[...] for part in own_parts[1:]), own_parts[0][...])
    targets, (near, window, tile, folded, flipped) = refs[:groups], refs[groups:]
    rows, snps = near.shape[0], tile.shape[1]
    half = rows // 2
    above = odd_block() == far
    mixed = side_ref[0:half, 2 * LANES :]
    turned = pltpu.roll(mixed.astype(jnp.float32), HALF_LANES, 1).astype(mixed.dtype)

    def fill(whole, shared):
        near[0:half, whole : whole + LANES] = side_ref[0:half, 0:LANES]
        near[half:, whole : whole + LANES] = side_ref[0:half, LANES : 2 * LANES]
        near[0:half, shared : shared + LANES] = mixed
        near[half:, shared : shared + LANES] = turned

    @pl.when(above)
    def _():
        fill(0, LANES)

    @pl.when(jnp.logical_not(above))
    def _():
        fill(LANES, 0)

    window[...] = jnp.dot(weighted_ref[...], near[...], preferred_element_type=jnp.float32)

    @pl.when(above)
    def _():
        tile[:, 0 : 2 * LANES] = window[...]
        fold_by_column(tile, flipped, folded, 0)

    @pl.when(jnp.logical_not(above))
    def _():
        tile[:, LANES:] = window[...]
        fold_by_column(tile, flipped, folded, groups // 2)

    square = (snps, snps)
    apart = jnp.sum(
        jnp.where(iota(square, 0) == iota(square, 1), tile[0:snps, :], 0.0), axis=0, keepdims=True
    )
    extras = to_fields(
        jnp.concatenate(
            [totals_ref[0:2, :], tile[snps : snps + 1, :], apart, jnp.zeros((4, snps))], axis=0
        )
    )
    me = lax.axis_index("hap")
    for step, target in enumerate(targets):
        chunk = partner(me, step, groups) & 1
        target[0:share, :] = folded[pl.ds(pl.multiple_of(chunk * share, 8), share), :]
        target[share:, :] = extras


def near_kernel(groups, share, weighted_ref, far_ref, close_ref, totals_ref, *refs):
    own_parts, own_sum_ref = refs[:groups], refs[groups]
    targets, (near, tile, folded) = refs[groups + 1 : 2 * groups + 1], refs[2 * groups + 1 :]
    rows, snps = near.shape
    half = snps // 2
    odd = odd_block()

    def unpack(up_ref, down_ref):
        pieces = load_packed(up_ref[0 : rows // 2, :], down_ref[0 : rows // 2, :])
        for side in range(2):
            where = slice(side * (rows // 2), (side + 1) * (rows // 2))
            for number in range(3):
                near[where, number * LANES : (number + 1) * LANES] = pieces[side][number]

    @pl.when(odd)
    def _():
        unpack(far_ref, close_ref)

    @pl.when(jnp.logical_not(odd))
    def _():
        unpack(close_ref, far_ref)

    tile[...] = jnp.dot(weighted_ref[...], near[...], preferred_element_type=jnp.float32)
    row, col = iota((half, snps), 0), iota((half, snps), 1)
    moved = (col >= half) & (col - half < row)
    turned = pltpu.roll(tile[0:half, :], half, 1)
    folded[0:half, :] = to_fields(jnp.where(moved, turned, tile[half:snps, :]))
    if folded.shape[0] > half:
        folded[half:, :] = jnp.zeros((folded.shape[0] - half, snps), jnp.int32)
    square = (snps, snps)
    far = jnp.sum(
        jnp.where(iota(square, 0) == iota(square, 1), tile[0:snps, :], 0.0), axis=0, keepdims=True
    )
    extras = to_fields(
        jnp.concatenate(
            [totals_ref[0:2, :], tile[snps : snps + 1, :], far, jnp.zeros((4, snps))], axis=0
        )
    )
    send_shares(groups, folded, share, targets)
    for target in targets:
        target[share:, :] = extras
    own_sum_ref[...] = sum((part[...] for part in own_parts[1:]), own_parts[0][...])


def annots_kernel(annot_ref, far_ref, close_ref, own_ref, near_ref):
    snps = annot_ref.shape[1]
    part = far_ref.shape[0]
    wide = 2 * part
    own = annot_ref[...].astype(jnp.float32)
    own = jnp.concatenate([own, jnp.zeros((LANES - own.shape[0], snps), jnp.float32)], axis=0)
    own_ref[...] = own.T
    odd = odd_block()
    far, close = far_ref[...].astype(jnp.float32), close_ref[...].astype(jnp.float32)
    first, second = load_packed(jnp.where(odd, far, close), jnp.where(odd, close, far))
    near = jnp.concatenate(
        [
            jnp.concatenate([piece.astype(jnp.float32) for piece in first], axis=1),
            jnp.concatenate([piece.astype(jnp.float32) for piece in second], axis=1),
            jnp.zeros((LANES - wide, snps), jnp.float32),
        ],
        axis=0,
    )
    near_ref[...] = near.T


def column_stats(totals, count):
    size = jnp.maximum(count, 1.0)
    frequency = totals / size
    variance = jnp.maximum(frequency * (1.0 - frequency), VARIANCE_FLOOR)
    inverse = 1.0 / jnp.sqrt(size * variance)
    low = ((0.0 - frequency) * inverse).astype(jnp.bfloat16).astype(jnp.float32)
    high = ((1.0 - frequency) * inverse).astype(jnp.bfloat16).astype(jnp.float32)
    step = high - low
    root = 1.0 / jnp.sqrt(size)
    return step, step * totals * root, (low * count + step * totals) * root


def correlation(row, col, count):
    return row[0] * col[0] * count - row[1] * col[1] + row[2] * col[2]


def split(values):
    high = values.astype(jnp.bfloat16)
    return high, (values - high.astype(jnp.float32)).astype(jnp.bfloat16)


def dot_split(values, right, axis):
    dims = (((axis,), (0,)), ((), ()))
    return sum(
        lax.dot_general(part, right, dims, preferred_element_type=jnp.float32)
        for part in split(values)
    )


def score_kernel(groups, share, reach_ref, *refs):
    own_sum_ref, near_parts = refs[0], refs[1 : groups + 1]
    annot_ref, near_annot_ref = refs[groups + 1 : groups + 3]
    targets = refs[groups + 3 : 2 * groups + 3]
    table, annots, near_annots, scores = refs[2 * groups + 3 :]
    snps = annot_ref.shape[0]
    half = snps // 2
    out_share = snps // groups
    me = lax.axis_index("hap")
    block = lax.axis_index("snp")
    last = reach_ref.shape[0] - 1
    reach_here = reach_ref[block]
    reach_up = reach_ref[jnp.minimum(block + 1, last)]
    reach_down = reach_ref[jnp.maximum(block - 1, 0)]

    own_counts = own_sum_ref[...]
    near_sums = sum((part[...] for part in near_parts[1:]), near_parts[0][...])
    extras = from_fields(near_sums[share:, :])
    near_counts = near_sums[0:share, :]

    own_stats, near_stats, lines = [], [], []
    for pop in range(2):
        count = extras[pop][1:2, :]
        own_stats.append(column_stats(extras[pop][0:1, :], count))
        near_stats.append(column_stats(extras[pop][2:3, :], count))
        lines += [*own_stats[pop], *near_stats[pop], extras[pop][0:1, :], extras[pop][3:4, :]]
    by_row = jnp.concatenate(lines, axis=0).T
    table[0:snps, 0:16] = by_row
    if table.shape[0] > snps:
        table[snps:, 0:16] = jnp.zeros((table.shape[0] - snps, 16), jnp.float32)
    annots[0:snps, :] = annot_ref[...]
    near_annots[0:snps, :] = near_annot_ref[...]
    if annots.shape[0] > snps:
        annots[snps:, :] = jnp.zeros((annots.shape[0] - snps, LANES), jnp.float32)

    low_rows = pl.multiple_of(me * share, 8)
    high_rows = pl.multiple_of(half + me * share, 8)

    def both(ref):
        return jnp.concatenate([ref[pl.ds(low_rows, share), :], ref[pl.ds(high_rows, share), :]], axis=0)

    here = both(table)
    own_count = jnp.concatenate([pltpu.roll(own_counts, half, 1), own_counts], axis=0)
    near_count = jnp.concatenate([pltpu.roll(near_counts, half, 1), near_counts], axis=0)
    shape = (2 * share, snps)
    local, col = iota(shape, 0), iota(shape, 1)
    low = local < share
    place = jnp.where(low, local, local - share) + me * share
    row = jnp.where(low, place, place + half)
    own_fields, near_fields = from_fields(own_count), from_fields(near_count)
    own_product, near_product = 1.0, 1.0
    for pop in range(2):
        row_stats = [here[:, 8 * pop + k : 8 * pop + k + 1] for k in range(3)]
        own_product *= correlation(row_stats, own_stats[pop], own_fields[pop])
        near_product *= correlation(row_stats, near_stats[pop], near_fields[pop])
    real = place < half
    own_inside = real & ((low & (col > row)) | (~low & (col >= half) & (col < row)))
    own_inside &= jnp.abs(col - row) <= reach_here
    own_kept = jnp.where(own_inside, own_product, 0.0)
    in_upper = col < half
    near_inside = real & ((low & (col < row)) | (~low & (in_upper | (col > row))))
    distance = jnp.where(in_upper, snps + col - row, snps + row - col)
    near_here = jnp.where(near_inside & (distance <= reach_here), near_product, 0.0)
    reach_there = jnp.where(in_upper, reach_up, reach_down)
    near_there = jnp.where(near_inside & (distance <= reach_there), near_product, 0.0)

    rows_here = both(annots)
    rows_there = pltpu.roll(rows_here, HALF_LANES, 1)
    scores[0:snps, :] = dot_split(
        jnp.concatenate([own_kept, near_there], axis=0),
        jnp.concatenate([rows_here, rows_there], axis=0).astype(jnp.bfloat16),
        0,
    )
    direct = dot_split(
        jnp.concatenate([own_kept, near_here], axis=1),
        jnp.concatenate([annot_ref[...], near_annot_ref[...]], axis=0).astype(jnp.bfloat16),
        1,
    )
    scores[pl.ds(low_rows, share), :] += direct[0:share, :]
    scores[pl.ds(high_rows, share), :] += direct[share:, :]

    out_rows = pl.ds(pl.multiple_of(me * out_share, 8), out_share)
    mine = table[out_rows, :]
    self_product, far_product = 1.0, 1.0
    for pop in range(2):
        k = 8 * pop
        own_row = [mine[:, k + s : k + s + 1] for s in range(3)]
        near_row = [mine[:, k + 3 + s : k + 4 + s] for s in range(3)]
        self_product *= correlation(own_row, own_row, mine[:, k + 6 : k + 7])
        far_product *= correlation(own_row, near_row, mine[:, k + 7 : k + 8])
    mine_annots = annots[out_rows, :]
    far_reach = jnp.where(me < groups // 2, reach_up, reach_down)
    scores[out_rows, :] += (
        mine_annots * self_product
        + near_annots[out_rows, :] * jnp.where(reach_here >= snps, far_product, 0.0)
        + pltpu.roll(mine_annots, HALF_LANES, 1) * jnp.where(far_reach >= snps, far_product, 0.0)
    )
    send_shares(groups, scores, out_share, targets)


def pack_halves(values):
    half = values.shape[0] // 2
    left = iota((half, LANES), 1) < HALF_LANES
    return jnp.where(left, values[0:half], pltpu.roll(values[half:], HALF_LANES, 1))


def unpack_halves(packed):
    return jnp.concatenate([packed, pltpu.roll(packed, HALF_LANES, 1)], axis=0)


def column_score_kernel(groups, share, reach_ref, *refs):
    own_sum_ref, far_parts, close_parts = refs[0], refs[1 : groups + 1], refs[groups + 1 : 2 * groups + 1]
    annot_ref, near_annot_ref = refs[2 * groups + 1 : 2 * groups + 3]
    out_ref, *targets = refs[2 * groups + 3 : 3 * groups + 3]
    near_out_ref, table, flipped, scores = refs[3 * groups + 3 :]
    snps = annot_ref.shape[0]
    half = snps // 2
    wide = snps // groups
    size = wide // 2
    me = lax.axis_index("hap")
    block = lax.axis_index("snp")
    last = reach_ref.shape[0] - 1
    upper = me < groups // 2
    reach_here = reach_ref[block]
    reach_there = jnp.where(
        upper, reach_ref[jnp.minimum(block + 1, last)], reach_ref[jnp.maximum(block - 1, 0)]
    )

    def mine(choices):
        value = choices[0]
        for group in range(1, groups):
            value = jnp.where(me == group, choices[group], value)
        return value

    own_counts = own_sum_ref[...]
    from_far = odd_block() == upper
    near_sums = sum(
        jnp.where(from_far, far[...], close[...]) for far, close in zip(far_parts, close_parts)
    )
    extras = from_fields(near_sums[share:, :])
    near_counts = near_sums[0:share, :]

    own_stats, near_stats, lines = [], [], []
    for pop in range(2):
        count = extras[pop][1:2, :]
        own_stats.append(column_stats(extras[pop][0:1, :], count))
        near_stats.append(column_stats(extras[pop][2:3, :], count))
        lines += [*own_stats[pop], *near_stats[pop], extras[pop][0:1, :], extras[pop][3:4, :]]
    table[:, 0:16] = jnp.concatenate(lines, axis=0).T

    low_rows = pl.multiple_of(me * share, 8)
    high_rows = pl.multiple_of(half + me * share, 8)

    def both(ref):
        return jnp.concatenate([ref[pl.ds(low_rows, share), :], ref[pl.ds(high_rows, share), :]], axis=0)

    here = both(table)
    own_fields = from_fields(
        jnp.concatenate([pltpu.roll(own_counts, half, 1), own_counts], axis=0)
    )
    shape = (2 * share, snps)
    local, col = iota(shape, 0), iota(shape, 1)
    low = local < share
    row = jnp.where(low, local, local + half - share) + me * share
    product = 1.0
    for pop in range(2):
        row_stats = [here[:, 8 * pop + k : 8 * pop + k + 1] for k in range(3)]
        product *= correlation(row_stats, own_stats[pop], own_fields[pop])
    inside = (low & (col > row)) | (~low & (col >= half) & (col < row))
    own_kept = jnp.where(inside & (jnp.abs(col - row) <= reach_here), product, 0.0)
    rows_here = both(annot_ref).astype(jnp.bfloat16)
    scores[...] = dot_split(own_kept, rows_here, 0)
    direct = dot_split(own_kept, annot_ref[...].astype(jnp.bfloat16), 1)
    scores[pl.ds(low_rows, share), :] += direct[0:share, :]
    scores[pl.ds(high_rows, share), :] += direct[share:, :]

    slots = [near_counts[:, 0:LANES]]
    for slot in range(1, groups):
        slots.append(pltpu.roll(near_counts, snps - slot * wide, 1)[:, 0:LANES])
    flipped[:, 0:size] = slots[0].T
    slots.append(pltpu.roll(flipped[0:size, :], size, 1))
    left_places = [mine([LEFT_BLOCKS[g][slot] for g in range(groups)]) * size for slot in range(groups)]
    right_places = [mine([RIGHT_BLOCKS[g][slot] for g in range(groups)]) * size for slot in range(groups)]
    left_places.append(left_places[0])
    right_places.append((2 * me + 1) * size)

    def rows_of(ref, places):
        return [ref[pl.ds(pl.multiple_of(place, 8), size), :] for place in places]

    near_fields = from_fields(jnp.concatenate(slots, axis=0))
    left_table = jnp.concatenate(rows_of(table, left_places), axis=0)
    right_table = jnp.concatenate(rows_of(table, right_places), axis=0)
    local, lane = iota((size, LANES), 0), iota((size, LANES), 1)
    is_left = lane < size
    own_row = jnp.concatenate(
        [local + jnp.where(is_left, a, b) for a, b in zip(left_places, right_places)], axis=0
    )
    shape = own_row.shape
    lane = iota(shape, 1)
    is_left = lane < size
    apart = jnp.abs(own_row - (lane + me * wide))
    ahead = (own_row - (lane + me * wide)) * jnp.where(upper, 1, -1) > 0
    real = ahead & (lane < wide) & ((lane >= size) | (iota(shape, 0) < groups * size))
    near_lines = jnp.concatenate([*near_stats[0], *near_stats[1], *near_stats[0][0:2]], axis=0)
    near_lines = mine(
        [near_lines[:, 0:LANES]]
        + [pltpu.roll(near_lines, snps - group * wide, 1)[:, 0:LANES] for group in range(1, groups)]
    )
    product = 1.0
    for pop in range(2):
        row_stats = [
            jnp.where(
                is_left,
                left_table[:, 8 * pop + k : 8 * pop + k + 1],
                right_table[:, 8 * pop + k : 8 * pop + k + 1],
            )
            for k in range(3)
        ]
        col_stats = [near_lines[3 * pop + k : 3 * pop + k + 1, :] for k in range(3)]
        product *= correlation(row_stats, col_stats, near_fields[pop])
    near_here = jnp.where(real & (snps - apart <= reach_here), product, 0.0)
    near_there = jnp.where(real & (snps - apart <= reach_there), product, 0.0)

    def sides(values):
        return jnp.concatenate(
            [jnp.where(is_left, values, 0.0), jnp.where(is_left, 0.0, values)], axis=0
        )

    slice_rows = pl.ds(pl.multiple_of(me * wide, 8), wide)
    their_annots = near_annot_ref[slice_rows, :]
    columns = jnp.concatenate([their_annots, jnp.zeros((LANES - wide, LANES), jnp.float32)], axis=0)
    direct = dot_split(sides(near_here), columns.astype(jnp.bfloat16), 1)
    places = left_places + right_places
    for number, place in enumerate(places):
        scores[pl.ds(pl.multiple_of(place, 8), size), :] += direct[number * size : (number + 1) * size, :]
    own_rows = jnp.concatenate(rows_of(annot_ref, places), axis=0).astype(jnp.bfloat16)
    near_scores = dot_split(sides(near_there), own_rows, 0)[0:wide, :]

    mine_table = table[slice_rows, :]
    self_product, far_product = 1.0, 1.0
    for pop in range(2):
        k = 8 * pop
        own_row = [mine_table[:, k + s : k + s + 1] for s in range(3)]
        near_row = [mine_table[:, k + 3 + s : k + 4 + s] for s in range(3)]
        self_product *= correlation(own_row, own_row, mine_table[:, k + 6 : k + 7])
        far_product *= correlation(own_row, near_row, mine_table[:, k + 7 : k + 8])
    my_annots = annot_ref[slice_rows, :]
    out_ref[...] = (
        scores[slice_rows, :]
        + my_annots * self_product
        + their_annots * jnp.where(reach_here >= snps, far_product, 0.0)
    )
    near_scores += my_annots * jnp.where(reach_there >= snps, far_product, 0.0)
    near_out_ref[...] = pack_halves(near_scores)
    for step, target in enumerate(targets, 1):
        group = partner(me, step, groups)
        rows = scores[pl.ds(pl.multiple_of(group * wide, 8), wide), :]
        target[...] = pack_halves(rows).astype(target.dtype)


def column_finish_kernel(own_ref, there_ref, *refs):
    *parts, out_ref = refs
    packed = sum((part[...].astype(jnp.float32) for part in parts), there_ref[...])
    out_ref[...] = (own_ref[...] + unpack_halves(packed)).T[0 : out_ref.shape[0], :]


def sum_kernel(*refs):
    *parts, own_ref, there_ref = refs
    total = sum((part[...].astype(jnp.float32) for part in parts[1:]), parts[0][...])
    own_ref[...] = total
    half = there_ref.shape[0]
    left = iota((half, LANES), 1) < HALF_LANES
    second = total[half:]
    if second.shape[0] < half:
        second = jnp.concatenate([second, jnp.zeros((half - second.shape[0], LANES))], axis=0)
    there_ref[...] = jnp.where(left, pltpu.roll(total[0:half], HALF_LANES, 1), second)


def finish_kernel(own_ref, there_ref, out_ref):
    annots, rows = out_ref.shape
    there = there_ref[...]
    there = jnp.concatenate([there, pltpu.roll(there, HALF_LANES, 1)], axis=0)
    out_ref[...] = (own_ref[...] + there[0:rows]).T[0:annots, :]


def around(value, groups, step):
    return lax.ppermute(
        value, "hap", [(source, partner(source, step, groups)) for source in range(groups)]
    )


def to_owners(value, groups, step, far):
    pairs = []
    for block in range(lax.axis_size("snp")):
        above = (block % 2 == 1) == far
        for group in range(groups):
            target = partner(group, step, groups)
            if (target < groups // 2) == above:
                pairs.append((block * groups + group, block * groups + target))
    return lax.ppermute(value, ("snp", "hap"), pairs)


def swapped(value, first):
    pairs = []
    for block in range(first, lax.axis_size("snp") - 1, 2):
        pairs += [(block, block + 1), (block + 1, block)]
    return lax.ppermute(value, "snp", pairs)


def per_device(haplotypes, labels, annotations, reach):
    rows, snps = haplotypes.shape
    half = snps // 2
    groups = lax.axis_size("hap")
    blocks = lax.axis_size("snp")
    share = round_up(-(-half // groups), 16)
    folded_rows = share * groups
    out_share = snps // groups
    padded = half + folded_rows
    annot_part = 32
    bf16, f32, i32 = jnp.bfloat16, jnp.float32, jnp.int32
    shape = jax.ShapeDtypeStruct

    packed = shape((rows // 2 + annot_part, snps), bf16)
    haplotypes = pltpu.with_memory_space_constraint(haplotypes, pltpu.HBM)
    annots_in = pltpu.with_memory_space_constraint(annotations, pltpu.HBM)
    alleles, far, close = call(
        prepare_kernel,
        [shape((rows, snps), bf16), packed, packed],
        [HBM, HBM],
        [
            pltpu.VMEM((rows, snps), i32),
            pltpu.VMEM(annotations.shape, i32),
            pltpu.SemaphoreType.DMA((2 * CHUNKS + 1,)),
        ],
        moved=rows * snps * 8,
    )(haplotypes, annots_in)
    from_far = swapped(far, 1)
    from_close = swapped(close, 0)

    tile = pltpu.VMEM((snps + 16, snps), f32)
    folded = pltpu.VMEM((folded_rows, snps), i32)
    weighted, totals, *own_parts = call(
        functools.partial(own_kernel, groups, share),
        [shape((snps + 16, rows), bf16), shape((8, snps), f32)] + [shape((share, snps), i32)] * groups,
        [VMEM, VMEM],
        [tile, folded],
        flops=2 * rows * snps * snps,
        moved=rows * snps * 4,
    )(alleles, labels.reshape(1, rows))
    own_parts = [own_parts[0]] + [around(own_parts[k], groups, k) for k in range(groups - 1, 0, -1)]

    side_share = shape((share + 8, snps), i32)

    def side(far, payload, *more):
        outs = call(
            functools.partial(side_kernel, far, share),
            [shape((share, snps), i32)] * far + [side_share] * groups,
            [VMEM] * (3 + len(more)),
            [
                pltpu.VMEM((rows, 2 * LANES), bf16),
                pltpu.VMEM((snps + 16, 2 * LANES), f32),
                tile,
                pltpu.VMEM((folded_rows // 2, snps), i32),
                pltpu.VMEM((snps, LANES), f32),
            ],
            flops=4 * rows * snps * LANES,
            moved=rows * snps * 4,
        )(weighted, payload, totals, *more)
        parts = list(outs[far:])
        parts[1:] = [to_owners(parts[k], groups, k, far) for k in range(1, groups)]
        return outs[:far], parts

    by_column = groups == len(LEFT_BLOCKS)
    if by_column:
        _, close_parts = side(False, from_close)
        (own_sum,), far_parts = side(True, from_far, *own_parts, close_parts[0])
    else:
        own_sum, *near_parts = call(
            functools.partial(near_kernel, groups, share),
            [shape((share, snps), i32)] + [shape((share + 8, snps), i32)] * groups,
            [VMEM] * (4 + groups),
            [pltpu.VMEM((rows, snps), bf16), tile, folded],
            flops=2 * rows * snps * snps,
            moved=rows * snps * 4,
        )(weighted, from_far, from_close, totals, *own_parts)
        near_parts = [near_parts[0]] + [around(near_parts[k], groups, k) for k in range(groups - 1, 0, -1)]

    by_snp = shape((snps, LANES), f32)
    own_annots, near_annots = call(annots_kernel, [by_snp, by_snp], [VMEM] * 3, moved=1 << 20)(
        annotations, from_far[rows // 2 :], from_close[rows // 2 :]
    )
    pairs = []
    for block in range(blocks):
        for group in range(groups):
            target = block + 1 if group < groups // 2 else block - 1
            if 0 <= target < blocks:
                pairs.append((block * groups + group, target * groups + group))

    def to_neighbour(value):
        return lax.ppermute(value, ("snp", "hap"), pairs)

    result = shape((annotations.shape[0], out_share), f32)
    half_share = round_up(-(-out_share // 2), 8)
    own_share = shape((out_share, LANES), f32)
    packed_share = shape((half_share, LANES), f32)
    if by_column:
        own_scores, *scores, near_scores = call(
            functools.partial(column_score_kernel, groups, share),
            [own_share] + [shape((half_share, LANES), bf16)] * (groups - 1) + [packed_share],
            [SMEM] + [VMEM] * (2 * groups + 3),
            [pltpu.VMEM((snps, LANES), f32), pltpu.VMEM((LANES, LANES), i32), pltpu.VMEM((snps, LANES), f32)],
            flops=1 << 26,
            moved=1 << 21,
        )(reach, own_sum, *far_parts, *close_parts, own_annots, near_annots)
        scores = [around(scores[k - 1], groups, k) for k in range(groups - 1, 0, -1)]
        there = to_neighbour(near_scores)
        return call(column_finish_kernel, result, [VMEM] * (groups + 1))(own_scores, there, *scores)

    tall = pltpu.VMEM((padded, LANES), f32)
    scores = call(
        functools.partial(score_kernel, groups, share),
        [own_share] + [shape((out_share, LANES), bf16)] * (groups - 1),
        [SMEM] + [VMEM] * (groups + 3),
        [tall, tall, tall, tall],
        flops=1 << 26,
        moved=1 << 21,
    )(reach, own_sum, *near_parts, own_annots, near_annots)
    scores = [scores[0]] + [around(scores[k], groups, k) for k in range(groups - 1, 0, -1)]
    own_scores, near_scores = call(sum_kernel, [own_share, packed_share], [VMEM] * groups)(*scores)
    return call(finish_kernel, result, [VMEM] * 2)(own_scores, to_neighbour(near_scores))


def solution(mesh):
    in_specs = (
        P("hap", ("parts", "snp")),
        P(("parts", "hap")),
        P(None, ("parts", "snp")),
        P("parts"),
    )
    out_specs = P(None, ("parts", "snp", "hap"))
    return jax.shard_map(
        per_device, mesh=mesh, in_specs=in_specs, out_specs=out_specs, check_vma=False
    )
```

```python
import functools

import jax
import jax.numpy as jnp
from jax import lax
from jax.experimental import pallas as pl
from jax.experimental.pallas import tpu as pltpu
from jax.sharding import PartitionSpec as P

VARIANCE_FLOOR = 0.01
BASE_BITS = 12
BASE = 1 << BASE_BITS
FIELD_BITS = 16
LANES = 128
HALF_LANES = LANES // 2
CHUNKS = 4
VMEM = pl.BlockSpec(memory_space=pltpu.VMEM)
SMEM = pl.BlockSpec(memory_space=pltpu.SMEM)
HBM = pl.BlockSpec(memory_space=pltpu.HBM)
VMEM_LIMIT = 24 * 1024 * 1024


def iota(shape, axis):
    return lax.broadcasted_iota(jnp.int32, shape, axis)


def round_up(value, step):
    return -(-value // step) * step


def to_fields(values):
    whole = values.astype(jnp.int32)
    return whole + (whole >> BASE_BITS) * ((1 << FIELD_BITS) - BASE)


def from_fields(packed):
    first = packed & ((1 << FIELD_BITS) - 1)
    second = lax.shift_right_logical(packed, FIELD_BITS)
    return first.astype(jnp.float32), second.astype(jnp.float32)


def call(kernel, out_shape, in_specs, scratch_shapes=(), flops=0, moved=0):
    several = isinstance(out_shape, (list, tuple))
    return pl.pallas_call(
        kernel,
        out_shape=out_shape,
        in_specs=in_specs,
        out_specs=[VMEM] * len(out_shape) if several else VMEM,
        scratch_shapes=list(scratch_shapes),
        compiler_params=pltpu.CompilerParams(vmem_limit_bytes=VMEM_LIMIT),
        cost_estimate=pl.CostEstimate(flops=flops, bytes_accessed=moved, transcendentals=0),
    )


def odd_block():
    return lax.rem(lax.axis_index("snp"), 2) == 1


def store_packed(up_ref, down_ref, where, first, second):
    left = iota((first.shape[0], LANES), 1) < HALF_LANES
    middle = first[:, LANES : 2 * LANES]
    turned = pltpu.roll(second[:, LANES : 2 * LANES], HALF_LANES, 1)
    for ref, side, mixed in (
        (up_ref, slice(0, LANES), jnp.where(left, middle, turned)),
        (down_ref, slice(2 * LANES, 3 * LANES), jnp.where(left, turned, middle)),
    ):
        ref[where, 0:LANES] = first[:, side].astype(jnp.bfloat16)
        ref[where, LANES : 2 * LANES] = second[:, side].astype(jnp.bfloat16)
        ref[where, 2 * LANES : 3 * LANES] = mixed.astype(jnp.bfloat16)


def load_packed(up, down):
    left = iota((up.shape[0], LANES), 1) < HALF_LANES
    up_mixed, down_mixed = up[:, 2 * LANES :], down[:, 2 * LANES :]
    first = jnp.where(left, up_mixed, down_mixed)
    second = jnp.where(left, down_mixed, up_mixed)
    second = pltpu.roll(second.astype(jnp.float32), HALF_LANES, 1).astype(second.dtype)
    return (
        (up[:, :LANES], first, down[:, :LANES]),
        (up[:, LANES : 2 * LANES], second, down[:, LANES : 2 * LANES]),
    )


def prepare_kernel(hap_ref, annot_ref, alleles_ref, far_ref, close_ref, held, held_annots, sems):
    rows = hap_ref.shape[0]
    annot_rows = annot_ref.shape[0]
    size = rows // (2 * CHUNKS)
    starts = [side * (rows // 2) + chunk * size for chunk in range(CHUNKS) for side in range(2)]
    copies = [
        pltpu.make_async_copy(
            hap_ref.at[pl.ds(start, size)], held.at[pl.ds(start, size)], sems.at[number]
        )
        for number, start in enumerate(starts)
    ]
    copies.append(pltpu.make_async_copy(annot_ref, held_annots, sems.at[2 * CHUNKS]))
    for copy in copies:
        copy.start()
    part = far_ref.shape[0] - rows // 2
    odd = odd_block()

    def store(where, first, second):
        @pl.when(odd)
        def _():
            store_packed(close_ref, far_ref, where, first, second)

        @pl.when(jnp.logical_not(odd))
        def _():
            store_packed(far_ref, close_ref, where, first, second)

    for chunk in range(CHUNKS):
        pair = []
        for side in range(2):
            number = 2 * chunk + side
            copies[number].wait()
            where = slice(starts[number], starts[number] + size)
            values = held[where, :].astype(jnp.float32)
            alleles_ref[where, :] = values.astype(jnp.bfloat16)
            pair.append(values)
        store(slice(chunk * size, (chunk + 1) * size), *pair)
    copies[-1].wait()
    annots = jnp.concatenate(
        [
            held_annots[...].astype(jnp.float32),
            jnp.zeros((2 * part - annot_rows, annot_ref.shape[1]), jnp.float32),
        ],
        axis=0,
    )
    store(slice(rows // 2, rows // 2 + part), annots[:part], annots[part:])


def partner(group, step, groups):
    if groups & (groups - 1) == 0:
        return group ^ step
    return (group + step) % groups


def send_shares(groups, source, share, targets):
    me = lax.axis_index("hap")
    for step, target in enumerate(targets):
        group = partner(me, step, groups)
        rows = source[pl.ds(pl.multiple_of(group * share, 8), share), :]
        target[0:share, :] = rows.astype(target.dtype)


def own_kernel(groups, share, alleles_ref, label_ref, *refs):
    weighted_ref, totals_ref, *targets = refs[: 2 + groups]
    tile, folded = refs[2 + groups :]
    rows, snps = alleles_ref.shape
    half = snps // 2
    weight = jnp.where(label_ref[...] > 0, float(BASE), 1.0)
    weighted_ref[0:snps, :] = alleles_ref[...].T * weight.astype(jnp.bfloat16)
    extra = weighted_ref.shape[0] - snps
    weighted_ref[snps:, :] = jnp.broadcast_to(weight, (extra, rows)).astype(jnp.bfloat16)
    tile[...] = jnp.dot(weighted_ref[...], alleles_ref[...], preferred_element_type=jnp.float32)
    count = jnp.sum(weight, axis=1, keepdims=True)
    totals_ref[...] = jnp.concatenate(
        [tile[snps : snps + 1, :], jnp.broadcast_to(count, (1, snps)), jnp.zeros((6, snps))], axis=0
    )
    row, col = iota((half, snps), 0), iota((half, snps), 1)
    moved = (col < half) | (col - half > row)
    turned = pltpu.roll(tile[0:half, :], half, 1)
    folded[0:half, :] = to_fields(jnp.where(moved, turned, tile[half:snps, :]))
    if folded.shape[0] > half:
        folded[half:, :] = jnp.zeros((folded.shape[0] - half, snps), jnp.int32)
    send_shares(groups, folded, share, targets)


LEFT_BLOCKS = ((0, 1, 2, 3), (2, 3, 6, 7), (4, 0, 1, 2), (6, 0, 4, 5))
RIGHT_BLOCKS = ((2, 3, 6, 7), (4, 5, 6, 7), (0, 1, 2, 4), (0, 4, 5, 6))


def fold_by_column(tile, flipped, folded):
    owners = len(LEFT_BLOCKS)
    snps = folded.shape[1]
    wide = snps // owners
    size = wide // 2
    shape = (size, snps)
    row, lane = iota(shape, 0), iota(shape, 1)

    def block(number):
        return tile[number * size : (number + 1) * size, :]

    diagonal = block(0)
    for number in range(1, 2 * owners):
        diagonal = jnp.where(lane >= number * size, block(number), diagonal)
    flipped[:, 0:size] = diagonal.T
    corner = diagonal
    for owner in range(owners):
        start = (2 * owner + 1) * size
        turned = jnp.concatenate(
            [flipped[start : start + size, :], jnp.zeros((size, snps - LANES), jnp.float32)], axis=1
        )
        if owner:
            turned = pltpu.roll(turned, owner * wide, 1)
        inside = lane - owner * wide
        other = (row <= inside) if owner < owners // 2 else (row >= inside)
        corner = jnp.where((inside >= 0) & (inside < size) & other, turned, corner)
    rolled = []
    for shift in range(owners):
        mixed = None
        for owner in range(owners):
            slot = (owner + shift) % owners
            left = block(LEFT_BLOCKS[owner][slot]) if slot else corner
            start = owner * wide
            mixed = left if mixed is None else jnp.where(lane >= start, left, mixed)
            mixed = jnp.where(lane >= start + size, block(RIGHT_BLOCKS[owner][slot]), mixed)
        rolled.append(pltpu.roll(mixed, shift * wide, 1) if shift else mixed)
    for owner in range(owners):
        mixed = rolled[(0 - owner) % owners]
        for slot in range(1, owners):
            mixed = jnp.where(lane >= slot * wide, rolled[(slot - owner) % owners], mixed)
        folded[owner * size : (owner + 1) * size, :] = to_fields(mixed)


def above(far):
    return odd_block() == far


def side_dot(far, weighted_ref, side_ref, near):
    half = near.shape[0] // 2
    mixed = side_ref[0:half, 2 * LANES :]
    turned = pltpu.roll(mixed.astype(jnp.float32), HALF_LANES, 1).astype(mixed.dtype)

    def fill(whole, shared):
        near[0:half, whole : whole + LANES] = side_ref[0:half, 0:LANES]
        near[half:, whole : whole + LANES] = side_ref[0:half, LANES : 2 * LANES]
        near[0:half, shared : shared + LANES] = mixed
        near[half:, shared : shared + LANES] = turned

    @pl.when(above(far))
    def _():
        fill(0, LANES)

    @pl.when(jnp.logical_not(above(far)))
    def _():
        fill(LANES, 0)

    return jnp.dot(weighted_ref[...], near[...], preferred_element_type=jnp.float32)


def close_kernel(weighted_ref, side_ref, window_ref, near):
    window_ref[...] = side_dot(False, weighted_ref, side_ref, near)


def far_kernel(groups, share, weighted_ref, side_ref, close_ref, totals_ref, *refs):
    own_parts, own_sum_ref = refs[:groups], refs[groups]
    targets, (near, window, tile, folded, flipped) = refs[groups + 1 : 2 * groups + 1], refs[2 * groups + 1 :]
    snps = tile.shape[1]
    own_sum_ref[...] = sum((part[...] for part in own_parts[1:]), own_parts[0][...])
    window[...] = side_dot(True, weighted_ref, side_ref, near)
    left = iota((tile.shape[0], LANES), 1) < HALF_LANES

    def place(up, down):
        tile[:, 0:LANES] = up[:, 0:LANES]
        tile[:, LANES : 2 * LANES] = jnp.where(left, up[:, LANES:], down[:, 0:LANES])
        tile[:, 2 * LANES :] = down[:, LANES:]

    @pl.when(above(True))
    def _():
        place(window, close_ref)

    @pl.when(jnp.logical_not(above(True)))
    def _():
        place(close_ref, window)

    fold_by_column(tile, flipped, folded)
    square = (snps, snps)
    apart = jnp.sum(
        jnp.where(iota(square, 0) == iota(square, 1), tile[0:snps, :], 0.0), axis=0, keepdims=True
    )
    extras = to_fields(
        jnp.concatenate(
            [totals_ref[0:2, :], tile[snps : snps + 1, :], apart, jnp.zeros((4, snps))], axis=0
        )
    )
    send_shares(groups, folded, share, targets)
    for target in targets:
        target[share:, :] = extras


def near_kernel(groups, share, weighted_ref, far_ref, close_ref, totals_ref, *refs):
    own_parts, own_sum_ref = refs[:groups], refs[groups]
    targets, (near, tile, folded) = refs[groups + 1 : 2 * groups + 1], refs[2 * groups + 1 :]
    rows, snps = near.shape
    half = snps // 2
    odd = odd_block()

    def unpack(up_ref, down_ref):
        pieces = load_packed(up_ref[0 : rows // 2, :], down_ref[0 : rows // 2, :])
        for side in range(2):
            where = slice(side * (rows // 2), (side + 1) * (rows // 2))
            for number in range(3):
                near[where, number * LANES : (number + 1) * LANES] = pieces[side][number]

    @pl.when(odd)
    def _():
        unpack(far_ref, close_ref)

    @pl.when(jnp.logical_not(odd))
    def _():
        unpack(close_ref, far_ref)

    tile[...] = jnp.dot(weighted_ref[...], near[...], preferred_element_type=jnp.float32)
    row, col = iota((half, snps), 0), iota((half, snps), 1)
    moved = (col >= half) & (col - half < row)
    turned = pltpu.roll(tile[0:half, :], half, 1)
    folded[0:half, :] = to_fields(jnp.where(moved, turned, tile[half:snps, :]))
    if folded.shape[0] > half:
        folded[half:, :] = jnp.zeros((folded.shape[0] - half, snps), jnp.int32)
    square = (snps, snps)
    far = jnp.sum(
        jnp.where(iota(square, 0) == iota(square, 1), tile[0:snps, :], 0.0), axis=0, keepdims=True
    )
    extras = to_fields(
        jnp.concatenate(
            [totals_ref[0:2, :], tile[snps : snps + 1, :], far, jnp.zeros((4, snps))], axis=0
        )
    )
    send_shares(groups, folded, share, targets)
    for target in targets:
        target[share:, :] = extras
    own_sum_ref[...] = sum((part[...] for part in own_parts[1:]), own_parts[0][...])


def annots_kernel(annot_ref, far_ref, close_ref, own_ref, near_ref):
    snps = annot_ref.shape[1]
    part = far_ref.shape[0]
    wide = 2 * part
    own = annot_ref[...].astype(jnp.float32)
    own = jnp.concatenate([own, jnp.zeros((LANES - own.shape[0], snps), jnp.float32)], axis=0)
    own_ref[...] = own.T
    odd = odd_block()
    far, close = far_ref[...].astype(jnp.float32), close_ref[...].astype(jnp.float32)
    first, second = load_packed(jnp.where(odd, far, close), jnp.where(odd, close, far))
    near = jnp.concatenate(
        [
            jnp.concatenate([piece.astype(jnp.float32) for piece in first], axis=1),
            jnp.concatenate([piece.astype(jnp.float32) for piece in second], axis=1),
            jnp.zeros((LANES - wide, snps), jnp.float32),
        ],
        axis=0,
    )
    near_ref[...] = near.T


def column_stats(totals, count):
    size = jnp.maximum(count, 1.0)
    frequency = totals / size
    variance = jnp.maximum(frequency * (1.0 - frequency), VARIANCE_FLOOR)
    inverse = 1.0 / jnp.sqrt(size * variance)
    low = ((0.0 - frequency) * inverse).astype(jnp.bfloat16).astype(jnp.float32)
    high = ((1.0 - frequency) * inverse).astype(jnp.bfloat16).astype(jnp.float32)
    step = high - low
    root = 1.0 / jnp.sqrt(size)
    return step, step * totals * root, (low * count + step * totals) * root


def correlation(row, col, count):
    return row[0] * col[0] * count - row[1] * col[1] + row[2] * col[2]


def split(values):
    high = values.astype(jnp.bfloat16)
    return high, (values - high.astype(jnp.float32)).astype(jnp.bfloat16)


def dot_split(values, right, axis):
    dims = (((axis,), (0,)), ((), ()))
    return sum(
        lax.dot_general(part, right, dims, preferred_element_type=jnp.float32)
        for part in split(values)
    )


def score_kernel(groups, share, reach_ref, *refs):
    own_sum_ref, near_parts = refs[0], refs[1 : groups + 1]
    annot_ref, near_annot_ref = refs[groups + 1 : groups + 3]
    targets = refs[groups + 3 : 2 * groups + 3]
    table, annots, near_annots, scores = refs[2 * groups + 3 :]
    snps = annot_ref.shape[0]
    half = snps // 2
    out_share = snps // groups
    me = lax.axis_index("hap")
    block = lax.axis_index("snp")
    last = reach_ref.shape[0] - 1
    reach_here = reach_ref[block]
    reach_up = reach_ref[jnp.minimum(block + 1, last)]
    reach_down = reach_ref[jnp.maximum(block - 1, 0)]

    own_counts = own_sum_ref[...]
    near_sums = sum((part[...] for part in near_parts[1:]), near_parts[0][...])
    extras = from_fields(near_sums[share:, :])
    near_counts = near_sums[0:share, :]

    own_stats, near_stats, lines = [], [], []
    for pop in range(2):
        count = extras[pop][1:2, :]
        own_stats.append(column_stats(extras[pop][0:1, :], count))
        near_stats.append(column_stats(extras[pop][2:3, :], count))
        lines += [*own_stats[pop], *near_stats[pop], extras[pop][0:1, :], extras[pop][3:4, :]]
    by_row = jnp.concatenate(lines, axis=0).T
    table[0:snps, 0:16] = by_row
    if table.shape[0] > snps:
        table[snps:, 0:16] = jnp.zeros((table.shape[0] - snps, 16), jnp.float32)
    annots[0:snps, :] = annot_ref[...]
    near_annots[0:snps, :] = near_annot_ref[...]
    if annots.shape[0] > snps:
        annots[snps:, :] = jnp.zeros((annots.shape[0] - snps, LANES), jnp.float32)

    low_rows = pl.multiple_of(me * share, 8)
    high_rows = pl.multiple_of(half + me * share, 8)

    def both(ref):
        return jnp.concatenate([ref[pl.ds(low_rows, share), :], ref[pl.ds(high_rows, share), :]], axis=0)

    here = both(table)
    own_count = jnp.concatenate([pltpu.roll(own_counts, half, 1), own_counts], axis=0)
    near_count = jnp.concatenate([pltpu.roll(near_counts, half, 1), near_counts], axis=0)
    shape = (2 * share, snps)
    local, col = iota(shape, 0), iota(shape, 1)
    low = local < share
    place = jnp.where(low, local, local - share) + me * share
    row = jnp.where(low, place, place + half)
    own_fields, near_fields = from_fields(own_count), from_fields(near_count)
    own_product, near_product = 1.0, 1.0
    for pop in range(2):
        row_stats = [here[:, 8 * pop + k : 8 * pop + k + 1] for k in range(3)]
        own_product *= correlation(row_stats, own_stats[pop], own_fields[pop])
        near_product *= correlation(row_stats, near_stats[pop], near_fields[pop])
    real = place < half
    own_inside = real & ((low & (col > row)) | (~low & (col >= half) & (col < row)))
    own_inside &= jnp.abs(col - row) <= reach_here
    own_kept = jnp.where(own_inside, own_product, 0.0)
    in_upper = col < half
    near_inside = real & ((low & (col < row)) | (~low & (in_upper | (col > row))))
    distance = jnp.where(in_upper, snps + col - row, snps + row - col)
    near_here = jnp.where(near_inside & (distance <= reach_here), near_product, 0.0)
    reach_there = jnp.where(in_upper, reach_up, reach_down)
    near_there = jnp.where(near_inside & (distance <= reach_there), near_product, 0.0)

    rows_here = both(annots)
    rows_there = pltpu.roll(rows_here, HALF_LANES, 1)
    scores[0:snps, :] = dot_split(
        jnp.concatenate([own_kept, near_there], axis=0),
        jnp.concatenate([rows_here, rows_there], axis=0).astype(jnp.bfloat16),
        0,
    )
    direct = dot_split(
        jnp.concatenate([own_kept, near_here], axis=1),
        jnp.concatenate([annot_ref[...], near_annot_ref[...]], axis=0).astype(jnp.bfloat16),
        1,
    )
    scores[pl.ds(low_rows, share), :] += direct[0:share, :]
    scores[pl.ds(high_rows, share), :] += direct[share:, :]

    out_rows = pl.ds(pl.multiple_of(me * out_share, 8), out_share)
    mine = table[out_rows, :]
    self_product, far_product = 1.0, 1.0
    for pop in range(2):
        k = 8 * pop
        own_row = [mine[:, k + s : k + s + 1] for s in range(3)]
        near_row = [mine[:, k + 3 + s : k + 4 + s] for s in range(3)]
        self_product *= correlation(own_row, own_row, mine[:, k + 6 : k + 7])
        far_product *= correlation(own_row, near_row, mine[:, k + 7 : k + 8])
    mine_annots = annots[out_rows, :]
    far_reach = jnp.where(me < groups // 2, reach_up, reach_down)
    scores[out_rows, :] += (
        mine_annots * self_product
        + near_annots[out_rows, :] * jnp.where(reach_here >= snps, far_product, 0.0)
        + pltpu.roll(mine_annots, HALF_LANES, 1) * jnp.where(far_reach >= snps, far_product, 0.0)
    )
    send_shares(groups, scores, out_share, targets)


def pack_halves(values):
    half = values.shape[0] // 2
    left = iota((half, LANES), 1) < HALF_LANES
    return jnp.where(left, values[0:half], pltpu.roll(values[half:], HALF_LANES, 1))


def unpack_halves(packed):
    return jnp.concatenate([packed, pltpu.roll(packed, HALF_LANES, 1)], axis=0)


def column_score_kernel(groups, share, reach_ref, *refs):
    own_sum_ref, near_parts = refs[0], refs[1 : groups + 1]
    annot_ref, near_annot_ref = refs[groups + 1 : groups + 3]
    out_ref, *targets = refs[groups + 3 : 2 * groups + 3]
    near_out_ref, table, flipped, scores = refs[2 * groups + 3 :]
    snps = annot_ref.shape[0]
    half = snps // 2
    wide = snps // groups
    size = wide // 2
    me = lax.axis_index("hap")
    block = lax.axis_index("snp")
    last = reach_ref.shape[0] - 1
    upper = me < groups // 2
    reach_here = reach_ref[block]
    reach_there = jnp.where(
        upper, reach_ref[jnp.minimum(block + 1, last)], reach_ref[jnp.maximum(block - 1, 0)]
    )

    def mine(choices):
        value = choices[0]
        for group in range(1, groups):
            value = jnp.where(me == group, choices[group], value)
        return value

    own_counts = own_sum_ref[...]
    near_sums = sum((part[...] for part in near_parts[1:]), near_parts[0][...])
    extras = from_fields(near_sums[share:, :])
    near_counts = near_sums[0:share, :]

    own_stats, near_stats, lines = [], [], []
    for pop in range(2):
        count = extras[pop][1:2, :]
        own_stats.append(column_stats(extras[pop][0:1, :], count))
        near_stats.append(column_stats(extras[pop][2:3, :], count))
        lines += [*own_stats[pop], *near_stats[pop], extras[pop][0:1, :], extras[pop][3:4, :]]
    table[:, 0:16] = jnp.concatenate(lines, axis=0).T

    low_rows = pl.multiple_of(me * share, 8)
    high_rows = pl.multiple_of(half + me * share, 8)

    def both(ref):
        return jnp.concatenate([ref[pl.ds(low_rows, share), :], ref[pl.ds(high_rows, share), :]], axis=0)

    here = both(table)
    own_fields = from_fields(
        jnp.concatenate([pltpu.roll(own_counts, half, 1), own_counts], axis=0)
    )
    shape = (2 * share, snps)
    local, col = iota(shape, 0), iota(shape, 1)
    low = local < share
    row = jnp.where(low, local, local + half - share) + me * share
    product = 1.0
    for pop in range(2):
        row_stats = [here[:, 8 * pop + k : 8 * pop + k + 1] for k in range(3)]
        product *= correlation(row_stats, own_stats[pop], own_fields[pop])
    inside = (low & (col > row)) | (~low & (col >= half) & (col < row))
    own_kept = jnp.where(inside & (jnp.abs(col - row) <= reach_here), product, 0.0)
    rows_here = both(annot_ref).astype(jnp.bfloat16)
    scores[...] = dot_split(own_kept, rows_here, 0)
    direct = dot_split(own_kept, annot_ref[...].astype(jnp.bfloat16), 1)
    scores[pl.ds(low_rows, share), :] += direct[0:share, :]
    scores[pl.ds(high_rows, share), :] += direct[share:, :]

    slots = [near_counts[:, 0:LANES]]
    for slot in range(1, groups):
        slots.append(pltpu.roll(near_counts, snps - slot * wide, 1)[:, 0:LANES])
    flipped[:, 0:size] = slots[0].T
    slots.append(pltpu.roll(flipped[0:size, :], size, 1))
    left_places = [mine([LEFT_BLOCKS[g][slot] for g in range(groups)]) * size for slot in range(groups)]
    right_places = [mine([RIGHT_BLOCKS[g][slot] for g in range(groups)]) * size for slot in range(groups)]
    left_places.append(left_places[0])
    right_places.append((2 * me + 1) * size)

    def rows_of(ref, places):
        return [ref[pl.ds(pl.multiple_of(place, 8), size), :] for place in places]

    near_fields = from_fields(jnp.concatenate(slots, axis=0))
    left_table = jnp.concatenate(rows_of(table, left_places), axis=0)
    right_table = jnp.concatenate(rows_of(table, right_places), axis=0)
    local, lane = iota((size, LANES), 0), iota((size, LANES), 1)
    is_left = lane < size
    own_row = jnp.concatenate(
        [local + jnp.where(is_left, a, b) for a, b in zip(left_places, right_places)], axis=0
    )
    shape = own_row.shape
    lane = iota(shape, 1)
    is_left = lane < size
    apart = jnp.abs(own_row - (lane + me * wide))
    ahead = (own_row - (lane + me * wide)) * jnp.where(upper, 1, -1) > 0
    real = ahead & (lane < wide) & ((lane >= size) | (iota(shape, 0) < groups * size))
    near_lines = jnp.concatenate([*near_stats[0], *near_stats[1], *near_stats[0][0:2]], axis=0)
    near_lines = mine(
        [near_lines[:, 0:LANES]]
        + [pltpu.roll(near_lines, snps - group * wide, 1)[:, 0:LANES] for group in range(1, groups)]
    )
    product = 1.0
    for pop in range(2):
        row_stats = [
            jnp.where(
                is_left,
                left_table[:, 8 * pop + k : 8 * pop + k + 1],
                right_table[:, 8 * pop + k : 8 * pop + k + 1],
            )
            for k in range(3)
        ]
        col_stats = [near_lines[3 * pop + k : 3 * pop + k + 1, :] for k in range(3)]
        product *= correlation(row_stats, col_stats, near_fields[pop])
    near_here = jnp.where(real & (snps - apart <= reach_here), product, 0.0)
    near_there = jnp.where(real & (snps - apart <= reach_there), product, 0.0)

    def sides(values):
        return jnp.concatenate(
            [jnp.where(is_left, values, 0.0), jnp.where(is_left, 0.0, values)], axis=0
        )

    slice_rows = pl.ds(pl.multiple_of(me * wide, 8), wide)
    their_annots = near_annot_ref[slice_rows, :]
    columns = jnp.concatenate([their_annots, jnp.zeros((LANES - wide, LANES), jnp.float32)], axis=0)
    direct = dot_split(sides(near_here), columns.astype(jnp.bfloat16), 1)
    places = left_places + right_places
    for number, place in enumerate(places):
        scores[pl.ds(pl.multiple_of(place, 8), size), :] += direct[number * size : (number + 1) * size, :]
    own_rows = jnp.concatenate(rows_of(annot_ref, places), axis=0).astype(jnp.bfloat16)
    near_scores = dot_split(sides(near_there), own_rows, 0)[0:wide, :]

    mine_table = table[slice_rows, :]
    self_product, far_product = 1.0, 1.0
    for pop in range(2):
        k = 8 * pop
        own_row = [mine_table[:, k + s : k + s + 1] for s in range(3)]
        near_row = [mine_table[:, k + 3 + s : k + 4 + s] for s in range(3)]
        self_product *= correlation(own_row, own_row, mine_table[:, k + 6 : k + 7])
        far_product *= correlation(own_row, near_row, mine_table[:, k + 7 : k + 8])
    my_annots = annot_ref[slice_rows, :]
    out_ref[...] = (
        scores[slice_rows, :]
        + my_annots * self_product
        + their_annots * jnp.where(reach_here >= snps, far_product, 0.0)
    )
    near_scores += my_annots * jnp.where(reach_there >= snps, far_product, 0.0)
    near_out_ref[...] = pack_halves(near_scores)
    for step, target in enumerate(targets, 1):
        group = partner(me, step, groups)
        rows = scores[pl.ds(pl.multiple_of(group * wide, 8), wide), :]
        target[...] = pack_halves(rows).astype(target.dtype)


def column_finish_kernel(own_ref, *refs):
    *parts, there_ref, out_ref = refs
    packed = sum((part[...].astype(jnp.float32) for part in parts), there_ref[...])
    out_ref[...] = (own_ref[...] + unpack_halves(packed)).T[0 : out_ref.shape[0], :]


def sum_kernel(*refs):
    *parts, own_ref, there_ref = refs
    total = sum((part[...].astype(jnp.float32) for part in parts[1:]), parts[0][...])
    own_ref[...] = total
    half = there_ref.shape[0]
    left = iota((half, LANES), 1) < HALF_LANES
    second = total[half:]
    if second.shape[0] < half:
        second = jnp.concatenate([second, jnp.zeros((half - second.shape[0], LANES))], axis=0)
    there_ref[...] = jnp.where(left, pltpu.roll(total[0:half], HALF_LANES, 1), second)


def finish_kernel(own_ref, there_ref, out_ref):
    annots, rows = out_ref.shape
    there = there_ref[...]
    there = jnp.concatenate([there, pltpu.roll(there, HALF_LANES, 1)], axis=0)
    out_ref[...] = (own_ref[...] + there[0:rows]).T[0:annots, :]


def around(value, groups, step):
    return lax.ppermute(
        value, "hap", [(source, partner(source, step, groups)) for source in range(groups)]
    )


def swapped(value, first):
    pairs = []
    for block in range(first, lax.axis_size("snp") - 1, 2):
        pairs += [(block, block + 1), (block + 1, block)]
    return lax.ppermute(value, "snp", pairs)


def per_device(haplotypes, labels, annotations, reach):
    rows, snps = haplotypes.shape
    half = snps // 2
    groups = lax.axis_size("hap")
    blocks = lax.axis_size("snp")
    share = round_up(-(-half // groups), 16)
    folded_rows = share * groups
    out_share = snps // groups
    padded = half + folded_rows
    annot_part = 32
    bf16, f32, i32 = jnp.bfloat16, jnp.float32, jnp.int32
    shape = jax.ShapeDtypeStruct

    packed = shape((rows // 2 + annot_part, snps), bf16)
    haplotypes = pltpu.with_memory_space_constraint(haplotypes, pltpu.HBM)
    annots_in = pltpu.with_memory_space_constraint(annotations, pltpu.HBM)
    alleles, far, close = call(
        prepare_kernel,
        [shape((rows, snps), bf16), packed, packed],
        [HBM, HBM],
        [
            pltpu.VMEM((rows, snps), i32),
            pltpu.VMEM(annotations.shape, i32),
            pltpu.SemaphoreType.DMA((2 * CHUNKS + 1,)),
        ],
        moved=rows * snps * 8,
    )(haplotypes, annots_in)
    from_far = swapped(far, 1)
    from_close = swapped(close, 0)

    tile = pltpu.VMEM((snps + 16, snps), f32)
    folded = pltpu.VMEM((folded_rows, snps), i32)
    weighted, totals, *own_parts = call(
        functools.partial(own_kernel, groups, share),
        [shape((snps + 16, rows), bf16), shape((8, snps), f32)] + [shape((share, snps), i32)] * groups,
        [VMEM, VMEM],
        [tile, folded],
        flops=2 * rows * snps * snps,
        moved=rows * snps * 4,
    )(alleles, labels.reshape(1, rows))
    own_parts = [own_parts[0]] + [around(own_parts[k], groups, k) for k in range(groups - 1, 0, -1)]

    by_column = groups == len(LEFT_BLOCKS)
    near_shapes = [shape((share, snps), i32)] + [shape((share + 8, snps), i32)] * groups
    if by_column:
        near = pltpu.VMEM((rows, 2 * LANES), bf16)
        window = (snps + 16, 2 * LANES)
        work = dict(flops=4 * rows * snps * LANES, moved=rows * snps * 4)
        close_counts = call(close_kernel, shape(window, f32), [VMEM] * 2, [near], **work)(
            weighted, from_close
        )
        own_sum, *near_parts = call(
            functools.partial(far_kernel, groups, share),
            near_shapes,
            [VMEM] * (4 + groups),
            [near, pltpu.VMEM(window, f32), tile, folded, pltpu.VMEM((snps, LANES), f32)],
            **work,
        )(weighted, from_far, close_counts, totals, *own_parts)
    else:
        own_sum, *near_parts = call(
            functools.partial(near_kernel, groups, share),
            near_shapes,
            [VMEM] * (4 + groups),
            [pltpu.VMEM((rows, snps), bf16), tile, folded],
            flops=2 * rows * snps * snps,
            moved=rows * snps * 4,
        )(weighted, from_far, from_close, totals, *own_parts)
    near_parts = [near_parts[0]] + [around(near_parts[k], groups, k) for k in range(groups - 1, 0, -1)]

    by_snp = shape((snps, LANES), f32)
    own_annots, near_annots = call(annots_kernel, [by_snp, by_snp], [VMEM] * 3, moved=1 << 20)(
        annotations, from_far[rows // 2 :], from_close[rows // 2 :]
    )
    pairs = []
    for block in range(blocks):
        for group in range(groups):
            target = block + 1 if group < groups // 2 else block - 1
            if 0 <= target < blocks:
                pairs.append((block * groups + group, target * groups + group))

    def to_neighbour(value):
        return lax.ppermute(value, ("snp", "hap"), pairs)

    result = shape((annotations.shape[0], out_share), f32)
    half_share = round_up(-(-out_share // 2), 8)
    own_share = shape((out_share, LANES), f32)
    packed_share = shape((half_share, LANES), f32)
    if by_column:
        own_scores, *scores, near_scores = call(
            functools.partial(column_score_kernel, groups, share),
            [own_share] + [shape((half_share, LANES), bf16)] * (groups - 1) + [packed_share],
            [SMEM] + [VMEM] * (groups + 3),
            [pltpu.VMEM((snps, LANES), f32), pltpu.VMEM((LANES, LANES), i32), pltpu.VMEM((snps, LANES), f32)],
            flops=1 << 26,
            moved=1 << 21,
        )(reach, own_sum, *near_parts, own_annots, near_annots)
        scores = [around(scores[k - 1], groups, k) for k in range(groups - 1, 0, -1)]
        there = to_neighbour(near_scores)
        return call(column_finish_kernel, result, [VMEM] * (groups + 1))(own_scores, *scores, there)

    tall = pltpu.VMEM((padded, LANES), f32)
    scores = call(
        functools.partial(score_kernel, groups, share),
        [own_share] + [shape((out_share, LANES), bf16)] * (groups - 1),
        [SMEM] + [VMEM] * (groups + 3),
        [tall, tall, tall, tall],
        flops=1 << 26,
        moved=1 << 21,
    )(reach, own_sum, *near_parts, own_annots, near_annots)
    scores = [scores[0]] + [around(scores[k], groups, k) for k in range(groups - 1, 0, -1)]
    own_scores, near_scores = call(sum_kernel, [own_share, packed_share], [VMEM] * groups)(*scores)
    return call(finish_kernel, result, [VMEM] * 2)(own_scores, to_neighbour(near_scores))


def solution(mesh):
    in_specs = (
        P("hap", ("parts", "snp")),
        P(("parts", "hap")),
        P(None, ("parts", "snp")),
        P("parts"),
    )
    out_specs = P(None, ("parts", "snp", "hap"))
    return jax.shard_map(
        per_device, mesh=mesh, in_specs=in_specs, out_specs=out_specs, check_vma=False
    )
```

```python
import functools

import jax
import jax.numpy as jnp
from jax import lax
from jax.experimental import pallas as pl
from jax.experimental.pallas import tpu as pltpu
from jax.sharding import PartitionSpec as P

VARIANCE_FLOOR = 0.01
BASE_BITS = 12
BASE = 1 << BASE_BITS
FIELD_BITS = 16
LANES = 128
HALF_LANES = LANES // 2
CHUNKS = 4
VMEM = pl.BlockSpec(memory_space=pltpu.VMEM)
SMEM = pl.BlockSpec(memory_space=pltpu.SMEM)
HBM = pl.BlockSpec(memory_space=pltpu.HBM)
VMEM_LIMIT = 24 * 1024 * 1024


def iota(shape, axis):
    return lax.broadcasted_iota(jnp.int32, shape, axis)


def round_up(value, step):
    return -(-value // step) * step


def to_fields(values):
    whole = values.astype(jnp.int32)
    return whole + (whole >> BASE_BITS) * ((1 << FIELD_BITS) - BASE)


def from_fields(packed):
    first = packed & ((1 << FIELD_BITS) - 1)
    second = lax.shift_right_logical(packed, FIELD_BITS)
    return first.astype(jnp.float32), second.astype(jnp.float32)


def call(kernel, out_shape, in_specs, scratch_shapes=(), flops=0, moved=0):
    several = isinstance(out_shape, (list, tuple))
    return pl.pallas_call(
        kernel,
        out_shape=out_shape,
        in_specs=in_specs,
        out_specs=[VMEM] * len(out_shape) if several else VMEM,
        scratch_shapes=list(scratch_shapes),
        compiler_params=pltpu.CompilerParams(vmem_limit_bytes=VMEM_LIMIT),
        cost_estimate=pl.CostEstimate(flops=flops, bytes_accessed=moved, transcendentals=0),
    )


def odd_block():
    return lax.rem(lax.axis_index("snp"), 2) == 1


def store_packed(up_ref, down_ref, where, first, second):
    left = iota((first.shape[0], LANES), 1) < HALF_LANES
    middle = first[:, LANES : 2 * LANES]
    turned = pltpu.roll(second[:, LANES : 2 * LANES], HALF_LANES, 1)
    for ref, side, mixed in (
        (up_ref, slice(0, LANES), jnp.where(left, middle, turned)),
        (down_ref, slice(2 * LANES, 3 * LANES), jnp.where(left, turned, middle)),
    ):
        ref[where, 0:LANES] = first[:, side].astype(jnp.bfloat16)
        ref[where, LANES : 2 * LANES] = second[:, side].astype(jnp.bfloat16)
        ref[where, 2 * LANES : 3 * LANES] = mixed.astype(jnp.bfloat16)


def load_packed(up, down):
    left = iota((up.shape[0], LANES), 1) < HALF_LANES
    up_mixed, down_mixed = up[:, 2 * LANES :], down[:, 2 * LANES :]
    first = jnp.where(left, up_mixed, down_mixed)
    second = jnp.where(left, down_mixed, up_mixed)
    second = pltpu.roll(second.astype(jnp.float32), HALF_LANES, 1).astype(second.dtype)
    return (
        (up[:, :LANES], first, down[:, :LANES]),
        (up[:, LANES : 2 * LANES], second, down[:, LANES : 2 * LANES]),
    )


def prepare_kernel(hap_ref, annot_ref, alleles_ref, far_ref, close_ref, held, held_annots, sems):
    rows = hap_ref.shape[0]
    annot_rows = annot_ref.shape[0]
    size = rows // (2 * CHUNKS)
    starts = [side * (rows // 2) + chunk * size for chunk in range(CHUNKS) for side in range(2)]
    copies = [
        pltpu.make_async_copy(
            hap_ref.at[pl.ds(start, size)], held.at[pl.ds(start, size)], sems.at[number]
        )
        for number, start in enumerate(starts)
    ]
    copies.append(pltpu.make_async_copy(annot_ref, held_annots, sems.at[2 * CHUNKS]))
    for copy in copies:
        copy.start()
    part = far_ref.shape[0] - rows // 2
    odd = odd_block()

    def store(where, first, second):
        @pl.when(odd)
        def _():
            store_packed(close_ref, far_ref, where, first, second)

        @pl.when(jnp.logical_not(odd))
        def _():
            store_packed(far_ref, close_ref, where, first, second)

    for chunk in range(CHUNKS):
        pair = []
        for side in range(2):
            number = 2 * chunk + side
            copies[number].wait()
            where = slice(starts[number], starts[number] + size)
            values = held[where, :].astype(jnp.float32)
            alleles_ref[where, :] = values.astype(jnp.bfloat16)
            pair.append(values)
        store(slice(chunk * size, (chunk + 1) * size), *pair)
    copies[-1].wait()
    annots = jnp.concatenate(
        [
            held_annots[...].astype(jnp.float32),
            jnp.zeros((2 * part - annot_rows, annot_ref.shape[1]), jnp.float32),
        ],
        axis=0,
    )
    store(slice(rows // 2, rows // 2 + part), annots[:part], annots[part:])


def partner(group, step, groups):
    if groups & (groups - 1) == 0:
        return group ^ step
    return (group + step) % groups


def send_shares(groups, source, share, targets):
    me = lax.axis_index("hap")
    for step, target in enumerate(targets):
        group = partner(me, step, groups)
        rows = source[pl.ds(pl.multiple_of(group * share, 8), share), :]
        target[0:share, :] = rows.astype(target.dtype)


def own_kernel(groups, share, alleles_ref, label_ref, *refs):
    weighted_ref, totals_ref, *targets = refs[: 2 + groups]
    tile, folded = refs[2 + groups :]
    rows, snps = alleles_ref.shape
    half = snps // 2
    weight = jnp.where(label_ref[...] > 0, float(BASE), 1.0)
    weighted_ref[0:snps, :] = alleles_ref[...].T * weight.astype(jnp.bfloat16)
    extra = weighted_ref.shape[0] - snps
    weighted_ref[snps:, :] = jnp.broadcast_to(weight, (extra, rows)).astype(jnp.bfloat16)
    tile[...] = jnp.dot(weighted_ref[...], alleles_ref[...], preferred_element_type=jnp.float32)
    count = jnp.sum(weight, axis=1, keepdims=True)
    totals_ref[...] = jnp.concatenate(
        [tile[snps : snps + 1, :], jnp.broadcast_to(count, (1, snps)), jnp.zeros((6, snps))], axis=0
    )
    row, col = iota((half, snps), 0), iota((half, snps), 1)
    moved = (col < half) | (col - half > row)
    turned = pltpu.roll(tile[0:half, :], half, 1)
    folded[0:half, :] = to_fields(jnp.where(moved, turned, tile[half:snps, :]))
    if folded.shape[0] > half:
        folded[half:, :] = jnp.zeros((folded.shape[0] - half, snps), jnp.int32)
    send_shares(groups, folded, share, targets)


LEFT_BLOCKS = ((0, 1, 2, 3), (2, 3, 6, 7), (4, 0, 1, 2), (6, 0, 4, 5))
RIGHT_BLOCKS = ((2, 3, 6, 7), (4, 5, 6, 7), (0, 1, 2, 4), (0, 4, 5, 6))


def fold_by_column(tile, flipped, folded):
    owners = len(LEFT_BLOCKS)
    snps = folded.shape[1]
    wide = snps // owners
    size = wide // 2
    shape = (size, snps)
    row, lane = iota(shape, 0), iota(shape, 1)

    def block(number):
        return tile[number * size : (number + 1) * size, :]

    diagonal = block(0)
    for number in range(1, 2 * owners):
        diagonal = jnp.where(lane >= number * size, block(number), diagonal)
    flipped[:, 0:size] = diagonal.T
    corner = diagonal
    for owner in range(owners):
        start = (2 * owner + 1) * size
        turned = jnp.concatenate(
            [flipped[start : start + size, :], jnp.zeros((size, snps - LANES), jnp.float32)], axis=1
        )
        if owner:
            turned = pltpu.roll(turned, owner * wide, 1)
        inside = lane - owner * wide
        other = (row <= inside) if owner < owners // 2 else (row >= inside)
        corner = jnp.where((inside >= 0) & (inside < size) & other, turned, corner)
    rolled = []
    for shift in range(owners):
        mixed = None
        for owner in range(owners):
            slot = (owner + shift) % owners
            left = block(LEFT_BLOCKS[owner][slot]) if slot else corner
            start = owner * wide
            mixed = left if mixed is None else jnp.where(lane >= start, left, mixed)
            mixed = jnp.where(lane >= start + size, block(RIGHT_BLOCKS[owner][slot]), mixed)
        rolled.append(pltpu.roll(mixed, shift * wide, 1) if shift else mixed)
    for owner in range(owners):
        mixed = rolled[(0 - owner) % owners]
        for slot in range(1, owners):
            mixed = jnp.where(lane >= slot * wide, rolled[(slot - owner) % owners], mixed)
        folded[owner * size : (owner + 1) * size, :] = to_fields(mixed)


def above(far):
    return odd_block() == far


def side_dot(far, weighted_ref, side_ref, near):
    half = near.shape[0] // 2
    mixed = side_ref[0:half, 2 * LANES :]
    turned = pltpu.roll(mixed.astype(jnp.float32), HALF_LANES, 1).astype(mixed.dtype)

    def fill(whole, shared):
        near[0:half, whole : whole + LANES] = side_ref[0:half, 0:LANES]
        near[half:, whole : whole + LANES] = side_ref[0:half, LANES : 2 * LANES]
        near[0:half, shared : shared + LANES] = mixed
        near[half:, shared : shared + LANES] = turned

    @pl.when(above(far))
    def _():
        fill(0, LANES)

    @pl.when(jnp.logical_not(above(far)))
    def _():
        fill(LANES, 0)

    return jnp.dot(weighted_ref[...], near[...], preferred_element_type=jnp.float32)


def close_kernel(weighted_ref, side_ref, window_ref, near):
    window_ref[...] = side_dot(False, weighted_ref, side_ref, near)


def far_kernel(groups, share, weighted_ref, side_ref, close_ref, totals_ref, *refs):
    own_parts, own_sum_ref = refs[:groups], refs[groups]
    targets, (near, window, tile, folded, flipped, extras) = refs[groups + 1 : 2 * groups + 1], refs[2 * groups + 1 :]
    snps = tile.shape[1]
    own_sum_ref[...] = sum((part[...] for part in own_parts[1:]), own_parts[0][...])
    window[...] = side_dot(True, weighted_ref, side_ref, near)
    left = iota((tile.shape[0], LANES), 1) < HALF_LANES

    def place(up, down):
        tile[:, 0:LANES] = up[:, 0:LANES]
        tile[:, LANES : 2 * LANES] = jnp.where(left, up[:, LANES:], down[:, 0:LANES])
        tile[:, 2 * LANES :] = down[:, LANES:]

    @pl.when(above(True))
    def _():
        place(window, close_ref)

    @pl.when(jnp.logical_not(above(True)))
    def _():
        place(close_ref, window)

    fold_by_column(tile, flipped, folded)
    square = (snps, snps)
    apart = jnp.sum(
        jnp.where(iota(square, 0) == iota(square, 1), tile[0:snps, :], 0.0), axis=0, keepdims=True
    )
    tiles = snps // LANES
    shared = [totals_ref[0:1, k * LANES : (k + 1) * LANES] for k in range(tiles)]
    shared.append(totals_ref[1:2, 0:LANES])
    by_column = jnp.concatenate([tile[snps : snps + 1, :], apart, jnp.zeros((6, snps))], axis=0)
    for owner in range(groups):
        start = owner * (snps // groups)
        columns = pltpu.roll(by_column, snps - start, 1) if owner else by_column
        extras[8 * owner : 8 * (owner + 1), :] = to_fields(
            jnp.concatenate(
                [*shared, columns[0:2, 0:LANES], jnp.zeros((6 - tiles - 1, LANES))], axis=0
            )
        )
    me = lax.axis_index("hap")
    for step, target in enumerate(targets):
        owner = partner(me, step, groups)
        counts = folded[pl.ds(pl.multiple_of(owner * share, 8), share), :]
        for k in range(tiles):
            target[k * share : (k + 1) * share, :] = counts[:, k * LANES : (k + 1) * LANES]
        target[tiles * share :, :] = extras[pl.ds(pl.multiple_of(owner * 8, 8), 8), :]


def near_kernel(groups, share, weighted_ref, far_ref, close_ref, totals_ref, *refs):
    own_parts, own_sum_ref = refs[:groups], refs[groups]
    targets, (near, tile, folded) = refs[groups + 1 : 2 * groups + 1], refs[2 * groups + 1 :]
    rows, snps = near.shape
    half = snps // 2
    odd = odd_block()

    def unpack(up_ref, down_ref):
        pieces = load_packed(up_ref[0 : rows // 2, :], down_ref[0 : rows // 2, :])
        for side in range(2):
            where = slice(side * (rows // 2), (side + 1) * (rows // 2))
            for number in range(3):
                near[where, number * LANES : (number + 1) * LANES] = pieces[side][number]

    @pl.when(odd)
    def _():
        unpack(far_ref, close_ref)

    @pl.when(jnp.logical_not(odd))
    def _():
        unpack(close_ref, far_ref)

    tile[...] = jnp.dot(weighted_ref[...], near[...], preferred_element_type=jnp.float32)
    row, col = iota((half, snps), 0), iota((half, snps), 1)
    moved = (col >= half) & (col - half < row)
    turned = pltpu.roll(tile[0:half, :], half, 1)
    folded[0:half, :] = to_fields(jnp.where(moved, turned, tile[half:snps, :]))
    if folded.shape[0] > half:
        folded[half:, :] = jnp.zeros((folded.shape[0] - half, snps), jnp.int32)
    square = (snps, snps)
    far = jnp.sum(
        jnp.where(iota(square, 0) == iota(square, 1), tile[0:snps, :], 0.0), axis=0, keepdims=True
    )
    extras = to_fields(
        jnp.concatenate(
            [totals_ref[0:2, :], tile[snps : snps + 1, :], far, jnp.zeros((4, snps))], axis=0
        )
    )
    send_shares(groups, folded, share, targets)
    for target in targets:
        target[share:, :] = extras
    own_sum_ref[...] = sum((part[...] for part in own_parts[1:]), own_parts[0][...])


def annots_kernel(annot_ref, far_ref, close_ref, own_ref, near_ref):
    snps = annot_ref.shape[1]
    part = far_ref.shape[0]
    wide = 2 * part
    own = annot_ref[...].astype(jnp.float32)
    own = jnp.concatenate([own, jnp.zeros((LANES - own.shape[0], snps), jnp.float32)], axis=0)
    own_ref[...] = own.T
    odd = odd_block()
    far, close = far_ref[...].astype(jnp.float32), close_ref[...].astype(jnp.float32)
    first, second = load_packed(jnp.where(odd, far, close), jnp.where(odd, close, far))
    near = jnp.concatenate(
        [
            jnp.concatenate([piece.astype(jnp.float32) for piece in first], axis=1),
            jnp.concatenate([piece.astype(jnp.float32) for piece in second], axis=1),
            jnp.zeros((LANES - wide, snps), jnp.float32),
        ],
        axis=0,
    )
    near_ref[...] = near.T


def column_stats(totals, count):
    size = jnp.maximum(count, 1.0)
    frequency = totals / size
    variance = jnp.maximum(frequency * (1.0 - frequency), VARIANCE_FLOOR)
    inverse = 1.0 / jnp.sqrt(size * variance)
    low = ((0.0 - frequency) * inverse).astype(jnp.bfloat16).astype(jnp.float32)
    high = ((1.0 - frequency) * inverse).astype(jnp.bfloat16).astype(jnp.float32)
    step = high - low
    root = 1.0 / jnp.sqrt(size)
    return step, step * totals * root, (low * count + step * totals) * root


def correlation(row, col, count):
    return row[0] * col[0] * count - row[1] * col[1] + row[2] * col[2]


def split(values):
    high = values.astype(jnp.bfloat16)
    return high, (values - high.astype(jnp.float32)).astype(jnp.bfloat16)


def dot_split(values, right, axis):
    dims = (((axis,), (0,)), ((), ()))
    return sum(
        lax.dot_general(part, right, dims, preferred_element_type=jnp.float32)
        for part in split(values)
    )


def score_kernel(groups, share, reach_ref, *refs):
    own_sum_ref, near_parts = refs[0], refs[1 : groups + 1]
    annot_ref, near_annot_ref = refs[groups + 1 : groups + 3]
    targets = refs[groups + 3 : 2 * groups + 3]
    table, annots, near_annots, scores = refs[2 * groups + 3 :]
    snps = annot_ref.shape[0]
    half = snps // 2
    out_share = snps // groups
    me = lax.axis_index("hap")
    block = lax.axis_index("snp")
    last = reach_ref.shape[0] - 1
    reach_here = reach_ref[block]
    reach_up = reach_ref[jnp.minimum(block + 1, last)]
    reach_down = reach_ref[jnp.maximum(block - 1, 0)]

    own_counts = own_sum_ref[...]
    near_sums = sum((part[...] for part in near_parts[1:]), near_parts[0][...])
    extras = from_fields(near_sums[share:, :])
    near_counts = near_sums[0:share, :]

    own_stats, near_stats, lines = [], [], []
    for pop in range(2):
        count = extras[pop][1:2, :]
        own_stats.append(column_stats(extras[pop][0:1, :], count))
        near_stats.append(column_stats(extras[pop][2:3, :], count))
        lines += [*own_stats[pop], *near_stats[pop], extras[pop][0:1, :], extras[pop][3:4, :]]
    by_row = jnp.concatenate(lines, axis=0).T
    table[0:snps, 0:16] = by_row
    if table.shape[0] > snps:
        table[snps:, 0:16] = jnp.zeros((table.shape[0] - snps, 16), jnp.float32)
    annots[0:snps, :] = annot_ref[...]
    near_annots[0:snps, :] = near_annot_ref[...]
    if annots.shape[0] > snps:
        annots[snps:, :] = jnp.zeros((annots.shape[0] - snps, LANES), jnp.float32)

    low_rows = pl.multiple_of(me * share, 8)
    high_rows = pl.multiple_of(half + me * share, 8)

    def both(ref):
        return jnp.concatenate([ref[pl.ds(low_rows, share), :], ref[pl.ds(high_rows, share), :]], axis=0)

    here = both(table)
    own_count = jnp.concatenate([pltpu.roll(own_counts, half, 1), own_counts], axis=0)
    near_count = jnp.concatenate([pltpu.roll(near_counts, half, 1), near_counts], axis=0)
    shape = (2 * share, snps)
    local, col = iota(shape, 0), iota(shape, 1)
    low = local < share
    place = jnp.where(low, local, local - share) + me * share
    row = jnp.where(low, place, place + half)
    own_fields, near_fields = from_fields(own_count), from_fields(near_count)
    own_product, near_product = 1.0, 1.0
    for pop in range(2):
        row_stats = [here[:, 8 * pop + k : 8 * pop + k + 1] for k in range(3)]
        own_product *= correlation(row_stats, own_stats[pop], own_fields[pop])
        near_product *= correlation(row_stats, near_stats[pop], near_fields[pop])
    real = place < half
    own_inside = real & ((low & (col > row)) | (~low & (col >= half) & (col < row)))
    own_inside &= jnp.abs(col - row) <= reach_here
    own_kept = jnp.where(own_inside, own_product, 0.0)
    in_upper = col < half
    near_inside = real & ((low & (col < row)) | (~low & (in_upper | (col > row))))
    distance = jnp.where(in_upper, snps + col - row, snps + row - col)
    near_here = jnp.where(near_inside & (distance <= reach_here), near_product, 0.0)
    reach_there = jnp.where(in_upper, reach_up, reach_down)
    near_there = jnp.where(near_inside & (distance <= reach_there), near_product, 0.0)

    rows_here = both(annots)
    rows_there = pltpu.roll(rows_here, HALF_LANES, 1)
    scores[0:snps, :] = dot_split(
        jnp.concatenate([own_kept, near_there], axis=0),
        jnp.concatenate([rows_here, rows_there], axis=0).astype(jnp.bfloat16),
        0,
    )
    direct = dot_split(
        jnp.concatenate([own_kept, near_here], axis=1),
        jnp.concatenate([annot_ref[...], near_annot_ref[...]], axis=0).astype(jnp.bfloat16),
        1,
    )
    scores[pl.ds(low_rows, share), :] += direct[0:share, :]
    scores[pl.ds(high_rows, share), :] += direct[share:, :]

    out_rows = pl.ds(pl.multiple_of(me * out_share, 8), out_share)
    mine = table[out_rows, :]
    self_product, far_product = 1.0, 1.0
    for pop in range(2):
        k = 8 * pop
        own_row = [mine[:, k + s : k + s + 1] for s in range(3)]
        near_row = [mine[:, k + 3 + s : k + 4 + s] for s in range(3)]
        self_product *= correlation(own_row, own_row, mine[:, k + 6 : k + 7])
        far_product *= correlation(own_row, near_row, mine[:, k + 7 : k + 8])
    mine_annots = annots[out_rows, :]
    far_reach = jnp.where(me < groups // 2, reach_up, reach_down)
    scores[out_rows, :] += (
        mine_annots * self_product
        + near_annots[out_rows, :] * jnp.where(reach_here >= snps, far_product, 0.0)
        + pltpu.roll(mine_annots, HALF_LANES, 1) * jnp.where(far_reach >= snps, far_product, 0.0)
    )
    send_shares(groups, scores, out_share, targets)


def pack_halves(values):
    half = values.shape[0] // 2
    left = iota((half, LANES), 1) < HALF_LANES
    return jnp.where(left, values[0:half], pltpu.roll(values[half:], HALF_LANES, 1))


def unpack_halves(packed):
    return jnp.concatenate([packed, pltpu.roll(packed, HALF_LANES, 1)], axis=0)


def dot_rounded(values, right, axis):
    dims = (((axis,), (0,)), ((), ()))
    return lax.dot_general(
        values.astype(jnp.bfloat16), right, dims, preferred_element_type=jnp.float32
    )


def column_score_kernel(groups, share, reach_ref, *refs):
    own_sum_ref, near_parts = refs[0], refs[1 : groups + 1]
    annot_ref, near_annot_ref = refs[groups + 1 : groups + 3]
    out_ref, *targets = refs[groups + 3 : 2 * groups + 3]
    near_out_ref, table, flipped, scores = refs[2 * groups + 3 :]
    snps = annot_ref.shape[0]
    half = snps // 2
    wide = snps // groups
    size = wide // 2
    me = lax.axis_index("hap")
    block = lax.axis_index("snp")
    last = reach_ref.shape[0] - 1
    upper = me < groups // 2
    reach_here = reach_ref[block]
    reach_there = jnp.where(
        upper, reach_ref[jnp.minimum(block + 1, last)], reach_ref[jnp.maximum(block - 1, 0)]
    )

    def mine(choices):
        value = choices[0]
        for group in range(1, groups):
            value = jnp.where(me == group, choices[group], value)
        return value

    own_counts = own_sum_ref[...]
    near_sums = sum((part[...] for part in near_parts[1:]), near_parts[0][...])
    tiles = snps // LANES
    near_counts = jnp.concatenate(
        [near_sums[k * share : (k + 1) * share, :] for k in range(tiles)], axis=1
    )
    extras = from_fields(near_sums[tiles * share :, :])

    own_stats, near_stats, lines, near_lines = [], [], [], []
    for pop in range(2):
        count = extras[pop][tiles : tiles + 1, :]
        totals = jnp.concatenate([extras[pop][k : k + 1, :] for k in range(tiles)], axis=1)
        own_stats.append(column_stats(totals, jnp.concatenate([count] * tiles, axis=1)))
        near_stats.append(column_stats(extras[pop][tiles + 1 : tiles + 2, :], count))
        lines += [*own_stats[pop], totals]
        near_lines += [*near_stats[pop], extras[pop][tiles + 2 : tiles + 3, :]]
    table[:, 0:8] = jnp.concatenate(lines, axis=0).T
    near_table = jnp.concatenate(near_lines, axis=0).T[0:wide, :]

    low_rows = pl.multiple_of(me * share, 8)
    high_rows = pl.multiple_of(half + me * share, 8)

    def both(ref):
        return jnp.concatenate([ref[pl.ds(low_rows, share), :], ref[pl.ds(high_rows, share), :]], axis=0)

    here = both(table)
    own_fields = from_fields(
        jnp.concatenate([pltpu.roll(own_counts, half, 1), own_counts], axis=0)
    )
    shape = (2 * share, snps)
    local, col = iota(shape, 0), iota(shape, 1)
    low = local < share
    row = jnp.where(low, local, local + half - share) + me * share
    product = 1.0
    for pop in range(2):
        row_stats = [here[:, 4 * pop + k : 4 * pop + k + 1] for k in range(3)]
        product *= correlation(row_stats, own_stats[pop], own_fields[pop])
    inside = (low & (col > row)) | (~low & (col >= half) & (col < row))
    own_kept = jnp.where(inside & (jnp.abs(col - row) <= reach_here), product, 0.0)
    rows_here = both(annot_ref).astype(jnp.bfloat16)
    scores[...] = dot_rounded(own_kept, rows_here, 0)
    direct = dot_rounded(own_kept, annot_ref[...].astype(jnp.bfloat16), 1)
    scores[pl.ds(low_rows, share), :] += direct[0:share, :]
    scores[pl.ds(high_rows, share), :] += direct[share:, :]

    slots = [near_counts[:, 0:LANES]]
    for slot in range(1, groups):
        slots.append(pltpu.roll(near_counts, snps - slot * wide, 1)[:, 0:LANES])
    flipped[:, 0:size] = slots[0].T
    slots.append(pltpu.roll(flipped[0:size, :], size, 1))
    left_places = [mine([LEFT_BLOCKS[g][slot] for g in range(groups)]) * size for slot in range(groups)]
    right_places = [mine([RIGHT_BLOCKS[g][slot] for g in range(groups)]) * size for slot in range(groups)]
    left_places.append(left_places[0])
    right_places.append((2 * me + 1) * size)

    def rows_of(ref, places):
        return [ref[pl.ds(pl.multiple_of(place, 8), size), :] for place in places]

    near_fields = from_fields(jnp.concatenate(slots, axis=0))
    left_table = jnp.concatenate(rows_of(table, left_places), axis=0)
    right_table = jnp.concatenate(rows_of(table, right_places), axis=0)
    local, lane = iota((size, LANES), 0), iota((size, LANES), 1)
    is_left = lane < size
    own_row = jnp.concatenate(
        [local + jnp.where(is_left, a, b) for a, b in zip(left_places, right_places)], axis=0
    )
    shape = own_row.shape
    lane = iota(shape, 1)
    is_left = lane < size
    apart = jnp.abs(own_row - (lane + me * wide))
    ahead = (own_row - (lane + me * wide)) * jnp.where(upper, 1, -1) > 0
    real = ahead & (lane < wide) & ((lane >= size) | (iota(shape, 0) < groups * size))
    product = 1.0
    for pop in range(2):
        row_stats = [
            jnp.where(
                is_left,
                left_table[:, 4 * pop + k : 4 * pop + k + 1],
                right_table[:, 4 * pop + k : 4 * pop + k + 1],
            )
            for k in range(3)
        ]
        product *= correlation(row_stats, near_stats[pop], near_fields[pop])
    near_here = jnp.where(real & (snps - apart <= reach_here), product, 0.0)
    near_there = jnp.where(real & (snps - apart <= reach_there), product, 0.0)

    def sides(values):
        return jnp.concatenate(
            [jnp.where(is_left, values, 0.0), jnp.where(is_left, 0.0, values)], axis=0
        )

    slice_rows = pl.ds(pl.multiple_of(me * wide, 8), wide)
    their_annots = near_annot_ref[slice_rows, :]
    columns = jnp.concatenate([their_annots, jnp.zeros((LANES - wide, LANES), jnp.float32)], axis=0)
    direct = dot_rounded(sides(near_here), columns.astype(jnp.bfloat16), 1)
    places = left_places + right_places
    for number, place in enumerate(places):
        scores[pl.ds(pl.multiple_of(place, 8), size), :] += direct[number * size : (number + 1) * size, :]
    own_rows = jnp.concatenate(rows_of(annot_ref, places), axis=0).astype(jnp.bfloat16)
    near_scores = dot_rounded(sides(near_there), own_rows, 0)[0:wide, :]

    mine_table = table[slice_rows, :]
    self_product, far_product = 1.0, 1.0
    for pop in range(2):
        own_row = [mine_table[:, 4 * pop + k : 4 * pop + k + 1] for k in range(4)]
        near_row = [near_table[:, 4 * pop + k : 4 * pop + k + 1] for k in range(4)]
        self_product *= correlation(own_row, own_row, own_row[3])
        far_product *= correlation(own_row, near_row, near_row[3])
    my_annots = annot_ref[slice_rows, :]
    out_ref[...] = (
        scores[slice_rows, :]
        + my_annots * self_product
        + their_annots * jnp.where(reach_here >= snps, far_product, 0.0)
    )
    near_scores += my_annots * jnp.where(reach_there >= snps, far_product, 0.0)
    near_out_ref[...] = pack_halves(near_scores)
    for step, target in enumerate(targets, 1):
        group = partner(me, step, groups)
        rows = scores[pl.ds(pl.multiple_of(group * wide, 8), wide), :]
        target[...] = pack_halves(rows).astype(target.dtype)


def column_finish_kernel(own_ref, *refs):
    *parts, there_ref, out_ref = refs
    packed = sum((part[...].astype(jnp.float32) for part in parts), there_ref[...])
    out_ref[...] = (own_ref[...] + unpack_halves(packed)).T[0 : out_ref.shape[0], :]


def sum_kernel(*refs):
    *parts, own_ref, there_ref = refs
    total = sum((part[...].astype(jnp.float32) for part in parts[1:]), parts[0][...])
    own_ref[...] = total
    half = there_ref.shape[0]
    left = iota((half, LANES), 1) < HALF_LANES
    second = total[half:]
    if second.shape[0] < half:
        second = jnp.concatenate([second, jnp.zeros((half - second.shape[0], LANES))], axis=0)
    there_ref[...] = jnp.where(left, pltpu.roll(total[0:half], HALF_LANES, 1), second)


def finish_kernel(own_ref, there_ref, out_ref):
    annots, rows = out_ref.shape
    there = there_ref[...]
    there = jnp.concatenate([there, pltpu.roll(there, HALF_LANES, 1)], axis=0)
    out_ref[...] = (own_ref[...] + there[0:rows]).T[0:annots, :]


def around(value, groups, step):
    return lax.ppermute(
        value, "hap", [(source, partner(source, step, groups)) for source in range(groups)]
    )


def swapped(value, first):
    pairs = []
    for block in range(first, lax.axis_size("snp") - 1, 2):
        pairs += [(block, block + 1), (block + 1, block)]
    return lax.ppermute(value, "snp", pairs)


def per_device(haplotypes, labels, annotations, reach):
    rows, snps = haplotypes.shape
    half = snps // 2
    groups = lax.axis_size("hap")
    blocks = lax.axis_size("snp")
    share = round_up(-(-half // groups), 16)
    folded_rows = share * groups
    out_share = snps // groups
    padded = half + folded_rows
    annot_part = 32
    bf16, f32, i32 = jnp.bfloat16, jnp.float32, jnp.int32
    shape = jax.ShapeDtypeStruct

    packed = shape((rows // 2 + annot_part, snps), bf16)
    haplotypes = pltpu.with_memory_space_constraint(haplotypes, pltpu.HBM)
    annots_in = pltpu.with_memory_space_constraint(annotations, pltpu.HBM)
    alleles, far, close = call(
        prepare_kernel,
        [shape((rows, snps), bf16), packed, packed],
        [HBM, HBM],
        [
            pltpu.VMEM((rows, snps), i32),
            pltpu.VMEM(annotations.shape, i32),
            pltpu.SemaphoreType.DMA((2 * CHUNKS + 1,)),
        ],
        moved=rows * snps * 8,
    )(haplotypes, annots_in)
    from_far = swapped(far, 1)
    from_close = swapped(close, 0)

    tile = pltpu.VMEM((snps + 16, snps), f32)
    folded = pltpu.VMEM((folded_rows, snps), i32)
    weighted, totals, *own_parts = call(
        functools.partial(own_kernel, groups, share),
        [shape((snps + 16, rows), bf16), shape((8, snps), f32)] + [shape((share, snps), i32)] * groups,
        [VMEM, VMEM],
        [tile, folded],
        flops=2 * rows * snps * snps,
        moved=rows * snps * 4,
    )(alleles, labels.reshape(1, rows))
    own_parts = [own_parts[0]] + [around(own_parts[k], groups, k) for k in range(groups - 1, 0, -1)]

    by_column = groups == len(LEFT_BLOCKS)
    near_shapes = [shape((share, snps), i32)] + [shape((share + 8, snps), i32)] * groups
    if by_column:
        near = pltpu.VMEM((rows, 2 * LANES), bf16)
        window = (snps + 16, 2 * LANES)
        work = dict(flops=4 * rows * snps * LANES, moved=rows * snps * 4)
        close_counts = call(close_kernel, shape(window, f32), [VMEM] * 2, [near], **work)(
            weighted, from_close
        )
        own_sum, *near_parts = call(
            functools.partial(far_kernel, groups, share),
            [near_shapes[0]] + [shape((share * (snps // LANES) + 8, LANES), i32)] * groups,
            [VMEM] * (4 + groups),
            [
                near,
                pltpu.VMEM(window, f32),
                tile,
                folded,
                pltpu.VMEM((snps, LANES), f32),
                pltpu.VMEM((8 * groups, LANES), i32),
            ],
            **work,
        )(weighted, from_far, close_counts, totals, *own_parts)
    else:
        own_sum, *near_parts = call(
            functools.partial(near_kernel, groups, share),
            near_shapes,
            [VMEM] * (4 + groups),
            [pltpu.VMEM((rows, snps), bf16), tile, folded],
            flops=2 * rows * snps * snps,
            moved=rows * snps * 4,
        )(weighted, from_far, from_close, totals, *own_parts)
    near_parts = [near_parts[0]] + [around(near_parts[k], groups, k) for k in range(groups - 1, 0, -1)]

    by_snp = shape((snps, LANES), f32)
    own_annots, near_annots = call(annots_kernel, [by_snp, by_snp], [VMEM] * 3, moved=1 << 20)(
        annotations, from_far[rows // 2 :], from_close[rows // 2 :]
    )
    pairs = []
    for block in range(blocks):
        for group in range(groups):
            target = block + 1 if group < groups // 2 else block - 1
            if 0 <= target < blocks:
                pairs.append((block * groups + group, target * groups + group))

    def to_neighbour(value):
        return lax.ppermute(value, ("snp", "hap"), pairs)

    result = shape((annotations.shape[0], out_share), f32)
    half_share = round_up(-(-out_share // 2), 8)
    own_share = shape((out_share, LANES), f32)
    packed_share = shape((half_share, LANES), f32)
    if by_column:
        own_scores, *scores, near_scores = call(
            functools.partial(column_score_kernel, groups, share),
            [own_share] + [shape((half_share, LANES), bf16)] * (groups - 1) + [packed_share],
            [SMEM] + [VMEM] * (groups + 3),
            [pltpu.VMEM((snps, LANES), f32), pltpu.VMEM((LANES, LANES), i32), pltpu.VMEM((snps, LANES), f32)],
            flops=1 << 26,
            moved=1 << 21,
        )(reach, own_sum, *near_parts, own_annots, near_annots)
        scores = [around(scores[k - 1], groups, k) for k in range(groups - 1, 0, -1)]
        there = to_neighbour(near_scores)
        return call(column_finish_kernel, result, [VMEM] * (groups + 1))(own_scores, *scores, there)

    tall = pltpu.VMEM((padded, LANES), f32)
    scores = call(
        functools.partial(score_kernel, groups, share),
        [own_share] + [shape((out_share, LANES), bf16)] * (groups - 1),
        [SMEM] + [VMEM] * (groups + 3),
        [tall, tall, tall, tall],
        flops=1 << 26,
        moved=1 << 21,
    )(reach, own_sum, *near_parts, own_annots, near_annots)
    scores = [scores[0]] + [around(scores[k], groups, k) for k in range(groups - 1, 0, -1)]
    own_scores, near_scores = call(sum_kernel, [own_share, packed_share], [VMEM] * groups)(*scores)
    return call(finish_kernel, result, [VMEM] * 2)(own_scores, to_neighbour(near_scores))


def solution(mesh):
    in_specs = (
        P("hap", ("parts", "snp")),
        P(("parts", "hap")),
        P(None, ("parts", "snp")),
        P("parts"),
    )
    out_specs = P(None, ("parts", "snp", "hap"))
    return jax.shard_map(
        per_device, mesh=mesh, in_specs=in_specs, out_specs=out_specs, check_vma=False
    )
```

```python
import functools

import jax
import jax.numpy as jnp
from jax import lax
from jax.experimental import pallas as pl
from jax.experimental.pallas import tpu as pltpu
from jax.sharding import PartitionSpec as P

VARIANCE_FLOOR = 0.01
BASE_BITS = 12
BASE = 1 << BASE_BITS
FIELD_BITS = 16
LANES = 128
HALF_LANES = LANES // 2
CHUNKS = 4
VMEM = pl.BlockSpec(memory_space=pltpu.VMEM)
SMEM = pl.BlockSpec(memory_space=pltpu.SMEM)
HBM = pl.BlockSpec(memory_space=pltpu.HBM)
VMEM_LIMIT = 24 * 1024 * 1024


def iota(shape, axis):
    return lax.broadcasted_iota(jnp.int32, shape, axis)


def round_up(value, step):
    return -(-value // step) * step


def to_fields(values):
    whole = values.astype(jnp.int32)
    return whole + (whole >> BASE_BITS) * ((1 << FIELD_BITS) - BASE)


def from_fields(packed):
    first = packed & ((1 << FIELD_BITS) - 1)
    second = lax.shift_right_logical(packed, FIELD_BITS)
    return first.astype(jnp.float32), second.astype(jnp.float32)


def call(kernel, out_shape, in_specs, scratch_shapes=(), flops=0, moved=0):
    several = isinstance(out_shape, (list, tuple))
    return pl.pallas_call(
        kernel,
        out_shape=out_shape,
        in_specs=in_specs,
        out_specs=[VMEM] * len(out_shape) if several else VMEM,
        scratch_shapes=list(scratch_shapes),
        compiler_params=pltpu.CompilerParams(vmem_limit_bytes=VMEM_LIMIT),
        cost_estimate=pl.CostEstimate(flops=flops, bytes_accessed=moved, transcendentals=0),
    )


def odd_block():
    return lax.rem(lax.axis_index("snp"), 2) == 1


def store_packed(up_ref, down_ref, where, first, second):
    left = iota((first.shape[0], LANES), 1) < HALF_LANES
    middle = first[:, LANES : 2 * LANES]
    turned = pltpu.roll(second[:, LANES : 2 * LANES], HALF_LANES, 1)
    for ref, side, mixed in (
        (up_ref, slice(0, LANES), jnp.where(left, middle, turned)),
        (down_ref, slice(2 * LANES, 3 * LANES), jnp.where(left, turned, middle)),
    ):
        ref[where, 0:LANES] = first[:, side].astype(jnp.bfloat16)
        ref[where, LANES : 2 * LANES] = second[:, side].astype(jnp.bfloat16)
        ref[where, 2 * LANES : 3 * LANES] = mixed.astype(jnp.bfloat16)


def load_packed(up, down):
    left = iota((up.shape[0], LANES), 1) < HALF_LANES
    up_mixed, down_mixed = up[:, 2 * LANES :], down[:, 2 * LANES :]
    first = jnp.where(left, up_mixed, down_mixed)
    second = jnp.where(left, down_mixed, up_mixed)
    second = pltpu.roll(second.astype(jnp.float32), HALF_LANES, 1).astype(second.dtype)
    return (
        (up[:, :LANES], first, down[:, :LANES]),
        (up[:, LANES : 2 * LANES], second, down[:, LANES : 2 * LANES]),
    )


def prepare_kernel(hap_ref, annot_ref, alleles_ref, far_ref, close_ref, held, held_annots, sems):
    rows = hap_ref.shape[0]
    annot_rows = annot_ref.shape[0]
    size = rows // (2 * CHUNKS)
    starts = [side * (rows // 2) + chunk * size for chunk in range(CHUNKS) for side in range(2)]
    copies = [
        pltpu.make_async_copy(
            hap_ref.at[pl.ds(start, size)], held.at[pl.ds(start, size)], sems.at[number]
        )
        for number, start in enumerate(starts)
    ]
    copies.append(pltpu.make_async_copy(annot_ref, held_annots, sems.at[2 * CHUNKS]))
    for copy in copies:
        copy.start()
    part = far_ref.shape[0] - rows // 2
    odd = odd_block()

    def store(where, first, second):
        @pl.when(odd)
        def _():
            store_packed(close_ref, far_ref, where, first, second)

        @pl.when(jnp.logical_not(odd))
        def _():
            store_packed(far_ref, close_ref, where, first, second)

    for chunk in range(CHUNKS):
        pair = []
        for side in range(2):
            number = 2 * chunk + side
            copies[number].wait()
            where = slice(starts[number], starts[number] + size)
            values = held[where, :].astype(jnp.float32)
            alleles_ref[where, :] = values.astype(jnp.bfloat16)
            pair.append(values)
        store(slice(chunk * size, (chunk + 1) * size), *pair)
    copies[-1].wait()
    annots = jnp.concatenate(
        [
            held_annots[...].astype(jnp.float32),
            jnp.zeros((2 * part - annot_rows, annot_ref.shape[1]), jnp.float32),
        ],
        axis=0,
    )
    store(slice(rows // 2, rows // 2 + part), annots[:part], annots[part:])


def partner(group, step, groups):
    if groups & (groups - 1) == 0:
        return group ^ step
    return (group + step) % groups


def send_shares(groups, source, share, targets):
    me = lax.axis_index("hap")
    for step, target in enumerate(targets):
        group = partner(me, step, groups)
        rows = source[pl.ds(pl.multiple_of(group * share, 8), share), :]
        target[0:share, :] = rows.astype(target.dtype)


def send_tiles(groups, source, share, targets):
    me = lax.axis_index("hap")
    for step, target in enumerate(targets):
        owner = partner(me, step, groups)
        counts = source[pl.ds(pl.multiple_of(owner * share, 8), share), :]
        for k in range(source.shape[1] // LANES):
            target[k * share : (k + 1) * share, :] = counts[:, k * LANES : (k + 1) * LANES]


def from_tiles(counts, share):
    tiles = counts.shape[0] // share
    return jnp.concatenate([counts[k * share : (k + 1) * share, :] for k in range(tiles)], axis=1)


def own_kernel(groups, share, alleles_ref, label_ref, *refs):
    weighted_ref, totals_ref, *targets = refs[: 2 + groups]
    tile, folded = refs[2 + groups :]
    rows, snps = alleles_ref.shape
    half = snps // 2
    weight = jnp.where(label_ref[...] > 0, float(BASE), 1.0)
    weighted_ref[0:snps, :] = alleles_ref[...].T * weight.astype(jnp.bfloat16)
    extra = weighted_ref.shape[0] - snps
    weighted_ref[snps:, :] = jnp.broadcast_to(weight, (extra, rows)).astype(jnp.bfloat16)
    tile[...] = jnp.dot(weighted_ref[...], alleles_ref[...], preferred_element_type=jnp.float32)
    count = jnp.sum(weight, axis=1, keepdims=True)
    totals_ref[...] = jnp.concatenate(
        [tile[snps : snps + 1, :], jnp.broadcast_to(count, (1, snps)), jnp.zeros((6, snps))], axis=0
    )
    row, col = iota((half, snps), 0), iota((half, snps), 1)
    moved = (col < half) | (col - half > row)
    turned = pltpu.roll(tile[0:half, :], half, 1)
    folded[0:half, :] = to_fields(jnp.where(moved, turned, tile[half:snps, :]))
    if folded.shape[0] > half:
        folded[half:, :] = jnp.zeros((folded.shape[0] - half, snps), jnp.int32)
    if groups != len(LEFT_BLOCKS):
        send_shares(groups, folded, share, targets)
        return
    tiles = snps // LANES
    shared = [totals_ref[0:1, k * LANES : (k + 1) * LANES] for k in range(tiles)]
    shared += [totals_ref[1:2, 0:LANES], jnp.zeros((7 - tiles, LANES))]
    extras = to_fields(jnp.concatenate(shared, axis=0))
    send_tiles(groups, folded, share, targets)
    for target in targets:
        target[tiles * share :, :] = extras


LEFT_BLOCKS = ((0, 1, 2, 3), (2, 3, 6, 7), (4, 0, 1, 2), (6, 0, 4, 5))
RIGHT_BLOCKS = ((2, 3, 6, 7), (4, 5, 6, 7), (0, 1, 2, 4), (0, 4, 5, 6))


def fold_by_column(tile, flipped, folded):
    owners = len(LEFT_BLOCKS)
    snps = folded.shape[1]
    wide = snps // owners
    size = wide // 2
    shape = (size, snps)
    row, lane = iota(shape, 0), iota(shape, 1)

    def block(number):
        return tile[number * size : (number + 1) * size, :]

    diagonal = block(0)
    for number in range(1, 2 * owners):
        diagonal = jnp.where(lane >= number * size, block(number), diagonal)
    flipped[:, 0:size] = diagonal.T
    corner = diagonal
    for owner in range(owners):
        start = (2 * owner + 1) * size
        turned = jnp.concatenate(
            [flipped[start : start + size, :], jnp.zeros((size, snps - LANES), jnp.float32)], axis=1
        )
        if owner:
            turned = pltpu.roll(turned, owner * wide, 1)
        inside = lane - owner * wide
        other = (row <= inside) if owner < owners // 2 else (row >= inside)
        corner = jnp.where((inside >= 0) & (inside < size) & other, turned, corner)
    rolled = []
    for shift in range(owners):
        mixed = None
        for owner in range(owners):
            slot = (owner + shift) % owners
            left = block(LEFT_BLOCKS[owner][slot]) if slot else corner
            start = owner * wide
            mixed = left if mixed is None else jnp.where(lane >= start, left, mixed)
            mixed = jnp.where(lane >= start + size, block(RIGHT_BLOCKS[owner][slot]), mixed)
        rolled.append(pltpu.roll(mixed, shift * wide, 1) if shift else mixed)
    for owner in range(owners):
        mixed = rolled[(0 - owner) % owners]
        for slot in range(1, owners):
            mixed = jnp.where(lane >= slot * wide, rolled[(slot - owner) % owners], mixed)
        folded[owner * size : (owner + 1) * size, :] = to_fields(mixed)


def above(far):
    return odd_block() == far


def side_dot(far, weighted_ref, side_ref, near):
    half = near.shape[0] // 2
    mixed = side_ref[0:half, 2 * LANES :]
    turned = pltpu.roll(mixed.astype(jnp.float32), HALF_LANES, 1).astype(mixed.dtype)

    def fill(whole, shared):
        near[0:half, whole : whole + LANES] = side_ref[0:half, 0:LANES]
        near[half:, whole : whole + LANES] = side_ref[0:half, LANES : 2 * LANES]
        near[0:half, shared : shared + LANES] = mixed
        near[half:, shared : shared + LANES] = turned

    @pl.when(above(far))
    def _():
        fill(0, LANES)

    @pl.when(jnp.logical_not(above(far)))
    def _():
        fill(LANES, 0)

    return jnp.dot(weighted_ref[...], near[...], preferred_element_type=jnp.float32)


def close_kernel(weighted_ref, side_ref, window_ref, near):
    window_ref[...] = side_dot(False, weighted_ref, side_ref, near)


def far_kernel(groups, share, weighted_ref, side_ref, close_ref, totals_ref, *refs):
    own_parts, own_sum_ref = refs[:groups], refs[groups]
    targets, (near, window, tile, folded, flipped, extras) = refs[groups + 1 : 2 * groups + 1], refs[2 * groups + 1 :]
    snps = tile.shape[1]
    own_sum_ref[...] = sum((part[...] for part in own_parts[1:]), own_parts[0][...])
    window[...] = side_dot(True, weighted_ref, side_ref, near)
    left = iota((tile.shape[0], LANES), 1) < HALF_LANES

    def place(up, down):
        tile[:, 0:LANES] = up[:, 0:LANES]
        tile[:, LANES : 2 * LANES] = jnp.where(left, up[:, LANES:], down[:, 0:LANES])
        tile[:, 2 * LANES :] = down[:, LANES:]

    @pl.when(above(True))
    def _():
        place(window, close_ref)

    @pl.when(jnp.logical_not(above(True)))
    def _():
        place(close_ref, window)

    fold_by_column(tile, flipped, folded)
    square = (snps, snps)
    apart = jnp.sum(
        jnp.where(iota(square, 0) == iota(square, 1), tile[0:snps, :], 0.0), axis=0, keepdims=True
    )
    tiles = snps // LANES
    sizes = totals_ref[1:2, :]
    by_column = jnp.concatenate([sizes, tile[snps : snps + 1, :], apart, jnp.zeros((5, snps))], axis=0)
    for owner in range(groups):
        start = owner * (snps // groups)
        columns = pltpu.roll(by_column, snps - start, 1) if owner else by_column
        extras[8 * owner : 8 * (owner + 1), :] = to_fields(columns[:, 0:LANES])
    me = lax.axis_index("hap")
    send_tiles(groups, folded, share, targets)
    for step, target in enumerate(targets):
        owner = partner(me, step, groups)
        target[tiles * share :, :] = extras[pl.ds(pl.multiple_of(owner * 8, 8), 8), :]


def near_kernel(groups, share, weighted_ref, far_ref, close_ref, totals_ref, *refs):
    own_parts, own_sum_ref = refs[:groups], refs[groups]
    targets, (near, tile, folded) = refs[groups + 1 : 2 * groups + 1], refs[2 * groups + 1 :]
    rows, snps = near.shape
    half = snps // 2
    odd = odd_block()

    def unpack(up_ref, down_ref):
        pieces = load_packed(up_ref[0 : rows // 2, :], down_ref[0 : rows // 2, :])
        for side in range(2):
            where = slice(side * (rows // 2), (side + 1) * (rows // 2))
            for number in range(3):
                near[where, number * LANES : (number + 1) * LANES] = pieces[side][number]

    @pl.when(odd)
    def _():
        unpack(far_ref, close_ref)

    @pl.when(jnp.logical_not(odd))
    def _():
        unpack(close_ref, far_ref)

    tile[...] = jnp.dot(weighted_ref[...], near[...], preferred_element_type=jnp.float32)
    row, col = iota((half, snps), 0), iota((half, snps), 1)
    moved = (col >= half) & (col - half < row)
    turned = pltpu.roll(tile[0:half, :], half, 1)
    folded[0:half, :] = to_fields(jnp.where(moved, turned, tile[half:snps, :]))
    if folded.shape[0] > half:
        folded[half:, :] = jnp.zeros((folded.shape[0] - half, snps), jnp.int32)
    square = (snps, snps)
    far = jnp.sum(
        jnp.where(iota(square, 0) == iota(square, 1), tile[0:snps, :], 0.0), axis=0, keepdims=True
    )
    extras = to_fields(
        jnp.concatenate(
            [totals_ref[0:2, :], tile[snps : snps + 1, :], far, jnp.zeros((4, snps))], axis=0
        )
    )
    send_shares(groups, folded, share, targets)
    for target in targets:
        target[share:, :] = extras
    own_sum_ref[...] = sum((part[...] for part in own_parts[1:]), own_parts[0][...])


def annots_kernel(annot_ref, far_ref, close_ref, own_ref, near_ref):
    snps = annot_ref.shape[1]
    part = far_ref.shape[0]
    wide = 2 * part
    own = annot_ref[...].astype(jnp.float32)
    own = jnp.concatenate([own, jnp.zeros((LANES - own.shape[0], snps), jnp.float32)], axis=0)
    own_ref[...] = own.T
    odd = odd_block()
    far, close = far_ref[...].astype(jnp.float32), close_ref[...].astype(jnp.float32)
    first, second = load_packed(jnp.where(odd, far, close), jnp.where(odd, close, far))
    near = jnp.concatenate(
        [
            jnp.concatenate([piece.astype(jnp.float32) for piece in first], axis=1),
            jnp.concatenate([piece.astype(jnp.float32) for piece in second], axis=1),
            jnp.zeros((LANES - wide, snps), jnp.float32),
        ],
        axis=0,
    )
    near_ref[...] = near.T


def column_stats(totals, count):
    size = jnp.maximum(count, 1.0)
    frequency = totals / size
    variance = jnp.maximum(frequency * (1.0 - frequency), VARIANCE_FLOOR)
    inverse = 1.0 / jnp.sqrt(size * variance)
    low = ((0.0 - frequency) * inverse).astype(jnp.bfloat16).astype(jnp.float32)
    high = ((1.0 - frequency) * inverse).astype(jnp.bfloat16).astype(jnp.float32)
    step = high - low
    root = 1.0 / jnp.sqrt(size)
    return step, step * totals * root, (low * count + step * totals) * root


def correlation(row, col, count):
    return row[0] * col[0] * count - row[1] * col[1] + row[2] * col[2]


def split(values):
    high = values.astype(jnp.bfloat16)
    return high, (values - high.astype(jnp.float32)).astype(jnp.bfloat16)


def dot_split(values, right, axis):
    dims = (((axis,), (0,)), ((), ()))
    return sum(
        lax.dot_general(part, right, dims, preferred_element_type=jnp.float32)
        for part in split(values)
    )


def score_kernel(groups, share, reach_ref, *refs):
    own_sum_ref, near_parts = refs[0], refs[1 : groups + 1]
    annot_ref, near_annot_ref = refs[groups + 1 : groups + 3]
    targets = refs[groups + 3 : 2 * groups + 3]
    table, annots, near_annots, scores = refs[2 * groups + 3 :]
    snps = annot_ref.shape[0]
    half = snps // 2
    out_share = snps // groups
    me = lax.axis_index("hap")
    block = lax.axis_index("snp")
    last = reach_ref.shape[0] - 1
    reach_here = reach_ref[block]
    reach_up = reach_ref[jnp.minimum(block + 1, last)]
    reach_down = reach_ref[jnp.maximum(block - 1, 0)]

    own_counts = own_sum_ref[...]
    near_sums = sum((part[...] for part in near_parts[1:]), near_parts[0][...])
    extras = from_fields(near_sums[share:, :])
    near_counts = near_sums[0:share, :]

    own_stats, near_stats, lines = [], [], []
    for pop in range(2):
        count = extras[pop][1:2, :]
        own_stats.append(column_stats(extras[pop][0:1, :], count))
        near_stats.append(column_stats(extras[pop][2:3, :], count))
        lines += [*own_stats[pop], *near_stats[pop], extras[pop][0:1, :], extras[pop][3:4, :]]
    by_row = jnp.concatenate(lines, axis=0).T
    table[0:snps, 0:16] = by_row
    if table.shape[0] > snps:
        table[snps:, 0:16] = jnp.zeros((table.shape[0] - snps, 16), jnp.float32)
    annots[0:snps, :] = annot_ref[...]
    near_annots[0:snps, :] = near_annot_ref[...]
    if annots.shape[0] > snps:
        annots[snps:, :] = jnp.zeros((annots.shape[0] - snps, LANES), jnp.float32)

    low_rows = pl.multiple_of(me * share, 8)
    high_rows = pl.multiple_of(half + me * share, 8)

    def both(ref):
        return jnp.concatenate([ref[pl.ds(low_rows, share), :], ref[pl.ds(high_rows, share), :]], axis=0)

    here = both(table)
    own_count = jnp.concatenate([pltpu.roll(own_counts, half, 1), own_counts], axis=0)
    near_count = jnp.concatenate([pltpu.roll(near_counts, half, 1), near_counts], axis=0)
    shape = (2 * share, snps)
    local, col = iota(shape, 0), iota(shape, 1)
    low = local < share
    place = jnp.where(low, local, local - share) + me * share
    row = jnp.where(low, place, place + half)
    own_fields, near_fields = from_fields(own_count), from_fields(near_count)
    own_product, near_product = 1.0, 1.0
    for pop in range(2):
        row_stats = [here[:, 8 * pop + k : 8 * pop + k + 1] for k in range(3)]
        own_product *= correlation(row_stats, own_stats[pop], own_fields[pop])
        near_product *= correlation(row_stats, near_stats[pop], near_fields[pop])
    real = place < half
    own_inside = real & ((low & (col > row)) | (~low & (col >= half) & (col < row)))
    own_inside &= jnp.abs(col - row) <= reach_here
    own_kept = jnp.where(own_inside, own_product, 0.0)
    in_upper = col < half
    near_inside = real & ((low & (col < row)) | (~low & (in_upper | (col > row))))
    distance = jnp.where(in_upper, snps + col - row, snps + row - col)
    near_here = jnp.where(near_inside & (distance <= reach_here), near_product, 0.0)
    reach_there = jnp.where(in_upper, reach_up, reach_down)
    near_there = jnp.where(near_inside & (distance <= reach_there), near_product, 0.0)

    rows_here = both(annots)
    rows_there = pltpu.roll(rows_here, HALF_LANES, 1)
    scores[0:snps, :] = dot_split(
        jnp.concatenate([own_kept, near_there], axis=0),
        jnp.concatenate([rows_here, rows_there], axis=0).astype(jnp.bfloat16),
        0,
    )
    direct = dot_split(
        jnp.concatenate([own_kept, near_here], axis=1),
        jnp.concatenate([annot_ref[...], near_annot_ref[...]], axis=0).astype(jnp.bfloat16),
        1,
    )
    scores[pl.ds(low_rows, share), :] += direct[0:share, :]
    scores[pl.ds(high_rows, share), :] += direct[share:, :]

    out_rows = pl.ds(pl.multiple_of(me * out_share, 8), out_share)
    mine = table[out_rows, :]
    self_product, far_product = 1.0, 1.0
    for pop in range(2):
        k = 8 * pop
        own_row = [mine[:, k + s : k + s + 1] for s in range(3)]
        near_row = [mine[:, k + 3 + s : k + 4 + s] for s in range(3)]
        self_product *= correlation(own_row, own_row, mine[:, k + 6 : k + 7])
        far_product *= correlation(own_row, near_row, mine[:, k + 7 : k + 8])
    mine_annots = annots[out_rows, :]
    far_reach = jnp.where(me < groups // 2, reach_up, reach_down)
    scores[out_rows, :] += (
        mine_annots * self_product
        + near_annots[out_rows, :] * jnp.where(reach_here >= snps, far_product, 0.0)
        + pltpu.roll(mine_annots, HALF_LANES, 1) * jnp.where(far_reach >= snps, far_product, 0.0)
    )
    send_shares(groups, scores, out_share, targets)


def pack_halves(values):
    half = values.shape[0] // 2
    left = iota((half, LANES), 1) < HALF_LANES
    return jnp.where(left, values[0:half], pltpu.roll(values[half:], HALF_LANES, 1))


def unpack_halves(packed):
    return jnp.concatenate([packed, pltpu.roll(packed, HALF_LANES, 1)], axis=0)


def dot_rounded(values, right, axis):
    dims = (((axis,), (0,)), ((), ()))
    return lax.dot_general(
        values.astype(jnp.bfloat16), right, dims, preferred_element_type=jnp.float32
    )


def own_score_kernel(groups, share, reach_ref, own_sum_ref, annot_ref, scores, table):
    snps = annot_ref.shape[0]
    half = snps // 2
    wide = snps // groups
    tiles = snps // LANES
    me = lax.axis_index("hap")
    reach_here = reach_ref[lax.axis_index("snp")]
    own_counts = from_tiles(own_sum_ref[0 : tiles * share, :], share)
    extras = from_fields(own_sum_ref[tiles * share :, :])

    own_stats, lines = [], []
    for pop in range(2):
        count = jnp.concatenate([extras[pop][tiles : tiles + 1, :]] * tiles, axis=1)
        totals = jnp.concatenate([extras[pop][k : k + 1, :] for k in range(tiles)], axis=1)
        own_stats.append(column_stats(totals, count))
        lines += [*own_stats[pop], totals]
    table[:, 0:8] = jnp.concatenate(lines, axis=0).T

    low_rows = pl.multiple_of(me * share, 8)
    high_rows = pl.multiple_of(half + me * share, 8)

    def both(ref):
        return jnp.concatenate([ref[pl.ds(low_rows, share), :], ref[pl.ds(high_rows, share), :]], axis=0)

    here = both(table)
    own_fields = from_fields(
        jnp.concatenate([pltpu.roll(own_counts, half, 1), own_counts], axis=0)
    )
    shape = (2 * share, snps)
    local, col = iota(shape, 0), iota(shape, 1)
    low = local < share
    row = jnp.where(low, local, local + half - share) + me * share
    product = 1.0
    for pop in range(2):
        row_stats = [here[:, 4 * pop + k : 4 * pop + k + 1] for k in range(3)]
        product *= correlation(row_stats, own_stats[pop], own_fields[pop])
    inside = (low & (col > row)) | (~low & (col >= half) & (col < row))
    own_kept = jnp.where(inside & (jnp.abs(col - row) <= reach_here), product, 0.0)
    rows_here = both(annot_ref).astype(jnp.bfloat16)
    scores[...] = dot_rounded(own_kept, rows_here, 0)
    direct = dot_rounded(own_kept, annot_ref[...].astype(jnp.bfloat16), 1)
    scores[pl.ds(low_rows, share), :] += direct[0:share, :]
    scores[pl.ds(high_rows, share), :] += direct[share:, :]

    slice_rows = pl.ds(pl.multiple_of(me * wide, 8), wide)
    mine = table[slice_rows, :]
    product = 1.0
    for pop in range(2):
        own_row = [mine[:, 4 * pop + k : 4 * pop + k + 1] for k in range(4)]
        product *= correlation(own_row, own_row, own_row[3])
    scores[slice_rows, :] += annot_ref[slice_rows, :] * product


def near_score_kernel(groups, share, reach_ref, *refs):
    near_parts, (own_ref, table, annot_ref, near_annot_ref) = refs[:groups], refs[groups : groups + 4]
    keep_ref, send_ref, near_out_ref, flipped, scores = refs[groups + 4 :]
    snps = annot_ref.shape[0]
    wide = snps // groups
    size = wide // 2
    tiles = snps // LANES
    me = lax.axis_index("hap")
    block = lax.axis_index("snp")
    last = reach_ref.shape[0] - 1
    upper = me < groups // 2
    reach_here = reach_ref[block]
    reach_there = jnp.where(
        upper, reach_ref[jnp.minimum(block + 1, last)], reach_ref[jnp.maximum(block - 1, 0)]
    )

    def mine(choices):
        value = choices[0]
        for group in range(1, groups):
            value = jnp.where(me == group, choices[group], value)
        return value

    scores[...] = own_ref[...]
    near_sums = sum((part[...] for part in near_parts[1:]), near_parts[0][...])
    near_counts = from_tiles(near_sums[0 : tiles * share, :], share)
    extras = from_fields(near_sums[tiles * share :, :])
    near_stats, near_lines = [], []
    for pop in range(2):
        near_stats.append(column_stats(extras[pop][1:2, :], extras[pop][0:1, :]))
        near_lines += [*near_stats[pop], extras[pop][2:3, :]]
    near_table = jnp.concatenate(near_lines, axis=0).T[0:wide, :]

    slots = [near_counts[:, 0:LANES]]
    for slot in range(1, groups):
        slots.append(pltpu.roll(near_counts, snps - slot * wide, 1)[:, 0:LANES])
    flipped[:, 0:size] = slots[0].T
    slots.append(pltpu.roll(flipped[0:size, :], size, 1))
    left_places = [mine([LEFT_BLOCKS[g][slot] for g in range(groups)]) * size for slot in range(groups)]
    right_places = [mine([RIGHT_BLOCKS[g][slot] for g in range(groups)]) * size for slot in range(groups)]
    left_places.append(left_places[0])
    right_places.append((2 * me + 1) * size)

    def rows_of(ref, places):
        return [ref[pl.ds(pl.multiple_of(place, 8), size), :] for place in places]

    near_fields = from_fields(jnp.concatenate(slots, axis=0))
    left_table = jnp.concatenate(rows_of(table, left_places), axis=0)
    right_table = jnp.concatenate(rows_of(table, right_places), axis=0)
    local, lane = iota((size, LANES), 0), iota((size, LANES), 1)
    is_left = lane < size
    own_row = jnp.concatenate(
        [local + jnp.where(is_left, a, b) for a, b in zip(left_places, right_places)], axis=0
    )
    shape = own_row.shape
    lane = iota(shape, 1)
    is_left = lane < size
    apart = jnp.abs(own_row - (lane + me * wide))
    ahead = (own_row - (lane + me * wide)) * jnp.where(upper, 1, -1) > 0
    real = ahead & (lane < wide) & ((lane >= size) | (iota(shape, 0) < groups * size))
    product = 1.0
    for pop in range(2):
        row_stats = [
            jnp.where(
                is_left,
                left_table[:, 4 * pop + k : 4 * pop + k + 1],
                right_table[:, 4 * pop + k : 4 * pop + k + 1],
            )
            for k in range(3)
        ]
        product *= correlation(row_stats, near_stats[pop], near_fields[pop])
    near_here = jnp.where(real & (snps - apart <= reach_here), product, 0.0)
    near_there = jnp.where(real & (snps - apart <= reach_there), product, 0.0)

    def sides(values):
        return jnp.concatenate(
            [jnp.where(is_left, values, 0.0), jnp.where(is_left, 0.0, values)], axis=0
        )

    slice_rows = pl.ds(pl.multiple_of(me * wide, 8), wide)
    their_annots = near_annot_ref[slice_rows, :]
    columns = jnp.concatenate([their_annots, jnp.zeros((LANES - wide, LANES), jnp.float32)], axis=0)
    direct = dot_rounded(sides(near_here), columns.astype(jnp.bfloat16), 1)
    places = left_places + right_places
    for number, place in enumerate(places):
        scores[pl.ds(pl.multiple_of(place, 8), size), :] += direct[number * size : (number + 1) * size, :]
    own_rows = jnp.concatenate(rows_of(annot_ref, places), axis=0).astype(jnp.bfloat16)
    near_scores = dot_rounded(sides(near_there), own_rows, 0)[0:wide, :]

    mine_table = table[slice_rows, :]
    far_product = 1.0
    for pop in range(2):
        own_row = [mine_table[:, 4 * pop + k : 4 * pop + k + 1] for k in range(3)]
        near_row = [near_table[:, 4 * pop + k : 4 * pop + k + 1] for k in range(4)]
        far_product *= correlation(own_row, near_row, near_row[3])
    scores[slice_rows, :] += their_annots * jnp.where(reach_here >= snps, far_product, 0.0)
    near_scores += annot_ref[slice_rows, :] * jnp.where(reach_there >= snps, far_product, 0.0)
    near_out_ref[...] = pack_halves(near_scores)

    def packed(step):
        group = partner(me, step, groups)
        return pack_halves(scores[pl.ds(pl.multiple_of(group * wide, 8), wide), :])

    for ref, steps in ((keep_ref, (0, 2)), (send_ref, (1, 3))):
        for number, step in enumerate(steps):
            ref[number * size : (number + 1) * size, :] = packed(step).astype(ref.dtype)


def middle_kernel(keep_ref, part_ref, mine_ref, send_ref):
    total = keep_ref[...] + part_ref[...].astype(jnp.float32)
    half = mine_ref.shape[0]
    mine_ref[...] = total[0:half]
    send_ref[...] = total[half:].astype(send_ref.dtype)


def column_finish_kernel(mine_ref, part_ref, there_ref, out_ref):
    packed = mine_ref[...] + part_ref[...].astype(jnp.float32) + there_ref[...]
    out_ref[...] = unpack_halves(packed).T[0 : out_ref.shape[0], :]


def sum_kernel(*refs):
    *parts, own_ref, there_ref = refs
    total = sum((part[...].astype(jnp.float32) for part in parts[1:]), parts[0][...])
    own_ref[...] = total
    half = there_ref.shape[0]
    left = iota((half, LANES), 1) < HALF_LANES
    second = total[half:]
    if second.shape[0] < half:
        second = jnp.concatenate([second, jnp.zeros((half - second.shape[0], LANES))], axis=0)
    there_ref[...] = jnp.where(left, pltpu.roll(total[0:half], HALF_LANES, 1), second)


def finish_kernel(own_ref, there_ref, out_ref):
    annots, rows = out_ref.shape
    there = there_ref[...]
    there = jnp.concatenate([there, pltpu.roll(there, HALF_LANES, 1)], axis=0)
    out_ref[...] = (own_ref[...] + there[0:rows]).T[0:annots, :]


def around(value, groups, step):
    return lax.ppermute(
        value, "hap", [(source, partner(source, step, groups)) for source in range(groups)]
    )


def swapped(value, first):
    pairs = []
    for block in range(first, lax.axis_size("snp") - 1, 2):
        pairs += [(block, block + 1), (block + 1, block)]
    return lax.ppermute(value, "snp", pairs)


def per_device(haplotypes, labels, annotations, reach):
    rows, snps = haplotypes.shape
    half = snps // 2
    groups = lax.axis_size("hap")
    blocks = lax.axis_size("snp")
    share = round_up(-(-half // groups), 16)
    folded_rows = share * groups
    out_share = snps // groups
    padded = half + folded_rows
    annot_part = 32
    bf16, f32, i32 = jnp.bfloat16, jnp.float32, jnp.int32
    shape = jax.ShapeDtypeStruct

    packed = shape((rows // 2 + annot_part, snps), bf16)
    haplotypes = pltpu.with_memory_space_constraint(haplotypes, pltpu.HBM)
    annots_in = pltpu.with_memory_space_constraint(annotations, pltpu.HBM)
    alleles, far, close = call(
        prepare_kernel,
        [shape((rows, snps), bf16), packed, packed],
        [HBM, HBM],
        [
            pltpu.VMEM((rows, snps), i32),
            pltpu.VMEM(annotations.shape, i32),
            pltpu.SemaphoreType.DMA((2 * CHUNKS + 1,)),
        ],
        moved=rows * snps * 8,
    )(haplotypes, annots_in)
    from_far = swapped(far, 1)
    from_close = swapped(close, 0)

    by_column = groups == len(LEFT_BLOCKS)
    compact = shape((share * (snps // LANES) + 8, LANES), i32)
    own_share_counts = compact if by_column else shape((share, snps), i32)
    tile = pltpu.VMEM((snps + 16, snps), f32)
    folded = pltpu.VMEM((folded_rows, snps), i32)
    weighted, totals, *own_parts = call(
        functools.partial(own_kernel, groups, share),
        [shape((snps + 16, rows), bf16), shape((8, snps), f32)] + [own_share_counts] * groups,
        [VMEM, VMEM],
        [tile, folded],
        flops=2 * rows * snps * snps,
        moved=rows * snps * 4,
    )(alleles, labels.reshape(1, rows))
    own_parts = [own_parts[0]] + [around(own_parts[k], groups, k) for k in range(groups - 1, 0, -1)]

    near_shapes = [own_share_counts] + [compact if by_column else shape((share + 8, snps), i32)] * groups
    if by_column:
        near = pltpu.VMEM((rows, 2 * LANES), bf16)
        window = (snps + 16, 2 * LANES)
        work = dict(flops=4 * rows * snps * LANES, moved=rows * snps * 4)
        close_counts = call(close_kernel, shape(window, f32), [VMEM] * 2, [near], **work)(
            weighted, from_close
        )
        own_sum, *near_parts = call(
            functools.partial(far_kernel, groups, share),
            near_shapes,
            [VMEM] * (4 + groups),
            [
                near,
                pltpu.VMEM(window, f32),
                tile,
                folded,
                pltpu.VMEM((snps, LANES), f32),
                pltpu.VMEM((8 * groups, LANES), i32),
            ],
            **work,
        )(weighted, from_far, close_counts, totals, *own_parts)
    else:
        own_sum, *near_parts = call(
            functools.partial(near_kernel, groups, share),
            near_shapes,
            [VMEM] * (4 + groups),
            [pltpu.VMEM((rows, snps), bf16), tile, folded],
            flops=2 * rows * snps * snps,
            moved=rows * snps * 4,
        )(weighted, from_far, from_close, totals, *own_parts)
    near_parts = [near_parts[0]] + [around(near_parts[k], groups, k) for k in range(groups - 1, 0, -1)]

    by_snp = shape((snps, LANES), f32)
    own_annots, near_annots = call(annots_kernel, [by_snp, by_snp], [VMEM] * 3, moved=1 << 20)(
        annotations, from_far[rows // 2 :], from_close[rows // 2 :]
    )
    pairs = []
    for block in range(blocks):
        for group in range(groups):
            target = block + 1 if group < groups // 2 else block - 1
            if 0 <= target < blocks:
                pairs.append((block * groups + group, target * groups + group))

    def to_neighbour(value):
        return lax.ppermute(value, ("snp", "hap"), pairs)

    result = shape((annotations.shape[0], out_share), f32)
    half_share = round_up(-(-out_share // 2), 8)
    own_share = shape((out_share, LANES), f32)
    packed_share = shape((half_share, LANES), f32)
    if by_column:
        own_scores, table = call(
            functools.partial(own_score_kernel, groups, share),
            [by_snp, by_snp],
            [SMEM, VMEM, VMEM],
            flops=1 << 25,
            moved=1 << 20,
        )(reach, own_sum, own_annots)
        both = (2 * half_share, LANES)
        keep, send, near_scores = call(
            functools.partial(near_score_kernel, groups, share),
            [shape(both, f32), shape(both, bf16), packed_share],
            [SMEM] + [VMEM] * (groups + 4),
            [pltpu.VMEM((LANES, LANES), i32), pltpu.VMEM((snps, LANES), f32)],
            flops=1 << 26,
            moved=1 << 21,
        )(reach, *near_parts, own_scores, table, own_annots, near_annots)
        part = around(send, groups, 1)
        there = to_neighbour(near_scores)
        mine, send = call(
            middle_kernel, [packed_share, shape((half_share, LANES), bf16)], [VMEM] * 2
        )(keep, part)
        part = around(send, groups, 2)
        return call(column_finish_kernel, result, [VMEM] * 3)(mine, part, there)

    tall = pltpu.VMEM((padded, LANES), f32)
    scores = call(
        functools.partial(score_kernel, groups, share),
        [own_share] + [shape((out_share, LANES), bf16)] * (groups - 1),
        [SMEM] + [VMEM] * (groups + 3),
        [tall, tall, tall, tall],
        flops=1 << 26,
        moved=1 << 21,
    )(reach, own_sum, *near_parts, own_annots, near_annots)
    scores = [scores[0]] + [around(scores[k], groups, k) for k in range(groups - 1, 0, -1)]
    own_scores, near_scores = call(sum_kernel, [own_share, packed_share], [VMEM] * groups)(*scores)
    return call(finish_kernel, result, [VMEM] * 2)(own_scores, to_neighbour(near_scores))


def solution(mesh):
    in_specs = (
        P("hap", ("parts", "snp")),
        P(("parts", "hap")),
        P(None, ("parts", "snp")),
        P("parts"),
    )
    out_specs = P(None, ("parts", "snp", "hap"))
    return jax.shard_map(
        per_device, mesh=mesh, in_specs=in_specs, out_specs=out_specs, check_vma=False
    )
```

```python
import functools

import jax
import jax.numpy as jnp
from jax import lax
from jax.experimental import pallas as pl
from jax.experimental.pallas import tpu as pltpu
from jax.sharding import PartitionSpec as P

VARIANCE_FLOOR = 0.01
BASE_BITS = 12
BASE = 1 << BASE_BITS
FIELD_BITS = 16
LANES = 128
HALF_LANES = LANES // 2
CHUNKS = 4
VMEM = pl.BlockSpec(memory_space=pltpu.VMEM)
SMEM = pl.BlockSpec(memory_space=pltpu.SMEM)
HBM = pl.BlockSpec(memory_space=pltpu.HBM)
VMEM_LIMIT = 24 * 1024 * 1024


def iota(shape, axis):
    return lax.broadcasted_iota(jnp.int32, shape, axis)


def round_up(value, step):
    return -(-value // step) * step


def to_fields(values):
    whole = values.astype(jnp.int32)
    return whole + (whole >> BASE_BITS) * ((1 << FIELD_BITS) - BASE)


def from_fields(packed):
    first = packed & ((1 << FIELD_BITS) - 1)
    second = lax.shift_right_logical(packed, FIELD_BITS)
    return first.astype(jnp.float32), second.astype(jnp.float32)


def call(kernel, out_shape, in_specs, scratch_shapes=(), flops=0, moved=0):
    several = isinstance(out_shape, (list, tuple))
    return pl.pallas_call(
        kernel,
        out_shape=out_shape,
        in_specs=in_specs,
        out_specs=[VMEM] * len(out_shape) if several else VMEM,
        scratch_shapes=list(scratch_shapes),
        compiler_params=pltpu.CompilerParams(vmem_limit_bytes=VMEM_LIMIT),
        cost_estimate=pl.CostEstimate(flops=flops, bytes_accessed=moved, transcendentals=0),
    )


def odd_block():
    return lax.rem(lax.axis_index("snp"), 2) == 1


def store_packed(up_ref, down_ref, where, first, second):
    left = iota((first.shape[0], LANES), 1) < HALF_LANES
    middle = first[:, LANES : 2 * LANES]
    turned = pltpu.roll(second[:, LANES : 2 * LANES], HALF_LANES, 1)
    for ref, side, mixed in (
        (up_ref, slice(0, LANES), jnp.where(left, middle, turned)),
        (down_ref, slice(2 * LANES, 3 * LANES), jnp.where(left, turned, middle)),
    ):
        ref[where, 0:LANES] = first[:, side].astype(jnp.bfloat16)
        ref[where, LANES : 2 * LANES] = mixed.astype(jnp.bfloat16)
        ref[where, 2 * LANES : 3 * LANES] = second[:, side].astype(jnp.bfloat16)


def load_packed(up, down):
    left = iota((up.shape[0], LANES), 1) < HALF_LANES
    up_mixed, down_mixed = up[:, LANES : 2 * LANES], down[:, LANES : 2 * LANES]
    first = jnp.where(left, up_mixed, down_mixed)
    second = jnp.where(left, down_mixed, up_mixed)
    second = pltpu.roll(second.astype(jnp.float32), HALF_LANES, 1).astype(second.dtype)
    return (
        (up[:, :LANES], first, down[:, :LANES]),
        (up[:, 2 * LANES :], second, down[:, 2 * LANES :]),
    )


def prepare_kernel(hap_ref, annot_ref, alleles_ref, far_ref, close_ref, held, held_annots, sems):
    rows = hap_ref.shape[0]
    annot_rows = annot_ref.shape[0]
    size = rows // (2 * CHUNKS)
    starts = [side * (rows // 2) + chunk * size for chunk in range(CHUNKS) for side in range(2)]
    copies = [
        pltpu.make_async_copy(
            hap_ref.at[pl.ds(start, size)], held.at[pl.ds(start, size)], sems.at[number]
        )
        for number, start in enumerate(starts)
    ]
    copies.append(pltpu.make_async_copy(annot_ref, held_annots, sems.at[2 * CHUNKS]))
    for copy in copies:
        copy.start()
    part = far_ref.shape[0] - rows // 2
    odd = odd_block()

    def store(where, first, second):
        @pl.when(odd)
        def _():
            store_packed(close_ref, far_ref, where, first, second)

        @pl.when(jnp.logical_not(odd))
        def _():
            store_packed(far_ref, close_ref, where, first, second)

    for chunk in range(CHUNKS):
        pair = []
        for side in range(2):
            number = 2 * chunk + side
            copies[number].wait()
            where = slice(starts[number], starts[number] + size)
            values = held[where, :].astype(jnp.float32)
            alleles_ref[where, :] = values.astype(jnp.bfloat16)
            pair.append(values)
        store(slice(chunk * size, (chunk + 1) * size), *pair)
    copies[-1].wait()
    annots = jnp.concatenate(
        [
            held_annots[...].astype(jnp.float32),
            jnp.zeros((2 * part - annot_rows, annot_ref.shape[1]), jnp.float32),
        ],
        axis=0,
    )
    store(slice(rows // 2, rows // 2 + part), annots[:part], annots[part:])


def partner(group, step, groups):
    if groups & (groups - 1) == 0:
        return group ^ step
    return (group + step) % groups


def send_shares(groups, source, share, targets):
    me = lax.axis_index("hap")
    for step, target in enumerate(targets):
        group = partner(me, step, groups)
        rows = source[pl.ds(pl.multiple_of(group * share, 8), share), :]
        target[0:share, :] = rows.astype(target.dtype)


def send_tiles(groups, source, share, targets):
    me = lax.axis_index("hap")
    for step, target in enumerate(targets):
        owner = partner(me, step, groups)
        counts = source[pl.ds(pl.multiple_of(owner * share, 8), share), :]
        for k in range(source.shape[1] // LANES):
            target[k * share : (k + 1) * share, :] = counts[:, k * LANES : (k + 1) * LANES]


def from_tiles(counts, share):
    tiles = counts.shape[0] // share
    return jnp.concatenate([counts[k * share : (k + 1) * share, :] for k in range(tiles)], axis=1)


def own_kernel(groups, share, alleles_ref, label_ref, *refs):
    weighted_ref, totals_ref, *targets = refs[: 2 + groups]
    tile, folded = refs[2 + groups :]
    rows, snps = alleles_ref.shape
    half = snps // 2
    weight = jnp.where(label_ref[...] > 0, float(BASE), 1.0)
    weighted_ref[0:snps, :] = alleles_ref[...].T * weight.astype(jnp.bfloat16)
    extra = weighted_ref.shape[0] - snps
    weighted_ref[snps:, :] = jnp.broadcast_to(weight, (extra, rows)).astype(jnp.bfloat16)
    tile[...] = jnp.dot(weighted_ref[...], alleles_ref[...], preferred_element_type=jnp.float32)
    count = jnp.sum(weight, axis=1, keepdims=True)
    totals_ref[...] = jnp.concatenate(
        [tile[snps : snps + 1, :], jnp.broadcast_to(count, (1, snps)), jnp.zeros((6, snps))], axis=0
    )
    row, col = iota((half, snps), 0), iota((half, snps), 1)
    moved = (col < half) | (col - half > row)
    turned = pltpu.roll(tile[0:half, :], half, 1)
    folded[0:half, :] = to_fields(jnp.where(moved, turned, tile[half:snps, :]))
    if folded.shape[0] > half:
        folded[half:, :] = jnp.zeros((folded.shape[0] - half, snps), jnp.int32)
    if groups != len(LEFT_BLOCKS):
        send_shares(groups, folded, share, targets)
        return
    tiles = snps // LANES
    shared = [totals_ref[0:1, k * LANES : (k + 1) * LANES] for k in range(tiles)]
    shared += [totals_ref[1:2, 0:LANES], jnp.zeros((7 - tiles, LANES))]
    extras = to_fields(jnp.concatenate(shared, axis=0))
    send_tiles(groups, folded, share, targets)
    for target in targets:
        target[tiles * share :, :] = extras


LEFT_BLOCKS = ((0, 1, 2, 3), (2, 3, 6, 7), (4, 0, 1, 2), (6, 0, 4, 5))
RIGHT_BLOCKS = ((2, 3, 6, 7), (4, 5, 6, 7), (0, 1, 2, 4), (0, 4, 5, 6))


def fold_by_column(tile, flipped, folded):
    owners = len(LEFT_BLOCKS)
    snps = folded.shape[1]
    wide = snps // owners
    size = wide // 2
    shape = (size, snps)
    row, lane = iota(shape, 0), iota(shape, 1)

    def block(number):
        return tile[number * size : (number + 1) * size, :]

    diagonal = block(0)
    for number in range(1, 2 * owners):
        diagonal = jnp.where(lane >= number * size, block(number), diagonal)
    flipped[:, 0:size] = diagonal.T
    corner = diagonal
    for owner in range(owners):
        start = (2 * owner + 1) * size
        turned = jnp.concatenate(
            [flipped[start : start + size, :], jnp.zeros((size, snps - LANES), jnp.float32)], axis=1
        )
        if owner:
            turned = pltpu.roll(turned, owner * wide, 1)
        inside = lane - owner * wide
        other = (row <= inside) if owner < owners // 2 else (row >= inside)
        corner = jnp.where((inside >= 0) & (inside < size) & other, turned, corner)
    rolled = []
    for shift in range(owners):
        mixed = None
        for owner in range(owners):
            slot = (owner + shift) % owners
            left = block(LEFT_BLOCKS[owner][slot]) if slot else corner
            start = owner * wide
            mixed = left if mixed is None else jnp.where(lane >= start, left, mixed)
            mixed = jnp.where(lane >= start + size, block(RIGHT_BLOCKS[owner][slot]), mixed)
        rolled.append(pltpu.roll(mixed, shift * wide, 1) if shift else mixed)
    for owner in range(owners):
        mixed = rolled[(0 - owner) % owners]
        for slot in range(1, owners):
            mixed = jnp.where(lane >= slot * wide, rolled[(slot - owner) % owners], mixed)
        folded[owner * size : (owner + 1) * size, :] = to_fields(mixed)


def above(far):
    return odd_block() == far


def side_dot(weighted_ref, side_ref):
    rows = weighted_ref.shape[1]
    half = rows // 2

    def dot(which, columns):
        return jnp.dot(
            weighted_ref[:, which], side_ref[0:half, columns], preferred_element_type=jnp.float32
        )

    first = dot(slice(0, half), slice(0, 2 * LANES))
    second = dot(slice(half, rows), slice(LANES, 3 * LANES))
    whole = first[:, 0:LANES] + second[:, LANES:]
    return whole, first[:, LANES:] + pltpu.roll(second[:, 0:LANES], HALF_LANES, 1)


def close_kernel(weighted_ref, side_ref, whole_ref, shared_ref):
    whole_ref[...], shared_ref[...] = side_dot(weighted_ref, side_ref)


def far_kernel(groups, share, weighted_ref, side_ref, whole_ref, shared_ref, totals_ref, *refs):
    own_parts, own_sum_ref = refs[:groups], refs[groups]
    targets, (tile, folded, flipped, extras) = refs[groups + 1 : 2 * groups + 1], refs[2 * groups + 1 :]
    snps = tile.shape[1]
    own_sum_ref[...] = sum((part[...] for part in own_parts[1:]), own_parts[0][...])
    whole, shared = side_dot(weighted_ref, side_ref)
    left = iota(shared.shape, 1) < HALF_LANES

    @pl.when(above(True))
    def _():
        tile[:, 0:LANES] = whole
        tile[:, LANES : 2 * LANES] = jnp.where(left, shared, shared_ref[...])
        tile[:, 2 * LANES :] = whole_ref[...]

    @pl.when(jnp.logical_not(above(True)))
    def _():
        tile[:, 0:LANES] = whole_ref[...]
        tile[:, LANES : 2 * LANES] = jnp.where(left, shared_ref[...], shared)
        tile[:, 2 * LANES :] = whole

    fold_by_column(tile, flipped, folded)
    square = (snps, snps)
    apart = jnp.sum(
        jnp.where(iota(square, 0) == iota(square, 1), tile[0:snps, :], 0.0), axis=0, keepdims=True
    )
    tiles = snps // LANES
    sizes = totals_ref[1:2, :]
    by_column = jnp.concatenate([sizes, tile[snps : snps + 1, :], apart, jnp.zeros((5, snps))], axis=0)
    for owner in range(groups):
        start = owner * (snps // groups)
        columns = pltpu.roll(by_column, snps - start, 1) if owner else by_column
        extras[8 * owner : 8 * (owner + 1), :] = to_fields(columns[:, 0:LANES])
    me = lax.axis_index("hap")
    send_tiles(groups, folded, share, targets)
    for step, target in enumerate(targets):
        owner = partner(me, step, groups)
        target[tiles * share :, :] = extras[pl.ds(pl.multiple_of(owner * 8, 8), 8), :]


def near_kernel(groups, share, weighted_ref, far_ref, close_ref, totals_ref, *refs):
    own_parts, own_sum_ref = refs[:groups], refs[groups]
    targets, (near, tile, folded) = refs[groups + 1 : 2 * groups + 1], refs[2 * groups + 1 :]
    rows, snps = near.shape
    half = snps // 2
    odd = odd_block()

    def unpack(up_ref, down_ref):
        pieces = load_packed(up_ref[0 : rows // 2, :], down_ref[0 : rows // 2, :])
        for side in range(2):
            where = slice(side * (rows // 2), (side + 1) * (rows // 2))
            for number in range(3):
                near[where, number * LANES : (number + 1) * LANES] = pieces[side][number]

    @pl.when(odd)
    def _():
        unpack(far_ref, close_ref)

    @pl.when(jnp.logical_not(odd))
    def _():
        unpack(close_ref, far_ref)

    tile[...] = jnp.dot(weighted_ref[...], near[...], preferred_element_type=jnp.float32)
    row, col = iota((half, snps), 0), iota((half, snps), 1)
    moved = (col >= half) & (col - half < row)
    turned = pltpu.roll(tile[0:half, :], half, 1)
    folded[0:half, :] = to_fields(jnp.where(moved, turned, tile[half:snps, :]))
    if folded.shape[0] > half:
        folded[half:, :] = jnp.zeros((folded.shape[0] - half, snps), jnp.int32)
    square = (snps, snps)
    far = jnp.sum(
        jnp.where(iota(square, 0) == iota(square, 1), tile[0:snps, :], 0.0), axis=0, keepdims=True
    )
    extras = to_fields(
        jnp.concatenate(
            [totals_ref[0:2, :], tile[snps : snps + 1, :], far, jnp.zeros((4, snps))], axis=0
        )
    )
    send_shares(groups, folded, share, targets)
    for target in targets:
        target[share:, :] = extras
    own_sum_ref[...] = sum((part[...] for part in own_parts[1:]), own_parts[0][...])


def annots_kernel(annot_ref, far_ref, close_ref, own_ref, near_ref):
    snps = annot_ref.shape[1]
    part = far_ref.shape[0]
    wide = 2 * part
    own = annot_ref[...].astype(jnp.float32)
    own = jnp.concatenate([own, jnp.zeros((LANES - own.shape[0], snps), jnp.float32)], axis=0)
    own_ref[...] = own.T
    odd = odd_block()
    far, close = far_ref[...].astype(jnp.float32), close_ref[...].astype(jnp.float32)
    first, second = load_packed(jnp.where(odd, far, close), jnp.where(odd, close, far))
    near = jnp.concatenate(
        [
            jnp.concatenate([piece.astype(jnp.float32) for piece in first], axis=1),
            jnp.concatenate([piece.astype(jnp.float32) for piece in second], axis=1),
            jnp.zeros((LANES - wide, snps), jnp.float32),
        ],
        axis=0,
    )
    near_ref[...] = near.T


def column_stats(totals, count):
    size = jnp.maximum(count, 1.0)
    frequency = totals / size
    variance = jnp.maximum(frequency * (1.0 - frequency), VARIANCE_FLOOR)
    inverse = 1.0 / jnp.sqrt(size * variance)
    low = ((0.0 - frequency) * inverse).astype(jnp.bfloat16).astype(jnp.float32)
    high = ((1.0 - frequency) * inverse).astype(jnp.bfloat16).astype(jnp.float32)
    step = high - low
    root = 1.0 / jnp.sqrt(size)
    return step, step * totals * root, (low * count + step * totals) * root


def correlation(row, col, count):
    return row[0] * col[0] * count - row[1] * col[1] + row[2] * col[2]


def split(values):
    high = values.astype(jnp.bfloat16)
    return high, (values - high.astype(jnp.float32)).astype(jnp.bfloat16)


def dot_split(values, right, axis):
    dims = (((axis,), (0,)), ((), ()))
    return sum(
        lax.dot_general(part, right, dims, preferred_element_type=jnp.float32)
        for part in split(values)
    )


def score_kernel(groups, share, reach_ref, *refs):
    own_sum_ref, near_parts = refs[0], refs[1 : groups + 1]
    annot_ref, near_annot_ref = refs[groups + 1 : groups + 3]
    targets = refs[groups + 3 : 2 * groups + 3]
    table, annots, near_annots, scores = refs[2 * groups + 3 :]
    snps = annot_ref.shape[0]
    half = snps // 2
    out_share = snps // groups
    me = lax.axis_index("hap")
    block = lax.axis_index("snp")
    last = reach_ref.shape[0] - 1
    reach_here = reach_ref[block]
    reach_up = reach_ref[jnp.minimum(block + 1, last)]
    reach_down = reach_ref[jnp.maximum(block - 1, 0)]

    own_counts = own_sum_ref[...]
    near_sums = sum((part[...] for part in near_parts[1:]), near_parts[0][...])
    extras = from_fields(near_sums[share:, :])
    near_counts = near_sums[0:share, :]

    own_stats, near_stats, lines = [], [], []
    for pop in range(2):
        count = extras[pop][1:2, :]
        own_stats.append(column_stats(extras[pop][0:1, :], count))
        near_stats.append(column_stats(extras[pop][2:3, :], count))
        lines += [*own_stats[pop], *near_stats[pop], extras[pop][0:1, :], extras[pop][3:4, :]]
    by_row = jnp.concatenate(lines, axis=0).T
    table[0:snps, 0:16] = by_row
    if table.shape[0] > snps:
        table[snps:, 0:16] = jnp.zeros((table.shape[0] - snps, 16), jnp.float32)
    annots[0:snps, :] = annot_ref[...]
    near_annots[0:snps, :] = near_annot_ref[...]
    if annots.shape[0] > snps:
        annots[snps:, :] = jnp.zeros((annots.shape[0] - snps, LANES), jnp.float32)

    low_rows = pl.multiple_of(me * share, 8)
    high_rows = pl.multiple_of(half + me * share, 8)

    def both(ref):
        return jnp.concatenate([ref[pl.ds(low_rows, share), :], ref[pl.ds(high_rows, share), :]], axis=0)

    here = both(table)
    own_count = jnp.concatenate([pltpu.roll(own_counts, half, 1), own_counts], axis=0)
    near_count = jnp.concatenate([pltpu.roll(near_counts, half, 1), near_counts], axis=0)
    shape = (2 * share, snps)
    local, col = iota(shape, 0), iota(shape, 1)
    low = local < share
    place = jnp.where(low, local, local - share) + me * share
    row = jnp.where(low, place, place + half)
    own_fields, near_fields = from_fields(own_count), from_fields(near_count)
    own_product, near_product = 1.0, 1.0
    for pop in range(2):
        row_stats = [here[:, 8 * pop + k : 8 * pop + k + 1] for k in range(3)]
        own_product *= correlation(row_stats, own_stats[pop], own_fields[pop])
        near_product *= correlation(row_stats, near_stats[pop], near_fields[pop])
    real = place < half
    own_inside = real & ((low & (col > row)) | (~low & (col >= half) & (col < row)))
    own_inside &= jnp.abs(col - row) <= reach_here
    own_kept = jnp.where(own_inside, own_product, 0.0)
    in_upper = col < half
    near_inside = real & ((low & (col < row)) | (~low & (in_upper | (col > row))))
    distance = jnp.where(in_upper, snps + col - row, snps + row - col)
    near_here = jnp.where(near_inside & (distance <= reach_here), near_product, 0.0)
    reach_there = jnp.where(in_upper, reach_up, reach_down)
    near_there = jnp.where(near_inside & (distance <= reach_there), near_product, 0.0)

    rows_here = both(annots)
    rows_there = pltpu.roll(rows_here, HALF_LANES, 1)
    scores[0:snps, :] = dot_split(
        jnp.concatenate([own_kept, near_there], axis=0),
        jnp.concatenate([rows_here, rows_there], axis=0).astype(jnp.bfloat16),
        0,
    )
    direct = dot_split(
        jnp.concatenate([own_kept, near_here], axis=1),
        jnp.concatenate([annot_ref[...], near_annot_ref[...]], axis=0).astype(jnp.bfloat16),
        1,
    )
    scores[pl.ds(low_rows, share), :] += direct[0:share, :]
    scores[pl.ds(high_rows, share), :] += direct[share:, :]

    out_rows = pl.ds(pl.multiple_of(me * out_share, 8), out_share)
    mine = table[out_rows, :]
    self_product, far_product = 1.0, 1.0
    for pop in range(2):
        k = 8 * pop
        own_row = [mine[:, k + s : k + s + 1] for s in range(3)]
        near_row = [mine[:, k + 3 + s : k + 4 + s] for s in range(3)]
        self_product *= correlation(own_row, own_row, mine[:, k + 6 : k + 7])
        far_product *= correlation(own_row, near_row, mine[:, k + 7 : k + 8])
    mine_annots = annots[out_rows, :]
    far_reach = jnp.where(me < groups // 2, reach_up, reach_down)
    scores[out_rows, :] += (
        mine_annots * self_product
        + near_annots[out_rows, :] * jnp.where(reach_here >= snps, far_product, 0.0)
        + pltpu.roll(mine_annots, HALF_LANES, 1) * jnp.where(far_reach >= snps, far_product, 0.0)
    )
    send_shares(groups, scores, out_share, targets)


def pack_halves(values):
    half = values.shape[0] // 2
    left = iota((half, LANES), 1) < HALF_LANES
    return jnp.where(left, values[0:half], pltpu.roll(values[half:], HALF_LANES, 1))


def unpack_halves(packed):
    return jnp.concatenate([packed, pltpu.roll(packed, HALF_LANES, 1)], axis=0)


def dot_rounded(values, right, axis):
    dims = (((axis,), (0,)), ((), ()))
    return lax.dot_general(
        values.astype(jnp.bfloat16), right, dims, preferred_element_type=jnp.float32
    )


def owner_places(groups, size):
    me = lax.axis_index("hap")

    def mine(blocks, slot):
        value = blocks[0][slot]
        for group in range(1, groups):
            value = jnp.where(me == group, blocks[group][slot], value)
        return value * size

    left = [mine(LEFT_BLOCKS, slot) for slot in range(groups)]
    right = [mine(RIGHT_BLOCKS, slot) for slot in range(groups)]
    return left + left[0:1], right + [(2 * me + 1) * size]


def rows_at(ref, places, size):
    return jnp.concatenate([ref[pl.ds(pl.multiple_of(place, 8), size), :] for place in places], axis=0)


def own_score_kernel(
    groups, share, reach_ref, own_sum_ref, annot_ref, near_annot_ref, scores, mine_ref, rows_ref, masks_ref, columns_ref, own_rows_ref, table
):
    snps = annot_ref.shape[0]
    half = snps // 2
    wide = snps // groups
    tiles = snps // LANES
    me = lax.axis_index("hap")
    reach_here = reach_ref[lax.axis_index("snp")]
    own_counts = from_tiles(own_sum_ref[0 : tiles * share, :], share)
    extras = from_fields(own_sum_ref[tiles * share :, :])

    own_stats, lines = [], []
    for pop in range(2):
        count = jnp.concatenate([extras[pop][tiles : tiles + 1, :]] * tiles, axis=1)
        totals = jnp.concatenate([extras[pop][k : k + 1, :] for k in range(tiles)], axis=1)
        own_stats.append(column_stats(totals, count))
        lines += [*own_stats[pop], totals]
    table[:, 0:8] = jnp.concatenate(lines, axis=0).T

    low_rows = pl.multiple_of(me * share, 8)
    high_rows = pl.multiple_of(half + me * share, 8)

    def both(ref):
        return jnp.concatenate([ref[pl.ds(low_rows, share), :], ref[pl.ds(high_rows, share), :]], axis=0)

    here = both(table)
    own_fields = from_fields(
        jnp.concatenate([pltpu.roll(own_counts, half, 1), own_counts], axis=0)
    )
    shape = (2 * share, snps)
    local, col = iota(shape, 0), iota(shape, 1)
    low = local < share
    row = jnp.where(low, local, local + half - share) + me * share
    product = 1.0
    for pop in range(2):
        row_stats = [here[:, 4 * pop + k : 4 * pop + k + 1] for k in range(3)]
        product *= correlation(row_stats, own_stats[pop], own_fields[pop])
    inside = (low & (col > row)) | (~low & (col >= half) & (col < row))
    own_kept = jnp.where(inside & (jnp.abs(col - row) <= reach_here), product, 0.0)
    rows_here = both(annot_ref).astype(jnp.bfloat16)
    scores[...] = dot_rounded(own_kept, rows_here, 0)
    direct = dot_rounded(own_kept, annot_ref[...].astype(jnp.bfloat16), 1)
    scores[pl.ds(low_rows, share), :] += direct[0:share, :]
    scores[pl.ds(high_rows, share), :] += direct[share:, :]

    slice_rows = pl.ds(pl.multiple_of(me * wide, 8), wide)
    mine = table[slice_rows, :]
    mine_ref[...] = mine
    product = 1.0
    for pop in range(2):
        own_row = [mine[:, 4 * pop + k : 4 * pop + k + 1] for k in range(4)]
        product *= correlation(own_row, own_row, own_row[3])
    scores[slice_rows, :] += annot_ref[slice_rows, :] * product

    size = wide // 2
    left_places, right_places = owner_places(groups, size)
    left_table, right_table = rows_at(table, left_places, size), rows_at(table, right_places, size)
    local, lane = iota((size, LANES), 0), iota((size, LANES), 1)
    own_row = jnp.concatenate(
        [local + jnp.where(lane < size, a, b) for a, b in zip(left_places, right_places)], axis=0
    )
    shape = own_row.shape
    lane = iota(shape, 1)
    is_left = lane < size
    for pop in range(2):
        for k in range(3):
            column = slice(4 * pop + k, 4 * pop + k + 1)
            rows_ref[3 * pop + k] = jnp.where(is_left, left_table[:, column], right_table[:, column])
    upper = me < groups // 2
    block = lax.axis_index("snp")
    last = reach_ref.shape[0] - 1
    reach_there = jnp.where(
        upper, reach_ref[jnp.minimum(block + 1, last)], reach_ref[jnp.maximum(block - 1, 0)]
    )
    apart = jnp.abs(own_row - (lane + me * wide))
    ahead = (own_row - (lane + me * wide)) * jnp.where(upper, 1, -1) > 0
    real = ahead & (lane < wide) & ((lane >= size) | (iota(shape, 0) < groups * size))
    for number, limit in enumerate((reach_here, reach_there)):
        masks_ref[number] = jnp.where(real & (snps - apart <= limit), 1.0, 0.0)
    their_annots = near_annot_ref[slice_rows, :]
    columns = jnp.concatenate([their_annots, jnp.zeros((LANES - wide, LANES), jnp.float32)], axis=0)
    columns_ref[...] = columns.astype(jnp.bfloat16)
    own_rows_ref[...] = rows_at(annot_ref, left_places + right_places, size).astype(jnp.bfloat16)


def near_score_kernel(groups, share, reach_ref, *refs):
    near_parts, refs = refs[:groups], refs[groups:]
    own_ref, mine_ref, rows_ref, masks_ref, columns_ref, own_rows_ref, annot_ref, near_annot_ref = refs[:8]
    keep_ref, send_ref, near_out_ref, flipped, scores = refs[8:]
    snps = annot_ref.shape[0]
    wide = snps // groups
    size = wide // 2
    tiles = snps // LANES
    me = lax.axis_index("hap")
    block = lax.axis_index("snp")
    last = reach_ref.shape[0] - 1
    reach_here = reach_ref[block]
    reach_there = jnp.where(
        me < groups // 2, reach_ref[jnp.minimum(block + 1, last)], reach_ref[jnp.maximum(block - 1, 0)]
    )

    scores[...] = own_ref[...]
    near_sums = sum((part[...] for part in near_parts[1:]), near_parts[0][...])
    near_counts = from_tiles(near_sums[0 : tiles * share, :], share)
    extras = from_fields(near_sums[tiles * share :, :])
    near_stats, near_lines = [], []
    for pop in range(2):
        near_stats.append(column_stats(extras[pop][1:2, :], extras[pop][0:1, :]))
        near_lines += [*near_stats[pop], extras[pop][2:3, :]]
    near_table = jnp.concatenate(near_lines, axis=0).T[0:wide, :]

    slots = [near_counts[:, 0:LANES]]
    for slot in range(1, groups):
        slots.append(pltpu.roll(near_counts, snps - slot * wide, 1)[:, 0:LANES])
    flipped[:, 0:size] = slots[0].T
    slots.append(pltpu.roll(flipped[0:size, :], size, 1))
    near_fields = from_fields(jnp.concatenate(slots, axis=0))
    product = 1.0
    for pop in range(2):
        row_stats = [rows_ref[3 * pop + k] for k in range(3)]
        product *= correlation(row_stats, near_stats[pop], near_fields[pop])
    near_here = jnp.where(masks_ref[0] > 0.0, product, 0.0)
    near_there = jnp.where(masks_ref[1] > 0.0, product, 0.0)
    is_left = iota(product.shape, 1) < size

    def sides(values):
        return jnp.concatenate(
            [jnp.where(is_left, values, 0.0), jnp.where(is_left, 0.0, values)], axis=0
        )

    slice_rows = pl.ds(pl.multiple_of(me * wide, 8), wide)
    direct = dot_rounded(sides(near_here), columns_ref[...], 1)
    left_places, right_places = owner_places(groups, size)
    for number, place in enumerate(left_places + right_places):
        scores[pl.ds(pl.multiple_of(place, 8), size), :] += direct[number * size : (number + 1) * size, :]
    near_scores = dot_rounded(sides(near_there), own_rows_ref[...], 0)[0:wide, :]

    mine_table = mine_ref[...]
    far_product = 1.0
    for pop in range(2):
        own_row = [mine_table[:, 4 * pop + k : 4 * pop + k + 1] for k in range(3)]
        near_row = [near_table[:, 4 * pop + k : 4 * pop + k + 1] for k in range(4)]
        far_product *= correlation(own_row, near_row, near_row[3])
    scores[slice_rows, :] += near_annot_ref[slice_rows, :] * jnp.where(reach_here >= snps, far_product, 0.0)
    near_scores += annot_ref[slice_rows, :] * jnp.where(reach_there >= snps, far_product, 0.0)
    near_out_ref[...] = pack_halves(near_scores)

    def packed(step):
        group = partner(me, step, groups)
        return pack_halves(scores[pl.ds(pl.multiple_of(group * wide, 8), wide), :])

    for ref, steps in ((keep_ref, (0, 1)), (send_ref, (2, 3))):
        for number, step in enumerate(steps):
            ref[number * size : (number + 1) * size, :] = packed(step).astype(ref.dtype)


def middle_kernel(keep_ref, part_ref, mine_ref, send_ref):
    total = keep_ref[...] + part_ref[...].astype(jnp.float32)
    half = mine_ref.shape[0]
    mine_ref[...] = total[0:half]
    send_ref[...] = total[half:].astype(send_ref.dtype)


def column_finish_kernel(mine_ref, part_ref, there_ref, out_ref):
    packed = mine_ref[...] + part_ref[...].astype(jnp.float32) + there_ref[...]
    out_ref[...] = unpack_halves(packed).T[0 : out_ref.shape[0], :]


def sum_kernel(*refs):
    *parts, own_ref, there_ref = refs
    total = sum((part[...].astype(jnp.float32) for part in parts[1:]), parts[0][...])
    own_ref[...] = total
    half = there_ref.shape[0]
    left = iota((half, LANES), 1) < HALF_LANES
    second = total[half:]
    if second.shape[0] < half:
        second = jnp.concatenate([second, jnp.zeros((half - second.shape[0], LANES))], axis=0)
    there_ref[...] = jnp.where(left, pltpu.roll(total[0:half], HALF_LANES, 1), second)


def finish_kernel(own_ref, there_ref, out_ref):
    annots, rows = out_ref.shape
    there = there_ref[...]
    there = jnp.concatenate([there, pltpu.roll(there, HALF_LANES, 1)], axis=0)
    out_ref[...] = (own_ref[...] + there[0:rows]).T[0:annots, :]


def around(value, groups, step):
    return lax.ppermute(
        value, "hap", [(source, partner(source, step, groups)) for source in range(groups)]
    )


def swapped(value, first):
    pairs = []
    for block in range(first, lax.axis_size("snp") - 1, 2):
        pairs += [(block, block + 1), (block + 1, block)]
    return lax.ppermute(value, "snp", pairs)


def per_device(haplotypes, labels, annotations, reach):
    rows, snps = haplotypes.shape
    half = snps // 2
    groups = lax.axis_size("hap")
    blocks = lax.axis_size("snp")
    share = round_up(-(-half // groups), 16)
    folded_rows = share * groups
    out_share = snps // groups
    padded = half + folded_rows
    annot_part = 32
    bf16, f32, i32 = jnp.bfloat16, jnp.float32, jnp.int32
    shape = jax.ShapeDtypeStruct

    packed = shape((rows // 2 + annot_part, snps), bf16)
    haplotypes = pltpu.with_memory_space_constraint(haplotypes, pltpu.HBM)
    annots_in = pltpu.with_memory_space_constraint(annotations, pltpu.HBM)
    alleles, far, close = call(
        prepare_kernel,
        [shape((rows, snps), bf16), packed, packed],
        [HBM, HBM],
        [
            pltpu.VMEM((rows, snps), i32),
            pltpu.VMEM(annotations.shape, i32),
            pltpu.SemaphoreType.DMA((2 * CHUNKS + 1,)),
        ],
        moved=rows * snps * 8,
    )(haplotypes, annots_in)
    from_far = swapped(far, 1)
    from_close = swapped(close, 0)

    by_column = groups == len(LEFT_BLOCKS)
    compact = shape((share * (snps // LANES) + 8, LANES), i32)
    own_share_counts = compact if by_column else shape((share, snps), i32)
    tile = pltpu.VMEM((snps + 16, snps), f32)
    folded = pltpu.VMEM((folded_rows, snps), i32)
    weighted, totals, *own_parts = call(
        functools.partial(own_kernel, groups, share),
        [shape((snps + 16, rows), bf16), shape((8, snps), f32)] + [own_share_counts] * groups,
        [VMEM, VMEM],
        [tile, folded],
        flops=2 * rows * snps * snps,
        moved=rows * snps * 4,
    )(alleles, labels.reshape(1, rows))
    own_parts = [own_parts[0]] + [around(own_parts[k], groups, k) for k in range(groups - 1, 0, -1)]

    near_shapes = [own_share_counts] + [compact if by_column else shape((share + 8, snps), i32)] * groups
    if by_column:
        piece = shape((snps + 16, LANES), f32)
        work = dict(flops=4 * rows * snps * LANES, moved=rows * snps * 4)
        close_counts = call(close_kernel, [piece, piece], [VMEM] * 2, **work)(weighted, from_close)
        own_sum, *near_parts = call(
            functools.partial(far_kernel, groups, share),
            near_shapes,
            [VMEM] * (5 + groups),
            [
                tile,
                folded,
                pltpu.VMEM((snps, LANES), f32),
                pltpu.VMEM((8 * groups, LANES), i32),
            ],
            **work,
        )(weighted, from_far, *close_counts, totals, *own_parts)
    else:
        own_sum, *near_parts = call(
            functools.partial(near_kernel, groups, share),
            near_shapes,
            [VMEM] * (4 + groups),
            [pltpu.VMEM((rows, snps), bf16), tile, folded],
            flops=2 * rows * snps * snps,
            moved=rows * snps * 4,
        )(weighted, from_far, from_close, totals, *own_parts)
    near_parts = [near_parts[0]] + [around(near_parts[k], groups, k) for k in range(groups - 1, 0, -1)]

    by_snp = shape((snps, LANES), f32)
    own_annots, near_annots = call(annots_kernel, [by_snp, by_snp], [VMEM] * 3, moved=1 << 20)(
        annotations, from_far[rows // 2 :], from_close[rows // 2 :]
    )
    pairs = []
    for block in range(blocks):
        for group in range(groups):
            target = block + 1 if group < groups // 2 else block - 1
            if 0 <= target < blocks:
                pairs.append((block * groups + group, target * groups + group))

    def to_neighbour(value):
        return lax.ppermute(value, ("snp", "hap"), pairs)

    result = shape((annotations.shape[0], out_share), f32)
    half_share = round_up(-(-out_share // 2), 8)
    own_share = shape((out_share, LANES), f32)
    packed_share = shape((half_share, LANES), f32)
    if by_column:
        pair_rows = (groups + 1) * (out_share // 2)
        prepared = call(
            functools.partial(own_score_kernel, groups, share),
            [
                by_snp,
                shape((out_share, LANES), f32),
                shape((6, pair_rows, LANES), f32),
                shape((2, pair_rows, LANES), f32),
                shape((LANES, LANES), bf16),
                shape((2 * pair_rows, LANES), bf16),
            ],
            [SMEM] + [VMEM] * 3,
            [pltpu.VMEM((snps, LANES), f32)],
            flops=1 << 25,
            moved=1 << 20,
        )(reach, own_sum, own_annots, near_annots)
        both = (2 * half_share, LANES)
        keep, send, near_scores = call(
            functools.partial(near_score_kernel, groups, share),
            [shape(both, f32), shape(both, bf16), packed_share],
            [SMEM] + [VMEM] * (groups + 8),
            [pltpu.VMEM((LANES, LANES), i32), pltpu.VMEM((snps, LANES), f32)],
            flops=1 << 26,
            moved=1 << 21,
        )(reach, *near_parts, *prepared, own_annots, near_annots)
        part = around(send, groups, 2)
        there = to_neighbour(near_scores)
        mine, send = call(
            middle_kernel, [packed_share, shape((half_share, LANES), bf16)], [VMEM] * 2
        )(keep, part)
        part = around(send, groups, 1)
        return call(column_finish_kernel, result, [VMEM] * 3)(mine, part, there)

    tall = pltpu.VMEM((padded, LANES), f32)
    scores = call(
        functools.partial(score_kernel, groups, share),
        [own_share] + [shape((out_share, LANES), bf16)] * (groups - 1),
        [SMEM] + [VMEM] * (groups + 3),
        [tall, tall, tall, tall],
        flops=1 << 26,
        moved=1 << 21,
    )(reach, own_sum, *near_parts, own_annots, near_annots)
    scores = [scores[0]] + [around(scores[k], groups, k) for k in range(groups - 1, 0, -1)]
    own_scores, near_scores = call(sum_kernel, [own_share, packed_share], [VMEM] * groups)(*scores)
    return call(finish_kernel, result, [VMEM] * 2)(own_scores, to_neighbour(near_scores))


def solution(mesh):
    in_specs = (
        P("hap", ("parts", "snp")),
        P(("parts", "hap")),
        P(None, ("parts", "snp")),
        P("parts"),
    )
    out_specs = P(None, ("parts", "snp", "hap"))
    return jax.shard_map(
        per_device, mesh=mesh, in_specs=in_specs, out_specs=out_specs, check_vma=False
    )
```

```python
import functools

import jax
import jax.numpy as jnp
from jax import lax
from jax.experimental import pallas as pl
from jax.experimental.pallas import tpu as pltpu
from jax.sharding import PartitionSpec as P

VARIANCE_FLOOR = 0.01
BASE_BITS = 12
BASE = 1 << BASE_BITS
FIELD_BITS = 16
LANES = 128
HALF_LANES = LANES // 2
CHUNKS = 8
VMEM = pl.BlockSpec(memory_space=pltpu.VMEM)
SMEM = pl.BlockSpec(memory_space=pltpu.SMEM)
HBM = pl.BlockSpec(memory_space=pltpu.HBM)
VMEM_LIMIT = 24 * 1024 * 1024


def iota(shape, axis):
    return lax.broadcasted_iota(jnp.int32, shape, axis)


def round_up(value, step):
    return -(-value // step) * step


def to_fields(values):
    whole = values.astype(jnp.int32)
    return whole + (whole >> BASE_BITS) * ((1 << FIELD_BITS) - BASE)


def from_fields(packed):
    first = packed & ((1 << FIELD_BITS) - 1)
    second = lax.shift_right_logical(packed, FIELD_BITS)
    return first.astype(jnp.float32), second.astype(jnp.float32)


def call(kernel, out_shape, in_specs, scratch_shapes=(), flops=0, moved=0):
    several = isinstance(out_shape, (list, tuple))
    return pl.pallas_call(
        kernel,
        out_shape=out_shape,
        in_specs=in_specs,
        out_specs=[VMEM] * len(out_shape) if several else VMEM,
        scratch_shapes=list(scratch_shapes),
        compiler_params=pltpu.CompilerParams(vmem_limit_bytes=VMEM_LIMIT),
        cost_estimate=pl.CostEstimate(flops=flops, bytes_accessed=moved, transcendentals=0),
    )


def odd_block():
    return lax.rem(lax.axis_index("snp"), 2) == 1


def store_packed(up_ref, down_ref, where, first, second):
    left = iota((first.shape[0], LANES), 1) < HALF_LANES
    middle = first[:, LANES : 2 * LANES]
    turned = pltpu.roll(second[:, LANES : 2 * LANES], HALF_LANES, 1)
    for ref, side, mixed in (
        (up_ref, slice(0, LANES), jnp.where(left, middle, turned)),
        (down_ref, slice(2 * LANES, 3 * LANES), jnp.where(left, turned, middle)),
    ):
        ref[where, 0:LANES] = first[:, side].astype(jnp.bfloat16)
        ref[where, LANES : 2 * LANES] = mixed.astype(jnp.bfloat16)
        ref[where, 2 * LANES : 3 * LANES] = second[:, side].astype(jnp.bfloat16)


def load_packed(up, down):
    left = iota((up.shape[0], LANES), 1) < HALF_LANES
    up_mixed, down_mixed = up[:, LANES : 2 * LANES], down[:, LANES : 2 * LANES]
    first = jnp.where(left, up_mixed, down_mixed)
    second = jnp.where(left, down_mixed, up_mixed)
    second = pltpu.roll(second.astype(jnp.float32), HALF_LANES, 1).astype(second.dtype)
    return (
        (up[:, :LANES], first, down[:, :LANES]),
        (up[:, 2 * LANES :], second, down[:, 2 * LANES :]),
    )


def prepare_kernel(hap_ref, annot_ref, alleles_ref, far_ref, close_ref, held, held_annots, sems):
    rows = hap_ref.shape[0]
    annot_rows = annot_ref.shape[0]
    size = rows // (2 * CHUNKS)
    starts = [side * (rows // 2) + chunk * size for chunk in range(CHUNKS) for side in range(2)]
    copies = [
        pltpu.make_async_copy(
            hap_ref.at[pl.ds(start, size)], held.at[pl.ds(start, size)], sems.at[number]
        )
        for number, start in enumerate(starts)
    ]
    copies.append(pltpu.make_async_copy(annot_ref, held_annots, sems.at[2 * CHUNKS]))
    for number, copy in enumerate(copies):
        copy.start(priority=number % 2)
    part = far_ref.shape[0] - rows // 2
    odd = odd_block()

    def store(where, first, second):
        @pl.when(odd)
        def _():
            store_packed(close_ref, far_ref, where, first, second)

        @pl.when(jnp.logical_not(odd))
        def _():
            store_packed(far_ref, close_ref, where, first, second)

    for chunk in range(CHUNKS):
        pair = []
        for side in range(2):
            number = 2 * chunk + side
            copies[number].wait()
            where = slice(starts[number], starts[number] + size)
            values = held[where, :].astype(jnp.float32)
            alleles_ref[where, :] = values.astype(jnp.bfloat16)
            pair.append(values)
        store(slice(chunk * size, (chunk + 1) * size), *pair)
    copies[-1].wait()
    annots = jnp.concatenate(
        [
            held_annots[...].astype(jnp.float32),
            jnp.zeros((2 * part - annot_rows, annot_ref.shape[1]), jnp.float32),
        ],
        axis=0,
    )
    store(slice(rows // 2, rows // 2 + part), annots[:part], annots[part:])


def partner(group, step, groups):
    if groups & (groups - 1) == 0:
        return group ^ step
    return (group + step) % groups


def send_shares(groups, source, share, targets):
    me = lax.axis_index("hap")
    for step, target in enumerate(targets):
        group = partner(me, step, groups)
        rows = source[pl.ds(pl.multiple_of(group * share, 8), share), :]
        target[0:share, :] = rows.astype(target.dtype)


def send_tiles(groups, source, share, targets):
    me = lax.axis_index("hap")
    for step, target in enumerate(targets):
        owner = partner(me, step, groups)
        counts = source[pl.ds(pl.multiple_of(owner * share, 8), share), :]
        for k in range(source.shape[1] // LANES):
            target[k * share : (k + 1) * share, :] = counts[:, k * LANES : (k + 1) * LANES]


def from_tiles(counts, share):
    tiles = counts.shape[0] // share
    return jnp.concatenate([counts[k * share : (k + 1) * share, :] for k in range(tiles)], axis=1)


def own_kernel(groups, share, alleles_ref, label_ref, *refs):
    weighted_ref, totals_ref, *targets = refs[: 2 + groups]
    tile, folded = refs[2 + groups :]
    rows, snps = alleles_ref.shape
    half = snps // 2
    weight = jnp.where(label_ref[...] > 0, float(BASE), 1.0)
    weighted_ref[0:snps, :] = alleles_ref[...].T * weight.astype(jnp.bfloat16)
    extra = weighted_ref.shape[0] - snps
    weighted_ref[snps:, :] = jnp.broadcast_to(weight, (extra, rows)).astype(jnp.bfloat16)
    tile[...] = jnp.dot(weighted_ref[...], alleles_ref[...], preferred_element_type=jnp.float32)
    count = jnp.sum(weight, axis=1, keepdims=True)
    totals_ref[...] = jnp.concatenate(
        [tile[snps : snps + 1, :], jnp.broadcast_to(count, (1, snps)), jnp.zeros((6, snps))], axis=0
    )
    row, col = iota((half, snps), 0), iota((half, snps), 1)
    moved = (col < half) | (col - half > row)
    turned = pltpu.roll(tile[0:half, :], half, 1)
    folded[0:half, :] = to_fields(jnp.where(moved, turned, tile[half:snps, :]))
    if folded.shape[0] > half:
        folded[half:, :] = jnp.zeros((folded.shape[0] - half, snps), jnp.int32)
    if groups != len(LEFT_BLOCKS):
        send_shares(groups, folded, share, targets)
        return
    tiles = snps // LANES
    shared = [totals_ref[0:1, k * LANES : (k + 1) * LANES] for k in range(tiles)]
    shared += [totals_ref[1:2, 0:LANES], jnp.zeros((7 - tiles, LANES))]
    extras = to_fields(jnp.concatenate(shared, axis=0))
    send_tiles(groups, folded, share, targets)
    for target in targets:
        target[tiles * share :, :] = extras


LEFT_BLOCKS = ((0, 1, 2, 3), (2, 3, 6, 7), (4, 0, 1, 2), (6, 0, 4, 5))
RIGHT_BLOCKS = ((2, 3, 6, 7), (4, 5, 6, 7), (0, 1, 2, 4), (0, 4, 5, 6))


def fold_by_column(tile, flipped, folded):
    owners = len(LEFT_BLOCKS)
    snps = folded.shape[1]
    wide = snps // owners
    size = wide // 2
    shape = (size, snps)
    row, lane = iota(shape, 0), iota(shape, 1)

    def block(number):
        return tile[number * size : (number + 1) * size, :]

    diagonal = block(0)
    for number in range(1, 2 * owners):
        diagonal = jnp.where(lane >= number * size, block(number), diagonal)
    inside = lane
    for number in range(1, 2 * owners):
        inside = jnp.where(lane >= number * size, lane - number * size, inside)
    apart = jnp.sum(jnp.where(row == inside, diagonal, 0.0), axis=0, keepdims=True)
    flipped[:, 0:size] = diagonal.T
    corner = diagonal
    for owner in range(owners):
        start = (2 * owner + 1) * size
        turned = jnp.concatenate(
            [flipped[start : start + size, :], jnp.zeros((size, snps - LANES), jnp.float32)], axis=1
        )
        if owner:
            turned = pltpu.roll(turned, owner * wide, 1)
        inside = lane - owner * wide
        other = (row <= inside) if owner < owners // 2 else (row >= inside)
        corner = jnp.where((inside >= 0) & (inside < size) & other, turned, corner)
    rolled = []
    for shift in range(owners):
        mixed = None
        for owner in range(owners):
            slot = (owner + shift) % owners
            left = block(LEFT_BLOCKS[owner][slot]) if slot else corner
            start = owner * wide
            mixed = left if mixed is None else jnp.where(lane >= start, left, mixed)
            mixed = jnp.where(lane >= start + size, block(RIGHT_BLOCKS[owner][slot]), mixed)
        rolled.append(pltpu.roll(mixed, shift * wide, 1) if shift else mixed)
    for owner in range(owners):
        mixed = rolled[(0 - owner) % owners]
        for slot in range(1, owners):
            mixed = jnp.where(lane >= slot * wide, rolled[(slot - owner) % owners], mixed)
        folded[owner * size : (owner + 1) * size, :] = to_fields(mixed)
    return apart


def above(far):
    return odd_block() == far


def side_dot(weighted_ref, side_ref):
    rows = weighted_ref.shape[1]
    half = rows // 2

    def dot(which, columns):
        return jnp.dot(
            weighted_ref[:, which], side_ref[0:half, columns], preferred_element_type=jnp.float32
        )

    first = dot(slice(0, half), slice(0, 2 * LANES))
    second = dot(slice(half, rows), slice(LANES, 3 * LANES))
    whole = first[:, 0:LANES] + second[:, LANES:]
    return whole, first[:, LANES:] + pltpu.roll(second[:, 0:LANES], HALF_LANES, 1)


def close_kernel(weighted_ref, side_ref, whole_ref, shared_ref):
    whole_ref[...], shared_ref[...] = side_dot(weighted_ref, side_ref)


def far_kernel(groups, share, weighted_ref, side_ref, whole_ref, shared_ref, totals_ref, *refs):
    own_parts, own_sum_ref = refs[:groups], refs[groups]
    targets, (tile, folded, flipped, extras) = refs[groups + 1 : 2 * groups + 1], refs[2 * groups + 1 :]
    snps = tile.shape[1]
    own_sum_ref[...] = sum((part[...] for part in own_parts[1:]), own_parts[0][...])
    whole, shared = side_dot(weighted_ref, side_ref)
    left = iota(shared.shape, 1) < HALF_LANES

    @pl.when(above(True))
    def _():
        tile[:, 0:LANES] = whole
        tile[:, LANES : 2 * LANES] = jnp.where(left, shared, shared_ref[...])
        tile[:, 2 * LANES :] = whole_ref[...]

    @pl.when(jnp.logical_not(above(True)))
    def _():
        tile[:, 0:LANES] = whole_ref[...]
        tile[:, LANES : 2 * LANES] = jnp.where(left, shared_ref[...], shared)
        tile[:, 2 * LANES :] = whole

    apart = fold_by_column(tile, flipped, folded)
    tiles = snps // LANES
    sizes = totals_ref[1:2, :]
    by_column = jnp.concatenate([sizes, tile[snps : snps + 1, :], apart, jnp.zeros((5, snps))], axis=0)
    for owner in range(groups):
        start = owner * (snps // groups)
        columns = pltpu.roll(by_column, snps - start, 1) if owner else by_column
        extras[8 * owner : 8 * (owner + 1), :] = to_fields(columns[:, 0:LANES])
    me = lax.axis_index("hap")
    send_tiles(groups, folded, share, targets)
    for step, target in enumerate(targets):
        owner = partner(me, step, groups)
        target[tiles * share :, :] = extras[pl.ds(pl.multiple_of(owner * 8, 8), 8), :]


def near_kernel(groups, share, weighted_ref, far_ref, close_ref, totals_ref, *refs):
    own_parts, own_sum_ref = refs[:groups], refs[groups]
    targets, (near, tile, folded) = refs[groups + 1 : 2 * groups + 1], refs[2 * groups + 1 :]
    rows, snps = near.shape
    half = snps // 2
    odd = odd_block()

    def unpack(up_ref, down_ref):
        pieces = load_packed(up_ref[0 : rows // 2, :], down_ref[0 : rows // 2, :])
        for side in range(2):
            where = slice(side * (rows // 2), (side + 1) * (rows // 2))
            for number in range(3):
                near[where, number * LANES : (number + 1) * LANES] = pieces[side][number]

    @pl.when(odd)
    def _():
        unpack(far_ref, close_ref)

    @pl.when(jnp.logical_not(odd))
    def _():
        unpack(close_ref, far_ref)

    tile[...] = jnp.dot(weighted_ref[...], near[...], preferred_element_type=jnp.float32)
    row, col = iota((half, snps), 0), iota((half, snps), 1)
    moved = (col >= half) & (col - half < row)
    turned = pltpu.roll(tile[0:half, :], half, 1)
    folded[0:half, :] = to_fields(jnp.where(moved, turned, tile[half:snps, :]))
    if folded.shape[0] > half:
        folded[half:, :] = jnp.zeros((folded.shape[0] - half, snps), jnp.int32)
    square = (snps, snps)
    far = jnp.sum(
        jnp.where(iota(square, 0) == iota(square, 1), tile[0:snps, :], 0.0), axis=0, keepdims=True
    )
    extras = to_fields(
        jnp.concatenate(
            [totals_ref[0:2, :], tile[snps : snps + 1, :], far, jnp.zeros((4, snps))], axis=0
        )
    )
    send_shares(groups, folded, share, targets)
    for target in targets:
        target[share:, :] = extras
    own_sum_ref[...] = sum((part[...] for part in own_parts[1:]), own_parts[0][...])


def annots_kernel(annot_ref, far_ref, close_ref, own_ref, near_ref):
    snps = annot_ref.shape[1]
    part = far_ref.shape[0]
    wide = 2 * part
    own = annot_ref[...].astype(jnp.float32)
    own = jnp.concatenate([own, jnp.zeros((LANES - own.shape[0], snps), jnp.float32)], axis=0)
    own_ref[...] = own.T
    odd = odd_block()
    far, close = far_ref[...].astype(jnp.float32), close_ref[...].astype(jnp.float32)
    first, second = load_packed(jnp.where(odd, far, close), jnp.where(odd, close, far))
    near = jnp.concatenate(
        [
            jnp.concatenate([piece.astype(jnp.float32) for piece in first], axis=1),
            jnp.concatenate([piece.astype(jnp.float32) for piece in second], axis=1),
            jnp.zeros((LANES - wide, snps), jnp.float32),
        ],
        axis=0,
    )
    near_ref[...] = near.T


def column_stats(totals, count):
    size = jnp.maximum(count, 1.0)
    frequency = totals / size
    variance = jnp.maximum(frequency * (1.0 - frequency), VARIANCE_FLOOR)
    inverse = 1.0 / jnp.sqrt(size * variance)
    low = ((0.0 - frequency) * inverse).astype(jnp.bfloat16).astype(jnp.float32)
    high = ((1.0 - frequency) * inverse).astype(jnp.bfloat16).astype(jnp.float32)
    step = high - low
    root = 1.0 / jnp.sqrt(size)
    return step, step * totals * root, (low * count + step * totals) * root


def correlation(row, col, count):
    return row[0] * col[0] * count - row[1] * col[1] + row[2] * col[2]


def split(values):
    high = values.astype(jnp.bfloat16)
    return high, (values - high.astype(jnp.float32)).astype(jnp.bfloat16)


def dot_split(values, right, axis):
    dims = (((axis,), (0,)), ((), ()))
    return sum(
        lax.dot_general(part, right, dims, preferred_element_type=jnp.float32)
        for part in split(values)
    )


def score_kernel(groups, share, reach_ref, *refs):
    own_sum_ref, near_parts = refs[0], refs[1 : groups + 1]
    annot_ref, near_annot_ref = refs[groups + 1 : groups + 3]
    targets = refs[groups + 3 : 2 * groups + 3]
    table, annots, near_annots, scores = refs[2 * groups + 3 :]
    snps = annot_ref.shape[0]
    half = snps // 2
    out_share = snps // groups
    me = lax.axis_index("hap")
    block = lax.axis_index("snp")
    last = reach_ref.shape[0] - 1
    reach_here = reach_ref[block]
    reach_up = reach_ref[jnp.minimum(block + 1, last)]
    reach_down = reach_ref[jnp.maximum(block - 1, 0)]

    own_counts = own_sum_ref[...]
    near_sums = sum((part[...] for part in near_parts[1:]), near_parts[0][...])
    extras = from_fields(near_sums[share:, :])
    near_counts = near_sums[0:share, :]

    own_stats, near_stats, lines = [], [], []
    for pop in range(2):
        count = extras[pop][1:2, :]
        own_stats.append(column_stats(extras[pop][0:1, :], count))
        near_stats.append(column_stats(extras[pop][2:3, :], count))
        lines += [*own_stats[pop], *near_stats[pop], extras[pop][0:1, :], extras[pop][3:4, :]]
    by_row = jnp.concatenate(lines, axis=0).T
    table[0:snps, 0:16] = by_row
    if table.shape[0] > snps:
        table[snps:, 0:16] = jnp.zeros((table.shape[0] - snps, 16), jnp.float32)
    annots[0:snps, :] = annot_ref[...]
    near_annots[0:snps, :] = near_annot_ref[...]
    if annots.shape[0] > snps:
        annots[snps:, :] = jnp.zeros((annots.shape[0] - snps, LANES), jnp.float32)

    low_rows = pl.multiple_of(me * share, 8)
    high_rows = pl.multiple_of(half + me * share, 8)

    def both(ref):
        return jnp.concatenate([ref[pl.ds(low_rows, share), :], ref[pl.ds(high_rows, share), :]], axis=0)

    here = both(table)
    own_count = jnp.concatenate([pltpu.roll(own_counts, half, 1), own_counts], axis=0)
    near_count = jnp.concatenate([pltpu.roll(near_counts, half, 1), near_counts], axis=0)
    shape = (2 * share, snps)
    local, col = iota(shape, 0), iota(shape, 1)
    low = local < share
    place = jnp.where(low, local, local - share) + me * share
    row = jnp.where(low, place, place + half)
    own_fields, near_fields = from_fields(own_count), from_fields(near_count)
    own_product, near_product = 1.0, 1.0
    for pop in range(2):
        row_stats = [here[:, 8 * pop + k : 8 * pop + k + 1] for k in range(3)]
        own_product *= correlation(row_stats, own_stats[pop], own_fields[pop])
        near_product *= correlation(row_stats, near_stats[pop], near_fields[pop])
    real = place < half
    own_inside = real & ((low & (col > row)) | (~low & (col >= half) & (col < row)))
    own_inside &= jnp.abs(col - row) <= reach_here
    own_kept = jnp.where(own_inside, own_product, 0.0)
    in_upper = col < half
    near_inside = real & ((low & (col < row)) | (~low & (in_upper | (col > row))))
    distance = jnp.where(in_upper, snps + col - row, snps + row - col)
    near_here = jnp.where(near_inside & (distance <= reach_here), near_product, 0.0)
    reach_there = jnp.where(in_upper, reach_up, reach_down)
    near_there = jnp.where(near_inside & (distance <= reach_there), near_product, 0.0)

    rows_here = both(annots)
    rows_there = pltpu.roll(rows_here, HALF_LANES, 1)
    scores[0:snps, :] = dot_split(
        jnp.concatenate([own_kept, near_there], axis=0),
        jnp.concatenate([rows_here, rows_there], axis=0).astype(jnp.bfloat16),
        0,
    )
    direct = dot_split(
        jnp.concatenate([own_kept, near_here], axis=1),
        jnp.concatenate([annot_ref[...], near_annot_ref[...]], axis=0).astype(jnp.bfloat16),
        1,
    )
    scores[pl.ds(low_rows, share), :] += direct[0:share, :]
    scores[pl.ds(high_rows, share), :] += direct[share:, :]

    out_rows = pl.ds(pl.multiple_of(me * out_share, 8), out_share)
    mine = table[out_rows, :]
    self_product, far_product = 1.0, 1.0
    for pop in range(2):
        k = 8 * pop
        own_row = [mine[:, k + s : k + s + 1] for s in range(3)]
        near_row = [mine[:, k + 3 + s : k + 4 + s] for s in range(3)]
        self_product *= correlation(own_row, own_row, mine[:, k + 6 : k + 7])
        far_product *= correlation(own_row, near_row, mine[:, k + 7 : k + 8])
    mine_annots = annots[out_rows, :]
    far_reach = jnp.where(me < groups // 2, reach_up, reach_down)
    scores[out_rows, :] += (
        mine_annots * self_product
        + near_annots[out_rows, :] * jnp.where(reach_here >= snps, far_product, 0.0)
        + pltpu.roll(mine_annots, HALF_LANES, 1) * jnp.where(far_reach >= snps, far_product, 0.0)
    )
    send_shares(groups, scores, out_share, targets)


def pack_halves(values):
    half = values.shape[0] // 2
    left = iota((half, LANES), 1) < HALF_LANES
    return jnp.where(left, values[0:half], pltpu.roll(values[half:], HALF_LANES, 1))


def unpack_halves(packed):
    return jnp.concatenate([packed, pltpu.roll(packed, HALF_LANES, 1)], axis=0)


def dot_rounded(values, right, axis):
    dims = (((axis,), (0,)), ((), ()))
    return lax.dot_general(
        values.astype(jnp.bfloat16), right, dims, preferred_element_type=jnp.float32
    )


def owner_places(groups, size):
    me = lax.axis_index("hap")

    def mine(blocks, slot):
        value = blocks[0][slot]
        for group in range(1, groups):
            value = jnp.where(me == group, blocks[group][slot], value)
        return value * size

    left = [mine(LEFT_BLOCKS, slot) for slot in range(groups)]
    right = [mine(RIGHT_BLOCKS, slot) for slot in range(groups)]
    return left + left[0:1], right + [(2 * me + 1) * size]


def rows_at(ref, places, size):
    return jnp.concatenate([ref[pl.ds(pl.multiple_of(place, 8), size), :] for place in places], axis=0)


def own_score_kernel(
    groups, share, reach_ref, own_sum_ref, annot_ref, near_annot_ref, scores, mine_ref, rows_ref, masks_ref, columns_ref, own_rows_ref, table
):
    snps = annot_ref.shape[0]
    half = snps // 2
    wide = snps // groups
    tiles = snps // LANES
    me = lax.axis_index("hap")
    reach_here = reach_ref[lax.axis_index("snp")]
    own_counts = from_tiles(own_sum_ref[0 : tiles * share, :], share)
    extras = from_fields(own_sum_ref[tiles * share :, :])

    own_stats, lines = [], []
    for pop in range(2):
        count = jnp.concatenate([extras[pop][tiles : tiles + 1, :]] * tiles, axis=1)
        totals = jnp.concatenate([extras[pop][k : k + 1, :] for k in range(tiles)], axis=1)
        own_stats.append(column_stats(totals, count))
        lines += [*own_stats[pop], totals]
    table[:, 0:8] = jnp.concatenate(lines, axis=0).T

    low_rows = pl.multiple_of(me * share, 8)
    high_rows = pl.multiple_of(half + me * share, 8)

    def both(ref):
        return jnp.concatenate([ref[pl.ds(low_rows, share), :], ref[pl.ds(high_rows, share), :]], axis=0)

    here = both(table)
    own_fields = from_fields(
        jnp.concatenate([pltpu.roll(own_counts, half, 1), own_counts], axis=0)
    )
    shape = (2 * share, snps)
    local, col = iota(shape, 0), iota(shape, 1)
    low = local < share
    row = jnp.where(low, local, local + half - share) + me * share
    product = 1.0
    for pop in range(2):
        row_stats = [here[:, 4 * pop + k : 4 * pop + k + 1] for k in range(3)]
        product *= correlation(row_stats, own_stats[pop], own_fields[pop])
    inside = (low & (col > row)) | (~low & (col >= half) & (col < row))
    own_kept = jnp.where(inside & (jnp.abs(col - row) <= reach_here), product, 0.0)
    rows_here = both(annot_ref).astype(jnp.bfloat16)
    scores[...] = dot_rounded(own_kept, rows_here, 0)
    direct = dot_rounded(own_kept, annot_ref[...].astype(jnp.bfloat16), 1)
    scores[pl.ds(low_rows, share), :] += direct[0:share, :]
    scores[pl.ds(high_rows, share), :] += direct[share:, :]

    slice_rows = pl.ds(pl.multiple_of(me * wide, 8), wide)
    mine = table[slice_rows, :]
    mine_ref[...] = mine
    product = 1.0
    for pop in range(2):
        own_row = [mine[:, 4 * pop + k : 4 * pop + k + 1] for k in range(4)]
        product *= correlation(own_row, own_row, own_row[3])
    scores[slice_rows, :] += annot_ref[slice_rows, :] * product

    size = wide // 2
    left_places, right_places = owner_places(groups, size)
    left_table, right_table = rows_at(table, left_places, size), rows_at(table, right_places, size)
    local, lane = iota((size, LANES), 0), iota((size, LANES), 1)
    own_row = jnp.concatenate(
        [local + jnp.where(lane < size, a, b) for a, b in zip(left_places, right_places)], axis=0
    )
    shape = own_row.shape
    lane = iota(shape, 1)
    is_left = lane < size
    for pop in range(2):
        for k in range(3):
            column = slice(4 * pop + k, 4 * pop + k + 1)
            rows_ref[3 * pop + k] = jnp.where(is_left, left_table[:, column], right_table[:, column])
    upper = me < groups // 2
    block = lax.axis_index("snp")
    last = reach_ref.shape[0] - 1
    reach_there = jnp.where(
        upper, reach_ref[jnp.minimum(block + 1, last)], reach_ref[jnp.maximum(block - 1, 0)]
    )
    apart = jnp.abs(own_row - (lane + me * wide))
    ahead = (own_row - (lane + me * wide)) * jnp.where(upper, 1, -1) > 0
    real = ahead & (lane < wide) & ((lane >= size) | (iota(shape, 0) < groups * size))
    for number, limit in enumerate((reach_here, reach_there)):
        masks_ref[number] = jnp.where(real & (snps - apart <= limit), 1.0, 0.0)
    their_annots = near_annot_ref[slice_rows, :]
    columns = jnp.concatenate([their_annots, jnp.zeros((LANES - wide, LANES), jnp.float32)], axis=0)
    columns_ref[...] = columns.astype(jnp.bfloat16)
    own_rows_ref[...] = rows_at(annot_ref, left_places + right_places, size).astype(jnp.bfloat16)


def near_score_kernel(groups, share, reach_ref, *refs):
    near_parts, refs = refs[:groups], refs[groups:]
    own_ref, mine_ref, rows_ref, masks_ref, columns_ref, near_annot_ref = refs[:6]
    keep_ref, send_ref, there_ref, far_ref, flipped, scores = refs[6:]
    snps = near_annot_ref.shape[0]
    wide = snps // groups
    size = wide // 2
    tiles = snps // LANES
    me = lax.axis_index("hap")
    reach_here = reach_ref[lax.axis_index("snp")]

    scores[...] = own_ref[...]
    near_sums = sum((part[...] for part in near_parts[1:]), near_parts[0][...])
    near_counts = from_tiles(near_sums[0 : tiles * share, :], share)
    extras = from_fields(near_sums[tiles * share :, :])
    near_stats, near_lines = [], []
    for pop in range(2):
        near_stats.append(column_stats(extras[pop][1:2, :], extras[pop][0:1, :]))
        near_lines += [*near_stats[pop], extras[pop][2:3, :]]
    near_table = jnp.concatenate(near_lines, axis=0).T[0:wide, :]

    slots = [near_counts[:, 0:LANES]]
    for slot in range(1, groups):
        slots.append(pltpu.roll(near_counts, snps - slot * wide, 1)[:, 0:LANES])
    flipped[:, 0:size] = slots[0].T
    slots.append(pltpu.roll(flipped[0:size, :], size, 1))
    near_fields = from_fields(jnp.concatenate(slots, axis=0))
    product = 1.0
    for pop in range(2):
        row_stats = [rows_ref[3 * pop + k] for k in range(3)]
        product *= correlation(row_stats, near_stats[pop], near_fields[pop])
    here = jnp.where(masks_ref[0] > 0.0, product, 0.0)
    there_ref[...] = jnp.where(masks_ref[1] > 0.0, product, 0.0)
    direct = dot_rounded(sides(here, size), columns_ref[...], 1)
    left_places, right_places = owner_places(groups, size)
    for number, place in enumerate(left_places + right_places):
        scores[pl.ds(pl.multiple_of(place, 8), size), :] += direct[number * size : (number + 1) * size, :]

    mine_table = mine_ref[...]
    far_product = 1.0
    for pop in range(2):
        own_row = [mine_table[:, 4 * pop + k : 4 * pop + k + 1] for k in range(3)]
        near_row = [near_table[:, 4 * pop + k : 4 * pop + k + 1] for k in range(4)]
        far_product *= correlation(own_row, near_row, near_row[3])
    far_ref[...] = jnp.broadcast_to(far_product, far_ref.shape)
    slice_rows = pl.ds(pl.multiple_of(me * wide, 8), wide)
    scores[slice_rows, :] += near_annot_ref[slice_rows, :] * jnp.where(reach_here >= snps, far_product, 0.0)

    def packed(step):
        group = partner(me, step, groups)
        return pack_halves(scores[pl.ds(pl.multiple_of(group * wide, 8), wide), :])

    for ref, steps in ((keep_ref, (0, 1)), (send_ref, (2, 3))):
        for number, step in enumerate(steps):
            ref[number * size : (number + 1) * size, :] = packed(step).astype(ref.dtype)


def sides(values, size):
    is_left = iota(values.shape, 1) < size
    return jnp.concatenate(
        [jnp.where(is_left, values, 0.0), jnp.where(is_left, 0.0, values)], axis=0
    )


def there_kernel(groups, reach_ref, there_ref, far_ref, own_rows_ref, annot_ref, out_ref):
    snps = annot_ref.shape[0]
    wide = snps // groups
    me = lax.axis_index("hap")
    block = lax.axis_index("snp")
    last = reach_ref.shape[0] - 1
    reach_there = jnp.where(
        me < groups // 2, reach_ref[jnp.minimum(block + 1, last)], reach_ref[jnp.maximum(block - 1, 0)]
    )
    scores = dot_rounded(sides(there_ref[...], wide // 2), own_rows_ref[...], 0)[0:wide, :]
    slice_rows = pl.ds(pl.multiple_of(me * wide, 8), wide)
    scores += annot_ref[slice_rows, :] * jnp.where(reach_there >= snps, far_ref[...], 0.0)
    out_ref[...] = pack_halves(scores)


def middle_kernel(keep_ref, part_ref, mine_ref, send_ref):
    total = keep_ref[...] + part_ref[...].astype(jnp.float32)
    half = mine_ref.shape[0]
    mine_ref[...] = total[0:half]
    send_ref[...] = total[half:].astype(send_ref.dtype)


def column_finish_kernel(mine_ref, part_ref, there_ref, out_ref):
    packed = mine_ref[...] + part_ref[...].astype(jnp.float32) + there_ref[...]
    out_ref[...] = unpack_halves(packed).T[0 : out_ref.shape[0], :]


def sum_kernel(*refs):
    *parts, own_ref, there_ref = refs
    total = sum((part[...].astype(jnp.float32) for part in parts[1:]), parts[0][...])
    own_ref[...] = total
    half = there_ref.shape[0]
    left = iota((half, LANES), 1) < HALF_LANES
    second = total[half:]
    if second.shape[0] < half:
        second = jnp.concatenate([second, jnp.zeros((half - second.shape[0], LANES))], axis=0)
    there_ref[...] = jnp.where(left, pltpu.roll(total[0:half], HALF_LANES, 1), second)


def finish_kernel(own_ref, there_ref, out_ref):
    annots, rows = out_ref.shape
    there = there_ref[...]
    there = jnp.concatenate([there, pltpu.roll(there, HALF_LANES, 1)], axis=0)
    out_ref[...] = (own_ref[...] + there[0:rows]).T[0:annots, :]


def around(value, groups, step):
    return lax.ppermute(
        value, "hap", [(source, partner(source, step, groups)) for source in range(groups)]
    )


def swapped(value, first):
    pairs = []
    for block in range(first, lax.axis_size("snp") - 1, 2):
        pairs += [(block, block + 1), (block + 1, block)]
    return lax.ppermute(value, "snp", pairs)


def per_device(haplotypes, labels, annotations, reach):
    rows, snps = haplotypes.shape
    half = snps // 2
    groups = lax.axis_size("hap")
    blocks = lax.axis_size("snp")
    share = round_up(-(-half // groups), 16)
    folded_rows = share * groups
    out_share = snps // groups
    padded = half + folded_rows
    annot_part = 32
    bf16, f32, i32 = jnp.bfloat16, jnp.float32, jnp.int32
    shape = jax.ShapeDtypeStruct

    packed = shape((rows // 2 + annot_part, snps), bf16)
    haplotypes = pltpu.with_memory_space_constraint(haplotypes, pltpu.HBM)
    annots_in = pltpu.with_memory_space_constraint(annotations, pltpu.HBM)
    alleles, far, close = call(
        prepare_kernel,
        [shape((rows, snps), bf16), packed, packed],
        [HBM, HBM],
        [
            pltpu.VMEM((rows, snps), i32),
            pltpu.VMEM(annotations.shape, i32),
            pltpu.SemaphoreType.DMA((2 * CHUNKS + 1,)),
        ],
        moved=rows * snps * 8,
    )(haplotypes, annots_in)
    from_far = swapped(far, 1)
    from_close = swapped(close, 0)

    by_column = groups == len(LEFT_BLOCKS)
    compact = shape((share * (snps // LANES) + 8, LANES), i32)
    own_share_counts = compact if by_column else shape((share, snps), i32)
    tile = pltpu.VMEM((snps + 16, snps), f32)
    folded = pltpu.VMEM((folded_rows, snps), i32)
    weighted, totals, *own_parts = call(
        functools.partial(own_kernel, groups, share),
        [shape((snps + 16, rows), bf16), shape((8, snps), f32)] + [own_share_counts] * groups,
        [VMEM, VMEM],
        [tile, folded],
        flops=2 * rows * snps * snps,
        moved=rows * snps * 4,
    )(alleles, labels.reshape(1, rows))
    own_parts = [own_parts[0]] + [around(own_parts[k], groups, k) for k in range(groups - 1, 0, -1)]

    near_shapes = [own_share_counts] + [compact if by_column else shape((share + 8, snps), i32)] * groups
    if by_column:
        piece = shape((snps + 16, LANES), f32)
        work = dict(flops=4 * rows * snps * LANES, moved=rows * snps * 4)
        close_counts = call(close_kernel, [piece, piece], [VMEM] * 2, **work)(weighted, from_close)
        own_sum, *near_parts = call(
            functools.partial(far_kernel, groups, share),
            near_shapes,
            [VMEM] * (5 + groups),
            [
                tile,
                folded,
                pltpu.VMEM((snps, LANES), f32),
                pltpu.VMEM((8 * groups, LANES), i32),
            ],
            **work,
        )(weighted, from_far, *close_counts, totals, *own_parts)
    else:
        own_sum, *near_parts = call(
            functools.partial(near_kernel, groups, share),
            near_shapes,
            [VMEM] * (4 + groups),
            [pltpu.VMEM((rows, snps), bf16), tile, folded],
            flops=2 * rows * snps * snps,
            moved=rows * snps * 4,
        )(weighted, from_far, from_close, totals, *own_parts)
    near_parts = [near_parts[0]] + [around(near_parts[k], groups, k) for k in range(groups - 1, 0, -1)]

    by_snp = shape((snps, LANES), f32)
    own_annots, near_annots = call(annots_kernel, [by_snp, by_snp], [VMEM] * 3, moved=1 << 20)(
        annotations, from_far[rows // 2 :], from_close[rows // 2 :]
    )
    pairs = []
    for block in range(blocks):
        for group in range(groups):
            target = block + 1 if group < groups // 2 else block - 1
            if 0 <= target < blocks:
                pairs.append((block * groups + group, target * groups + group))

    def to_neighbour(value):
        return lax.ppermute(value, ("snp", "hap"), pairs)

    result = shape((annotations.shape[0], out_share), f32)
    half_share = round_up(-(-out_share // 2), 8)
    own_share = shape((out_share, LANES), f32)
    packed_share = shape((half_share, LANES), f32)
    if by_column:
        pair_rows = (groups + 1) * (out_share // 2)
        own_scores, mine, rows_stats, masks, columns, own_rows = call(
            functools.partial(own_score_kernel, groups, share),
            [
                by_snp,
                shape((out_share, LANES), f32),
                shape((6, pair_rows, LANES), f32),
                shape((2, pair_rows, LANES), f32),
                shape((LANES, LANES), bf16),
                shape((2 * pair_rows, LANES), bf16),
            ],
            [SMEM] + [VMEM] * 3,
            [pltpu.VMEM((snps, LANES), f32)],
            flops=1 << 25,
            moved=1 << 20,
        )(reach, own_sum, own_annots, near_annots)
        both = (2 * half_share, LANES)
        keep, send, near_there, far_product = call(
            functools.partial(near_score_kernel, groups, share),
            [shape(both, f32), shape(both, bf16), shape((pair_rows, LANES), f32), own_share],
            [SMEM] + [VMEM] * (groups + 6),
            [pltpu.VMEM((LANES, LANES), i32), pltpu.VMEM((snps, LANES), f32)],
            flops=1 << 26,
            moved=1 << 21,
        )(reach, *near_parts, own_scores, mine, rows_stats, masks, columns, near_annots)
        near_scores = call(
            functools.partial(there_kernel, groups), packed_share, [SMEM] + [VMEM] * 4, moved=1 << 19
        )(reach, near_there, far_product, own_rows, own_annots)
        part = around(send, groups, 2)
        there = to_neighbour(near_scores)
        mine, send = call(
            middle_kernel, [packed_share, shape((half_share, LANES), bf16)], [VMEM] * 2
        )(keep, part)
        part = around(send, groups, 1)
        return call(column_finish_kernel, result, [VMEM] * 3)(mine, part, there)

    tall = pltpu.VMEM((padded, LANES), f32)
    scores = call(
        functools.partial(score_kernel, groups, share),
        [own_share] + [shape((out_share, LANES), bf16)] * (groups - 1),
        [SMEM] + [VMEM] * (groups + 3),
        [tall, tall, tall, tall],
        flops=1 << 26,
        moved=1 << 21,
    )(reach, own_sum, *near_parts, own_annots, near_annots)
    scores = [scores[0]] + [around(scores[k], groups, k) for k in range(groups - 1, 0, -1)]
    own_scores, near_scores = call(sum_kernel, [own_share, packed_share], [VMEM] * groups)(*scores)
    return call(finish_kernel, result, [VMEM] * 2)(own_scores, to_neighbour(near_scores))


def solution(mesh):
    in_specs = (
        P("hap", ("parts", "snp")),
        P(("parts", "hap")),
        P(None, ("parts", "snp")),
        P("parts"),
    )
    out_specs = P(None, ("parts", "snp", "hap"))
    return jax.shard_map(
        per_device, mesh=mesh, in_specs=in_specs, out_specs=out_specs, check_vma=False
    )
```

```python
import functools

import jax
import jax.numpy as jnp
from jax import lax
from jax.experimental import pallas as pl
from jax.experimental.pallas import tpu as pltpu
from jax.sharding import PartitionSpec as P

VARIANCE_FLOOR = 0.01
BASE_BITS = 12
BASE = 1 << BASE_BITS
FIELD_BITS = 16
LANES = 128
HALF_LANES = LANES // 2
CHUNKS = 8
VMEM = pl.BlockSpec(memory_space=pltpu.VMEM)
SMEM = pl.BlockSpec(memory_space=pltpu.SMEM)
HBM = pl.BlockSpec(memory_space=pltpu.HBM)
VMEM_LIMIT = 24 * 1024 * 1024


def iota(shape, axis):
    return lax.broadcasted_iota(jnp.int32, shape, axis)


def round_up(value, step):
    return -(-value // step) * step


def to_fields(values):
    whole = values.astype(jnp.int32)
    return whole + (whole >> BASE_BITS) * ((1 << FIELD_BITS) - BASE)


def from_fields(packed):
    first = packed & ((1 << FIELD_BITS) - 1)
    second = lax.shift_right_logical(packed, FIELD_BITS)
    return first.astype(jnp.float32), second.astype(jnp.float32)


def call(kernel, out_shape, in_specs, scratch_shapes=(), flops=0, moved=0):
    several = isinstance(out_shape, (list, tuple))
    return pl.pallas_call(
        kernel,
        out_shape=out_shape,
        in_specs=in_specs,
        out_specs=[VMEM] * len(out_shape) if several else VMEM,
        scratch_shapes=list(scratch_shapes),
        compiler_params=pltpu.CompilerParams(vmem_limit_bytes=VMEM_LIMIT),
        cost_estimate=pl.CostEstimate(flops=flops, bytes_accessed=moved, transcendentals=0),
    )


def odd_block():
    return lax.rem(lax.axis_index("snp"), 2) == 1


def store_packed(up_ref, down_ref, where, first, second):
    left = iota((first.shape[0], LANES), 1) < HALF_LANES
    middle = first[:, LANES : 2 * LANES]
    turned = pltpu.roll(second[:, LANES : 2 * LANES], HALF_LANES, 1)
    for ref, side, mixed in (
        (up_ref, slice(0, LANES), jnp.where(left, middle, turned)),
        (down_ref, slice(2 * LANES, 3 * LANES), jnp.where(left, turned, middle)),
    ):
        ref[where, 0:LANES] = first[:, side].astype(jnp.bfloat16)
        ref[where, LANES : 2 * LANES] = mixed.astype(jnp.bfloat16)
        ref[where, 2 * LANES : 3 * LANES] = second[:, side].astype(jnp.bfloat16)


def load_packed(up, down):
    left = iota((up.shape[0], LANES), 1) < HALF_LANES
    up_mixed, down_mixed = up[:, LANES : 2 * LANES], down[:, LANES : 2 * LANES]
    first = jnp.where(left, up_mixed, down_mixed)
    second = jnp.where(left, down_mixed, up_mixed)
    second = pltpu.roll(second.astype(jnp.float32), HALF_LANES, 1).astype(second.dtype)
    return (
        (up[:, :LANES], first, down[:, :LANES]),
        (up[:, 2 * LANES :], second, down[:, 2 * LANES :]),
    )


def prepare_kernel(hap_ref, annot_ref, alleles_ref, far_ref, close_ref, held, held_annots, sems):
    rows = hap_ref.shape[0]
    annot_rows = annot_ref.shape[0]
    size = rows // (2 * CHUNKS)
    starts = [side * (rows // 2) + chunk * size for chunk in range(CHUNKS) for side in range(2)]
    copies = [
        pltpu.make_async_copy(
            hap_ref.at[pl.ds(start, size)], held.at[pl.ds(start, size)], sems.at[number]
        )
        for number, start in enumerate(starts)
    ]
    copies.append(pltpu.make_async_copy(annot_ref, held_annots, sems.at[2 * CHUNKS]))
    for copy in copies:
        copy.start()
    part = far_ref.shape[0] - rows // 2
    odd = odd_block()

    def store(where, first, second):
        @pl.when(odd)
        def _():
            store_packed(close_ref, far_ref, where, first, second)

        @pl.when(jnp.logical_not(odd))
        def _():
            store_packed(far_ref, close_ref, where, first, second)

    for chunk in range(CHUNKS):
        pair = []
        for side in range(2):
            number = 2 * chunk + side
            copies[number].wait()
            where = slice(starts[number], starts[number] + size)
            values = held[where, :].astype(jnp.float32)
            alleles_ref[where, :] = values.astype(jnp.bfloat16)
            pair.append(values)
        store(slice(chunk * size, (chunk + 1) * size), *pair)
    copies[-1].wait()
    annots = jnp.concatenate(
        [
            held_annots[...].astype(jnp.float32),
            jnp.zeros((2 * part - annot_rows, annot_ref.shape[1]), jnp.float32),
        ],
        axis=0,
    )
    store(slice(rows // 2, rows // 2 + part), annots[:part], annots[part:])


def partner(group, step, groups):
    if groups & (groups - 1) == 0:
        return group ^ step
    return (group + step) % groups


def send_shares(groups, source, share, targets):
    me = lax.axis_index("hap")
    for step, target in enumerate(targets):
        group = partner(me, step, groups)
        rows = source[pl.ds(pl.multiple_of(group * share, 8), share), :]
        target[0:share, :] = rows.astype(target.dtype)


def send_tiles(groups, source, share, targets):
    me = lax.axis_index("hap")
    for step, target in enumerate(targets):
        owner = partner(me, step, groups)
        counts = source[pl.ds(pl.multiple_of(owner * share, 8), share), :]
        for k in range(source.shape[1] // LANES):
            target[k * share : (k + 1) * share, :] = counts[:, k * LANES : (k + 1) * LANES]


def from_tiles(counts, share):
    tiles = counts.shape[0] // share
    return jnp.concatenate([counts[k * share : (k + 1) * share, :] for k in range(tiles)], axis=1)


def own_kernel(groups, share, alleles_ref, label_ref, *refs):
    weighted_ref, totals_ref, *targets = refs[: 2 + groups]
    tile, folded = refs[2 + groups :]
    rows, snps = alleles_ref.shape
    half = snps // 2
    weight = jnp.where(label_ref[...] > 0, float(BASE), 1.0)
    weighted_ref[0:snps, :] = alleles_ref[...].T * weight.astype(jnp.bfloat16)
    extra = weighted_ref.shape[0] - snps
    weighted_ref[snps:, :] = jnp.broadcast_to(weight, (extra, rows)).astype(jnp.bfloat16)
    tile[...] = jnp.dot(weighted_ref[...], alleles_ref[...], preferred_element_type=jnp.float32)
    count = jnp.sum(weight, axis=1, keepdims=True)
    totals_ref[...] = jnp.concatenate(
        [tile[snps : snps + 1, :], jnp.broadcast_to(count, (1, snps)), jnp.zeros((6, snps))], axis=0
    )
    row, col = iota((half, snps), 0), iota((half, snps), 1)
    moved = (col < half) | (col - half > row)
    turned = pltpu.roll(tile[0:half, :], half, 1)
    folded[0:half, :] = to_fields(jnp.where(moved, turned, tile[half:snps, :]))
    if folded.shape[0] > half:
        folded[half:, :] = jnp.zeros((folded.shape[0] - half, snps), jnp.int32)
    if groups != len(LEFT_BLOCKS):
        send_shares(groups, folded, share, targets)
        return
    tiles = snps // LANES
    shared = [totals_ref[0:1, k * LANES : (k + 1) * LANES] for k in range(tiles)]
    shared += [totals_ref[1:2, 0:LANES], jnp.zeros((7 - tiles, LANES))]
    extras = to_fields(jnp.concatenate(shared, axis=0))
    send_tiles(groups, folded, share, targets)
    for target in targets:
        target[tiles * share :, :] = extras


LEFT_BLOCKS = ((0, 1, 2, 3), (2, 3, 6, 7), (4, 0, 1, 2), (6, 0, 4, 5))
RIGHT_BLOCKS = ((2, 3, 6, 7), (4, 5, 6, 7), (0, 1, 2, 4), (0, 4, 5, 6))


def fold_by_column(tile, flipped, folded):
    owners = len(LEFT_BLOCKS)
    snps = folded.shape[1]
    wide = snps // owners
    size = wide // 2
    shape = (size, snps)
    row, lane = iota(shape, 0), iota(shape, 1)

    def block(number):
        return tile[number * size : (number + 1) * size, :]

    diagonal = block(0)
    for number in range(1, 2 * owners):
        diagonal = jnp.where(lane >= number * size, block(number), diagonal)
    flipped[:, 0:size] = diagonal.T
    corner = diagonal
    for owner in range(owners):
        start = (2 * owner + 1) * size
        turned = jnp.concatenate(
            [flipped[start : start + size, :], jnp.zeros((size, snps - LANES), jnp.float32)], axis=1
        )
        if owner:
            turned = pltpu.roll(turned, owner * wide, 1)
        inside = lane - owner * wide
        other = (row <= inside) if owner < owners // 2 else (row >= inside)
        corner = jnp.where((inside >= 0) & (inside < size) & other, turned, corner)
    rolled = []
    for shift in range(owners):
        mixed = None
        for owner in range(owners):
            slot = (owner + shift) % owners
            left = block(LEFT_BLOCKS[owner][slot]) if slot else corner
            start = owner * wide
            mixed = left if mixed is None else jnp.where(lane >= start, left, mixed)
            mixed = jnp.where(lane >= start + size, block(RIGHT_BLOCKS[owner][slot]), mixed)
        rolled.append(pltpu.roll(mixed, shift * wide, 1) if shift else mixed)
    for owner in range(owners):
        mixed = rolled[(0 - owner) % owners]
        for slot in range(1, owners):
            mixed = jnp.where(lane >= slot * wide, rolled[(slot - owner) % owners], mixed)
        folded[owner * size : (owner + 1) * size, :] = to_fields(mixed)


def above(far):
    return odd_block() == far


def side_dot(weighted_ref, side_ref):
    rows = weighted_ref.shape[1]
    half = rows // 2

    def dot(which, columns):
        return jnp.dot(
            weighted_ref[:, which], side_ref[0:half, columns], preferred_element_type=jnp.float32
        )

    first = dot(slice(0, half), slice(0, 2 * LANES))
    second = dot(slice(half, rows), slice(LANES, 3 * LANES))
    whole = first[:, 0:LANES] + second[:, LANES:]
    return whole, first[:, LANES:] + pltpu.roll(second[:, 0:LANES], HALF_LANES, 1)


def close_kernel(weighted_ref, side_ref, whole_ref, shared_ref):
    whole_ref[...], shared_ref[...] = side_dot(weighted_ref, side_ref)


def far_kernel(
    groups, share, weighted_ref, side_ref, whole_ref, shared_ref, totals_ref, mine_ref, nearest_ref, own_sum_ref, *refs
):
    targets, (tile, folded, flipped, extras) = refs[:groups], refs[groups:]
    snps = tile.shape[1]
    own_sum_ref[...] = mine_ref[...] + nearest_ref[...]
    whole, shared = side_dot(weighted_ref, side_ref)
    left = iota(shared.shape, 1) < HALF_LANES

    @pl.when(above(True))
    def _():
        tile[:, 0:LANES] = whole
        tile[:, LANES : 2 * LANES] = jnp.where(left, shared, shared_ref[...])
        tile[:, 2 * LANES :] = whole_ref[...]

    @pl.when(jnp.logical_not(above(True)))
    def _():
        tile[:, 0:LANES] = whole_ref[...]
        tile[:, LANES : 2 * LANES] = jnp.where(left, shared_ref[...], shared)
        tile[:, 2 * LANES :] = whole

    fold_by_column(tile, flipped, folded)
    square = (snps, snps)
    apart = jnp.sum(
        jnp.where(iota(square, 0) == iota(square, 1), tile[0:snps, :], 0.0), axis=0, keepdims=True
    )
    tiles = snps // LANES
    sizes = totals_ref[1:2, :]
    by_column = jnp.concatenate([sizes, tile[snps : snps + 1, :], apart, jnp.zeros((5, snps))], axis=0)
    for owner in range(groups):
        start = owner * (snps // groups)
        columns = pltpu.roll(by_column, snps - start, 1) if owner else by_column
        extras[8 * owner : 8 * (owner + 1), :] = to_fields(columns[:, 0:LANES])
    me = lax.axis_index("hap")
    send_tiles(groups, folded, share, targets)
    for step, target in enumerate(targets):
        owner = partner(me, step, groups)
        target[tiles * share :, :] = extras[pl.ds(pl.multiple_of(owner * 8, 8), 8), :]


def near_kernel(groups, share, weighted_ref, far_ref, close_ref, totals_ref, *refs):
    own_parts, own_sum_ref = refs[:groups], refs[groups]
    targets, (near, tile, folded) = refs[groups + 1 : 2 * groups + 1], refs[2 * groups + 1 :]
    rows, snps = near.shape
    half = snps // 2
    odd = odd_block()

    def unpack(up_ref, down_ref):
        pieces = load_packed(up_ref[0 : rows // 2, :], down_ref[0 : rows // 2, :])
        for side in range(2):
            where = slice(side * (rows // 2), (side + 1) * (rows // 2))
            for number in range(3):
                near[where, number * LANES : (number + 1) * LANES] = pieces[side][number]

    @pl.when(odd)
    def _():
        unpack(far_ref, close_ref)

    @pl.when(jnp.logical_not(odd))
    def _():
        unpack(close_ref, far_ref)

    tile[...] = jnp.dot(weighted_ref[...], near[...], preferred_element_type=jnp.float32)
    row, col = iota((half, snps), 0), iota((half, snps), 1)
    moved = (col >= half) & (col - half < row)
    turned = pltpu.roll(tile[0:half, :], half, 1)
    folded[0:half, :] = to_fields(jnp.where(moved, turned, tile[half:snps, :]))
    if folded.shape[0] > half:
        folded[half:, :] = jnp.zeros((folded.shape[0] - half, snps), jnp.int32)
    square = (snps, snps)
    far = jnp.sum(
        jnp.where(iota(square, 0) == iota(square, 1), tile[0:snps, :], 0.0), axis=0, keepdims=True
    )
    extras = to_fields(
        jnp.concatenate(
            [totals_ref[0:2, :], tile[snps : snps + 1, :], far, jnp.zeros((4, snps))], axis=0
        )
    )
    send_shares(groups, folded, share, targets)
    for target in targets:
        target[share:, :] = extras
    own_sum_ref[...] = sum((part[...] for part in own_parts[1:]), own_parts[0][...])


def annots_kernel(annot_ref, far_ref, close_ref, own_ref, near_ref):
    snps = annot_ref.shape[1]
    part = far_ref.shape[0]
    wide = 2 * part
    own = annot_ref[...].astype(jnp.float32)
    own = jnp.concatenate([own, jnp.zeros((LANES - own.shape[0], snps), jnp.float32)], axis=0)
    own_ref[...] = own.T
    odd = odd_block()
    far, close = far_ref[...].astype(jnp.float32), close_ref[...].astype(jnp.float32)
    first, second = load_packed(jnp.where(odd, far, close), jnp.where(odd, close, far))
    near = jnp.concatenate(
        [
            jnp.concatenate([piece.astype(jnp.float32) for piece in first], axis=1),
            jnp.concatenate([piece.astype(jnp.float32) for piece in second], axis=1),
            jnp.zeros((LANES - wide, snps), jnp.float32),
        ],
        axis=0,
    )
    near_ref[...] = near.T


def column_stats(totals, count):
    size = jnp.maximum(count, 1.0)
    frequency = totals / size
    variance = jnp.maximum(frequency * (1.0 - frequency), VARIANCE_FLOOR)
    inverse = 1.0 / jnp.sqrt(size * variance)
    low = ((0.0 - frequency) * inverse).astype(jnp.bfloat16).astype(jnp.float32)
    high = ((1.0 - frequency) * inverse).astype(jnp.bfloat16).astype(jnp.float32)
    step = high - low
    root = 1.0 / jnp.sqrt(size)
    return step, step * totals * root, (low * count + step * totals) * root


def correlation(row, col, count):
    return row[0] * col[0] * count - row[1] * col[1] + row[2] * col[2]


def split(values):
    high = values.astype(jnp.bfloat16)
    return high, (values - high.astype(jnp.float32)).astype(jnp.bfloat16)


def dot_split(values, right, axis):
    dims = (((axis,), (0,)), ((), ()))
    return sum(
        lax.dot_general(part, right, dims, preferred_element_type=jnp.float32)
        for part in split(values)
    )


def score_kernel(groups, share, reach_ref, *refs):
    own_sum_ref, near_parts = refs[0], refs[1 : groups + 1]
    annot_ref, near_annot_ref = refs[groups + 1 : groups + 3]
    targets = refs[groups + 3 : 2 * groups + 3]
    table, annots, near_annots, scores = refs[2 * groups + 3 :]
    snps = annot_ref.shape[0]
    half = snps // 2
    out_share = snps // groups
    me = lax.axis_index("hap")
    block = lax.axis_index("snp")
    last = reach_ref.shape[0] - 1
    reach_here = reach_ref[block]
    reach_up = reach_ref[jnp.minimum(block + 1, last)]
    reach_down = reach_ref[jnp.maximum(block - 1, 0)]

    own_counts = own_sum_ref[...]
    near_sums = sum((part[...] for part in near_parts[1:]), near_parts[0][...])
    extras = from_fields(near_sums[share:, :])
    near_counts = near_sums[0:share, :]

    own_stats, near_stats, lines = [], [], []
    for pop in range(2):
        count = extras[pop][1:2, :]
        own_stats.append(column_stats(extras[pop][0:1, :], count))
        near_stats.append(column_stats(extras[pop][2:3, :], count))
        lines += [*own_stats[pop], *near_stats[pop], extras[pop][0:1, :], extras[pop][3:4, :]]
    by_row = jnp.concatenate(lines, axis=0).T
    table[0:snps, 0:16] = by_row
    if table.shape[0] > snps:
        table[snps:, 0:16] = jnp.zeros((table.shape[0] - snps, 16), jnp.float32)
    annots[0:snps, :] = annot_ref[...]
    near_annots[0:snps, :] = near_annot_ref[...]
    if annots.shape[0] > snps:
        annots[snps:, :] = jnp.zeros((annots.shape[0] - snps, LANES), jnp.float32)

    low_rows = pl.multiple_of(me * share, 8)
    high_rows = pl.multiple_of(half + me * share, 8)

    def both(ref):
        return jnp.concatenate([ref[pl.ds(low_rows, share), :], ref[pl.ds(high_rows, share), :]], axis=0)

    here = both(table)
    own_count = jnp.concatenate([pltpu.roll(own_counts, half, 1), own_counts], axis=0)
    near_count = jnp.concatenate([pltpu.roll(near_counts, half, 1), near_counts], axis=0)
    shape = (2 * share, snps)
    local, col = iota(shape, 0), iota(shape, 1)
    low = local < share
    place = jnp.where(low, local, local - share) + me * share
    row = jnp.where(low, place, place + half)
    own_fields, near_fields = from_fields(own_count), from_fields(near_count)
    own_product, near_product = 1.0, 1.0
    for pop in range(2):
        row_stats = [here[:, 8 * pop + k : 8 * pop + k + 1] for k in range(3)]
        own_product *= correlation(row_stats, own_stats[pop], own_fields[pop])
        near_product *= correlation(row_stats, near_stats[pop], near_fields[pop])
    real = place < half
    own_inside = real & ((low & (col > row)) | (~low & (col >= half) & (col < row)))
    own_inside &= jnp.abs(col - row) <= reach_here
    own_kept = jnp.where(own_inside, own_product, 0.0)
    in_upper = col < half
    near_inside = real & ((low & (col < row)) | (~low & (in_upper | (col > row))))
    distance = jnp.where(in_upper, snps + col - row, snps + row - col)
    near_here = jnp.where(near_inside & (distance <= reach_here), near_product, 0.0)
    reach_there = jnp.where(in_upper, reach_up, reach_down)
    near_there = jnp.where(near_inside & (distance <= reach_there), near_product, 0.0)

    rows_here = both(annots)
    rows_there = pltpu.roll(rows_here, HALF_LANES, 1)
    scores[0:snps, :] = dot_split(
        jnp.concatenate([own_kept, near_there], axis=0),
        jnp.concatenate([rows_here, rows_there], axis=0).astype(jnp.bfloat16),
        0,
    )
    direct = dot_split(
        jnp.concatenate([own_kept, near_here], axis=1),
        jnp.concatenate([annot_ref[...], near_annot_ref[...]], axis=0).astype(jnp.bfloat16),
        1,
    )
    scores[pl.ds(low_rows, share), :] += direct[0:share, :]
    scores[pl.ds(high_rows, share), :] += direct[share:, :]

    out_rows = pl.ds(pl.multiple_of(me * out_share, 8), out_share)
    mine = table[out_rows, :]
    self_product, far_product = 1.0, 1.0
    for pop in range(2):
        k = 8 * pop
        own_row = [mine[:, k + s : k + s + 1] for s in range(3)]
        near_row = [mine[:, k + 3 + s : k + 4 + s] for s in range(3)]
        self_product *= correlation(own_row, own_row, mine[:, k + 6 : k + 7])
        far_product *= correlation(own_row, near_row, mine[:, k + 7 : k + 8])
    mine_annots = annots[out_rows, :]
    far_reach = jnp.where(me < groups // 2, reach_up, reach_down)
    scores[out_rows, :] += (
        mine_annots * self_product
        + near_annots[out_rows, :] * jnp.where(reach_here >= snps, far_product, 0.0)
        + pltpu.roll(mine_annots, HALF_LANES, 1) * jnp.where(far_reach >= snps, far_product, 0.0)
    )
    send_shares(groups, scores, out_share, targets)


def pack_halves(values):
    half = values.shape[0] // 2
    left = iota((half, LANES), 1) < HALF_LANES
    return jnp.where(left, values[0:half], pltpu.roll(values[half:], HALF_LANES, 1))


def unpack_halves(packed):
    return jnp.concatenate([packed, pltpu.roll(packed, HALF_LANES, 1)], axis=0)


def dot_rounded(values, right, axis):
    dims = (((axis,), (0,)), ((), ()))
    return lax.dot_general(
        values.astype(jnp.bfloat16), right, dims, preferred_element_type=jnp.float32
    )


def owner_places(groups, size):
    me = lax.axis_index("hap")

    def mine(blocks, slot):
        value = blocks[0][slot]
        for group in range(1, groups):
            value = jnp.where(me == group, blocks[group][slot], value)
        return value * size

    left = [mine(LEFT_BLOCKS, slot) for slot in range(groups)]
    right = [mine(RIGHT_BLOCKS, slot) for slot in range(groups)]
    return left + left[0:1], right + [(2 * me + 1) * size]


def rows_at(ref, places, size):
    return jnp.concatenate([ref[pl.ds(pl.multiple_of(place, 8), size), :] for place in places], axis=0)


def own_score_kernel(
    groups, share, reach_ref, *refs
):
    own_parts, refs = refs[: groups - 1], refs[groups - 1 :]
    annot_ref, near_annot_ref, scores, mine_ref, rows_ref, masks_ref, columns_ref, own_rows_ref, table = refs
    snps = annot_ref.shape[0]
    half = snps // 2
    wide = snps // groups
    tiles = snps // LANES
    me = lax.axis_index("hap")
    reach_here = reach_ref[lax.axis_index("snp")]
    own_sums = sum((part[...] for part in own_parts[1:]), own_parts[0][...])
    own_counts = from_tiles(own_sums[0 : tiles * share, :], share)
    extras = from_fields(own_sums[tiles * share :, :])

    own_stats, lines = [], []
    for pop in range(2):
        count = jnp.concatenate([extras[pop][tiles : tiles + 1, :]] * tiles, axis=1)
        totals = jnp.concatenate([extras[pop][k : k + 1, :] for k in range(tiles)], axis=1)
        own_stats.append(column_stats(totals, count))
        lines += [*own_stats[pop], totals]
    table[:, 0:8] = jnp.concatenate(lines, axis=0).T

    low_rows = pl.multiple_of(me * share, 8)
    high_rows = pl.multiple_of(half + me * share, 8)

    def both(ref):
        return jnp.concatenate([ref[pl.ds(low_rows, share), :], ref[pl.ds(high_rows, share), :]], axis=0)

    here = both(table)
    own_fields = from_fields(
        jnp.concatenate([pltpu.roll(own_counts, half, 1), own_counts], axis=0)
    )
    shape = (2 * share, snps)
    local, col = iota(shape, 0), iota(shape, 1)
    low = local < share
    row = jnp.where(low, local, local + half - share) + me * share
    product = 1.0
    for pop in range(2):
        row_stats = [here[:, 4 * pop + k : 4 * pop + k + 1] for k in range(3)]
        product *= correlation(row_stats, own_stats[pop], own_fields[pop])
    inside = (low & (col > row)) | (~low & (col >= half) & (col < row))
    own_kept = jnp.where(inside & (jnp.abs(col - row) <= reach_here), product, 0.0)
    rows_here = both(annot_ref).astype(jnp.bfloat16)
    scores[...] = dot_rounded(own_kept, rows_here, 0)
    direct = dot_rounded(own_kept, annot_ref[...].astype(jnp.bfloat16), 1)
    scores[pl.ds(low_rows, share), :] += direct[0:share, :]
    scores[pl.ds(high_rows, share), :] += direct[share:, :]

    slice_rows = pl.ds(pl.multiple_of(me * wide, 8), wide)
    mine = table[slice_rows, :]
    mine_ref[...] = mine
    product = 1.0
    for pop in range(2):
        own_row = [mine[:, 4 * pop + k : 4 * pop + k + 1] for k in range(4)]
        product *= correlation(own_row, own_row, own_row[3])
    scores[slice_rows, :] += annot_ref[slice_rows, :] * product

    size = wide // 2
    left_places, right_places = owner_places(groups, size)
    left_table, right_table = rows_at(table, left_places, size), rows_at(table, right_places, size)
    local, lane = iota((size, LANES), 0), iota((size, LANES), 1)
    own_row = jnp.concatenate(
        [local + jnp.where(lane < size, a, b) for a, b in zip(left_places, right_places)], axis=0
    )
    shape = own_row.shape
    lane = iota(shape, 1)
    is_left = lane < size
    for pop in range(2):
        for k in range(3):
            column = slice(4 * pop + k, 4 * pop + k + 1)
            rows_ref[3 * pop + k] = jnp.where(is_left, left_table[:, column], right_table[:, column])
    upper = me < groups // 2
    block = lax.axis_index("snp")
    last = reach_ref.shape[0] - 1
    reach_there = jnp.where(
        upper, reach_ref[jnp.minimum(block + 1, last)], reach_ref[jnp.maximum(block - 1, 0)]
    )
    apart = jnp.abs(own_row - (lane + me * wide))
    ahead = (own_row - (lane + me * wide)) * jnp.where(upper, 1, -1) > 0
    real = ahead & (lane < wide) & ((lane >= size) | (iota(shape, 0) < groups * size))
    for number, limit in enumerate((reach_here, reach_there)):
        masks_ref[number] = jnp.where(real & (snps - apart <= limit), 1.0, 0.0)
    theirs = near_annot_ref[slice_rows, :]
    columns = [theirs[0:size], pltpu.roll(theirs[size:], HALF_LANES, 1), jnp.zeros((LANES - wide, LANES))]
    columns_ref[...] = jnp.concatenate(columns, axis=0).astype(jnp.bfloat16)
    own_rows = rows_at(annot_ref, left_places, size) + pltpu.roll(
        rows_at(annot_ref, right_places, size), HALF_LANES, 1
    )
    own_rows_ref[...] = own_rows.astype(jnp.bfloat16)


def near_score_kernel(groups, share, reach_ref, *refs):
    near_parts, refs = refs[:groups], refs[groups:]
    own_ref, mine_ref, rows_ref, masks_ref, columns_ref, own_rows_ref, annot_ref, near_annot_ref = refs[:8]
    keep_ref, send_ref, near_out_ref, flipped, scores = refs[8:]
    snps = annot_ref.shape[0]
    wide = snps // groups
    size = wide // 2
    tiles = snps // LANES
    me = lax.axis_index("hap")
    block = lax.axis_index("snp")
    last = reach_ref.shape[0] - 1
    reach_here = reach_ref[block]
    reach_there = jnp.where(
        me < groups // 2, reach_ref[jnp.minimum(block + 1, last)], reach_ref[jnp.maximum(block - 1, 0)]
    )

    scores[...] = own_ref[...]
    near_sums = sum((part[...] for part in near_parts[1:]), near_parts[0][...])
    near_counts = from_tiles(near_sums[0 : tiles * share, :], share)
    extras = from_fields(near_sums[tiles * share :, :])
    near_stats, near_lines = [], []
    for pop in range(2):
        near_stats.append(column_stats(extras[pop][1:2, :], extras[pop][0:1, :]))
        near_lines += [*near_stats[pop], extras[pop][2:3, :]]
    near_table = jnp.concatenate(near_lines, axis=0).T[0:wide, :]

    slots = [near_counts[:, 0:LANES]]
    for slot in range(1, groups):
        slots.append(pltpu.roll(near_counts, snps - slot * wide, 1)[:, 0:LANES])
    flipped[:, 0:size] = slots[0].T
    slots.append(pltpu.roll(flipped[0:size, :], size, 1))
    near_fields = from_fields(jnp.concatenate(slots, axis=0))
    product = 1.0
    for pop in range(2):
        row_stats = [rows_ref[3 * pop + k] for k in range(3)]
        product *= correlation(row_stats, near_stats[pop], near_fields[pop])
    near_here = jnp.where(masks_ref[0] > 0.0, product, 0.0)
    near_there = jnp.where(masks_ref[1] > 0.0, product, 0.0)
    slice_rows = pl.ds(pl.multiple_of(me * wide, 8), wide)
    direct = dot_rounded(near_here, columns_ref[...], 1)
    turned = pltpu.roll(direct, HALF_LANES, 1)
    for values, places in zip((direct, turned), owner_places(groups, size)):
        for slot, place in enumerate(places):
            scores[pl.ds(pl.multiple_of(place, 8), size), :] += values[slot * size : (slot + 1) * size, :]
    near_scores = dot_rounded(near_there, own_rows_ref[...], 0)
    near_scores = jnp.where(
        iota((size, LANES), 1) < HALF_LANES, near_scores[0:size], near_scores[size:wide]
    )

    mine_table = mine_ref[...]
    far_product = 1.0
    for pop in range(2):
        own_row = [mine_table[:, 4 * pop + k : 4 * pop + k + 1] for k in range(3)]
        near_row = [near_table[:, 4 * pop + k : 4 * pop + k + 1] for k in range(4)]
        far_product *= correlation(own_row, near_row, near_row[3])
    scores[slice_rows, :] += near_annot_ref[slice_rows, :] * jnp.where(reach_here >= snps, far_product, 0.0)
    far_scores = annot_ref[slice_rows, :] * jnp.where(reach_there >= snps, far_product, 0.0)
    near_out_ref[...] = near_scores + pack_halves(far_scores)

    def packed(step):
        group = partner(me, step, groups)
        return pack_halves(scores[pl.ds(pl.multiple_of(group * wide, 8), wide), :])

    for ref, steps in ((keep_ref, (0, 1)), (send_ref, (2, 3))):
        for number, step in enumerate(steps):
            ref[number * size : (number + 1) * size, :] = packed(step).astype(ref.dtype)


def middle_kernel(keep_ref, part_ref, mine_ref, send_ref):
    total = keep_ref[...] + part_ref[...].astype(jnp.float32)
    half = mine_ref.shape[0]
    mine_ref[...] = total[0:half]
    send_ref[...] = total[half:].astype(send_ref.dtype)


def column_finish_kernel(mine_ref, part_ref, there_ref, out_ref):
    packed = mine_ref[...] + part_ref[...].astype(jnp.float32) + there_ref[...]
    out_ref[...] = unpack_halves(packed).T[0 : out_ref.shape[0], :]


def sum_kernel(*refs):
    *parts, own_ref, there_ref = refs
    total = sum((part[...].astype(jnp.float32) for part in parts[1:]), parts[0][...])
    own_ref[...] = total
    half = there_ref.shape[0]
    left = iota((half, LANES), 1) < HALF_LANES
    second = total[half:]
    if second.shape[0] < half:
        second = jnp.concatenate([second, jnp.zeros((half - second.shape[0], LANES))], axis=0)
    there_ref[...] = jnp.where(left, pltpu.roll(total[0:half], HALF_LANES, 1), second)


def finish_kernel(own_ref, there_ref, out_ref):
    annots, rows = out_ref.shape
    there = there_ref[...]
    there = jnp.concatenate([there, pltpu.roll(there, HALF_LANES, 1)], axis=0)
    out_ref[...] = (own_ref[...] + there[0:rows]).T[0:annots, :]


def around(value, groups, step):
    return lax.ppermute(
        value, "hap", [(source, partner(source, step, groups)) for source in range(groups)]
    )


def swapped(value, first):
    pairs = []
    for block in range(first, lax.axis_size("snp") - 1, 2):
        pairs += [(block, block + 1), (block + 1, block)]
    return lax.ppermute(value, "snp", pairs)


def per_device(haplotypes, labels, annotations, reach):
    rows, snps = haplotypes.shape
    half = snps // 2
    groups = lax.axis_size("hap")
    blocks = lax.axis_size("snp")
    share = round_up(-(-half // groups), 16)
    folded_rows = share * groups
    out_share = snps // groups
    padded = half + folded_rows
    annot_part = 32
    bf16, f32, i32 = jnp.bfloat16, jnp.float32, jnp.int32
    shape = jax.ShapeDtypeStruct

    packed = shape((rows // 2 + annot_part, snps), bf16)
    haplotypes = pltpu.with_memory_space_constraint(haplotypes, pltpu.HBM)
    annots_in = pltpu.with_memory_space_constraint(annotations, pltpu.HBM)
    alleles, far, close = call(
        prepare_kernel,
        [shape((rows, snps), bf16), packed, packed],
        [HBM, HBM],
        [
            pltpu.VMEM((rows, snps), i32),
            pltpu.VMEM(annotations.shape, i32),
            pltpu.SemaphoreType.DMA((2 * CHUNKS + 1,)),
        ],
        moved=rows * snps * 8,
    )(haplotypes, annots_in)
    from_far = swapped(far, 1)
    from_close = swapped(close, 0)

    by_column = groups == len(LEFT_BLOCKS)
    compact = shape((share * (snps // LANES) + 8, LANES), i32)
    own_share_counts = compact if by_column else shape((share, snps), i32)
    tile = pltpu.VMEM((snps + 16, snps), f32)
    folded = pltpu.VMEM((folded_rows, snps), i32)
    weighted, totals, *own_parts = call(
        functools.partial(own_kernel, groups, share),
        [shape((snps + 16, rows), bf16), shape((8, snps), f32)] + [own_share_counts] * groups,
        [VMEM, VMEM],
        [tile, folded],
        flops=2 * rows * snps * snps,
        moved=rows * snps * 4,
    )(alleles, labels.reshape(1, rows))
    own_parts = [own_parts[0]] + [around(own_parts[k], groups, k) for k in range(groups - 1, 0, -1)]

    near_shapes = [own_share_counts] + [compact if by_column else shape((share + 8, snps), i32)] * groups
    if by_column:
        piece = shape((snps + 16, LANES), f32)
        work = dict(flops=4 * rows * snps * LANES, moved=rows * snps * 4)
        close_counts = call(close_kernel, [piece, piece], [VMEM] * 2, **work)(weighted, from_close)
        own_sum, *near_parts = call(
            functools.partial(far_kernel, groups, share),
            near_shapes,
            [VMEM] * 7,
            [
                tile,
                folded,
                pltpu.VMEM((snps, LANES), f32),
                pltpu.VMEM((8 * groups, LANES), i32),
            ],
            **work,
        )(weighted, from_far, *close_counts, totals, own_parts[0], own_parts[-1])
    else:
        own_sum, *near_parts = call(
            functools.partial(near_kernel, groups, share),
            near_shapes,
            [VMEM] * (4 + groups),
            [pltpu.VMEM((rows, snps), bf16), tile, folded],
            flops=2 * rows * snps * snps,
            moved=rows * snps * 4,
        )(weighted, from_far, from_close, totals, *own_parts)
    near_parts = [near_parts[0]] + [around(near_parts[k], groups, k) for k in range(groups - 1, 0, -1)]

    by_snp = shape((snps, LANES), f32)
    own_annots, near_annots = call(annots_kernel, [by_snp, by_snp], [VMEM] * 3, moved=1 << 20)(
        annotations, from_far[rows // 2 :], from_close[rows // 2 :]
    )
    pairs = []
    for block in range(blocks):
        for group in range(groups):
            target = block + 1 if group < groups // 2 else block - 1
            if 0 <= target < blocks:
                pairs.append((block * groups + group, target * groups + group))

    def to_neighbour(value):
        return lax.ppermute(value, ("snp", "hap"), pairs)

    result = shape((annotations.shape[0], out_share), f32)
    half_share = round_up(-(-out_share // 2), 8)
    own_share = shape((out_share, LANES), f32)
    packed_share = shape((half_share, LANES), f32)
    if by_column:
        pair_rows = (groups + 1) * (out_share // 2)
        prepared = call(
            functools.partial(own_score_kernel, groups, share),
            [
                by_snp,
                shape((out_share, LANES), f32),
                shape((6, pair_rows, LANES), f32),
                shape((2, pair_rows, LANES), f32),
                shape((LANES, LANES), bf16),
                shape((pair_rows, LANES), bf16),
            ],
            [SMEM] + [VMEM] * (groups + 1),
            [pltpu.VMEM((snps, LANES), f32)],
            flops=1 << 25,
            moved=1 << 20,
        )(reach, own_sum, *own_parts[1:-1], own_annots, near_annots)
        both = (2 * half_share, LANES)
        keep, send, near_scores = call(
            functools.partial(near_score_kernel, groups, share),
            [shape(both, f32), shape(both, bf16), packed_share],
            [SMEM] + [VMEM] * (groups + 8),
            [pltpu.VMEM((LANES, LANES), i32), pltpu.VMEM((snps, LANES), f32)],
            flops=1 << 26,
            moved=1 << 21,
        )(reach, *near_parts, *prepared, own_annots, near_annots)
        part = around(send, groups, 2)
        there = to_neighbour(near_scores)
        mine, send = call(
            middle_kernel, [packed_share, shape((half_share, LANES), bf16)], [VMEM] * 2
        )(keep, part)
        part = around(send, groups, 1)
        return call(column_finish_kernel, result, [VMEM] * 3)(mine, part, there)

    tall = pltpu.VMEM((padded, LANES), f32)
    scores = call(
        functools.partial(score_kernel, groups, share),
        [own_share] + [shape((out_share, LANES), bf16)] * (groups - 1),
        [SMEM] + [VMEM] * (groups + 3),
        [tall, tall, tall, tall],
        flops=1 << 26,
        moved=1 << 21,
    )(reach, own_sum, *near_parts, own_annots, near_annots)
    scores = [scores[0]] + [around(scores[k], groups, k) for k in range(groups - 1, 0, -1)]
    own_scores, near_scores = call(sum_kernel, [own_share, packed_share], [VMEM] * groups)(*scores)
    return call(finish_kernel, result, [VMEM] * 2)(own_scores, to_neighbour(near_scores))


def solution(mesh):
    in_specs = (
        P("hap", ("parts", "snp")),
        P(("parts", "hap")),
        P(None, ("parts", "snp")),
        P("parts"),
    )
    out_specs = P(None, ("parts", "snp", "hap"))
    return jax.shard_map(
        per_device, mesh=mesh, in_specs=in_specs, out_specs=out_specs, check_vma=False
    )
```

```python
import functools

import jax
import jax.numpy as jnp
from jax import lax
from jax.experimental import pallas as pl
from jax.experimental.pallas import tpu as pltpu
from jax.sharding import PartitionSpec as P

VARIANCE_FLOOR = 0.01
BASE_BITS = 12
BASE = 1 << BASE_BITS
FIELD_BITS = 16
LANES = 128
HALF_LANES = LANES // 2
CHUNKS = 4
VMEM = pl.BlockSpec(memory_space=pltpu.VMEM)
SMEM = pl.BlockSpec(memory_space=pltpu.SMEM)
HBM = pl.BlockSpec(memory_space=pltpu.HBM)
VMEM_LIMIT = 24 * 1024 * 1024


def iota(shape, axis):
    return lax.broadcasted_iota(jnp.int32, shape, axis)


def round_up(value, step):
    return -(-value // step) * step


def to_fields(values):
    whole = values.astype(jnp.int32)
    return whole + (whole >> BASE_BITS) * ((1 << FIELD_BITS) - BASE)


def from_fields(packed):
    first = packed & ((1 << FIELD_BITS) - 1)
    second = lax.shift_right_logical(packed, FIELD_BITS)
    return first.astype(jnp.float32), second.astype(jnp.float32)


def call(kernel, out_shape, in_specs, scratch_shapes=(), flops=0, moved=0):
    several = isinstance(out_shape, (list, tuple))
    return pl.pallas_call(
        kernel,
        out_shape=out_shape,
        in_specs=in_specs,
        out_specs=[VMEM] * len(out_shape) if several else VMEM,
        scratch_shapes=list(scratch_shapes),
        compiler_params=pltpu.CompilerParams(vmem_limit_bytes=VMEM_LIMIT),
        cost_estimate=pl.CostEstimate(flops=flops, bytes_accessed=moved, transcendentals=0),
    )


def odd_block():
    return lax.rem(lax.axis_index("snp"), 2) == 1


def store_packed(up_ref, down_ref, where, first, second):
    left = iota((first.shape[0], LANES), 1) < HALF_LANES
    middle = first[:, LANES : 2 * LANES]
    turned = pltpu.roll(second[:, LANES : 2 * LANES], HALF_LANES, 1)
    for ref, side, mixed in (
        (up_ref, slice(0, LANES), jnp.where(left, middle, turned)),
        (down_ref, slice(2 * LANES, 3 * LANES), jnp.where(left, turned, middle)),
    ):
        ref[where, 0:LANES] = first[:, side].astype(jnp.bfloat16)
        ref[where, LANES : 2 * LANES] = mixed.astype(jnp.bfloat16)
        ref[where, 2 * LANES : 3 * LANES] = second[:, side].astype(jnp.bfloat16)


def load_packed(up, down):
    left = iota((up.shape[0], LANES), 1) < HALF_LANES
    up_mixed, down_mixed = up[:, LANES : 2 * LANES], down[:, LANES : 2 * LANES]
    first = jnp.where(left, up_mixed, down_mixed)
    second = jnp.where(left, down_mixed, up_mixed)
    second = pltpu.roll(second.astype(jnp.float32), HALF_LANES, 1).astype(second.dtype)
    return (
        (up[:, :LANES], first, down[:, :LANES]),
        (up[:, 2 * LANES :], second, down[:, 2 * LANES :]),
    )


def prepare_kernel(hap_ref, annot_ref, alleles_ref, far_ref, close_ref, held, held_annots, sems):
    rows = hap_ref.shape[0]
    annot_rows = annot_ref.shape[0]
    size = rows // (2 * CHUNKS)
    starts = [side * (rows // 2) + chunk * size for chunk in range(CHUNKS) for side in range(2)]
    copies = [
        pltpu.make_async_copy(
            hap_ref.at[pl.ds(start, size)], held.at[pl.ds(start, size)], sems.at[number]
        )
        for number, start in enumerate(starts)
    ]
    copies.append(pltpu.make_async_copy(annot_ref, held_annots, sems.at[2 * CHUNKS]))
    for copy in copies:
        copy.start()
    part = far_ref.shape[0] - rows // 2
    odd = odd_block()

    def store(where, first, second):
        @pl.when(odd)
        def _():
            store_packed(close_ref, far_ref, where, first, second)

        @pl.when(jnp.logical_not(odd))
        def _():
            store_packed(far_ref, close_ref, where, first, second)

    for chunk in range(CHUNKS):
        pair = []
        for side in range(2):
            number = 2 * chunk + side
            copies[number].wait()
            where = slice(starts[number], starts[number] + size)
            values = held[where, :].astype(jnp.float32)
            alleles_ref[where, :] = values.astype(jnp.bfloat16)
            pair.append(values)
        store(slice(chunk * size, (chunk + 1) * size), *pair)
    copies[-1].wait()
    annots = jnp.concatenate(
        [
            held_annots[...].astype(jnp.float32),
            jnp.zeros((2 * part - annot_rows, annot_ref.shape[1]), jnp.float32),
        ],
        axis=0,
    )
    store(slice(rows // 2, rows // 2 + part), annots[:part], annots[part:])


def partner(group, step, groups):
    if groups & (groups - 1) == 0:
        return group ^ step
    return (group + step) % groups


def send_shares(groups, source, share, targets):
    me = lax.axis_index("hap")
    for step, target in enumerate(targets):
        group = partner(me, step, groups)
        rows = source[pl.ds(pl.multiple_of(group * share, 8), share), :]
        target[0:share, :] = rows.astype(target.dtype)


def send_tiles(groups, source, share, targets):
    me = lax.axis_index("hap")
    for step, target in enumerate(targets):
        owner = partner(me, step, groups)
        counts = source[pl.ds(pl.multiple_of(owner * share, 8), share), :]
        for k in range(source.shape[1] // LANES):
            target[k * share : (k + 1) * share, :] = counts[:, k * LANES : (k + 1) * LANES]


def from_tiles(counts, share):
    tiles = counts.shape[0] // share
    return jnp.concatenate([counts[k * share : (k + 1) * share, :] for k in range(tiles)], axis=1)


def own_kernel(groups, share, alleles_ref, label_ref, *refs):
    weighted_ref, totals_ref, *targets = refs[: 2 + groups]
    tile, folded = refs[2 + groups :]
    rows, snps = alleles_ref.shape
    half = snps // 2
    weight = jnp.where(label_ref[...] > 0, float(BASE), 1.0)
    weighted_ref[0:snps, :] = alleles_ref[...].T * weight.astype(jnp.bfloat16)
    extra = weighted_ref.shape[0] - snps
    weighted_ref[snps:, :] = jnp.broadcast_to(weight, (extra, rows)).astype(jnp.bfloat16)
    tile[...] = jnp.dot(weighted_ref[...], alleles_ref[...], preferred_element_type=jnp.float32)
    count = jnp.sum(weight, axis=1, keepdims=True)
    totals_ref[...] = jnp.concatenate(
        [tile[snps : snps + 1, :], jnp.broadcast_to(count, (1, snps)), jnp.zeros((6, snps))], axis=0
    )
    row, col = iota((half, snps), 0), iota((half, snps), 1)
    moved = (col < half) | (col - half > row)
    turned = pltpu.roll(tile[0:half, :], half, 1)
    folded[0:half, :] = to_fields(jnp.where(moved, turned, tile[half:snps, :]))
    if folded.shape[0] > half:
        folded[half:, :] = jnp.zeros((folded.shape[0] - half, snps), jnp.int32)
    if groups != len(LEFT_BLOCKS):
        send_shares(groups, folded, share, targets)
        return
    tiles = snps // LANES
    shared = [totals_ref[0:1, k * LANES : (k + 1) * LANES] for k in range(tiles)]
    shared += [totals_ref[1:2, 0:LANES], jnp.zeros((7 - tiles, LANES))]
    extras = to_fields(jnp.concatenate(shared, axis=0))
    send_tiles(groups, folded, share, targets)
    for target in targets:
        target[tiles * share :, :] = extras


LEFT_BLOCKS = ((0, 1, 2, 3), (2, 3, 6, 7), (4, 0, 1, 2), (6, 0, 4, 5))
RIGHT_BLOCKS = ((2, 3, 6, 7), (4, 5, 6, 7), (0, 1, 2, 4), (0, 4, 5, 6))


def fold_by_column(tile, flipped, folded):
    owners = len(LEFT_BLOCKS)
    snps = folded.shape[1]
    wide = snps // owners
    size = wide // 2
    shape = (size, snps)
    row, lane = iota(shape, 0), iota(shape, 1)

    def block(number):
        return tile[number * size : (number + 1) * size, :]

    diagonal = block(0)
    for number in range(1, 2 * owners):
        diagonal = jnp.where(lane >= number * size, block(number), diagonal)
    flipped[:, 0:size] = diagonal.T
    corner = diagonal
    for owner in range(owners):
        start = (2 * owner + 1) * size
        turned = jnp.concatenate(
            [flipped[start : start + size, :], jnp.zeros((size, snps - LANES), jnp.float32)], axis=1
        )
        if owner:
            turned = pltpu.roll(turned, owner * wide, 1)
        inside = lane - owner * wide
        other = (row <= inside) if owner < owners // 2 else (row >= inside)
        corner = jnp.where((inside >= 0) & (inside < size) & other, turned, corner)
    rolled = []
    for shift in range(owners):
        mixed = None
        for owner in range(owners):
            slot = (owner + shift) % owners
            left = block(LEFT_BLOCKS[owner][slot]) if slot else corner
            start = owner * wide
            mixed = left if mixed is None else jnp.where(lane >= start, left, mixed)
            mixed = jnp.where(lane >= start + size, block(RIGHT_BLOCKS[owner][slot]), mixed)
        rolled.append(pltpu.roll(mixed, shift * wide, 1) if shift else mixed)
    for owner in range(owners):
        mixed = rolled[(0 - owner) % owners]
        for slot in range(1, owners):
            mixed = jnp.where(lane >= slot * wide, rolled[(slot - owner) % owners], mixed)
        folded[owner * size : (owner + 1) * size, :] = to_fields(mixed)


def above(far):
    return odd_block() == far


def side_dot(weighted_ref, side_ref):
    rows = weighted_ref.shape[1]
    half = rows // 2

    def dot(which, columns):
        return jnp.dot(
            weighted_ref[:, which], side_ref[0:half, columns], preferred_element_type=jnp.float32
        )

    first = dot(slice(0, half), slice(0, 2 * LANES))
    second = dot(slice(half, rows), slice(LANES, 3 * LANES))
    whole = first[:, 0:LANES] + second[:, LANES:]
    return whole, first[:, LANES:] + pltpu.roll(second[:, 0:LANES], HALF_LANES, 1)


def close_kernel(weighted_ref, side_ref, whole_ref, shared_ref):
    whole_ref[...], shared_ref[...] = side_dot(weighted_ref, side_ref)


def far_kernel(
    groups, share, weighted_ref, side_ref, whole_ref, shared_ref, totals_ref, mine_ref, nearest_ref, own_sum_ref, *refs
):
    targets, (tile, folded, flipped, extras) = refs[:groups], refs[groups:]
    snps = tile.shape[1]
    own_sum_ref[...] = mine_ref[...] + nearest_ref[...]
    whole, shared = side_dot(weighted_ref, side_ref)
    left = iota(shared.shape, 1) < HALF_LANES

    @pl.when(above(True))
    def _():
        tile[:, 0:LANES] = whole
        tile[:, LANES : 2 * LANES] = jnp.where(left, shared, shared_ref[...])
        tile[:, 2 * LANES :] = whole_ref[...]

    @pl.when(jnp.logical_not(above(True)))
    def _():
        tile[:, 0:LANES] = whole_ref[...]
        tile[:, LANES : 2 * LANES] = jnp.where(left, shared_ref[...], shared)
        tile[:, 2 * LANES :] = whole

    fold_by_column(tile, flipped, folded)
    square = (snps, snps)
    apart = jnp.sum(
        jnp.where(iota(square, 0) == iota(square, 1), tile[0:snps, :], 0.0), axis=0, keepdims=True
    )
    tiles = snps // LANES
    sizes = totals_ref[1:2, :]
    by_column = jnp.concatenate([sizes, tile[snps : snps + 1, :], apart, jnp.zeros((5, snps))], axis=0)
    for owner in range(groups):
        start = owner * (snps // groups)
        columns = pltpu.roll(by_column, snps - start, 1) if owner else by_column
        extras[8 * owner : 8 * (owner + 1), :] = to_fields(columns[:, 0:LANES])
    me = lax.axis_index("hap")
    send_tiles(groups, folded, share, targets)
    for step, target in enumerate(targets):
        owner = partner(me, step, groups)
        target[tiles * share :, :] = extras[pl.ds(pl.multiple_of(owner * 8, 8), 8), :]


def near_kernel(groups, share, weighted_ref, far_ref, close_ref, totals_ref, *refs):
    own_parts, own_sum_ref = refs[:groups], refs[groups]
    targets, (near, tile, folded) = refs[groups + 1 : 2 * groups + 1], refs[2 * groups + 1 :]
    rows, snps = near.shape
    half = snps // 2
    odd = odd_block()

    def unpack(up_ref, down_ref):
        pieces = load_packed(up_ref[0 : rows // 2, :], down_ref[0 : rows // 2, :])
        for side in range(2):
            where = slice(side * (rows // 2), (side + 1) * (rows // 2))
            for number in range(3):
                near[where, number * LANES : (number + 1) * LANES] = pieces[side][number]

    @pl.when(odd)
    def _():
        unpack(far_ref, close_ref)

    @pl.when(jnp.logical_not(odd))
    def _():
        unpack(close_ref, far_ref)

    tile[...] = jnp.dot(weighted_ref[...], near[...], preferred_element_type=jnp.float32)
    row, col = iota((half, snps), 0), iota((half, snps), 1)
    moved = (col >= half) & (col - half < row)
    turned = pltpu.roll(tile[0:half, :], half, 1)
    folded[0:half, :] = to_fields(jnp.where(moved, turned, tile[half:snps, :]))
    if folded.shape[0] > half:
        folded[half:, :] = jnp.zeros((folded.shape[0] - half, snps), jnp.int32)
    square = (snps, snps)
    far = jnp.sum(
        jnp.where(iota(square, 0) == iota(square, 1), tile[0:snps, :], 0.0), axis=0, keepdims=True
    )
    extras = to_fields(
        jnp.concatenate(
            [totals_ref[0:2, :], tile[snps : snps + 1, :], far, jnp.zeros((4, snps))], axis=0
        )
    )
    send_shares(groups, folded, share, targets)
    for target in targets:
        target[share:, :] = extras
    own_sum_ref[...] = sum((part[...] for part in own_parts[1:]), own_parts[0][...])


def annots_kernel(annot_ref, far_ref, close_ref, own_ref, near_ref):
    snps = annot_ref.shape[1]
    part = far_ref.shape[0]
    wide = 2 * part
    own = annot_ref[...].astype(jnp.float32)
    own = jnp.concatenate([own, jnp.zeros((LANES - own.shape[0], snps), jnp.float32)], axis=0)
    own_ref[...] = own.T
    odd = odd_block()
    far, close = far_ref[...].astype(jnp.float32), close_ref[...].astype(jnp.float32)
    first, second = load_packed(jnp.where(odd, far, close), jnp.where(odd, close, far))
    near = jnp.concatenate(
        [
            jnp.concatenate([piece.astype(jnp.float32) for piece in first], axis=1),
            jnp.concatenate([piece.astype(jnp.float32) for piece in second], axis=1),
            jnp.zeros((LANES - wide, snps), jnp.float32),
        ],
        axis=0,
    )
    near_ref[...] = near.T


def column_stats(totals, count):
    size = jnp.maximum(count, 1.0)
    frequency = totals / size
    variance = jnp.maximum(frequency * (1.0 - frequency), VARIANCE_FLOOR)
    inverse = 1.0 / jnp.sqrt(size * variance)
    low = ((0.0 - frequency) * inverse).astype(jnp.bfloat16).astype(jnp.float32)
    high = ((1.0 - frequency) * inverse).astype(jnp.bfloat16).astype(jnp.float32)
    step = high - low
    root = 1.0 / jnp.sqrt(size)
    return step, step * totals * root, (low * count + step * totals) * root


def correlation(row, col, count):
    return row[0] * col[0] * count - row[1] * col[1] + row[2] * col[2]


def split(values):
    high = values.astype(jnp.bfloat16)
    return high, (values - high.astype(jnp.float32)).astype(jnp.bfloat16)


def dot_split(values, right, axis):
    dims = (((axis,), (0,)), ((), ()))
    return sum(
        lax.dot_general(part, right, dims, preferred_element_type=jnp.float32)
        for part in split(values)
    )


def score_kernel(groups, share, reach_ref, *refs):
    own_sum_ref, near_parts = refs[0], refs[1 : groups + 1]
    annot_ref, near_annot_ref = refs[groups + 1 : groups + 3]
    targets = refs[groups + 3 : 2 * groups + 3]
    table, annots, near_annots, scores = refs[2 * groups + 3 :]
    snps = annot_ref.shape[0]
    half = snps // 2
    out_share = snps // groups
    me = lax.axis_index("hap")
    block = lax.axis_index("snp")
    last = reach_ref.shape[0] - 1
    reach_here = reach_ref[block]
    reach_up = reach_ref[jnp.minimum(block + 1, last)]
    reach_down = reach_ref[jnp.maximum(block - 1, 0)]

    own_counts = own_sum_ref[...]
    near_sums = sum((part[...] for part in near_parts[1:]), near_parts[0][...])
    extras = from_fields(near_sums[share:, :])
    near_counts = near_sums[0:share, :]

    own_stats, near_stats, lines = [], [], []
    for pop in range(2):
        count = extras[pop][1:2, :]
        own_stats.append(column_stats(extras[pop][0:1, :], count))
        near_stats.append(column_stats(extras[pop][2:3, :], count))
        lines += [*own_stats[pop], *near_stats[pop], extras[pop][0:1, :], extras[pop][3:4, :]]
    by_row = jnp.concatenate(lines, axis=0).T
    table[0:snps, 0:16] = by_row
    if table.shape[0] > snps:
        table[snps:, 0:16] = jnp.zeros((table.shape[0] - snps, 16), jnp.float32)
    annots[0:snps, :] = annot_ref[...]
    near_annots[0:snps, :] = near_annot_ref[...]
    if annots.shape[0] > snps:
        annots[snps:, :] = jnp.zeros((annots.shape[0] - snps, LANES), jnp.float32)

    low_rows = pl.multiple_of(me * share, 8)
    high_rows = pl.multiple_of(half + me * share, 8)

    def both(ref):
        return jnp.concatenate([ref[pl.ds(low_rows, share), :], ref[pl.ds(high_rows, share), :]], axis=0)

    here = both(table)
    own_count = jnp.concatenate([pltpu.roll(own_counts, half, 1), own_counts], axis=0)
    near_count = jnp.concatenate([pltpu.roll(near_counts, half, 1), near_counts], axis=0)
    shape = (2 * share, snps)
    local, col = iota(shape, 0), iota(shape, 1)
    low = local < share
    place = jnp.where(low, local, local - share) + me * share
    row = jnp.where(low, place, place + half)
    own_fields, near_fields = from_fields(own_count), from_fields(near_count)
    own_product, near_product = 1.0, 1.0
    for pop in range(2):
        row_stats = [here[:, 8 * pop + k : 8 * pop + k + 1] for k in range(3)]
        own_product *= correlation(row_stats, own_stats[pop], own_fields[pop])
        near_product *= correlation(row_stats, near_stats[pop], near_fields[pop])
    real = place < half
    own_inside = real & ((low & (col > row)) | (~low & (col >= half) & (col < row)))
    own_inside &= jnp.abs(col - row) <= reach_here
    own_kept = jnp.where(own_inside, own_product, 0.0)
    in_upper = col < half
    near_inside = real & ((low & (col < row)) | (~low & (in_upper | (col > row))))
    distance = jnp.where(in_upper, snps + col - row, snps + row - col)
    near_here = jnp.where(near_inside & (distance <= reach_here), near_product, 0.0)
    reach_there = jnp.where(in_upper, reach_up, reach_down)
    near_there = jnp.where(near_inside & (distance <= reach_there), near_product, 0.0)

    rows_here = both(annots)
    rows_there = pltpu.roll(rows_here, HALF_LANES, 1)
    scores[0:snps, :] = dot_split(
        jnp.concatenate([own_kept, near_there], axis=0),
        jnp.concatenate([rows_here, rows_there], axis=0).astype(jnp.bfloat16),
        0,
    )
    direct = dot_split(
        jnp.concatenate([own_kept, near_here], axis=1),
        jnp.concatenate([annot_ref[...], near_annot_ref[...]], axis=0).astype(jnp.bfloat16),
        1,
    )
    scores[pl.ds(low_rows, share), :] += direct[0:share, :]
    scores[pl.ds(high_rows, share), :] += direct[share:, :]

    out_rows = pl.ds(pl.multiple_of(me * out_share, 8), out_share)
    mine = table[out_rows, :]
    self_product, far_product = 1.0, 1.0
    for pop in range(2):
        k = 8 * pop
        own_row = [mine[:, k + s : k + s + 1] for s in range(3)]
        near_row = [mine[:, k + 3 + s : k + 4 + s] for s in range(3)]
        self_product *= correlation(own_row, own_row, mine[:, k + 6 : k + 7])
        far_product *= correlation(own_row, near_row, mine[:, k + 7 : k + 8])
    mine_annots = annots[out_rows, :]
    far_reach = jnp.where(me < groups // 2, reach_up, reach_down)
    scores[out_rows, :] += (
        mine_annots * self_product
        + near_annots[out_rows, :] * jnp.where(reach_here >= snps, far_product, 0.0)
        + pltpu.roll(mine_annots, HALF_LANES, 1) * jnp.where(far_reach >= snps, far_product, 0.0)
    )
    send_shares(groups, scores, out_share, targets)


def pack_halves(values):
    half = values.shape[0] // 2
    left = iota((half, LANES), 1) < HALF_LANES
    return jnp.where(left, values[0:half], pltpu.roll(values[half:], HALF_LANES, 1))


def unpack_halves(packed):
    return jnp.concatenate([packed, pltpu.roll(packed, HALF_LANES, 1)], axis=0)


def dot_rounded(values, right, axis):
    dims = (((axis,), (0,)), ((), ()))
    return lax.dot_general(
        values.astype(jnp.bfloat16), right, dims, preferred_element_type=jnp.float32
    )


def owner_places(groups, size):
    me = lax.axis_index("hap")

    def mine(blocks, slot):
        value = blocks[0][slot]
        for group in range(1, groups):
            value = jnp.where(me == group, blocks[group][slot], value)
        return value * size

    left = [mine(LEFT_BLOCKS, slot) for slot in range(groups)]
    right = [mine(RIGHT_BLOCKS, slot) for slot in range(groups)]
    return left + left[0:1], right + [(2 * me + 1) * size]


def rows_at(ref, places, size):
    return jnp.concatenate([ref[pl.ds(pl.multiple_of(place, 8), size), :] for place in places], axis=0)


def own_score_kernel(
    groups, share, reach_ref, *refs
):
    own_parts, refs = refs[: groups - 1], refs[groups - 1 :]
    annot_ref, near_annot_ref, scores, mine_ref, rows_ref, masks_ref, columns_ref, own_rows_ref, table = refs
    snps = annot_ref.shape[0]
    half = snps // 2
    wide = snps // groups
    tiles = snps // LANES
    me = lax.axis_index("hap")
    reach_here = reach_ref[lax.axis_index("snp")]
    own_sums = sum((part[...] for part in own_parts[1:]), own_parts[0][...])
    own_counts = from_tiles(own_sums[0 : tiles * share, :], share)
    extras = from_fields(own_sums[tiles * share :, :])

    own_stats, lines = [], []
    for pop in range(2):
        count = jnp.concatenate([extras[pop][tiles : tiles + 1, :]] * tiles, axis=1)
        totals = jnp.concatenate([extras[pop][k : k + 1, :] for k in range(tiles)], axis=1)
        own_stats.append(column_stats(totals, count))
        lines += [*own_stats[pop], totals]
    table[:, 0:8] = jnp.concatenate(lines, axis=0).T

    low_rows = pl.multiple_of(me * share, 8)
    high_rows = pl.multiple_of(half + me * share, 8)

    def both(ref):
        return jnp.concatenate([ref[pl.ds(low_rows, share), :], ref[pl.ds(high_rows, share), :]], axis=0)

    here = both(table)
    own_fields = from_fields(
        jnp.concatenate([pltpu.roll(own_counts, half, 1), own_counts], axis=0)
    )
    shape = (2 * share, snps)
    local, col = iota(shape, 0), iota(shape, 1)
    low = local < share
    row = jnp.where(low, local, local + half - share) + me * share
    product = 1.0
    for pop in range(2):
        row_stats = [here[:, 4 * pop + k : 4 * pop + k + 1] for k in range(3)]
        product *= correlation(row_stats, own_stats[pop], own_fields[pop])
    inside = (low & (col > row)) | (~low & (col >= half) & (col < row))
    own_kept = jnp.where(inside & (jnp.abs(col - row) <= reach_here), product, 0.0)
    rows_here = both(annot_ref).astype(jnp.bfloat16)
    scores[...] = dot_rounded(own_kept, rows_here, 0)
    direct = dot_rounded(own_kept, annot_ref[...].astype(jnp.bfloat16), 1)
    scores[pl.ds(low_rows, share), :] += direct[0:share, :]
    scores[pl.ds(high_rows, share), :] += direct[share:, :]

    slice_rows = pl.ds(pl.multiple_of(me * wide, 8), wide)
    mine = table[slice_rows, :]
    mine_ref[...] = mine
    product = 1.0
    for pop in range(2):
        own_row = [mine[:, 4 * pop + k : 4 * pop + k + 1] for k in range(4)]
        product *= correlation(own_row, own_row, own_row[3])
    scores[slice_rows, :] += annot_ref[slice_rows, :] * product

    size = wide // 2
    left_places, right_places = owner_places(groups, size)
    left_table, right_table = rows_at(table, left_places, size), rows_at(table, right_places, size)
    local, lane = iota((size, LANES), 0), iota((size, LANES), 1)
    own_row = jnp.concatenate(
        [local + jnp.where(lane < size, a, b) for a, b in zip(left_places, right_places)], axis=0
    )
    shape = own_row.shape
    lane = iota(shape, 1)
    is_left = lane < size
    for pop in range(2):
        for k in range(3):
            column = slice(4 * pop + k, 4 * pop + k + 1)
            rows_ref[3 * pop + k] = jnp.where(is_left, left_table[:, column], right_table[:, column])
    upper = me < groups // 2
    block = lax.axis_index("snp")
    last = reach_ref.shape[0] - 1
    reach_there = jnp.where(
        upper, reach_ref[jnp.minimum(block + 1, last)], reach_ref[jnp.maximum(block - 1, 0)]
    )
    apart = jnp.abs(own_row - (lane + me * wide))
    ahead = (own_row - (lane + me * wide)) * jnp.where(upper, 1, -1) > 0
    real = ahead & (lane < wide) & ((lane >= size) | (iota(shape, 0) < groups * size))
    for number, limit in enumerate((reach_here, reach_there)):
        masks_ref[number] = jnp.where(real & (snps - apart <= limit), 1.0, 0.0)
    theirs = near_annot_ref[slice_rows, :]
    columns = [theirs[0:size], pltpu.roll(theirs[size:], HALF_LANES, 1), jnp.zeros((LANES - wide, LANES))]
    columns_ref[...] = jnp.concatenate(columns, axis=0).astype(jnp.bfloat16)
    own_rows = rows_at(annot_ref, left_places, size) + pltpu.roll(
        rows_at(annot_ref, right_places, size), HALF_LANES, 1
    )
    own_rows_ref[...] = own_rows.astype(jnp.bfloat16)


def near_score_kernel(groups, share, reach_ref, *refs):
    near_parts, refs = refs[:groups], refs[groups:]
    own_ref, mine_ref, rows_ref, masks_ref, columns_ref, own_rows_ref, annot_ref, near_annot_ref = refs[:8]
    keep_ref, send_ref, near_out_ref, flipped, scores = refs[8:]
    snps = annot_ref.shape[0]
    wide = snps // groups
    size = wide // 2
    tiles = snps // LANES
    me = lax.axis_index("hap")
    block = lax.axis_index("snp")
    last = reach_ref.shape[0] - 1
    reach_here = reach_ref[block]
    reach_there = jnp.where(
        me < groups // 2, reach_ref[jnp.minimum(block + 1, last)], reach_ref[jnp.maximum(block - 1, 0)]
    )

    scores[...] = own_ref[...]
    near_sums = sum((part[...] for part in near_parts[1:]), near_parts[0][...])
    near_counts = from_tiles(near_sums[0 : tiles * share, :], share)
    extras = from_fields(near_sums[tiles * share :, :])
    near_stats, near_lines = [], []
    for pop in range(2):
        near_stats.append(column_stats(extras[pop][1:2, :], extras[pop][0:1, :]))
        near_lines += [*near_stats[pop], extras[pop][2:3, :]]
    near_table = jnp.concatenate(near_lines, axis=0).T[0:wide, :]

    slots = [near_counts[:, 0:LANES]]
    for slot in range(1, groups):
        slots.append(pltpu.roll(near_counts, snps - slot * wide, 1)[:, 0:LANES])
    flipped[:, 0:size] = slots[0].T
    slots.append(pltpu.roll(flipped[0:size, :], size, 1))
    near_fields = from_fields(jnp.concatenate(slots, axis=0))
    product = 1.0
    for pop in range(2):
        row_stats = [rows_ref[3 * pop + k] for k in range(3)]
        product *= correlation(row_stats, near_stats[pop], near_fields[pop])
    near_here = jnp.where(masks_ref[0] > 0.0, product, 0.0)
    near_there = jnp.where(masks_ref[1] > 0.0, product, 0.0)
    slice_rows = pl.ds(pl.multiple_of(me * wide, 8), wide)
    direct = dot_rounded(near_here, columns_ref[...], 1)
    turned = pltpu.roll(direct, HALF_LANES, 1)
    for values, places in zip((direct, turned), owner_places(groups, size)):
        for slot, place in enumerate(places):
            scores[pl.ds(pl.multiple_of(place, 8), size), :] += values[slot * size : (slot + 1) * size, :]
    near_scores = dot_rounded(near_there, own_rows_ref[...], 0)
    near_scores = jnp.where(
        iota((size, LANES), 1) < HALF_LANES, near_scores[0:size], near_scores[size:wide]
    )

    mine_table = mine_ref[...]
    far_product = 1.0
    for pop in range(2):
        own_row = [mine_table[:, 4 * pop + k : 4 * pop + k + 1] for k in range(3)]
        near_row = [near_table[:, 4 * pop + k : 4 * pop + k + 1] for k in range(4)]
        far_product *= correlation(own_row, near_row, near_row[3])
    scores[slice_rows, :] += near_annot_ref[slice_rows, :] * jnp.where(reach_here >= snps, far_product, 0.0)
    far_scores = annot_ref[slice_rows, :] * jnp.where(reach_there >= snps, far_product, 0.0)
    near_out_ref[...] = near_scores + pack_halves(far_scores)

    def packed(step):
        group = partner(me, step, groups)
        return pack_halves(scores[pl.ds(pl.multiple_of(group * wide, 8), wide), :])

    for ref, steps in ((keep_ref, (0, 1)), (send_ref, (2, 3))):
        for number, step in enumerate(steps):
            ref[number * size : (number + 1) * size, :] = packed(step).astype(ref.dtype)


def middle_kernel(keep_ref, part_ref, mine_ref, send_ref):
    total = keep_ref[...] + part_ref[...].astype(jnp.float32)
    half = mine_ref.shape[0]
    mine_ref[...] = total[0:half]
    send_ref[...] = total[half:].astype(send_ref.dtype)


def column_finish_kernel(mine_ref, part_ref, there_ref, out_ref):
    packed = mine_ref[...] + part_ref[...].astype(jnp.float32) + there_ref[...]
    out_ref[...] = unpack_halves(packed).T[0 : out_ref.shape[0], :]


def sum_kernel(*refs):
    *parts, own_ref, there_ref = refs
    total = sum((part[...].astype(jnp.float32) for part in parts[1:]), parts[0][...])
    own_ref[...] = total
    half = there_ref.shape[0]
    left = iota((half, LANES), 1) < HALF_LANES
    second = total[half:]
    if second.shape[0] < half:
        second = jnp.concatenate([second, jnp.zeros((half - second.shape[0], LANES))], axis=0)
    there_ref[...] = jnp.where(left, pltpu.roll(total[0:half], HALF_LANES, 1), second)


def finish_kernel(own_ref, there_ref, out_ref):
    annots, rows = out_ref.shape
    there = there_ref[...]
    there = jnp.concatenate([there, pltpu.roll(there, HALF_LANES, 1)], axis=0)
    out_ref[...] = (own_ref[...] + there[0:rows]).T[0:annots, :]


def around(value, groups, step):
    return lax.ppermute(
        value, "hap", [(source, partner(source, step, groups)) for source in range(groups)]
    )


def swapped(value, first):
    pairs = []
    for block in range(first, lax.axis_size("snp") - 1, 2):
        pairs += [(block, block + 1), (block + 1, block)]
    return lax.ppermute(value, "snp", pairs)


def per_device(haplotypes, labels, annotations, reach):
    rows, snps = haplotypes.shape
    half = snps // 2
    groups = lax.axis_size("hap")
    blocks = lax.axis_size("snp")
    share = round_up(-(-half // groups), 16)
    folded_rows = share * groups
    out_share = snps // groups
    padded = half + folded_rows
    annot_part = 32
    bf16, f32, i32 = jnp.bfloat16, jnp.float32, jnp.int32
    shape = jax.ShapeDtypeStruct

    packed = shape((rows // 2 + annot_part, snps), bf16)
    haplotypes = pltpu.with_memory_space_constraint(haplotypes, pltpu.HBM)
    annots_in = pltpu.with_memory_space_constraint(annotations, pltpu.HBM)
    alleles, far, close = call(
        prepare_kernel,
        [shape((rows, snps), bf16), packed, packed],
        [HBM, HBM],
        [
            pltpu.VMEM((rows, snps), i32),
            pltpu.VMEM(annotations.shape, i32),
            pltpu.SemaphoreType.DMA((2 * CHUNKS + 1,)),
        ],
        moved=rows * snps * 8,
    )(haplotypes, annots_in)
    from_far = swapped(far, 1)
    from_close = swapped(close, 0)

    by_column = groups == len(LEFT_BLOCKS)
    compact = shape((share * (snps // LANES) + 8, LANES), i32)
    own_share_counts = compact if by_column else shape((share, snps), i32)
    tile = pltpu.VMEM((snps + 16, snps), f32)
    folded = pltpu.VMEM((folded_rows, snps), i32)
    weighted, totals, *own_parts = call(
        functools.partial(own_kernel, groups, share),
        [shape((snps + 16, rows), bf16), shape((8, snps), f32)] + [own_share_counts] * groups,
        [VMEM, VMEM],
        [tile, folded],
        flops=2 * rows * snps * snps,
        moved=rows * snps * 4,
    )(alleles, labels.reshape(1, rows))
    own_parts = [own_parts[0]] + [around(own_parts[k], groups, k) for k in range(groups - 1, 0, -1)]

    near_shapes = [own_share_counts] + [compact if by_column else shape((share + 8, snps), i32)] * groups
    if by_column:
        piece = shape((snps + 16, LANES), f32)
        work = dict(flops=4 * rows * snps * LANES, moved=rows * snps * 4)
        close_counts = call(close_kernel, [piece, piece], [VMEM] * 2, **work)(weighted, from_close)
        own_sum, *near_parts = call(
            functools.partial(far_kernel, groups, share),
            near_shapes,
            [VMEM] * 7,
            [
                tile,
                folded,
                pltpu.VMEM((snps, LANES), f32),
                pltpu.VMEM((8 * groups, LANES), i32),
            ],
            **work,
        )(weighted, from_far, *close_counts, totals, own_parts[0], own_parts[-1])
    else:
        own_sum, *near_parts = call(
            functools.partial(near_kernel, groups, share),
            near_shapes,
            [VMEM] * (4 + groups),
            [pltpu.VMEM((rows, snps), bf16), tile, folded],
            flops=2 * rows * snps * snps,
            moved=rows * snps * 4,
        )(weighted, from_far, from_close, totals, *own_parts)
    order = (2, 3, 1) if by_column else range(groups - 1, 0, -1)
    near_parts = [near_parts[0]] + [around(near_parts[k], groups, k) for k in order]

    by_snp = shape((snps, LANES), f32)
    own_annots, near_annots = call(annots_kernel, [by_snp, by_snp], [VMEM] * 3, moved=1 << 20)(
        annotations, from_far[rows // 2 :], from_close[rows // 2 :]
    )
    pairs = []
    for block in range(blocks):
        for group in range(groups):
            target = block + 1 if group < groups // 2 else block - 1
            if 0 <= target < blocks:
                pairs.append((block * groups + group, target * groups + group))

    def to_neighbour(value):
        return lax.ppermute(value, ("snp", "hap"), pairs)

    result = shape((annotations.shape[0], out_share), f32)
    half_share = round_up(-(-out_share // 2), 8)
    own_share = shape((out_share, LANES), f32)
    packed_share = shape((half_share, LANES), f32)
    if by_column:
        pair_rows = (groups + 1) * (out_share // 2)
        prepared = call(
            functools.partial(own_score_kernel, groups, share),
            [
                by_snp,
                shape((out_share, LANES), f32),
                shape((6, pair_rows, LANES), f32),
                shape((2, pair_rows, LANES), f32),
                shape((LANES, LANES), bf16),
                shape((pair_rows, LANES), bf16),
            ],
            [SMEM] + [VMEM] * (groups + 1),
            [pltpu.VMEM((snps, LANES), f32)],
            flops=1 << 25,
            moved=1 << 20,
        )(reach, own_sum, *own_parts[1:-1], own_annots, near_annots)
        both = (2 * half_share, LANES)
        keep, send, near_scores = call(
            functools.partial(near_score_kernel, groups, share),
            [shape(both, f32), shape(both, bf16), packed_share],
            [SMEM] + [VMEM] * (groups + 8),
            [pltpu.VMEM((LANES, LANES), i32), pltpu.VMEM((snps, LANES), f32)],
            flops=1 << 26,
            moved=1 << 21,
        )(reach, *near_parts, *prepared, own_annots, near_annots)
        part = around(send, groups, 2)
        there = to_neighbour(near_scores)
        mine, send = call(
            middle_kernel, [packed_share, shape((half_share, LANES), bf16)], [VMEM] * 2
        )(keep, part)
        part = around(send, groups, 1)
        return call(column_finish_kernel, result, [VMEM] * 3)(mine, part, there)

    tall = pltpu.VMEM((padded, LANES), f32)
    scores = call(
        functools.partial(score_kernel, groups, share),
        [own_share] + [shape((out_share, LANES), bf16)] * (groups - 1),
        [SMEM] + [VMEM] * (groups + 3),
        [tall, tall, tall, tall],
        flops=1 << 26,
        moved=1 << 21,
    )(reach, own_sum, *near_parts, own_annots, near_annots)
    scores = [scores[0]] + [around(scores[k], groups, k) for k in range(groups - 1, 0, -1)]
    own_scores, near_scores = call(sum_kernel, [own_share, packed_share], [VMEM] * groups)(*scores)
    return call(finish_kernel, result, [VMEM] * 2)(own_scores, to_neighbour(near_scores))


def solution(mesh):
    in_specs = (
        P("hap", ("parts", "snp")),
        P(("parts", "hap")),
        P(None, ("parts", "snp")),
        P("parts"),
    )
    out_specs = P(None, ("parts", "snp", "hap"))
    return jax.shard_map(
        per_device, mesh=mesh, in_specs=in_specs, out_specs=out_specs, check_vma=False
    )
```

```python
import functools

import jax
import jax.numpy as jnp
from jax import lax
from jax.experimental import pallas as pl
from jax.experimental.pallas import tpu as pltpu
from jax.sharding import PartitionSpec as P

VARIANCE_FLOOR = 0.01
BASE_BITS = 12
BASE = 1 << BASE_BITS
FIELD_BITS = 16
LANES = 128
HALF_LANES = LANES // 2
CHUNKS = 4
VMEM = pl.BlockSpec(memory_space=pltpu.VMEM)
SMEM = pl.BlockSpec(memory_space=pltpu.SMEM)
HBM = pl.BlockSpec(memory_space=pltpu.HBM)
VMEM_LIMIT = 24 * 1024 * 1024


def iota(shape, axis):
    return lax.broadcasted_iota(jnp.int32, shape, axis)


def round_up(value, step):
    return -(-value // step) * step


def to_fields(values):
    whole = values.astype(jnp.int32)
    return whole + (whole >> BASE_BITS) * ((1 << FIELD_BITS) - BASE)


def from_fields(packed):
    first = packed & ((1 << FIELD_BITS) - 1)
    second = lax.shift_right_logical(packed, FIELD_BITS)
    return first.astype(jnp.float32), second.astype(jnp.float32)


def call(kernel, out_shape, in_specs, scratch_shapes=(), flops=0, moved=0):
    several = isinstance(out_shape, (list, tuple))
    return pl.pallas_call(
        kernel,
        out_shape=out_shape,
        in_specs=in_specs,
        out_specs=[VMEM] * len(out_shape) if several else VMEM,
        scratch_shapes=list(scratch_shapes),
        compiler_params=pltpu.CompilerParams(vmem_limit_bytes=VMEM_LIMIT),
        cost_estimate=pl.CostEstimate(flops=flops, bytes_accessed=moved, transcendentals=0),
    )


def odd_block():
    return lax.rem(lax.axis_index("snp"), 2) == 1


def store_packed(up_ref, down_ref, where, first, second):
    left = iota((first.shape[0], LANES), 1) < HALF_LANES
    middle = first[:, LANES : 2 * LANES]
    turned = pltpu.roll(second[:, LANES : 2 * LANES], HALF_LANES, 1)
    for ref, side, mixed in (
        (up_ref, slice(0, LANES), jnp.where(left, middle, turned)),
        (down_ref, slice(2 * LANES, 3 * LANES), jnp.where(left, turned, middle)),
    ):
        ref[where, 0:LANES] = first[:, side].astype(jnp.bfloat16)
        ref[where, LANES : 2 * LANES] = mixed.astype(jnp.bfloat16)
        ref[where, 2 * LANES : 3 * LANES] = second[:, side].astype(jnp.bfloat16)


def load_packed(up, down):
    left = iota((up.shape[0], LANES), 1) < HALF_LANES
    up_mixed, down_mixed = up[:, LANES : 2 * LANES], down[:, LANES : 2 * LANES]
    first = jnp.where(left, up_mixed, down_mixed)
    second = jnp.where(left, down_mixed, up_mixed)
    second = pltpu.roll(second.astype(jnp.float32), HALF_LANES, 1).astype(second.dtype)
    return (
        (up[:, :LANES], first, down[:, :LANES]),
        (up[:, 2 * LANES :], second, down[:, 2 * LANES :]),
    )


def prepare_kernel(hap_ref, annot_ref, alleles_ref, far_ref, close_ref, held, held_annots, sems):
    rows = hap_ref.shape[0]
    annot_rows = annot_ref.shape[0]
    size = rows // (2 * CHUNKS)
    starts = [side * (rows // 2) + chunk * size for chunk in range(CHUNKS) for side in range(2)]
    copies = [
        pltpu.make_async_copy(
            hap_ref.at[pl.ds(start, size)], held.at[pl.ds(start, size)], sems.at[number]
        )
        for number, start in enumerate(starts)
    ]
    copies.append(pltpu.make_async_copy(annot_ref, held_annots, sems.at[2 * CHUNKS]))
    for copy in copies:
        copy.start()
    part = far_ref.shape[0] - rows // 2
    odd = odd_block()

    def store(where, first, second):
        @pl.when(odd)
        def _():
            store_packed(close_ref, far_ref, where, first, second)

        @pl.when(jnp.logical_not(odd))
        def _():
            store_packed(far_ref, close_ref, where, first, second)

    for chunk in range(CHUNKS):
        pair = []
        for side in range(2):
            number = 2 * chunk + side
            copies[number].wait()
            where = slice(starts[number], starts[number] + size)
            values = held[where, :].astype(jnp.float32)
            alleles_ref[where, :] = values.astype(jnp.bfloat16)
            pair.append(values)
        store(slice(chunk * size, (chunk + 1) * size), *pair)
    copies[-1].wait()
    annots = jnp.concatenate(
        [
            held_annots[...].astype(jnp.float32),
            jnp.zeros((2 * part - annot_rows, annot_ref.shape[1]), jnp.float32),
        ],
        axis=0,
    )
    store(slice(rows // 2, rows // 2 + part), annots[:part], annots[part:])


def partner(group, step, groups):
    if groups & (groups - 1) == 0:
        return group ^ step
    return (group + step) % groups


def send_shares(groups, source, share, targets):
    me = lax.axis_index("hap")
    for step, target in enumerate(targets):
        group = partner(me, step, groups)
        rows = source[pl.ds(pl.multiple_of(group * share, 8), share), :]
        target[0:share, :] = rows.astype(target.dtype)


def send_tiles(groups, source, share, targets):
    me = lax.axis_index("hap")
    for step, target in enumerate(targets):
        owner = partner(me, step, groups)
        counts = source[pl.ds(pl.multiple_of(owner * share, 8), share), :]
        for k in range(source.shape[1] // LANES):
            target[k * share : (k + 1) * share, :] = counts[:, k * LANES : (k + 1) * LANES]


def from_tiles(counts, share):
    tiles = counts.shape[0] // share
    return jnp.concatenate([counts[k * share : (k + 1) * share, :] for k in range(tiles)], axis=1)


def own_kernel(groups, share, alleles_ref, label_ref, *refs):
    weighted_ref, totals_ref, *targets = refs[: 2 + groups]
    tile, folded = refs[2 + groups :]
    rows, snps = alleles_ref.shape
    half = snps // 2
    weight = jnp.where(label_ref[...] > 0, float(BASE), 1.0)
    weighted_ref[0:snps, :] = alleles_ref[...].T * weight.astype(jnp.bfloat16)
    extra = weighted_ref.shape[0] - snps
    weighted_ref[snps:, :] = jnp.broadcast_to(weight, (extra, rows)).astype(jnp.bfloat16)
    tile[...] = jnp.dot(weighted_ref[...], alleles_ref[...], preferred_element_type=jnp.float32)
    count = jnp.sum(weight, axis=1, keepdims=True)
    totals_ref[...] = jnp.concatenate(
        [tile[snps : snps + 1, :], jnp.broadcast_to(count, (1, snps)), jnp.zeros((6, snps))], axis=0
    )
    row, col = iota((half, snps), 0), iota((half, snps), 1)
    moved = (col < half) | (col - half > row)
    turned = pltpu.roll(tile[0:half, :], half, 1)
    folded[0:half, :] = to_fields(jnp.where(moved, turned, tile[half:snps, :]))
    if folded.shape[0] > half:
        folded[half:, :] = jnp.zeros((folded.shape[0] - half, snps), jnp.int32)
    if groups != len(LEFT_BLOCKS):
        send_shares(groups, folded, share, targets)
        return
    tiles = snps // LANES
    shared = [totals_ref[0:1, k * LANES : (k + 1) * LANES] for k in range(tiles)]
    shared += [totals_ref[1:2, 0:LANES], jnp.zeros((7 - tiles, LANES))]
    extras = to_fields(jnp.concatenate(shared, axis=0))
    send_tiles(groups, folded, share, targets)
    for target in targets:
        target[tiles * share :, :] = extras


LEFT_BLOCKS = ((0, 1, 2, 3), (2, 3, 6, 7), (4, 0, 1, 2), (6, 0, 4, 5))
RIGHT_BLOCKS = ((2, 3, 6, 7), (4, 5, 6, 7), (0, 1, 2, 4), (0, 4, 5, 6))


def fold_by_column(tile, flipped, folded):
    owners = len(LEFT_BLOCKS)
    snps = folded.shape[1]
    wide = snps // owners
    size = wide // 2
    shape = (size, snps)
    row, lane = iota(shape, 0), iota(shape, 1)

    def block(number):
        return tile[number * size : (number + 1) * size, :]

    diagonal = block(0)
    for number in range(1, 2 * owners):
        diagonal = jnp.where(lane >= number * size, block(number), diagonal)
    flipped[:, 0:size] = diagonal.T
    corner = diagonal
    for owner in range(owners):
        start = (2 * owner + 1) * size
        turned = jnp.concatenate(
            [flipped[start : start + size, :], jnp.zeros((size, snps - LANES), jnp.float32)], axis=1
        )
        if owner:
            turned = pltpu.roll(turned, owner * wide, 1)
        inside = lane - owner * wide
        other = (row <= inside) if owner < owners // 2 else (row >= inside)
        corner = jnp.where((inside >= 0) & (inside < size) & other, turned, corner)
    rolled = []
    for shift in range(owners):
        mixed = None
        for owner in range(owners):
            slot = (owner + shift) % owners
            left = block(LEFT_BLOCKS[owner][slot]) if slot else corner
            start = owner * wide
            mixed = left if mixed is None else jnp.where(lane >= start, left, mixed)
            mixed = jnp.where(lane >= start + size, block(RIGHT_BLOCKS[owner][slot]), mixed)
        rolled.append(pltpu.roll(mixed, shift * wide, 1) if shift else mixed)
    for owner in range(owners):
        mixed = rolled[(0 - owner) % owners]
        for slot in range(1, owners):
            mixed = jnp.where(lane >= slot * wide, rolled[(slot - owner) % owners], mixed)
        folded[owner * size : (owner + 1) * size, :] = to_fields(mixed)


def above(far):
    return odd_block() == far


def side_dot(weighted_ref, side_ref):
    rows = weighted_ref.shape[1]
    half = rows // 2

    def dot(which, columns):
        return jnp.dot(
            weighted_ref[:, which], side_ref[0:half, columns], preferred_element_type=jnp.float32
        )

    first = dot(slice(0, half), slice(0, 2 * LANES))
    second = dot(slice(half, rows), slice(LANES, 3 * LANES))
    whole = first[:, 0:LANES] + second[:, LANES:]
    return whole, first[:, LANES:] + pltpu.roll(second[:, 0:LANES], HALF_LANES, 1)


def close_kernel(weighted_ref, side_ref, whole_ref, shared_ref):
    whole_ref[...], shared_ref[...] = side_dot(weighted_ref, side_ref)


def far_kernel(
    groups, share, weighted_ref, side_ref, whole_ref, shared_ref, totals_ref, mine_ref, nearest_ref, own_sum_ref, *refs
):
    targets, (tile, folded, flipped, extras) = refs[:groups], refs[groups:]
    snps = tile.shape[1]
    own_sum_ref[...] = mine_ref[...] + nearest_ref[...]
    whole, shared = side_dot(weighted_ref, side_ref)
    left = iota(shared.shape, 1) < HALF_LANES

    @pl.when(above(True))
    def _():
        tile[:, 0:LANES] = whole
        tile[:, LANES : 2 * LANES] = jnp.where(left, shared, shared_ref[...])
        tile[:, 2 * LANES :] = whole_ref[...]

    @pl.when(jnp.logical_not(above(True)))
    def _():
        tile[:, 0:LANES] = whole_ref[...]
        tile[:, LANES : 2 * LANES] = jnp.where(left, shared_ref[...], shared)
        tile[:, 2 * LANES :] = whole

    fold_by_column(tile, flipped, folded)
    square = (snps, snps)
    apart = jnp.sum(
        jnp.where(iota(square, 0) == iota(square, 1), tile[0:snps, :], 0.0), axis=0, keepdims=True
    )
    tiles = snps // LANES
    sizes = totals_ref[1:2, :]
    by_column = jnp.concatenate([sizes, tile[snps : snps + 1, :], apart, jnp.zeros((5, snps))], axis=0)
    for owner in range(groups):
        start = owner * (snps // groups)
        columns = pltpu.roll(by_column, snps - start, 1) if owner else by_column
        extras[8 * owner : 8 * (owner + 1), :] = to_fields(columns[:, 0:LANES])
    me = lax.axis_index("hap")
    send_tiles(groups, folded, share, targets)
    for step, target in enumerate(targets):
        owner = partner(me, step, groups)
        target[tiles * share :, :] = extras[pl.ds(pl.multiple_of(owner * 8, 8), 8), :]


def near_kernel(groups, share, weighted_ref, far_ref, close_ref, totals_ref, *refs):
    own_parts, own_sum_ref = refs[:groups], refs[groups]
    targets, (near, tile, folded) = refs[groups + 1 : 2 * groups + 1], refs[2 * groups + 1 :]
    rows, snps = near.shape
    half = snps // 2
    odd = odd_block()

    def unpack(up_ref, down_ref):
        pieces = load_packed(up_ref[0 : rows // 2, :], down_ref[0 : rows // 2, :])
        for side in range(2):
            where = slice(side * (rows // 2), (side + 1) * (rows // 2))
            for number in range(3):
                near[where, number * LANES : (number + 1) * LANES] = pieces[side][number]

    @pl.when(odd)
    def _():
        unpack(far_ref, close_ref)

    @pl.when(jnp.logical_not(odd))
    def _():
        unpack(close_ref, far_ref)

    tile[...] = jnp.dot(weighted_ref[...], near[...], preferred_element_type=jnp.float32)
    row, col = iota((half, snps), 0), iota((half, snps), 1)
    moved = (col >= half) & (col - half < row)
    turned = pltpu.roll(tile[0:half, :], half, 1)
    folded[0:half, :] = to_fields(jnp.where(moved, turned, tile[half:snps, :]))
    if folded.shape[0] > half:
        folded[half:, :] = jnp.zeros((folded.shape[0] - half, snps), jnp.int32)
    square = (snps, snps)
    far = jnp.sum(
        jnp.where(iota(square, 0) == iota(square, 1), tile[0:snps, :], 0.0), axis=0, keepdims=True
    )
    extras = to_fields(
        jnp.concatenate(
            [totals_ref[0:2, :], tile[snps : snps + 1, :], far, jnp.zeros((4, snps))], axis=0
        )
    )
    send_shares(groups, folded, share, targets)
    for target in targets:
        target[share:, :] = extras
    own_sum_ref[...] = sum((part[...] for part in own_parts[1:]), own_parts[0][...])


def annots_kernel(annot_ref, far_ref, close_ref, own_ref, near_ref):
    snps = annot_ref.shape[1]
    part = far_ref.shape[0]
    wide = 2 * part
    own = annot_ref[...].astype(jnp.float32)
    own = jnp.concatenate([own, jnp.zeros((LANES - own.shape[0], snps), jnp.float32)], axis=0)
    own_ref[...] = own.T
    odd = odd_block()
    far, close = far_ref[...].astype(jnp.float32), close_ref[...].astype(jnp.float32)
    first, second = load_packed(jnp.where(odd, far, close), jnp.where(odd, close, far))
    near = jnp.concatenate(
        [
            jnp.concatenate([piece.astype(jnp.float32) for piece in first], axis=1),
            jnp.concatenate([piece.astype(jnp.float32) for piece in second], axis=1),
            jnp.zeros((LANES - wide, snps), jnp.float32),
        ],
        axis=0,
    )
    near_ref[...] = near.T


def column_stats(totals, count):
    size = jnp.maximum(count, 1.0)
    frequency = totals / size
    variance = jnp.maximum(frequency * (1.0 - frequency), VARIANCE_FLOOR)
    inverse = 1.0 / jnp.sqrt(size * variance)
    low = ((0.0 - frequency) * inverse).astype(jnp.bfloat16).astype(jnp.float32)
    high = ((1.0 - frequency) * inverse).astype(jnp.bfloat16).astype(jnp.float32)
    step = high - low
    root = 1.0 / jnp.sqrt(size)
    return step, step * totals * root, (low * count + step * totals) * root


def correlation(row, col, count):
    return row[0] * col[0] * count - row[1] * col[1] + row[2] * col[2]


def split(values):
    high = values.astype(jnp.bfloat16)
    return high, (values - high.astype(jnp.float32)).astype(jnp.bfloat16)


def dot_split(values, right, axis):
    dims = (((axis,), (0,)), ((), ()))
    return sum(
        lax.dot_general(part, right, dims, preferred_element_type=jnp.float32)
        for part in split(values)
    )


def score_kernel(groups, share, reach_ref, *refs):
    own_sum_ref, near_parts = refs[0], refs[1 : groups + 1]
    annot_ref, near_annot_ref = refs[groups + 1 : groups + 3]
    targets = refs[groups + 3 : 2 * groups + 3]
    table, annots, near_annots, scores = refs[2 * groups + 3 :]
    snps = annot_ref.shape[0]
    half = snps // 2
    out_share = snps // groups
    me = lax.axis_index("hap")
    block = lax.axis_index("snp")
    last = reach_ref.shape[0] - 1
    reach_here = reach_ref[block]
    reach_up = reach_ref[jnp.minimum(block + 1, last)]
    reach_down = reach_ref[jnp.maximum(block - 1, 0)]

    own_counts = own_sum_ref[...]
    near_sums = sum((part[...] for part in near_parts[1:]), near_parts[0][...])
    extras = from_fields(near_sums[share:, :])
    near_counts = near_sums[0:share, :]

    own_stats, near_stats, lines = [], [], []
    for pop in range(2):
        count = extras[pop][1:2, :]
        own_stats.append(column_stats(extras[pop][0:1, :], count))
        near_stats.append(column_stats(extras[pop][2:3, :], count))
        lines += [*own_stats[pop], *near_stats[pop], extras[pop][0:1, :], extras[pop][3:4, :]]
    by_row = jnp.concatenate(lines, axis=0).T
    table[0:snps, 0:16] = by_row
    if table.shape[0] > snps:
        table[snps:, 0:16] = jnp.zeros((table.shape[0] - snps, 16), jnp.float32)
    annots[0:snps, :] = annot_ref[...]
    near_annots[0:snps, :] = near_annot_ref[...]
    if annots.shape[0] > snps:
        annots[snps:, :] = jnp.zeros((annots.shape[0] - snps, LANES), jnp.float32)

    low_rows = pl.multiple_of(me * share, 8)
    high_rows = pl.multiple_of(half + me * share, 8)

    def both(ref):
        return jnp.concatenate([ref[pl.ds(low_rows, share), :], ref[pl.ds(high_rows, share), :]], axis=0)

    here = both(table)
    own_count = jnp.concatenate([pltpu.roll(own_counts, half, 1), own_counts], axis=0)
    near_count = jnp.concatenate([pltpu.roll(near_counts, half, 1), near_counts], axis=0)
    shape = (2 * share, snps)
    local, col = iota(shape, 0), iota(shape, 1)
    low = local < share
    place = jnp.where(low, local, local - share) + me * share
    row = jnp.where(low, place, place + half)
    own_fields, near_fields = from_fields(own_count), from_fields(near_count)
    own_product, near_product = 1.0, 1.0
    for pop in range(2):
        row_stats = [here[:, 8 * pop + k : 8 * pop + k + 1] for k in range(3)]
        own_product *= correlation(row_stats, own_stats[pop], own_fields[pop])
        near_product *= correlation(row_stats, near_stats[pop], near_fields[pop])
    real = place < half
    own_inside = real & ((low & (col > row)) | (~low & (col >= half) & (col < row)))
    own_inside &= jnp.abs(col - row) <= reach_here
    own_kept = jnp.where(own_inside, own_product, 0.0)
    in_upper = col < half
    near_inside = real & ((low & (col < row)) | (~low & (in_upper | (col > row))))
    distance = jnp.where(in_upper, snps + col - row, snps + row - col)
    near_here = jnp.where(near_inside & (distance <= reach_here), near_product, 0.0)
    reach_there = jnp.where(in_upper, reach_up, reach_down)
    near_there = jnp.where(near_inside & (distance <= reach_there), near_product, 0.0)

    rows_here = both(annots)
    rows_there = pltpu.roll(rows_here, HALF_LANES, 1)
    scores[0:snps, :] = dot_split(
        jnp.concatenate([own_kept, near_there], axis=0),
        jnp.concatenate([rows_here, rows_there], axis=0).astype(jnp.bfloat16),
        0,
    )
    direct = dot_split(
        jnp.concatenate([own_kept, near_here], axis=1),
        jnp.concatenate([annot_ref[...], near_annot_ref[...]], axis=0).astype(jnp.bfloat16),
        1,
    )
    scores[pl.ds(low_rows, share), :] += direct[0:share, :]
    scores[pl.ds(high_rows, share), :] += direct[share:, :]

    out_rows = pl.ds(pl.multiple_of(me * out_share, 8), out_share)
    mine = table[out_rows, :]
    self_product, far_product = 1.0, 1.0
    for pop in range(2):
        k = 8 * pop
        own_row = [mine[:, k + s : k + s + 1] for s in range(3)]
        near_row = [mine[:, k + 3 + s : k + 4 + s] for s in range(3)]
        self_product *= correlation(own_row, own_row, mine[:, k + 6 : k + 7])
        far_product *= correlation(own_row, near_row, mine[:, k + 7 : k + 8])
    mine_annots = annots[out_rows, :]
    far_reach = jnp.where(me < groups // 2, reach_up, reach_down)
    scores[out_rows, :] += (
        mine_annots * self_product
        + near_annots[out_rows, :] * jnp.where(reach_here >= snps, far_product, 0.0)
        + pltpu.roll(mine_annots, HALF_LANES, 1) * jnp.where(far_reach >= snps, far_product, 0.0)
    )
    send_shares(groups, scores, out_share, targets)


def pack_halves(values):
    half = values.shape[0] // 2
    left = iota((half, LANES), 1) < HALF_LANES
    return jnp.where(left, values[0:half], pltpu.roll(values[half:], HALF_LANES, 1))


def unpack_halves(packed):
    return jnp.concatenate([packed, pltpu.roll(packed, HALF_LANES, 1)], axis=0)


def dot_rounded(values, right, axis):
    dims = (((axis,), (0,)), ((), ()))
    return lax.dot_general(
        values.astype(jnp.bfloat16), right, dims, preferred_element_type=jnp.float32
    )


def owner_places(groups, size):
    me = lax.axis_index("hap")

    def mine(blocks, slot):
        value = blocks[0][slot]
        for group in range(1, groups):
            value = jnp.where(me == group, blocks[group][slot], value)
        return value * size

    left = [mine(LEFT_BLOCKS, slot) for slot in range(groups)]
    right = [mine(RIGHT_BLOCKS, slot) for slot in range(groups)]
    return left + left[0:1], right + [(2 * me + 1) * size]


def rows_at(ref, places, size):
    return jnp.concatenate([ref[pl.ds(pl.multiple_of(place, 8), size), :] for place in places], axis=0)


def own_score_kernel(
    groups, share, reach_ref, *refs
):
    own_parts, refs = refs[: groups - 1], refs[groups - 1 :]
    annot_ref, near_annot_ref, scores, mine_ref, rows_ref, masks_ref, columns_ref, own_rows_ref, table = refs
    snps = annot_ref.shape[0]
    half = snps // 2
    wide = snps // groups
    tiles = snps // LANES
    me = lax.axis_index("hap")
    reach_here = reach_ref[lax.axis_index("snp")]
    own_sums = sum((part[...] for part in own_parts[1:]), own_parts[0][...])
    own_counts = from_tiles(own_sums[0 : tiles * share, :], share)
    extras = from_fields(own_sums[tiles * share :, :])

    own_stats, lines = [], []
    for pop in range(2):
        count = jnp.concatenate([extras[pop][tiles : tiles + 1, :]] * tiles, axis=1)
        totals = jnp.concatenate([extras[pop][k : k + 1, :] for k in range(tiles)], axis=1)
        own_stats.append(column_stats(totals, count))
        lines += [*own_stats[pop], totals]
    table[:, 0:8] = jnp.concatenate(lines, axis=0).T

    low_rows = pl.multiple_of(me * share, 8)
    high_rows = pl.multiple_of(half + me * share, 8)

    def both(ref):
        return jnp.concatenate([ref[pl.ds(low_rows, share), :], ref[pl.ds(high_rows, share), :]], axis=0)

    here = both(table)
    own_fields = from_fields(
        jnp.concatenate([pltpu.roll(own_counts, half, 1), own_counts], axis=0)
    )
    shape = (2 * share, snps)
    local, col = iota(shape, 0), iota(shape, 1)
    low = local < share
    row = jnp.where(low, local, local + half - share) + me * share
    product = 1.0
    for pop in range(2):
        row_stats = [here[:, 4 * pop + k : 4 * pop + k + 1] for k in range(3)]
        product *= correlation(row_stats, own_stats[pop], own_fields[pop])
    inside = (low & (col > row)) | (~low & (col >= half) & (col < row))
    own_kept = jnp.where(inside & (jnp.abs(col - row) <= reach_here), product, 0.0)
    rows_here = both(annot_ref).astype(jnp.bfloat16)
    scores[...] = dot_rounded(own_kept, rows_here, 0)
    direct = dot_rounded(own_kept, annot_ref[...].astype(jnp.bfloat16), 1)
    scores[pl.ds(low_rows, share), :] += direct[0:share, :]
    scores[pl.ds(high_rows, share), :] += direct[share:, :]

    slice_rows = pl.ds(pl.multiple_of(me * wide, 8), wide)
    mine = table[slice_rows, :]
    mine_ref[...] = mine
    product = 1.0
    for pop in range(2):
        own_row = [mine[:, 4 * pop + k : 4 * pop + k + 1] for k in range(4)]
        product *= correlation(own_row, own_row, own_row[3])
    scores[slice_rows, :] += annot_ref[slice_rows, :] * product

    size = wide // 2
    left_places, right_places = owner_places(groups, size)
    left_table, right_table = rows_at(table, left_places, size), rows_at(table, right_places, size)
    local, lane = iota((size, LANES), 0), iota((size, LANES), 1)
    own_row = jnp.concatenate(
        [local + jnp.where(lane < size, a, b) for a, b in zip(left_places, right_places)], axis=0
    )
    shape = own_row.shape
    lane = iota(shape, 1)
    is_left = lane < size
    for pop in range(2):
        for k in range(3):
            column = slice(4 * pop + k, 4 * pop + k + 1)
            rows_ref[3 * pop + k] = jnp.where(is_left, left_table[:, column], right_table[:, column])
    upper = me < groups // 2
    block = lax.axis_index("snp")
    last = reach_ref.shape[0] - 1
    reach_there = jnp.where(
        upper, reach_ref[jnp.minimum(block + 1, last)], reach_ref[jnp.maximum(block - 1, 0)]
    )
    apart = jnp.abs(own_row - (lane + me * wide))
    ahead = (own_row - (lane + me * wide)) * jnp.where(upper, 1, -1) > 0
    real = ahead & (lane < wide) & ((lane >= size) | (iota(shape, 0) < groups * size))
    for number, limit in enumerate((reach_here, reach_there)):
        masks_ref[number] = jnp.where(real & (snps - apart <= limit), 1.0, 0.0)
    theirs = near_annot_ref[slice_rows, :]
    columns = [theirs[0:size], pltpu.roll(theirs[size:], HALF_LANES, 1), jnp.zeros((LANES - wide, LANES))]
    columns_ref[...] = jnp.concatenate(columns, axis=0).astype(jnp.bfloat16)
    own_rows = rows_at(annot_ref, left_places, size) + pltpu.roll(
        rows_at(annot_ref, right_places, size), HALF_LANES, 1
    )
    own_rows_ref[...] = own_rows.astype(jnp.bfloat16)


def near_score_kernel(groups, share, reach_ref, *refs):
    near_parts, refs = refs[:groups], refs[groups:]
    own_ref, mine_ref, rows_ref, masks_ref, columns_ref, own_rows_ref, annot_ref, near_annot_ref = refs[:8]
    out_ref, *targets, near_out_ref, flipped, scores = refs[8:]
    snps = annot_ref.shape[0]
    wide = snps // groups
    size = wide // 2
    tiles = snps // LANES
    me = lax.axis_index("hap")
    block = lax.axis_index("snp")
    last = reach_ref.shape[0] - 1
    reach_here = reach_ref[block]
    reach_there = jnp.where(
        me < groups // 2, reach_ref[jnp.minimum(block + 1, last)], reach_ref[jnp.maximum(block - 1, 0)]
    )

    scores[...] = own_ref[...]
    near_sums = sum((part[...] for part in near_parts[1:]), near_parts[0][...])
    near_counts = from_tiles(near_sums[0 : tiles * share, :], share)
    extras = from_fields(near_sums[tiles * share :, :])
    near_stats, near_lines = [], []
    for pop in range(2):
        near_stats.append(column_stats(extras[pop][1:2, :], extras[pop][0:1, :]))
        near_lines += [*near_stats[pop], extras[pop][2:3, :]]
    near_table = jnp.concatenate(near_lines, axis=0).T[0:wide, :]

    slots = [near_counts[:, 0:LANES]]
    for slot in range(1, groups):
        slots.append(pltpu.roll(near_counts, snps - slot * wide, 1)[:, 0:LANES])
    flipped[:, 0:size] = slots[0].T
    slots.append(pltpu.roll(flipped[0:size, :], size, 1))
    near_fields = from_fields(jnp.concatenate(slots, axis=0))
    product = 1.0
    for pop in range(2):
        row_stats = [rows_ref[3 * pop + k] for k in range(3)]
        product *= correlation(row_stats, near_stats[pop], near_fields[pop])
    near_here = jnp.where(masks_ref[0] > 0.0, product, 0.0)
    near_there = jnp.where(masks_ref[1] > 0.0, product, 0.0)
    slice_rows = pl.ds(pl.multiple_of(me * wide, 8), wide)
    direct = dot_rounded(near_here, columns_ref[...], 1)
    turned = pltpu.roll(direct, HALF_LANES, 1)
    for values, places in zip((direct, turned), owner_places(groups, size)):
        for slot, place in enumerate(places):
            scores[pl.ds(pl.multiple_of(place, 8), size), :] += values[slot * size : (slot + 1) * size, :]
    near_scores = dot_rounded(near_there, own_rows_ref[...], 0)
    near_scores = jnp.where(
        iota((size, LANES), 1) < HALF_LANES, near_scores[0:size], near_scores[size:wide]
    )

    mine_table = mine_ref[...]
    far_product = 1.0
    for pop in range(2):
        own_row = [mine_table[:, 4 * pop + k : 4 * pop + k + 1] for k in range(3)]
        near_row = [near_table[:, 4 * pop + k : 4 * pop + k + 1] for k in range(4)]
        far_product *= correlation(own_row, near_row, near_row[3])
    scores[slice_rows, :] += near_annot_ref[slice_rows, :] * jnp.where(reach_here >= snps, far_product, 0.0)
    far_scores = annot_ref[slice_rows, :] * jnp.where(reach_there >= snps, far_product, 0.0)
    near_out_ref[...] = (near_scores + pack_halves(far_scores)).astype(near_out_ref.dtype)

    def packed(step):
        group = partner(me, step, groups)
        return pack_halves(scores[pl.ds(pl.multiple_of(group * wide, 8), wide), :])

    out_ref[...] = packed(0)
    for step, target in enumerate(targets, 1):
        target[...] = packed(step).astype(target.dtype)


def column_finish_kernel(*refs):
    *parts, out_ref = refs
    packed = sum(part[...].astype(jnp.float32) for part in parts)
    out_ref[...] = unpack_halves(packed).T[0 : out_ref.shape[0], :]


def sum_kernel(*refs):
    *parts, own_ref, there_ref = refs
    total = sum((part[...].astype(jnp.float32) for part in parts[1:]), parts[0][...])
    own_ref[...] = total
    half = there_ref.shape[0]
    left = iota((half, LANES), 1) < HALF_LANES
    second = total[half:]
    if second.shape[0] < half:
        second = jnp.concatenate([second, jnp.zeros((half - second.shape[0], LANES))], axis=0)
    there_ref[...] = jnp.where(left, pltpu.roll(total[0:half], HALF_LANES, 1), second)


def finish_kernel(own_ref, there_ref, out_ref):
    annots, rows = out_ref.shape
    there = there_ref[...]
    there = jnp.concatenate([there, pltpu.roll(there, HALF_LANES, 1)], axis=0)
    out_ref[...] = (own_ref[...] + there[0:rows]).T[0:annots, :]


def around(value, groups, step):
    return lax.ppermute(
        value, "hap", [(source, partner(source, step, groups)) for source in range(groups)]
    )


def swapped(value, first):
    pairs = []
    for block in range(first, lax.axis_size("snp") - 1, 2):
        pairs += [(block, block + 1), (block + 1, block)]
    return lax.ppermute(value, "snp", pairs)


def per_device(haplotypes, labels, annotations, reach):
    rows, snps = haplotypes.shape
    half = snps // 2
    groups = lax.axis_size("hap")
    blocks = lax.axis_size("snp")
    share = round_up(-(-half // groups), 16)
    folded_rows = share * groups
    out_share = snps // groups
    padded = half + folded_rows
    annot_part = 32
    bf16, f32, i32 = jnp.bfloat16, jnp.float32, jnp.int32
    shape = jax.ShapeDtypeStruct

    packed = shape((rows // 2 + annot_part, snps), bf16)
    haplotypes = pltpu.with_memory_space_constraint(haplotypes, pltpu.HBM)
    annots_in = pltpu.with_memory_space_constraint(annotations, pltpu.HBM)
    alleles, far, close = call(
        prepare_kernel,
        [shape((rows, snps), bf16), packed, packed],
        [HBM, HBM],
        [
            pltpu.VMEM((rows, snps), i32),
            pltpu.VMEM(annotations.shape, i32),
            pltpu.SemaphoreType.DMA((2 * CHUNKS + 1,)),
        ],
        moved=rows * snps * 8,
    )(haplotypes, annots_in)
    from_far = swapped(far, 1)
    from_close = swapped(close, 0)

    by_column = groups == len(LEFT_BLOCKS)
    compact = shape((share * (snps // LANES) + 8, LANES), i32)
    own_share_counts = compact if by_column else shape((share, snps), i32)
    tile = pltpu.VMEM((snps + 16, snps), f32)
    folded = pltpu.VMEM((folded_rows, snps), i32)
    weighted, totals, *own_parts = call(
        functools.partial(own_kernel, groups, share),
        [shape((snps + 16, rows), bf16), shape((8, snps), f32)] + [own_share_counts] * groups,
        [VMEM, VMEM],
        [tile, folded],
        flops=2 * rows * snps * snps,
        moved=rows * snps * 4,
    )(alleles, labels.reshape(1, rows))
    own_parts = [own_parts[0]] + [around(own_parts[k], groups, k) for k in range(groups - 1, 0, -1)]

    near_shapes = [own_share_counts] + [compact if by_column else shape((share + 8, snps), i32)] * groups
    if by_column:
        piece = shape((snps + 16, LANES), f32)
        work = dict(flops=4 * rows * snps * LANES, moved=rows * snps * 4)
        close_counts = call(close_kernel, [piece, piece], [VMEM] * 2, **work)(weighted, from_close)
        own_sum, *near_parts = call(
            functools.partial(far_kernel, groups, share),
            near_shapes,
            [VMEM] * 7,
            [
                tile,
                folded,
                pltpu.VMEM((snps, LANES), f32),
                pltpu.VMEM((8 * groups, LANES), i32),
            ],
            **work,
        )(weighted, from_far, *close_counts, totals, own_parts[0], own_parts[-1])
    else:
        own_sum, *near_parts = call(
            functools.partial(near_kernel, groups, share),
            near_shapes,
            [VMEM] * (4 + groups),
            [pltpu.VMEM((rows, snps), bf16), tile, folded],
            flops=2 * rows * snps * snps,
            moved=rows * snps * 4,
        )(weighted, from_far, from_close, totals, *own_parts)
    order = (2, 3, 1) if by_column else range(groups - 1, 0, -1)
    near_parts = [near_parts[0]] + [around(near_parts[k], groups, k) for k in order]

    by_snp = shape((snps, LANES), f32)
    own_annots, near_annots = call(annots_kernel, [by_snp, by_snp], [VMEM] * 3, moved=1 << 20)(
        annotations, from_far[rows // 2 :], from_close[rows // 2 :]
    )
    pairs = []
    for block in range(blocks):
        for group in range(groups):
            target = block + 1 if group < groups // 2 else block - 1
            if 0 <= target < blocks:
                pairs.append((block * groups + group, target * groups + group))

    def to_neighbour(value):
        return lax.ppermute(value, ("snp", "hap"), pairs)

    result = shape((annotations.shape[0], out_share), f32)
    half_share = round_up(-(-out_share // 2), 8)
    own_share = shape((out_share, LANES), f32)
    packed_share = shape((half_share, LANES), f32)
    if by_column:
        pair_rows = (groups + 1) * (out_share // 2)
        prepared = call(
            functools.partial(own_score_kernel, groups, share),
            [
                by_snp,
                shape((out_share, LANES), f32),
                shape((6, pair_rows, LANES), f32),
                shape((2, pair_rows, LANES), f32),
                shape((LANES, LANES), bf16),
                shape((pair_rows, LANES), bf16),
            ],
            [SMEM] + [VMEM] * (groups + 1),
            [pltpu.VMEM((snps, LANES), f32)],
            flops=1 << 25,
            moved=1 << 20,
        )(reach, own_sum, *own_parts[1:-1], own_annots, near_annots)
        sent = shape((half_share, LANES), bf16)
        own_scores, *scores = call(
            functools.partial(near_score_kernel, groups, share),
            [packed_share] + [sent] * groups,
            [SMEM] + [VMEM] * (groups + 8),
            [pltpu.VMEM((LANES, LANES), i32), pltpu.VMEM((snps, LANES), f32)],
            flops=1 << 26,
            moved=1 << 21,
        )(reach, *near_parts, *prepared, own_annots, near_annots)
        *scores, there = scores
        scores = [around(scores[k - 1], groups, k) for k in order]
        return call(column_finish_kernel, result, [VMEM] * (groups + 1))(
            own_scores, *scores, to_neighbour(there)
        )

    tall = pltpu.VMEM((padded, LANES), f32)
    scores = call(
        functools.partial(score_kernel, groups, share),
        [own_share] + [shape((out_share, LANES), bf16)] * (groups - 1),
        [SMEM] + [VMEM] * (groups + 3),
        [tall, tall, tall, tall],
        flops=1 << 26,
        moved=1 << 21,
    )(reach, own_sum, *near_parts, own_annots, near_annots)
    scores = [scores[0]] + [around(scores[k], groups, k) for k in range(groups - 1, 0, -1)]
    own_scores, near_scores = call(sum_kernel, [own_share, packed_share], [VMEM] * groups)(*scores)
    return call(finish_kernel, result, [VMEM] * 2)(own_scores, to_neighbour(near_scores))


def solution(mesh):
    in_specs = (
        P("hap", ("parts", "snp")),
        P(("parts", "hap")),
        P(None, ("parts", "snp")),
        P("parts"),
    )
    out_specs = P(None, ("parts", "snp", "hap"))
    return jax.shard_map(
        per_device, mesh=mesh, in_specs=in_specs, out_specs=out_specs, check_vma=False
    )
```

```python
import functools

import jax
import jax.numpy as jnp
from jax import lax
from jax.experimental import pallas as pl
from jax.experimental.pallas import tpu as pltpu
from jax.sharding import PartitionSpec as P

VARIANCE_FLOOR = 0.01
BASE_BITS = 12
BASE = 1 << BASE_BITS
FIELD_BITS = 16
LANES = 128
HALF_LANES = LANES // 2
CHUNKS = 4
VMEM = pl.BlockSpec(memory_space=pltpu.VMEM)
SMEM = pl.BlockSpec(memory_space=pltpu.SMEM)
HBM = pl.BlockSpec(memory_space=pltpu.HBM)
VMEM_LIMIT = 24 * 1024 * 1024


def iota(shape, axis):
    return lax.broadcasted_iota(jnp.int32, shape, axis)


def round_up(value, step):
    return -(-value // step) * step


def to_fields(values):
    whole = values.astype(jnp.int32)
    return whole + (whole >> BASE_BITS) * ((1 << FIELD_BITS) - BASE)


def from_fields(packed):
    first = packed & ((1 << FIELD_BITS) - 1)
    second = lax.shift_right_logical(packed, FIELD_BITS)
    return first.astype(jnp.float32), second.astype(jnp.float32)


def call(kernel, out_shape, in_specs, scratch_shapes=(), flops=0, moved=0):
    several = isinstance(out_shape, (list, tuple))
    return pl.pallas_call(
        kernel,
        out_shape=out_shape,
        in_specs=in_specs,
        out_specs=[VMEM] * len(out_shape) if several else VMEM,
        scratch_shapes=list(scratch_shapes),
        compiler_params=pltpu.CompilerParams(vmem_limit_bytes=VMEM_LIMIT),
        cost_estimate=pl.CostEstimate(flops=flops, bytes_accessed=moved, transcendentals=0),
    )


def odd_block():
    return lax.rem(lax.axis_index("snp"), 2) == 1


def store_packed(up_ref, down_ref, where, first, second):
    left = iota((first.shape[0], LANES), 1) < HALF_LANES
    middle = first[:, LANES : 2 * LANES]
    turned = pltpu.roll(second[:, LANES : 2 * LANES], HALF_LANES, 1)
    for ref, side, mixed in (
        (up_ref, slice(0, LANES), jnp.where(left, middle, turned)),
        (down_ref, slice(2 * LANES, 3 * LANES), jnp.where(left, turned, middle)),
    ):
        ref[where, 0:LANES] = first[:, side].astype(jnp.bfloat16)
        ref[where, LANES : 2 * LANES] = mixed.astype(jnp.bfloat16)
        ref[where, 2 * LANES : 3 * LANES] = second[:, side].astype(jnp.bfloat16)


def load_packed(up, down):
    left = iota((up.shape[0], LANES), 1) < HALF_LANES
    up_mixed, down_mixed = up[:, LANES : 2 * LANES], down[:, LANES : 2 * LANES]
    first = jnp.where(left, up_mixed, down_mixed)
    second = jnp.where(left, down_mixed, up_mixed)
    second = pltpu.roll(second.astype(jnp.float32), HALF_LANES, 1).astype(second.dtype)
    return (
        (up[:, :LANES], first, down[:, :LANES]),
        (up[:, 2 * LANES :], second, down[:, 2 * LANES :]),
    )


def prepare_kernel(hap_ref, annot_ref, alleles_ref, far_ref, close_ref, held, held_annots, sems):
    rows = hap_ref.shape[0]
    annot_rows = annot_ref.shape[0]
    size = rows // (2 * CHUNKS)
    starts = [side * (rows // 2) + chunk * size for chunk in range(CHUNKS) for side in range(2)]
    copies = [
        pltpu.make_async_copy(
            hap_ref.at[pl.ds(start, size)], held.at[pl.ds(start, size)], sems.at[number]
        )
        for number, start in enumerate(starts)
    ]
    copies.append(pltpu.make_async_copy(annot_ref, held_annots, sems.at[2 * CHUNKS]))
    for copy in copies:
        copy.start()
    part = far_ref.shape[0] - rows // 2
    odd = odd_block()

    def store(where, first, second):
        @pl.when(odd)
        def _():
            store_packed(close_ref, far_ref, where, first, second)

        @pl.when(jnp.logical_not(odd))
        def _():
            store_packed(far_ref, close_ref, where, first, second)

    for chunk in range(CHUNKS):
        pair = []
        for side in range(2):
            number = 2 * chunk + side
            copies[number].wait()
            where = slice(starts[number], starts[number] + size)
            values = held[where, :].astype(jnp.float32)
            alleles_ref[where, :] = values.astype(jnp.bfloat16)
            pair.append(values)
        store(slice(chunk * size, (chunk + 1) * size), *pair)
    copies[-1].wait()
    annots = jnp.concatenate(
        [
            held_annots[...].astype(jnp.float32),
            jnp.zeros((2 * part - annot_rows, annot_ref.shape[1]), jnp.float32),
        ],
        axis=0,
    )
    store(slice(rows // 2, rows // 2 + part), annots[:part], annots[part:])


def partner(group, step, groups):
    if groups & (groups - 1) == 0:
        return group ^ step
    return (group + step) % groups


def send_shares(groups, source, share, targets):
    me = lax.axis_index("hap")
    for step, target in enumerate(targets):
        group = partner(me, step, groups)
        rows = source[pl.ds(pl.multiple_of(group * share, 8), share), :]
        target[0:share, :] = rows.astype(target.dtype)


def send_tiles(groups, source, share, targets):
    me = lax.axis_index("hap")
    for step, target in enumerate(targets):
        owner = partner(me, step, groups)
        counts = source[pl.ds(pl.multiple_of(owner * share, 8), share), :]
        for k in range(source.shape[1] // LANES):
            target[k * share : (k + 1) * share, :] = counts[:, k * LANES : (k + 1) * LANES]


def from_tiles(counts, share):
    tiles = counts.shape[0] // share
    return jnp.concatenate([counts[k * share : (k + 1) * share, :] for k in range(tiles)], axis=1)


def own_kernel(groups, share, alleles_ref, label_ref, *refs):
    weighted_ref, totals_ref, *targets = refs[: 2 + groups]
    tile, folded = refs[2 + groups :]
    rows, snps = alleles_ref.shape
    half = snps // 2
    weight = jnp.where(label_ref[...] > 0, float(BASE), 1.0)
    weighted_ref[0:snps, :] = alleles_ref[...].T * weight.astype(jnp.bfloat16)
    extra = weighted_ref.shape[0] - snps
    weighted_ref[snps:, :] = jnp.broadcast_to(weight, (extra, rows)).astype(jnp.bfloat16)
    tile[...] = jnp.dot(weighted_ref[...], alleles_ref[...], preferred_element_type=jnp.float32)
    count = jnp.sum(weight, axis=1, keepdims=True)
    totals_ref[...] = jnp.concatenate(
        [tile[snps : snps + 1, :], jnp.broadcast_to(count, (1, snps)), jnp.zeros((6, snps))], axis=0
    )
    if groups == len(LEFT_BLOCKS):
        fold_halves(tile, folded)
        shared = [totals_ref[0:1, k * LANES : (k + 1) * LANES] for k in range(snps // LANES)]
        shared += [totals_ref[1:2, 0:LANES], jnp.zeros((7 - len(shared), LANES))]
        extras = to_fields(jnp.concatenate(shared, axis=0))
        me = lax.axis_index("hap")
        count = folded.shape[0] // groups
        for step, target in enumerate(targets):
            start = partner(me, step, groups) * count
            done = 0
            for first, size in ((0, share), (share, share // 2)):
                counts = folded[pl.ds(pl.multiple_of(start + first, 8), size), :]
                for k in range(snps // LANES):
                    target[done : done + size, :] = counts[:, k * LANES : (k + 1) * LANES]
                    done += size
            target[done:, :] = extras
        return
    row, col = iota((half, snps), 0), iota((half, snps), 1)
    moved = (col < half) | (col - half > row)
    turned = pltpu.roll(tile[0:half, :], half, 1)
    folded[0:half, :] = to_fields(jnp.where(moved, turned, tile[half:snps, :]))
    if folded.shape[0] > half:
        folded[half:, :] = jnp.zeros((folded.shape[0] - half, snps), jnp.int32)
    send_shares(groups, folded, share, targets)


def fold_halves(tile, folded):
    snps = tile.shape[1]
    half, wide = snps // 2, snps // 4
    size, count = wide // 2, folded.shape[0] // 4
    top, bottom = tile[0:half, :], tile[half:snps, :]
    top_turned, bottom_turned = pltpu.roll(top, half, 1), pltpu.roll(bottom, half, 1)
    row, lane = iota((wide, snps), 0), iota((wide, snps), 1)
    for side, square in enumerate((top, bottom_turned)):
        first = square[0:wide]
        within = jnp.where(
            lane < wide,
            pltpu.roll(first, snps - wide, 1),
            jnp.where(lane - wide > row, pltpu.roll(first, wide, 1), square[wide:]),
        )
        for part in range(2):
            start = (2 * side + part) * count
            rows = part * wide
            between = jnp.where(
                lane[0:size] < half, top_turned[rows : rows + size], top[rows + size : rows + wide]
            )
            folded[start : start + size, :] = to_fields(between)
            rows = within[part * size : (part + 1) * size]
            rows = jnp.where(
                lane[0 : size // 2] < half, rows[0 : size // 2], pltpu.roll(rows[size // 2 :], half, 1)
            )
            folded[start + size : start + count, :] = to_fields(rows)


LEFT_BLOCKS = ((0, 1, 2, 3), (2, 3, 6, 7), (4, 0, 1, 2), (6, 0, 4, 5))
RIGHT_BLOCKS = ((2, 3, 6, 7), (4, 5, 6, 7), (0, 1, 2, 4), (0, 4, 5, 6))


SPARE_OWN = ((0, 0, 0, 0), (1, 1, 2, 2), (4, 5, 6, 7), (6, 6, 7, 7))
SPARE_NEAR = ((4, 5, 6, 7), (4, 5, 4, 5), (3, 3, 3, 3), (1, 2, 1, 2))


def fold_spare(tile, spare):
    owners = len(SPARE_OWN)
    snps = tile.shape[1]
    size = snps // (2 * owners)
    count = spare.shape[0] // owners
    totals = tile[snps : snps + count - size, :]
    lane = iota((count, snps), 1)
    for owner in range(owners):
        mixed = None
        for slot in range(owners):
            own, near = SPARE_OWN[owner][slot], SPARE_NEAR[owner][slot]
            before = (SPARE_OWN[owner][slot - 1], SPARE_NEAR[owner][slot - 1] + 1) if slot else None
            if before == (own, near):
                continue
            values = jnp.concatenate([tile[own * size : (own + 1) * size, :], totals], axis=0)
            shift = (slot - near) * size % snps
            values = pltpu.roll(values, shift, 1) if shift else values
            mixed = values if mixed is None else jnp.where(lane >= slot * size, values, mixed)
        spare[owner * count : (owner + 1) * count, :] = to_fields(mixed[:, 0 : spare.shape[1]])


def fold_by_column(tile, flipped, folded):
    owners = len(LEFT_BLOCKS)
    snps = folded.shape[1]
    wide = snps // owners
    size = wide // 2
    shape = (size, snps)
    row, lane = iota(shape, 0), iota(shape, 1)

    def block(number):
        return tile[number * size : (number + 1) * size, :]

    diagonal = block(0)
    for number in range(1, 2 * owners):
        diagonal = jnp.where(lane >= number * size, block(number), diagonal)
    flipped[:, 0:size] = diagonal.T
    corner = diagonal
    for owner in range(owners):
        start = (2 * owner + 1) * size
        turned = jnp.concatenate(
            [flipped[start : start + size, :], jnp.zeros((size, snps - LANES), jnp.float32)], axis=1
        )
        if owner:
            turned = pltpu.roll(turned, owner * wide, 1)
        inside = lane - owner * wide
        other = (row <= inside) if owner < owners // 2 else (row >= inside)
        corner = jnp.where((inside >= 0) & (inside < size) & other, turned, corner)
    rolled = []
    for shift in range(owners):
        mixed = None
        for owner in range(owners):
            slot = (owner + shift) % owners
            left = block(LEFT_BLOCKS[owner][slot]) if slot else corner
            start = owner * wide
            mixed = left if mixed is None else jnp.where(lane >= start, left, mixed)
            mixed = jnp.where(lane >= start + size, block(RIGHT_BLOCKS[owner][slot]), mixed)
        rolled.append(pltpu.roll(mixed, shift * wide, 1) if shift else mixed)
    for owner in range(owners):
        mixed = rolled[(0 - owner) % owners]
        for slot in range(1, owners):
            mixed = jnp.where(lane >= slot * wide, rolled[(slot - owner) % owners], mixed)
        folded[owner * size : (owner + 1) * size, :] = to_fields(mixed)


def above(far):
    return odd_block() == far


def side_dot(weighted_ref, side_ref):
    rows = weighted_ref.shape[1]
    half = rows // 2

    def dot(which, columns):
        return jnp.dot(
            weighted_ref[:, which], side_ref[0:half, columns], preferred_element_type=jnp.float32
        )

    first = dot(slice(0, half), slice(0, 2 * LANES))
    second = dot(slice(half, rows), slice(LANES, 3 * LANES))
    whole = first[:, 0:LANES] + second[:, LANES:]
    return whole, first[:, LANES:] + pltpu.roll(second[:, 0:LANES], HALF_LANES, 1)


def close_kernel(weighted_ref, side_ref, whole_ref, shared_ref):
    whole_ref[...], shared_ref[...] = side_dot(weighted_ref, side_ref)


def far_kernel(
    groups, share, weighted_ref, side_ref, whole_ref, shared_ref, totals_ref, mine_ref, nearest_ref, own_sum_ref, *refs
):
    targets, (tile, folded, flipped, spare, extras) = refs[:groups], refs[groups:]
    snps = tile.shape[1]
    own_sum_ref[...] = mine_ref[...] + nearest_ref[...]
    whole, shared = side_dot(weighted_ref, side_ref)
    left = iota(shared.shape, 1) < HALF_LANES

    @pl.when(above(True))
    def _():
        tile[:, 0:LANES] = whole
        tile[:, LANES : 2 * LANES] = jnp.where(left, shared, shared_ref[...])
        tile[:, 2 * LANES :] = whole_ref[...]

    @pl.when(jnp.logical_not(above(True)))
    def _():
        tile[:, 0:LANES] = whole_ref[...]
        tile[:, LANES : 2 * LANES] = jnp.where(left, shared_ref[...], shared)
        tile[:, 2 * LANES :] = whole

    fold_by_column(tile, flipped, folded)
    square = (snps, snps)
    apart = jnp.sum(
        jnp.where(iota(square, 0) == iota(square, 1), tile[0:snps, :], 0.0), axis=0, keepdims=True
    )
    fold_spare(tile, spare)
    tiles = snps // LANES
    size = share
    count = spare.shape[0] // groups
    sizes = totals_ref[1:2, :]
    by_column = jnp.concatenate([sizes, tile[snps : snps + 1, :], apart, jnp.zeros((5, snps))], axis=0)
    for owner in range(groups):
        start = owner * (snps // groups)
        columns = pltpu.roll(by_column, snps - start, 1) if owner else by_column
        spare_totals = spare[owner * count + size : owner * count + size + 1, :]
        extras[8 * owner : 8 * (owner + 1), :] = jnp.concatenate(
            [
                to_fields(columns[0:3, 0:LANES]),
                spare_totals[:, 0:LANES],
                spare_totals[:, LANES:],
                jnp.zeros((3, LANES), jnp.int32),
            ],
            axis=0,
        )
    me = lax.axis_index("hap")
    send_tiles(groups, folded, share, targets)
    left = iota((size // 2, LANES), 1) < HALF_LANES
    for step, target in enumerate(targets):
        owner = partner(me, step, groups)
        counts = spare[pl.ds(pl.multiple_of(owner * count, 8), size), :]
        start = tiles * size
        target[start : start + size, :] = counts[:, 0:LANES]
        rest = counts[:, LANES:]
        target[start + size : start + size + size // 2, :] = jnp.where(
            left, rest[0 : size // 2], pltpu.roll(rest[size // 2 :], HALF_LANES, 1)
        )
        target[start + size + size // 2 :, :] = extras[pl.ds(pl.multiple_of(owner * 8, 8), 8), :]


def near_kernel(groups, share, weighted_ref, far_ref, close_ref, totals_ref, *refs):
    own_parts, own_sum_ref = refs[:groups], refs[groups]
    targets, (near, tile, folded) = refs[groups + 1 : 2 * groups + 1], refs[2 * groups + 1 :]
    rows, snps = near.shape
    half = snps // 2
    odd = odd_block()

    def unpack(up_ref, down_ref):
        pieces = load_packed(up_ref[0 : rows // 2, :], down_ref[0 : rows // 2, :])
        for side in range(2):
            where = slice(side * (rows // 2), (side + 1) * (rows // 2))
            for number in range(3):
                near[where, number * LANES : (number + 1) * LANES] = pieces[side][number]

    @pl.when(odd)
    def _():
        unpack(far_ref, close_ref)

    @pl.when(jnp.logical_not(odd))
    def _():
        unpack(close_ref, far_ref)

    tile[...] = jnp.dot(weighted_ref[...], near[...], preferred_element_type=jnp.float32)
    row, col = iota((half, snps), 0), iota((half, snps), 1)
    moved = (col >= half) & (col - half < row)
    turned = pltpu.roll(tile[0:half, :], half, 1)
    folded[0:half, :] = to_fields(jnp.where(moved, turned, tile[half:snps, :]))
    if folded.shape[0] > half:
        folded[half:, :] = jnp.zeros((folded.shape[0] - half, snps), jnp.int32)
    square = (snps, snps)
    far = jnp.sum(
        jnp.where(iota(square, 0) == iota(square, 1), tile[0:snps, :], 0.0), axis=0, keepdims=True
    )
    extras = to_fields(
        jnp.concatenate(
            [totals_ref[0:2, :], tile[snps : snps + 1, :], far, jnp.zeros((4, snps))], axis=0
        )
    )
    send_shares(groups, folded, share, targets)
    for target in targets:
        target[share:, :] = extras
    own_sum_ref[...] = sum((part[...] for part in own_parts[1:]), own_parts[0][...])


def annots_kernel(annot_ref, far_ref, close_ref, own_ref, near_ref):
    snps = annot_ref.shape[1]
    part = far_ref.shape[0]
    wide = 2 * part
    own = annot_ref[...].astype(jnp.float32)
    own = jnp.concatenate([own, jnp.zeros((LANES - own.shape[0], snps), jnp.float32)], axis=0)
    own_ref[...] = own.T
    odd = odd_block()
    far, close = far_ref[...].astype(jnp.float32), close_ref[...].astype(jnp.float32)
    first, second = load_packed(jnp.where(odd, far, close), jnp.where(odd, close, far))
    near = jnp.concatenate(
        [
            jnp.concatenate([piece.astype(jnp.float32) for piece in first], axis=1),
            jnp.concatenate([piece.astype(jnp.float32) for piece in second], axis=1),
            jnp.zeros((LANES - wide, snps), jnp.float32),
        ],
        axis=0,
    )
    near_ref[...] = near.T


def column_stats(totals, count):
    size = jnp.maximum(count, 1.0)
    frequency = totals / size
    variance = jnp.maximum(frequency * (1.0 - frequency), VARIANCE_FLOOR)
    inverse = 1.0 / jnp.sqrt(size * variance)
    low = ((0.0 - frequency) * inverse).astype(jnp.bfloat16).astype(jnp.float32)
    high = ((1.0 - frequency) * inverse).astype(jnp.bfloat16).astype(jnp.float32)
    step = high - low
    root = 1.0 / jnp.sqrt(size)
    return step, step * totals * root, (low * count + step * totals) * root


def correlation(row, col, count):
    return row[0] * col[0] * count - row[1] * col[1] + row[2] * col[2]


def split(values):
    high = values.astype(jnp.bfloat16)
    return high, (values - high.astype(jnp.float32)).astype(jnp.bfloat16)


def dot_split(values, right, axis):
    dims = (((axis,), (0,)), ((), ()))
    return sum(
        lax.dot_general(part, right, dims, preferred_element_type=jnp.float32)
        for part in split(values)
    )


def score_kernel(groups, share, reach_ref, *refs):
    own_sum_ref, near_parts = refs[0], refs[1 : groups + 1]
    annot_ref, near_annot_ref = refs[groups + 1 : groups + 3]
    targets = refs[groups + 3 : 2 * groups + 3]
    table, annots, near_annots, scores = refs[2 * groups + 3 :]
    snps = annot_ref.shape[0]
    half = snps // 2
    out_share = snps // groups
    me = lax.axis_index("hap")
    block = lax.axis_index("snp")
    last = reach_ref.shape[0] - 1
    reach_here = reach_ref[block]
    reach_up = reach_ref[jnp.minimum(block + 1, last)]
    reach_down = reach_ref[jnp.maximum(block - 1, 0)]

    own_counts = own_sum_ref[...]
    near_sums = sum((part[...] for part in near_parts[1:]), near_parts[0][...])
    extras = from_fields(near_sums[share:, :])
    near_counts = near_sums[0:share, :]

    own_stats, near_stats, lines = [], [], []
    for pop in range(2):
        count = extras[pop][1:2, :]
        own_stats.append(column_stats(extras[pop][0:1, :], count))
        near_stats.append(column_stats(extras[pop][2:3, :], count))
        lines += [*own_stats[pop], *near_stats[pop], extras[pop][0:1, :], extras[pop][3:4, :]]
    by_row = jnp.concatenate(lines, axis=0).T
    table[0:snps, 0:16] = by_row
    if table.shape[0] > snps:
        table[snps:, 0:16] = jnp.zeros((table.shape[0] - snps, 16), jnp.float32)
    annots[0:snps, :] = annot_ref[...]
    near_annots[0:snps, :] = near_annot_ref[...]
    if annots.shape[0] > snps:
        annots[snps:, :] = jnp.zeros((annots.shape[0] - snps, LANES), jnp.float32)

    low_rows = pl.multiple_of(me * share, 8)
    high_rows = pl.multiple_of(half + me * share, 8)

    def both(ref):
        return jnp.concatenate([ref[pl.ds(low_rows, share), :], ref[pl.ds(high_rows, share), :]], axis=0)

    here = both(table)
    own_count = jnp.concatenate([pltpu.roll(own_counts, half, 1), own_counts], axis=0)
    near_count = jnp.concatenate([pltpu.roll(near_counts, half, 1), near_counts], axis=0)
    shape = (2 * share, snps)
    local, col = iota(shape, 0), iota(shape, 1)
    low = local < share
    place = jnp.where(low, local, local - share) + me * share
    row = jnp.where(low, place, place + half)
    own_fields, near_fields = from_fields(own_count), from_fields(near_count)
    own_product, near_product = 1.0, 1.0
    for pop in range(2):
        row_stats = [here[:, 8 * pop + k : 8 * pop + k + 1] for k in range(3)]
        own_product *= correlation(row_stats, own_stats[pop], own_fields[pop])
        near_product *= correlation(row_stats, near_stats[pop], near_fields[pop])
    real = place < half
    own_inside = real & ((low & (col > row)) | (~low & (col >= half) & (col < row)))
    own_inside &= jnp.abs(col - row) <= reach_here
    own_kept = jnp.where(own_inside, own_product, 0.0)
    in_upper = col < half
    near_inside = real & ((low & (col < row)) | (~low & (in_upper | (col > row))))
    distance = jnp.where(in_upper, snps + col - row, snps + row - col)
    near_here = jnp.where(near_inside & (distance <= reach_here), near_product, 0.0)
    reach_there = jnp.where(in_upper, reach_up, reach_down)
    near_there = jnp.where(near_inside & (distance <= reach_there), near_product, 0.0)

    rows_here = both(annots)
    rows_there = pltpu.roll(rows_here, HALF_LANES, 1)
    scores[0:snps, :] = dot_split(
        jnp.concatenate([own_kept, near_there], axis=0),
        jnp.concatenate([rows_here, rows_there], axis=0).astype(jnp.bfloat16),
        0,
    )
    direct = dot_split(
        jnp.concatenate([own_kept, near_here], axis=1),
        jnp.concatenate([annot_ref[...], near_annot_ref[...]], axis=0).astype(jnp.bfloat16),
        1,
    )
    scores[pl.ds(low_rows, share), :] += direct[0:share, :]
    scores[pl.ds(high_rows, share), :] += direct[share:, :]

    out_rows = pl.ds(pl.multiple_of(me * out_share, 8), out_share)
    mine = table[out_rows, :]
    self_product, far_product = 1.0, 1.0
    for pop in range(2):
        k = 8 * pop
        own_row = [mine[:, k + s : k + s + 1] for s in range(3)]
        near_row = [mine[:, k + 3 + s : k + 4 + s] for s in range(3)]
        self_product *= correlation(own_row, own_row, mine[:, k + 6 : k + 7])
        far_product *= correlation(own_row, near_row, mine[:, k + 7 : k + 8])
    mine_annots = annots[out_rows, :]
    far_reach = jnp.where(me < groups // 2, reach_up, reach_down)
    scores[out_rows, :] += (
        mine_annots * self_product
        + near_annots[out_rows, :] * jnp.where(reach_here >= snps, far_product, 0.0)
        + pltpu.roll(mine_annots, HALF_LANES, 1) * jnp.where(far_reach >= snps, far_product, 0.0)
    )
    send_shares(groups, scores, out_share, targets)


def pack_halves(values):
    half = values.shape[0] // 2
    left = iota((half, LANES), 1) < HALF_LANES
    return jnp.where(left, values[0:half], pltpu.roll(values[half:], HALF_LANES, 1))


def unpack_halves(packed):
    return jnp.concatenate([packed, pltpu.roll(packed, HALF_LANES, 1)], axis=0)


def dot_rounded(values, right, axis):
    dims = (((axis,), (0,)), ((), ()))
    return lax.dot_general(
        values.astype(jnp.bfloat16), right, dims, preferred_element_type=jnp.float32
    )


def owner_places(groups, size):
    me = lax.axis_index("hap")

    def mine(blocks, slot):
        value = blocks[0][slot]
        for group in range(1, groups):
            value = jnp.where(me == group, blocks[group][slot], value)
        return value * size

    left = [mine(LEFT_BLOCKS, slot) for slot in range(groups)]
    right = [mine(RIGHT_BLOCKS, slot) for slot in range(groups)]
    return left + left[0:1], right + [(2 * me + 1) * size]


def spare_places(groups, size):
    me = lax.axis_index("hap")

    def mine(blocks, slot):
        value = blocks[0][slot]
        for group in range(1, groups):
            value = jnp.where(me == group, blocks[group][slot], value)
        return value * size

    return [[mine(blocks, slot) for slot in range(groups)] for blocks in (SPARE_OWN, SPARE_NEAR)]


def rows_at(ref, places, size):
    return jnp.concatenate([ref[pl.ds(pl.multiple_of(place, 8), size), :] for place in places], axis=0)


def own_score_kernel(
    groups, share, reach_ref, *refs
):
    own_parts, refs = refs[: groups - 1], refs[groups - 1 :]
    annot_ref, near_annot_ref, scores, mine_ref, rows_ref, masks_ref, columns_ref, own_rows_ref, *refs = refs
    spare_rows_ref, spare_mask_ref, spare_columns_ref, table = refs
    snps = annot_ref.shape[0]
    half = snps // 2
    wide = snps // groups
    tiles = snps // LANES
    me = lax.axis_index("hap")
    reach_here = reach_ref[lax.axis_index("snp")]
    own_sums = sum((part[...] for part in own_parts[1:]), own_parts[0][...])
    size = wide // 2
    between = from_tiles(own_sums[0 : tiles * size, :], size)
    done = tiles * (size + size // 2)
    within = from_tiles(own_sums[tiles * size : done, :], size // 2)
    extras = from_fields(own_sums[done:, :])

    own_stats, lines = [], []
    for pop in range(2):
        count = jnp.concatenate([extras[pop][tiles : tiles + 1, :]] * tiles, axis=1)
        totals = jnp.concatenate([extras[pop][k : k + 1, :] for k in range(tiles)], axis=1)
        own_stats.append(column_stats(totals, count))
        lines += [*own_stats[pop], totals]
    table[:, 0:8] = jnp.concatenate(lines, axis=0).T

    upper = me < groups // 2
    part = me & 1
    base = jnp.where(upper, 0, half)
    lanes = 2 * LANES
    between = jnp.concatenate([between, pltpu.roll(between, half, 1)], axis=0)[:, 0:lanes]
    within = jnp.concatenate([within, pltpu.roll(within, half, 1)], axis=0)
    within = jnp.concatenate(
        [
            jnp.where(
                iota(within.shape, 1) >= wide,
                pltpu.roll(within, wide, 1),
                pltpu.roll(within, snps - wide, 1),
            ),
            within,
        ],
        axis=0,
    )[:, 0:lanes]
    between_place = pl.multiple_of(part * wide, 8)
    within_places = [base + part * size, base + wide + part * size]
    between_table = table[pl.ds(between_place, wide), :]
    within_table = rows_at(table, within_places, size)
    between_fields, within_fields = from_fields(between), from_fields(within)
    between_product, within_product = 1.0, 1.0
    for pop in range(2):
        turned = [pltpu.roll(stat, half, 1)[:, 0:lanes] for stat in own_stats[pop]]
        mine = [jnp.where(upper, stat[:, 0:lanes], other) for stat, other in zip(own_stats[pop], turned)]
        columns = [slice(4 * pop + k, 4 * pop + k + 1) for k in range(3)]
        row_stats = [between_table[:, column] for column in columns]
        between_product *= correlation(row_stats, turned, between_fields[pop])
        row_stats = [within_table[:, column] for column in columns]
        within_product *= correlation(row_stats, mine, within_fields[pop])
    shape = (wide, lanes)
    local, col = iota(shape, 0), iota(shape, 1)
    inside = (col < half) & (half + col - local - part * wide <= reach_here)
    between_kept = jnp.where(inside, between_product, 0.0)
    low = local < size
    row = jnp.where(low, local, local + size) + part * size
    inside = (low & (col > row)) | (~low & (col >= wide) & (col < row))
    inside &= (col < half) & (jnp.abs(col - row) <= reach_here)
    within_kept = jnp.where(inside, within_product, 0.0)

    def half_annots(place):
        rows = annot_ref[pl.ds(pl.multiple_of(place, 8), half), :]
        rows = jnp.concatenate([rows, jnp.zeros((lanes - half, LANES), jnp.float32)], axis=0)
        return rows.astype(jnp.bfloat16)

    scores[...] = jnp.zeros_like(scores)
    half_rows = pl.ds(pl.multiple_of(base, 8), half)
    rows = rows_at(annot_ref, within_places, size).astype(jnp.bfloat16)
    scores[half_rows, :] = dot_rounded(within_kept, rows, 0)[0:half, :]
    direct = dot_rounded(within_kept, half_annots(base), 1)
    for number, place in enumerate(within_places):
        scores[pl.ds(pl.multiple_of(place, 8), size), :] += direct[number * size : (number + 1) * size, :]

    @pl.when(upper)
    def _():
        scores[pl.ds(between_place, wide), :] += dot_rounded(between_kept, half_annots(half), 1)

    @pl.when(jnp.logical_not(upper))
    def _():
        rows = annot_ref[pl.ds(between_place, wide), :].astype(jnp.bfloat16)
        scores[half:, :] += dot_rounded(between_kept, rows, 0)[0:half, :]

    slice_rows = pl.ds(pl.multiple_of(me * wide, 8), wide)
    mine = table[slice_rows, :]
    mine_ref[...] = mine
    product = 1.0
    for pop in range(2):
        own_row = [mine[:, 4 * pop + k : 4 * pop + k + 1] for k in range(4)]
        product *= correlation(own_row, own_row, own_row[3])
    scores[slice_rows, :] += annot_ref[slice_rows, :] * product
    left_places, right_places = owner_places(groups, size)
    left_table, right_table = rows_at(table, left_places, size), rows_at(table, right_places, size)
    local, lane = iota((size, LANES), 0), iota((size, LANES), 1)
    own_row = jnp.concatenate(
        [local + jnp.where(lane < size, a, b) for a, b in zip(left_places, right_places)], axis=0
    )
    shape = own_row.shape
    lane = iota(shape, 1)
    is_left = lane < size
    for pop in range(2):
        for k in range(3):
            column = slice(4 * pop + k, 4 * pop + k + 1)
            rows_ref[3 * pop + k] = jnp.where(is_left, left_table[:, column], right_table[:, column])
    block = lax.axis_index("snp")
    last = reach_ref.shape[0] - 1
    reach_there = jnp.where(
        upper, reach_ref[jnp.minimum(block + 1, last)], reach_ref[jnp.maximum(block - 1, 0)]
    )
    apart = jnp.abs(own_row - (lane + me * wide))
    ahead = (own_row - (lane + me * wide)) * jnp.where(upper, 1, -1) > 0
    real = ahead & (lane < wide) & ((lane >= size) | (iota(shape, 0) < groups * size))
    inside = (own_row - half) * jnp.where(upper, 1, -1) < jnp.where(upper, 0, 1)
    masks_ref[0] = jnp.where(real & inside & (snps - apart <= reach_here), 1.0, 0.0)
    masks_ref[1] = jnp.where(real & (snps - apart <= reach_there), 1.0, 0.0)
    theirs = near_annot_ref[slice_rows, :]
    columns = [theirs[0:size], pltpu.roll(theirs[size:], HALF_LANES, 1), jnp.zeros((LANES - wide, LANES))]
    columns_ref[...] = jnp.concatenate(columns, axis=0).astype(jnp.bfloat16)
    own_rows = rows_at(annot_ref, left_places, size) + pltpu.roll(
        rows_at(annot_ref, right_places, size), HALF_LANES, 1
    )
    own_rows_ref[...] = own_rows.astype(jnp.bfloat16)

    own_places, near_places = spare_places(groups, size)
    shape = (size, spare_mask_ref.shape[1])
    local, lane = iota(shape, 0), iota(shape, 1)

    def by_slot(values):
        mixed = values[0]
        for slot in range(1, groups):
            mixed = jnp.where(lane >= slot * size, values[slot], mixed)
        return mixed

    tables = [table[pl.ds(pl.multiple_of(place, 8), size), :] for place in own_places]
    for pop in range(2):
        for k in range(3):
            column = slice(4 * pop + k, 4 * pop + k + 1)
            spare_rows_ref[3 * pop + k] = by_slot(
                [jnp.broadcast_to(values[:, column], shape) for values in tables]
            )
    own_row = by_slot([local + place for place in own_places])
    near_col = by_slot([lane + (place - slot * size) for slot, place in enumerate(near_places)])
    close = snps - jnp.abs(own_row - near_col) <= reach_here
    spare_mask_ref[...] = jnp.where(close & (lane < groups * size), 1.0, 0.0)
    columns = [rows_at(near_annot_ref, near_places, size)]
    columns.append(jnp.zeros((shape[1] - groups * size, LANES), jnp.float32))
    spare_columns_ref[...] = jnp.concatenate(columns, axis=0).astype(jnp.bfloat16)


def near_score_kernel(groups, share, reach_ref, *refs):
    near_parts, refs = refs[:groups], refs[groups:]
    own_ref, mine_ref, rows_ref, masks_ref, columns_ref, own_rows_ref = refs[:6]
    spare_rows_ref, spare_mask_ref, spare_columns_ref, annot_ref, near_annot_ref = refs[6:11]
    out_ref, send_ref, near_out_ref, flipped, scores = refs[11:]
    snps = annot_ref.shape[0]
    wide = snps // groups
    size = wide // 2
    tiles = snps // LANES
    me = lax.axis_index("hap")
    block = lax.axis_index("snp")
    last = reach_ref.shape[0] - 1
    reach_here = reach_ref[block]
    reach_there = jnp.where(
        me < groups // 2, reach_ref[jnp.minimum(block + 1, last)], reach_ref[jnp.maximum(block - 1, 0)]
    )

    scores[...] = own_ref[...]
    near_sums = sum((part[...] for part in near_parts[1:]), near_parts[0][...])
    near_counts = from_tiles(near_sums[0 : tiles * share, :], share)
    start = tiles * share
    rest = near_sums[start + size : start + size + size // 2, :]
    rest = jnp.concatenate([rest, pltpu.roll(rest, HALF_LANES, 1)], axis=0)
    spare_fields = from_fields(jnp.concatenate([near_sums[start : start + size, :], rest], axis=1))
    extras = from_fields(near_sums[start + size + size // 2 :, :])
    near_stats, near_lines, spare_stats = [], [], []
    for pop in range(2):
        count = extras[pop][0:1, :]
        totals = jnp.concatenate([extras[pop][3:4, :], extras[pop][4:5, :]], axis=1)
        spare_stats.append(column_stats(totals, jnp.concatenate([count, count], axis=1)))
        near_stats.append(column_stats(extras[pop][1:2, :], extras[pop][0:1, :]))
        near_lines += [*near_stats[pop], extras[pop][2:3, :]]
    near_table = jnp.concatenate(near_lines, axis=0).T[0:wide, :]

    slots = [near_counts[:, 0:LANES]]
    for slot in range(1, groups):
        slots.append(pltpu.roll(near_counts, snps - slot * wide, 1)[:, 0:LANES])
    flipped[:, 0:size] = slots[0].T
    slots.append(pltpu.roll(flipped[0:size, :], size, 1))
    near_fields = from_fields(jnp.concatenate(slots, axis=0))
    product = 1.0
    for pop in range(2):
        row_stats = [rows_ref[3 * pop + k] for k in range(3)]
        product *= correlation(row_stats, near_stats[pop], near_fields[pop])
    near_here = jnp.where(masks_ref[0] > 0.0, product, 0.0)
    near_there = jnp.where(masks_ref[1] > 0.0, product, 0.0)
    slice_rows = pl.ds(pl.multiple_of(me * wide, 8), wide)
    direct = dot_rounded(near_here, columns_ref[...], 1)
    turned = pltpu.roll(direct, HALF_LANES, 1)
    for values, places in zip((direct, turned), owner_places(groups, size)):
        for slot, place in enumerate(places):
            scores[pl.ds(pl.multiple_of(place, 8), size), :] += values[slot * size : (slot + 1) * size, :]
    product = 1.0
    for pop in range(2):
        row_stats = [spare_rows_ref[3 * pop + k] for k in range(3)]
        product *= correlation(row_stats, spare_stats[pop], spare_fields[pop])
    spare_here = jnp.where(spare_mask_ref[...] > 0.0, product, 0.0)
    lane = iota(spare_here.shape, 1)
    spare_here = [
        jnp.where((lane >= slot * size) & (lane < (slot + 1) * size), spare_here, 0.0)
        for slot in range(groups)
    ]
    direct = dot_rounded(jnp.concatenate(spare_here, axis=0), spare_columns_ref[...], 1)
    for slot, place in enumerate(spare_places(groups, size)[0]):
        scores[pl.ds(pl.multiple_of(place, 8), size), :] += direct[slot * size : (slot + 1) * size, :]
    near_scores = dot_rounded(near_there, own_rows_ref[...], 0)
    near_scores = jnp.where(
        iota((size, LANES), 1) < HALF_LANES, near_scores[0:size], near_scores[size:wide]
    )

    mine_table = mine_ref[...]
    far_product = 1.0
    for pop in range(2):
        own_row = [mine_table[:, 4 * pop + k : 4 * pop + k + 1] for k in range(3)]
        near_row = [near_table[:, 4 * pop + k : 4 * pop + k + 1] for k in range(4)]
        far_product *= correlation(own_row, near_row, near_row[3])
    scores[slice_rows, :] += near_annot_ref[slice_rows, :] * jnp.where(reach_here >= snps, far_product, 0.0)
    far_scores = annot_ref[slice_rows, :] * jnp.where(reach_there >= snps, far_product, 0.0)
    near_out_ref[...] = (near_scores + pack_halves(far_scores)).astype(near_out_ref.dtype)

    def packed(step):
        group = partner(me, step, groups)
        return pack_halves(scores[pl.ds(pl.multiple_of(group * wide, 8), wide), :])

    out_ref[...] = packed(0)
    send_ref[...] = packed(1)


def column_finish_kernel(*refs):
    *parts, out_ref = refs
    packed = sum(part[...].astype(jnp.float32) for part in parts)
    out_ref[...] = unpack_halves(packed).T[0 : out_ref.shape[0], :]


def sum_kernel(*refs):
    *parts, own_ref, there_ref = refs
    total = sum((part[...].astype(jnp.float32) for part in parts[1:]), parts[0][...])
    own_ref[...] = total
    half = there_ref.shape[0]
    left = iota((half, LANES), 1) < HALF_LANES
    second = total[half:]
    if second.shape[0] < half:
        second = jnp.concatenate([second, jnp.zeros((half - second.shape[0], LANES))], axis=0)
    there_ref[...] = jnp.where(left, pltpu.roll(total[0:half], HALF_LANES, 1), second)


def finish_kernel(own_ref, there_ref, out_ref):
    annots, rows = out_ref.shape
    there = there_ref[...]
    there = jnp.concatenate([there, pltpu.roll(there, HALF_LANES, 1)], axis=0)
    out_ref[...] = (own_ref[...] + there[0:rows]).T[0:annots, :]


def around(value, groups, step):
    return lax.ppermute(
        value, "hap", [(source, partner(source, step, groups)) for source in range(groups)]
    )


def swapped(value, first):
    pairs = []
    for block in range(first, lax.axis_size("snp") - 1, 2):
        pairs += [(block, block + 1), (block + 1, block)]
    return lax.ppermute(value, "snp", pairs)


def per_device(haplotypes, labels, annotations, reach):
    rows, snps = haplotypes.shape
    half = snps // 2
    groups = lax.axis_size("hap")
    blocks = lax.axis_size("snp")
    share = round_up(-(-half // groups), 16)
    folded_rows = share * groups
    out_share = snps // groups
    padded = half + folded_rows
    annot_part = 32
    bf16, f32, i32 = jnp.bfloat16, jnp.float32, jnp.int32
    shape = jax.ShapeDtypeStruct

    packed = shape((rows // 2 + annot_part, snps), bf16)
    haplotypes = pltpu.with_memory_space_constraint(haplotypes, pltpu.HBM)
    annots_in = pltpu.with_memory_space_constraint(annotations, pltpu.HBM)
    alleles, far, close = call(
        prepare_kernel,
        [shape((rows, snps), bf16), packed, packed],
        [HBM, HBM],
        [
            pltpu.VMEM((rows, snps), i32),
            pltpu.VMEM(annotations.shape, i32),
            pltpu.SemaphoreType.DMA((2 * CHUNKS + 1,)),
        ],
        moved=rows * snps * 8,
    )(haplotypes, annots_in)
    from_far = swapped(far, 1)
    from_close = swapped(close, 0)

    by_column = groups == len(LEFT_BLOCKS)
    compact = shape(((share + share // 2) * (snps // LANES) + 8, LANES), i32)
    own_share_counts = compact if by_column else shape((share, snps), i32)
    tile = pltpu.VMEM((snps + 16, snps), f32)
    folded = pltpu.VMEM((folded_rows, snps), i32)
    weighted, totals, *own_parts = call(
        functools.partial(own_kernel, groups, share),
        [shape((snps + 16, rows), bf16), shape((8, snps), f32)] + [own_share_counts] * groups,
        [VMEM, VMEM],
        [tile, pltpu.VMEM((groups * (share + share // 2), snps), i32) if by_column else folded],
        flops=2 * rows * snps * snps,
        moved=rows * snps * 4,
    )(alleles, labels.reshape(1, rows))
    own_parts = [own_parts[0]] + [around(own_parts[k], groups, k) for k in range(groups - 1, 0, -1)]

    near_shapes = [own_share_counts] + [compact if by_column else shape((share + 8, snps), i32)] * groups
    if by_column:
        piece = shape((snps + 16, LANES), f32)
        work = dict(flops=4 * rows * snps * LANES, moved=rows * snps * 4)
        close_counts = call(close_kernel, [piece, piece], [VMEM] * 2, **work)(weighted, from_close)
        own_sum, *near_parts = call(
            functools.partial(far_kernel, groups, share),
            near_shapes,
            [VMEM] * 7,
            [
                tile,
                folded,
                pltpu.VMEM((snps, LANES), f32),
                pltpu.VMEM(((share + 8) * groups, 2 * LANES), i32),
                pltpu.VMEM((8 * groups, LANES), i32),
            ],
            **work,
        )(weighted, from_far, *close_counts, totals, own_parts[0], own_parts[-1])
    else:
        own_sum, *near_parts = call(
            functools.partial(near_kernel, groups, share),
            near_shapes,
            [VMEM] * (4 + groups),
            [pltpu.VMEM((rows, snps), bf16), tile, folded],
            flops=2 * rows * snps * snps,
            moved=rows * snps * 4,
        )(weighted, from_far, from_close, totals, *own_parts)
    order = (2, 3, 1) if by_column else range(groups - 1, 0, -1)
    near_parts = [near_parts[0]] + [around(near_parts[k], groups, k) for k in order]

    by_snp = shape((snps, LANES), f32)
    own_annots, near_annots = call(annots_kernel, [by_snp, by_snp], [VMEM] * 3, moved=1 << 20)(
        annotations, from_far[rows // 2 :], from_close[rows // 2 :]
    )
    pairs = []
    for block in range(blocks):
        for group in range(groups):
            target = block + 1 if group < groups // 2 else block - 1
            if 0 <= target < blocks:
                pairs.append((block * groups + group, target * groups + group))

    def to_neighbour(value):
        return lax.ppermute(value, ("snp", "hap"), pairs)

    result = shape((annotations.shape[0], out_share), f32)
    half_share = round_up(-(-out_share // 2), 8)
    own_share = shape((out_share, LANES), f32)
    packed_share = shape((half_share, LANES), f32)
    if by_column:
        pair_rows = (groups + 1) * (out_share // 2)
        prepared = call(
            functools.partial(own_score_kernel, groups, share),
            [
                by_snp,
                shape((out_share, LANES), f32),
                shape((6, pair_rows, LANES), f32),
                shape((2, pair_rows, LANES), f32),
                shape((LANES, LANES), bf16),
                shape((pair_rows, LANES), bf16),
                shape((6, share, 2 * LANES), f32),
                shape((share, 2 * LANES), f32),
                shape((2 * LANES, LANES), bf16),
            ],
            [SMEM] + [VMEM] * (groups + 1),
            [pltpu.VMEM((snps, LANES), f32)],
            flops=1 << 25,
            moved=1 << 20,
        )(reach, own_sum, *own_parts[1:-1], own_annots, near_annots)
        own_scores, send, there = call(
            functools.partial(near_score_kernel, groups, share),
            [packed_share] * 3,
            [SMEM] + [VMEM] * (groups + 11),
            [pltpu.VMEM((LANES, LANES), i32), pltpu.VMEM((snps, LANES), f32)],
            flops=1 << 26,
            moved=1 << 21,
        )(reach, *near_parts, *prepared, own_annots, near_annots)
        return call(column_finish_kernel, result, [VMEM] * 3)(
            own_scores, around(send, groups, 1), to_neighbour(there)
        )

    tall = pltpu.VMEM((padded, LANES), f32)
    scores = call(
        functools.partial(score_kernel, groups, share),
        [own_share] + [shape((out_share, LANES), bf16)] * (groups - 1),
        [SMEM] + [VMEM] * (groups + 3),
        [tall, tall, tall, tall],
        flops=1 << 26,
        moved=1 << 21,
    )(reach, own_sum, *near_parts, own_annots, near_annots)
    scores = [scores[0]] + [around(scores[k], groups, k) for k in range(groups - 1, 0, -1)]
    own_scores, near_scores = call(sum_kernel, [own_share, packed_share], [VMEM] * groups)(*scores)
    return call(finish_kernel, result, [VMEM] * 2)(own_scores, to_neighbour(near_scores))


def solution(mesh):
    in_specs = (
        P("hap", ("parts", "snp")),
        P(("parts", "hap")),
        P(None, ("parts", "snp")),
        P("parts"),
    )
    out_specs = P(None, ("parts", "snp", "hap"))
    return jax.shard_map(
        per_device, mesh=mesh, in_specs=in_specs, out_specs=out_specs, check_vma=False
    )
```

```python
import functools

import jax
import jax.numpy as jnp
from jax import lax
from jax.experimental import pallas as pl
from jax.experimental.pallas import tpu as pltpu
from jax.sharding import PartitionSpec as P

VARIANCE_FLOOR = 0.01
BASE_BITS = 12
BASE = 1 << BASE_BITS
FIELD_BITS = 16
LANES = 128
HALF_LANES = LANES // 2
CHUNKS = 4
VMEM = pl.BlockSpec(memory_space=pltpu.VMEM)
SMEM = pl.BlockSpec(memory_space=pltpu.SMEM)
HBM = pl.BlockSpec(memory_space=pltpu.HBM)
VMEM_LIMIT = 24 * 1024 * 1024


def iota(shape, axis):
    return lax.broadcasted_iota(jnp.int32, shape, axis)


def round_up(value, step):
    return -(-value // step) * step


def to_fields(values):
    whole = values.astype(jnp.int32)
    return whole + (whole >> BASE_BITS) * ((1 << FIELD_BITS) - BASE)


def from_fields(packed):
    first = packed & ((1 << FIELD_BITS) - 1)
    second = lax.shift_right_logical(packed, FIELD_BITS)
    return first.astype(jnp.float32), second.astype(jnp.float32)


def call(kernel, out_shape, in_specs, scratch_shapes=(), flops=0, moved=0):
    several = isinstance(out_shape, (list, tuple))
    return pl.pallas_call(
        kernel,
        out_shape=out_shape,
        in_specs=in_specs,
        out_specs=[VMEM] * len(out_shape) if several else VMEM,
        scratch_shapes=list(scratch_shapes),
        compiler_params=pltpu.CompilerParams(vmem_limit_bytes=VMEM_LIMIT),
        cost_estimate=pl.CostEstimate(flops=flops, bytes_accessed=moved, transcendentals=0),
    )


def odd_block():
    return lax.rem(lax.axis_index("snp"), 2) == 1


def store_packed(up_ref, down_ref, where, first, second):
    left = iota((first.shape[0], LANES), 1) < HALF_LANES
    middle = first[:, LANES : 2 * LANES]
    turned = pltpu.roll(second[:, LANES : 2 * LANES], HALF_LANES, 1)
    for ref, side, mixed in (
        (up_ref, slice(0, LANES), jnp.where(left, middle, turned)),
        (down_ref, slice(2 * LANES, 3 * LANES), jnp.where(left, turned, middle)),
    ):
        ref[where, 0:LANES] = first[:, side].astype(jnp.bfloat16)
        ref[where, LANES : 2 * LANES] = mixed.astype(jnp.bfloat16)
        ref[where, 2 * LANES : 3 * LANES] = second[:, side].astype(jnp.bfloat16)


def load_packed(up, down):
    left = iota((up.shape[0], LANES), 1) < HALF_LANES
    up_mixed, down_mixed = up[:, LANES : 2 * LANES], down[:, LANES : 2 * LANES]
    first = jnp.where(left, up_mixed, down_mixed)
    second = jnp.where(left, down_mixed, up_mixed)
    second = pltpu.roll(second.astype(jnp.float32), HALF_LANES, 1).astype(second.dtype)
    return (
        (up[:, :LANES], first, down[:, :LANES]),
        (up[:, 2 * LANES :], second, down[:, 2 * LANES :]),
    )


def prepare_kernel(hap_ref, annot_ref, alleles_ref, far_ref, close_ref, held, held_annots, sems):
    rows = hap_ref.shape[0]
    annot_rows = annot_ref.shape[0]
    size = rows // (2 * CHUNKS)
    starts = [side * (rows // 2) + chunk * size for chunk in range(CHUNKS) for side in range(2)]
    copies = [
        pltpu.make_async_copy(
            hap_ref.at[pl.ds(start, size)], held.at[pl.ds(start, size)], sems.at[number]
        )
        for number, start in enumerate(starts)
    ]
    copies.append(pltpu.make_async_copy(annot_ref, held_annots, sems.at[2 * CHUNKS]))
    for copy in copies:
        copy.start()
    part = far_ref.shape[0] - rows // 2
    odd = odd_block()

    def store(where, first, second):
        @pl.when(odd)
        def _():
            store_packed(close_ref, far_ref, where, first, second)

        @pl.when(jnp.logical_not(odd))
        def _():
            store_packed(far_ref, close_ref, where, first, second)

    for chunk in range(CHUNKS):
        pair = []
        for side in range(2):
            number = 2 * chunk + side
            copies[number].wait()
            where = slice(starts[number], starts[number] + size)
            values = held[where, :].astype(jnp.float32)
            alleles_ref[where, :] = values.astype(jnp.bfloat16)
            pair.append(values)
        store(slice(chunk * size, (chunk + 1) * size), *pair)
    copies[-1].wait()
    annots = jnp.concatenate(
        [
            held_annots[...].astype(jnp.float32),
            jnp.zeros((2 * part - annot_rows, annot_ref.shape[1]), jnp.float32),
        ],
        axis=0,
    )
    store(slice(rows // 2, rows // 2 + part), annots[:part], annots[part:])


def partner(group, step, groups):
    if groups & (groups - 1) == 0:
        return group ^ step
    return (group + step) % groups


def send_shares(groups, source, share, targets):
    me = lax.axis_index("hap")
    for step, target in enumerate(targets):
        group = partner(me, step, groups)
        rows = source[pl.ds(pl.multiple_of(group * share, 8), share), :]
        target[0:share, :] = rows.astype(target.dtype)


def send_tiles(groups, source, share, targets):
    me = lax.axis_index("hap")
    for step, target in enumerate(targets):
        owner = partner(me, step, groups)
        counts = source[pl.ds(pl.multiple_of(owner * share, 8), share), :]
        for k in range(source.shape[1] // LANES):
            target[k * share : (k + 1) * share, :] = counts[:, k * LANES : (k + 1) * LANES]


def from_tiles(counts, share):
    tiles = counts.shape[0] // share
    return jnp.concatenate([counts[k * share : (k + 1) * share, :] for k in range(tiles)], axis=1)


def own_kernel(groups, share, alleles_ref, label_ref, *refs):
    weighted_ref, totals_ref, *targets = refs[: 2 + groups]
    tile, folded = refs[2 + groups :]
    rows, snps = alleles_ref.shape
    half = snps // 2
    weight = jnp.where(label_ref[...] > 0, float(BASE), 1.0)
    weighted_ref[0:snps, :] = alleles_ref[...].T * weight.astype(jnp.bfloat16)
    extra = weighted_ref.shape[0] - snps
    weighted_ref[snps:, :] = jnp.broadcast_to(weight, (extra, rows)).astype(jnp.bfloat16)
    tile[...] = jnp.dot(weighted_ref[...], alleles_ref[...], preferred_element_type=jnp.float32)
    count = jnp.sum(weight, axis=1, keepdims=True)
    totals_ref[...] = jnp.concatenate(
        [tile[snps : snps + 1, :], jnp.broadcast_to(count, (1, snps)), jnp.zeros((6, snps))], axis=0
    )
    row, col = iota((half, snps), 0), iota((half, snps), 1)
    moved = (col < half) | (col - half > row)
    turned = pltpu.roll(tile[0:half, :], half, 1)
    folded[0:half, :] = to_fields(jnp.where(moved, turned, tile[half:snps, :]))
    if folded.shape[0] > half:
        folded[half:, :] = jnp.zeros((folded.shape[0] - half, snps), jnp.int32)
    if groups != len(LEFT_BLOCKS):
        send_shares(groups, folded, share, targets)
        return
    tiles = snps // LANES
    shared = [totals_ref[0:1, k * LANES : (k + 1) * LANES] for k in range(tiles)]
    shared += [totals_ref[1:2, 0:LANES], jnp.zeros((7 - tiles, LANES))]
    extras = to_fields(jnp.concatenate(shared, axis=0))
    send_tiles(groups, folded, share, targets)
    for target in targets:
        target[tiles * share :, :] = extras


LEFT_BLOCKS = ((0, 1, 2, 3), (2, 3, 6, 7), (4, 0, 1, 2), (6, 0, 4, 5))
RIGHT_BLOCKS = ((2, 3, 6, 7), (4, 5, 6, 7), (0, 1, 2, 4), (0, 4, 5, 6))


SPARE_OWN = ((0, 0, 0, 0), (1, 1, 2, 2), (4, 5, 6, 7), (6, 6, 7, 7))
SPARE_NEAR = ((4, 5, 6, 7), (4, 5, 4, 5), (3, 3, 3, 3), (1, 2, 1, 2))


def fold_spare(tile, spare):
    owners = len(SPARE_OWN)
    snps = tile.shape[1]
    size = snps // (2 * owners)
    count = spare.shape[0] // owners
    totals = tile[snps : snps + count - size, :]
    lane = iota((count, snps), 1)
    for owner in range(owners):
        mixed = None
        for slot in range(owners):
            own, near = SPARE_OWN[owner][slot], SPARE_NEAR[owner][slot]
            before = (SPARE_OWN[owner][slot - 1], SPARE_NEAR[owner][slot - 1] + 1) if slot else None
            if before == (own, near):
                continue
            values = jnp.concatenate([tile[own * size : (own + 1) * size, :], totals], axis=0)
            shift = (slot - near) * size % snps
            values = pltpu.roll(values, shift, 1) if shift else values
            mixed = values if mixed is None else jnp.where(lane >= slot * size, values, mixed)
        spare[owner * count : (owner + 1) * count, :] = to_fields(mixed[:, 0 : spare.shape[1]])


def fold_by_column(tile, flipped, folded):
    owners = len(LEFT_BLOCKS)
    snps = folded.shape[1]
    wide = snps // owners
    size = wide // 2
    shape = (size, snps)
    row, lane = iota(shape, 0), iota(shape, 1)

    def block(number):
        return tile[number * size : (number + 1) * size, :]

    diagonal = block(0)
    for number in range(1, 2 * owners):
        diagonal = jnp.where(lane >= number * size, block(number), diagonal)
    flipped[:, 0:size] = diagonal.T
    corner = diagonal
    for owner in range(owners):
        start = (2 * owner + 1) * size
        turned = jnp.concatenate(
            [flipped[start : start + size, :], jnp.zeros((size, snps - LANES), jnp.float32)], axis=1
        )
        if owner:
            turned = pltpu.roll(turned, owner * wide, 1)
        inside = lane - owner * wide
        other = (row <= inside) if owner < owners // 2 else (row >= inside)
        corner = jnp.where((inside >= 0) & (inside < size) & other, turned, corner)
    rolled = []
    for shift in range(owners):
        mixed = None
        for owner in range(owners):
            slot = (owner + shift) % owners
            left = block(LEFT_BLOCKS[owner][slot]) if slot else corner
            start = owner * wide
            mixed = left if mixed is None else jnp.where(lane >= start, left, mixed)
            mixed = jnp.where(lane >= start + size, block(RIGHT_BLOCKS[owner][slot]), mixed)
        rolled.append(pltpu.roll(mixed, shift * wide, 1) if shift else mixed)
    for owner in range(owners):
        mixed = rolled[(0 - owner) % owners]
        for slot in range(1, owners):
            mixed = jnp.where(lane >= slot * wide, rolled[(slot - owner) % owners], mixed)
        folded[owner * size : (owner + 1) * size, :] = to_fields(mixed)


def above(far):
    return odd_block() == far


def side_dot(weighted_ref, side_ref):
    rows = weighted_ref.shape[1]
    half = rows // 2

    def dot(which, columns):
        return jnp.dot(
            weighted_ref[:, which], side_ref[0:half, columns], preferred_element_type=jnp.float32
        )

    first = dot(slice(0, half), slice(0, 2 * LANES))
    second = dot(slice(half, rows), slice(LANES, 3 * LANES))
    whole = first[:, 0:LANES] + second[:, LANES:]
    return whole, first[:, LANES:] + pltpu.roll(second[:, 0:LANES], HALF_LANES, 1)


def close_kernel(weighted_ref, side_ref, whole_ref, shared_ref):
    whole_ref[...], shared_ref[...] = side_dot(weighted_ref, side_ref)


def far_kernel(
    groups, share, weighted_ref, side_ref, whole_ref, shared_ref, totals_ref, mine_ref, nearest_ref, own_sum_ref, *refs
):
    targets, (tile, folded, flipped, spare, extras) = refs[:groups], refs[groups:]
    snps = tile.shape[1]
    own_sum_ref[...] = mine_ref[...] + nearest_ref[...]
    whole, shared = side_dot(weighted_ref, side_ref)
    left = iota(shared.shape, 1) < HALF_LANES

    @pl.when(above(True))
    def _():
        tile[:, 0:LANES] = whole
        tile[:, LANES : 2 * LANES] = jnp.where(left, shared, shared_ref[...])
        tile[:, 2 * LANES :] = whole_ref[...]

    @pl.when(jnp.logical_not(above(True)))
    def _():
        tile[:, 0:LANES] = whole_ref[...]
        tile[:, LANES : 2 * LANES] = jnp.where(left, shared_ref[...], shared)
        tile[:, 2 * LANES :] = whole

    fold_by_column(tile, flipped, folded)
    square = (snps, snps)
    apart = jnp.sum(
        jnp.where(iota(square, 0) == iota(square, 1), tile[0:snps, :], 0.0), axis=0, keepdims=True
    )
    fold_spare(tile, spare)
    tiles = snps // LANES
    size = share
    count = spare.shape[0] // groups
    sizes = totals_ref[1:2, :]
    by_column = jnp.concatenate([sizes, tile[snps : snps + 1, :], apart, jnp.zeros((5, snps))], axis=0)
    for owner in range(groups):
        start = owner * (snps // groups)
        columns = pltpu.roll(by_column, snps - start, 1) if owner else by_column
        spare_totals = spare[owner * count + size : owner * count + size + 1, :]
        extras[8 * owner : 8 * (owner + 1), :] = jnp.concatenate(
            [
                to_fields(columns[0:3, 0:LANES]),
                spare_totals[:, 0:LANES],
                spare_totals[:, LANES:],
                jnp.zeros((3, LANES), jnp.int32),
            ],
            axis=0,
        )
    me = lax.axis_index("hap")
    send_tiles(groups, folded, share, targets)
    left = iota((size // 2, LANES), 1) < HALF_LANES
    for step, target in enumerate(targets):
        owner = partner(me, step, groups)
        counts = spare[pl.ds(pl.multiple_of(owner * count, 8), size), :]
        start = tiles * size
        target[start : start + size, :] = counts[:, 0:LANES]
        rest = counts[:, LANES:]
        target[start + size : start + size + size // 2, :] = jnp.where(
            left, rest[0 : size // 2], pltpu.roll(rest[size // 2 :], HALF_LANES, 1)
        )
        target[start + size + size // 2 :, :] = extras[pl.ds(pl.multiple_of(owner * 8, 8), 8), :]


def near_kernel(groups, share, weighted_ref, far_ref, close_ref, totals_ref, *refs):
    own_parts, own_sum_ref = refs[:groups], refs[groups]
    targets, (near, tile, folded) = refs[groups + 1 : 2 * groups + 1], refs[2 * groups + 1 :]
    rows, snps = near.shape
    half = snps // 2
    odd = odd_block()

    def unpack(up_ref, down_ref):
        pieces = load_packed(up_ref[0 : rows // 2, :], down_ref[0 : rows // 2, :])
        for side in range(2):
            where = slice(side * (rows // 2), (side + 1) * (rows // 2))
            for number in range(3):
                near[where, number * LANES : (number + 1) * LANES] = pieces[side][number]

    @pl.when(odd)
    def _():
        unpack(far_ref, close_ref)

    @pl.when(jnp.logical_not(odd))
    def _():
        unpack(close_ref, far_ref)

    tile[...] = jnp.dot(weighted_ref[...], near[...], preferred_element_type=jnp.float32)
    row, col = iota((half, snps), 0), iota((half, snps), 1)
    moved = (col >= half) & (col - half < row)
    turned = pltpu.roll(tile[0:half, :], half, 1)
    folded[0:half, :] = to_fields(jnp.where(moved, turned, tile[half:snps, :]))
    if folded.shape[0] > half:
        folded[half:, :] = jnp.zeros((folded.shape[0] - half, snps), jnp.int32)
    square = (snps, snps)
    far = jnp.sum(
        jnp.where(iota(square, 0) == iota(square, 1), tile[0:snps, :], 0.0), axis=0, keepdims=True
    )
    extras = to_fields(
        jnp.concatenate(
            [totals_ref[0:2, :], tile[snps : snps + 1, :], far, jnp.zeros((4, snps))], axis=0
        )
    )
    send_shares(groups, folded, share, targets)
    for target in targets:
        target[share:, :] = extras
    own_sum_ref[...] = sum((part[...] for part in own_parts[1:]), own_parts[0][...])


def annots_kernel(annot_ref, far_ref, close_ref, own_ref, near_ref):
    snps = annot_ref.shape[1]
    part = far_ref.shape[0]
    wide = 2 * part
    own = annot_ref[...].astype(jnp.float32)
    own = jnp.concatenate([own, jnp.zeros((LANES - own.shape[0], snps), jnp.float32)], axis=0)
    own_ref[...] = own.T
    odd = odd_block()
    far, close = far_ref[...].astype(jnp.float32), close_ref[...].astype(jnp.float32)
    first, second = load_packed(jnp.where(odd, far, close), jnp.where(odd, close, far))
    near = jnp.concatenate(
        [
            jnp.concatenate([piece.astype(jnp.float32) for piece in first], axis=1),
            jnp.concatenate([piece.astype(jnp.float32) for piece in second], axis=1),
            jnp.zeros((LANES - wide, snps), jnp.float32),
        ],
        axis=0,
    )
    near_ref[...] = near.T


def column_stats(totals, count):
    size = jnp.maximum(count, 1.0)
    frequency = totals / size
    variance = jnp.maximum(frequency * (1.0 - frequency), VARIANCE_FLOOR)
    inverse = 1.0 / jnp.sqrt(size * variance)
    low = ((0.0 - frequency) * inverse).astype(jnp.bfloat16).astype(jnp.float32)
    high = ((1.0 - frequency) * inverse).astype(jnp.bfloat16).astype(jnp.float32)
    step = high - low
    root = 1.0 / jnp.sqrt(size)
    return step, step * totals * root, (low * count + step * totals) * root


def correlation(row, col, count):
    return row[0] * col[0] * count - row[1] * col[1] + row[2] * col[2]


def split(values):
    high = values.astype(jnp.bfloat16)
    return high, (values - high.astype(jnp.float32)).astype(jnp.bfloat16)


def dot_split(values, right, axis):
    dims = (((axis,), (0,)), ((), ()))
    return sum(
        lax.dot_general(part, right, dims, preferred_element_type=jnp.float32)
        for part in split(values)
    )


def score_kernel(groups, share, reach_ref, *refs):
    own_sum_ref, near_parts = refs[0], refs[1 : groups + 1]
    annot_ref, near_annot_ref = refs[groups + 1 : groups + 3]
    targets = refs[groups + 3 : 2 * groups + 3]
    table, annots, near_annots, scores = refs[2 * groups + 3 :]
    snps = annot_ref.shape[0]
    half = snps // 2
    out_share = snps // groups
    me = lax.axis_index("hap")
    block = lax.axis_index("snp")
    last = reach_ref.shape[0] - 1
    reach_here = reach_ref[block]
    reach_up = reach_ref[jnp.minimum(block + 1, last)]
    reach_down = reach_ref[jnp.maximum(block - 1, 0)]

    own_counts = own_sum_ref[...]
    near_sums = sum((part[...] for part in near_parts[1:]), near_parts[0][...])
    extras = from_fields(near_sums[share:, :])
    near_counts = near_sums[0:share, :]

    own_stats, near_stats, lines = [], [], []
    for pop in range(2):
        count = extras[pop][1:2, :]
        own_stats.append(column_stats(extras[pop][0:1, :], count))
        near_stats.append(column_stats(extras[pop][2:3, :], count))
        lines += [*own_stats[pop], *near_stats[pop], extras[pop][0:1, :], extras[pop][3:4, :]]
    by_row = jnp.concatenate(lines, axis=0).T
    table[0:snps, 0:16] = by_row
    if table.shape[0] > snps:
        table[snps:, 0:16] = jnp.zeros((table.shape[0] - snps, 16), jnp.float32)
    annots[0:snps, :] = annot_ref[...]
    near_annots[0:snps, :] = near_annot_ref[...]
    if annots.shape[0] > snps:
        annots[snps:, :] = jnp.zeros((annots.shape[0] - snps, LANES), jnp.float32)

    low_rows = pl.multiple_of(me * share, 8)
    high_rows = pl.multiple_of(half + me * share, 8)

    def both(ref):
        return jnp.concatenate([ref[pl.ds(low_rows, share), :], ref[pl.ds(high_rows, share), :]], axis=0)

    here = both(table)
    own_count = jnp.concatenate([pltpu.roll(own_counts, half, 1), own_counts], axis=0)
    near_count = jnp.concatenate([pltpu.roll(near_counts, half, 1), near_counts], axis=0)
    shape = (2 * share, snps)
    local, col = iota(shape, 0), iota(shape, 1)
    low = local < share
    place = jnp.where(low, local, local - share) + me * share
    row = jnp.where(low, place, place + half)
    own_fields, near_fields = from_fields(own_count), from_fields(near_count)
    own_product, near_product = 1.0, 1.0
    for pop in range(2):
        row_stats = [here[:, 8 * pop + k : 8 * pop + k + 1] for k in range(3)]
        own_product *= correlation(row_stats, own_stats[pop], own_fields[pop])
        near_product *= correlation(row_stats, near_stats[pop], near_fields[pop])
    real = place < half
    own_inside = real & ((low & (col > row)) | (~low & (col >= half) & (col < row)))
    own_inside &= jnp.abs(col - row) <= reach_here
    own_kept = jnp.where(own_inside, own_product, 0.0)
    in_upper = col < half
    near_inside = real & ((low & (col < row)) | (~low & (in_upper | (col > row))))
    distance = jnp.where(in_upper, snps + col - row, snps + row - col)
    near_here = jnp.where(near_inside & (distance <= reach_here), near_product, 0.0)
    reach_there = jnp.where(in_upper, reach_up, reach_down)
    near_there = jnp.where(near_inside & (distance <= reach_there), near_product, 0.0)

    rows_here = both(annots)
    rows_there = pltpu.roll(rows_here, HALF_LANES, 1)
    scores[0:snps, :] = dot_split(
        jnp.concatenate([own_kept, near_there], axis=0),
        jnp.concatenate([rows_here, rows_there], axis=0).astype(jnp.bfloat16),
        0,
    )
    direct = dot_split(
        jnp.concatenate([own_kept, near_here], axis=1),
        jnp.concatenate([annot_ref[...], near_annot_ref[...]], axis=0).astype(jnp.bfloat16),
        1,
    )
    scores[pl.ds(low_rows, share), :] += direct[0:share, :]
    scores[pl.ds(high_rows, share), :] += direct[share:, :]

    out_rows = pl.ds(pl.multiple_of(me * out_share, 8), out_share)
    mine = table[out_rows, :]
    self_product, far_product = 1.0, 1.0
    for pop in range(2):
        k = 8 * pop
        own_row = [mine[:, k + s : k + s + 1] for s in range(3)]
        near_row = [mine[:, k + 3 + s : k + 4 + s] for s in range(3)]
        self_product *= correlation(own_row, own_row, mine[:, k + 6 : k + 7])
        far_product *= correlation(own_row, near_row, mine[:, k + 7 : k + 8])
    mine_annots = annots[out_rows, :]
    far_reach = jnp.where(me < groups // 2, reach_up, reach_down)
    scores[out_rows, :] += (
        mine_annots * self_product
        + near_annots[out_rows, :] * jnp.where(reach_here >= snps, far_product, 0.0)
        + pltpu.roll(mine_annots, HALF_LANES, 1) * jnp.where(far_reach >= snps, far_product, 0.0)
    )
    send_shares(groups, scores, out_share, targets)


def pack_halves(values):
    half = values.shape[0] // 2
    left = iota((half, LANES), 1) < HALF_LANES
    return jnp.where(left, values[0:half], pltpu.roll(values[half:], HALF_LANES, 1))


def unpack_halves(packed):
    return jnp.concatenate([packed, pltpu.roll(packed, HALF_LANES, 1)], axis=0)


def dot_rounded(values, right, axis):
    dims = (((axis,), (0,)), ((), ()))
    return lax.dot_general(
        values.astype(jnp.bfloat16), right, dims, preferred_element_type=jnp.float32
    )


def owner_places(groups, size):
    me = lax.axis_index("hap")

    def mine(blocks, slot):
        value = blocks[0][slot]
        for group in range(1, groups):
            value = jnp.where(me == group, blocks[group][slot], value)
        return value * size

    left = [mine(LEFT_BLOCKS, slot) for slot in range(groups)]
    right = [mine(RIGHT_BLOCKS, slot) for slot in range(groups)]
    return left + left[0:1], right + [(2 * me + 1) * size]


def spare_places(groups, size):
    me = lax.axis_index("hap")

    def mine(blocks, slot):
        value = blocks[0][slot]
        for group in range(1, groups):
            value = jnp.where(me == group, blocks[group][slot], value)
        return value * size

    return [[mine(blocks, slot) for slot in range(groups)] for blocks in (SPARE_OWN, SPARE_NEAR)]


def rows_at(ref, places, size):
    return jnp.concatenate([ref[pl.ds(pl.multiple_of(place, 8), size), :] for place in places], axis=0)


def own_score_kernel(
    groups, share, reach_ref, *refs
):
    own_parts, refs = refs[: groups - 1], refs[groups - 1 :]
    annot_ref, near_annot_ref, scores, mine_ref, rows_ref, masks_ref, columns_ref, own_rows_ref, *refs = refs
    spare_rows_ref, spare_mask_ref, spare_columns_ref, *targets, table = refs
    snps = annot_ref.shape[0]
    half = snps // 2
    wide = snps // groups
    tiles = snps // LANES
    me = lax.axis_index("hap")
    reach_here = reach_ref[lax.axis_index("snp")]
    own_sums = sum((part[...] for part in own_parts[1:]), own_parts[0][...])
    own_counts = from_tiles(own_sums[0 : tiles * share, :], share)
    extras = from_fields(own_sums[tiles * share :, :])

    own_stats, lines = [], []
    for pop in range(2):
        count = jnp.concatenate([extras[pop][tiles : tiles + 1, :]] * tiles, axis=1)
        totals = jnp.concatenate([extras[pop][k : k + 1, :] for k in range(tiles)], axis=1)
        own_stats.append(column_stats(totals, count))
        lines += [*own_stats[pop], totals]
    table[:, 0:8] = jnp.concatenate(lines, axis=0).T

    low_rows = pl.multiple_of(me * share, 8)
    high_rows = pl.multiple_of(half + me * share, 8)

    def both(ref):
        return jnp.concatenate([ref[pl.ds(low_rows, share), :], ref[pl.ds(high_rows, share), :]], axis=0)

    here = both(table)
    own_fields = from_fields(
        jnp.concatenate([pltpu.roll(own_counts, half, 1), own_counts], axis=0)
    )
    shape = (2 * share, snps)
    local, col = iota(shape, 0), iota(shape, 1)
    low = local < share
    row = jnp.where(low, local, local + half - share) + me * share
    product = 1.0
    for pop in range(2):
        row_stats = [here[:, 4 * pop + k : 4 * pop + k + 1] for k in range(3)]
        product *= correlation(row_stats, own_stats[pop], own_fields[pop])
    inside = (low & (col > row)) | (~low & (col >= half) & (col < row))
    own_kept = jnp.where(inside & (jnp.abs(col - row) <= reach_here), product, 0.0)
    rows_here = both(annot_ref).astype(jnp.bfloat16)
    scores[...] = dot_rounded(own_kept, rows_here, 0)
    direct = dot_rounded(own_kept, annot_ref[...].astype(jnp.bfloat16), 1)
    scores[pl.ds(low_rows, share), :] += direct[0:share, :]
    scores[pl.ds(high_rows, share), :] += direct[share:, :]

    slice_rows = pl.ds(pl.multiple_of(me * wide, 8), wide)
    mine = table[slice_rows, :]
    mine_ref[...] = mine
    product = 1.0
    for pop in range(2):
        own_row = [mine[:, 4 * pop + k : 4 * pop + k + 1] for k in range(4)]
        product *= correlation(own_row, own_row, own_row[3])
    scores[slice_rows, :] += annot_ref[slice_rows, :] * product
    for step, target in enumerate(targets, 2):
        group = partner(me, step, groups)
        rows = scores[pl.ds(pl.multiple_of(group * wide, 8), wide), :]
        target[...] = pack_halves(rows).astype(target.dtype)

    size = wide // 2
    left_places, right_places = owner_places(groups, size)
    left_table, right_table = rows_at(table, left_places, size), rows_at(table, right_places, size)
    local, lane = iota((size, LANES), 0), iota((size, LANES), 1)
    own_row = jnp.concatenate(
        [local + jnp.where(lane < size, a, b) for a, b in zip(left_places, right_places)], axis=0
    )
    shape = own_row.shape
    lane = iota(shape, 1)
    is_left = lane < size
    for pop in range(2):
        for k in range(3):
            column = slice(4 * pop + k, 4 * pop + k + 1)
            rows_ref[3 * pop + k] = jnp.where(is_left, left_table[:, column], right_table[:, column])
    upper = me < groups // 2
    block = lax.axis_index("snp")
    last = reach_ref.shape[0] - 1
    reach_there = jnp.where(
        upper, reach_ref[jnp.minimum(block + 1, last)], reach_ref[jnp.maximum(block - 1, 0)]
    )
    apart = jnp.abs(own_row - (lane + me * wide))
    ahead = (own_row - (lane + me * wide)) * jnp.where(upper, 1, -1) > 0
    real = ahead & (lane < wide) & ((lane >= size) | (iota(shape, 0) < groups * size))
    inside = (own_row - half) * jnp.where(upper, 1, -1) < jnp.where(upper, 0, 1)
    masks_ref[0] = jnp.where(real & inside & (snps - apart <= reach_here), 1.0, 0.0)
    masks_ref[1] = jnp.where(real & (snps - apart <= reach_there), 1.0, 0.0)
    theirs = near_annot_ref[slice_rows, :]
    columns = [theirs[0:size], pltpu.roll(theirs[size:], HALF_LANES, 1), jnp.zeros((LANES - wide, LANES))]
    columns_ref[...] = jnp.concatenate(columns, axis=0).astype(jnp.bfloat16)
    own_rows = rows_at(annot_ref, left_places, size) + pltpu.roll(
        rows_at(annot_ref, right_places, size), HALF_LANES, 1
    )
    own_rows_ref[...] = own_rows.astype(jnp.bfloat16)

    own_places, near_places = spare_places(groups, size)
    shape = (size, spare_mask_ref.shape[1])
    local, lane = iota(shape, 0), iota(shape, 1)

    def by_slot(values):
        mixed = values[0]
        for slot in range(1, groups):
            mixed = jnp.where(lane >= slot * size, values[slot], mixed)
        return mixed

    tables = [table[pl.ds(pl.multiple_of(place, 8), size), :] for place in own_places]
    for pop in range(2):
        for k in range(3):
            column = slice(4 * pop + k, 4 * pop + k + 1)
            spare_rows_ref[3 * pop + k] = by_slot(
                [jnp.broadcast_to(values[:, column], shape) for values in tables]
            )
    own_row = by_slot([local + place for place in own_places])
    near_col = by_slot([lane + (place - slot * size) for slot, place in enumerate(near_places)])
    close = snps - jnp.abs(own_row - near_col) <= reach_here
    spare_mask_ref[...] = jnp.where(close & (lane < groups * size), 1.0, 0.0)
    columns = [rows_at(near_annot_ref, near_places, size)]
    columns.append(jnp.zeros((shape[1] - groups * size, LANES), jnp.float32))
    spare_columns_ref[...] = jnp.concatenate(columns, axis=0).astype(jnp.bfloat16)


def near_score_kernel(groups, share, reach_ref, *refs):
    near_parts, refs = refs[:groups], refs[groups:]
    own_ref, mine_ref, rows_ref, masks_ref, columns_ref, own_rows_ref = refs[:6]
    spare_rows_ref, spare_mask_ref, spare_columns_ref, annot_ref, near_annot_ref = refs[6:11]
    out_ref, send_ref, near_out_ref, flipped, scores = refs[11:]
    snps = annot_ref.shape[0]
    wide = snps // groups
    size = wide // 2
    tiles = snps // LANES
    me = lax.axis_index("hap")
    block = lax.axis_index("snp")
    last = reach_ref.shape[0] - 1
    reach_here = reach_ref[block]
    reach_there = jnp.where(
        me < groups // 2, reach_ref[jnp.minimum(block + 1, last)], reach_ref[jnp.maximum(block - 1, 0)]
    )

    scores[...] = own_ref[...]
    near_sums = sum((part[...] for part in near_parts[1:]), near_parts[0][...])
    near_counts = from_tiles(near_sums[0 : tiles * share, :], share)
    start = tiles * share
    rest = near_sums[start + size : start + size + size // 2, :]
    rest = jnp.concatenate([rest, pltpu.roll(rest, HALF_LANES, 1)], axis=0)
    spare_fields = from_fields(jnp.concatenate([near_sums[start : start + size, :], rest], axis=1))
    extras = from_fields(near_sums[start + size + size // 2 :, :])
    near_stats, near_lines, spare_stats = [], [], []
    for pop in range(2):
        count = extras[pop][0:1, :]
        totals = jnp.concatenate([extras[pop][3:4, :], extras[pop][4:5, :]], axis=1)
        spare_stats.append(column_stats(totals, jnp.concatenate([count, count], axis=1)))
        near_stats.append(column_stats(extras[pop][1:2, :], extras[pop][0:1, :]))
        near_lines += [*near_stats[pop], extras[pop][2:3, :]]
    near_table = jnp.concatenate(near_lines, axis=0).T[0:wide, :]

    slots = [near_counts[:, 0:LANES]]
    for slot in range(1, groups):
        slots.append(pltpu.roll(near_counts, snps - slot * wide, 1)[:, 0:LANES])
    flipped[:, 0:size] = slots[0].T
    slots.append(pltpu.roll(flipped[0:size, :], size, 1))
    near_fields = from_fields(jnp.concatenate(slots, axis=0))
    product = 1.0
    for pop in range(2):
        row_stats = [rows_ref[3 * pop + k] for k in range(3)]
        product *= correlation(row_stats, near_stats[pop], near_fields[pop])
    near_here = jnp.where(masks_ref[0] > 0.0, product, 0.0)
    near_there = jnp.where(masks_ref[1] > 0.0, product, 0.0)
    slice_rows = pl.ds(pl.multiple_of(me * wide, 8), wide)
    direct = dot_rounded(near_here, columns_ref[...], 1)
    turned = pltpu.roll(direct, HALF_LANES, 1)
    for values, places in zip((direct, turned), owner_places(groups, size)):
        for slot, place in enumerate(places):
            scores[pl.ds(pl.multiple_of(place, 8), size), :] += values[slot * size : (slot + 1) * size, :]
    product = 1.0
    for pop in range(2):
        row_stats = [spare_rows_ref[3 * pop + k] for k in range(3)]
        product *= correlation(row_stats, spare_stats[pop], spare_fields[pop])
    spare_here = jnp.where(spare_mask_ref[...] > 0.0, product, 0.0)
    lane = iota(spare_here.shape, 1)
    spare_here = [
        jnp.where((lane >= slot * size) & (lane < (slot + 1) * size), spare_here, 0.0)
        for slot in range(groups)
    ]
    direct = dot_rounded(jnp.concatenate(spare_here, axis=0), spare_columns_ref[...], 1)
    for slot, place in enumerate(spare_places(groups, size)[0]):
        scores[pl.ds(pl.multiple_of(place, 8), size), :] += direct[slot * size : (slot + 1) * size, :]
    near_scores = dot_rounded(near_there, own_rows_ref[...], 0)
    near_scores = jnp.where(
        iota((size, LANES), 1) < HALF_LANES, near_scores[0:size], near_scores[size:wide]
    )

    mine_table = mine_ref[...]
    far_product = 1.0
    for pop in range(2):
        own_row = [mine_table[:, 4 * pop + k : 4 * pop + k + 1] for k in range(3)]
        near_row = [near_table[:, 4 * pop + k : 4 * pop + k + 1] for k in range(4)]
        far_product *= correlation(own_row, near_row, near_row[3])
    scores[slice_rows, :] += near_annot_ref[slice_rows, :] * jnp.where(reach_here >= snps, far_product, 0.0)
    far_scores = annot_ref[slice_rows, :] * jnp.where(reach_there >= snps, far_product, 0.0)
    near_out_ref[...] = (near_scores + pack_halves(far_scores)).astype(near_out_ref.dtype)

    def packed(step):
        group = partner(me, step, groups)
        return pack_halves(scores[pl.ds(pl.multiple_of(group * wide, 8), wide), :])

    out_ref[...] = packed(0)
    send_ref[...] = packed(1).astype(send_ref.dtype)


def column_finish_kernel(*refs):
    *parts, out_ref = refs
    packed = sum(part[...].astype(jnp.float32) for part in parts)
    out_ref[...] = unpack_halves(packed).T[0 : out_ref.shape[0], :]


def sum_kernel(*refs):
    *parts, own_ref, there_ref = refs
    total = sum((part[...].astype(jnp.float32) for part in parts[1:]), parts[0][...])
    own_ref[...] = total
    half = there_ref.shape[0]
    left = iota((half, LANES), 1) < HALF_LANES
    second = total[half:]
    if second.shape[0] < half:
        second = jnp.concatenate([second, jnp.zeros((half - second.shape[0], LANES))], axis=0)
    there_ref[...] = jnp.where(left, pltpu.roll(total[0:half], HALF_LANES, 1), second)


def finish_kernel(own_ref, there_ref, out_ref):
    annots, rows = out_ref.shape
    there = there_ref[...]
    there = jnp.concatenate([there, pltpu.roll(there, HALF_LANES, 1)], axis=0)
    out_ref[...] = (own_ref[...] + there[0:rows]).T[0:annots, :]


def around(value, groups, step):
    return lax.ppermute(
        value, "hap", [(source, partner(source, step, groups)) for source in range(groups)]
    )


def swapped(value, first):
    pairs = []
    for block in range(first, lax.axis_size("snp") - 1, 2):
        pairs += [(block, block + 1), (block + 1, block)]
    return lax.ppermute(value, "snp", pairs)


def per_device(haplotypes, labels, annotations, reach):
    rows, snps = haplotypes.shape
    half = snps // 2
    groups = lax.axis_size("hap")
    blocks = lax.axis_size("snp")
    share = round_up(-(-half // groups), 16)
    folded_rows = share * groups
    out_share = snps // groups
    padded = half + folded_rows
    annot_part = 32
    bf16, f32, i32 = jnp.bfloat16, jnp.float32, jnp.int32
    shape = jax.ShapeDtypeStruct

    packed = shape((rows // 2 + annot_part, snps), bf16)
    haplotypes = pltpu.with_memory_space_constraint(haplotypes, pltpu.HBM)
    annots_in = pltpu.with_memory_space_constraint(annotations, pltpu.HBM)
    alleles, far, close = call(
        prepare_kernel,
        [shape((rows, snps), bf16), packed, packed],
        [HBM, HBM],
        [
            pltpu.VMEM((rows, snps), i32),
            pltpu.VMEM(annotations.shape, i32),
            pltpu.SemaphoreType.DMA((2 * CHUNKS + 1,)),
        ],
        moved=rows * snps * 8,
    )(haplotypes, annots_in)
    from_far = swapped(far, 1)
    from_close = swapped(close, 0)

    by_column = groups == len(LEFT_BLOCKS)
    compact = shape((share * (snps // LANES) + 8, LANES), i32)
    own_share_counts = compact if by_column else shape((share, snps), i32)
    near_share_counts = shape((compact.shape[0] + share + share // 2, LANES), i32)
    tile = pltpu.VMEM((snps + 16, snps), f32)
    folded = pltpu.VMEM((folded_rows, snps), i32)
    weighted, totals, *own_parts = call(
        functools.partial(own_kernel, groups, share),
        [shape((snps + 16, rows), bf16), shape((8, snps), f32)] + [own_share_counts] * groups,
        [VMEM, VMEM],
        [tile, folded],
        flops=2 * rows * snps * snps,
        moved=rows * snps * 4,
    )(alleles, labels.reshape(1, rows))
    own_parts = [own_parts[0]] + [around(own_parts[k], groups, k) for k in range(groups - 1, 0, -1)]

    near_shapes = [own_share_counts] + [near_share_counts if by_column else shape((share + 8, snps), i32)] * groups
    if by_column:
        piece = shape((snps + 16, LANES), f32)
        work = dict(flops=4 * rows * snps * LANES, moved=rows * snps * 4)
        close_counts = call(close_kernel, [piece, piece], [VMEM] * 2, **work)(weighted, from_close)
        own_sum, *near_parts = call(
            functools.partial(far_kernel, groups, share),
            near_shapes,
            [VMEM] * 7,
            [
                tile,
                folded,
                pltpu.VMEM((snps, LANES), f32),
                pltpu.VMEM(((share + 8) * groups, 2 * LANES), i32),
                pltpu.VMEM((8 * groups, LANES), i32),
            ],
            **work,
        )(weighted, from_far, *close_counts, totals, own_parts[0], own_parts[-1])
    else:
        own_sum, *near_parts = call(
            functools.partial(near_kernel, groups, share),
            near_shapes,
            [VMEM] * (4 + groups),
            [pltpu.VMEM((rows, snps), bf16), tile, folded],
            flops=2 * rows * snps * snps,
            moved=rows * snps * 4,
        )(weighted, from_far, from_close, totals, *own_parts)
    order = (2, 3, 1) if by_column else range(groups - 1, 0, -1)
    near_parts = [near_parts[0]] + [around(near_parts[k], groups, k) for k in order]

    by_snp = shape((snps, LANES), f32)
    own_annots, near_annots = call(annots_kernel, [by_snp, by_snp], [VMEM] * 3, moved=1 << 20)(
        annotations, from_far[rows // 2 :], from_close[rows // 2 :]
    )
    pairs = []
    for block in range(blocks):
        for group in range(groups):
            target = block + 1 if group < groups // 2 else block - 1
            if 0 <= target < blocks:
                pairs.append((block * groups + group, target * groups + group))

    def to_neighbour(value):
        return lax.ppermute(value, ("snp", "hap"), pairs)

    result = shape((annotations.shape[0], out_share), f32)
    half_share = round_up(-(-out_share // 2), 8)
    own_share = shape((out_share, LANES), f32)
    packed_share = shape((half_share, LANES), f32)
    if by_column:
        pair_rows = (groups + 1) * (out_share // 2)
        sent = shape((half_share, LANES), bf16)
        *prepared, second, third = call(
            functools.partial(own_score_kernel, groups, share),
            [
                by_snp,
                shape((out_share, LANES), f32),
                shape((6, pair_rows, LANES), f32),
                shape((2, pair_rows, LANES), f32),
                shape((LANES, LANES), bf16),
                shape((pair_rows, LANES), bf16),
                shape((6, share, 2 * LANES), f32),
                shape((share, 2 * LANES), f32),
                shape((2 * LANES, LANES), bf16),
                packed_share,
                packed_share,
            ],
            [SMEM] + [VMEM] * (groups + 1),
            [pltpu.VMEM((snps, LANES), f32)],
            flops=1 << 33,
            moved=1 << 20,
        )(reach, own_sum, *own_parts[1:-1], own_annots, near_annots)
        parts = [around(second, groups, 2), around(third, groups, 3)]
        own_scores, send, there = call(
            functools.partial(near_score_kernel, groups, share),
            [packed_share, sent, sent],
            [SMEM] + [VMEM] * (groups + 11),
            [pltpu.VMEM((LANES, LANES), i32), pltpu.VMEM((snps, LANES), f32)],
            flops=1 << 26,
            moved=1 << 21,
        )(reach, *near_parts, *prepared, own_annots, near_annots)
        parts += [around(send, groups, 1), to_neighbour(there)]
        return call(column_finish_kernel, result, [VMEM] * 5)(own_scores, *parts)

    tall = pltpu.VMEM((padded, LANES), f32)
    scores = call(
        functools.partial(score_kernel, groups, share),
        [own_share] + [shape((out_share, LANES), bf16)] * (groups - 1),
        [SMEM] + [VMEM] * (groups + 3),
        [tall, tall, tall, tall],
        flops=1 << 26,
        moved=1 << 21,
    )(reach, own_sum, *near_parts, own_annots, near_annots)
    scores = [scores[0]] + [around(scores[k], groups, k) for k in range(groups - 1, 0, -1)]
    own_scores, near_scores = call(sum_kernel, [own_share, packed_share], [VMEM] * groups)(*scores)
    return call(finish_kernel, result, [VMEM] * 2)(own_scores, to_neighbour(near_scores))


def solution(mesh):
    in_specs = (
        P("hap", ("parts", "snp")),
        P(("parts", "hap")),
        P(None, ("parts", "snp")),
        P("parts"),
    )
    out_specs = P(None, ("parts", "snp", "hap"))
    return jax.shard_map(
        per_device, mesh=mesh, in_specs=in_specs, out_specs=out_specs, check_vma=False
    )
```

```python
import functools

import jax
import jax.numpy as jnp
from jax import lax
from jax.experimental import pallas as pl
from jax.experimental.pallas import tpu as pltpu
from jax.sharding import PartitionSpec as P

VARIANCE_FLOOR = 0.01
BASE_BITS = 12
BASE = 1 << BASE_BITS
FIELD_BITS = 16
LANES = 128
HALF_LANES = LANES // 2
CHUNKS = 4
VMEM = pl.BlockSpec(memory_space=pltpu.VMEM)
SMEM = pl.BlockSpec(memory_space=pltpu.SMEM)
HBM = pl.BlockSpec(memory_space=pltpu.HBM)
VMEM_LIMIT = 24 * 1024 * 1024


def iota(shape, axis):
    return lax.broadcasted_iota(jnp.int32, shape, axis)


def round_up(value, step):
    return -(-value // step) * step


def to_fields(values):
    whole = values.astype(jnp.int32)
    return whole + (whole >> BASE_BITS) * ((1 << FIELD_BITS) - BASE)


def from_fields(packed):
    first = packed & ((1 << FIELD_BITS) - 1)
    second = lax.shift_right_logical(packed, FIELD_BITS)
    return first.astype(jnp.float32), second.astype(jnp.float32)


def call(kernel, out_shape, in_specs, scratch_shapes=(), flops=0, moved=0):
    several = isinstance(out_shape, (list, tuple))
    return pl.pallas_call(
        kernel,
        out_shape=out_shape,
        in_specs=in_specs,
        out_specs=[VMEM] * len(out_shape) if several else VMEM,
        scratch_shapes=list(scratch_shapes),
        compiler_params=pltpu.CompilerParams(vmem_limit_bytes=VMEM_LIMIT),
        cost_estimate=pl.CostEstimate(flops=flops, bytes_accessed=moved, transcendentals=0),
    )


def odd_block():
    return lax.rem(lax.axis_index("snp"), 2) == 1


def store_packed(up_ref, down_ref, where, first, second):
    left = iota((first.shape[0], LANES), 1) < HALF_LANES
    middle = first[:, LANES : 2 * LANES]
    turned = pltpu.roll(second[:, LANES : 2 * LANES], HALF_LANES, 1)
    for ref, side, mixed in (
        (up_ref, slice(0, LANES), jnp.where(left, middle, turned)),
        (down_ref, slice(2 * LANES, 3 * LANES), jnp.where(left, turned, middle)),
    ):
        ref[where, 0:LANES] = first[:, side].astype(jnp.bfloat16)
        ref[where, LANES : 2 * LANES] = mixed.astype(jnp.bfloat16)
        ref[where, 2 * LANES : 3 * LANES] = second[:, side].astype(jnp.bfloat16)


def load_packed(up, down):
    left = iota((up.shape[0], LANES), 1) < HALF_LANES
    up_mixed, down_mixed = up[:, LANES : 2 * LANES], down[:, LANES : 2 * LANES]
    first = jnp.where(left, up_mixed, down_mixed)
    second = jnp.where(left, down_mixed, up_mixed)
    second = pltpu.roll(second.astype(jnp.float32), HALF_LANES, 1).astype(second.dtype)
    return (
        (up[:, :LANES], first, down[:, :LANES]),
        (up[:, 2 * LANES :], second, down[:, 2 * LANES :]),
    )


def prepare_kernel(hap_ref, annot_ref, alleles_ref, far_ref, close_ref, held, held_annots, sems):
    rows = hap_ref.shape[0]
    annot_rows = annot_ref.shape[0]
    size = rows // (2 * CHUNKS)
    starts = [side * (rows // 2) + chunk * size for chunk in range(CHUNKS) for side in range(2)]
    copies = [
        pltpu.make_async_copy(
            hap_ref.at[pl.ds(start, size)], held.at[pl.ds(start, size)], sems.at[number]
        )
        for number, start in enumerate(starts)
    ]
    copies.append(pltpu.make_async_copy(annot_ref, held_annots, sems.at[2 * CHUNKS]))
    for copy in copies:
        copy.start()
    part = far_ref.shape[0] - rows // 2
    odd = odd_block()

    def store(where, first, second):
        @pl.when(odd)
        def _():
            store_packed(close_ref, far_ref, where, first, second)

        @pl.when(jnp.logical_not(odd))
        def _():
            store_packed(far_ref, close_ref, where, first, second)

    for chunk in range(CHUNKS):
        pair = []
        for side in range(2):
            number = 2 * chunk + side
            copies[number].wait()
            where = slice(starts[number], starts[number] + size)
            values = held[where, :].astype(jnp.float32)
            alleles_ref[where, :] = values.astype(jnp.bfloat16)
            pair.append(values)
        store(slice(chunk * size, (chunk + 1) * size), *pair)
    copies[-1].wait()
    annots = jnp.concatenate(
        [
            held_annots[...].astype(jnp.float32),
            jnp.zeros((2 * part - annot_rows, annot_ref.shape[1]), jnp.float32),
        ],
        axis=0,
    )
    store(slice(rows // 2, rows // 2 + part), annots[:part], annots[part:])


def partner(group, step, groups):
    if groups & (groups - 1) == 0:
        return group ^ step
    return (group + step) % groups


def send_shares(groups, source, share, targets):
    me = lax.axis_index("hap")
    for step, target in enumerate(targets):
        group = partner(me, step, groups)
        rows = source[pl.ds(pl.multiple_of(group * share, 8), share), :]
        target[0:share, :] = rows.astype(target.dtype)


def send_tiles(groups, source, share, targets):
    me = lax.axis_index("hap")
    for step, target in enumerate(targets):
        owner = partner(me, step, groups)
        counts = source[pl.ds(pl.multiple_of(owner * share, 8), share), :]
        for k in range(source.shape[1] // LANES):
            target[k * share : (k + 1) * share, :] = counts[:, k * LANES : (k + 1) * LANES]


def from_tiles(counts, share):
    tiles = counts.shape[0] // share
    return jnp.concatenate([counts[k * share : (k + 1) * share, :] for k in range(tiles)], axis=1)


def own_kernel(groups, share, alleles_ref, label_ref, *refs):
    weighted_ref, totals_ref, *targets = refs[: 2 + groups]
    tile, folded = refs[2 + groups :]
    rows, snps = alleles_ref.shape
    half = snps // 2
    weight = jnp.where(label_ref[...] > 0, float(BASE), 1.0)
    weighted_ref[0:snps, :] = alleles_ref[...].T * weight.astype(jnp.bfloat16)
    extra = weighted_ref.shape[0] - snps
    weighted_ref[snps:, :] = jnp.broadcast_to(weight, (extra, rows)).astype(jnp.bfloat16)
    tile[...] = jnp.dot(weighted_ref[...], alleles_ref[...], preferred_element_type=jnp.float32)
    count = jnp.sum(weight, axis=1, keepdims=True)
    totals_ref[...] = jnp.concatenate(
        [tile[snps : snps + 1, :], jnp.broadcast_to(count, (1, snps)), jnp.zeros((6, snps))], axis=0
    )
    row, col = iota((half, snps), 0), iota((half, snps), 1)
    moved = (col < half) | (col - half > row)
    turned = pltpu.roll(tile[0:half, :], half, 1)
    folded[0:half, :] = to_fields(jnp.where(moved, turned, tile[half:snps, :]))
    if folded.shape[0] > half:
        folded[half:, :] = jnp.zeros((folded.shape[0] - half, snps), jnp.int32)
    if groups != len(LEFT_BLOCKS):
        send_shares(groups, folded, share, targets)
        return
    tiles = snps // LANES
    shared = [totals_ref[0:1, k * LANES : (k + 1) * LANES] for k in range(tiles)]
    shared += [totals_ref[1:2, 0:LANES], jnp.zeros((7 - tiles, LANES))]
    extras = to_fields(jnp.concatenate(shared, axis=0))
    send_tiles(groups, folded, share, targets)
    for target in targets:
        target[tiles * share :, :] = extras


LEFT_BLOCKS = ((0, 1, 2, 3), (2, 3, 6, 7), (4, 0, 1, 2), (6, 0, 4, 5))
RIGHT_BLOCKS = ((2, 3, 6, 7), (4, 5, 6, 7), (0, 1, 2, 4), (0, 4, 5, 6))


SPARE_OWN = ((0, 0, 0, 0), (1, 1, 2, 2), (4, 5, 6, 7), (6, 6, 7, 7))
SPARE_NEAR = ((4, 5, 6, 7), (4, 5, 4, 5), (3, 3, 3, 3), (1, 2, 1, 2))


def fold_spare(tile, spare):
    owners = len(SPARE_OWN)
    snps = tile.shape[1]
    size = snps // (2 * owners)
    count = spare.shape[0] // owners
    totals = tile[snps : snps + count - size, :]
    lane = iota((count, snps), 1)
    for owner in range(owners):
        mixed = None
        for slot in range(owners):
            own, near = SPARE_OWN[owner][slot], SPARE_NEAR[owner][slot]
            before = (SPARE_OWN[owner][slot - 1], SPARE_NEAR[owner][slot - 1] + 1) if slot else None
            if before == (own, near):
                continue
            values = jnp.concatenate([tile[own * size : (own + 1) * size, :], totals], axis=0)
            shift = (slot - near) * size % snps
            values = pltpu.roll(values, shift, 1) if shift else values
            mixed = values if mixed is None else jnp.where(lane >= slot * size, values, mixed)
        spare[owner * count : (owner + 1) * count, :] = to_fields(mixed[:, 0 : spare.shape[1]])


def fold_by_column(tile, flipped, folded):
    owners = len(LEFT_BLOCKS)
    snps = folded.shape[1]
    wide = snps // owners
    size = wide // 2
    shape = (size, snps)
    row, lane = iota(shape, 0), iota(shape, 1)

    def block(number):
        return tile[number * size : (number + 1) * size, :]

    diagonal = block(0)
    for number in range(1, 2 * owners):
        diagonal = jnp.where(lane >= number * size, block(number), diagonal)
    flipped[:, 0:size] = diagonal.T
    corner = diagonal
    for owner in range(owners):
        start = (2 * owner + 1) * size
        turned = jnp.concatenate(
            [flipped[start : start + size, :], jnp.zeros((size, snps - LANES), jnp.float32)], axis=1
        )
        if owner:
            turned = pltpu.roll(turned, owner * wide, 1)
        inside = lane - owner * wide
        other = (row <= inside) if owner < owners // 2 else (row >= inside)
        corner = jnp.where((inside >= 0) & (inside < size) & other, turned, corner)
    rolled = []
    for shift in range(owners):
        mixed = None
        for owner in range(owners):
            slot = (owner + shift) % owners
            left = block(LEFT_BLOCKS[owner][slot]) if slot else corner
            start = owner * wide
            mixed = left if mixed is None else jnp.where(lane >= start, left, mixed)
            mixed = jnp.where(lane >= start + size, block(RIGHT_BLOCKS[owner][slot]), mixed)
        rolled.append(pltpu.roll(mixed, shift * wide, 1) if shift else mixed)
    for owner in range(owners):
        mixed = rolled[(0 - owner) % owners]
        for slot in range(1, owners):
            mixed = jnp.where(lane >= slot * wide, rolled[(slot - owner) % owners], mixed)
        folded[owner * size : (owner + 1) * size, :] = to_fields(mixed)


def above(far):
    return odd_block() == far


def side_dot(weighted_ref, side_ref):
    rows = weighted_ref.shape[1]
    half = rows // 2

    def dot(which, columns):
        return jnp.dot(
            weighted_ref[:, which], side_ref[0:half, columns], preferred_element_type=jnp.float32
        )

    first = dot(slice(0, half), slice(0, 2 * LANES))
    second = dot(slice(half, rows), slice(LANES, 3 * LANES))
    whole = first[:, 0:LANES] + second[:, LANES:]
    return whole, first[:, LANES:] + pltpu.roll(second[:, 0:LANES], HALF_LANES, 1)


def close_kernel(weighted_ref, side_ref, whole_ref, shared_ref):
    whole_ref[...], shared_ref[...] = side_dot(weighted_ref, side_ref)


def far_kernel(
    groups, share, weighted_ref, side_ref, whole_ref, shared_ref, totals_ref, mine_ref, nearest_ref, own_sum_ref, *refs
):
    targets, (tile, folded, flipped, spare, extras) = refs[:groups], refs[groups:]
    snps = tile.shape[1]
    own_sum_ref[...] = mine_ref[...] + nearest_ref[...]
    whole, shared = side_dot(weighted_ref, side_ref)
    left = iota(shared.shape, 1) < HALF_LANES

    @pl.when(above(True))
    def _():
        tile[:, 0:LANES] = whole
        tile[:, LANES : 2 * LANES] = jnp.where(left, shared, shared_ref[...])
        tile[:, 2 * LANES :] = whole_ref[...]

    @pl.when(jnp.logical_not(above(True)))
    def _():
        tile[:, 0:LANES] = whole_ref[...]
        tile[:, LANES : 2 * LANES] = jnp.where(left, shared_ref[...], shared)
        tile[:, 2 * LANES :] = whole

    fold_by_column(tile, flipped, folded)
    square = (snps, snps)
    apart = jnp.sum(
        jnp.where(iota(square, 0) == iota(square, 1), tile[0:snps, :], 0.0), axis=0, keepdims=True
    )
    fold_spare(tile, spare)
    tiles = snps // LANES
    size = share
    count = spare.shape[0] // groups
    sizes = totals_ref[1:2, :]
    by_column = jnp.concatenate([sizes, tile[snps : snps + 1, :], apart, jnp.zeros((5, snps))], axis=0)
    for owner in range(groups):
        start = owner * (snps // groups)
        columns = pltpu.roll(by_column, snps - start, 1) if owner else by_column
        spare_totals = spare[owner * count + size : owner * count + size + 1, :]
        extras[8 * owner : 8 * (owner + 1), :] = jnp.concatenate(
            [
                to_fields(columns[0:3, 0:LANES]),
                spare_totals[:, 0:LANES],
                spare_totals[:, LANES:],
                jnp.zeros((3, LANES), jnp.int32),
            ],
            axis=0,
        )
    me = lax.axis_index("hap")
    send_tiles(groups, folded, share, targets)
    left = iota((size // 2, LANES), 1) < HALF_LANES
    for step, target in enumerate(targets):
        owner = partner(me, step, groups)
        counts = spare[pl.ds(pl.multiple_of(owner * count, 8), size), :]
        start = tiles * size
        target[start : start + size, :] = counts[:, 0:LANES]
        rest = counts[:, LANES:]
        target[start + size : start + size + size // 2, :] = jnp.where(
            left, rest[0 : size // 2], pltpu.roll(rest[size // 2 :], HALF_LANES, 1)
        )
        target[start + size + size // 2 :, :] = extras[pl.ds(pl.multiple_of(owner * 8, 8), 8), :]


def near_kernel(groups, share, weighted_ref, far_ref, close_ref, totals_ref, *refs):
    own_parts, own_sum_ref = refs[:groups], refs[groups]
    targets, (near, tile, folded) = refs[groups + 1 : 2 * groups + 1], refs[2 * groups + 1 :]
    rows, snps = near.shape
    half = snps // 2
    odd = odd_block()

    def unpack(up_ref, down_ref):
        pieces = load_packed(up_ref[0 : rows // 2, :], down_ref[0 : rows // 2, :])
        for side in range(2):
            where = slice(side * (rows // 2), (side + 1) * (rows // 2))
            for number in range(3):
                near[where, number * LANES : (number + 1) * LANES] = pieces[side][number]

    @pl.when(odd)
    def _():
        unpack(far_ref, close_ref)

    @pl.when(jnp.logical_not(odd))
    def _():
        unpack(close_ref, far_ref)

    tile[...] = jnp.dot(weighted_ref[...], near[...], preferred_element_type=jnp.float32)
    row, col = iota((half, snps), 0), iota((half, snps), 1)
    moved = (col >= half) & (col - half < row)
    turned = pltpu.roll(tile[0:half, :], half, 1)
    folded[0:half, :] = to_fields(jnp.where(moved, turned, tile[half:snps, :]))
    if folded.shape[0] > half:
        folded[half:, :] = jnp.zeros((folded.shape[0] - half, snps), jnp.int32)
    square = (snps, snps)
    far = jnp.sum(
        jnp.where(iota(square, 0) == iota(square, 1), tile[0:snps, :], 0.0), axis=0, keepdims=True
    )
    extras = to_fields(
        jnp.concatenate(
            [totals_ref[0:2, :], tile[snps : snps + 1, :], far, jnp.zeros((4, snps))], axis=0
        )
    )
    send_shares(groups, folded, share, targets)
    for target in targets:
        target[share:, :] = extras
    own_sum_ref[...] = sum((part[...] for part in own_parts[1:]), own_parts[0][...])


def annots_kernel(annot_ref, far_ref, close_ref, own_ref, near_ref):
    snps = annot_ref.shape[1]
    part = far_ref.shape[0]
    wide = 2 * part
    own = annot_ref[...].astype(jnp.float32)
    own = jnp.concatenate([own, jnp.zeros((LANES - own.shape[0], snps), jnp.float32)], axis=0)
    own_ref[...] = own.T
    odd = odd_block()
    far, close = far_ref[...].astype(jnp.float32), close_ref[...].astype(jnp.float32)
    first, second = load_packed(jnp.where(odd, far, close), jnp.where(odd, close, far))
    near = jnp.concatenate(
        [
            jnp.concatenate([piece.astype(jnp.float32) for piece in first], axis=1),
            jnp.concatenate([piece.astype(jnp.float32) for piece in second], axis=1),
            jnp.zeros((LANES - wide, snps), jnp.float32),
        ],
        axis=0,
    )
    near_ref[...] = near.T


def column_stats(totals, count):
    size = jnp.maximum(count, 1.0)
    frequency = totals / size
    variance = jnp.maximum(frequency * (1.0 - frequency), VARIANCE_FLOOR)
    inverse = 1.0 / jnp.sqrt(size * variance)
    low = ((0.0 - frequency) * inverse).astype(jnp.bfloat16).astype(jnp.float32)
    high = ((1.0 - frequency) * inverse).astype(jnp.bfloat16).astype(jnp.float32)
    step = high - low
    root = 1.0 / jnp.sqrt(size)
    return step, step * totals * root, (low * count + step * totals) * root


def correlation(row, col, count):
    return row[0] * col[0] * count - row[1] * col[1] + row[2] * col[2]


def split(values):
    high = values.astype(jnp.bfloat16)
    return high, (values - high.astype(jnp.float32)).astype(jnp.bfloat16)


def dot_split(values, right, axis):
    dims = (((axis,), (0,)), ((), ()))
    return sum(
        lax.dot_general(part, right, dims, preferred_element_type=jnp.float32)
        for part in split(values)
    )


def score_kernel(groups, share, reach_ref, *refs):
    own_sum_ref, near_parts = refs[0], refs[1 : groups + 1]
    annot_ref, near_annot_ref = refs[groups + 1 : groups + 3]
    targets = refs[groups + 3 : 2 * groups + 3]
    table, annots, near_annots, scores = refs[2 * groups + 3 :]
    snps = annot_ref.shape[0]
    half = snps // 2
    out_share = snps // groups
    me = lax.axis_index("hap")
    block = lax.axis_index("snp")
    last = reach_ref.shape[0] - 1
    reach_here = reach_ref[block]
    reach_up = reach_ref[jnp.minimum(block + 1, last)]
    reach_down = reach_ref[jnp.maximum(block - 1, 0)]

    own_counts = own_sum_ref[...]
    near_sums = sum((part[...] for part in near_parts[1:]), near_parts[0][...])
    extras = from_fields(near_sums[share:, :])
    near_counts = near_sums[0:share, :]

    own_stats, near_stats, lines = [], [], []
    for pop in range(2):
        count = extras[pop][1:2, :]
        own_stats.append(column_stats(extras[pop][0:1, :], count))
        near_stats.append(column_stats(extras[pop][2:3, :], count))
        lines += [*own_stats[pop], *near_stats[pop], extras[pop][0:1, :], extras[pop][3:4, :]]
    by_row = jnp.concatenate(lines, axis=0).T
    table[0:snps, 0:16] = by_row
    if table.shape[0] > snps:
        table[snps:, 0:16] = jnp.zeros((table.shape[0] - snps, 16), jnp.float32)
    annots[0:snps, :] = annot_ref[...]
    near_annots[0:snps, :] = near_annot_ref[...]
    if annots.shape[0] > snps:
        annots[snps:, :] = jnp.zeros((annots.shape[0] - snps, LANES), jnp.float32)

    low_rows = pl.multiple_of(me * share, 8)
    high_rows = pl.multiple_of(half + me * share, 8)

    def both(ref):
        return jnp.concatenate([ref[pl.ds(low_rows, share), :], ref[pl.ds(high_rows, share), :]], axis=0)

    here = both(table)
    own_count = jnp.concatenate([pltpu.roll(own_counts, half, 1), own_counts], axis=0)
    near_count = jnp.concatenate([pltpu.roll(near_counts, half, 1), near_counts], axis=0)
    shape = (2 * share, snps)
    local, col = iota(shape, 0), iota(shape, 1)
    low = local < share
    place = jnp.where(low, local, local - share) + me * share
    row = jnp.where(low, place, place + half)
    own_fields, near_fields = from_fields(own_count), from_fields(near_count)
    own_product, near_product = 1.0, 1.0
    for pop in range(2):
        row_stats = [here[:, 8 * pop + k : 8 * pop + k + 1] for k in range(3)]
        own_product *= correlation(row_stats, own_stats[pop], own_fields[pop])
        near_product *= correlation(row_stats, near_stats[pop], near_fields[pop])
    real = place < half
    own_inside = real & ((low & (col > row)) | (~low & (col >= half) & (col < row)))
    own_inside &= jnp.abs(col - row) <= reach_here
    own_kept = jnp.where(own_inside, own_product, 0.0)
    in_upper = col < half
    near_inside = real & ((low & (col < row)) | (~low & (in_upper | (col > row))))
    distance = jnp.where(in_upper, snps + col - row, snps + row - col)
    near_here = jnp.where(near_inside & (distance <= reach_here), near_product, 0.0)
    reach_there = jnp.where(in_upper, reach_up, reach_down)
    near_there = jnp.where(near_inside & (distance <= reach_there), near_product, 0.0)

    rows_here = both(annots)
    rows_there = pltpu.roll(rows_here, HALF_LANES, 1)
    scores[0:snps, :] = dot_split(
        jnp.concatenate([own_kept, near_there], axis=0),
        jnp.concatenate([rows_here, rows_there], axis=0).astype(jnp.bfloat16),
        0,
    )
    direct = dot_split(
        jnp.concatenate([own_kept, near_here], axis=1),
        jnp.concatenate([annot_ref[...], near_annot_ref[...]], axis=0).astype(jnp.bfloat16),
        1,
    )
    scores[pl.ds(low_rows, share), :] += direct[0:share, :]
    scores[pl.ds(high_rows, share), :] += direct[share:, :]

    out_rows = pl.ds(pl.multiple_of(me * out_share, 8), out_share)
    mine = table[out_rows, :]
    self_product, far_product = 1.0, 1.0
    for pop in range(2):
        k = 8 * pop
        own_row = [mine[:, k + s : k + s + 1] for s in range(3)]
        near_row = [mine[:, k + 3 + s : k + 4 + s] for s in range(3)]
        self_product *= correlation(own_row, own_row, mine[:, k + 6 : k + 7])
        far_product *= correlation(own_row, near_row, mine[:, k + 7 : k + 8])
    mine_annots = annots[out_rows, :]
    far_reach = jnp.where(me < groups // 2, reach_up, reach_down)
    scores[out_rows, :] += (
        mine_annots * self_product
        + near_annots[out_rows, :] * jnp.where(reach_here >= snps, far_product, 0.0)
        + pltpu.roll(mine_annots, HALF_LANES, 1) * jnp.where(far_reach >= snps, far_product, 0.0)
    )
    send_shares(groups, scores, out_share, targets)


def pack_halves(values):
    half = values.shape[0] // 2
    left = iota((half, LANES), 1) < HALF_LANES
    return jnp.where(left, values[0:half], pltpu.roll(values[half:], HALF_LANES, 1))


def unpack_halves(packed):
    return jnp.concatenate([packed, pltpu.roll(packed, HALF_LANES, 1)], axis=0)


def dot_rounded(values, right, axis):
    dims = (((axis,), (0,)), ((), ()))
    return lax.dot_general(
        values.astype(jnp.bfloat16), right, dims, preferred_element_type=jnp.float32
    )


def owner_places(groups, size):
    me = lax.axis_index("hap")

    def mine(blocks, slot):
        value = blocks[0][slot]
        for group in range(1, groups):
            value = jnp.where(me == group, blocks[group][slot], value)
        return value * size

    left = [mine(LEFT_BLOCKS, slot) for slot in range(groups)]
    right = [mine(RIGHT_BLOCKS, slot) for slot in range(groups)]
    return left + left[0:1], right + [(2 * me + 1) * size]


def spare_places(groups, size):
    me = lax.axis_index("hap")

    def mine(blocks, slot):
        value = blocks[0][slot]
        for group in range(1, groups):
            value = jnp.where(me == group, blocks[group][slot], value)
        return value * size

    return [[mine(blocks, slot) for slot in range(groups)] for blocks in (SPARE_OWN, SPARE_NEAR)]


def rows_at(ref, places, size):
    return jnp.concatenate([ref[pl.ds(pl.multiple_of(place, 8), size), :] for place in places], axis=0)


def own_score_kernel(
    groups, share, reach_ref, *refs
):
    own_parts, refs = refs[: groups - 1], refs[groups - 1 :]
    annot_ref, near_annot_ref, scores, mine_ref, rows_ref, masks_ref, columns_ref, own_rows_ref, *refs = refs
    spare_rows_ref, spare_mask_ref, spare_columns_ref, *targets, table = refs
    snps = annot_ref.shape[0]
    half = snps // 2
    wide = snps // groups
    tiles = snps // LANES
    me = lax.axis_index("hap")
    reach_here = reach_ref[lax.axis_index("snp")]
    own_sums = sum((part[...] for part in own_parts[1:]), own_parts[0][...])
    own_counts = from_tiles(own_sums[0 : tiles * share, :], share)
    extras = from_fields(own_sums[tiles * share :, :])

    own_stats, lines = [], []
    for pop in range(2):
        count = jnp.concatenate([extras[pop][tiles : tiles + 1, :]] * tiles, axis=1)
        totals = jnp.concatenate([extras[pop][k : k + 1, :] for k in range(tiles)], axis=1)
        own_stats.append(column_stats(totals, count))
        lines += [*own_stats[pop], totals]
    table[:, 0:8] = jnp.concatenate(lines, axis=0).T

    low_rows = pl.multiple_of(me * share, 8)
    high_rows = pl.multiple_of(half + me * share, 8)

    def both(ref):
        return jnp.concatenate([ref[pl.ds(low_rows, share), :], ref[pl.ds(high_rows, share), :]], axis=0)

    here = both(table)
    own_fields = from_fields(
        jnp.concatenate([pltpu.roll(own_counts, half, 1), own_counts], axis=0)
    )
    shape = (2 * share, snps)
    local, col = iota(shape, 0), iota(shape, 1)
    low = local < share
    row = jnp.where(low, local, local + half - share) + me * share
    product = 1.0
    for pop in range(2):
        row_stats = [here[:, 4 * pop + k : 4 * pop + k + 1] for k in range(3)]
        product *= correlation(row_stats, own_stats[pop], own_fields[pop])
    inside = (low & (col > row)) | (~low & (col >= half) & (col < row))
    own_kept = jnp.where(inside & (jnp.abs(col - row) <= reach_here), product, 0.0)
    rows_here = both(annot_ref).astype(jnp.bfloat16)
    scores[...] = dot_rounded(own_kept, rows_here, 0)
    direct = dot_rounded(own_kept, annot_ref[...].astype(jnp.bfloat16), 1)
    scores[pl.ds(low_rows, share), :] += direct[0:share, :]
    scores[pl.ds(high_rows, share), :] += direct[share:, :]

    slice_rows = pl.ds(pl.multiple_of(me * wide, 8), wide)
    mine = table[slice_rows, :]
    mine_ref[...] = mine
    product = 1.0
    for pop in range(2):
        own_row = [mine[:, 4 * pop + k : 4 * pop + k + 1] for k in range(4)]
        product *= correlation(own_row, own_row, own_row[3])
    scores[slice_rows, :] += annot_ref[slice_rows, :] * product
    for step, target in enumerate(targets, 2):
        group = partner(me, step, groups)
        rows = scores[pl.ds(pl.multiple_of(group * wide, 8), wide), :]
        target[...] = pack_halves(rows).astype(target.dtype)

    size = wide // 2
    left_places, right_places = owner_places(groups, size)
    left_table, right_table = rows_at(table, left_places, size), rows_at(table, right_places, size)
    local, lane = iota((size, LANES), 0), iota((size, LANES), 1)
    own_row = jnp.concatenate(
        [local + jnp.where(lane < size, a, b) for a, b in zip(left_places, right_places)], axis=0
    )
    shape = own_row.shape
    lane = iota(shape, 1)
    is_left = lane < size
    for pop in range(2):
        for k in range(3):
            column = slice(4 * pop + k, 4 * pop + k + 1)
            rows_ref[3 * pop + k] = jnp.where(is_left, left_table[:, column], right_table[:, column])
    upper = me < groups // 2
    block = lax.axis_index("snp")
    last = reach_ref.shape[0] - 1
    reach_there = jnp.where(
        upper, reach_ref[jnp.minimum(block + 1, last)], reach_ref[jnp.maximum(block - 1, 0)]
    )
    apart = jnp.abs(own_row - (lane + me * wide))
    ahead = (own_row - (lane + me * wide)) * jnp.where(upper, 1, -1) > 0
    real = ahead & (lane < wide) & ((lane >= size) | (iota(shape, 0) < groups * size))
    inside = (own_row - half) * jnp.where(upper, 1, -1) < jnp.where(upper, 0, 1)
    masks_ref[0] = jnp.where(real & inside & (snps - apart <= reach_here), 1.0, 0.0)
    masks_ref[1] = jnp.where(real & (snps - apart <= reach_there), 1.0, 0.0)
    theirs = near_annot_ref[slice_rows, :]
    columns = [theirs[0:size], pltpu.roll(theirs[size:], HALF_LANES, 1), jnp.zeros((LANES - wide, LANES))]
    columns_ref[...] = jnp.concatenate(columns, axis=0).astype(jnp.bfloat16)
    own_rows = rows_at(annot_ref, left_places, size) + pltpu.roll(
        rows_at(annot_ref, right_places, size), HALF_LANES, 1
    )
    own_rows_ref[...] = own_rows.astype(jnp.bfloat16)

    own_places, near_places = spare_places(groups, size)
    shape = (size, spare_mask_ref.shape[1])
    local, lane = iota(shape, 0), iota(shape, 1)

    def by_slot(values):
        mixed = values[0]
        for slot in range(1, groups):
            mixed = jnp.where(lane >= slot * size, values[slot], mixed)
        return mixed

    tables = [table[pl.ds(pl.multiple_of(place, 8), size), :] for place in own_places]
    for pop in range(2):
        for k in range(3):
            column = slice(4 * pop + k, 4 * pop + k + 1)
            spare_rows_ref[3 * pop + k] = by_slot(
                [jnp.broadcast_to(values[:, column], shape) for values in tables]
            )
    own_row = by_slot([local + place for place in own_places])
    near_col = by_slot([lane + (place - slot * size) for slot, place in enumerate(near_places)])
    close = snps - jnp.abs(own_row - near_col) <= reach_here
    spare_mask_ref[...] = jnp.where(close & (lane < groups * size), 1.0, 0.0)
    columns = [rows_at(near_annot_ref, near_places, size)]
    columns.append(jnp.zeros((shape[1] - groups * size, LANES), jnp.float32))
    spare_columns_ref[...] = jnp.concatenate(columns, axis=0).astype(jnp.bfloat16)


def near_score_kernel(groups, share, reach_ref, *refs):
    near_parts, refs = refs[:groups], refs[groups:]
    own_ref, mine_ref, rows_ref, masks_ref, columns_ref, own_rows_ref = refs[:6]
    spare_rows_ref, spare_mask_ref, spare_columns_ref, annot_ref, near_annot_ref = refs[6:11]
    out_ref, send_ref, near_out_ref, flipped, scores = refs[11:]
    snps = annot_ref.shape[0]
    wide = snps // groups
    size = wide // 2
    tiles = snps // LANES
    me = lax.axis_index("hap")
    block = lax.axis_index("snp")
    last = reach_ref.shape[0] - 1
    reach_here = reach_ref[block]
    reach_there = jnp.where(
        me < groups // 2, reach_ref[jnp.minimum(block + 1, last)], reach_ref[jnp.maximum(block - 1, 0)]
    )

    scores[...] = own_ref[...]
    near_sums = sum((part[...] for part in near_parts[1:]), near_parts[0][...])
    near_counts = from_tiles(near_sums[0 : tiles * share, :], share)
    start = tiles * share
    rest = near_sums[start + size : start + size + size // 2, :]
    rest = jnp.concatenate([rest, pltpu.roll(rest, HALF_LANES, 1)], axis=0)
    spare_fields = from_fields(jnp.concatenate([near_sums[start : start + size, :], rest], axis=1))
    extras = from_fields(near_sums[start + size + size // 2 :, :])
    near_stats, near_lines, spare_stats = [], [], []
    for pop in range(2):
        count = extras[pop][0:1, :]
        totals = jnp.concatenate([extras[pop][3:4, :], extras[pop][4:5, :]], axis=1)
        spare_stats.append(column_stats(totals, jnp.concatenate([count, count], axis=1)))
        near_stats.append(column_stats(extras[pop][1:2, :], extras[pop][0:1, :]))
        near_lines += [*near_stats[pop], extras[pop][2:3, :]]
    near_table = jnp.concatenate(near_lines, axis=0).T[0:wide, :]

    slots = [near_counts[:, 0:LANES]]
    for slot in range(1, groups):
        slots.append(pltpu.roll(near_counts, snps - slot * wide, 1)[:, 0:LANES])
    flipped[:, 0:size] = slots[0].T
    slots.append(pltpu.roll(flipped[0:size, :], size, 1))
    near_fields = from_fields(jnp.concatenate(slots, axis=0))
    product = 1.0
    for pop in range(2):
        row_stats = [rows_ref[3 * pop + k] for k in range(3)]
        product *= correlation(row_stats, near_stats[pop], near_fields[pop])
    near_here = jnp.where(masks_ref[0] > 0.0, product, 0.0)
    near_there = jnp.where(masks_ref[1] > 0.0, product, 0.0)
    slice_rows = pl.ds(pl.multiple_of(me * wide, 8), wide)
    direct = dot_rounded(near_here, columns_ref[...], 1)
    turned = pltpu.roll(direct, HALF_LANES, 1)
    for values, places in zip((direct, turned), owner_places(groups, size)):
        for slot, place in enumerate(places):
            scores[pl.ds(pl.multiple_of(place, 8), size), :] += values[slot * size : (slot + 1) * size, :]
    product = 1.0
    for pop in range(2):
        row_stats = [spare_rows_ref[3 * pop + k] for k in range(3)]
        product *= correlation(row_stats, spare_stats[pop], spare_fields[pop])
    spare_here = jnp.where(spare_mask_ref[...] > 0.0, product, 0.0)
    lane = iota(spare_here.shape, 1)
    spare_here = [
        jnp.where((lane >= slot * size) & (lane < (slot + 1) * size), spare_here, 0.0)
        for slot in range(groups)
    ]
    direct = dot_rounded(jnp.concatenate(spare_here, axis=0), spare_columns_ref[...], 1)
    for slot, place in enumerate(spare_places(groups, size)[0]):
        scores[pl.ds(pl.multiple_of(place, 8), size), :] += direct[slot * size : (slot + 1) * size, :]
    near_scores = dot_rounded(near_there, own_rows_ref[...], 0)
    near_scores = jnp.where(
        iota((size, LANES), 1) < HALF_LANES, near_scores[0:size], near_scores[size:wide]
    )

    mine_table = mine_ref[...]
    far_product = 1.0
    for pop in range(2):
        own_row = [mine_table[:, 4 * pop + k : 4 * pop + k + 1] for k in range(3)]
        near_row = [near_table[:, 4 * pop + k : 4 * pop + k + 1] for k in range(4)]
        far_product *= correlation(own_row, near_row, near_row[3])
    scores[slice_rows, :] += near_annot_ref[slice_rows, :] * jnp.where(reach_here >= snps, far_product, 0.0)
    far_scores = annot_ref[slice_rows, :] * jnp.where(reach_there >= snps, far_product, 0.0)
    near_out_ref[...] = (near_scores + pack_halves(far_scores)).astype(near_out_ref.dtype)

    def packed(step):
        group = partner(me, step, groups)
        return pack_halves(scores[pl.ds(pl.multiple_of(group * wide, 8), wide), :])

    out_ref[...] = packed(0)
    send_ref[...] = packed(1).astype(send_ref.dtype)


def column_finish_kernel(*refs):
    *parts, out_ref = refs
    packed = sum(part[...].astype(jnp.float32) for part in parts)
    out_ref[...] = unpack_halves(packed).T[0 : out_ref.shape[0], :]


def sum_kernel(*refs):
    *parts, own_ref, there_ref = refs
    total = sum((part[...].astype(jnp.float32) for part in parts[1:]), parts[0][...])
    own_ref[...] = total
    half = there_ref.shape[0]
    left = iota((half, LANES), 1) < HALF_LANES
    second = total[half:]
    if second.shape[0] < half:
        second = jnp.concatenate([second, jnp.zeros((half - second.shape[0], LANES))], axis=0)
    there_ref[...] = jnp.where(left, pltpu.roll(total[0:half], HALF_LANES, 1), second)


def finish_kernel(own_ref, there_ref, out_ref):
    annots, rows = out_ref.shape
    there = there_ref[...]
    there = jnp.concatenate([there, pltpu.roll(there, HALF_LANES, 1)], axis=0)
    out_ref[...] = (own_ref[...] + there[0:rows]).T[0:annots, :]


def around(value, groups, step):
    return lax.ppermute(
        value, "hap", [(source, partner(source, step, groups)) for source in range(groups)]
    )


def swapped(value, first):
    pairs = []
    for block in range(first, lax.axis_size("snp") - 1, 2):
        pairs += [(block, block + 1), (block + 1, block)]
    return lax.ppermute(value, "snp", pairs)


def per_device(haplotypes, labels, annotations, reach):
    rows, snps = haplotypes.shape
    half = snps // 2
    groups = lax.axis_size("hap")
    blocks = lax.axis_size("snp")
    share = round_up(-(-half // groups), 16)
    folded_rows = share * groups
    out_share = snps // groups
    padded = half + folded_rows
    annot_part = 32
    bf16, f32, i32 = jnp.bfloat16, jnp.float32, jnp.int32
    shape = jax.ShapeDtypeStruct

    packed = shape((rows // 2 + annot_part, snps), bf16)
    haplotypes = pltpu.with_memory_space_constraint(haplotypes, pltpu.HBM)
    annots_in = pltpu.with_memory_space_constraint(annotations, pltpu.HBM)
    alleles, far, close = call(
        prepare_kernel,
        [shape((rows, snps), bf16), packed, packed],
        [HBM, HBM],
        [
            pltpu.VMEM((rows, snps), i32),
            pltpu.VMEM(annotations.shape, i32),
            pltpu.SemaphoreType.DMA((2 * CHUNKS + 1,)),
        ],
        moved=rows * snps * 8,
    )(haplotypes, annots_in)
    from_far = swapped(far, 1)
    from_close = swapped(close, 0)

    by_column = groups == len(LEFT_BLOCKS)
    compact = shape((share * (snps // LANES) + 8, LANES), i32)
    own_share_counts = compact if by_column else shape((share, snps), i32)
    near_share_counts = shape((compact.shape[0] + share + share // 2, LANES), i32)
    tile = pltpu.VMEM((snps + 16, snps), f32)
    folded = pltpu.VMEM((folded_rows, snps), i32)
    weighted, totals, *own_parts = call(
        functools.partial(own_kernel, groups, share),
        [shape((snps + 16, rows), bf16), shape((8, snps), f32)] + [own_share_counts] * groups,
        [VMEM, VMEM],
        [tile, folded],
        flops=2 * rows * snps * snps,
        moved=rows * snps * 4,
    )(alleles, labels.reshape(1, rows))
    own_parts = [own_parts[0]] + [around(own_parts[k], groups, k) for k in range(groups - 1, 0, -1)]

    near_shapes = [own_share_counts] + [near_share_counts if by_column else shape((share + 8, snps), i32)] * groups
    if by_column:
        piece = shape((snps + 16, LANES), f32)
        work = dict(flops=4 * rows * snps * LANES, moved=rows * snps * 4)
        close_counts = call(close_kernel, [piece, piece], [VMEM] * 2, **work)(weighted, from_close)
        own_sum, *near_parts = call(
            functools.partial(far_kernel, groups, share),
            near_shapes,
            [VMEM] * 7,
            [
                tile,
                folded,
                pltpu.VMEM((snps, LANES), f32),
                pltpu.VMEM(((share + 8) * groups, 2 * LANES), i32),
                pltpu.VMEM((8 * groups, LANES), i32),
            ],
            **work,
        )(weighted, from_far, *close_counts, totals, own_parts[0], own_parts[-1])
    else:
        own_sum, *near_parts = call(
            functools.partial(near_kernel, groups, share),
            near_shapes,
            [VMEM] * (4 + groups),
            [pltpu.VMEM((rows, snps), bf16), tile, folded],
            flops=2 * rows * snps * snps,
            moved=rows * snps * 4,
        )(weighted, from_far, from_close, totals, *own_parts)
    order = (2, 3, 1) if by_column else range(groups - 1, 0, -1)
    near_parts = [near_parts[0]] + [around(near_parts[k], groups, k) for k in order]

    by_snp = shape((snps, LANES), f32)
    own_annots, near_annots = call(annots_kernel, [by_snp, by_snp], [VMEM] * 3, moved=1 << 20)(
        annotations, from_far[rows // 2 :], from_close[rows // 2 :]
    )
    pairs = []
    for block in range(blocks):
        for group in range(groups):
            target = block + 1 if group < groups // 2 else block - 1
            if 0 <= target < blocks:
                pairs.append((block * groups + group, target * groups + group))

    def to_neighbour(value):
        return lax.ppermute(value, ("snp", "hap"), pairs)

    result = shape((annotations.shape[0], out_share), f32)
    half_share = round_up(-(-out_share // 2), 8)
    own_share = shape((out_share, LANES), f32)
    packed_share = shape((half_share, LANES), f32)
    if by_column:
        pair_rows = (groups + 1) * (out_share // 2)
        sent = shape((half_share, LANES), bf16)
        *prepared, second, third = call(
            functools.partial(own_score_kernel, groups, share),
            [
                by_snp,
                shape((out_share, LANES), f32),
                shape((6, pair_rows, LANES), f32),
                shape((2, pair_rows, LANES), f32),
                shape((LANES, LANES), bf16),
                shape((pair_rows, LANES), bf16),
                shape((6, share, 2 * LANES), f32),
                shape((share, 2 * LANES), f32),
                shape((2 * LANES, LANES), bf16),
                packed_share,
                packed_share,
            ],
            [SMEM] + [VMEM] * (groups + 1),
            [pltpu.VMEM((snps, LANES), f32)],
            flops=1 << 33,
            moved=1 << 20,
        )(reach, own_sum, *own_parts[1:-1], own_annots, near_annots)
        parts = [around(third, groups, 3), around(second, groups, 2)]
        own_scores, send, there = call(
            functools.partial(near_score_kernel, groups, share),
            [packed_share, sent, sent],
            [SMEM] + [VMEM] * (groups + 11),
            [pltpu.VMEM((LANES, LANES), i32), pltpu.VMEM((snps, LANES), f32)],
            flops=1 << 26,
            moved=1 << 21,
        )(reach, *near_parts, *prepared, own_annots, near_annots)
        parts += [around(send, groups, 1), to_neighbour(there)]
        return call(column_finish_kernel, result, [VMEM] * 5)(own_scores, *parts)

    tall = pltpu.VMEM((padded, LANES), f32)
    scores = call(
        functools.partial(score_kernel, groups, share),
        [own_share] + [shape((out_share, LANES), bf16)] * (groups - 1),
        [SMEM] + [VMEM] * (groups + 3),
        [tall, tall, tall, tall],
        flops=1 << 26,
        moved=1 << 21,
    )(reach, own_sum, *near_parts, own_annots, near_annots)
    scores = [scores[0]] + [around(scores[k], groups, k) for k in range(groups - 1, 0, -1)]
    own_scores, near_scores = call(sum_kernel, [own_share, packed_share], [VMEM] * groups)(*scores)
    return call(finish_kernel, result, [VMEM] * 2)(own_scores, to_neighbour(near_scores))


def solution(mesh):
    in_specs = (
        P("hap", ("parts", "snp")),
        P(("parts", "hap")),
        P(None, ("parts", "snp")),
        P("parts"),
    )
    out_specs = P(None, ("parts", "snp", "hap"))
    return jax.shard_map(
        per_device, mesh=mesh, in_specs=in_specs, out_specs=out_specs, check_vma=False
    )
```

```python
import functools

import jax
import jax.numpy as jnp
from jax import lax
from jax.experimental import pallas as pl
from jax.experimental.pallas import tpu as pltpu
from jax.sharding import PartitionSpec as P

VARIANCE_FLOOR = 0.01
BASE_BITS = 12
BASE = 1 << BASE_BITS
FIELD_BITS = 16
LANES = 128
HALF_LANES = LANES // 2
CHUNKS = 4
VMEM = pl.BlockSpec(memory_space=pltpu.VMEM)
SMEM = pl.BlockSpec(memory_space=pltpu.SMEM)
HBM = pl.BlockSpec(memory_space=pltpu.HBM)
VMEM_LIMIT = 24 * 1024 * 1024


def iota(shape, axis):
    return lax.broadcasted_iota(jnp.int32, shape, axis)


def round_up(value, step):
    return -(-value // step) * step


def to_fields(values):
    whole = values.astype(jnp.int32)
    return whole + (whole >> BASE_BITS) * ((1 << FIELD_BITS) - BASE)


def from_fields(packed):
    first = packed & ((1 << FIELD_BITS) - 1)
    second = lax.shift_right_logical(packed, FIELD_BITS)
    return first.astype(jnp.float32), second.astype(jnp.float32)


def call(kernel, out_shape, in_specs, scratch_shapes=(), flops=0, moved=0):
    several = isinstance(out_shape, (list, tuple))
    return pl.pallas_call(
        kernel,
        out_shape=out_shape,
        in_specs=in_specs,
        out_specs=[VMEM] * len(out_shape) if several else VMEM,
        scratch_shapes=list(scratch_shapes),
        compiler_params=pltpu.CompilerParams(vmem_limit_bytes=VMEM_LIMIT),
        cost_estimate=pl.CostEstimate(flops=flops, bytes_accessed=moved, transcendentals=0),
    )


def odd_block():
    return lax.rem(lax.axis_index("snp"), 2) == 1


def store_packed(up_ref, down_ref, where, first, second):
    left = iota((first.shape[0], LANES), 1) < HALF_LANES
    middle = first[:, LANES : 2 * LANES]
    turned = pltpu.roll(second[:, LANES : 2 * LANES], HALF_LANES, 1)
    for ref, side, mixed in (
        (up_ref, slice(0, LANES), jnp.where(left, middle, turned)),
        (down_ref, slice(2 * LANES, 3 * LANES), jnp.where(left, turned, middle)),
    ):
        ref[where, 0:LANES] = first[:, side].astype(jnp.bfloat16)
        ref[where, LANES : 2 * LANES] = mixed.astype(jnp.bfloat16)
        ref[where, 2 * LANES : 3 * LANES] = second[:, side].astype(jnp.bfloat16)


def load_packed(up, down):
    left = iota((up.shape[0], LANES), 1) < HALF_LANES
    up_mixed, down_mixed = up[:, LANES : 2 * LANES], down[:, LANES : 2 * LANES]
    first = jnp.where(left, up_mixed, down_mixed)
    second = jnp.where(left, down_mixed, up_mixed)
    second = pltpu.roll(second.astype(jnp.float32), HALF_LANES, 1).astype(second.dtype)
    return (
        (up[:, :LANES], first, down[:, :LANES]),
        (up[:, 2 * LANES :], second, down[:, 2 * LANES :]),
    )


def prepare_kernel(hap_ref, annot_ref, alleles_ref, far_ref, close_ref, held, held_annots, sems):
    rows = hap_ref.shape[0]
    annot_rows = annot_ref.shape[0]
    size = rows // (2 * CHUNKS)
    starts = [side * (rows // 2) + chunk * size for chunk in range(CHUNKS) for side in range(2)]
    copies = [
        pltpu.make_async_copy(
            hap_ref.at[pl.ds(start, size)], held.at[pl.ds(start, size)], sems.at[number]
        )
        for number, start in enumerate(starts)
    ]
    copies.append(pltpu.make_async_copy(annot_ref, held_annots, sems.at[2 * CHUNKS]))
    for copy in copies:
        copy.start()
    part = far_ref.shape[0] - rows // 2
    odd = odd_block()

    def store(where, first, second):
        @pl.when(odd)
        def _():
            store_packed(close_ref, far_ref, where, first, second)

        @pl.when(jnp.logical_not(odd))
        def _():
            store_packed(far_ref, close_ref, where, first, second)

    for chunk in range(CHUNKS):
        pair = []
        for side in range(2):
            number = 2 * chunk + side
            copies[number].wait()
            where = slice(starts[number], starts[number] + size)
            values = held[where, :].astype(jnp.float32)
            alleles_ref[where, :] = values.astype(jnp.bfloat16)
            pair.append(values)
        store(slice(chunk * size, (chunk + 1) * size), *pair)
    copies[-1].wait()
    annots = jnp.concatenate(
        [
            held_annots[...].astype(jnp.float32),
            jnp.zeros((2 * part - annot_rows, annot_ref.shape[1]), jnp.float32),
        ],
        axis=0,
    )
    store(slice(rows // 2, rows // 2 + part), annots[:part], annots[part:])


def partner(group, step, groups):
    if groups & (groups - 1) == 0:
        return group ^ step
    return (group + step) % groups


def send_shares(groups, source, share, targets):
    me = lax.axis_index("hap")
    for step, target in enumerate(targets):
        group = partner(me, step, groups)
        rows = source[pl.ds(pl.multiple_of(group * share, 8), share), :]
        target[0:share, :] = rows.astype(target.dtype)


def send_tiles(groups, source, share, targets):
    me = lax.axis_index("hap")
    for step, target in enumerate(targets):
        owner = partner(me, step, groups)
        counts = source[pl.ds(pl.multiple_of(owner * share, 8), share), :]
        for k in range(source.shape[1] // LANES):
            target[k * share : (k + 1) * share, :] = counts[:, k * LANES : (k + 1) * LANES]


def from_tiles(counts, share):
    tiles = counts.shape[0] // share
    return jnp.concatenate([counts[k * share : (k + 1) * share, :] for k in range(tiles)], axis=1)


def own_kernel(groups, share, alleles_ref, label_ref, *refs):
    weighted_ref, totals_ref, *targets = refs[: 2 + groups]
    tile, folded = refs[2 + groups :]
    rows, snps = alleles_ref.shape
    half = snps // 2
    weight = jnp.where(label_ref[...] > 0, float(BASE), 1.0)
    weighted_ref[0:snps, :] = alleles_ref[...].T * weight.astype(jnp.bfloat16)
    extra = weighted_ref.shape[0] - snps
    weighted_ref[snps:, :] = jnp.broadcast_to(weight, (extra, rows)).astype(jnp.bfloat16)
    tile[...] = jnp.dot(weighted_ref[...], alleles_ref[...], preferred_element_type=jnp.float32)
    count = jnp.sum(weight, axis=1, keepdims=True)
    totals_ref[...] = jnp.concatenate(
        [tile[snps : snps + 1, :], jnp.broadcast_to(count, (1, snps)), jnp.zeros((6, snps))], axis=0
    )
    row, col = iota((half, snps), 0), iota((half, snps), 1)
    moved = (col < half) | (col - half > row)
    turned = pltpu.roll(tile[0:half, :], half, 1)
    folded[0:half, :] = to_fields(jnp.where(moved, turned, tile[half:snps, :]))
    if folded.shape[0] > half:
        folded[half:, :] = jnp.zeros((folded.shape[0] - half, snps), jnp.int32)
    if groups != len(LEFT_BLOCKS):
        send_shares(groups, folded, share, targets)
        return
    tiles = snps // LANES
    shared = [totals_ref[0:1, k * LANES : (k + 1) * LANES] for k in range(tiles)]
    shared += [totals_ref[1:2, 0:LANES], jnp.zeros((7 - tiles, LANES))]
    extras = to_fields(jnp.concatenate(shared, axis=0))
    send_tiles(groups, folded, share, targets)
    for target in targets:
        target[tiles * share :, :] = extras


LEFT_BLOCKS = ((0, 1, 2, 3), (2, 3, 6, 7), (4, 0, 1, 2), (6, 0, 4, 5))
RIGHT_BLOCKS = ((2, 3, 6, 7), (4, 5, 6, 7), (0, 1, 2, 4), (0, 4, 5, 6))


SPARE_OWN = ((0, 0, 0, 0), (1, 1, 2, 2), (4, 5, 6, 7), (6, 6, 7, 7))
SPARE_NEAR = ((4, 5, 6, 7), (4, 5, 4, 5), (3, 3, 3, 3), (1, 2, 1, 2))


def fold_spare(tile, spare):
    owners = len(SPARE_OWN)
    snps = tile.shape[1]
    size = snps // (2 * owners)
    count = spare.shape[0] // owners
    totals = tile[snps : snps + count - size, :]
    lane = iota((count, snps), 1)
    for owner in range(owners):
        mixed = None
        for slot in range(owners):
            own, near = SPARE_OWN[owner][slot], SPARE_NEAR[owner][slot]
            before = (SPARE_OWN[owner][slot - 1], SPARE_NEAR[owner][slot - 1] + 1) if slot else None
            if before == (own, near):
                continue
            values = jnp.concatenate([tile[own * size : (own + 1) * size, :], totals], axis=0)
            shift = (slot - near) * size % snps
            values = pltpu.roll(values, shift, 1) if shift else values
            mixed = values if mixed is None else jnp.where(lane >= slot * size, values, mixed)
        spare[owner * count : (owner + 1) * count, :] = to_fields(mixed[:, 0 : spare.shape[1]])


def fold_by_column(tile, flipped, folded):
    owners = len(LEFT_BLOCKS)
    snps = folded.shape[1]
    wide = snps // owners
    size = wide // 2
    shape = (size, snps)
    row, lane = iota(shape, 0), iota(shape, 1)

    def block(number):
        return tile[number * size : (number + 1) * size, :]

    diagonal = block(0)
    for number in range(1, 2 * owners):
        diagonal = jnp.where(lane >= number * size, block(number), diagonal)
    flipped[:, 0:size] = diagonal.T
    corner = diagonal
    for owner in range(owners):
        start = (2 * owner + 1) * size
        turned = jnp.concatenate(
            [flipped[start : start + size, :], jnp.zeros((size, snps - LANES), jnp.float32)], axis=1
        )
        if owner:
            turned = pltpu.roll(turned, owner * wide, 1)
        inside = lane - owner * wide
        other = (row <= inside) if owner < owners // 2 else (row >= inside)
        corner = jnp.where((inside >= 0) & (inside < size) & other, turned, corner)
    rolled = []
    for shift in range(owners):
        mixed = None
        for owner in range(owners):
            slot = (owner + shift) % owners
            left = block(LEFT_BLOCKS[owner][slot]) if slot else corner
            start = owner * wide
            mixed = left if mixed is None else jnp.where(lane >= start, left, mixed)
            mixed = jnp.where(lane >= start + size, block(RIGHT_BLOCKS[owner][slot]), mixed)
        rolled.append(pltpu.roll(mixed, shift * wide, 1) if shift else mixed)
    for owner in range(owners):
        mixed = rolled[(0 - owner) % owners]
        for slot in range(1, owners):
            mixed = jnp.where(lane >= slot * wide, rolled[(slot - owner) % owners], mixed)
        folded[owner * size : (owner + 1) * size, :] = to_fields(mixed)


def above(far):
    return odd_block() == far


def side_dot(weighted_ref, side_ref):
    rows = weighted_ref.shape[1]
    half = rows // 2

    def dot(which, columns):
        return jnp.dot(
            weighted_ref[:, which], side_ref[0:half, columns], preferred_element_type=jnp.float32
        )

    first = dot(slice(0, half), slice(0, 2 * LANES))
    second = dot(slice(half, rows), slice(LANES, 3 * LANES))
    whole = first[:, 0:LANES] + second[:, LANES:]
    return whole, first[:, LANES:] + pltpu.roll(second[:, 0:LANES], HALF_LANES, 1)


def close_kernel(weighted_ref, side_ref, whole_ref, shared_ref):
    whole_ref[...], shared_ref[...] = side_dot(weighted_ref, side_ref)


def far_kernel(
    groups, share, weighted_ref, side_ref, whole_ref, shared_ref, totals_ref, mine_ref, first_ref, own_sum_ref, *refs
):
    targets, (tile, folded, flipped, spare, extras) = refs[:groups], refs[groups:]
    snps = tile.shape[1]
    own_sum_ref[...] = mine_ref[...] + first_ref[...]
    whole, shared = side_dot(weighted_ref, side_ref)
    left = iota(shared.shape, 1) < HALF_LANES

    @pl.when(above(True))
    def _():
        tile[:, 0:LANES] = whole
        tile[:, LANES : 2 * LANES] = jnp.where(left, shared, shared_ref[...])
        tile[:, 2 * LANES :] = whole_ref[...]

    @pl.when(jnp.logical_not(above(True)))
    def _():
        tile[:, 0:LANES] = whole_ref[...]
        tile[:, LANES : 2 * LANES] = jnp.where(left, shared_ref[...], shared)
        tile[:, 2 * LANES :] = whole

    fold_by_column(tile, flipped, folded)
    square = (snps, snps)
    apart = jnp.sum(
        jnp.where(iota(square, 0) == iota(square, 1), tile[0:snps, :], 0.0), axis=0, keepdims=True
    )
    fold_spare(tile, spare)
    tiles = snps // LANES
    size = share
    count = spare.shape[0] // groups
    sizes = totals_ref[1:2, :]
    by_column = jnp.concatenate([sizes, tile[snps : snps + 1, :], apart, jnp.zeros((5, snps))], axis=0)
    for owner in range(groups):
        start = owner * (snps // groups)
        columns = pltpu.roll(by_column, snps - start, 1) if owner else by_column
        spare_totals = spare[owner * count + size : owner * count + size + 1, :]
        extras[8 * owner : 8 * (owner + 1), :] = jnp.concatenate(
            [
                to_fields(columns[0:3, 0:LANES]),
                spare_totals[:, 0:LANES],
                spare_totals[:, LANES:],
                jnp.zeros((3, LANES), jnp.int32),
            ],
            axis=0,
        )
    me = lax.axis_index("hap")
    send_tiles(groups, folded, share, targets)
    left = iota((size // 2, LANES), 1) < HALF_LANES
    for step, target in enumerate(targets):
        owner = partner(me, step, groups)
        counts = spare[pl.ds(pl.multiple_of(owner * count, 8), size), :]
        start = tiles * size
        target[start : start + size, :] = counts[:, 0:LANES]
        rest = counts[:, LANES:]
        target[start + size : start + size + size // 2, :] = jnp.where(
            left, rest[0 : size // 2], pltpu.roll(rest[size // 2 :], HALF_LANES, 1)
        )
        target[start + size + size // 2 :, :] = extras[pl.ds(pl.multiple_of(owner * 8, 8), 8), :]


def near_kernel(groups, share, weighted_ref, far_ref, close_ref, totals_ref, *refs):
    own_parts, own_sum_ref = refs[:groups], refs[groups]
    targets, (near, tile, folded) = refs[groups + 1 : 2 * groups + 1], refs[2 * groups + 1 :]
    rows, snps = near.shape
    half = snps // 2
    odd = odd_block()

    def unpack(up_ref, down_ref):
        pieces = load_packed(up_ref[0 : rows // 2, :], down_ref[0 : rows // 2, :])
        for side in range(2):
            where = slice(side * (rows // 2), (side + 1) * (rows // 2))
            for number in range(3):
                near[where, number * LANES : (number + 1) * LANES] = pieces[side][number]

    @pl.when(odd)
    def _():
        unpack(far_ref, close_ref)

    @pl.when(jnp.logical_not(odd))
    def _():
        unpack(close_ref, far_ref)

    tile[...] = jnp.dot(weighted_ref[...], near[...], preferred_element_type=jnp.float32)
    row, col = iota((half, snps), 0), iota((half, snps), 1)
    moved = (col >= half) & (col - half < row)
    turned = pltpu.roll(tile[0:half, :], half, 1)
    folded[0:half, :] = to_fields(jnp.where(moved, turned, tile[half:snps, :]))
    if folded.shape[0] > half:
        folded[half:, :] = jnp.zeros((folded.shape[0] - half, snps), jnp.int32)
    square = (snps, snps)
    far = jnp.sum(
        jnp.where(iota(square, 0) == iota(square, 1), tile[0:snps, :], 0.0), axis=0, keepdims=True
    )
    extras = to_fields(
        jnp.concatenate(
            [totals_ref[0:2, :], tile[snps : snps + 1, :], far, jnp.zeros((4, snps))], axis=0
        )
    )
    send_shares(groups, folded, share, targets)
    for target in targets:
        target[share:, :] = extras
    own_sum_ref[...] = sum((part[...] for part in own_parts[1:]), own_parts[0][...])


def annots_kernel(annot_ref, far_ref, close_ref, own_ref, near_ref):
    snps = annot_ref.shape[1]
    part = far_ref.shape[0]
    wide = 2 * part
    own = annot_ref[...].astype(jnp.float32)
    own = jnp.concatenate([own, jnp.zeros((LANES - own.shape[0], snps), jnp.float32)], axis=0)
    own_ref[...] = own.T
    odd = odd_block()
    far, close = far_ref[...].astype(jnp.float32), close_ref[...].astype(jnp.float32)
    first, second = load_packed(jnp.where(odd, far, close), jnp.where(odd, close, far))
    near = jnp.concatenate(
        [
            jnp.concatenate([piece.astype(jnp.float32) for piece in first], axis=1),
            jnp.concatenate([piece.astype(jnp.float32) for piece in second], axis=1),
            jnp.zeros((LANES - wide, snps), jnp.float32),
        ],
        axis=0,
    )
    near_ref[...] = near.T


def column_stats(totals, count):
    size = jnp.maximum(count, 1.0)
    frequency = totals / size
    variance = jnp.maximum(frequency * (1.0 - frequency), VARIANCE_FLOOR)
    inverse = 1.0 / jnp.sqrt(size * variance)
    low = ((0.0 - frequency) * inverse).astype(jnp.bfloat16).astype(jnp.float32)
    high = ((1.0 - frequency) * inverse).astype(jnp.bfloat16).astype(jnp.float32)
    step = high - low
    root = 1.0 / jnp.sqrt(size)
    return step, step * totals * root, (low * count + step * totals) * root


def correlation(row, col, count):
    return row[0] * col[0] * count - row[1] * col[1] + row[2] * col[2]


def split(values):
    high = values.astype(jnp.bfloat16)
    return high, (values - high.astype(jnp.float32)).astype(jnp.bfloat16)


def dot_split(values, right, axis):
    dims = (((axis,), (0,)), ((), ()))
    return sum(
        lax.dot_general(part, right, dims, preferred_element_type=jnp.float32)
        for part in split(values)
    )


def score_kernel(groups, share, reach_ref, *refs):
    own_sum_ref, near_parts = refs[0], refs[1 : groups + 1]
    annot_ref, near_annot_ref = refs[groups + 1 : groups + 3]
    targets = refs[groups + 3 : 2 * groups + 3]
    table, annots, near_annots, scores = refs[2 * groups + 3 :]
    snps = annot_ref.shape[0]
    half = snps // 2
    out_share = snps // groups
    me = lax.axis_index("hap")
    block = lax.axis_index("snp")
    last = reach_ref.shape[0] - 1
    reach_here = reach_ref[block]
    reach_up = reach_ref[jnp.minimum(block + 1, last)]
    reach_down = reach_ref[jnp.maximum(block - 1, 0)]

    own_counts = own_sum_ref[...]
    near_sums = sum((part[...] for part in near_parts[1:]), near_parts[0][...])
    extras = from_fields(near_sums[share:, :])
    near_counts = near_sums[0:share, :]

    own_stats, near_stats, lines = [], [], []
    for pop in range(2):
        count = extras[pop][1:2, :]
        own_stats.append(column_stats(extras[pop][0:1, :], count))
        near_stats.append(column_stats(extras[pop][2:3, :], count))
        lines += [*own_stats[pop], *near_stats[pop], extras[pop][0:1, :], extras[pop][3:4, :]]
    by_row = jnp.concatenate(lines, axis=0).T
    table[0:snps, 0:16] = by_row
    if table.shape[0] > snps:
        table[snps:, 0:16] = jnp.zeros((table.shape[0] - snps, 16), jnp.float32)
    annots[0:snps, :] = annot_ref[...]
    near_annots[0:snps, :] = near_annot_ref[...]
    if annots.shape[0] > snps:
        annots[snps:, :] = jnp.zeros((annots.shape[0] - snps, LANES), jnp.float32)

    low_rows = pl.multiple_of(me * share, 8)
    high_rows = pl.multiple_of(half + me * share, 8)

    def both(ref):
        return jnp.concatenate([ref[pl.ds(low_rows, share), :], ref[pl.ds(high_rows, share), :]], axis=0)

    here = both(table)
    own_count = jnp.concatenate([pltpu.roll(own_counts, half, 1), own_counts], axis=0)
    near_count = jnp.concatenate([pltpu.roll(near_counts, half, 1), near_counts], axis=0)
    shape = (2 * share, snps)
    local, col = iota(shape, 0), iota(shape, 1)
    low = local < share
    place = jnp.where(low, local, local - share) + me * share
    row = jnp.where(low, place, place + half)
    own_fields, near_fields = from_fields(own_count), from_fields(near_count)
    own_product, near_product = 1.0, 1.0
    for pop in range(2):
        row_stats = [here[:, 8 * pop + k : 8 * pop + k + 1] for k in range(3)]
        own_product *= correlation(row_stats, own_stats[pop], own_fields[pop])
        near_product *= correlation(row_stats, near_stats[pop], near_fields[pop])
    real = place < half
    own_inside = real & ((low & (col > row)) | (~low & (col >= half) & (col < row)))
    own_inside &= jnp.abs(col - row) <= reach_here
    own_kept = jnp.where(own_inside, own_product, 0.0)
    in_upper = col < half
    near_inside = real & ((low & (col < row)) | (~low & (in_upper | (col > row))))
    distance = jnp.where(in_upper, snps + col - row, snps + row - col)
    near_here = jnp.where(near_inside & (distance <= reach_here), near_product, 0.0)
    reach_there = jnp.where(in_upper, reach_up, reach_down)
    near_there = jnp.where(near_inside & (distance <= reach_there), near_product, 0.0)

    rows_here = both(annots)
    rows_there = pltpu.roll(rows_here, HALF_LANES, 1)
    scores[0:snps, :] = dot_split(
        jnp.concatenate([own_kept, near_there], axis=0),
        jnp.concatenate([rows_here, rows_there], axis=0).astype(jnp.bfloat16),
        0,
    )
    direct = dot_split(
        jnp.concatenate([own_kept, near_here], axis=1),
        jnp.concatenate([annot_ref[...], near_annot_ref[...]], axis=0).astype(jnp.bfloat16),
        1,
    )
    scores[pl.ds(low_rows, share), :] += direct[0:share, :]
    scores[pl.ds(high_rows, share), :] += direct[share:, :]

    out_rows = pl.ds(pl.multiple_of(me * out_share, 8), out_share)
    mine = table[out_rows, :]
    self_product, far_product = 1.0, 1.0
    for pop in range(2):
        k = 8 * pop
        own_row = [mine[:, k + s : k + s + 1] for s in range(3)]
        near_row = [mine[:, k + 3 + s : k + 4 + s] for s in range(3)]
        self_product *= correlation(own_row, own_row, mine[:, k + 6 : k + 7])
        far_product *= correlation(own_row, near_row, mine[:, k + 7 : k + 8])
    mine_annots = annots[out_rows, :]
    far_reach = jnp.where(me < groups // 2, reach_up, reach_down)
    scores[out_rows, :] += (
        mine_annots * self_product
        + near_annots[out_rows, :] * jnp.where(reach_here >= snps, far_product, 0.0)
        + pltpu.roll(mine_annots, HALF_LANES, 1) * jnp.where(far_reach >= snps, far_product, 0.0)
    )
    send_shares(groups, scores, out_share, targets)


def pack_halves(values):
    half = values.shape[0] // 2
    left = iota((half, LANES), 1) < HALF_LANES
    return jnp.where(left, values[0:half], pltpu.roll(values[half:], HALF_LANES, 1))


def unpack_halves(packed):
    return jnp.concatenate([packed, pltpu.roll(packed, HALF_LANES, 1)], axis=0)


def dot_rounded(values, right, axis):
    dims = (((axis,), (0,)), ((), ()))
    return lax.dot_general(
        values.astype(jnp.bfloat16), right, dims, preferred_element_type=jnp.float32
    )


def owner_places(groups, size):
    me = lax.axis_index("hap")

    def mine(blocks, slot):
        value = blocks[0][slot]
        for group in range(1, groups):
            value = jnp.where(me == group, blocks[group][slot], value)
        return value * size

    left = [mine(LEFT_BLOCKS, slot) for slot in range(groups)]
    right = [mine(RIGHT_BLOCKS, slot) for slot in range(groups)]
    return left + left[0:1], right + [(2 * me + 1) * size]


def spare_places(groups, size):
    me = lax.axis_index("hap")

    def mine(blocks, slot):
        value = blocks[0][slot]
        for group in range(1, groups):
            value = jnp.where(me == group, blocks[group][slot], value)
        return value * size

    return [[mine(blocks, slot) for slot in range(groups)] for blocks in (SPARE_OWN, SPARE_NEAR)]


def rows_at(ref, places, size):
    return jnp.concatenate([ref[pl.ds(pl.multiple_of(place, 8), size), :] for place in places], axis=0)


def own_score_kernel(
    groups, share, reach_ref, *refs
):
    own_parts, refs = refs[: groups - 1], refs[groups - 1 :]
    annot_ref, near_annot_ref, scores, mine_ref, rows_ref, masks_ref, columns_ref, own_rows_ref, *refs = refs
    spare_rows_ref, spare_mask_ref, spare_columns_ref, *targets, table = refs
    snps = annot_ref.shape[0]
    half = snps // 2
    wide = snps // groups
    tiles = snps // LANES
    me = lax.axis_index("hap")
    reach_here = reach_ref[lax.axis_index("snp")]
    own_sums = sum((part[...] for part in own_parts[1:]), own_parts[0][...])
    own_counts = from_tiles(own_sums[0 : tiles * share, :], share)
    extras = from_fields(own_sums[tiles * share :, :])

    own_stats, lines = [], []
    for pop in range(2):
        count = jnp.concatenate([extras[pop][tiles : tiles + 1, :]] * tiles, axis=1)
        totals = jnp.concatenate([extras[pop][k : k + 1, :] for k in range(tiles)], axis=1)
        own_stats.append(column_stats(totals, count))
        lines += [*own_stats[pop], totals]
    table[:, 0:8] = jnp.concatenate(lines, axis=0).T

    low_rows = pl.multiple_of(me * share, 8)
    high_rows = pl.multiple_of(half + me * share, 8)

    def both(ref):
        return jnp.concatenate([ref[pl.ds(low_rows, share), :], ref[pl.ds(high_rows, share), :]], axis=0)

    here = both(table)
    own_fields = from_fields(
        jnp.concatenate([pltpu.roll(own_counts, half, 1), own_counts], axis=0)
    )
    shape = (2 * share, snps)
    local, col = iota(shape, 0), iota(shape, 1)
    low = local < share
    row = jnp.where(low, local, local + half - share) + me * share
    product = 1.0
    for pop in range(2):
        row_stats = [here[:, 4 * pop + k : 4 * pop + k + 1] for k in range(3)]
        product *= correlation(row_stats, own_stats[pop], own_fields[pop])
    inside = (low & (col > row)) | (~low & (col >= half) & (col < row))
    own_kept = jnp.where(inside & (jnp.abs(col - row) <= reach_here), product, 0.0)
    rows_here = both(annot_ref).astype(jnp.bfloat16)
    scores[...] = dot_rounded(own_kept, rows_here, 0)
    direct = dot_rounded(own_kept, annot_ref[...].astype(jnp.bfloat16), 1)
    scores[pl.ds(low_rows, share), :] += direct[0:share, :]
    scores[pl.ds(high_rows, share), :] += direct[share:, :]

    slice_rows = pl.ds(pl.multiple_of(me * wide, 8), wide)
    mine = table[slice_rows, :]
    mine_ref[...] = mine
    product = 1.0
    for pop in range(2):
        own_row = [mine[:, 4 * pop + k : 4 * pop + k + 1] for k in range(4)]
        product *= correlation(own_row, own_row, own_row[3])
    scores[slice_rows, :] += annot_ref[slice_rows, :] * product
    for step, target in enumerate(targets, 2):
        group = partner(me, step, groups)
        rows = scores[pl.ds(pl.multiple_of(group * wide, 8), wide), :]
        target[...] = pack_halves(rows).astype(target.dtype)

    size = wide // 2
    left_places, right_places = owner_places(groups, size)
    left_table, right_table = rows_at(table, left_places, size), rows_at(table, right_places, size)
    local, lane = iota((size, LANES), 0), iota((size, LANES), 1)
    own_row = jnp.concatenate(
        [local + jnp.where(lane < size, a, b) for a, b in zip(left_places, right_places)], axis=0
    )
    shape = own_row.shape
    lane = iota(shape, 1)
    is_left = lane < size
    for pop in range(2):
        for k in range(3):
            column = slice(4 * pop + k, 4 * pop + k + 1)
            rows_ref[3 * pop + k] = jnp.where(is_left, left_table[:, column], right_table[:, column])
    upper = me < groups // 2
    block = lax.axis_index("snp")
    last = reach_ref.shape[0] - 1
    reach_there = jnp.where(
        upper, reach_ref[jnp.minimum(block + 1, last)], reach_ref[jnp.maximum(block - 1, 0)]
    )
    apart = jnp.abs(own_row - (lane + me * wide))
    ahead = (own_row - (lane + me * wide)) * jnp.where(upper, 1, -1) > 0
    real = ahead & (lane < wide) & ((lane >= size) | (iota(shape, 0) < groups * size))
    inside = (own_row - half) * jnp.where(upper, 1, -1) < jnp.where(upper, 0, 1)
    masks_ref[0] = jnp.where(real & inside & (snps - apart <= reach_here), 1.0, 0.0)
    masks_ref[1] = jnp.where(real & (snps - apart <= reach_there), 1.0, 0.0)
    theirs = near_annot_ref[slice_rows, :]
    columns = [theirs[0:size], pltpu.roll(theirs[size:], HALF_LANES, 1), jnp.zeros((LANES - wide, LANES))]
    columns_ref[...] = jnp.concatenate(columns, axis=0).astype(jnp.bfloat16)
    own_rows = rows_at(annot_ref, left_places, size) + pltpu.roll(
        rows_at(annot_ref, right_places, size), HALF_LANES, 1
    )
    own_rows_ref[...] = own_rows.astype(jnp.bfloat16)

    own_places, near_places = spare_places(groups, size)
    shape = (size, spare_mask_ref.shape[1])
    local, lane = iota(shape, 0), iota(shape, 1)

    def by_slot(values):
        mixed = values[0]
        for slot in range(1, groups):
            mixed = jnp.where(lane >= slot * size, values[slot], mixed)
        return mixed

    tables = [table[pl.ds(pl.multiple_of(place, 8), size), :] for place in own_places]
    for pop in range(2):
        for k in range(3):
            column = slice(4 * pop + k, 4 * pop + k + 1)
            spare_rows_ref[3 * pop + k] = by_slot(
                [jnp.broadcast_to(values[:, column], shape) for values in tables]
            )
    own_row = by_slot([local + place for place in own_places])
    near_col = by_slot([lane + (place - slot * size) for slot, place in enumerate(near_places)])
    close = snps - jnp.abs(own_row - near_col) <= reach_here
    spare_mask_ref[...] = jnp.where(close & (lane < groups * size), 1.0, 0.0)
    columns = [rows_at(near_annot_ref, near_places, size)]
    columns.append(jnp.zeros((shape[1] - groups * size, LANES), jnp.float32))
    spare_columns_ref[...] = jnp.concatenate(columns, axis=0).astype(jnp.bfloat16)


def near_score_kernel(groups, share, reach_ref, *refs):
    near_parts, refs = refs[:groups], refs[groups:]
    own_ref, mine_ref, rows_ref, masks_ref, columns_ref, own_rows_ref = refs[:6]
    spare_rows_ref, spare_mask_ref, spare_columns_ref, annot_ref, near_annot_ref = refs[6:11]
    out_ref, send_ref, near_out_ref, flipped, scores = refs[11:]
    snps = annot_ref.shape[0]
    wide = snps // groups
    size = wide // 2
    tiles = snps // LANES
    me = lax.axis_index("hap")
    block = lax.axis_index("snp")
    last = reach_ref.shape[0] - 1
    reach_here = reach_ref[block]
    reach_there = jnp.where(
        me < groups // 2, reach_ref[jnp.minimum(block + 1, last)], reach_ref[jnp.maximum(block - 1, 0)]
    )

    scores[...] = own_ref[...]
    near_sums = sum((part[...] for part in near_parts[1:]), near_parts[0][...])
    near_counts = from_tiles(near_sums[0 : tiles * share, :], share)
    start = tiles * share
    rest = near_sums[start + size : start + size + size // 2, :]
    rest = jnp.concatenate([rest, pltpu.roll(rest, HALF_LANES, 1)], axis=0)
    spare_fields = from_fields(jnp.concatenate([near_sums[start : start + size, :], rest], axis=1))
    extras = from_fields(near_sums[start + size + size // 2 :, :])
    near_stats, near_lines, spare_stats = [], [], []
    for pop in range(2):
        count = extras[pop][0:1, :]
        totals = jnp.concatenate([extras[pop][3:4, :], extras[pop][4:5, :]], axis=1)
        spare_stats.append(column_stats(totals, jnp.concatenate([count, count], axis=1)))
        near_stats.append(column_stats(extras[pop][1:2, :], extras[pop][0:1, :]))
        near_lines += [*near_stats[pop], extras[pop][2:3, :]]
    near_table = jnp.concatenate(near_lines, axis=0).T[0:wide, :]

    slots = [near_counts[:, 0:LANES]]
    for slot in range(1, groups):
        slots.append(pltpu.roll(near_counts, snps - slot * wide, 1)[:, 0:LANES])
    flipped[:, 0:size] = slots[0].T
    slots.append(pltpu.roll(flipped[0:size, :], size, 1))
    near_fields = from_fields(jnp.concatenate(slots, axis=0))
    product = 1.0
    for pop in range(2):
        row_stats = [rows_ref[3 * pop + k] for k in range(3)]
        product *= correlation(row_stats, near_stats[pop], near_fields[pop])
    near_here = jnp.where(masks_ref[0] > 0.0, product, 0.0)
    near_there = jnp.where(masks_ref[1] > 0.0, product, 0.0)
    slice_rows = pl.ds(pl.multiple_of(me * wide, 8), wide)
    direct = dot_rounded(near_here, columns_ref[...], 1)
    turned = pltpu.roll(direct, HALF_LANES, 1)
    for values, places in zip((direct, turned), owner_places(groups, size)):
        for slot, place in enumerate(places):
            scores[pl.ds(pl.multiple_of(place, 8), size), :] += values[slot * size : (slot + 1) * size, :]
    product = 1.0
    for pop in range(2):
        row_stats = [spare_rows_ref[3 * pop + k] for k in range(3)]
        product *= correlation(row_stats, spare_stats[pop], spare_fields[pop])
    spare_here = jnp.where(spare_mask_ref[...] > 0.0, product, 0.0)
    lane = iota(spare_here.shape, 1)
    spare_here = [
        jnp.where((lane >= slot * size) & (lane < (slot + 1) * size), spare_here, 0.0)
        for slot in range(groups)
    ]
    direct = dot_rounded(jnp.concatenate(spare_here, axis=0), spare_columns_ref[...], 1)
    for slot, place in enumerate(spare_places(groups, size)[0]):
        scores[pl.ds(pl.multiple_of(place, 8), size), :] += direct[slot * size : (slot + 1) * size, :]
    near_scores = dot_rounded(near_there, own_rows_ref[...], 0)
    near_scores = jnp.where(
        iota((size, LANES), 1) < HALF_LANES, near_scores[0:size], near_scores[size:wide]
    )

    mine_table = mine_ref[...]
    far_product = 1.0
    for pop in range(2):
        own_row = [mine_table[:, 4 * pop + k : 4 * pop + k + 1] for k in range(3)]
        near_row = [near_table[:, 4 * pop + k : 4 * pop + k + 1] for k in range(4)]
        far_product *= correlation(own_row, near_row, near_row[3])
    scores[slice_rows, :] += near_annot_ref[slice_rows, :] * jnp.where(reach_here >= snps, far_product, 0.0)
    far_scores = annot_ref[slice_rows, :] * jnp.where(reach_there >= snps, far_product, 0.0)
    near_out_ref[...] = (near_scores + pack_halves(far_scores)).astype(near_out_ref.dtype)

    def packed(step):
        group = partner(me, step, groups)
        return pack_halves(scores[pl.ds(pl.multiple_of(group * wide, 8), wide), :])

    out_ref[...] = packed(0)
    send_ref[...] = packed(1).astype(send_ref.dtype)


def column_finish_kernel(*refs):
    *parts, out_ref = refs
    packed = sum(part[...].astype(jnp.float32) for part in parts)
    out_ref[...] = unpack_halves(packed).T[0 : out_ref.shape[0], :]


def sum_kernel(*refs):
    *parts, own_ref, there_ref = refs
    total = sum((part[...].astype(jnp.float32) for part in parts[1:]), parts[0][...])
    own_ref[...] = total
    half = there_ref.shape[0]
    left = iota((half, LANES), 1) < HALF_LANES
    second = total[half:]
    if second.shape[0] < half:
        second = jnp.concatenate([second, jnp.zeros((half - second.shape[0], LANES))], axis=0)
    there_ref[...] = jnp.where(left, pltpu.roll(total[0:half], HALF_LANES, 1), second)


def finish_kernel(own_ref, there_ref, out_ref):
    annots, rows = out_ref.shape
    there = there_ref[...]
    there = jnp.concatenate([there, pltpu.roll(there, HALF_LANES, 1)], axis=0)
    out_ref[...] = (own_ref[...] + there[0:rows]).T[0:annots, :]


def around(value, groups, step):
    return lax.ppermute(
        value, "hap", [(source, partner(source, step, groups)) for source in range(groups)]
    )


def swapped(value, first):
    pairs = []
    for block in range(first, lax.axis_size("snp") - 1, 2):
        pairs += [(block, block + 1), (block + 1, block)]
    return lax.ppermute(value, "snp", pairs)


def per_device(haplotypes, labels, annotations, reach):
    rows, snps = haplotypes.shape
    half = snps // 2
    groups = lax.axis_size("hap")
    blocks = lax.axis_size("snp")
    share = round_up(-(-half // groups), 16)
    folded_rows = share * groups
    out_share = snps // groups
    padded = half + folded_rows
    annot_part = 32
    bf16, f32, i32 = jnp.bfloat16, jnp.float32, jnp.int32
    shape = jax.ShapeDtypeStruct

    packed = shape((rows // 2 + annot_part, snps), bf16)
    haplotypes = pltpu.with_memory_space_constraint(haplotypes, pltpu.HBM)
    annots_in = pltpu.with_memory_space_constraint(annotations, pltpu.HBM)
    alleles, far, close = call(
        prepare_kernel,
        [shape((rows, snps), bf16), packed, packed],
        [HBM, HBM],
        [
            pltpu.VMEM((rows, snps), i32),
            pltpu.VMEM(annotations.shape, i32),
            pltpu.SemaphoreType.DMA((2 * CHUNKS + 1,)),
        ],
        moved=rows * snps * 8,
    )(haplotypes, annots_in)
    from_far = swapped(far, 1)
    from_close = swapped(close, 0)

    by_column = groups == len(LEFT_BLOCKS)
    compact = shape((share * (snps // LANES) + 8, LANES), i32)
    own_share_counts = compact if by_column else shape((share, snps), i32)
    near_share_counts = shape((compact.shape[0] + share + share // 2, LANES), i32)
    tile = pltpu.VMEM((snps + 16, snps), f32)
    folded = pltpu.VMEM((folded_rows, snps), i32)
    weighted, totals, *own_parts = call(
        functools.partial(own_kernel, groups, share),
        [shape((snps + 16, rows), bf16), shape((8, snps), f32)] + [own_share_counts] * groups,
        [VMEM, VMEM],
        [tile, folded],
        flops=2 * rows * snps * snps,
        moved=rows * snps * 4,
    )(alleles, labels.reshape(1, rows))
    order = (2, 3, 1) if by_column else range(groups - 1, 0, -1)
    own_parts = [own_parts[0]] + [around(own_parts[k], groups, k) for k in order]

    near_shapes = [own_share_counts] + [near_share_counts if by_column else shape((share + 8, snps), i32)] * groups
    if by_column:
        piece = shape((snps + 16, LANES), f32)
        work = dict(flops=4 * rows * snps * LANES, moved=rows * snps * 4)
        close_counts = call(close_kernel, [piece, piece], [VMEM] * 2, **work)(weighted, from_close)
        own_sum, *near_parts = call(
            functools.partial(far_kernel, groups, share),
            near_shapes,
            [VMEM] * 7,
            [
                tile,
                folded,
                pltpu.VMEM((snps, LANES), f32),
                pltpu.VMEM(((share + 8) * groups, 2 * LANES), i32),
                pltpu.VMEM((8 * groups, LANES), i32),
            ],
            **work,
        )(weighted, from_far, *close_counts, totals, *own_parts[:2])
    else:
        own_sum, *near_parts = call(
            functools.partial(near_kernel, groups, share),
            near_shapes,
            [VMEM] * (4 + groups),
            [pltpu.VMEM((rows, snps), bf16), tile, folded],
            flops=2 * rows * snps * snps,
            moved=rows * snps * 4,
        )(weighted, from_far, from_close, totals, *own_parts)
    near_parts = [near_parts[0]] + [around(near_parts[k], groups, k) for k in order]

    by_snp = shape((snps, LANES), f32)
    own_annots, near_annots = call(annots_kernel, [by_snp, by_snp], [VMEM] * 3, moved=1 << 20)(
        annotations, from_far[rows // 2 :], from_close[rows // 2 :]
    )
    pairs = []
    for block in range(blocks):
        for group in range(groups):
            target = block + 1 if group < groups // 2 else block - 1
            if 0 <= target < blocks:
                pairs.append((block * groups + group, target * groups + group))

    def to_neighbour(value):
        return lax.ppermute(value, ("snp", "hap"), pairs)

    result = shape((annotations.shape[0], out_share), f32)
    half_share = round_up(-(-out_share // 2), 8)
    own_share = shape((out_share, LANES), f32)
    packed_share = shape((half_share, LANES), f32)
    if by_column:
        pair_rows = (groups + 1) * (out_share // 2)
        sent = shape((half_share, LANES), bf16)
        *prepared, second, third = call(
            functools.partial(own_score_kernel, groups, share),
            [
                by_snp,
                shape((out_share, LANES), f32),
                shape((6, pair_rows, LANES), f32),
                shape((2, pair_rows, LANES), f32),
                shape((LANES, LANES), bf16),
                shape((pair_rows, LANES), bf16),
                shape((6, share, 2 * LANES), f32),
                shape((share, 2 * LANES), f32),
                shape((2 * LANES, LANES), bf16),
                sent,
                sent,
            ],
            [SMEM] + [VMEM] * (groups + 1),
            [pltpu.VMEM((snps, LANES), f32)],
            flops=1 << 33,
            moved=1 << 20,
        )(reach, own_sum, *own_parts[2:], own_annots, near_annots)
        parts = [around(third, groups, 3), around(second, groups, 2)]
        own_scores, send, there = call(
            functools.partial(near_score_kernel, groups, share),
            [packed_share, sent, sent],
            [SMEM] + [VMEM] * (groups + 11),
            [pltpu.VMEM((LANES, LANES), i32), pltpu.VMEM((snps, LANES), f32)],
            flops=1 << 26,
            moved=1 << 21,
        )(reach, *near_parts, *prepared, own_annots, near_annots)
        parts += [around(send, groups, 1), to_neighbour(there)]
        return call(column_finish_kernel, result, [VMEM] * 5)(own_scores, *parts)

    tall = pltpu.VMEM((padded, LANES), f32)
    scores = call(
        functools.partial(score_kernel, groups, share),
        [own_share] + [shape((out_share, LANES), bf16)] * (groups - 1),
        [SMEM] + [VMEM] * (groups + 3),
        [tall, tall, tall, tall],
        flops=1 << 26,
        moved=1 << 21,
    )(reach, own_sum, *near_parts, own_annots, near_annots)
    scores = [scores[0]] + [around(scores[k], groups, k) for k in range(groups - 1, 0, -1)]
    own_scores, near_scores = call(sum_kernel, [own_share, packed_share], [VMEM] * groups)(*scores)
    return call(finish_kernel, result, [VMEM] * 2)(own_scores, to_neighbour(near_scores))


def solution(mesh):
    in_specs = (
        P("hap", ("parts", "snp")),
        P(("parts", "hap")),
        P(None, ("parts", "snp")),
        P("parts"),
    )
    out_specs = P(None, ("parts", "snp", "hap"))
    return jax.shard_map(
        per_device, mesh=mesh, in_specs=in_specs, out_specs=out_specs, check_vma=False
    )
```

```python
import functools

import jax
import jax.numpy as jnp
from jax import lax
from jax.experimental import pallas as pl
from jax.experimental.pallas import tpu as pltpu
from jax.sharding import PartitionSpec as P

VARIANCE_FLOOR = 0.01
BASE_BITS = 12
BASE = 1 << BASE_BITS
FIELD_BITS = 16
LANES = 128
HALF_LANES = LANES // 2
CHUNKS = 4
VMEM = pl.BlockSpec(memory_space=pltpu.VMEM)
SMEM = pl.BlockSpec(memory_space=pltpu.SMEM)
HBM = pl.BlockSpec(memory_space=pltpu.HBM)
VMEM_LIMIT = 24 * 1024 * 1024


def iota(shape, axis):
    return lax.broadcasted_iota(jnp.int32, shape, axis)


def round_up(value, step):
    return -(-value // step) * step


def to_fields(values):
    whole = values.astype(jnp.int32)
    return whole + (whole >> BASE_BITS) * ((1 << FIELD_BITS) - BASE)


def from_fields(packed):
    first = packed & ((1 << FIELD_BITS) - 1)
    second = lax.shift_right_logical(packed, FIELD_BITS)
    return first.astype(jnp.float32), second.astype(jnp.float32)


def call(kernel, out_shape, in_specs, scratch_shapes=(), flops=0, moved=0):
    several = isinstance(out_shape, (list, tuple))
    return pl.pallas_call(
        kernel,
        out_shape=out_shape,
        in_specs=in_specs,
        out_specs=[VMEM] * len(out_shape) if several else VMEM,
        scratch_shapes=list(scratch_shapes),
        compiler_params=pltpu.CompilerParams(vmem_limit_bytes=VMEM_LIMIT),
        cost_estimate=pl.CostEstimate(flops=flops, bytes_accessed=moved, transcendentals=0),
    )


def odd_block():
    return lax.rem(lax.axis_index("snp"), 2) == 1


def store_packed(up_ref, down_ref, where, first, second):
    left = iota((first.shape[0], LANES), 1) < HALF_LANES
    middle = first[:, LANES : 2 * LANES]
    turned = pltpu.roll(second[:, LANES : 2 * LANES], HALF_LANES, 1)
    for ref, side, mixed in (
        (up_ref, slice(0, LANES), jnp.where(left, middle, turned)),
        (down_ref, slice(2 * LANES, 3 * LANES), jnp.where(left, turned, middle)),
    ):
        ref[where, 0:LANES] = first[:, side].astype(jnp.bfloat16)
        ref[where, LANES : 2 * LANES] = mixed.astype(jnp.bfloat16)
        ref[where, 2 * LANES : 3 * LANES] = second[:, side].astype(jnp.bfloat16)


def load_packed(up, down):
    left = iota((up.shape[0], LANES), 1) < HALF_LANES
    up_mixed, down_mixed = up[:, LANES : 2 * LANES], down[:, LANES : 2 * LANES]
    first = jnp.where(left, up_mixed, down_mixed)
    second = jnp.where(left, down_mixed, up_mixed)
    second = pltpu.roll(second.astype(jnp.float32), HALF_LANES, 1).astype(second.dtype)
    return (
        (up[:, :LANES], first, down[:, :LANES]),
        (up[:, 2 * LANES :], second, down[:, 2 * LANES :]),
    )


def prepare_kernel(hap_ref, annot_ref, alleles_ref, far_ref, close_ref, held, held_annots, sems):
    rows = hap_ref.shape[0]
    annot_rows = annot_ref.shape[0]
    size = rows // (2 * CHUNKS)
    starts = [side * (rows // 2) + chunk * size for chunk in range(CHUNKS) for side in range(2)]
    copies = [
        pltpu.make_async_copy(
            hap_ref.at[pl.ds(start, size)], held.at[pl.ds(start, size)], sems.at[number]
        )
        for number, start in enumerate(starts)
    ]
    copies.append(pltpu.make_async_copy(annot_ref, held_annots, sems.at[2 * CHUNKS]))
    for copy in copies:
        copy.start()
    part = far_ref.shape[0] - rows // 2
    odd = odd_block()

    def store(where, first, second):
        @pl.when(odd)
        def _():
            store_packed(close_ref, far_ref, where, first, second)

        @pl.when(jnp.logical_not(odd))
        def _():
            store_packed(far_ref, close_ref, where, first, second)

    for chunk in range(CHUNKS):
        pair = []
        for side in range(2):
            number = 2 * chunk + side
            copies[number].wait()
            where = slice(starts[number], starts[number] + size)
            values = held[where, :].astype(jnp.float32)
            alleles_ref[where, :] = values.astype(jnp.bfloat16)
            pair.append(values)
        store(slice(chunk * size, (chunk + 1) * size), *pair)
    copies[-1].wait()
    annots = jnp.concatenate(
        [
            held_annots[...].astype(jnp.float32),
            jnp.zeros((2 * part - annot_rows, annot_ref.shape[1]), jnp.float32),
        ],
        axis=0,
    )
    store(slice(rows // 2, rows // 2 + part), annots[:part], annots[part:])


def partner(group, step, groups):
    if groups & (groups - 1) == 0:
        return group ^ step
    return (group + step) % groups


def send_shares(groups, source, share, targets):
    me = lax.axis_index("hap")
    for step, target in enumerate(targets):
        group = partner(me, step, groups)
        rows = source[pl.ds(pl.multiple_of(group * share, 8), share), :]
        target[0:share, :] = rows.astype(target.dtype)


def send_tiles(groups, source, share, targets):
    me = lax.axis_index("hap")
    for step, target in enumerate(targets):
        owner = partner(me, step, groups)
        counts = source[pl.ds(pl.multiple_of(owner * share, 8), share), :]
        for k in range(source.shape[1] // LANES):
            target[k * share : (k + 1) * share, :] = counts[:, k * LANES : (k + 1) * LANES]


def from_tiles(counts, share):
    tiles = counts.shape[0] // share
    return jnp.concatenate([counts[k * share : (k + 1) * share, :] for k in range(tiles)], axis=1)


def own_kernel(groups, share, alleles_ref, label_ref, *refs):
    weighted_ref, totals_ref, *targets = refs[: 2 + groups]
    tile, folded = refs[2 + groups :]
    rows, snps = alleles_ref.shape
    half = snps // 2
    weight = jnp.where(label_ref[...] > 0, float(BASE), 1.0)
    weighted_ref[0:snps, :] = alleles_ref[...].T * weight.astype(jnp.bfloat16)
    extra = weighted_ref.shape[0] - snps
    weighted_ref[snps:, :] = jnp.broadcast_to(weight, (extra, rows)).astype(jnp.bfloat16)
    tile[...] = jnp.dot(weighted_ref[...], alleles_ref[...], preferred_element_type=jnp.float32)
    count = jnp.sum(weight, axis=1, keepdims=True)
    totals_ref[...] = jnp.concatenate(
        [tile[snps : snps + 1, :], jnp.broadcast_to(count, (1, snps)), jnp.zeros((6, snps))], axis=0
    )
    row, col = iota((half, snps), 0), iota((half, snps), 1)
    moved = (col < half) | (col - half > row)
    turned = pltpu.roll(tile[0:half, :], half, 1)
    folded[0:half, :] = to_fields(jnp.where(moved, turned, tile[half:snps, :]))
    if folded.shape[0] > half:
        folded[half:, :] = jnp.zeros((folded.shape[0] - half, snps), jnp.int32)
    if groups != len(LEFT_BLOCKS):
        send_shares(groups, folded, share, targets)
        return
    tiles = snps // LANES
    shared = [totals_ref[0:1, k * LANES : (k + 1) * LANES] for k in range(tiles)]
    shared += [totals_ref[1:2, 0:LANES], jnp.zeros((7 - tiles, LANES))]
    extras = to_fields(jnp.concatenate(shared, axis=0))
    send_tiles(groups, folded, share, targets)
    for target in targets:
        target[tiles * share :, :] = extras


LEFT_BLOCKS = ((0, 1, 2, 3), (2, 3, 6, 7), (4, 0, 1, 2), (6, 0, 4, 5))
RIGHT_BLOCKS = ((2, 3, 6, 7), (4, 5, 6, 7), (0, 1, 2, 4), (0, 4, 5, 6))


SPARE_OWN = ((0, 0, 0, 0), (1, 1, 2, 2), (4, 5, 6, 7), (6, 6, 7, 7))
SPARE_NEAR = ((4, 5, 6, 7), (4, 5, 4, 5), (3, 3, 3, 3), (1, 2, 1, 2))


def fold_spare(tile, spare):
    owners = len(SPARE_OWN)
    snps = tile.shape[1]
    size = snps // (2 * owners)
    count = spare.shape[0] // owners
    totals = tile[snps : snps + count - size, :]
    lane = iota((count, snps), 1)
    for owner in range(owners):
        mixed = None
        for slot in range(owners):
            own, near = SPARE_OWN[owner][slot], SPARE_NEAR[owner][slot]
            before = (SPARE_OWN[owner][slot - 1], SPARE_NEAR[owner][slot - 1] + 1) if slot else None
            if before == (own, near):
                continue
            values = jnp.concatenate([tile[own * size : (own + 1) * size, :], totals], axis=0)
            shift = (slot - near) * size % snps
            values = pltpu.roll(values, shift, 1) if shift else values
            mixed = values if mixed is None else jnp.where(lane >= slot * size, values, mixed)
        spare[owner * count : (owner + 1) * count, :] = to_fields(mixed[:, 0 : spare.shape[1]])


def fold_by_column(tile, flipped, folded):
    owners = len(LEFT_BLOCKS)
    snps = folded.shape[1]
    wide = snps // owners
    size = wide // 2
    shape = (size, snps)
    row, lane = iota(shape, 0), iota(shape, 1)

    def block(number):
        return tile[number * size : (number + 1) * size, :]

    diagonal = block(0)
    for number in range(1, 2 * owners):
        diagonal = jnp.where(lane >= number * size, block(number), diagonal)
    flipped[:, 0:size] = diagonal.T
    corner = diagonal
    for owner in range(owners):
        start = (2 * owner + 1) * size
        turned = jnp.concatenate(
            [flipped[start : start + size, :], jnp.zeros((size, snps - LANES), jnp.float32)], axis=1
        )
        if owner:
            turned = pltpu.roll(turned, owner * wide, 1)
        inside = lane - owner * wide
        other = (row <= inside) if owner < owners // 2 else (row >= inside)
        corner = jnp.where((inside >= 0) & (inside < size) & other, turned, corner)
    rolled = []
    for shift in range(owners):
        mixed = None
        for owner in range(owners):
            slot = (owner + shift) % owners
            left = block(LEFT_BLOCKS[owner][slot]) if slot else corner
            start = owner * wide
            mixed = left if mixed is None else jnp.where(lane >= start, left, mixed)
            mixed = jnp.where(lane >= start + size, block(RIGHT_BLOCKS[owner][slot]), mixed)
        rolled.append(pltpu.roll(mixed, shift * wide, 1) if shift else mixed)
    for owner in range(owners):
        mixed = rolled[(0 - owner) % owners]
        for slot in range(1, owners):
            mixed = jnp.where(lane >= slot * wide, rolled[(slot - owner) % owners], mixed)
        folded[owner * size : (owner + 1) * size, :] = to_fields(mixed)


def above(far):
    return odd_block() == far


def side_dot(weighted_ref, side_ref):
    rows = weighted_ref.shape[1]
    half = rows // 2

    def dot(which, columns):
        return jnp.dot(
            weighted_ref[:, which], side_ref[0:half, columns], preferred_element_type=jnp.float32
        )

    first = dot(slice(0, half), slice(0, 2 * LANES))
    second = dot(slice(half, rows), slice(LANES, 3 * LANES))
    whole = first[:, 0:LANES] + second[:, LANES:]
    return whole, first[:, LANES:] + pltpu.roll(second[:, 0:LANES], HALF_LANES, 1)


def close_kernel(weighted_ref, side_ref, whole_ref, shared_ref):
    whole_ref[...], shared_ref[...] = side_dot(weighted_ref, side_ref)


def far_kernel(
    groups, share, weighted_ref, side_ref, whole_ref, shared_ref, totals_ref, *refs
):
    targets, (tile, folded, flipped, spare, extras) = refs[:groups], refs[groups:]
    snps = tile.shape[1]
    whole, shared = side_dot(weighted_ref, side_ref)
    left = iota(shared.shape, 1) < HALF_LANES

    @pl.when(above(True))
    def _():
        tile[:, 0:LANES] = whole
        tile[:, LANES : 2 * LANES] = jnp.where(left, shared, shared_ref[...])
        tile[:, 2 * LANES :] = whole_ref[...]

    @pl.when(jnp.logical_not(above(True)))
    def _():
        tile[:, 0:LANES] = whole_ref[...]
        tile[:, LANES : 2 * LANES] = jnp.where(left, shared_ref[...], shared)
        tile[:, 2 * LANES :] = whole

    fold_by_column(tile, flipped, folded)
    square = (snps, snps)
    apart = jnp.sum(
        jnp.where(iota(square, 0) == iota(square, 1), tile[0:snps, :], 0.0), axis=0, keepdims=True
    )
    fold_spare(tile, spare)
    tiles = snps // LANES
    size = share
    count = spare.shape[0] // groups
    sizes = totals_ref[1:2, :]
    by_column = jnp.concatenate([sizes, tile[snps : snps + 1, :], apart, jnp.zeros((5, snps))], axis=0)
    for owner in range(groups):
        start = owner * (snps // groups)
        columns = pltpu.roll(by_column, snps - start, 1) if owner else by_column
        spare_totals = spare[owner * count + size : owner * count + size + 1, :]
        extras[8 * owner : 8 * (owner + 1), :] = jnp.concatenate(
            [
                to_fields(columns[0:3, 0:LANES]),
                spare_totals[:, 0:LANES],
                spare_totals[:, LANES:],
                jnp.zeros((3, LANES), jnp.int32),
            ],
            axis=0,
        )
    me = lax.axis_index("hap")
    send_tiles(groups, folded, share, targets)
    left = iota((size // 2, LANES), 1) < HALF_LANES
    for step, target in enumerate(targets):
        owner = partner(me, step, groups)
        counts = spare[pl.ds(pl.multiple_of(owner * count, 8), size), :]
        start = tiles * size
        target[start : start + size, :] = counts[:, 0:LANES]
        rest = counts[:, LANES:]
        target[start + size : start + size + size // 2, :] = jnp.where(
            left, rest[0 : size // 2], pltpu.roll(rest[size // 2 :], HALF_LANES, 1)
        )
        target[start + size + size // 2 :, :] = extras[pl.ds(pl.multiple_of(owner * 8, 8), 8), :]


def near_kernel(groups, share, weighted_ref, far_ref, close_ref, totals_ref, *refs):
    own_parts, own_sum_ref = refs[:groups], refs[groups]
    targets, (near, tile, folded) = refs[groups + 1 : 2 * groups + 1], refs[2 * groups + 1 :]
    rows, snps = near.shape
    half = snps // 2
    odd = odd_block()

    def unpack(up_ref, down_ref):
        pieces = load_packed(up_ref[0 : rows // 2, :], down_ref[0 : rows // 2, :])
        for side in range(2):
            where = slice(side * (rows // 2), (side + 1) * (rows // 2))
            for number in range(3):
                near[where, number * LANES : (number + 1) * LANES] = pieces[side][number]

    @pl.when(odd)
    def _():
        unpack(far_ref, close_ref)

    @pl.when(jnp.logical_not(odd))
    def _():
        unpack(close_ref, far_ref)

    tile[...] = jnp.dot(weighted_ref[...], near[...], preferred_element_type=jnp.float32)
    row, col = iota((half, snps), 0), iota((half, snps), 1)
    moved = (col >= half) & (col - half < row)
    turned = pltpu.roll(tile[0:half, :], half, 1)
    folded[0:half, :] = to_fields(jnp.where(moved, turned, tile[half:snps, :]))
    if folded.shape[0] > half:
        folded[half:, :] = jnp.zeros((folded.shape[0] - half, snps), jnp.int32)
    square = (snps, snps)
    far = jnp.sum(
        jnp.where(iota(square, 0) == iota(square, 1), tile[0:snps, :], 0.0), axis=0, keepdims=True
    )
    extras = to_fields(
        jnp.concatenate(
            [totals_ref[0:2, :], tile[snps : snps + 1, :], far, jnp.zeros((4, snps))], axis=0
        )
    )
    send_shares(groups, folded, share, targets)
    for target in targets:
        target[share:, :] = extras
    own_sum_ref[...] = sum((part[...] for part in own_parts[1:]), own_parts[0][...])


def annots_kernel(annot_ref, far_ref, close_ref, own_ref, near_ref):
    snps = annot_ref.shape[1]
    part = far_ref.shape[0]
    wide = 2 * part
    own = annot_ref[...].astype(jnp.float32)
    own = jnp.concatenate([own, jnp.zeros((LANES - own.shape[0], snps), jnp.float32)], axis=0)
    own_ref[...] = own.T
    odd = odd_block()
    far, close = far_ref[...].astype(jnp.float32), close_ref[...].astype(jnp.float32)
    first, second = load_packed(jnp.where(odd, far, close), jnp.where(odd, close, far))
    near = jnp.concatenate(
        [
            jnp.concatenate([piece.astype(jnp.float32) for piece in first], axis=1),
            jnp.concatenate([piece.astype(jnp.float32) for piece in second], axis=1),
            jnp.zeros((LANES - wide, snps), jnp.float32),
        ],
        axis=0,
    )
    near_ref[...] = near.T


def column_stats(totals, count):
    size = jnp.maximum(count, 1.0)
    frequency = totals / size
    variance = jnp.maximum(frequency * (1.0 - frequency), VARIANCE_FLOOR)
    inverse = 1.0 / jnp.sqrt(size * variance)
    low = ((0.0 - frequency) * inverse).astype(jnp.bfloat16).astype(jnp.float32)
    high = ((1.0 - frequency) * inverse).astype(jnp.bfloat16).astype(jnp.float32)
    step = high - low
    root = 1.0 / jnp.sqrt(size)
    return step, step * totals * root, (low * count + step * totals) * root


def correlation(row, col, count):
    return row[0] * col[0] * count - row[1] * col[1] + row[2] * col[2]


def split(values):
    high = values.astype(jnp.bfloat16)
    return high, (values - high.astype(jnp.float32)).astype(jnp.bfloat16)


def dot_split(values, right, axis):
    dims = (((axis,), (0,)), ((), ()))
    return sum(
        lax.dot_general(part, right, dims, preferred_element_type=jnp.float32)
        for part in split(values)
    )


def score_kernel(groups, share, reach_ref, *refs):
    own_sum_ref, near_parts = refs[0], refs[1 : groups + 1]
    annot_ref, near_annot_ref = refs[groups + 1 : groups + 3]
    targets = refs[groups + 3 : 2 * groups + 3]
    table, annots, near_annots, scores = refs[2 * groups + 3 :]
    snps = annot_ref.shape[0]
    half = snps // 2
    out_share = snps // groups
    me = lax.axis_index("hap")
    block = lax.axis_index("snp")
    last = reach_ref.shape[0] - 1
    reach_here = reach_ref[block]
    reach_up = reach_ref[jnp.minimum(block + 1, last)]
    reach_down = reach_ref[jnp.maximum(block - 1, 0)]

    own_counts = own_sum_ref[...]
    near_sums = sum((part[...] for part in near_parts[1:]), near_parts[0][...])
    extras = from_fields(near_sums[share:, :])
    near_counts = near_sums[0:share, :]

    own_stats, near_stats, lines = [], [], []
    for pop in range(2):
        count = extras[pop][1:2, :]
        own_stats.append(column_stats(extras[pop][0:1, :], count))
        near_stats.append(column_stats(extras[pop][2:3, :], count))
        lines += [*own_stats[pop], *near_stats[pop], extras[pop][0:1, :], extras[pop][3:4, :]]
    by_row = jnp.concatenate(lines, axis=0).T
    table[0:snps, 0:16] = by_row
    if table.shape[0] > snps:
        table[snps:, 0:16] = jnp.zeros((table.shape[0] - snps, 16), jnp.float32)
    annots[0:snps, :] = annot_ref[...]
    near_annots[0:snps, :] = near_annot_ref[...]
    if annots.shape[0] > snps:
        annots[snps:, :] = jnp.zeros((annots.shape[0] - snps, LANES), jnp.float32)

    low_rows = pl.multiple_of(me * share, 8)
    high_rows = pl.multiple_of(half + me * share, 8)

    def both(ref):
        return jnp.concatenate([ref[pl.ds(low_rows, share), :], ref[pl.ds(high_rows, share), :]], axis=0)

    here = both(table)
    own_count = jnp.concatenate([pltpu.roll(own_counts, half, 1), own_counts], axis=0)
    near_count = jnp.concatenate([pltpu.roll(near_counts, half, 1), near_counts], axis=0)
    shape = (2 * share, snps)
    local, col = iota(shape, 0), iota(shape, 1)
    low = local < share
    place = jnp.where(low, local, local - share) + me * share
    row = jnp.where(low, place, place + half)
    own_fields, near_fields = from_fields(own_count), from_fields(near_count)
    own_product, near_product = 1.0, 1.0
    for pop in range(2):
        row_stats = [here[:, 8 * pop + k : 8 * pop + k + 1] for k in range(3)]
        own_product *= correlation(row_stats, own_stats[pop], own_fields[pop])
        near_product *= correlation(row_stats, near_stats[pop], near_fields[pop])
    real = place < half
    own_inside = real & ((low & (col > row)) | (~low & (col >= half) & (col < row)))
    own_inside &= jnp.abs(col - row) <= reach_here
    own_kept = jnp.where(own_inside, own_product, 0.0)
    in_upper = col < half
    near_inside = real & ((low & (col < row)) | (~low & (in_upper | (col > row))))
    distance = jnp.where(in_upper, snps + col - row, snps + row - col)
    near_here = jnp.where(near_inside & (distance <= reach_here), near_product, 0.0)
    reach_there = jnp.where(in_upper, reach_up, reach_down)
    near_there = jnp.where(near_inside & (distance <= reach_there), near_product, 0.0)

    rows_here = both(annots)
    rows_there = pltpu.roll(rows_here, HALF_LANES, 1)
    scores[0:snps, :] = dot_split(
        jnp.concatenate([own_kept, near_there], axis=0),
        jnp.concatenate([rows_here, rows_there], axis=0).astype(jnp.bfloat16),
        0,
    )
    direct = dot_split(
        jnp.concatenate([own_kept, near_here], axis=1),
        jnp.concatenate([annot_ref[...], near_annot_ref[...]], axis=0).astype(jnp.bfloat16),
        1,
    )
    scores[pl.ds(low_rows, share), :] += direct[0:share, :]
    scores[pl.ds(high_rows, share), :] += direct[share:, :]

    out_rows = pl.ds(pl.multiple_of(me * out_share, 8), out_share)
    mine = table[out_rows, :]
    self_product, far_product = 1.0, 1.0
    for pop in range(2):
        k = 8 * pop
        own_row = [mine[:, k + s : k + s + 1] for s in range(3)]
        near_row = [mine[:, k + 3 + s : k + 4 + s] for s in range(3)]
        self_product *= correlation(own_row, own_row, mine[:, k + 6 : k + 7])
        far_product *= correlation(own_row, near_row, mine[:, k + 7 : k + 8])
    mine_annots = annots[out_rows, :]
    far_reach = jnp.where(me < groups // 2, reach_up, reach_down)
    scores[out_rows, :] += (
        mine_annots * self_product
        + near_annots[out_rows, :] * jnp.where(reach_here >= snps, far_product, 0.0)
        + pltpu.roll(mine_annots, HALF_LANES, 1) * jnp.where(far_reach >= snps, far_product, 0.0)
    )
    send_shares(groups, scores, out_share, targets)


def pack_halves(values):
    half = values.shape[0] // 2
    left = iota((half, LANES), 1) < HALF_LANES
    return jnp.where(left, values[0:half], pltpu.roll(values[half:], HALF_LANES, 1))


def unpack_halves(packed):
    return jnp.concatenate([packed, pltpu.roll(packed, HALF_LANES, 1)], axis=0)


def dot_rounded(values, right, axis):
    dims = (((axis,), (0,)), ((), ()))
    return lax.dot_general(
        values.astype(jnp.bfloat16), right, dims, preferred_element_type=jnp.float32
    )


def owner_places(groups, size):
    me = lax.axis_index("hap")

    def mine(blocks, slot):
        value = blocks[0][slot]
        for group in range(1, groups):
            value = jnp.where(me == group, blocks[group][slot], value)
        return value * size

    left = [mine(LEFT_BLOCKS, slot) for slot in range(groups)]
    right = [mine(RIGHT_BLOCKS, slot) for slot in range(groups)]
    return left + left[0:1], right + [(2 * me + 1) * size]


def spare_places(groups, size):
    me = lax.axis_index("hap")

    def mine(blocks, slot):
        value = blocks[0][slot]
        for group in range(1, groups):
            value = jnp.where(me == group, blocks[group][slot], value)
        return value * size

    return [[mine(blocks, slot) for slot in range(groups)] for blocks in (SPARE_OWN, SPARE_NEAR)]


def rows_at(ref, places, size):
    return jnp.concatenate([ref[pl.ds(pl.multiple_of(place, 8), size), :] for place in places], axis=0)


def own_score_kernel(
    groups, share, reach_ref, *refs
):
    own_parts, refs = refs[:groups], refs[groups:]
    annot_ref, near_annot_ref, scores, mine_ref, rows_ref, masks_ref, columns_ref, own_rows_ref, *refs = refs
    spare_rows_ref, spare_mask_ref, spare_columns_ref, *targets, table = refs
    snps = annot_ref.shape[0]
    half = snps // 2
    wide = snps // groups
    tiles = snps // LANES
    me = lax.axis_index("hap")
    reach_here = reach_ref[lax.axis_index("snp")]
    own_sums = sum((part[...] for part in own_parts[1:]), own_parts[0][...])
    own_counts = from_tiles(own_sums[0 : tiles * share, :], share)
    extras = from_fields(own_sums[tiles * share :, :])

    own_stats, lines = [], []
    for pop in range(2):
        count = jnp.concatenate([extras[pop][tiles : tiles + 1, :]] * tiles, axis=1)
        totals = jnp.concatenate([extras[pop][k : k + 1, :] for k in range(tiles)], axis=1)
        own_stats.append(column_stats(totals, count))
        lines += [*own_stats[pop], totals]
    table[:, 0:8] = jnp.concatenate(lines, axis=0).T

    low_rows = pl.multiple_of(me * share, 8)
    high_rows = pl.multiple_of(half + me * share, 8)

    def both(ref):
        return jnp.concatenate([ref[pl.ds(low_rows, share), :], ref[pl.ds(high_rows, share), :]], axis=0)

    here = both(table)
    own_fields = from_fields(
        jnp.concatenate([pltpu.roll(own_counts, half, 1), own_counts], axis=0)
    )
    shape = (2 * share, snps)
    local, col = iota(shape, 0), iota(shape, 1)
    low = local < share
    row = jnp.where(low, local, local + half - share) + me * share
    product = 1.0
    for pop in range(2):
        row_stats = [here[:, 4 * pop + k : 4 * pop + k + 1] for k in range(3)]
        product *= correlation(row_stats, own_stats[pop], own_fields[pop])
    inside = (low & (col > row)) | (~low & (col >= half) & (col < row))
    own_kept = jnp.where(inside & (jnp.abs(col - row) <= reach_here), product, 0.0)
    rows_here = both(annot_ref).astype(jnp.bfloat16)
    scores[...] = dot_rounded(own_kept, rows_here, 0)
    direct = dot_rounded(own_kept, annot_ref[...].astype(jnp.bfloat16), 1)
    scores[pl.ds(low_rows, share), :] += direct[0:share, :]
    scores[pl.ds(high_rows, share), :] += direct[share:, :]

    slice_rows = pl.ds(pl.multiple_of(me * wide, 8), wide)
    mine = table[slice_rows, :]
    mine_ref[...] = mine
    product = 1.0
    for pop in range(2):
        own_row = [mine[:, 4 * pop + k : 4 * pop + k + 1] for k in range(4)]
        product *= correlation(own_row, own_row, own_row[3])
    scores[slice_rows, :] += annot_ref[slice_rows, :] * product
    for step, target in enumerate(targets, 2):
        group = partner(me, step, groups)
        rows = scores[pl.ds(pl.multiple_of(group * wide, 8), wide), :]
        target[...] = pack_halves(rows).astype(target.dtype)

    size = wide // 2
    left_places, right_places = owner_places(groups, size)
    left_table, right_table = rows_at(table, left_places, size), rows_at(table, right_places, size)
    local, lane = iota((size, LANES), 0), iota((size, LANES), 1)
    own_row = jnp.concatenate(
        [local + jnp.where(lane < size, a, b) for a, b in zip(left_places, right_places)], axis=0
    )
    shape = own_row.shape
    lane = iota(shape, 1)
    is_left = lane < size
    for pop in range(2):
        for k in range(3):
            column = slice(4 * pop + k, 4 * pop + k + 1)
            rows_ref[3 * pop + k] = jnp.where(is_left, left_table[:, column], right_table[:, column])
    upper = me < groups // 2
    block = lax.axis_index("snp")
    last = reach_ref.shape[0] - 1
    reach_there = jnp.where(
        upper, reach_ref[jnp.minimum(block + 1, last)], reach_ref[jnp.maximum(block - 1, 0)]
    )
    apart = jnp.abs(own_row - (lane + me * wide))
    ahead = (own_row - (lane + me * wide)) * jnp.where(upper, 1, -1) > 0
    real = ahead & (lane < wide) & ((lane >= size) | (iota(shape, 0) < groups * size))
    inside = (own_row - half) * jnp.where(upper, 1, -1) < jnp.where(upper, 0, 1)
    masks_ref[0] = jnp.where(real & inside & (snps - apart <= reach_here), 1.0, 0.0)
    masks_ref[1] = jnp.where(real & (snps - apart <= reach_there), 1.0, 0.0)
    theirs = near_annot_ref[slice_rows, :]
    columns = [theirs[0:size], pltpu.roll(theirs[size:], HALF_LANES, 1), jnp.zeros((LANES - wide, LANES))]
    columns_ref[...] = jnp.concatenate(columns, axis=0).astype(jnp.bfloat16)
    own_rows = rows_at(annot_ref, left_places, size) + pltpu.roll(
        rows_at(annot_ref, right_places, size), HALF_LANES, 1
    )
    own_rows_ref[...] = own_rows.astype(jnp.bfloat16)

    own_places, near_places = spare_places(groups, size)
    shape = (size, spare_mask_ref.shape[1])
    local, lane = iota(shape, 0), iota(shape, 1)

    def by_slot(values):
        mixed = values[0]
        for slot in range(1, groups):
            mixed = jnp.where(lane >= slot * size, values[slot], mixed)
        return mixed

    tables = [table[pl.ds(pl.multiple_of(place, 8), size), :] for place in own_places]
    for pop in range(2):
        for k in range(3):
            column = slice(4 * pop + k, 4 * pop + k + 1)
            spare_rows_ref[3 * pop + k] = by_slot(
                [jnp.broadcast_to(values[:, column], shape) for values in tables]
            )
    own_row = by_slot([local + place for place in own_places])
    near_col = by_slot([lane + (place - slot * size) for slot, place in enumerate(near_places)])
    close = snps - jnp.abs(own_row - near_col) <= reach_here
    spare_mask_ref[...] = jnp.where(close & (lane < groups * size), 1.0, 0.0)
    columns = [rows_at(near_annot_ref, near_places, size)]
    columns.append(jnp.zeros((shape[1] - groups * size, LANES), jnp.float32))
    spare_columns_ref[...] = jnp.concatenate(columns, axis=0).astype(jnp.bfloat16)


def near_score_kernel(groups, share, reach_ref, *refs):
    near_parts, refs = refs[:groups], refs[groups:]
    own_ref, mine_ref, rows_ref, masks_ref, columns_ref, own_rows_ref = refs[:6]
    spare_rows_ref, spare_mask_ref, spare_columns_ref, annot_ref, near_annot_ref = refs[6:11]
    out_ref, send_ref, near_out_ref, flipped, scores = refs[11:]
    snps = annot_ref.shape[0]
    wide = snps // groups
    size = wide // 2
    tiles = snps // LANES
    me = lax.axis_index("hap")
    block = lax.axis_index("snp")
    last = reach_ref.shape[0] - 1
    reach_here = reach_ref[block]
    reach_there = jnp.where(
        me < groups // 2, reach_ref[jnp.minimum(block + 1, last)], reach_ref[jnp.maximum(block - 1, 0)]
    )

    scores[...] = own_ref[...]
    near_sums = sum((part[...] for part in near_parts[1:]), near_parts[0][...])
    near_counts = from_tiles(near_sums[0 : tiles * share, :], share)
    start = tiles * share
    rest = near_sums[start + size : start + size + size // 2, :]
    rest = jnp.concatenate([rest, pltpu.roll(rest, HALF_LANES, 1)], axis=0)
    spare_fields = from_fields(jnp.concatenate([near_sums[start : start + size, :], rest], axis=1))
    extras = from_fields(near_sums[start + size + size // 2 :, :])
    near_stats, near_lines, spare_stats = [], [], []
    for pop in range(2):
        count = extras[pop][0:1, :]
        totals = jnp.concatenate([extras[pop][3:4, :], extras[pop][4:5, :]], axis=1)
        spare_stats.append(column_stats(totals, jnp.concatenate([count, count], axis=1)))
        near_stats.append(column_stats(extras[pop][1:2, :], extras[pop][0:1, :]))
        near_lines += [*near_stats[pop], extras[pop][2:3, :]]
    near_table = jnp.concatenate(near_lines, axis=0).T[0:wide, :]

    slots = [near_counts[:, 0:LANES]]
    for slot in range(1, groups):
        slots.append(pltpu.roll(near_counts, snps - slot * wide, 1)[:, 0:LANES])
    flipped[:, 0:size] = slots[0].T
    slots.append(pltpu.roll(flipped[0:size, :], size, 1))
    near_fields = from_fields(jnp.concatenate(slots, axis=0))
    product = 1.0
    for pop in range(2):
        row_stats = [rows_ref[3 * pop + k] for k in range(3)]
        product *= correlation(row_stats, near_stats[pop], near_fields[pop])
    near_here = jnp.where(masks_ref[0] > 0.0, product, 0.0)
    near_there = jnp.where(masks_ref[1] > 0.0, product, 0.0)
    slice_rows = pl.ds(pl.multiple_of(me * wide, 8), wide)
    direct = dot_rounded(near_here, columns_ref[...], 1)
    turned = pltpu.roll(direct, HALF_LANES, 1)
    for values, places in zip((direct, turned), owner_places(groups, size)):
        for slot, place in enumerate(places):
            scores[pl.ds(pl.multiple_of(place, 8), size), :] += values[slot * size : (slot + 1) * size, :]
    product = 1.0
    for pop in range(2):
        row_stats = [spare_rows_ref[3 * pop + k] for k in range(3)]
        product *= correlation(row_stats, spare_stats[pop], spare_fields[pop])
    spare_here = jnp.where(spare_mask_ref[...] > 0.0, product, 0.0)
    lane = iota(spare_here.shape, 1)
    spare_here = [
        jnp.where((lane >= slot * size) & (lane < (slot + 1) * size), spare_here, 0.0)
        for slot in range(groups)
    ]
    direct = dot_rounded(jnp.concatenate(spare_here, axis=0), spare_columns_ref[...], 1)
    for slot, place in enumerate(spare_places(groups, size)[0]):
        scores[pl.ds(pl.multiple_of(place, 8), size), :] += direct[slot * size : (slot + 1) * size, :]
    near_scores = dot_rounded(near_there, own_rows_ref[...], 0)
    near_scores = jnp.where(
        iota((size, LANES), 1) < HALF_LANES, near_scores[0:size], near_scores[size:wide]
    )

    mine_table = mine_ref[...]
    far_product = 1.0
    for pop in range(2):
        own_row = [mine_table[:, 4 * pop + k : 4 * pop + k + 1] for k in range(3)]
        near_row = [near_table[:, 4 * pop + k : 4 * pop + k + 1] for k in range(4)]
        far_product *= correlation(own_row, near_row, near_row[3])
    scores[slice_rows, :] += near_annot_ref[slice_rows, :] * jnp.where(reach_here >= snps, far_product, 0.0)
    far_scores = annot_ref[slice_rows, :] * jnp.where(reach_there >= snps, far_product, 0.0)
    near_out_ref[...] = (near_scores + pack_halves(far_scores)).astype(near_out_ref.dtype)

    def packed(step):
        group = partner(me, step, groups)
        return pack_halves(scores[pl.ds(pl.multiple_of(group * wide, 8), wide), :])

    out_ref[...] = packed(0)
    send_ref[...] = packed(1).astype(send_ref.dtype)


def column_finish_kernel(*refs):
    *parts, out_ref = refs
    packed = sum(part[...].astype(jnp.float32) for part in parts)
    out_ref[...] = unpack_halves(packed).T[0 : out_ref.shape[0], :]


def sum_kernel(*refs):
    *parts, own_ref, there_ref = refs
    total = sum((part[...].astype(jnp.float32) for part in parts[1:]), parts[0][...])
    own_ref[...] = total
    half = there_ref.shape[0]
    left = iota((half, LANES), 1) < HALF_LANES
    second = total[half:]
    if second.shape[0] < half:
        second = jnp.concatenate([second, jnp.zeros((half - second.shape[0], LANES))], axis=0)
    there_ref[...] = jnp.where(left, pltpu.roll(total[0:half], HALF_LANES, 1), second)


def finish_kernel(own_ref, there_ref, out_ref):
    annots, rows = out_ref.shape
    there = there_ref[...]
    there = jnp.concatenate([there, pltpu.roll(there, HALF_LANES, 1)], axis=0)
    out_ref[...] = (own_ref[...] + there[0:rows]).T[0:annots, :]


def around(value, groups, step):
    return lax.ppermute(
        value, "hap", [(source, partner(source, step, groups)) for source in range(groups)]
    )


def swapped(value, first):
    pairs = []
    for block in range(first, lax.axis_size("snp") - 1, 2):
        pairs += [(block, block + 1), (block + 1, block)]
    return lax.ppermute(value, "snp", pairs)


def per_device(haplotypes, labels, annotations, reach):
    rows, snps = haplotypes.shape
    half = snps // 2
    groups = lax.axis_size("hap")
    blocks = lax.axis_size("snp")
    share = round_up(-(-half // groups), 16)
    folded_rows = share * groups
    out_share = snps // groups
    padded = half + folded_rows
    annot_part = 32
    bf16, f32, i32 = jnp.bfloat16, jnp.float32, jnp.int32
    shape = jax.ShapeDtypeStruct

    packed = shape((rows // 2 + annot_part, snps), bf16)
    haplotypes = pltpu.with_memory_space_constraint(haplotypes, pltpu.HBM)
    annots_in = pltpu.with_memory_space_constraint(annotations, pltpu.HBM)
    alleles, far, close = call(
        prepare_kernel,
        [shape((rows, snps), bf16), packed, packed],
        [HBM, HBM],
        [
            pltpu.VMEM((rows, snps), i32),
            pltpu.VMEM(annotations.shape, i32),
            pltpu.SemaphoreType.DMA((2 * CHUNKS + 1,)),
        ],
        moved=rows * snps * 8,
    )(haplotypes, annots_in)
    from_far = swapped(far, 1)
    from_close = swapped(close, 0)

    by_column = groups == len(LEFT_BLOCKS)
    compact = shape((share * (snps // LANES) + 8, LANES), i32)
    own_share_counts = compact if by_column else shape((share, snps), i32)
    near_share_counts = shape((compact.shape[0] + share + share // 2, LANES), i32)
    tile = pltpu.VMEM((snps + 16, snps), f32)
    folded = pltpu.VMEM((folded_rows, snps), i32)
    weighted, totals, *own_parts = call(
        functools.partial(own_kernel, groups, share),
        [shape((snps + 16, rows), bf16), shape((8, snps), f32)] + [own_share_counts] * groups,
        [VMEM, VMEM],
        [tile, folded],
        flops=2 * rows * snps * snps,
        moved=rows * snps * 4,
    )(alleles, labels.reshape(1, rows))
    order = (2, 3, 1) if by_column else range(groups - 1, 0, -1)
    own_parts = [own_parts[0]] + [around(own_parts[k], groups, k) for k in order]

    near_shapes = [own_share_counts] + [near_share_counts if by_column else shape((share + 8, snps), i32)] * groups
    if by_column:
        piece = shape((snps + 16, LANES), f32)
        work = dict(flops=4 * rows * snps * LANES, moved=rows * snps * 4)
        close_counts = call(close_kernel, [piece, piece], [VMEM] * 2, **work)(weighted, from_close)
        near_parts = call(
            functools.partial(far_kernel, groups, share),
            near_shapes[1:],
            [VMEM] * 5,
            [
                tile,
                folded,
                pltpu.VMEM((snps, LANES), f32),
                pltpu.VMEM(((share + 8) * groups, 2 * LANES), i32),
                pltpu.VMEM((8 * groups, LANES), i32),
            ],
            **work,
        )(weighted, from_far, *close_counts, totals)
    else:
        own_sum, *near_parts = call(
            functools.partial(near_kernel, groups, share),
            near_shapes,
            [VMEM] * (4 + groups),
            [pltpu.VMEM((rows, snps), bf16), tile, folded],
            flops=2 * rows * snps * snps,
            moved=rows * snps * 4,
        )(weighted, from_far, from_close, totals, *own_parts)
    near_parts = [near_parts[0]] + [around(near_parts[k], groups, k) for k in order]

    by_snp = shape((snps, LANES), f32)
    own_annots, near_annots = call(annots_kernel, [by_snp, by_snp], [VMEM] * 3, moved=1 << 20)(
        annotations, from_far[rows // 2 :], from_close[rows // 2 :]
    )
    pairs = []
    for block in range(blocks):
        for group in range(groups):
            target = block + 1 if group < groups // 2 else block - 1
            if 0 <= target < blocks:
                pairs.append((block * groups + group, target * groups + group))

    def to_neighbour(value):
        return lax.ppermute(value, ("snp", "hap"), pairs)

    result = shape((annotations.shape[0], out_share), f32)
    half_share = round_up(-(-out_share // 2), 8)
    own_share = shape((out_share, LANES), f32)
    packed_share = shape((half_share, LANES), f32)
    if by_column:
        pair_rows = (groups + 1) * (out_share // 2)
        sent = shape((half_share, LANES), bf16)
        *prepared, second, third = call(
            functools.partial(own_score_kernel, groups, share),
            [
                by_snp,
                shape((out_share, LANES), f32),
                shape((6, pair_rows, LANES), f32),
                shape((2, pair_rows, LANES), f32),
                shape((LANES, LANES), bf16),
                shape((pair_rows, LANES), bf16),
                shape((6, share, 2 * LANES), f32),
                shape((share, 2 * LANES), f32),
                shape((2 * LANES, LANES), bf16),
                sent,
                sent,
            ],
            [SMEM] + [VMEM] * (groups + 2),
            [pltpu.VMEM((snps, LANES), f32)],
            flops=1 << 33,
            moved=1 << 20,
        )(reach, *own_parts, own_annots, near_annots)
        parts = [around(third, groups, 3), around(second, groups, 2)]
        own_scores, send, there = call(
            functools.partial(near_score_kernel, groups, share),
            [packed_share, sent, sent],
            [SMEM] + [VMEM] * (groups + 11),
            [pltpu.VMEM((LANES, LANES), i32), pltpu.VMEM((snps, LANES), f32)],
            flops=1 << 26,
            moved=1 << 21,
        )(reach, *near_parts, *prepared, own_annots, near_annots)
        parts += [around(send, groups, 1), to_neighbour(there)]
        return call(column_finish_kernel, result, [VMEM] * 5)(own_scores, *parts)

    tall = pltpu.VMEM((padded, LANES), f32)
    scores = call(
        functools.partial(score_kernel, groups, share),
        [own_share] + [shape((out_share, LANES), bf16)] * (groups - 1),
        [SMEM] + [VMEM] * (groups + 3),
        [tall, tall, tall, tall],
        flops=1 << 26,
        moved=1 << 21,
    )(reach, own_sum, *near_parts, own_annots, near_annots)
    scores = [scores[0]] + [around(scores[k], groups, k) for k in range(groups - 1, 0, -1)]
    own_scores, near_scores = call(sum_kernel, [own_share, packed_share], [VMEM] * groups)(*scores)
    return call(finish_kernel, result, [VMEM] * 2)(own_scores, to_neighbour(near_scores))


def solution(mesh):
    in_specs = (
        P("hap", ("parts", "snp")),
        P(("parts", "hap")),
        P(None, ("parts", "snp")),
        P("parts"),
    )
    out_specs = P(None, ("parts", "snp", "hap"))
    return jax.shard_map(
        per_device, mesh=mesh, in_specs=in_specs, out_specs=out_specs, check_vma=False
    )
```

```python
import functools

import jax
import jax.numpy as jnp
from jax import lax
from jax.experimental import pallas as pl
from jax.experimental.pallas import tpu as pltpu
from jax.sharding import PartitionSpec as P

VARIANCE_FLOOR = 0.01
BASE_BITS = 12
BASE = 1 << BASE_BITS
FIELD_BITS = 16
LANES = 128
HALF_LANES = LANES // 2
CHUNKS = 4
VMEM = pl.BlockSpec(memory_space=pltpu.VMEM)
SMEM = pl.BlockSpec(memory_space=pltpu.SMEM)
HBM = pl.BlockSpec(memory_space=pltpu.HBM)
VMEM_LIMIT = 24 * 1024 * 1024


def iota(shape, axis):
    return lax.broadcasted_iota(jnp.int32, shape, axis)


def round_up(value, step):
    return -(-value // step) * step


def to_fields(values):
    whole = values.astype(jnp.int32)
    return whole + (whole >> BASE_BITS) * ((1 << FIELD_BITS) - BASE)


def from_fields(packed):
    first = packed & ((1 << FIELD_BITS) - 1)
    second = lax.shift_right_logical(packed, FIELD_BITS)
    return first.astype(jnp.float32), second.astype(jnp.float32)


def call(kernel, out_shape, in_specs, scratch_shapes=(), flops=0, moved=0):
    several = isinstance(out_shape, (list, tuple))
    return pl.pallas_call(
        kernel,
        out_shape=out_shape,
        in_specs=in_specs,
        out_specs=[VMEM] * len(out_shape) if several else VMEM,
        scratch_shapes=list(scratch_shapes),
        compiler_params=pltpu.CompilerParams(vmem_limit_bytes=VMEM_LIMIT),
        cost_estimate=pl.CostEstimate(flops=flops, bytes_accessed=moved, transcendentals=0),
    )


def odd_block():
    return lax.rem(lax.axis_index("snp"), 2) == 1


def store_packed(up_ref, down_ref, where, first, second):
    left = iota((first.shape[0], LANES), 1) < HALF_LANES
    middle = first[:, LANES : 2 * LANES]
    turned = pltpu.roll(second[:, LANES : 2 * LANES], HALF_LANES, 1)
    for ref, side, mixed in (
        (up_ref, slice(0, LANES), jnp.where(left, middle, turned)),
        (down_ref, slice(2 * LANES, 3 * LANES), jnp.where(left, turned, middle)),
    ):
        ref[where, 0:LANES] = first[:, side].astype(jnp.bfloat16)
        ref[where, LANES : 2 * LANES] = mixed.astype(jnp.bfloat16)
        ref[where, 2 * LANES : 3 * LANES] = second[:, side].astype(jnp.bfloat16)


def load_packed(up, down):
    left = iota((up.shape[0], LANES), 1) < HALF_LANES
    up_mixed, down_mixed = up[:, LANES : 2 * LANES], down[:, LANES : 2 * LANES]
    first = jnp.where(left, up_mixed, down_mixed)
    second = jnp.where(left, down_mixed, up_mixed)
    second = pltpu.roll(second.astype(jnp.float32), HALF_LANES, 1).astype(second.dtype)
    return (
        (up[:, :LANES], first, down[:, :LANES]),
        (up[:, 2 * LANES :], second, down[:, 2 * LANES :]),
    )


def prepare_kernel(hap_ref, annot_ref, alleles_ref, far_ref, close_ref, held, held_annots, sems):
    rows = hap_ref.shape[0]
    annot_rows = annot_ref.shape[0]
    size = rows // (2 * CHUNKS)
    starts = [side * (rows // 2) + chunk * size for chunk in range(CHUNKS) for side in range(2)]
    copies = [
        pltpu.make_async_copy(
            hap_ref.at[pl.ds(start, size)], held.at[pl.ds(start, size)], sems.at[number]
        )
        for number, start in enumerate(starts)
    ]
    copies.append(pltpu.make_async_copy(annot_ref, held_annots, sems.at[2 * CHUNKS]))
    for copy in copies:
        copy.start()
    part = far_ref.shape[0] - rows // 2
    odd = odd_block()

    def store(where, first, second):
        @pl.when(odd)
        def _():
            store_packed(close_ref, far_ref, where, first, second)

        @pl.when(jnp.logical_not(odd))
        def _():
            store_packed(far_ref, close_ref, where, first, second)

    for chunk in range(CHUNKS):
        pair = []
        for side in range(2):
            number = 2 * chunk + side
            copies[number].wait()
            where = slice(starts[number], starts[number] + size)
            values = held[where, :].astype(jnp.float32)
            alleles_ref[where, :] = values.astype(jnp.bfloat16)
            pair.append(values)
        store(slice(chunk * size, (chunk + 1) * size), *pair)
    copies[-1].wait()
    annots = jnp.concatenate(
        [
            held_annots[...].astype(jnp.float32),
            jnp.zeros((2 * part - annot_rows, annot_ref.shape[1]), jnp.float32),
        ],
        axis=0,
    )
    store(slice(rows // 2, rows // 2 + part), annots[:part], annots[part:])


def partner(group, step, groups):
    if groups & (groups - 1) == 0:
        return group ^ step
    return (group + step) % groups


def send_shares(groups, source, share, targets):
    me = lax.axis_index("hap")
    for step, target in enumerate(targets):
        group = partner(me, step, groups)
        rows = source[pl.ds(pl.multiple_of(group * share, 8), share), :]
        target[0:share, :] = rows.astype(target.dtype)


def send_tiles(groups, source, share, targets):
    me = lax.axis_index("hap")
    for step, target in enumerate(targets):
        owner = partner(me, step, groups)
        counts = source[pl.ds(pl.multiple_of(owner * share, 8), share), :]
        for k in range(source.shape[1] // LANES):
            target[k * share : (k + 1) * share, :] = counts[:, k * LANES : (k + 1) * LANES]


def from_tiles(counts, share):
    tiles = counts.shape[0] // share
    return jnp.concatenate([counts[k * share : (k + 1) * share, :] for k in range(tiles)], axis=1)


def own_kernel(groups, share, alleles_ref, label_ref, *refs):
    weighted_ref, totals_ref, *targets = refs[: 2 + groups]
    tile, folded = refs[2 + groups :]
    rows, snps = alleles_ref.shape
    half = snps // 2
    weight = jnp.where(label_ref[...] > 0, float(BASE), 1.0)
    weighted_ref[0:snps, :] = alleles_ref[...].T * weight.astype(jnp.bfloat16)
    extra = weighted_ref.shape[0] - snps
    weighted_ref[snps:, :] = jnp.broadcast_to(weight, (extra, rows)).astype(jnp.bfloat16)
    tile[...] = jnp.dot(weighted_ref[...], alleles_ref[...], preferred_element_type=jnp.float32)
    count = jnp.sum(weight, axis=1, keepdims=True)
    totals_ref[...] = jnp.concatenate(
        [tile[snps : snps + 1, :], jnp.broadcast_to(count, (1, snps)), jnp.zeros((6, snps))], axis=0
    )
    row, col = iota((half, snps), 0), iota((half, snps), 1)
    moved = (col < half) | (col - half > row)
    turned = pltpu.roll(tile[0:half, :], half, 1)
    folded[0:half, :] = to_fields(jnp.where(moved, turned, tile[half:snps, :]))
    if folded.shape[0] > half:
        folded[half:, :] = jnp.zeros((folded.shape[0] - half, snps), jnp.int32)
    if groups != len(LEFT_BLOCKS):
        send_shares(groups, folded, share, targets)
        return
    tiles = snps // LANES
    shared = [totals_ref[0:1, k * LANES : (k + 1) * LANES] for k in range(tiles)]
    shared += [totals_ref[1:2, 0:LANES], jnp.zeros((7 - tiles, LANES))]
    extras = to_fields(jnp.concatenate(shared, axis=0))
    send_tiles(groups, folded, share, targets)
    for target in targets:
        target[tiles * share :, :] = extras


LEFT_BLOCKS = ((0, 1, 2, 3), (2, 3, 6, 7), (4, 0, 1, 2), (6, 0, 4, 5))
RIGHT_BLOCKS = ((2, 3, 6, 7), (4, 5, 6, 7), (0, 1, 2, 4), (0, 4, 5, 6))


SPARE_OWN = ((0, 0, 0, 0), (1, 1, 2, 2), (4, 5, 6, 7), (6, 6, 7, 7))
SPARE_NEAR = ((4, 5, 6, 7), (4, 5, 4, 5), (3, 3, 3, 3), (1, 2, 1, 2))


def fold_spare(tile, spare, first):
    owners = len(SPARE_OWN)
    snps = tile.shape[1]
    size = snps // (2 * owners)
    count = spare.shape[0] // 2
    totals = tile[snps : snps + count - size, :]
    lane = iota((count, snps), 1)
    for number, owner in enumerate(range(first, first + 2)):
        mixed = None
        for slot in range(owners):
            own, near = SPARE_OWN[owner][slot], SPARE_NEAR[owner][slot]
            before = (SPARE_OWN[owner][slot - 1], SPARE_NEAR[owner][slot - 1] + 1) if slot else None
            if before == (own, near):
                continue
            values = jnp.concatenate([tile[own * size : (own + 1) * size, :], totals], axis=0)
            shift = (slot - near) * size % snps
            values = pltpu.roll(values, shift, 1) if shift else values
            mixed = values if mixed is None else jnp.where(lane >= slot * size, values, mixed)
        spare[number * count : (number + 1) * count, :] = to_fields(mixed[:, 0 : spare.shape[1]])


def fold_by_column(tile, flipped, folded, first):
    groups = len(LEFT_BLOCKS)
    owners = range(first, first + groups // 2)
    snps = folded.shape[1]
    wide = snps // groups
    size = wide // 2
    shape = (size, snps)
    row, lane = iota(shape, 0), iota(shape, 1)

    def block(number):
        return tile[number * size : (number + 1) * size, :]

    diagonal, within = block(2 * first), lane - 2 * first * size
    for number in range(2 * first + 1, 2 * first + groups):
        diagonal = jnp.where(lane >= number * size, block(number), diagonal)
        within = jnp.where(lane >= number * size, lane - number * size, within)
    apart = jnp.sum(jnp.where(row == within, diagonal, 0.0), axis=0, keepdims=True)
    flipped[:, 0:size] = diagonal.T
    corner = diagonal
    for owner in owners:
        start = (2 * owner + 1) * size
        turned = jnp.concatenate(
            [flipped[start : start + size, :], jnp.zeros((size, snps - LANES), jnp.float32)], axis=1
        )
        if owner:
            turned = pltpu.roll(turned, owner * wide, 1)
        inside = lane - owner * wide
        other = (row <= inside) if first == 0 else (row >= inside)
        corner = jnp.where((inside >= 0) & (inside < size) & other, turned, corner)
    rolled = []
    for shift in range(groups):
        mixed = None
        for owner in owners:
            slot = (owner + shift) % groups
            left = block(LEFT_BLOCKS[owner][slot]) if slot else corner
            start = owner * wide
            mixed = left if mixed is None else jnp.where(lane >= start, left, mixed)
            mixed = jnp.where(lane >= start + size, block(RIGHT_BLOCKS[owner][slot]), mixed)
        rolled.append(pltpu.roll(mixed, shift * wide, 1) if shift else mixed)
    for number, owner in enumerate(owners):
        mixed = rolled[(0 - owner) % groups]
        for slot in range(1, groups):
            mixed = jnp.where(lane >= slot * wide, rolled[(slot - owner) % groups], mixed)
        folded[number * size : (number + 1) * size, :] = to_fields(mixed)
    return apart


def above(far):
    return odd_block() == far


def side_dot(weighted_ref, side_ref):
    rows = weighted_ref.shape[1]
    half = rows // 2

    def dot(which, columns):
        return jnp.dot(
            weighted_ref[:, which], side_ref[0:half, columns], preferred_element_type=jnp.float32
        )

    first = dot(slice(0, half), slice(0, 2 * LANES))
    second = dot(slice(half, rows), slice(LANES, 3 * LANES))
    whole = first[:, 0:LANES] + second[:, LANES:]
    return whole, first[:, LANES:] + pltpu.roll(second[:, 0:LANES], HALF_LANES, 1)


def fold_side(far, weighted_ref, side_ref, main, spare, lines, tile, flipped):
    snps = tile.shape[1]
    whole, shared = side_dot(weighted_ref, side_ref)
    tile[:, LANES : 2 * LANES] = shared

    def fold(first, start):
        tile[:, start : start + LANES] = whole
        apart = fold_by_column(tile, flipped, main, first)
        fold_spare(tile, spare, 2 - first)
        lines[0:1, :] = tile[snps : snps + 1, :]
        lines[1:2, :] = apart

    @pl.when(above(far))
    def _():
        fold(0, 0)

    @pl.when(jnp.logical_not(above(far)))
    def _():
        fold(2, 2 * LANES)


def close_kernel(groups, reach_ref, weighted_ref, side_ref, annot_ref, *refs):
    main_ref, spare_ref, lines_ref, annots, masks_ref, spare_mask_ref, own_rows_ref, tile, flipped = refs
    fold_side(False, weighted_ref, side_ref, main_ref, spare_ref, lines_ref, tile, flipped)
    snps = annot_ref.shape[1]
    half, wide = snps // 2, snps // groups
    size = wide // 2
    own = annot_ref[...].astype(jnp.float32)
    own = jnp.concatenate([own, jnp.zeros((LANES - own.shape[0], snps), jnp.float32)], axis=0)
    annots[...] = own.T

    me = lax.axis_index("hap")
    block = lax.axis_index("snp")
    last = reach_ref.shape[0] - 1
    upper = me < groups // 2
    reach_here = reach_ref[block]
    reach_there = jnp.where(
        upper, reach_ref[jnp.minimum(block + 1, last)], reach_ref[jnp.maximum(block - 1, 0)]
    )
    left_places, right_places = owner_places(groups, size)
    local, lane = iota((size, LANES), 0), iota((size, LANES), 1)
    own_row = jnp.concatenate(
        [local + jnp.where(lane < size, a, b) for a, b in zip(left_places, right_places)], axis=0
    )
    shape = own_row.shape
    lane = iota(shape, 1)
    apart = jnp.abs(own_row - (lane + me * wide))
    ahead = (own_row - (lane + me * wide)) * jnp.where(upper, 1, -1) > 0
    real = ahead & (lane < wide) & ((lane >= size) | (iota(shape, 0) < groups * size))
    inside = (own_row - half) * jnp.where(upper, 1, -1) < jnp.where(upper, 0, 1)
    masks_ref[0] = jnp.where(real & inside & (snps - apart <= reach_here), 1.0, 0.0)
    masks_ref[1] = jnp.where(real & (snps - apart <= reach_there), 1.0, 0.0)
    own_rows = rows_at(annots, left_places, size) + pltpu.roll(
        rows_at(annots, right_places, size), HALF_LANES, 1
    )
    own_rows_ref[...] = own_rows.astype(jnp.bfloat16)

    own_places, near_places = spare_places(groups, size)
    shape = spare_mask_ref.shape
    local, lane = iota(shape, 0), iota(shape, 1)
    own_row = by_slot([local + place for place in own_places], lane, size)
    near_col = by_slot(
        [lane + (place - slot * size) for slot, place in enumerate(near_places)], lane, size
    )
    close = snps - jnp.abs(own_row - near_col) <= reach_here
    spare_mask_ref[...] = jnp.where(close & (lane < groups * size), 1.0, 0.0)


def by_slot(values, lane, size):
    mixed = values[0]
    for slot in range(1, len(values)):
        mixed = jnp.where(lane >= slot * size, values[slot], mixed)
    return mixed


def far_kernel(groups, share, weighted_ref, side_ref, close_ref, close_spare_ref, close_lines_ref, totals_ref, *refs):
    targets, (main, spare, lines, tile, flipped, extras) = refs[:groups], refs[groups:]
    fold_side(True, weighted_ref, side_ref, main, spare, lines, tile, flipped)
    snps = tile.shape[1]
    half, size = snps // 2, share
    odd = odd_block()

    tiles = snps // LANES
    count = spare.shape[0] // 2
    from_far = (iota((8, snps), 1) < half) == odd
    by_column = jnp.concatenate(
        [totals_ref[1:2, :], jnp.where(from_far, lines[...], close_lines_ref[...])[0:2, :]], axis=0
    )
    by_column = jnp.concatenate([by_column, jnp.zeros((5, snps))], axis=0)
    for owner in range(groups):
        start = owner * (snps // groups)
        columns = pltpu.roll(by_column, snps - start, 1) if owner else by_column
        where = slice((owner & 1) * count + size, (owner & 1) * count + size + 1)
        second = odd if owner >= groups // 2 else jnp.logical_not(odd)
        spare_totals = jnp.where(second, spare[where, :], close_spare_ref[where, :])
        extras[8 * owner : 8 * (owner + 1), :] = jnp.concatenate(
            [
                to_fields(columns[0:3, 0:LANES]),
                spare_totals[:, 0:LANES],
                spare_totals[:, LANES:],
                jnp.zeros((3, LANES), jnp.int32),
            ],
            axis=0,
        )
    me = lax.axis_index("hap")
    left = iota((size // 2, LANES), 1) < HALF_LANES
    for step, target in enumerate(targets):
        owner = partner(me, step, groups)
        first = (owner < groups // 2) == odd
        where = pl.ds(pl.multiple_of((owner & 1) * size, 8), size)
        counts = jnp.where(first, main[where, :], close_ref[where, :])
        for k in range(tiles):
            target[k * size : (k + 1) * size, :] = counts[:, k * LANES : (k + 1) * LANES]
        where = pl.ds(pl.multiple_of((owner & 1) * count, 8), size)
        counts = jnp.where(first, close_spare_ref[where, :], spare[where, :])
        start = tiles * size
        target[start : start + size, :] = counts[:, 0:LANES]
        rest = counts[:, LANES:]
        target[start + size : start + size + size // 2, :] = jnp.where(
            left, rest[0 : size // 2], pltpu.roll(rest[size // 2 :], HALF_LANES, 1)
        )
        target[start + size + size // 2 :, :] = extras[pl.ds(pl.multiple_of(owner * 8, 8), 8), :]


def near_kernel(groups, share, weighted_ref, far_ref, close_ref, totals_ref, *refs):
    own_parts, own_sum_ref = refs[:groups], refs[groups]
    targets, (near, tile, folded) = refs[groups + 1 : 2 * groups + 1], refs[2 * groups + 1 :]
    rows, snps = near.shape
    half = snps // 2
    odd = odd_block()

    def unpack(up_ref, down_ref):
        pieces = load_packed(up_ref[0 : rows // 2, :], down_ref[0 : rows // 2, :])
        for side in range(2):
            where = slice(side * (rows // 2), (side + 1) * (rows // 2))
            for number in range(3):
                near[where, number * LANES : (number + 1) * LANES] = pieces[side][number]

    @pl.when(odd)
    def _():
        unpack(far_ref, close_ref)

    @pl.when(jnp.logical_not(odd))
    def _():
        unpack(close_ref, far_ref)

    tile[...] = jnp.dot(weighted_ref[...], near[...], preferred_element_type=jnp.float32)
    row, col = iota((half, snps), 0), iota((half, snps), 1)
    moved = (col >= half) & (col - half < row)
    turned = pltpu.roll(tile[0:half, :], half, 1)
    folded[0:half, :] = to_fields(jnp.where(moved, turned, tile[half:snps, :]))
    if folded.shape[0] > half:
        folded[half:, :] = jnp.zeros((folded.shape[0] - half, snps), jnp.int32)
    square = (snps, snps)
    far = jnp.sum(
        jnp.where(iota(square, 0) == iota(square, 1), tile[0:snps, :], 0.0), axis=0, keepdims=True
    )
    extras = to_fields(
        jnp.concatenate(
            [totals_ref[0:2, :], tile[snps : snps + 1, :], far, jnp.zeros((4, snps))], axis=0
        )
    )
    send_shares(groups, folded, share, targets)
    for target in targets:
        target[share:, :] = extras
    own_sum_ref[...] = sum((part[...] for part in own_parts[1:]), own_parts[0][...])


def annots_kernel(annot_ref, far_ref, close_ref, own_ref, near_ref):
    snps = annot_ref.shape[1]
    own = annot_ref[...].astype(jnp.float32)
    own = jnp.concatenate([own, jnp.zeros((LANES - own.shape[0], snps), jnp.float32)], axis=0)
    own_ref[...] = own.T
    near_ref[...] = near_annots_by_snp(far_ref, close_ref)


def near_annots_by_snp(far_ref, close_ref):
    part, snps = far_ref.shape
    wide = 2 * part
    odd = odd_block()
    far, close = far_ref[...].astype(jnp.float32), close_ref[...].astype(jnp.float32)
    first, second = load_packed(jnp.where(odd, far, close), jnp.where(odd, close, far))
    near = jnp.concatenate(
        [
            jnp.concatenate([piece.astype(jnp.float32) for piece in first], axis=1),
            jnp.concatenate([piece.astype(jnp.float32) for piece in second], axis=1),
            jnp.zeros((LANES - wide, snps), jnp.float32),
        ],
        axis=0,
    )
    return near.T


def column_stats(totals, count):
    size = jnp.maximum(count, 1.0)
    frequency = totals / size
    variance = jnp.maximum(frequency * (1.0 - frequency), VARIANCE_FLOOR)
    inverse = 1.0 / jnp.sqrt(size * variance)
    low = ((0.0 - frequency) * inverse).astype(jnp.bfloat16).astype(jnp.float32)
    high = ((1.0 - frequency) * inverse).astype(jnp.bfloat16).astype(jnp.float32)
    step = high - low
    root = 1.0 / jnp.sqrt(size)
    return step, step * totals * root, (low * count + step * totals) * root


def correlation(row, col, count):
    return row[0] * col[0] * count - row[1] * col[1] + row[2] * col[2]


def split(values):
    high = values.astype(jnp.bfloat16)
    return high, (values - high.astype(jnp.float32)).astype(jnp.bfloat16)


def dot_split(values, right, axis):
    dims = (((axis,), (0,)), ((), ()))
    return sum(
        lax.dot_general(part, right, dims, preferred_element_type=jnp.float32)
        for part in split(values)
    )


def score_kernel(groups, share, reach_ref, *refs):
    own_sum_ref, near_parts = refs[0], refs[1 : groups + 1]
    annot_ref, near_annot_ref = refs[groups + 1 : groups + 3]
    targets = refs[groups + 3 : 2 * groups + 3]
    table, annots, near_annots, scores = refs[2 * groups + 3 :]
    snps = annot_ref.shape[0]
    half = snps // 2
    out_share = snps // groups
    me = lax.axis_index("hap")
    block = lax.axis_index("snp")
    last = reach_ref.shape[0] - 1
    reach_here = reach_ref[block]
    reach_up = reach_ref[jnp.minimum(block + 1, last)]
    reach_down = reach_ref[jnp.maximum(block - 1, 0)]

    own_counts = own_sum_ref[...]
    near_sums = sum((part[...] for part in near_parts[1:]), near_parts[0][...])
    extras = from_fields(near_sums[share:, :])
    near_counts = near_sums[0:share, :]

    own_stats, near_stats, lines = [], [], []
    for pop in range(2):
        count = extras[pop][1:2, :]
        own_stats.append(column_stats(extras[pop][0:1, :], count))
        near_stats.append(column_stats(extras[pop][2:3, :], count))
        lines += [*own_stats[pop], *near_stats[pop], extras[pop][0:1, :], extras[pop][3:4, :]]
    by_row = jnp.concatenate(lines, axis=0).T
    table[0:snps, 0:16] = by_row
    if table.shape[0] > snps:
        table[snps:, 0:16] = jnp.zeros((table.shape[0] - snps, 16), jnp.float32)
    annots[0:snps, :] = annot_ref[...]
    near_annots[0:snps, :] = near_annot_ref[...]
    if annots.shape[0] > snps:
        annots[snps:, :] = jnp.zeros((annots.shape[0] - snps, LANES), jnp.float32)

    low_rows = pl.multiple_of(me * share, 8)
    high_rows = pl.multiple_of(half + me * share, 8)

    def both(ref):
        return jnp.concatenate([ref[pl.ds(low_rows, share), :], ref[pl.ds(high_rows, share), :]], axis=0)

    here = both(table)
    own_count = jnp.concatenate([pltpu.roll(own_counts, half, 1), own_counts], axis=0)
    near_count = jnp.concatenate([pltpu.roll(near_counts, half, 1), near_counts], axis=0)
    shape = (2 * share, snps)
    local, col = iota(shape, 0), iota(shape, 1)
    low = local < share
    place = jnp.where(low, local, local - share) + me * share
    row = jnp.where(low, place, place + half)
    own_fields, near_fields = from_fields(own_count), from_fields(near_count)
    own_product, near_product = 1.0, 1.0
    for pop in range(2):
        row_stats = [here[:, 8 * pop + k : 8 * pop + k + 1] for k in range(3)]
        own_product *= correlation(row_stats, own_stats[pop], own_fields[pop])
        near_product *= correlation(row_stats, near_stats[pop], near_fields[pop])
    real = place < half
    own_inside = real & ((low & (col > row)) | (~low & (col >= half) & (col < row)))
    own_inside &= jnp.abs(col - row) <= reach_here
    own_kept = jnp.where(own_inside, own_product, 0.0)
    in_upper = col < half
    near_inside = real & ((low & (col < row)) | (~low & (in_upper | (col > row))))
    distance = jnp.where(in_upper, snps + col - row, snps + row - col)
    near_here = jnp.where(near_inside & (distance <= reach_here), near_product, 0.0)
    reach_there = jnp.where(in_upper, reach_up, reach_down)
    near_there = jnp.where(near_inside & (distance <= reach_there), near_product, 0.0)

    rows_here = both(annots)
    rows_there = pltpu.roll(rows_here, HALF_LANES, 1)
    scores[0:snps, :] = dot_split(
        jnp.concatenate([own_kept, near_there], axis=0),
        jnp.concatenate([rows_here, rows_there], axis=0).astype(jnp.bfloat16),
        0,
    )
    direct = dot_split(
        jnp.concatenate([own_kept, near_here], axis=1),
        jnp.concatenate([annot_ref[...], near_annot_ref[...]], axis=0).astype(jnp.bfloat16),
        1,
    )
    scores[pl.ds(low_rows, share), :] += direct[0:share, :]
    scores[pl.ds(high_rows, share), :] += direct[share:, :]

    out_rows = pl.ds(pl.multiple_of(me * out_share, 8), out_share)
    mine = table[out_rows, :]
    self_product, far_product = 1.0, 1.0
    for pop in range(2):
        k = 8 * pop
        own_row = [mine[:, k + s : k + s + 1] for s in range(3)]
        near_row = [mine[:, k + 3 + s : k + 4 + s] for s in range(3)]
        self_product *= correlation(own_row, own_row, mine[:, k + 6 : k + 7])
        far_product *= correlation(own_row, near_row, mine[:, k + 7 : k + 8])
    mine_annots = annots[out_rows, :]
    far_reach = jnp.where(me < groups // 2, reach_up, reach_down)
    scores[out_rows, :] += (
        mine_annots * self_product
        + near_annots[out_rows, :] * jnp.where(reach_here >= snps, far_product, 0.0)
        + pltpu.roll(mine_annots, HALF_LANES, 1) * jnp.where(far_reach >= snps, far_product, 0.0)
    )
    send_shares(groups, scores, out_share, targets)


def pack_halves(values):
    half = values.shape[0] // 2
    left = iota((half, LANES), 1) < HALF_LANES
    return jnp.where(left, values[0:half], pltpu.roll(values[half:], HALF_LANES, 1))


def unpack_halves(packed):
    return jnp.concatenate([packed, pltpu.roll(packed, HALF_LANES, 1)], axis=0)


def dot_rounded(values, right, axis):
    dims = (((axis,), (0,)), ((), ()))
    return lax.dot_general(
        values.astype(jnp.bfloat16), right, dims, preferred_element_type=jnp.float32
    )


def owner_places(groups, size):
    me = lax.axis_index("hap")

    def mine(blocks, slot):
        value = blocks[0][slot]
        for group in range(1, groups):
            value = jnp.where(me == group, blocks[group][slot], value)
        return value * size

    left = [mine(LEFT_BLOCKS, slot) for slot in range(groups)]
    right = [mine(RIGHT_BLOCKS, slot) for slot in range(groups)]
    return left + left[0:1], right + [(2 * me + 1) * size]


def spare_places(groups, size):
    me = lax.axis_index("hap")

    def mine(blocks, slot):
        value = blocks[0][slot]
        for group in range(1, groups):
            value = jnp.where(me == group, blocks[group][slot], value)
        return value * size

    return [[mine(blocks, slot) for slot in range(groups)] for blocks in (SPARE_OWN, SPARE_NEAR)]


def rows_at(ref, places, size):
    return jnp.concatenate([ref[pl.ds(pl.multiple_of(place, 8), size), :] for place in places], axis=0)


def own_score_kernel(
    groups, share, reach_ref, *refs
):
    own_parts, refs = refs[:groups], refs[groups:]
    annot_ref, far_ref, close_ref, scores, mine_ref, rows_ref, columns_ref, *refs = refs
    spare_rows_ref, spare_columns_ref, near_annot_ref, *targets, table = refs
    near_annot_ref[...] = near_annots_by_snp(far_ref, close_ref)
    snps = annot_ref.shape[0]
    half = snps // 2
    wide = snps // groups
    tiles = snps // LANES
    me = lax.axis_index("hap")
    reach_here = reach_ref[lax.axis_index("snp")]
    own_sums = sum((part[...] for part in own_parts[1:]), own_parts[0][...])
    own_counts = from_tiles(own_sums[0 : tiles * share, :], share)
    extras = from_fields(own_sums[tiles * share :, :])

    own_stats, lines = [], []
    for pop in range(2):
        count = jnp.concatenate([extras[pop][tiles : tiles + 1, :]] * tiles, axis=1)
        totals = jnp.concatenate([extras[pop][k : k + 1, :] for k in range(tiles)], axis=1)
        own_stats.append(column_stats(totals, count))
        lines += [*own_stats[pop], totals]
    table[:, 0:8] = jnp.concatenate(lines, axis=0).T

    low_rows = pl.multiple_of(me * share, 8)
    high_rows = pl.multiple_of(half + me * share, 8)

    def both(ref):
        return jnp.concatenate([ref[pl.ds(low_rows, share), :], ref[pl.ds(high_rows, share), :]], axis=0)

    here = both(table)
    own_fields = from_fields(
        jnp.concatenate([pltpu.roll(own_counts, half, 1), own_counts], axis=0)
    )
    shape = (2 * share, snps)
    local, col = iota(shape, 0), iota(shape, 1)
    low = local < share
    row = jnp.where(low, local, local + half - share) + me * share
    product = 1.0
    for pop in range(2):
        row_stats = [here[:, 4 * pop + k : 4 * pop + k + 1] for k in range(3)]
        product *= correlation(row_stats, own_stats[pop], own_fields[pop])
    inside = (low & (col > row)) | (~low & (col >= half) & (col < row))
    own_kept = jnp.where(inside & (jnp.abs(col - row) <= reach_here), product, 0.0)
    rows_here = both(annot_ref).astype(jnp.bfloat16)
    scores[...] = dot_rounded(own_kept, rows_here, 0)
    direct = dot_rounded(own_kept, annot_ref[...].astype(jnp.bfloat16), 1)
    scores[pl.ds(low_rows, share), :] += direct[0:share, :]
    scores[pl.ds(high_rows, share), :] += direct[share:, :]

    slice_rows = pl.ds(pl.multiple_of(me * wide, 8), wide)
    mine = table[slice_rows, :]
    mine_ref[...] = mine
    product = 1.0
    for pop in range(2):
        own_row = [mine[:, 4 * pop + k : 4 * pop + k + 1] for k in range(4)]
        product *= correlation(own_row, own_row, own_row[3])
    scores[slice_rows, :] += annot_ref[slice_rows, :] * product
    for step, target in enumerate(targets, 2):
        group = partner(me, step, groups)
        rows = scores[pl.ds(pl.multiple_of(group * wide, 8), wide), :]
        target[...] = pack_halves(rows).astype(target.dtype)

    size = wide // 2
    left_places, right_places = owner_places(groups, size)
    left_table, right_table = rows_at(table, left_places, size), rows_at(table, right_places, size)
    is_left = iota(rows_ref.shape[1:], 1) < size
    for pop in range(2):
        for k in range(3):
            column = slice(4 * pop + k, 4 * pop + k + 1)
            rows_ref[3 * pop + k] = jnp.where(is_left, left_table[:, column], right_table[:, column])
    theirs = near_annot_ref[slice_rows, :]
    columns = [theirs[0:size], pltpu.roll(theirs[size:], HALF_LANES, 1), jnp.zeros((LANES - wide, LANES))]
    columns_ref[...] = jnp.concatenate(columns, axis=0).astype(jnp.bfloat16)

    own_places, near_places = spare_places(groups, size)
    shape = spare_rows_ref.shape[1:]
    lane = iota(shape, 1)
    tables = [table[pl.ds(pl.multiple_of(place, 8), size), :] for place in own_places]
    for pop in range(2):
        for k in range(3):
            column = slice(4 * pop + k, 4 * pop + k + 1)
            spare_rows_ref[3 * pop + k] = by_slot(
                [jnp.broadcast_to(values[:, column], shape) for values in tables], lane, size
            )
    columns = [rows_at(near_annot_ref, near_places, size)]
    columns.append(jnp.zeros((shape[1] - groups * size, LANES), jnp.float32))
    spare_columns_ref[...] = jnp.concatenate(columns, axis=0).astype(jnp.bfloat16)


def near_score_kernel(groups, share, reach_ref, *refs):
    near_parts, refs = refs[:groups], refs[groups:]
    own_ref, mine_ref, rows_ref, columns_ref, spare_rows_ref, spare_columns_ref = refs[:6]
    near_annot_ref, annot_ref, masks_ref, spare_mask_ref, own_rows_ref = refs[6:11]
    out_ref, send_ref, near_out_ref, flipped, scores = refs[11:]
    snps = annot_ref.shape[0]
    wide = snps // groups
    size = wide // 2
    tiles = snps // LANES
    me = lax.axis_index("hap")
    block = lax.axis_index("snp")
    last = reach_ref.shape[0] - 1
    reach_here = reach_ref[block]
    reach_there = jnp.where(
        me < groups // 2, reach_ref[jnp.minimum(block + 1, last)], reach_ref[jnp.maximum(block - 1, 0)]
    )

    scores[...] = own_ref[...]
    near_sums = sum((part[...] for part in near_parts[1:]), near_parts[0][...])
    near_counts = from_tiles(near_sums[0 : tiles * share, :], share)
    start = tiles * share
    rest = near_sums[start + size : start + size + size // 2, :]
    rest = jnp.concatenate([rest, pltpu.roll(rest, HALF_LANES, 1)], axis=0)
    spare_fields = from_fields(jnp.concatenate([near_sums[start : start + size, :], rest], axis=1))
    extras = from_fields(near_sums[start + size + size // 2 :, :])
    near_stats, near_lines, spare_stats = [], [], []
    for pop in range(2):
        count = extras[pop][0:1, :]
        totals = jnp.concatenate([extras[pop][3:4, :], extras[pop][4:5, :]], axis=1)
        spare_stats.append(column_stats(totals, jnp.concatenate([count, count], axis=1)))
        near_stats.append(column_stats(extras[pop][1:2, :], extras[pop][0:1, :]))
        near_lines += [*near_stats[pop], extras[pop][2:3, :]]
    near_table = jnp.concatenate(near_lines, axis=0).T[0:wide, :]

    slots = [near_counts[:, 0:LANES]]
    for slot in range(1, groups):
        slots.append(pltpu.roll(near_counts, snps - slot * wide, 1)[:, 0:LANES])
    flipped[:, 0:size] = slots[0].T
    slots.append(pltpu.roll(flipped[0:size, :], size, 1))
    near_fields = from_fields(jnp.concatenate(slots, axis=0))
    product = 1.0
    for pop in range(2):
        row_stats = [rows_ref[3 * pop + k] for k in range(3)]
        product *= correlation(row_stats, near_stats[pop], near_fields[pop])
    near_here = jnp.where(masks_ref[0] > 0.0, product, 0.0)
    near_there = jnp.where(masks_ref[1] > 0.0, product, 0.0)
    slice_rows = pl.ds(pl.multiple_of(me * wide, 8), wide)
    direct = dot_rounded(near_here, columns_ref[...], 1)
    turned = pltpu.roll(direct, HALF_LANES, 1)
    for values, places in zip((direct, turned), owner_places(groups, size)):
        for slot, place in enumerate(places):
            scores[pl.ds(pl.multiple_of(place, 8), size), :] += values[slot * size : (slot + 1) * size, :]
    product = 1.0
    for pop in range(2):
        row_stats = [spare_rows_ref[3 * pop + k] for k in range(3)]
        product *= correlation(row_stats, spare_stats[pop], spare_fields[pop])
    spare_here = jnp.where(spare_mask_ref[...] > 0.0, product, 0.0)
    lane = iota(spare_here.shape, 1)
    spare_here = [
        jnp.where((lane >= slot * size) & (lane < (slot + 1) * size), spare_here, 0.0)
        for slot in range(groups)
    ]
    direct = dot_rounded(jnp.concatenate(spare_here, axis=0), spare_columns_ref[...], 1)
    for slot, place in enumerate(spare_places(groups, size)[0]):
        scores[pl.ds(pl.multiple_of(place, 8), size), :] += direct[slot * size : (slot + 1) * size, :]
    near_scores = dot_rounded(near_there, own_rows_ref[...], 0)
    near_scores = jnp.where(
        iota((size, LANES), 1) < HALF_LANES, near_scores[0:size], near_scores[size:wide]
    )

    mine_table = mine_ref[...]
    far_product = 1.0
    for pop in range(2):
        own_row = [mine_table[:, 4 * pop + k : 4 * pop + k + 1] for k in range(3)]
        near_row = [near_table[:, 4 * pop + k : 4 * pop + k + 1] for k in range(4)]
        far_product *= correlation(own_row, near_row, near_row[3])
    scores[slice_rows, :] += near_annot_ref[slice_rows, :] * jnp.where(reach_here >= snps, far_product, 0.0)
    far_scores = annot_ref[slice_rows, :] * jnp.where(reach_there >= snps, far_product, 0.0)
    near_out_ref[...] = (near_scores + pack_halves(far_scores)).astype(near_out_ref.dtype)

    def packed(step):
        group = partner(me, step, groups)
        return pack_halves(scores[pl.ds(pl.multiple_of(group * wide, 8), wide), :])

    out_ref[...] = packed(0)
    send_ref[...] = packed(1).astype(send_ref.dtype)


def column_finish_kernel(*refs):
    *parts, out_ref = refs
    packed = sum(part[...].astype(jnp.float32) for part in parts)
    out_ref[...] = unpack_halves(packed).T[0 : out_ref.shape[0], :]


def sum_kernel(*refs):
    *parts, own_ref, there_ref = refs
    total = sum((part[...].astype(jnp.float32) for part in parts[1:]), parts[0][...])
    own_ref[...] = total
    half = there_ref.shape[0]
    left = iota((half, LANES), 1) < HALF_LANES
    second = total[half:]
    if second.shape[0] < half:
        second = jnp.concatenate([second, jnp.zeros((half - second.shape[0], LANES))], axis=0)
    there_ref[...] = jnp.where(left, pltpu.roll(total[0:half], HALF_LANES, 1), second)


def finish_kernel(own_ref, there_ref, out_ref):
    annots, rows = out_ref.shape
    there = there_ref[...]
    there = jnp.concatenate([there, pltpu.roll(there, HALF_LANES, 1)], axis=0)
    out_ref[...] = (own_ref[...] + there[0:rows]).T[0:annots, :]


def around(value, groups, step):
    return lax.ppermute(
        value, "hap", [(source, partner(source, step, groups)) for source in range(groups)]
    )


def swapped(value, first):
    pairs = []
    for block in range(first, lax.axis_size("snp") - 1, 2):
        pairs += [(block, block + 1), (block + 1, block)]
    return lax.ppermute(value, "snp", pairs)


def per_device(haplotypes, labels, annotations, reach):
    rows, snps = haplotypes.shape
    half = snps // 2
    groups = lax.axis_size("hap")
    blocks = lax.axis_size("snp")
    share = round_up(-(-half // groups), 16)
    folded_rows = share * groups
    out_share = snps // groups
    padded = half + folded_rows
    annot_part = 32
    bf16, f32, i32 = jnp.bfloat16, jnp.float32, jnp.int32
    shape = jax.ShapeDtypeStruct

    packed = shape((rows // 2 + annot_part, snps), bf16)
    haplotypes = pltpu.with_memory_space_constraint(haplotypes, pltpu.HBM)
    annots_in = pltpu.with_memory_space_constraint(annotations, pltpu.HBM)
    alleles, far, close = call(
        prepare_kernel,
        [shape((rows, snps), bf16), packed, packed],
        [HBM, HBM],
        [
            pltpu.VMEM((rows, snps), i32),
            pltpu.VMEM(annotations.shape, i32),
            pltpu.SemaphoreType.DMA((2 * CHUNKS + 1,)),
        ],
        moved=rows * snps * 8,
    )(haplotypes, annots_in)
    from_far = swapped(far, 1)
    from_close = swapped(close, 0)

    by_column = groups == len(LEFT_BLOCKS)
    by_snp = shape((snps, LANES), f32)
    compact = shape((share * (snps // LANES) + 8, LANES), i32)
    own_share_counts = compact if by_column else shape((share, snps), i32)
    near_share_counts = shape((compact.shape[0] + share + share // 2, LANES), i32)
    tile = pltpu.VMEM((snps + 16, snps), f32)
    folded = pltpu.VMEM((folded_rows, snps), i32)
    weighted, totals, *own_parts = call(
        functools.partial(own_kernel, groups, share),
        [shape((snps + 16, rows), bf16), shape((8, snps), f32)] + [own_share_counts] * groups,
        [VMEM, VMEM],
        [tile, folded],
        flops=2 * rows * snps * snps,
        moved=rows * snps * 4,
    )(alleles, labels.reshape(1, rows))
    order = (2, 3, 1) if by_column else range(groups - 1, 0, -1)
    own_parts = [own_parts[0]] + [around(own_parts[k], groups, k) for k in order]

    near_shapes = [own_share_counts] + [near_share_counts if by_column else shape((share + 8, snps), i32)] * groups
    if by_column:
        work = dict(flops=4 * rows * snps * LANES, moved=rows * snps * 4)
        flipped = pltpu.VMEM((snps, LANES), f32)
        pair_rows = (groups + 1) * (out_share // 2)
        side_shapes = [((2 * share, snps), i32), ((2 * (share + 8), 2 * LANES), i32), ((8, snps), f32)]
        *close_counts, own_annots, masks, spare_mask, own_rows = call(
            functools.partial(close_kernel, groups),
            [shape(*args) for args in side_shapes]
            + [
                by_snp,
                shape((2, pair_rows, LANES), f32),
                shape((share, 2 * LANES), f32),
                shape((pair_rows, LANES), bf16),
            ],
            [SMEM] + [VMEM] * 3,
            [tile, flipped],
            **work,
        )(reach, weighted, from_close, annotations)
        near_parts = call(
            functools.partial(far_kernel, groups, share),
            near_shapes[1:],
            [VMEM] * 6,
            [pltpu.VMEM(*args) for args in side_shapes]
            + [tile, flipped, pltpu.VMEM((8 * groups, LANES), i32)],
            **work,
        )(weighted, from_far, *close_counts, totals)
    else:
        own_sum, *near_parts = call(
            functools.partial(near_kernel, groups, share),
            near_shapes,
            [VMEM] * (4 + groups),
            [pltpu.VMEM((rows, snps), bf16), tile, folded],
            flops=2 * rows * snps * snps,
            moved=rows * snps * 4,
        )(weighted, from_far, from_close, totals, *own_parts)
    near_parts = [near_parts[0]] + [around(near_parts[k], groups, k) for k in order]

    if not by_column:
        own_annots, near_annots = call(annots_kernel, [by_snp, by_snp], [VMEM] * 3, moved=1 << 20)(
            annotations, from_far[rows // 2 :], from_close[rows // 2 :]
        )
    pairs = []
    for block in range(blocks):
        for group in range(groups):
            target = block + 1 if group < groups // 2 else block - 1
            if 0 <= target < blocks:
                pairs.append((block * groups + group, target * groups + group))

    def to_neighbour(value):
        return lax.ppermute(value, ("snp", "hap"), pairs)

    result = shape((annotations.shape[0], out_share), f32)
    half_share = round_up(-(-out_share // 2), 8)
    own_share = shape((out_share, LANES), f32)
    packed_share = shape((half_share, LANES), f32)
    if by_column:
        sent = shape((half_share, LANES), bf16)
        *prepared, second, third = call(
            functools.partial(own_score_kernel, groups, share),
            [
                by_snp,
                shape((out_share, LANES), f32),
                shape((6, pair_rows, LANES), f32),
                shape((LANES, LANES), bf16),
                shape((6, share, 2 * LANES), f32),
                shape((2 * LANES, LANES), bf16),
                by_snp,
                sent,
                sent,
            ],
            [SMEM] + [VMEM] * (groups + 3),
            [pltpu.VMEM((snps, LANES), f32)],
            flops=1 << 33,
            moved=1 << 20,
        )(reach, *own_parts, own_annots, from_far[rows // 2 :], from_close[rows // 2 :])
        parts = [around(third, groups, 3), around(second, groups, 2)]
        own_scores, send, there = call(
            functools.partial(near_score_kernel, groups, share),
            [packed_share, sent, sent],
            [SMEM] + [VMEM] * (groups + 11),
            [pltpu.VMEM((LANES, LANES), i32), pltpu.VMEM((snps, LANES), f32)],
            flops=1 << 26,
            moved=1 << 21,
        )(reach, *near_parts, *prepared, own_annots, masks, spare_mask, own_rows)
        parts += [around(send, groups, 1), to_neighbour(there)]
        return call(column_finish_kernel, result, [VMEM] * 5)(own_scores, *parts)

    tall = pltpu.VMEM((padded, LANES), f32)
    scores = call(
        functools.partial(score_kernel, groups, share),
        [own_share] + [shape((out_share, LANES), bf16)] * (groups - 1),
        [SMEM] + [VMEM] * (groups + 3),
        [tall, tall, tall, tall],
        flops=1 << 26,
        moved=1 << 21,
    )(reach, own_sum, *near_parts, own_annots, near_annots)
    scores = [scores[0]] + [around(scores[k], groups, k) for k in range(groups - 1, 0, -1)]
    own_scores, near_scores = call(sum_kernel, [own_share, packed_share], [VMEM] * groups)(*scores)
    return call(finish_kernel, result, [VMEM] * 2)(own_scores, to_neighbour(near_scores))


def solution(mesh):
    in_specs = (
        P("hap", ("parts", "snp")),
        P(("parts", "hap")),
        P(None, ("parts", "snp")),
        P("parts"),
    )
    out_specs = P(None, ("parts", "snp", "hap"))
    return jax.shard_map(
        per_device, mesh=mesh, in_specs=in_specs, out_specs=out_specs, check_vma=False
    )
```

```python
import functools

import jax
import jax.numpy as jnp
from jax import lax
from jax.experimental import pallas as pl
from jax.experimental.pallas import tpu as pltpu
from jax.sharding import PartitionSpec as P

VARIANCE_FLOOR = 0.01
BASE_BITS = 12
BASE = 1 << BASE_BITS
FIELD_BITS = 16
LANES = 128
HALF_LANES = LANES // 2
CHUNKS = (6, 5, 3, 2)
VMEM = pl.BlockSpec(memory_space=pltpu.VMEM)
SMEM = pl.BlockSpec(memory_space=pltpu.SMEM)
HBM = pl.BlockSpec(memory_space=pltpu.HBM)
VMEM_LIMIT = 24 * 1024 * 1024


def iota(shape, axis):
    return lax.broadcasted_iota(jnp.int32, shape, axis)


def round_up(value, step):
    return -(-value // step) * step


def to_fields(values):
    whole = values.astype(jnp.int32)
    return whole + (whole >> BASE_BITS) * ((1 << FIELD_BITS) - BASE)


def from_fields(packed):
    first = packed & ((1 << FIELD_BITS) - 1)
    second = lax.shift_right_logical(packed, FIELD_BITS)
    return first.astype(jnp.float32), second.astype(jnp.float32)


def call(kernel, out_shape, in_specs, scratch_shapes=(), flops=0, moved=0):
    several = isinstance(out_shape, (list, tuple))
    return pl.pallas_call(
        kernel,
        out_shape=out_shape,
        in_specs=in_specs,
        out_specs=[VMEM] * len(out_shape) if several else VMEM,
        scratch_shapes=list(scratch_shapes),
        compiler_params=pltpu.CompilerParams(vmem_limit_bytes=VMEM_LIMIT),
        cost_estimate=pl.CostEstimate(flops=flops, bytes_accessed=moved, transcendentals=0),
    )


def odd_block():
    return lax.rem(lax.axis_index("snp"), 2) == 1


def store_packed(up_ref, down_ref, where, first, second):
    left = iota((first.shape[0], LANES), 1) < HALF_LANES
    middle = first[:, LANES : 2 * LANES]
    turned = pltpu.roll(second[:, LANES : 2 * LANES], HALF_LANES, 1)
    for ref, side, mixed in (
        (up_ref, slice(0, LANES), jnp.where(left, middle, turned)),
        (down_ref, slice(2 * LANES, 3 * LANES), jnp.where(left, turned, middle)),
    ):
        ref[where, 0:LANES] = first[:, side].astype(jnp.bfloat16)
        ref[where, LANES : 2 * LANES] = mixed.astype(jnp.bfloat16)
        ref[where, 2 * LANES : 3 * LANES] = second[:, side].astype(jnp.bfloat16)


def load_packed(up, down):
    left = iota((up.shape[0], LANES), 1) < HALF_LANES
    up_mixed, down_mixed = up[:, LANES : 2 * LANES], down[:, LANES : 2 * LANES]
    first = jnp.where(left, up_mixed, down_mixed)
    second = jnp.where(left, down_mixed, up_mixed)
    second = pltpu.roll(second.astype(jnp.float32), HALF_LANES, 1).astype(second.dtype)
    return (
        (up[:, :LANES], first, down[:, :LANES]),
        (up[:, 2 * LANES :], second, down[:, 2 * LANES :]),
    )


def prepare_kernel(hap_ref, annot_ref, alleles_ref, far_ref, close_ref, held, held_annots, sems):
    rows = hap_ref.shape[0]
    annot_rows = annot_ref.shape[0]
    sizes = [chunk * (rows // 32) for chunk in CHUNKS]
    places = [sum(sizes[:number]) for number in range(len(sizes))]
    pieces = [
        (side * (rows // 2) + place, size) for place, size in zip(places, sizes) for side in range(2)
    ]
    copies = [
        pltpu.make_async_copy(
            hap_ref.at[pl.ds(start, size)], held.at[pl.ds(start, size)], sems.at[number]
        )
        for number, (start, size) in enumerate(pieces)
    ]
    copies.append(pltpu.make_async_copy(annot_ref, held_annots, sems.at[len(pieces)]))
    for copy in copies:
        copy.start()
    part = far_ref.shape[0] - rows // 2
    odd = odd_block()

    def store(where, first, second):
        @pl.when(odd)
        def _():
            store_packed(close_ref, far_ref, where, first, second)

        @pl.when(jnp.logical_not(odd))
        def _():
            store_packed(far_ref, close_ref, where, first, second)

    for chunk, (place, size) in enumerate(zip(places, sizes)):
        pair = []
        for number in (2 * chunk, 2 * chunk + 1):
            copies[number].wait()
            where = slice(pieces[number][0], pieces[number][0] + size)
            values = held[where, :].astype(jnp.float32)
            alleles_ref[where, :] = values.astype(jnp.bfloat16)
            pair.append(values)
        store(slice(place, place + size), *pair)
    copies[-1].wait()
    annots = jnp.concatenate(
        [
            held_annots[...].astype(jnp.float32),
            jnp.zeros((2 * part - annot_rows, annot_ref.shape[1]), jnp.float32),
        ],
        axis=0,
    )
    store(slice(rows // 2, rows // 2 + part), annots[:part], annots[part:])


def partner(group, step, groups):
    if groups & (groups - 1) == 0:
        return group ^ step
    return (group + step) % groups


def send_shares(groups, source, share, targets):
    me = lax.axis_index("hap")
    for step, target in enumerate(targets):
        group = partner(me, step, groups)
        rows = source[pl.ds(pl.multiple_of(group * share, 8), share), :]
        target[0:share, :] = rows.astype(target.dtype)


def send_tiles(groups, source, share, targets):
    me = lax.axis_index("hap")
    for step, target in enumerate(targets):
        owner = partner(me, step, groups)
        counts = source[pl.ds(pl.multiple_of(owner * share, 8), share), :]
        for k in range(source.shape[1] // LANES):
            target[k * share : (k + 1) * share, :] = counts[:, k * LANES : (k + 1) * LANES]


def from_tiles(counts, share):
    tiles = counts.shape[0] // share
    return jnp.concatenate([counts[k * share : (k + 1) * share, :] for k in range(tiles)], axis=1)


def own_kernel(groups, share, alleles_ref, label_ref, *refs):
    weighted_ref, totals_ref, *targets = refs[: 2 + groups]
    tile, folded = refs[2 + groups :]
    rows, snps = alleles_ref.shape
    half = snps // 2
    weight = jnp.where(label_ref[...] > 0, float(BASE), 1.0)
    weighted_ref[0:snps, :] = alleles_ref[...].T * weight.astype(jnp.bfloat16)
    extra = weighted_ref.shape[0] - snps
    weighted_ref[snps:, :] = jnp.broadcast_to(weight, (extra, rows)).astype(jnp.bfloat16)
    tile[...] = jnp.dot(weighted_ref[...], alleles_ref[...], preferred_element_type=jnp.float32)
    count = jnp.sum(weight, axis=1, keepdims=True)
    totals_ref[...] = jnp.concatenate(
        [tile[snps : snps + 1, :], jnp.broadcast_to(count, (1, snps)), jnp.zeros((6, snps))], axis=0
    )
    row, col = iota((half, snps), 0), iota((half, snps), 1)
    moved = (col < half) | (col - half > row)
    turned = pltpu.roll(tile[0:half, :], half, 1)
    folded[0:half, :] = to_fields(jnp.where(moved, turned, tile[half:snps, :]))
    if folded.shape[0] > half:
        folded[half:, :] = jnp.zeros((folded.shape[0] - half, snps), jnp.int32)
    if groups != len(LEFT_BLOCKS):
        send_shares(groups, folded, share, targets)
        return
    tiles = snps // LANES
    shared = [totals_ref[0:1, k * LANES : (k + 1) * LANES] for k in range(tiles)]
    shared += [totals_ref[1:2, 0:LANES], jnp.zeros((7 - tiles, LANES))]
    extras = to_fields(jnp.concatenate(shared, axis=0))
    send_tiles(groups, folded, share, targets)
    for target in targets:
        target[tiles * share :, :] = extras


LEFT_BLOCKS = ((0, 1, 2, 3), (2, 3, 6, 7), (4, 0, 1, 2), (6, 0, 4, 5))
RIGHT_BLOCKS = ((2, 3, 6, 7), (4, 5, 6, 7), (0, 1, 2, 4), (0, 4, 5, 6))


SPARE_OWN = ((0, 0, 0, 0), (1, 1, 2, 2), (4, 5, 6, 7), (6, 6, 7, 7))
SPARE_NEAR = ((4, 5, 6, 7), (4, 5, 4, 5), (3, 3, 3, 3), (1, 2, 1, 2))


def fold_spare(tile, spare, first):
    owners = len(SPARE_OWN)
    snps = tile.shape[1]
    size = snps // (2 * owners)
    count = spare.shape[0] // 2
    totals = tile[snps : snps + count - size, :]
    lane = iota((count, snps), 1)
    for number, owner in enumerate(range(first, first + 2)):
        mixed = None
        for slot in range(owners):
            own, near = SPARE_OWN[owner][slot], SPARE_NEAR[owner][slot]
            before = (SPARE_OWN[owner][slot - 1], SPARE_NEAR[owner][slot - 1] + 1) if slot else None
            if before == (own, near):
                continue
            values = jnp.concatenate([tile[own * size : (own + 1) * size, :], totals], axis=0)
            shift = (slot - near) * size % snps
            values = pltpu.roll(values, shift, 1) if shift else values
            mixed = values if mixed is None else jnp.where(lane >= slot * size, values, mixed)
        spare[number * count : (number + 1) * count, :] = to_fields(mixed[:, 0 : spare.shape[1]])


def fold_by_column(tile, flipped, folded, first):
    groups = len(LEFT_BLOCKS)
    owners = range(first, first + groups // 2)
    snps = folded.shape[1]
    wide = snps // groups
    size = wide // 2
    shape = (size, snps)
    row, lane = iota(shape, 0), iota(shape, 1)

    def block(number):
        return tile[number * size : (number + 1) * size, :]

    diagonal, within = block(2 * first), lane - 2 * first * size
    for number in range(2 * first + 1, 2 * first + groups):
        diagonal = jnp.where(lane >= number * size, block(number), diagonal)
        within = jnp.where(lane >= number * size, lane - number * size, within)
    apart = jnp.sum(jnp.where(row == within, diagonal, 0.0), axis=0, keepdims=True)
    flipped[:, 0:size] = diagonal.T
    corner = diagonal
    for owner in owners:
        start = (2 * owner + 1) * size
        turned = jnp.concatenate(
            [flipped[start : start + size, :], jnp.zeros((size, snps - LANES), jnp.float32)], axis=1
        )
        if owner:
            turned = pltpu.roll(turned, owner * wide, 1)
        inside = lane - owner * wide
        other = (row <= inside) if first == 0 else (row >= inside)
        corner = jnp.where((inside >= 0) & (inside < size) & other, turned, corner)
    rolled = []
    for shift in range(groups):
        mixed = None
        for owner in owners:
            slot = (owner + shift) % groups
            left = block(LEFT_BLOCKS[owner][slot]) if slot else corner
            start = owner * wide
            mixed = left if mixed is None else jnp.where(lane >= start, left, mixed)
            mixed = jnp.where(lane >= start + size, block(RIGHT_BLOCKS[owner][slot]), mixed)
        rolled.append(pltpu.roll(mixed, shift * wide, 1) if shift else mixed)
    for number, owner in enumerate(owners):
        mixed = rolled[(0 - owner) % groups]
        for slot in range(1, groups):
            mixed = jnp.where(lane >= slot * wide, rolled[(slot - owner) % groups], mixed)
        folded[number * size : (number + 1) * size, :] = to_fields(mixed)
    return apart


def above(far):
    return odd_block() == far


def side_dot(weighted_ref, side_ref):
    rows = weighted_ref.shape[1]
    half = rows // 2

    def dot(which, columns):
        return jnp.dot(
            weighted_ref[:, which], side_ref[0:half, columns], preferred_element_type=jnp.float32
        )

    first = dot(slice(0, half), slice(0, 2 * LANES))
    second = dot(slice(half, rows), slice(LANES, 3 * LANES))
    whole = first[:, 0:LANES] + second[:, LANES:]
    return whole, first[:, LANES:] + pltpu.roll(second[:, 0:LANES], HALF_LANES, 1)


def fold_side(far, weighted_ref, side_ref, main, spare, lines, tile, flipped):
    snps = tile.shape[1]
    whole, shared = side_dot(weighted_ref, side_ref)
    tile[:, LANES : 2 * LANES] = shared

    def fold(first, start):
        tile[:, start : start + LANES] = whole
        apart = fold_by_column(tile, flipped, main, first)
        fold_spare(tile, spare, 2 - first)
        lines[0:1, :] = tile[snps : snps + 1, :]
        lines[1:2, :] = apart

    @pl.when(above(far))
    def _():
        fold(0, 0)

    @pl.when(jnp.logical_not(above(far)))
    def _():
        fold(2, 2 * LANES)


def close_kernel(groups, reach_ref, weighted_ref, side_ref, annot_ref, *refs):
    main_ref, spare_ref, lines_ref, annots, masks_ref, spare_mask_ref, own_rows_ref, tile, flipped = refs
    fold_side(False, weighted_ref, side_ref, main_ref, spare_ref, lines_ref, tile, flipped)
    snps = annot_ref.shape[1]
    half, wide = snps // 2, snps // groups
    size = wide // 2
    own = annot_ref[...].astype(jnp.float32)
    own = jnp.concatenate([own, jnp.zeros((LANES - own.shape[0], snps), jnp.float32)], axis=0)
    annots[...] = own.T

    me = lax.axis_index("hap")
    block = lax.axis_index("snp")
    last = reach_ref.shape[0] - 1
    upper = me < groups // 2
    reach_here = reach_ref[block]
    reach_there = jnp.where(
        upper, reach_ref[jnp.minimum(block + 1, last)], reach_ref[jnp.maximum(block - 1, 0)]
    )
    left_places, right_places = owner_places(groups, size)
    local, lane = iota((size, LANES), 0), iota((size, LANES), 1)
    own_row = jnp.concatenate(
        [local + jnp.where(lane < size, a, b) for a, b in zip(left_places, right_places)], axis=0
    )
    shape = own_row.shape
    lane = iota(shape, 1)
    apart = jnp.abs(own_row - (lane + me * wide))
    ahead = (own_row - (lane + me * wide)) * jnp.where(upper, 1, -1) > 0
    real = ahead & (lane < wide) & ((lane >= size) | (iota(shape, 0) < groups * size))
    inside = (own_row - half) * jnp.where(upper, 1, -1) < jnp.where(upper, 0, 1)
    masks_ref[0] = jnp.where(real & inside & (snps - apart <= reach_here), 1.0, 0.0)
    masks_ref[1] = jnp.where(real & (snps - apart <= reach_there), 1.0, 0.0)
    own_rows = rows_at(annots, left_places, size) + pltpu.roll(
        rows_at(annots, right_places, size), HALF_LANES, 1
    )
    own_rows_ref[...] = own_rows.astype(jnp.bfloat16)

    own_places, near_places = spare_places(groups, size)
    shape = spare_mask_ref.shape
    local, lane = iota(shape, 0), iota(shape, 1)
    own_row = by_slot([local + place for place in own_places], lane, size)
    near_col = by_slot(
        [lane + (place - slot * size) for slot, place in enumerate(near_places)], lane, size
    )
    close = snps - jnp.abs(own_row - near_col) <= reach_here
    spare_mask_ref[...] = jnp.where(close & (lane < groups * size), 1.0, 0.0)


def by_slot(values, lane, size):
    mixed = values[0]
    for slot in range(1, len(values)):
        mixed = jnp.where(lane >= slot * size, values[slot], mixed)
    return mixed


def far_kernel(groups, share, weighted_ref, side_ref, close_ref, close_spare_ref, close_lines_ref, totals_ref, *refs):
    targets, (main, spare, lines, tile, flipped, extras) = refs[:groups], refs[groups:]
    fold_side(True, weighted_ref, side_ref, main, spare, lines, tile, flipped)
    snps = tile.shape[1]
    half, size = snps // 2, share
    odd = odd_block()

    tiles = snps // LANES
    count = spare.shape[0] // 2
    from_far = (iota((8, snps), 1) < half) == odd
    by_column = jnp.concatenate(
        [totals_ref[1:2, :], jnp.where(from_far, lines[...], close_lines_ref[...])[0:2, :]], axis=0
    )
    by_column = jnp.concatenate([by_column, jnp.zeros((5, snps))], axis=0)
    for owner in range(groups):
        start = owner * (snps // groups)
        columns = pltpu.roll(by_column, snps - start, 1) if owner else by_column
        where = slice((owner & 1) * count + size, (owner & 1) * count + size + 1)
        second = odd if owner >= groups // 2 else jnp.logical_not(odd)
        spare_totals = jnp.where(second, spare[where, :], close_spare_ref[where, :])
        extras[8 * owner : 8 * (owner + 1), :] = jnp.concatenate(
            [
                to_fields(columns[0:3, 0:LANES]),
                spare_totals[:, 0:LANES],
                spare_totals[:, LANES:],
                jnp.zeros((3, LANES), jnp.int32),
            ],
            axis=0,
        )
    me = lax.axis_index("hap")
    left = iota((size // 2, LANES), 1) < HALF_LANES
    for step, target in enumerate(targets):
        owner = partner(me, step, groups)
        first = (owner < groups // 2) == odd
        where = pl.ds(pl.multiple_of((owner & 1) * size, 8), size)
        counts = jnp.where(first, main[where, :], close_ref[where, :])
        for k in range(tiles):
            target[k * size : (k + 1) * size, :] = counts[:, k * LANES : (k + 1) * LANES]
        where = pl.ds(pl.multiple_of((owner & 1) * count, 8), size)
        counts = jnp.where(first, close_spare_ref[where, :], spare[where, :])
        start = tiles * size
        target[start : start + size, :] = counts[:, 0:LANES]
        rest = counts[:, LANES:]
        target[start + size : start + size + size // 2, :] = jnp.where(
            left, rest[0 : size // 2], pltpu.roll(rest[size // 2 :], HALF_LANES, 1)
        )
        target[start + size + size // 2 :, :] = extras[pl.ds(pl.multiple_of(owner * 8, 8), 8), :]


def near_kernel(groups, share, weighted_ref, far_ref, close_ref, totals_ref, *refs):
    own_parts, own_sum_ref = refs[:groups], refs[groups]
    targets, (near, tile, folded) = refs[groups + 1 : 2 * groups + 1], refs[2 * groups + 1 :]
    rows, snps = near.shape
    half = snps // 2
    odd = odd_block()

    def unpack(up_ref, down_ref):
        pieces = load_packed(up_ref[0 : rows // 2, :], down_ref[0 : rows // 2, :])
        for side in range(2):
            where = slice(side * (rows // 2), (side + 1) * (rows // 2))
            for number in range(3):
                near[where, number * LANES : (number + 1) * LANES] = pieces[side][number]

    @pl.when(odd)
    def _():
        unpack(far_ref, close_ref)

    @pl.when(jnp.logical_not(odd))
    def _():
        unpack(close_ref, far_ref)

    tile[...] = jnp.dot(weighted_ref[...], near[...], preferred_element_type=jnp.float32)
    row, col = iota((half, snps), 0), iota((half, snps), 1)
    moved = (col >= half) & (col - half < row)
    turned = pltpu.roll(tile[0:half, :], half, 1)
    folded[0:half, :] = to_fields(jnp.where(moved, turned, tile[half:snps, :]))
    if folded.shape[0] > half:
        folded[half:, :] = jnp.zeros((folded.shape[0] - half, snps), jnp.int32)
    square = (snps, snps)
    far = jnp.sum(
        jnp.where(iota(square, 0) == iota(square, 1), tile[0:snps, :], 0.0), axis=0, keepdims=True
    )
    extras = to_fields(
        jnp.concatenate(
            [totals_ref[0:2, :], tile[snps : snps + 1, :], far, jnp.zeros((4, snps))], axis=0
        )
    )
    send_shares(groups, folded, share, targets)
    for target in targets:
        target[share:, :] = extras
    own_sum_ref[...] = sum((part[...] for part in own_parts[1:]), own_parts[0][...])


def annots_kernel(annot_ref, far_ref, close_ref, own_ref, near_ref):
    snps = annot_ref.shape[1]
    own = annot_ref[...].astype(jnp.float32)
    own = jnp.concatenate([own, jnp.zeros((LANES - own.shape[0], snps), jnp.float32)], axis=0)
    own_ref[...] = own.T
    near_ref[...] = near_annots_by_snp(far_ref, close_ref)


def near_annots_by_snp(far_ref, close_ref):
    part, snps = far_ref.shape
    wide = 2 * part
    odd = odd_block()
    far, close = far_ref[...].astype(jnp.float32), close_ref[...].astype(jnp.float32)
    first, second = load_packed(jnp.where(odd, far, close), jnp.where(odd, close, far))
    near = jnp.concatenate(
        [
            jnp.concatenate([piece.astype(jnp.float32) for piece in first], axis=1),
            jnp.concatenate([piece.astype(jnp.float32) for piece in second], axis=1),
            jnp.zeros((LANES - wide, snps), jnp.float32),
        ],
        axis=0,
    )
    return near.T


def column_stats(totals, count):
    size = jnp.maximum(count, 1.0)
    frequency = totals / size
    variance = jnp.maximum(frequency * (1.0 - frequency), VARIANCE_FLOOR)
    inverse = 1.0 / jnp.sqrt(size * variance)
    low = ((0.0 - frequency) * inverse).astype(jnp.bfloat16).astype(jnp.float32)
    high = ((1.0 - frequency) * inverse).astype(jnp.bfloat16).astype(jnp.float32)
    step = high - low
    root = 1.0 / jnp.sqrt(size)
    return step, step * totals * root, (low * count + step * totals) * root


def correlation(row, col, count):
    return row[0] * col[0] * count - row[1] * col[1] + row[2] * col[2]


def split(values):
    high = values.astype(jnp.bfloat16)
    return high, (values - high.astype(jnp.float32)).astype(jnp.bfloat16)


def dot_split(values, right, axis):
    dims = (((axis,), (0,)), ((), ()))
    return sum(
        lax.dot_general(part, right, dims, preferred_element_type=jnp.float32)
        for part in split(values)
    )


def score_kernel(groups, share, reach_ref, *refs):
    own_sum_ref, near_parts = refs[0], refs[1 : groups + 1]
    annot_ref, near_annot_ref = refs[groups + 1 : groups + 3]
    targets = refs[groups + 3 : 2 * groups + 3]
    table, annots, near_annots, scores = refs[2 * groups + 3 :]
    snps = annot_ref.shape[0]
    half = snps // 2
    out_share = snps // groups
    me = lax.axis_index("hap")
    block = lax.axis_index("snp")
    last = reach_ref.shape[0] - 1
    reach_here = reach_ref[block]
    reach_up = reach_ref[jnp.minimum(block + 1, last)]
    reach_down = reach_ref[jnp.maximum(block - 1, 0)]

    own_counts = own_sum_ref[...]
    near_sums = sum((part[...] for part in near_parts[1:]), near_parts[0][...])
    extras = from_fields(near_sums[share:, :])
    near_counts = near_sums[0:share, :]

    own_stats, near_stats, lines = [], [], []
    for pop in range(2):
        count = extras[pop][1:2, :]
        own_stats.append(column_stats(extras[pop][0:1, :], count))
        near_stats.append(column_stats(extras[pop][2:3, :], count))
        lines += [*own_stats[pop], *near_stats[pop], extras[pop][0:1, :], extras[pop][3:4, :]]
    by_row = jnp.concatenate(lines, axis=0).T
    table[0:snps, 0:16] = by_row
    if table.shape[0] > snps:
        table[snps:, 0:16] = jnp.zeros((table.shape[0] - snps, 16), jnp.float32)
    annots[0:snps, :] = annot_ref[...]
    near_annots[0:snps, :] = near_annot_ref[...]
    if annots.shape[0] > snps:
        annots[snps:, :] = jnp.zeros((annots.shape[0] - snps, LANES), jnp.float32)

    low_rows = pl.multiple_of(me * share, 8)
    high_rows = pl.multiple_of(half + me * share, 8)

    def both(ref):
        return jnp.concatenate([ref[pl.ds(low_rows, share), :], ref[pl.ds(high_rows, share), :]], axis=0)

    here = both(table)
    own_count = jnp.concatenate([pltpu.roll(own_counts, half, 1), own_counts], axis=0)
    near_count = jnp.concatenate([pltpu.roll(near_counts, half, 1), near_counts], axis=0)
    shape = (2 * share, snps)
    local, col = iota(shape, 0), iota(shape, 1)
    low = local < share
    place = jnp.where(low, local, local - share) + me * share
    row = jnp.where(low, place, place + half)
    own_fields, near_fields = from_fields(own_count), from_fields(near_count)
    own_product, near_product = 1.0, 1.0
    for pop in range(2):
        row_stats = [here[:, 8 * pop + k : 8 * pop + k + 1] for k in range(3)]
        own_product *= correlation(row_stats, own_stats[pop], own_fields[pop])
        near_product *= correlation(row_stats, near_stats[pop], near_fields[pop])
    real = place < half
    own_inside = real & ((low & (col > row)) | (~low & (col >= half) & (col < row)))
    own_inside &= jnp.abs(col - row) <= reach_here
    own_kept = jnp.where(own_inside, own_product, 0.0)
    in_upper = col < half
    near_inside = real & ((low & (col < row)) | (~low & (in_upper | (col > row))))
    distance = jnp.where(in_upper, snps + col - row, snps + row - col)
    near_here = jnp.where(near_inside & (distance <= reach_here), near_product, 0.0)
    reach_there = jnp.where(in_upper, reach_up, reach_down)
    near_there = jnp.where(near_inside & (distance <= reach_there), near_product, 0.0)

    rows_here = both(annots)
    rows_there = pltpu.roll(rows_here, HALF_LANES, 1)
    scores[0:snps, :] = dot_split(
        jnp.concatenate([own_kept, near_there], axis=0),
        jnp.concatenate([rows_here, rows_there], axis=0).astype(jnp.bfloat16),
        0,
    )
    direct = dot_split(
        jnp.concatenate([own_kept, near_here], axis=1),
        jnp.concatenate([annot_ref[...], near_annot_ref[...]], axis=0).astype(jnp.bfloat16),
        1,
    )
    scores[pl.ds(low_rows, share), :] += direct[0:share, :]
    scores[pl.ds(high_rows, share), :] += direct[share:, :]

    out_rows = pl.ds(pl.multiple_of(me * out_share, 8), out_share)
    mine = table[out_rows, :]
    self_product, far_product = 1.0, 1.0
    for pop in range(2):
        k = 8 * pop
        own_row = [mine[:, k + s : k + s + 1] for s in range(3)]
        near_row = [mine[:, k + 3 + s : k + 4 + s] for s in range(3)]
        self_product *= correlation(own_row, own_row, mine[:, k + 6 : k + 7])
        far_product *= correlation(own_row, near_row, mine[:, k + 7 : k + 8])
    mine_annots = annots[out_rows, :]
    far_reach = jnp.where(me < groups // 2, reach_up, reach_down)
    scores[out_rows, :] += (
        mine_annots * self_product
        + near_annots[out_rows, :] * jnp.where(reach_here >= snps, far_product, 0.0)
        + pltpu.roll(mine_annots, HALF_LANES, 1) * jnp.where(far_reach >= snps, far_product, 0.0)
    )
    send_shares(groups, scores, out_share, targets)


def pack_halves(values):
    half = values.shape[0] // 2
    left = iota((half, LANES), 1) < HALF_LANES
    return jnp.where(left, values[0:half], pltpu.roll(values[half:], HALF_LANES, 1))


def unpack_halves(packed):
    return jnp.concatenate([packed, pltpu.roll(packed, HALF_LANES, 1)], axis=0)


def dot_rounded(values, right, axis):
    dims = (((axis,), (0,)), ((), ()))
    return lax.dot_general(
        values.astype(jnp.bfloat16), right, dims, preferred_element_type=jnp.float32
    )


def owner_places(groups, size):
    me = lax.axis_index("hap")

    def mine(blocks, slot):
        value = blocks[0][slot]
        for group in range(1, groups):
            value = jnp.where(me == group, blocks[group][slot], value)
        return value * size

    left = [mine(LEFT_BLOCKS, slot) for slot in range(groups)]
    right = [mine(RIGHT_BLOCKS, slot) for slot in range(groups)]
    return left + left[0:1], right + [(2 * me + 1) * size]


def spare_places(groups, size):
    me = lax.axis_index("hap")

    def mine(blocks, slot):
        value = blocks[0][slot]
        for group in range(1, groups):
            value = jnp.where(me == group, blocks[group][slot], value)
        return value * size

    return [[mine(blocks, slot) for slot in range(groups)] for blocks in (SPARE_OWN, SPARE_NEAR)]


def rows_at(ref, places, size):
    return jnp.concatenate([ref[pl.ds(pl.multiple_of(place, 8), size), :] for place in places], axis=0)


def own_score_kernel(
    groups, share, reach_ref, *refs
):
    own_parts, refs = refs[:groups], refs[groups:]
    annot_ref, far_ref, close_ref, scores, mine_ref, rows_ref, columns_ref, *refs = refs
    spare_rows_ref, spare_columns_ref, near_annot_ref, *targets, table = refs
    near_annot_ref[...] = near_annots_by_snp(far_ref, close_ref)
    snps = annot_ref.shape[0]
    half = snps // 2
    wide = snps // groups
    tiles = snps // LANES
    me = lax.axis_index("hap")
    reach_here = reach_ref[lax.axis_index("snp")]
    own_sums = sum((part[...] for part in own_parts[1:]), own_parts[0][...])
    own_counts = from_tiles(own_sums[0 : tiles * share, :], share)
    extras = from_fields(own_sums[tiles * share :, :])

    own_stats, lines = [], []
    for pop in range(2):
        count = jnp.concatenate([extras[pop][tiles : tiles + 1, :]] * tiles, axis=1)
        totals = jnp.concatenate([extras[pop][k : k + 1, :] for k in range(tiles)], axis=1)
        own_stats.append(column_stats(totals, count))
        lines += [*own_stats[pop], totals]
    table[:, 0:8] = jnp.concatenate(lines, axis=0).T

    low_rows = pl.multiple_of(me * share, 8)
    high_rows = pl.multiple_of(half + me * share, 8)

    def both(ref):
        return jnp.concatenate([ref[pl.ds(low_rows, share), :], ref[pl.ds(high_rows, share), :]], axis=0)

    here = both(table)
    own_fields = from_fields(
        jnp.concatenate([pltpu.roll(own_counts, half, 1), own_counts], axis=0)
    )
    shape = (2 * share, snps)
    local, col = iota(shape, 0), iota(shape, 1)
    low = local < share
    row = jnp.where(low, local, local + half - share) + me * share
    product = 1.0
    for pop in range(2):
        row_stats = [here[:, 4 * pop + k : 4 * pop + k + 1] for k in range(3)]
        product *= correlation(row_stats, own_stats[pop], own_fields[pop])
    inside = (low & (col > row)) | (~low & (col >= half) & (col < row))
    own_kept = jnp.where(inside & (jnp.abs(col - row) <= reach_here), product, 0.0)
    rows_here = both(annot_ref).astype(jnp.bfloat16)
    scores[...] = dot_rounded(own_kept, rows_here, 0)
    direct = dot_rounded(own_kept, annot_ref[...].astype(jnp.bfloat16), 1)
    scores[pl.ds(low_rows, share), :] += direct[0:share, :]
    scores[pl.ds(high_rows, share), :] += direct[share:, :]

    slice_rows = pl.ds(pl.multiple_of(me * wide, 8), wide)
    mine = table[slice_rows, :]
    mine_ref[...] = mine
    product = 1.0
    for pop in range(2):
        own_row = [mine[:, 4 * pop + k : 4 * pop + k + 1] for k in range(4)]
        product *= correlation(own_row, own_row, own_row[3])
    scores[slice_rows, :] += annot_ref[slice_rows, :] * product
    for step, target in enumerate(targets, 2):
        group = partner(me, step, groups)
        rows = scores[pl.ds(pl.multiple_of(group * wide, 8), wide), :]
        target[...] = pack_halves(rows).astype(target.dtype)

    size = wide // 2
    left_places, right_places = owner_places(groups, size)
    left_table, right_table = rows_at(table, left_places, size), rows_at(table, right_places, size)
    is_left = iota(rows_ref.shape[1:], 1) < size
    for pop in range(2):
        for k in range(3):
            column = slice(4 * pop + k, 4 * pop + k + 1)
            rows_ref[3 * pop + k] = jnp.where(is_left, left_table[:, column], right_table[:, column])
    theirs = near_annot_ref[slice_rows, :]
    columns = [theirs[0:size], pltpu.roll(theirs[size:], HALF_LANES, 1), jnp.zeros((LANES - wide, LANES))]
    columns_ref[...] = jnp.concatenate(columns, axis=0).astype(jnp.bfloat16)

    own_places, near_places = spare_places(groups, size)
    shape = spare_rows_ref.shape[1:]
    lane = iota(shape, 1)
    tables = [table[pl.ds(pl.multiple_of(place, 8), size), :] for place in own_places]
    for pop in range(2):
        for k in range(3):
            column = slice(4 * pop + k, 4 * pop + k + 1)
            spare_rows_ref[3 * pop + k] = by_slot(
                [jnp.broadcast_to(values[:, column], shape) for values in tables], lane, size
            )
    columns = [rows_at(near_annot_ref, near_places, size)]
    columns.append(jnp.zeros((shape[1] - groups * size, LANES), jnp.float32))
    spare_columns_ref[...] = jnp.concatenate(columns, axis=0).astype(jnp.bfloat16)


def near_score_kernel(groups, share, reach_ref, *refs):
    near_parts, refs = refs[:groups], refs[groups:]
    own_ref, mine_ref, rows_ref, columns_ref, spare_rows_ref, spare_columns_ref = refs[:6]
    near_annot_ref, annot_ref, masks_ref, spare_mask_ref, own_rows_ref = refs[6:11]
    out_ref, wide_ref, send_ref, near_out_ref, flipped, scores = refs[11:]
    snps = annot_ref.shape[0]
    wide = snps // groups
    size = wide // 2
    tiles = snps // LANES
    me = lax.axis_index("hap")
    block = lax.axis_index("snp")
    last = reach_ref.shape[0] - 1
    reach_here = reach_ref[block]
    reach_there = jnp.where(
        me < groups // 2, reach_ref[jnp.minimum(block + 1, last)], reach_ref[jnp.maximum(block - 1, 0)]
    )

    scores[...] = own_ref[...]
    near_sums = sum((part[...] for part in near_parts[1:]), near_parts[0][...])
    near_counts = from_tiles(near_sums[0 : tiles * share, :], share)
    start = tiles * share
    rest = near_sums[start + size : start + size + size // 2, :]
    rest = jnp.concatenate([rest, pltpu.roll(rest, HALF_LANES, 1)], axis=0)
    spare_fields = from_fields(jnp.concatenate([near_sums[start : start + size, :], rest], axis=1))
    extras = from_fields(near_sums[start + size + size // 2 :, :])
    near_stats, near_lines, spare_stats = [], [], []
    for pop in range(2):
        count = extras[pop][0:1, :]
        totals = jnp.concatenate([extras[pop][3:4, :], extras[pop][4:5, :]], axis=1)
        spare_stats.append(column_stats(totals, jnp.concatenate([count, count], axis=1)))
        near_stats.append(column_stats(extras[pop][1:2, :], extras[pop][0:1, :]))
        near_lines += [*near_stats[pop], extras[pop][2:3, :]]
    near_table = jnp.concatenate(near_lines, axis=0).T[0:wide, :]

    slots = [near_counts[:, 0:LANES]]
    for slot in range(1, groups):
        slots.append(pltpu.roll(near_counts, snps - slot * wide, 1)[:, 0:LANES])
    flipped[:, 0:size] = slots[0].T
    slots.append(pltpu.roll(flipped[0:size, :], size, 1))
    near_fields = from_fields(jnp.concatenate(slots, axis=0))
    product = 1.0
    for pop in range(2):
        row_stats = [rows_ref[3 * pop + k] for k in range(3)]
        product *= correlation(row_stats, near_stats[pop], near_fields[pop])
    near_here = jnp.where(masks_ref[0] > 0.0, product, 0.0)
    near_there = jnp.where(masks_ref[1] > 0.0, product, 0.0)
    slice_rows = pl.ds(pl.multiple_of(me * wide, 8), wide)
    direct = dot_rounded(near_here, columns_ref[...], 1)
    turned = pltpu.roll(direct, HALF_LANES, 1)
    for values, places in zip((direct, turned), owner_places(groups, size)):
        for slot, place in enumerate(places):
            scores[pl.ds(pl.multiple_of(place, 8), size), :] += values[slot * size : (slot + 1) * size, :]
    product = 1.0
    for pop in range(2):
        row_stats = [spare_rows_ref[3 * pop + k] for k in range(3)]
        product *= correlation(row_stats, spare_stats[pop], spare_fields[pop])
    spare_here = jnp.where(spare_mask_ref[...] > 0.0, product, 0.0)
    lane = iota(spare_here.shape, 1)
    spare_here = [
        jnp.where((lane >= slot * size) & (lane < (slot + 1) * size), spare_here, 0.0)
        for slot in range(groups)
    ]
    direct = dot_rounded(jnp.concatenate(spare_here, axis=0), spare_columns_ref[...], 1)
    for slot, place in enumerate(spare_places(groups, size)[0]):
        scores[pl.ds(pl.multiple_of(place, 8), size), :] += direct[slot * size : (slot + 1) * size, :]
    near_scores = dot_rounded(near_there, own_rows_ref[...], 0)
    near_scores = jnp.where(
        iota((size, LANES), 1) < HALF_LANES, near_scores[0:size], near_scores[size:wide]
    )

    mine_table = mine_ref[...]
    far_product = 1.0
    for pop in range(2):
        own_row = [mine_table[:, 4 * pop + k : 4 * pop + k + 1] for k in range(3)]
        near_row = [near_table[:, 4 * pop + k : 4 * pop + k + 1] for k in range(4)]
        far_product *= correlation(own_row, near_row, near_row[3])
    scores[slice_rows, :] += near_annot_ref[slice_rows, :] * jnp.where(reach_here >= snps, far_product, 0.0)
    far_scores = annot_ref[slice_rows, :] * jnp.where(reach_there >= snps, far_product, 0.0)
    near_out_ref[...] = (near_scores + pack_halves(far_scores)).astype(near_out_ref.dtype)

    def packed(step):
        group = partner(me, step, groups)
        return pack_halves(scores[pl.ds(pl.multiple_of(group * wide, 8), wide), :])

    out_ref[...] = packed(0)
    wide_ref[...] = packed(1)
    send_ref[...] = wide_ref[...].astype(send_ref.dtype)


def column_finish_kernel(*refs):
    *parts, out_ref = refs
    packed = sum(part[...].astype(jnp.float32) for part in parts)
    out_ref[...] = unpack_halves(packed).T[0 : out_ref.shape[0], :]


def sum_kernel(*refs):
    *parts, own_ref, there_ref = refs
    total = sum((part[...].astype(jnp.float32) for part in parts[1:]), parts[0][...])
    own_ref[...] = total
    half = there_ref.shape[0]
    left = iota((half, LANES), 1) < HALF_LANES
    second = total[half:]
    if second.shape[0] < half:
        second = jnp.concatenate([second, jnp.zeros((half - second.shape[0], LANES))], axis=0)
    there_ref[...] = jnp.where(left, pltpu.roll(total[0:half], HALF_LANES, 1), second)


def finish_kernel(own_ref, there_ref, out_ref):
    annots, rows = out_ref.shape
    there = there_ref[...]
    there = jnp.concatenate([there, pltpu.roll(there, HALF_LANES, 1)], axis=0)
    out_ref[...] = (own_ref[...] + there[0:rows]).T[0:annots, :]


def around(value, groups, step):
    return lax.ppermute(
        value, "hap", [(source, partner(source, step, groups)) for source in range(groups)]
    )


def swap_nearest(value, groups, of_blocks):
    pairs = [
        (block * groups + group, block * groups + partner(group, 1, groups))
        for block in of_blocks
        for group in range(groups)
    ]
    return lax.ppermute(value, ("snp", "hap"), pairs)


def swapped(value, first):
    pairs = []
    for block in range(first, lax.axis_size("snp") - 1, 2):
        pairs += [(block, block + 1), (block + 1, block)]
    return lax.ppermute(value, "snp", pairs)


def per_device(haplotypes, labels, annotations, reach):
    rows, snps = haplotypes.shape
    half = snps // 2
    groups = lax.axis_size("hap")
    blocks = lax.axis_size("snp")
    share = round_up(-(-half // groups), 16)
    folded_rows = share * groups
    out_share = snps // groups
    padded = half + folded_rows
    annot_part = 32
    bf16, f32, i32 = jnp.bfloat16, jnp.float32, jnp.int32
    shape = jax.ShapeDtypeStruct

    packed = shape((rows // 2 + annot_part, snps), bf16)
    haplotypes = pltpu.with_memory_space_constraint(haplotypes, pltpu.HBM)
    annots_in = pltpu.with_memory_space_constraint(annotations, pltpu.HBM)
    alleles, far, close = call(
        prepare_kernel,
        [shape((rows, snps), bf16), packed, packed],
        [HBM, HBM],
        [
            pltpu.VMEM((rows, snps), i32),
            pltpu.VMEM(annotations.shape, i32),
            pltpu.SemaphoreType.DMA((2 * len(CHUNKS) + 1,)),
        ],
        moved=rows * snps * 8,
    )(haplotypes, annots_in)
    from_far = swapped(far, 1)
    from_close = swapped(close, 0)

    by_column = groups == len(LEFT_BLOCKS)
    by_snp = shape((snps, LANES), f32)
    compact = shape((share * (snps // LANES) + 8, LANES), i32)
    own_share_counts = compact if by_column else shape((share, snps), i32)
    near_share_counts = shape((compact.shape[0] + share + share // 2, LANES), i32)
    tile = pltpu.VMEM((snps + 16, snps), f32)
    folded = pltpu.VMEM((folded_rows, snps), i32)
    weighted, totals, *own_parts = call(
        functools.partial(own_kernel, groups, share),
        [shape((snps + 16, rows), bf16), shape((8, snps), f32)] + [own_share_counts] * groups,
        [VMEM, VMEM],
        [tile, folded],
        flops=2 * rows * snps * snps,
        moved=rows * snps * 4,
    )(alleles, labels.reshape(1, rows))
    order = (2, 3, 1) if by_column else range(groups - 1, 0, -1)
    own_parts = [own_parts[0]] + [around(own_parts[k], groups, k) for k in order]

    near_shapes = [own_share_counts] + [near_share_counts if by_column else shape((share + 8, snps), i32)] * groups
    if by_column:
        work = dict(flops=4 * rows * snps * LANES, moved=rows * snps * 4)
        flipped = pltpu.VMEM((snps, LANES), f32)
        pair_rows = (groups + 1) * (out_share // 2)
        side_shapes = [((2 * share, snps), i32), ((2 * (share + 8), 2 * LANES), i32), ((8, snps), f32)]
        *close_counts, own_annots, masks, spare_mask, own_rows = call(
            functools.partial(close_kernel, groups),
            [shape(*args) for args in side_shapes]
            + [
                by_snp,
                shape((2, pair_rows, LANES), f32),
                shape((share, 2 * LANES), f32),
                shape((pair_rows, LANES), bf16),
            ],
            [SMEM] + [VMEM] * 3,
            [tile, flipped],
            **work,
        )(reach, weighted, from_close, annotations)
        near_parts = call(
            functools.partial(far_kernel, groups, share),
            near_shapes[1:],
            [VMEM] * 6,
            [pltpu.VMEM(*args) for args in side_shapes]
            + [tile, flipped, pltpu.VMEM((8 * groups, LANES), i32)],
            **work,
        )(weighted, from_far, *close_counts, totals)
    else:
        own_sum, *near_parts = call(
            functools.partial(near_kernel, groups, share),
            near_shapes,
            [VMEM] * (4 + groups),
            [pltpu.VMEM((rows, snps), bf16), tile, folded],
            flops=2 * rows * snps * snps,
            moved=rows * snps * 4,
        )(weighted, from_far, from_close, totals, *own_parts)
    near_parts = [near_parts[0]] + [around(near_parts[k], groups, k) for k in order]

    if not by_column:
        own_annots, near_annots = call(annots_kernel, [by_snp, by_snp], [VMEM] * 3, moved=1 << 20)(
            annotations, from_far[rows // 2 :], from_close[rows // 2 :]
        )
    pairs = []
    for block in range(blocks):
        for group in range(groups):
            target = block + 1 if group < groups // 2 else block - 1
            if 0 <= target < blocks:
                pairs.append((block * groups + group, target * groups + group))

    def to_neighbour(value):
        return lax.ppermute(value, ("snp", "hap"), pairs)

    result = shape((annotations.shape[0], out_share), f32)
    half_share = round_up(-(-out_share // 2), 8)
    own_share = shape((out_share, LANES), f32)
    packed_share = shape((half_share, LANES), f32)
    if by_column:
        sent = shape((half_share, LANES), bf16)
        *prepared, second, third = call(
            functools.partial(own_score_kernel, groups, share),
            [
                by_snp,
                shape((out_share, LANES), f32),
                shape((6, pair_rows, LANES), f32),
                shape((LANES, LANES), bf16),
                shape((6, share, 2 * LANES), f32),
                shape((2 * LANES, LANES), bf16),
                by_snp,
                packed_share,
                packed_share,
            ],
            [SMEM] + [VMEM] * (groups + 3),
            [pltpu.VMEM((snps, LANES), f32)],
            flops=1 << 33,
            moved=1 << 20,
        )(reach, *own_parts, own_annots, from_far[rows // 2 :], from_close[rows // 2 :])
        parts = [around(third, groups, 3), around(second, groups, 2)]
        own_scores, wide, send, there = call(
            functools.partial(near_score_kernel, groups, share),
            [packed_share, packed_share, sent, sent],
            [SMEM] + [VMEM] * (groups + 11),
            [pltpu.VMEM((LANES, LANES), i32), pltpu.VMEM((snps, LANES), f32)],
            flops=1 << 26,
            moved=1 << 21,
        )(reach, *near_parts, *prepared, own_annots, masks, spare_mask, own_rows)
        early, late = range(blocks // 2), range(blocks // 2, blocks)
        parts += [swap_nearest(wide, groups, early), to_neighbour(there), swap_nearest(send, groups, late)]
        return call(column_finish_kernel, result, [VMEM] * 6)(own_scores, *parts)

    tall = pltpu.VMEM((padded, LANES), f32)
    scores = call(
        functools.partial(score_kernel, groups, share),
        [own_share] + [shape((out_share, LANES), bf16)] * (groups - 1),
        [SMEM] + [VMEM] * (groups + 3),
        [tall, tall, tall, tall],
        flops=1 << 26,
        moved=1 << 21,
    )(reach, own_sum, *near_parts, own_annots, near_annots)
    scores = [scores[0]] + [around(scores[k], groups, k) for k in range(groups - 1, 0, -1)]
    own_scores, near_scores = call(sum_kernel, [own_share, packed_share], [VMEM] * groups)(*scores)
    return call(finish_kernel, result, [VMEM] * 2)(own_scores, to_neighbour(near_scores))


def solution(mesh):
    in_specs = (
        P("hap", ("parts", "snp")),
        P(("parts", "hap")),
        P(None, ("parts", "snp")),
        P("parts"),
    )
    out_specs = P(None, ("parts", "snp", "hap"))
    return jax.shard_map(
        per_device, mesh=mesh, in_specs=in_specs, out_specs=out_specs, check_vma=False
    )
```

```python
import functools

import jax
import jax.numpy as jnp
from jax import lax
from jax.experimental import pallas as pl
from jax.experimental.pallas import tpu as pltpu
from jax.sharding import PartitionSpec as P

VARIANCE_FLOOR = 0.01
BASE_BITS = 12
BASE = 1 << BASE_BITS
FIELD_BITS = 16
LANES = 128
HALF_LANES = LANES // 2
CHUNKS = 4
VMEM = pl.BlockSpec(memory_space=pltpu.VMEM)
SMEM = pl.BlockSpec(memory_space=pltpu.SMEM)
HBM = pl.BlockSpec(memory_space=pltpu.HBM)
VMEM_LIMIT = 24 * 1024 * 1024


def iota(shape, axis):
    return lax.broadcasted_iota(jnp.int32, shape, axis)


def round_up(value, step):
    return -(-value // step) * step


def to_fields(values):
    whole = values.astype(jnp.int32)
    return whole + (whole >> BASE_BITS) * ((1 << FIELD_BITS) - BASE)


def from_fields(packed):
    first = packed & ((1 << FIELD_BITS) - 1)
    second = lax.shift_right_logical(packed, FIELD_BITS)
    return first.astype(jnp.float32), second.astype(jnp.float32)


def call(kernel, out_shape, in_specs, scratch_shapes=(), flops=0, moved=0):
    several = isinstance(out_shape, (list, tuple))
    return pl.pallas_call(
        kernel,
        out_shape=out_shape,
        in_specs=in_specs,
        out_specs=[VMEM] * len(out_shape) if several else VMEM,
        scratch_shapes=list(scratch_shapes),
        compiler_params=pltpu.CompilerParams(vmem_limit_bytes=VMEM_LIMIT),
        cost_estimate=pl.CostEstimate(flops=flops, bytes_accessed=moved, transcendentals=0),
    )


def odd_block():
    return lax.rem(lax.axis_index("snp"), 2) == 1


def store_packed(up_ref, down_ref, where, first, second):
    left = iota((first.shape[0], LANES), 1) < HALF_LANES
    middle = first[:, LANES : 2 * LANES]
    turned = pltpu.roll(second[:, LANES : 2 * LANES], HALF_LANES, 1)
    for ref, side, mixed in (
        (up_ref, slice(0, LANES), jnp.where(left, middle, turned)),
        (down_ref, slice(2 * LANES, 3 * LANES), jnp.where(left, turned, middle)),
    ):
        ref[where, 0:LANES] = first[:, side].astype(jnp.bfloat16)
        ref[where, LANES : 2 * LANES] = mixed.astype(jnp.bfloat16)
        ref[where, 2 * LANES : 3 * LANES] = second[:, side].astype(jnp.bfloat16)


def load_packed(up, down):
    left = iota((up.shape[0], LANES), 1) < HALF_LANES
    up_mixed, down_mixed = up[:, LANES : 2 * LANES], down[:, LANES : 2 * LANES]
    first = jnp.where(left, up_mixed, down_mixed)
    second = jnp.where(left, down_mixed, up_mixed)
    second = pltpu.roll(second.astype(jnp.float32), HALF_LANES, 1).astype(second.dtype)
    return (
        (up[:, :LANES], first, down[:, :LANES]),
        (up[:, 2 * LANES :], second, down[:, 2 * LANES :]),
    )


def prepare_kernel(hap_ref, annot_ref, alleles_ref, far_ref, close_ref, held, held_annots, sems):
    rows = hap_ref.shape[0]
    annot_rows = annot_ref.shape[0]
    size = rows // (2 * CHUNKS)
    starts = [side * (rows // 2) + chunk * size for chunk in range(CHUNKS) for side in range(2)]
    copies = [
        pltpu.make_async_copy(
            hap_ref.at[pl.ds(start, size)], held.at[pl.ds(start, size)], sems.at[number]
        )
        for number, start in enumerate(starts)
    ]
    copies.append(pltpu.make_async_copy(annot_ref, held_annots, sems.at[2 * CHUNKS]))
    for copy in copies:
        copy.start()
    part = far_ref.shape[0] - rows // 2
    odd = odd_block()

    def store(where, first, second):
        @pl.when(odd)
        def _():
            store_packed(close_ref, far_ref, where, first, second)

        @pl.when(jnp.logical_not(odd))
        def _():
            store_packed(far_ref, close_ref, where, first, second)

    for chunk in range(CHUNKS):
        pair = []
        for side in range(2):
            number = 2 * chunk + side
            copies[number].wait()
            where = slice(starts[number], starts[number] + size)
            values = held[where, :].astype(jnp.float32)
            alleles_ref[where, :] = values.astype(jnp.bfloat16)
            pair.append(values)
        store(slice(chunk * size, (chunk + 1) * size), *pair)
    copies[-1].wait()
    annots = jnp.concatenate(
        [
            held_annots[...].astype(jnp.float32),
            jnp.zeros((2 * part - annot_rows, annot_ref.shape[1]), jnp.float32),
        ],
        axis=0,
    )
    store(slice(rows // 2, rows // 2 + part), annots[:part], annots[part:])


def partner(group, step, groups):
    if groups & (groups - 1) == 0:
        return group ^ step
    return (group + step) % groups


def send_shares(groups, source, share, targets):
    me = lax.axis_index("hap")
    for step, target in enumerate(targets):
        group = partner(me, step, groups)
        rows = source[pl.ds(pl.multiple_of(group * share, 8), share), :]
        target[0:share, :] = rows.astype(target.dtype)


def send_tiles(groups, source, share, targets):
    me = lax.axis_index("hap")
    for step, target in enumerate(targets):
        owner = partner(me, step, groups)
        counts = source[pl.ds(pl.multiple_of(owner * share, 8), share), :]
        for k in range(source.shape[1] // LANES):
            target[k * share : (k + 1) * share, :] = counts[:, k * LANES : (k + 1) * LANES]


def from_tiles(counts, share):
    tiles = counts.shape[0] // share
    return jnp.concatenate([counts[k * share : (k + 1) * share, :] for k in range(tiles)], axis=1)


def own_kernel(groups, share, alleles_ref, label_ref, *refs):
    weighted_ref, totals_ref, *targets = refs[: 2 + groups]
    tile, folded = refs[2 + groups :]
    rows, snps = alleles_ref.shape
    half = snps // 2
    weight = jnp.where(label_ref[...] > 0, float(BASE), 1.0)
    weighted_ref[0:snps, :] = alleles_ref[...].T * weight.astype(jnp.bfloat16)
    extra = weighted_ref.shape[0] - snps
    weighted_ref[snps:, :] = jnp.broadcast_to(weight, (extra, rows)).astype(jnp.bfloat16)
    tile[...] = jnp.dot(weighted_ref[...], alleles_ref[...], preferred_element_type=jnp.float32)
    count = jnp.sum(weight, axis=1, keepdims=True)
    totals_ref[...] = jnp.concatenate(
        [tile[snps : snps + 1, :], jnp.broadcast_to(count, (1, snps)), jnp.zeros((6, snps))], axis=0
    )
    row, col = iota((half, snps), 0), iota((half, snps), 1)
    moved = (col < half) | (col - half > row)
    turned = pltpu.roll(tile[0:half, :], half, 1)
    folded[0:half, :] = to_fields(jnp.where(moved, turned, tile[half:snps, :]))
    if folded.shape[0] > half:
        folded[half:, :] = jnp.zeros((folded.shape[0] - half, snps), jnp.int32)
    if groups != len(LEFT_BLOCKS):
        send_shares(groups, folded, share, targets)
        return
    tiles = snps // LANES
    shared = [totals_ref[0:1, k * LANES : (k + 1) * LANES] for k in range(tiles)]
    shared += [totals_ref[1:2, 0:LANES], jnp.zeros((7 - tiles, LANES))]
    extras = to_fields(jnp.concatenate(shared, axis=0))
    send_tiles(groups, folded, share, targets)
    for target in targets:
        target[tiles * share :, :] = extras


LEFT_BLOCKS = ((0, 1, 2, 3), (2, 3, 6, 7), (4, 0, 1, 2), (6, 0, 4, 5))
RIGHT_BLOCKS = ((2, 3, 6, 7), (4, 5, 6, 7), (0, 1, 2, 4), (0, 4, 5, 6))


SPARE_OWN = ((0, 0, 0, 0), (1, 1, 2, 2), (4, 5, 6, 7), (6, 6, 7, 7))
SPARE_NEAR = ((4, 5, 6, 7), (4, 5, 4, 5), (3, 3, 3, 3), (1, 2, 1, 2))


def fold_spare(tile, spare, first):
    owners = len(SPARE_OWN)
    snps = tile.shape[1]
    size = snps // (2 * owners)
    count = spare.shape[0] // 2
    totals = tile[snps : snps + count - size, :]
    lane = iota((count, snps), 1)
    for number, owner in enumerate(range(first, first + 2)):
        mixed = None
        for slot in range(owners):
            own, near = SPARE_OWN[owner][slot], SPARE_NEAR[owner][slot]
            before = (SPARE_OWN[owner][slot - 1], SPARE_NEAR[owner][slot - 1] + 1) if slot else None
            if before == (own, near):
                continue
            values = jnp.concatenate([tile[own * size : (own + 1) * size, :], totals], axis=0)
            shift = (slot - near) * size % snps
            values = pltpu.roll(values, shift, 1) if shift else values
            mixed = values if mixed is None else jnp.where(lane >= slot * size, values, mixed)
        spare[number * count : (number + 1) * count, :] = to_fields(mixed[:, 0 : spare.shape[1]])


def fold_by_column(tile, flipped, folded, first):
    groups = len(LEFT_BLOCKS)
    owners = range(first, first + groups // 2)
    snps = folded.shape[1]
    wide = snps // groups
    size = wide // 2
    shape = (size, snps)
    row, lane = iota(shape, 0), iota(shape, 1)

    def block(number):
        return tile[number * size : (number + 1) * size, :]

    diagonal, within = block(2 * first), lane - 2 * first * size
    for number in range(2 * first + 1, 2 * first + groups):
        diagonal = jnp.where(lane >= number * size, block(number), diagonal)
        within = jnp.where(lane >= number * size, lane - number * size, within)
    apart = jnp.sum(jnp.where(row == within, diagonal, 0.0), axis=0, keepdims=True)
    flipped[:, 0:size] = diagonal.T
    corner = diagonal
    for owner in owners:
        start = (2 * owner + 1) * size
        turned = jnp.concatenate(
            [flipped[start : start + size, :], jnp.zeros((size, snps - LANES), jnp.float32)], axis=1
        )
        if owner:
            turned = pltpu.roll(turned, owner * wide, 1)
        inside = lane - owner * wide
        other = (row <= inside) if first == 0 else (row >= inside)
        corner = jnp.where((inside >= 0) & (inside < size) & other, turned, corner)
    rolled = []
    for shift in range(groups):
        mixed = None
        for owner in owners:
            slot = (owner + shift) % groups
            left = block(LEFT_BLOCKS[owner][slot]) if slot else corner
            start = owner * wide
            mixed = left if mixed is None else jnp.where(lane >= start, left, mixed)
            mixed = jnp.where(lane >= start + size, block(RIGHT_BLOCKS[owner][slot]), mixed)
        rolled.append(pltpu.roll(mixed, shift * wide, 1) if shift else mixed)
    for number, owner in enumerate(owners):
        mixed = rolled[(0 - owner) % groups]
        for slot in range(1, groups):
            mixed = jnp.where(lane >= slot * wide, rolled[(slot - owner) % groups], mixed)
        folded[number * size : (number + 1) * size, :] = to_fields(mixed)
    return apart


def above(far):
    return odd_block() == far


def side_dot(weighted_ref, side_ref):
    rows = weighted_ref.shape[1]
    half = rows // 2

    def dot(which, columns):
        return jnp.dot(
            weighted_ref[:, which], side_ref[0:half, columns], preferred_element_type=jnp.float32
        )

    first = dot(slice(0, half), slice(0, 2 * LANES))
    second = dot(slice(half, rows), slice(LANES, 3 * LANES))
    whole = first[:, 0:LANES] + second[:, LANES:]
    return whole, first[:, LANES:] + pltpu.roll(second[:, 0:LANES], HALF_LANES, 1)


def fold_side(far, weighted_ref, side_ref, main, spare, lines, tile, flipped):
    snps = tile.shape[1]
    whole, shared = side_dot(weighted_ref, side_ref)
    tile[:, LANES : 2 * LANES] = shared

    def fold(first, start):
        tile[:, start : start + LANES] = whole
        apart = fold_by_column(tile, flipped, main, first)
        fold_spare(tile, spare, 2 - first)
        lines[0:1, :] = tile[snps : snps + 1, :]
        lines[1:2, :] = apart

    @pl.when(above(far))
    def _():
        fold(0, 0)

    @pl.when(jnp.logical_not(above(far)))
    def _():
        fold(2, 2 * LANES)


def close_kernel(groups, reach_ref, weighted_ref, side_ref, annot_ref, *refs):
    main_ref, spare_ref, lines_ref, annots, masks_ref, spare_mask_ref, own_rows_ref, tile, flipped = refs
    fold_side(False, weighted_ref, side_ref, main_ref, spare_ref, lines_ref, tile, flipped)
    snps = annot_ref.shape[1]
    half, wide = snps // 2, snps // groups
    size = wide // 2
    own = annot_ref[...].astype(jnp.float32)
    own = jnp.concatenate([own, jnp.zeros((LANES - own.shape[0], snps), jnp.float32)], axis=0)
    annots[...] = own.T

    me = lax.axis_index("hap")
    block = lax.axis_index("snp")
    last = reach_ref.shape[0] - 1
    upper = me < groups // 2
    reach_here = reach_ref[block]
    reach_there = jnp.where(
        upper, reach_ref[jnp.minimum(block + 1, last)], reach_ref[jnp.maximum(block - 1, 0)]
    )
    left_places, right_places = owner_places(groups, size)
    local, lane = iota((size, LANES), 0), iota((size, LANES), 1)
    own_row = jnp.concatenate(
        [local + jnp.where(lane < size, a, b) for a, b in zip(left_places, right_places)], axis=0
    )
    shape = own_row.shape
    lane = iota(shape, 1)
    apart = jnp.abs(own_row - (lane + me * wide))
    ahead = (own_row - (lane + me * wide)) * jnp.where(upper, 1, -1) > 0
    real = ahead & (lane < wide) & ((lane >= size) | (iota(shape, 0) < groups * size))
    inside = (own_row - half) * jnp.where(upper, 1, -1) < jnp.where(upper, 0, 1)
    masks_ref[0] = jnp.where(real & inside & (snps - apart <= reach_here), 1.0, 0.0)
    masks_ref[1] = jnp.where(real & (snps - apart <= reach_there), 1.0, 0.0)
    own_rows = rows_at(annots, left_places, size) + pltpu.roll(
        rows_at(annots, right_places, size), HALF_LANES, 1
    )
    own_rows_ref[...] = own_rows.astype(jnp.bfloat16)

    own_places, near_places = spare_places(groups, size)
    shape = spare_mask_ref.shape
    local, lane = iota(shape, 0), iota(shape, 1)
    own_row = by_slot([local + place for place in own_places], lane, size)
    near_col = by_slot(
        [lane + (place - slot * size) for slot, place in enumerate(near_places)], lane, size
    )
    close = snps - jnp.abs(own_row - near_col) <= reach_here
    spare_mask_ref[...] = jnp.where(close & (lane < groups * size), 1.0, 0.0)


def by_slot(values, lane, size):
    mixed = values[0]
    for slot in range(1, len(values)):
        mixed = jnp.where(lane >= slot * size, values[slot], mixed)
    return mixed


def far_kernel(groups, share, weighted_ref, side_ref, close_ref, close_spare_ref, close_lines_ref, totals_ref, *refs):
    targets, (main, spare, lines, tile, flipped, extras) = refs[:groups], refs[groups:]
    fold_side(True, weighted_ref, side_ref, main, spare, lines, tile, flipped)
    snps = tile.shape[1]
    half, size = snps // 2, share
    odd = odd_block()

    tiles = snps // LANES
    count = spare.shape[0] // 2
    from_far = (iota((8, snps), 1) < half) == odd
    by_column = jnp.concatenate(
        [totals_ref[1:2, :], jnp.where(from_far, lines[...], close_lines_ref[...])[0:2, :]], axis=0
    )
    by_column = jnp.concatenate([by_column, jnp.zeros((5, snps))], axis=0)
    for owner in range(groups):
        start = owner * (snps // groups)
        columns = pltpu.roll(by_column, snps - start, 1) if owner else by_column
        where = slice((owner & 1) * count + size, (owner & 1) * count + size + 1)
        second = odd if owner >= groups // 2 else jnp.logical_not(odd)
        spare_totals = jnp.where(second, spare[where, :], close_spare_ref[where, :])
        extras[8 * owner : 8 * (owner + 1), :] = jnp.concatenate(
            [
                to_fields(columns[0:3, 0:LANES]),
                spare_totals[:, 0:LANES],
                spare_totals[:, LANES:],
                jnp.zeros((3, LANES), jnp.int32),
            ],
            axis=0,
        )
    me = lax.axis_index("hap")
    left = iota((size // 2, LANES), 1) < HALF_LANES
    for step, target in enumerate(targets):
        owner = partner(me, step, groups)
        first = (owner < groups // 2) == odd
        where = pl.ds(pl.multiple_of((owner & 1) * size, 8), size)
        counts = jnp.where(first, main[where, :], close_ref[where, :])
        for k in range(tiles):
            target[k * size : (k + 1) * size, :] = counts[:, k * LANES : (k + 1) * LANES]
        where = pl.ds(pl.multiple_of((owner & 1) * count, 8), size)
        counts = jnp.where(first, close_spare_ref[where, :], spare[where, :])
        start = tiles * size
        target[start : start + size, :] = counts[:, 0:LANES]
        rest = counts[:, LANES:]
        target[start + size : start + size + size // 2, :] = jnp.where(
            left, rest[0 : size // 2], pltpu.roll(rest[size // 2 :], HALF_LANES, 1)
        )
        target[start + size + size // 2 :, :] = extras[pl.ds(pl.multiple_of(owner * 8, 8), 8), :]


def near_kernel(groups, share, weighted_ref, far_ref, close_ref, totals_ref, *refs):
    own_parts, own_sum_ref = refs[:groups], refs[groups]
    targets, (near, tile, folded) = refs[groups + 1 : 2 * groups + 1], refs[2 * groups + 1 :]
    rows, snps = near.shape
    half = snps // 2
    odd = odd_block()

    def unpack(up_ref, down_ref):
        pieces = load_packed(up_ref[0 : rows // 2, :], down_ref[0 : rows // 2, :])
        for side in range(2):
            where = slice(side * (rows // 2), (side + 1) * (rows // 2))
            for number in range(3):
                near[where, number * LANES : (number + 1) * LANES] = pieces[side][number]

    @pl.when(odd)
    def _():
        unpack(far_ref, close_ref)

    @pl.when(jnp.logical_not(odd))
    def _():
        unpack(close_ref, far_ref)

    tile[...] = jnp.dot(weighted_ref[...], near[...], preferred_element_type=jnp.float32)
    row, col = iota((half, snps), 0), iota((half, snps), 1)
    moved = (col >= half) & (col - half < row)
    turned = pltpu.roll(tile[0:half, :], half, 1)
    folded[0:half, :] = to_fields(jnp.where(moved, turned, tile[half:snps, :]))
    if folded.shape[0] > half:
        folded[half:, :] = jnp.zeros((folded.shape[0] - half, snps), jnp.int32)
    square = (snps, snps)
    far = jnp.sum(
        jnp.where(iota(square, 0) == iota(square, 1), tile[0:snps, :], 0.0), axis=0, keepdims=True
    )
    extras = to_fields(
        jnp.concatenate(
            [totals_ref[0:2, :], tile[snps : snps + 1, :], far, jnp.zeros((4, snps))], axis=0
        )
    )
    send_shares(groups, folded, share, targets)
    for target in targets:
        target[share:, :] = extras
    own_sum_ref[...] = sum((part[...] for part in own_parts[1:]), own_parts[0][...])


def annots_kernel(annot_ref, far_ref, close_ref, own_ref, near_ref):
    snps = annot_ref.shape[1]
    own = annot_ref[...].astype(jnp.float32)
    own = jnp.concatenate([own, jnp.zeros((LANES - own.shape[0], snps), jnp.float32)], axis=0)
    own_ref[...] = own.T
    near_ref[...] = near_annots_by_snp(far_ref, close_ref)


def near_annots_by_snp(far_ref, close_ref):
    part, snps = far_ref.shape
    wide = 2 * part
    odd = odd_block()
    far, close = far_ref[...].astype(jnp.float32), close_ref[...].astype(jnp.float32)
    first, second = load_packed(jnp.where(odd, far, close), jnp.where(odd, close, far))
    near = jnp.concatenate(
        [
            jnp.concatenate([piece.astype(jnp.float32) for piece in first], axis=1),
            jnp.concatenate([piece.astype(jnp.float32) for piece in second], axis=1),
            jnp.zeros((LANES - wide, snps), jnp.float32),
        ],
        axis=0,
    )
    return near.T


def column_stats(totals, count):
    size = jnp.maximum(count, 1.0)
    frequency = totals / size
    variance = jnp.maximum(frequency * (1.0 - frequency), VARIANCE_FLOOR)
    inverse = 1.0 / jnp.sqrt(size * variance)
    low = ((0.0 - frequency) * inverse).astype(jnp.bfloat16).astype(jnp.float32)
    high = ((1.0 - frequency) * inverse).astype(jnp.bfloat16).astype(jnp.float32)
    step = high - low
    root = 1.0 / jnp.sqrt(size)
    return step, step * totals * root, (low * count + step * totals) * root


def correlation(row, col, count):
    return row[0] * col[0] * count - row[1] * col[1] + row[2] * col[2]


def split(values):
    high = values.astype(jnp.bfloat16)
    return high, (values - high.astype(jnp.float32)).astype(jnp.bfloat16)


def dot_split(values, right, axis):
    dims = (((axis,), (0,)), ((), ()))
    return sum(
        lax.dot_general(part, right, dims, preferred_element_type=jnp.float32)
        for part in split(values)
    )


def score_kernel(groups, share, reach_ref, *refs):
    own_sum_ref, near_parts = refs[0], refs[1 : groups + 1]
    annot_ref, near_annot_ref = refs[groups + 1 : groups + 3]
    targets = refs[groups + 3 : 2 * groups + 3]
    table, annots, near_annots, scores = refs[2 * groups + 3 :]
    snps = annot_ref.shape[0]
    half = snps // 2
    out_share = snps // groups
    me = lax.axis_index("hap")
    block = lax.axis_index("snp")
    last = reach_ref.shape[0] - 1
    reach_here = reach_ref[block]
    reach_up = reach_ref[jnp.minimum(block + 1, last)]
    reach_down = reach_ref[jnp.maximum(block - 1, 0)]

    own_counts = own_sum_ref[...]
    near_sums = sum((part[...] for part in near_parts[1:]), near_parts[0][...])
    extras = from_fields(near_sums[share:, :])
    near_counts = near_sums[0:share, :]

    own_stats, near_stats, lines = [], [], []
    for pop in range(2):
        count = extras[pop][1:2, :]
        own_stats.append(column_stats(extras[pop][0:1, :], count))
        near_stats.append(column_stats(extras[pop][2:3, :], count))
        lines += [*own_stats[pop], *near_stats[pop], extras[pop][0:1, :], extras[pop][3:4, :]]
    by_row = jnp.concatenate(lines, axis=0).T
    table[0:snps, 0:16] = by_row
    if table.shape[0] > snps:
        table[snps:, 0:16] = jnp.zeros((table.shape[0] - snps, 16), jnp.float32)
    annots[0:snps, :] = annot_ref[...]
    near_annots[0:snps, :] = near_annot_ref[...]
    if annots.shape[0] > snps:
        annots[snps:, :] = jnp.zeros((annots.shape[0] - snps, LANES), jnp.float32)

    low_rows = pl.multiple_of(me * share, 8)
    high_rows = pl.multiple_of(half + me * share, 8)

    def both(ref):
        return jnp.concatenate([ref[pl.ds(low_rows, share), :], ref[pl.ds(high_rows, share), :]], axis=0)

    here = both(table)
    own_count = jnp.concatenate([pltpu.roll(own_counts, half, 1), own_counts], axis=0)
    near_count = jnp.concatenate([pltpu.roll(near_counts, half, 1), near_counts], axis=0)
    shape = (2 * share, snps)
    local, col = iota(shape, 0), iota(shape, 1)
    low = local < share
    place = jnp.where(low, local, local - share) + me * share
    row = jnp.where(low, place, place + half)
    own_fields, near_fields = from_fields(own_count), from_fields(near_count)
    own_product, near_product = 1.0, 1.0
    for pop in range(2):
        row_stats = [here[:, 8 * pop + k : 8 * pop + k + 1] for k in range(3)]
        own_product *= correlation(row_stats, own_stats[pop], own_fields[pop])
        near_product *= correlation(row_stats, near_stats[pop], near_fields[pop])
    real = place < half
    own_inside = real & ((low & (col > row)) | (~low & (col >= half) & (col < row)))
    own_inside &= jnp.abs(col - row) <= reach_here
    own_kept = jnp.where(own_inside, own_product, 0.0)
    in_upper = col < half
    near_inside = real & ((low & (col < row)) | (~low & (in_upper | (col > row))))
    distance = jnp.where(in_upper, snps + col - row, snps + row - col)
    near_here = jnp.where(near_inside & (distance <= reach_here), near_product, 0.0)
    reach_there = jnp.where(in_upper, reach_up, reach_down)
    near_there = jnp.where(near_inside & (distance <= reach_there), near_product, 0.0)

    rows_here = both(annots)
    rows_there = pltpu.roll(rows_here, HALF_LANES, 1)
    scores[0:snps, :] = dot_split(
        jnp.concatenate([own_kept, near_there], axis=0),
        jnp.concatenate([rows_here, rows_there], axis=0).astype(jnp.bfloat16),
        0,
    )
    direct = dot_split(
        jnp.concatenate([own_kept, near_here], axis=1),
        jnp.concatenate([annot_ref[...], near_annot_ref[...]], axis=0).astype(jnp.bfloat16),
        1,
    )
    scores[pl.ds(low_rows, share), :] += direct[0:share, :]
    scores[pl.ds(high_rows, share), :] += direct[share:, :]

    out_rows = pl.ds(pl.multiple_of(me * out_share, 8), out_share)
    mine = table[out_rows, :]
    self_product, far_product = 1.0, 1.0
    for pop in range(2):
        k = 8 * pop
        own_row = [mine[:, k + s : k + s + 1] for s in range(3)]
        near_row = [mine[:, k + 3 + s : k + 4 + s] for s in range(3)]
        self_product *= correlation(own_row, own_row, mine[:, k + 6 : k + 7])
        far_product *= correlation(own_row, near_row, mine[:, k + 7 : k + 8])
    mine_annots = annots[out_rows, :]
    far_reach = jnp.where(me < groups // 2, reach_up, reach_down)
    scores[out_rows, :] += (
        mine_annots * self_product
        + near_annots[out_rows, :] * jnp.where(reach_here >= snps, far_product, 0.0)
        + pltpu.roll(mine_annots, HALF_LANES, 1) * jnp.where(far_reach >= snps, far_product, 0.0)
    )
    send_shares(groups, scores, out_share, targets)


def pack_halves(values):
    half = values.shape[0] // 2
    left = iota((half, LANES), 1) < HALF_LANES
    return jnp.where(left, values[0:half], pltpu.roll(values[half:], HALF_LANES, 1))


def unpack_halves(packed):
    return jnp.concatenate([packed, pltpu.roll(packed, HALF_LANES, 1)], axis=0)


def dot_rounded(values, right, axis):
    dims = (((axis,), (0,)), ((), ()))
    return lax.dot_general(
        values.astype(jnp.bfloat16), right, dims, preferred_element_type=jnp.float32
    )


def owner_places(groups, size):
    me = lax.axis_index("hap")

    def mine(blocks, slot):
        value = blocks[0][slot]
        for group in range(1, groups):
            value = jnp.where(me == group, blocks[group][slot], value)
        return value * size

    left = [mine(LEFT_BLOCKS, slot) for slot in range(groups)]
    right = [mine(RIGHT_BLOCKS, slot) for slot in range(groups)]
    return left + left[0:1], right + [(2 * me + 1) * size]


def spare_places(groups, size):
    me = lax.axis_index("hap")

    def mine(blocks, slot):
        value = blocks[0][slot]
        for group in range(1, groups):
            value = jnp.where(me == group, blocks[group][slot], value)
        return value * size

    return [[mine(blocks, slot) for slot in range(groups)] for blocks in (SPARE_OWN, SPARE_NEAR)]


def rows_at(ref, places, size):
    return jnp.concatenate([ref[pl.ds(pl.multiple_of(place, 8), size), :] for place in places], axis=0)


def own_score_kernel(
    groups, share, reach_ref, *refs
):
    own_parts, refs = refs[:groups], refs[groups:]
    annot_ref, far_ref, close_ref, scores, mine_ref, rows_ref, columns_ref, *refs = refs
    spare_rows_ref, spare_columns_ref, near_annot_ref, *targets, table = refs
    near_annot_ref[...] = near_annots_by_snp(far_ref, close_ref)
    snps = annot_ref.shape[0]
    half = snps // 2
    wide = snps // groups
    tiles = snps // LANES
    me = lax.axis_index("hap")
    reach_here = reach_ref[lax.axis_index("snp")]
    own_sums = sum((part[...] for part in own_parts[1:]), own_parts[0][...])
    own_counts = from_tiles(own_sums[0 : tiles * share, :], share)
    extras = from_fields(own_sums[tiles * share :, :])

    own_stats, lines = [], []
    for pop in range(2):
        count = jnp.concatenate([extras[pop][tiles : tiles + 1, :]] * tiles, axis=1)
        totals = jnp.concatenate([extras[pop][k : k + 1, :] for k in range(tiles)], axis=1)
        own_stats.append(column_stats(totals, count))
        lines += [*own_stats[pop], totals]
    table[:, 0:8] = jnp.concatenate(lines, axis=0).T

    low_rows = pl.multiple_of(me * share, 8)
    high_rows = pl.multiple_of(half + me * share, 8)

    def both(ref):
        return jnp.concatenate([ref[pl.ds(low_rows, share), :], ref[pl.ds(high_rows, share), :]], axis=0)

    here = both(table)
    own_fields = from_fields(
        jnp.concatenate([pltpu.roll(own_counts, half, 1), own_counts], axis=0)
    )
    shape = (2 * share, snps)
    local, col = iota(shape, 0), iota(shape, 1)
    low = local < share
    row = jnp.where(low, local, local + half - share) + me * share
    product = 1.0
    for pop in range(2):
        row_stats = [here[:, 4 * pop + k : 4 * pop + k + 1] for k in range(3)]
        product *= correlation(row_stats, own_stats[pop], own_fields[pop])
    inside = (low & (col > row)) | (~low & (col >= half) & (col < row))
    own_kept = jnp.where(inside & (jnp.abs(col - row) <= reach_here), product, 0.0)
    rows_here = both(annot_ref).astype(jnp.bfloat16)
    scores[...] = dot_rounded(own_kept, rows_here, 0)
    direct = dot_rounded(own_kept, annot_ref[...].astype(jnp.bfloat16), 1)
    scores[pl.ds(low_rows, share), :] += direct[0:share, :]
    scores[pl.ds(high_rows, share), :] += direct[share:, :]

    slice_rows = pl.ds(pl.multiple_of(me * wide, 8), wide)
    mine = table[slice_rows, :]
    mine_ref[...] = mine
    product = 1.0
    for pop in range(2):
        own_row = [mine[:, 4 * pop + k : 4 * pop + k + 1] for k in range(4)]
        product *= correlation(own_row, own_row, own_row[3])
    scores[slice_rows, :] += annot_ref[slice_rows, :] * product
    for step, target in enumerate(targets, 2):
        group = partner(me, step, groups)
        rows = scores[pl.ds(pl.multiple_of(group * wide, 8), wide), :]
        target[...] = pack_halves(rows).astype(target.dtype)

    size = wide // 2
    left_places, right_places = owner_places(groups, size)
    left_table, right_table = rows_at(table, left_places, size), rows_at(table, right_places, size)
    is_left = iota(rows_ref.shape[1:], 1) < size
    for pop in range(2):
        for k in range(3):
            column = slice(4 * pop + k, 4 * pop + k + 1)
            rows_ref[3 * pop + k] = jnp.where(is_left, left_table[:, column], right_table[:, column])
    theirs = near_annot_ref[slice_rows, :]
    columns = [theirs[0:size], pltpu.roll(theirs[size:], HALF_LANES, 1), jnp.zeros((LANES - wide, LANES))]
    columns_ref[...] = jnp.concatenate(columns, axis=0).astype(jnp.bfloat16)

    own_places, near_places = spare_places(groups, size)
    shape = spare_rows_ref.shape[1:]
    lane = iota(shape, 1)
    tables = [table[pl.ds(pl.multiple_of(place, 8), size), :] for place in own_places]
    for pop in range(2):
        for k in range(3):
            column = slice(4 * pop + k, 4 * pop + k + 1)
            spare_rows_ref[3 * pop + k] = by_slot(
                [jnp.broadcast_to(values[:, column], shape) for values in tables], lane, size
            )
    columns = [rows_at(near_annot_ref, near_places, size)]
    columns.append(jnp.zeros((shape[1] - groups * size, LANES), jnp.float32))
    spare_columns_ref[...] = jnp.concatenate(columns, axis=0).astype(jnp.bfloat16)


def near_score_kernel(groups, share, reach_ref, *refs):
    near_parts, refs = refs[:groups], refs[groups:]
    own_ref, mine_ref, rows_ref, columns_ref, spare_rows_ref, spare_columns_ref = refs[:6]
    near_annot_ref, annot_ref, masks_ref, spare_mask_ref, own_rows_ref = refs[6:11]
    out_ref, send_ref, near_out_ref, flipped, scores, other = refs[11:]
    snps = annot_ref.shape[0]
    wide = snps // groups
    size = wide // 2
    tiles = snps // LANES
    me = lax.axis_index("hap")
    block = lax.axis_index("snp")
    last = reach_ref.shape[0] - 1
    reach_here = reach_ref[block]
    reach_there = jnp.where(
        me < groups // 2, reach_ref[jnp.minimum(block + 1, last)], reach_ref[jnp.maximum(block - 1, 0)]
    )

    scores[...] = own_ref[...]
    near_sums = sum((part[...] for part in near_parts[1:]), near_parts[0][...])
    near_counts = from_tiles(near_sums[0 : tiles * share, :], share)
    start = tiles * share
    rest = near_sums[start + size : start + size + size // 2, :]
    rest = jnp.concatenate([rest, pltpu.roll(rest, HALF_LANES, 1)], axis=0)
    spare_fields = from_fields(jnp.concatenate([near_sums[start : start + size, :], rest], axis=1))
    extras = from_fields(near_sums[start + size + size // 2 :, :])
    near_stats, near_lines, spare_stats = [], [], []
    for pop in range(2):
        count = extras[pop][0:1, :]
        totals = jnp.concatenate([extras[pop][3:4, :], extras[pop][4:5, :]], axis=1)
        spare_stats.append(column_stats(totals, jnp.concatenate([count, count], axis=1)))
        near_stats.append(column_stats(extras[pop][1:2, :], extras[pop][0:1, :]))
        near_lines += [*near_stats[pop], extras[pop][2:3, :]]
    near_table = jnp.concatenate(near_lines, axis=0).T[0:wide, :]

    slots = [near_counts[:, 0:LANES]]
    for slot in range(1, groups):
        slots.append(pltpu.roll(near_counts, snps - slot * wide, 1)[:, 0:LANES])
    flipped[:, 0:size] = slots[0].T
    slots.append(pltpu.roll(flipped[0:size, :], size, 1))
    near_fields = from_fields(jnp.concatenate(slots, axis=0))
    product = 1.0
    for pop in range(2):
        row_stats = [rows_ref[3 * pop + k] for k in range(3)]
        product *= correlation(row_stats, near_stats[pop], near_fields[pop])
    near_here = jnp.where(masks_ref[0] > 0.0, product, 0.0)
    near_there = jnp.where(masks_ref[1] > 0.0, product, 0.0)
    slice_rows = pl.ds(pl.multiple_of(me * wide, 8), wide)
    direct = dot_rounded(near_here, columns_ref[...], 1)
    turned = pltpu.roll(direct, HALF_LANES, 1)
    left_places, right_places = owner_places(groups, size)
    other[...] = jnp.zeros_like(other)
    for ref, values, places in ((scores, direct, left_places[:-1]), (other, turned, right_places)):
        for slot, place in enumerate(places):
            ref[pl.ds(pl.multiple_of(place, 8), size), :] += values[slot * size : (slot + 1) * size, :]
    product = 1.0
    for pop in range(2):
        row_stats = [spare_rows_ref[3 * pop + k] for k in range(3)]
        product *= correlation(row_stats, spare_stats[pop], spare_fields[pop])
    spare_here = jnp.where(spare_mask_ref[...] > 0.0, product, 0.0)
    lane = iota(spare_here.shape, 1)
    spare_here = [
        jnp.where((lane >= slot * size) & (lane < (slot + 1) * size), spare_here, 0.0)
        for slot in range(groups)
    ]
    direct = dot_rounded(jnp.concatenate(spare_here, axis=0), spare_columns_ref[...], 1)
    for slot, place in enumerate(spare_places(groups, size)[0]):
        scores[pl.ds(pl.multiple_of(place, 8), size), :] += direct[slot * size : (slot + 1) * size, :]
    near_scores = dot_rounded(near_there, own_rows_ref[...], 0)
    near_scores = jnp.where(
        iota((size, LANES), 1) < HALF_LANES, near_scores[0:size], near_scores[size:wide]
    )

    mine_table = mine_ref[...]
    far_product = 1.0
    for pop in range(2):
        own_row = [mine_table[:, 4 * pop + k : 4 * pop + k + 1] for k in range(3)]
        near_row = [near_table[:, 4 * pop + k : 4 * pop + k + 1] for k in range(4)]
        far_product *= correlation(own_row, near_row, near_row[3])
    scores[slice_rows, :] += near_annot_ref[slice_rows, :] * jnp.where(reach_here >= snps, far_product, 0.0)
    far_scores = annot_ref[slice_rows, :] * jnp.where(reach_there >= snps, far_product, 0.0)
    near_out_ref[...] = (near_scores + pack_halves(far_scores)).astype(near_out_ref.dtype)

    def packed(step):
        group = partner(me, step, groups)
        rows = pl.ds(pl.multiple_of(group * wide, 8), wide)
        return pack_halves(scores[rows, :] + other[rows, :])

    out_ref[...] = packed(0)
    send_ref[...] = packed(1).astype(send_ref.dtype)


def column_finish_kernel(*refs):
    *parts, out_ref = refs
    packed = sum(part[...].astype(jnp.float32) for part in parts)
    out_ref[...] = unpack_halves(packed).T[0 : out_ref.shape[0], :]


def sum_kernel(*refs):
    *parts, own_ref, there_ref = refs
    total = sum((part[...].astype(jnp.float32) for part in parts[1:]), parts[0][...])
    own_ref[...] = total
    half = there_ref.shape[0]
    left = iota((half, LANES), 1) < HALF_LANES
    second = total[half:]
    if second.shape[0] < half:
        second = jnp.concatenate([second, jnp.zeros((half - second.shape[0], LANES))], axis=0)
    there_ref[...] = jnp.where(left, pltpu.roll(total[0:half], HALF_LANES, 1), second)


def finish_kernel(own_ref, there_ref, out_ref):
    annots, rows = out_ref.shape
    there = there_ref[...]
    there = jnp.concatenate([there, pltpu.roll(there, HALF_LANES, 1)], axis=0)
    out_ref[...] = (own_ref[...] + there[0:rows]).T[0:annots, :]


def around(value, groups, step):
    return lax.ppermute(
        value, "hap", [(source, partner(source, step, groups)) for source in range(groups)]
    )


def swapped(value, first):
    pairs = []
    for block in range(first, lax.axis_size("snp") - 1, 2):
        pairs += [(block, block + 1), (block + 1, block)]
    return lax.ppermute(value, "snp", pairs)


def per_device(haplotypes, labels, annotations, reach):
    rows, snps = haplotypes.shape
    half = snps // 2
    groups = lax.axis_size("hap")
    blocks = lax.axis_size("snp")
    share = round_up(-(-half // groups), 16)
    folded_rows = share * groups
    out_share = snps // groups
    padded = half + folded_rows
    annot_part = 32
    bf16, f32, i32 = jnp.bfloat16, jnp.float32, jnp.int32
    shape = jax.ShapeDtypeStruct

    packed = shape((rows // 2 + annot_part, snps), bf16)
    haplotypes = pltpu.with_memory_space_constraint(haplotypes, pltpu.HBM)
    annots_in = pltpu.with_memory_space_constraint(annotations, pltpu.HBM)
    alleles, far, close = call(
        prepare_kernel,
        [shape((rows, snps), bf16), packed, packed],
        [HBM, HBM],
        [
            pltpu.VMEM((rows, snps), i32),
            pltpu.VMEM(annotations.shape, i32),
            pltpu.SemaphoreType.DMA((2 * CHUNKS + 1,)),
        ],
        moved=rows * snps * 8,
    )(haplotypes, annots_in)
    from_far = swapped(far, 1)
    from_close = swapped(close, 0)

    by_column = groups == len(LEFT_BLOCKS)
    by_snp = shape((snps, LANES), f32)
    compact = shape((share * (snps // LANES) + 8, LANES), i32)
    own_share_counts = compact if by_column else shape((share, snps), i32)
    near_share_counts = shape((compact.shape[0] + share + share // 2, LANES), i32)
    tile = pltpu.VMEM((snps + 16, snps), f32)
    folded = pltpu.VMEM((folded_rows, snps), i32)
    weighted, totals, *own_parts = call(
        functools.partial(own_kernel, groups, share),
        [shape((snps + 16, rows), bf16), shape((8, snps), f32)] + [own_share_counts] * groups,
        [VMEM, VMEM],
        [tile, folded],
        flops=2 * rows * snps * snps,
        moved=rows * snps * 4,
    )(alleles, labels.reshape(1, rows))
    order = (2, 3, 1) if by_column else range(groups - 1, 0, -1)
    own_parts = [own_parts[0]] + [around(own_parts[k], groups, k) for k in order]

    near_shapes = [own_share_counts] + [near_share_counts if by_column else shape((share + 8, snps), i32)] * groups
    if by_column:
        work = dict(flops=4 * rows * snps * LANES, moved=rows * snps * 4)
        flipped = pltpu.VMEM((snps, LANES), f32)
        pair_rows = (groups + 1) * (out_share // 2)
        side_shapes = [((2 * share, snps), i32), ((2 * (share + 8), 2 * LANES), i32), ((8, snps), f32)]
        *close_counts, own_annots, masks, spare_mask, own_rows = call(
            functools.partial(close_kernel, groups),
            [shape(*args) for args in side_shapes]
            + [
                by_snp,
                shape((2, pair_rows, LANES), f32),
                shape((share, 2 * LANES), f32),
                shape((pair_rows, LANES), bf16),
            ],
            [SMEM] + [VMEM] * 3,
            [tile, flipped],
            **work,
        )(reach, weighted, from_close, annotations)
        near_parts = call(
            functools.partial(far_kernel, groups, share),
            near_shapes[1:],
            [VMEM] * 6,
            [pltpu.VMEM(*args) for args in side_shapes]
            + [tile, flipped, pltpu.VMEM((8 * groups, LANES), i32)],
            **work,
        )(weighted, from_far, *close_counts, totals)
    else:
        own_sum, *near_parts = call(
            functools.partial(near_kernel, groups, share),
            near_shapes,
            [VMEM] * (4 + groups),
            [pltpu.VMEM((rows, snps), bf16), tile, folded],
            flops=2 * rows * snps * snps,
            moved=rows * snps * 4,
        )(weighted, from_far, from_close, totals, *own_parts)
    near_parts = [near_parts[0]] + [around(near_parts[k], groups, k) for k in order]

    if not by_column:
        own_annots, near_annots = call(annots_kernel, [by_snp, by_snp], [VMEM] * 3, moved=1 << 20)(
            annotations, from_far[rows // 2 :], from_close[rows // 2 :]
        )
    pairs = []
    for block in range(blocks):
        for group in range(groups):
            target = block + 1 if group < groups // 2 else block - 1
            if 0 <= target < blocks:
                pairs.append((block * groups + group, target * groups + group))

    def to_neighbour(value):
        return lax.ppermute(value, ("snp", "hap"), pairs)

    result = shape((annotations.shape[0], out_share), f32)
    half_share = round_up(-(-out_share // 2), 8)
    own_share = shape((out_share, LANES), f32)
    packed_share = shape((half_share, LANES), f32)
    if by_column:
        sent = shape((half_share, LANES), bf16)
        *prepared, second, third = call(
            functools.partial(own_score_kernel, groups, share),
            [
                by_snp,
                shape((out_share, LANES), f32),
                shape((6, pair_rows, LANES), f32),
                shape((LANES, LANES), bf16),
                shape((6, share, 2 * LANES), f32),
                shape((2 * LANES, LANES), bf16),
                by_snp,
                sent,
                sent,
            ],
            [SMEM] + [VMEM] * (groups + 3),
            [pltpu.VMEM((snps, LANES), f32)],
            flops=1 << 33,
            moved=1 << 20,
        )(reach, *own_parts, own_annots, from_far[rows // 2 :], from_close[rows // 2 :])
        parts = [around(third, groups, 3), around(second, groups, 2)]
        own_scores, send, there = call(
            functools.partial(near_score_kernel, groups, share),
            [packed_share, sent, sent],
            [SMEM] + [VMEM] * (groups + 11),
            [pltpu.VMEM((LANES, LANES), i32)] + [pltpu.VMEM((snps, LANES), f32)] * 2,
            flops=1 << 26,
            moved=1 << 21,
        )(reach, *near_parts, *prepared, own_annots, masks, spare_mask, own_rows)
        parts += [around(send, groups, 1), to_neighbour(there)]
        return call(column_finish_kernel, result, [VMEM] * 5)(own_scores, *parts)

    tall = pltpu.VMEM((padded, LANES), f32)
    scores = call(
        functools.partial(score_kernel, groups, share),
        [own_share] + [shape((out_share, LANES), bf16)] * (groups - 1),
        [SMEM] + [VMEM] * (groups + 3),
        [tall, tall, tall, tall],
        flops=1 << 26,
        moved=1 << 21,
    )(reach, own_sum, *near_parts, own_annots, near_annots)
    scores = [scores[0]] + [around(scores[k], groups, k) for k in range(groups - 1, 0, -1)]
    own_scores, near_scores = call(sum_kernel, [own_share, packed_share], [VMEM] * groups)(*scores)
    return call(finish_kernel, result, [VMEM] * 2)(own_scores, to_neighbour(near_scores))


def solution(mesh):
    in_specs = (
        P("hap", ("parts", "snp")),
        P(("parts", "hap")),
        P(None, ("parts", "snp")),
        P("parts"),
    )
    out_specs = P(None, ("parts", "snp", "hap"))
    return jax.shard_map(
        per_device, mesh=mesh, in_specs=in_specs, out_specs=out_specs, check_vma=False
    )
```

```python
import functools

import jax
import jax.numpy as jnp
from jax import lax
from jax.experimental import pallas as pl
from jax.experimental.pallas import tpu as pltpu
from jax.sharding import PartitionSpec as P

VARIANCE_FLOOR = 0.01
BASE_BITS = 12
BASE = 1 << BASE_BITS
FIELD_BITS = 16
LANES = 128
HALF_LANES = LANES // 2
CHUNKS = 4
VMEM = pl.BlockSpec(memory_space=pltpu.VMEM)
SMEM = pl.BlockSpec(memory_space=pltpu.SMEM)
HBM = pl.BlockSpec(memory_space=pltpu.HBM)
VMEM_LIMIT = 24 * 1024 * 1024


def iota(shape, axis):
    return lax.broadcasted_iota(jnp.int32, shape, axis)


def round_up(value, step):
    return -(-value // step) * step


def to_fields(values):
    whole = values.astype(jnp.int32)
    return whole + (whole >> BASE_BITS) * ((1 << FIELD_BITS) - BASE)


def from_fields(packed):
    first = packed & ((1 << FIELD_BITS) - 1)
    second = lax.shift_right_logical(packed, FIELD_BITS)
    return first.astype(jnp.float32), second.astype(jnp.float32)


def call(kernel, out_shape, in_specs, scratch_shapes=(), flops=0, moved=0):
    several = isinstance(out_shape, (list, tuple))
    return pl.pallas_call(
        kernel,
        out_shape=out_shape,
        in_specs=in_specs,
        out_specs=[VMEM] * len(out_shape) if several else VMEM,
        scratch_shapes=list(scratch_shapes),
        compiler_params=pltpu.CompilerParams(vmem_limit_bytes=VMEM_LIMIT),
        cost_estimate=pl.CostEstimate(flops=flops, bytes_accessed=moved, transcendentals=0),
    )


def odd_block():
    return lax.rem(lax.axis_index("snp"), 2) == 1


def store_packed(up_ref, down_ref, where, first, second):
    left = iota((first.shape[0], LANES), 1) < HALF_LANES
    middle = first[:, LANES : 2 * LANES]
    turned = pltpu.roll(second[:, LANES : 2 * LANES], HALF_LANES, 1)
    for ref, side, mixed in (
        (up_ref, slice(0, LANES), jnp.where(left, middle, turned)),
        (down_ref, slice(2 * LANES, 3 * LANES), jnp.where(left, turned, middle)),
    ):
        ref[where, 0:LANES] = first[:, side].astype(jnp.bfloat16)
        ref[where, LANES : 2 * LANES] = mixed.astype(jnp.bfloat16)
        ref[where, 2 * LANES : 3 * LANES] = second[:, side].astype(jnp.bfloat16)


def load_packed(up, down):
    left = iota((up.shape[0], LANES), 1) < HALF_LANES
    up_mixed, down_mixed = up[:, LANES : 2 * LANES], down[:, LANES : 2 * LANES]
    first = jnp.where(left, up_mixed, down_mixed)
    second = jnp.where(left, down_mixed, up_mixed)
    second = pltpu.roll(second.astype(jnp.float32), HALF_LANES, 1).astype(second.dtype)
    return (
        (up[:, :LANES], first, down[:, :LANES]),
        (up[:, 2 * LANES :], second, down[:, 2 * LANES :]),
    )


def prepare_kernel(hap_ref, annot_ref, alleles_ref, far_ref, close_ref, held, held_annots, sems):
    rows = hap_ref.shape[0]
    annot_rows = annot_ref.shape[0]
    size = rows // (2 * CHUNKS)
    starts = [side * (rows // 2) + chunk * size for chunk in range(CHUNKS) for side in range(2)]
    copies = [
        pltpu.make_async_copy(
            hap_ref.at[pl.ds(start, size)], held.at[pl.ds(start, size)], sems.at[number]
        )
        for number, start in enumerate(starts)
    ]
    copies.append(pltpu.make_async_copy(annot_ref, held_annots, sems.at[2 * CHUNKS]))
    for copy in copies:
        copy.start()
    part = far_ref.shape[0] - rows // 2
    odd = odd_block()

    def store(where, first, second):
        @pl.when(odd)
        def _():
            store_packed(close_ref, far_ref, where, first, second)

        @pl.when(jnp.logical_not(odd))
        def _():
            store_packed(far_ref, close_ref, where, first, second)

    for chunk in range(CHUNKS):
        pair = []
        for side in range(2):
            number = 2 * chunk + side
            copies[number].wait()
            where = slice(starts[number], starts[number] + size)
            values = held[where, :].astype(jnp.float32)
            alleles_ref[where, :] = values.astype(jnp.bfloat16)
            pair.append(values)
        store(slice(chunk * size, (chunk + 1) * size), *pair)
    copies[-1].wait()
    annots = jnp.concatenate(
        [
            held_annots[...].astype(jnp.float32),
            jnp.zeros((2 * part - annot_rows, annot_ref.shape[1]), jnp.float32),
        ],
        axis=0,
    )
    store(slice(rows // 2, rows // 2 + part), annots[:part], annots[part:])


def partner(group, step, groups):
    if groups & (groups - 1) == 0:
        return group ^ step
    return (group + step) % groups


def send_shares(groups, source, share, targets):
    me = lax.axis_index("hap")
    for step, target in enumerate(targets):
        group = partner(me, step, groups)
        rows = source[pl.ds(pl.multiple_of(group * share, 8), share), :]
        target[0:share, :] = rows.astype(target.dtype)


def send_tiles(groups, source, share, targets):
    me = lax.axis_index("hap")
    for step, target in enumerate(targets):
        owner = partner(me, step, groups)
        counts = source[pl.ds(pl.multiple_of(owner * share, 8), share), :]
        for k in range(source.shape[1] // LANES):
            target[k * share : (k + 1) * share, :] = counts[:, k * LANES : (k + 1) * LANES]


def from_tiles(counts, share):
    tiles = counts.shape[0] // share
    return jnp.concatenate([counts[k * share : (k + 1) * share, :] for k in range(tiles)], axis=1)


def own_kernel(groups, share, alleles_ref, label_ref, *refs):
    weighted_ref, totals_ref, *targets = refs[: 2 + groups]
    tile, folded = refs[2 + groups :]
    rows, snps = alleles_ref.shape
    half = snps // 2
    weight = jnp.where(label_ref[...] > 0, float(BASE), 1.0)
    weighted_ref[0:snps, :] = alleles_ref[...].T * weight.astype(jnp.bfloat16)
    extra = weighted_ref.shape[0] - snps
    weighted_ref[snps:, :] = jnp.broadcast_to(weight, (extra, rows)).astype(jnp.bfloat16)
    tile[...] = jnp.dot(weighted_ref[...], alleles_ref[...], preferred_element_type=jnp.float32)
    count = jnp.sum(weight, axis=1, keepdims=True)
    totals_ref[...] = jnp.concatenate(
        [tile[snps : snps + 1, :], jnp.broadcast_to(count, (1, snps)), jnp.zeros((6, snps))], axis=0
    )
    row, col = iota((half, snps), 0), iota((half, snps), 1)
    moved = (col < half) | (col - half > row)
    turned = pltpu.roll(tile[0:half, :], half, 1)
    folded[0:half, :] = to_fields(jnp.where(moved, turned, tile[half:snps, :]))
    if folded.shape[0] > half:
        folded[half:, :] = jnp.zeros((folded.shape[0] - half, snps), jnp.int32)
    if groups != len(LEFT_BLOCKS):
        send_shares(groups, folded, share, targets)
        return
    tiles = snps // LANES
    shared = [totals_ref[0:1, k * LANES : (k + 1) * LANES] for k in range(tiles)]
    shared += [totals_ref[1:2, 0:LANES], jnp.zeros((7 - tiles, LANES))]
    extras = to_fields(jnp.concatenate(shared, axis=0))
    send_tiles(groups, folded, share, targets)
    for target in targets:
        target[tiles * share :, :] = extras


LEFT_BLOCKS = ((0, 1, 2, 3), (2, 3, 6, 7), (4, 0, 1, 2), (6, 0, 4, 5))
RIGHT_BLOCKS = ((2, 3, 6, 7), (4, 5, 6, 7), (0, 1, 2, 4), (0, 4, 5, 6))


SPARE_OWN = ((0, 0, 0, 0), (1, 1, 2, 2), (4, 5, 6, 7), (6, 6, 7, 7))
SPARE_NEAR = ((4, 5, 6, 7), (4, 5, 4, 5), (3, 3, 3, 3), (1, 2, 1, 2))


def fold_spare(tile, spare, first):
    owners = len(SPARE_OWN)
    snps = tile.shape[1]
    size = snps // (2 * owners)
    count = spare.shape[0] // 2
    totals = tile[snps : snps + count - size, :]
    lane = iota((count, snps), 1)
    for number, owner in enumerate(range(first, first + 2)):
        mixed = None
        for slot in range(owners):
            own, near = SPARE_OWN[owner][slot], SPARE_NEAR[owner][slot]
            before = (SPARE_OWN[owner][slot - 1], SPARE_NEAR[owner][slot - 1] + 1) if slot else None
            if before == (own, near):
                continue
            values = jnp.concatenate([tile[own * size : (own + 1) * size, :], totals], axis=0)
            shift = (slot - near) * size % snps
            values = pltpu.roll(values, shift, 1) if shift else values
            mixed = values if mixed is None else jnp.where(lane >= slot * size, values, mixed)
        spare[number * count : (number + 1) * count, :] = to_fields(mixed[:, 0 : spare.shape[1]])


def fold_by_column(tile, flipped, folded, first):
    groups = len(LEFT_BLOCKS)
    owners = range(first, first + groups // 2)
    snps = folded.shape[1]
    wide = snps // groups
    size = wide // 2
    shape = (size, snps)
    row, lane = iota(shape, 0), iota(shape, 1)

    def block(number):
        return tile[number * size : (number + 1) * size, :]

    diagonal, within = block(2 * first), lane - 2 * first * size
    for number in range(2 * first + 1, 2 * first + groups):
        diagonal = jnp.where(lane >= number * size, block(number), diagonal)
        within = jnp.where(lane >= number * size, lane - number * size, within)
    apart = jnp.sum(jnp.where(row == within, diagonal, 0.0), axis=0, keepdims=True)
    flipped[:, 0:size] = diagonal.T
    corner = diagonal
    for owner in owners:
        start = (2 * owner + 1) * size
        turned = jnp.concatenate(
            [flipped[start : start + size, :], jnp.zeros((size, snps - LANES), jnp.float32)], axis=1
        )
        if owner:
            turned = pltpu.roll(turned, owner * wide, 1)
        inside = lane - owner * wide
        other = (row <= inside) if first == 0 else (row >= inside)
        corner = jnp.where((inside >= 0) & (inside < size) & other, turned, corner)
    rolled = []
    for shift in range(groups):
        mixed = None
        for owner in owners:
            slot = (owner + shift) % groups
            left = block(LEFT_BLOCKS[owner][slot]) if slot else corner
            start = owner * wide
            mixed = left if mixed is None else jnp.where(lane >= start, left, mixed)
            mixed = jnp.where(lane >= start + size, block(RIGHT_BLOCKS[owner][slot]), mixed)
        rolled.append(pltpu.roll(mixed, shift * wide, 1) if shift else mixed)
    for number, owner in enumerate(owners):
        mixed = rolled[(0 - owner) % groups]
        for slot in range(1, groups):
            mixed = jnp.where(lane >= slot * wide, rolled[(slot - owner) % groups], mixed)
        folded[number * size : (number + 1) * size, :] = to_fields(mixed)
    return apart


def above(far):
    return odd_block() == far


def side_dot(weighted_ref, side_ref):
    rows = weighted_ref.shape[1]
    half = rows // 2

    def dot(which, columns):
        return jnp.dot(
            weighted_ref[:, which], side_ref[0:half, columns], preferred_element_type=jnp.float32
        )

    first = dot(slice(0, half), slice(0, 2 * LANES))
    second = dot(slice(half, rows), slice(LANES, 3 * LANES))
    whole = first[:, 0:LANES] + second[:, LANES:]
    return whole, first[:, LANES:] + pltpu.roll(second[:, 0:LANES], HALF_LANES, 1)


def fold_side(far, weighted_ref, side_ref, main, spare, lines, tile, flipped):
    snps = tile.shape[1]
    whole, shared = side_dot(weighted_ref, side_ref)
    tile[:, LANES : 2 * LANES] = shared

    def fold(first, start):
        tile[:, start : start + LANES] = whole
        apart = fold_by_column(tile, flipped, main, first)
        fold_spare(tile, spare, 2 - first)
        lines[0:1, :] = tile[snps : snps + 1, :]
        lines[1:2, :] = apart

    @pl.when(above(far))
    def _():
        fold(0, 0)

    @pl.when(jnp.logical_not(above(far)))
    def _():
        fold(2, 2 * LANES)


def close_kernel(groups, reach_ref, weighted_ref, side_ref, annot_ref, *refs):
    main_ref, spare_ref, lines_ref, annots, masks_ref, spare_mask_ref, own_rows_ref, tile, flipped = refs
    fold_side(False, weighted_ref, side_ref, main_ref, spare_ref, lines_ref, tile, flipped)
    snps = annot_ref.shape[1]
    half, wide = snps // 2, snps // groups
    size = wide // 2
    own = annot_ref[...].astype(jnp.float32)
    own = jnp.concatenate([own, jnp.zeros((LANES - own.shape[0], snps), jnp.float32)], axis=0)
    annots[...] = own.T

    me = lax.axis_index("hap")
    block = lax.axis_index("snp")
    last = reach_ref.shape[0] - 1
    upper = me < groups // 2
    reach_here = reach_ref[block]
    reach_there = jnp.where(
        upper, reach_ref[jnp.minimum(block + 1, last)], reach_ref[jnp.maximum(block - 1, 0)]
    )
    left_places, right_places = owner_places(groups, size)
    local, lane = iota((size, LANES), 0), iota((size, LANES), 1)
    own_row = jnp.concatenate(
        [local + jnp.where(lane < size, a, b) for a, b in zip(left_places, right_places)], axis=0
    )
    shape = own_row.shape
    lane = iota(shape, 1)
    apart = jnp.abs(own_row - (lane + me * wide))
    ahead = (own_row - (lane + me * wide)) * jnp.where(upper, 1, -1) > 0
    real = ahead & (lane < wide) & ((lane >= size) | (iota(shape, 0) < groups * size))
    inside = (own_row - half) * jnp.where(upper, 1, -1) < jnp.where(upper, 0, 1)
    masks_ref[0] = jnp.where(real & inside & (snps - apart <= reach_here), 1.0, 0.0)
    masks_ref[1] = jnp.where(real & (snps - apart <= reach_there), 1.0, 0.0)
    own_rows = rows_at(annots, left_places, size) + pltpu.roll(
        rows_at(annots, right_places, size), HALF_LANES, 1
    )
    own_rows_ref[...] = own_rows.astype(jnp.bfloat16)

    own_places, near_places = spare_places(groups, size)
    shape = spare_mask_ref.shape
    local, lane = iota(shape, 0), iota(shape, 1)
    own_row = by_slot([local + place for place in own_places], lane, size)
    near_col = by_slot(
        [lane + (place - slot * size) for slot, place in enumerate(near_places)], lane, size
    )
    close = snps - jnp.abs(own_row - near_col) <= reach_here
    spare_mask_ref[...] = jnp.where(close & (lane < groups * size), 1.0, 0.0)


def by_slot(values, lane, size):
    mixed = values[0]
    for slot in range(1, len(values)):
        mixed = jnp.where(lane >= slot * size, values[slot], mixed)
    return mixed


def far_kernel(groups, share, weighted_ref, side_ref, close_ref, close_spare_ref, close_lines_ref, totals_ref, *refs):
    targets, (main, spare, lines, tile, flipped, extras) = refs[:groups], refs[groups:]
    fold_side(True, weighted_ref, side_ref, main, spare, lines, tile, flipped)
    snps = tile.shape[1]
    half, size = snps // 2, share
    odd = odd_block()

    tiles = snps // LANES
    count = spare.shape[0] // 2
    from_far = (iota((8, snps), 1) < half) == odd
    by_column = jnp.concatenate(
        [totals_ref[1:2, :], jnp.where(from_far, lines[...], close_lines_ref[...])[0:2, :]], axis=0
    )
    by_column = jnp.concatenate([by_column, jnp.zeros((5, snps))], axis=0)
    for owner in range(groups):
        start = owner * (snps // groups)
        columns = pltpu.roll(by_column, snps - start, 1) if owner else by_column
        where = slice((owner & 1) * count + size, (owner & 1) * count + size + 1)
        second = odd if owner >= groups // 2 else jnp.logical_not(odd)
        spare_totals = jnp.where(second, spare[where, :], close_spare_ref[where, :])
        extras[8 * owner : 8 * (owner + 1), :] = jnp.concatenate(
            [
                to_fields(columns[0:3, 0:LANES]),
                spare_totals[:, 0:LANES],
                spare_totals[:, LANES:],
                jnp.zeros((3, LANES), jnp.int32),
            ],
            axis=0,
        )
    me = lax.axis_index("hap")
    left = iota((size // 2, LANES), 1) < HALF_LANES
    for step, target in enumerate(targets):
        owner = partner(me, step, groups)
        first = (owner < groups // 2) == odd
        where = pl.ds(pl.multiple_of((owner & 1) * size, 8), size)
        counts = jnp.where(first, main[where, :], close_ref[where, :])
        for k in range(tiles):
            target[k * size : (k + 1) * size, :] = counts[:, k * LANES : (k + 1) * LANES]
        where = pl.ds(pl.multiple_of((owner & 1) * count, 8), size)
        counts = jnp.where(first, close_spare_ref[where, :], spare[where, :])
        start = tiles * size
        target[start : start + size, :] = counts[:, 0:LANES]
        rest = counts[:, LANES:]
        target[start + size : start + size + size // 2, :] = jnp.where(
            left, rest[0 : size // 2], pltpu.roll(rest[size // 2 :], HALF_LANES, 1)
        )
        target[start + size + size // 2 :, :] = extras[pl.ds(pl.multiple_of(owner * 8, 8), 8), :]


def near_kernel(groups, share, weighted_ref, far_ref, close_ref, totals_ref, *refs):
    own_parts, own_sum_ref = refs[:groups], refs[groups]
    targets, (near, tile, folded) = refs[groups + 1 : 2 * groups + 1], refs[2 * groups + 1 :]
    rows, snps = near.shape
    half = snps // 2
    odd = odd_block()

    def unpack(up_ref, down_ref):
        pieces = load_packed(up_ref[0 : rows // 2, :], down_ref[0 : rows // 2, :])
        for side in range(2):
            where = slice(side * (rows // 2), (side + 1) * (rows // 2))
            for number in range(3):
                near[where, number * LANES : (number + 1) * LANES] = pieces[side][number]

    @pl.when(odd)
    def _():
        unpack(far_ref, close_ref)

    @pl.when(jnp.logical_not(odd))
    def _():
        unpack(close_ref, far_ref)

    tile[...] = jnp.dot(weighted_ref[...], near[...], preferred_element_type=jnp.float32)
    row, col = iota((half, snps), 0), iota((half, snps), 1)
    moved = (col >= half) & (col - half < row)
    turned = pltpu.roll(tile[0:half, :], half, 1)
    folded[0:half, :] = to_fields(jnp.where(moved, turned, tile[half:snps, :]))
    if folded.shape[0] > half:
        folded[half:, :] = jnp.zeros((folded.shape[0] - half, snps), jnp.int32)
    square = (snps, snps)
    far = jnp.sum(
        jnp.where(iota(square, 0) == iota(square, 1), tile[0:snps, :], 0.0), axis=0, keepdims=True
    )
    extras = to_fields(
        jnp.concatenate(
            [totals_ref[0:2, :], tile[snps : snps + 1, :], far, jnp.zeros((4, snps))], axis=0
        )
    )
    send_shares(groups, folded, share, targets)
    for target in targets:
        target[share:, :] = extras
    own_sum_ref[...] = sum((part[...] for part in own_parts[1:]), own_parts[0][...])


def annots_kernel(annot_ref, far_ref, close_ref, own_ref, near_ref):
    snps = annot_ref.shape[1]
    own = annot_ref[...].astype(jnp.float32)
    own = jnp.concatenate([own, jnp.zeros((LANES - own.shape[0], snps), jnp.float32)], axis=0)
    own_ref[...] = own.T
    near_ref[...] = near_annots_by_snp(far_ref, close_ref)


def near_annots_by_snp(far_ref, close_ref):
    part, snps = far_ref.shape
    wide = 2 * part
    odd = odd_block()
    far, close = far_ref[...].astype(jnp.float32), close_ref[...].astype(jnp.float32)
    first, second = load_packed(jnp.where(odd, far, close), jnp.where(odd, close, far))
    near = jnp.concatenate(
        [
            jnp.concatenate([piece.astype(jnp.float32) for piece in first], axis=1),
            jnp.concatenate([piece.astype(jnp.float32) for piece in second], axis=1),
            jnp.zeros((LANES - wide, snps), jnp.float32),
        ],
        axis=0,
    )
    return near.T


def column_stats(totals, count):
    size = jnp.maximum(count, 1.0)
    frequency = totals / size
    variance = jnp.maximum(frequency * (1.0 - frequency), VARIANCE_FLOOR)
    inverse = 1.0 / jnp.sqrt(size * variance)
    low = ((0.0 - frequency) * inverse).astype(jnp.bfloat16).astype(jnp.float32)
    high = ((1.0 - frequency) * inverse).astype(jnp.bfloat16).astype(jnp.float32)
    step = high - low
    root = 1.0 / jnp.sqrt(size)
    return step, step * totals * root, (low * count + step * totals) * root


def correlation(row, col, count):
    return row[0] * col[0] * count - row[1] * col[1] + row[2] * col[2]


def split(values):
    high = values.astype(jnp.bfloat16)
    return high, (values - high.astype(jnp.float32)).astype(jnp.bfloat16)


def dot_split(values, right, axis):
    dims = (((axis,), (0,)), ((), ()))
    return sum(
        lax.dot_general(part, right, dims, preferred_element_type=jnp.float32)
        for part in split(values)
    )


def score_kernel(groups, share, reach_ref, *refs):
    own_sum_ref, near_parts = refs[0], refs[1 : groups + 1]
    annot_ref, near_annot_ref = refs[groups + 1 : groups + 3]
    targets = refs[groups + 3 : 2 * groups + 3]
    table, annots, near_annots, scores = refs[2 * groups + 3 :]
    snps = annot_ref.shape[0]
    half = snps // 2
    out_share = snps // groups
    me = lax.axis_index("hap")
    block = lax.axis_index("snp")
    last = reach_ref.shape[0] - 1
    reach_here = reach_ref[block]
    reach_up = reach_ref[jnp.minimum(block + 1, last)]
    reach_down = reach_ref[jnp.maximum(block - 1, 0)]

    own_counts = own_sum_ref[...]
    near_sums = sum((part[...] for part in near_parts[1:]), near_parts[0][...])
    extras = from_fields(near_sums[share:, :])
    near_counts = near_sums[0:share, :]

    own_stats, near_stats, lines = [], [], []
    for pop in range(2):
        count = extras[pop][1:2, :]
        own_stats.append(column_stats(extras[pop][0:1, :], count))
        near_stats.append(column_stats(extras[pop][2:3, :], count))
        lines += [*own_stats[pop], *near_stats[pop], extras[pop][0:1, :], extras[pop][3:4, :]]
    by_row = jnp.concatenate(lines, axis=0).T
    table[0:snps, 0:16] = by_row
    if table.shape[0] > snps:
        table[snps:, 0:16] = jnp.zeros((table.shape[0] - snps, 16), jnp.float32)
    annots[0:snps, :] = annot_ref[...]
    near_annots[0:snps, :] = near_annot_ref[...]
    if annots.shape[0] > snps:
        annots[snps:, :] = jnp.zeros((annots.shape[0] - snps, LANES), jnp.float32)

    low_rows = pl.multiple_of(me * share, 8)
    high_rows = pl.multiple_of(half + me * share, 8)

    def both(ref):
        return jnp.concatenate([ref[pl.ds(low_rows, share), :], ref[pl.ds(high_rows, share), :]], axis=0)

    here = both(table)
    own_count = jnp.concatenate([pltpu.roll(own_counts, half, 1), own_counts], axis=0)
    near_count = jnp.concatenate([pltpu.roll(near_counts, half, 1), near_counts], axis=0)
    shape = (2 * share, snps)
    local, col = iota(shape, 0), iota(shape, 1)
    low = local < share
    place = jnp.where(low, local, local - share) + me * share
    row = jnp.where(low, place, place + half)
    own_fields, near_fields = from_fields(own_count), from_fields(near_count)
    own_product, near_product = 1.0, 1.0
    for pop in range(2):
        row_stats = [here[:, 8 * pop + k : 8 * pop + k + 1] for k in range(3)]
        own_product *= correlation(row_stats, own_stats[pop], own_fields[pop])
        near_product *= correlation(row_stats, near_stats[pop], near_fields[pop])
    real = place < half
    own_inside = real & ((low & (col > row)) | (~low & (col >= half) & (col < row)))
    own_inside &= jnp.abs(col - row) <= reach_here
    own_kept = jnp.where(own_inside, own_product, 0.0)
    in_upper = col < half
    near_inside = real & ((low & (col < row)) | (~low & (in_upper | (col > row))))
    distance = jnp.where(in_upper, snps + col - row, snps + row - col)
    near_here = jnp.where(near_inside & (distance <= reach_here), near_product, 0.0)
    reach_there = jnp.where(in_upper, reach_up, reach_down)
    near_there = jnp.where(near_inside & (distance <= reach_there), near_product, 0.0)

    rows_here = both(annots)
    rows_there = pltpu.roll(rows_here, HALF_LANES, 1)
    scores[0:snps, :] = dot_split(
        jnp.concatenate([own_kept, near_there], axis=0),
        jnp.concatenate([rows_here, rows_there], axis=0).astype(jnp.bfloat16),
        0,
    )
    direct = dot_split(
        jnp.concatenate([own_kept, near_here], axis=1),
        jnp.concatenate([annot_ref[...], near_annot_ref[...]], axis=0).astype(jnp.bfloat16),
        1,
    )
    scores[pl.ds(low_rows, share), :] += direct[0:share, :]
    scores[pl.ds(high_rows, share), :] += direct[share:, :]

    out_rows = pl.ds(pl.multiple_of(me * out_share, 8), out_share)
    mine = table[out_rows, :]
    self_product, far_product = 1.0, 1.0
    for pop in range(2):
        k = 8 * pop
        own_row = [mine[:, k + s : k + s + 1] for s in range(3)]
        near_row = [mine[:, k + 3 + s : k + 4 + s] for s in range(3)]
        self_product *= correlation(own_row, own_row, mine[:, k + 6 : k + 7])
        far_product *= correlation(own_row, near_row, mine[:, k + 7 : k + 8])
    mine_annots = annots[out_rows, :]
    far_reach = jnp.where(me < groups // 2, reach_up, reach_down)
    scores[out_rows, :] += (
        mine_annots * self_product
        + near_annots[out_rows, :] * jnp.where(reach_here >= snps, far_product, 0.0)
        + pltpu.roll(mine_annots, HALF_LANES, 1) * jnp.where(far_reach >= snps, far_product, 0.0)
    )
    send_shares(groups, scores, out_share, targets)


def pack_halves(values):
    half = values.shape[0] // 2
    left = iota((half, LANES), 1) < HALF_LANES
    return jnp.where(left, values[0:half], pltpu.roll(values[half:], HALF_LANES, 1))


def unpack_halves(packed):
    return jnp.concatenate([packed, pltpu.roll(packed, HALF_LANES, 1)], axis=0)


def dot_rounded(values, right, axis):
    dims = (((axis,), (0,)), ((), ()))
    return lax.dot_general(
        values.astype(jnp.bfloat16), right, dims, preferred_element_type=jnp.float32
    )


def owner_places(groups, size):
    me = lax.axis_index("hap")

    def mine(blocks, slot):
        value = blocks[0][slot]
        for group in range(1, groups):
            value = jnp.where(me == group, blocks[group][slot], value)
        return value * size

    left = [mine(LEFT_BLOCKS, slot) for slot in range(groups)]
    right = [mine(RIGHT_BLOCKS, slot) for slot in range(groups)]
    return left + left[0:1], right + [(2 * me + 1) * size]


def spare_places(groups, size):
    me = lax.axis_index("hap")

    def mine(blocks, slot):
        value = blocks[0][slot]
        for group in range(1, groups):
            value = jnp.where(me == group, blocks[group][slot], value)
        return value * size

    return [[mine(blocks, slot) for slot in range(groups)] for blocks in (SPARE_OWN, SPARE_NEAR)]


def rows_at(ref, places, size):
    return jnp.concatenate([ref[pl.ds(pl.multiple_of(place, 8), size), :] for place in places], axis=0)


def own_score_kernel(
    groups, share, reach_ref, *refs
):
    own_parts, refs = refs[:groups], refs[groups:]
    annot_ref, far_ref, close_ref, scores, mine_ref, rows_ref, columns_ref, *refs = refs
    spare_rows_ref, spare_columns_ref, near_annot_ref, *targets, table = refs
    near_annot_ref[...] = near_annots_by_snp(far_ref, close_ref)
    snps = annot_ref.shape[0]
    half = snps // 2
    wide = snps // groups
    tiles = snps // LANES
    me = lax.axis_index("hap")
    reach_here = reach_ref[lax.axis_index("snp")]
    own_sums = sum((part[...] for part in own_parts[1:]), own_parts[0][...])
    own_counts = from_tiles(own_sums[0 : tiles * share, :], share)
    extras = from_fields(own_sums[tiles * share :, :])

    own_stats, lines = [], []
    for pop in range(2):
        count = jnp.concatenate([extras[pop][tiles : tiles + 1, :]] * tiles, axis=1)
        totals = jnp.concatenate([extras[pop][k : k + 1, :] for k in range(tiles)], axis=1)
        own_stats.append(column_stats(totals, count))
        lines += [*own_stats[pop], totals]
    table[:, 0:8] = jnp.concatenate(lines, axis=0).T

    low_rows = pl.multiple_of(me * share, 8)
    high_rows = pl.multiple_of(half + me * share, 8)

    def both(ref):
        return jnp.concatenate([ref[pl.ds(low_rows, share), :], ref[pl.ds(high_rows, share), :]], axis=0)

    here = both(table)
    own_fields = from_fields(
        jnp.concatenate([pltpu.roll(own_counts, half, 1), own_counts], axis=0)
    )
    shape = (2 * share, snps)
    local, col = iota(shape, 0), iota(shape, 1)
    low = local < share
    row = jnp.where(low, local, local + half - share) + me * share
    product = 1.0
    for pop in range(2):
        row_stats = [here[:, 4 * pop + k : 4 * pop + k + 1] for k in range(3)]
        product *= correlation(row_stats, own_stats[pop], own_fields[pop])
    inside = (low & (col > row)) | (~low & (col >= half) & (col < row))
    own_kept = jnp.where(inside & (jnp.abs(col - row) <= reach_here), product, 0.0)
    rows_here = both(annot_ref).astype(jnp.bfloat16)
    scores[...] = dot_rounded(own_kept, rows_here, 0)
    direct = dot_rounded(own_kept, annot_ref[...].astype(jnp.bfloat16), 1)
    scores[pl.ds(low_rows, share), :] += direct[0:share, :]
    scores[pl.ds(high_rows, share), :] += direct[share:, :]

    slice_rows = pl.ds(pl.multiple_of(me * wide, 8), wide)
    mine = table[slice_rows, :]
    mine_ref[...] = mine
    product = 1.0
    for pop in range(2):
        own_row = [mine[:, 4 * pop + k : 4 * pop + k + 1] for k in range(4)]
        product *= correlation(own_row, own_row, own_row[3])
    scores[slice_rows, :] += annot_ref[slice_rows, :] * product
    for step, target in enumerate(targets, 2):
        group = partner(me, step, groups)
        rows = scores[pl.ds(pl.multiple_of(group * wide, 8), wide), :]
        target[...] = pack_halves(rows).astype(target.dtype)

    size = wide // 2
    left_places, right_places = owner_places(groups, size)
    left_table, right_table = rows_at(table, left_places, size), rows_at(table, right_places, size)
    is_left = iota(rows_ref.shape[1:], 1) < size
    for pop in range(2):
        for k in range(3):
            column = slice(4 * pop + k, 4 * pop + k + 1)
            rows_ref[3 * pop + k] = jnp.where(is_left, left_table[:, column], right_table[:, column])
    theirs = near_annot_ref[slice_rows, :]
    columns = [theirs[0:size], pltpu.roll(theirs[size:], HALF_LANES, 1), jnp.zeros((LANES - wide, LANES))]
    columns_ref[...] = jnp.concatenate(columns, axis=0).astype(jnp.bfloat16)

    own_places, near_places = spare_places(groups, size)
    shape = spare_rows_ref.shape[1:]
    lane = iota(shape, 1)
    tables = [table[pl.ds(pl.multiple_of(place, 8), size), :] for place in own_places]
    for pop in range(2):
        for k in range(3):
            column = slice(4 * pop + k, 4 * pop + k + 1)
            spare_rows_ref[3 * pop + k] = by_slot(
                [jnp.broadcast_to(values[:, column], shape) for values in tables], lane, size
            )
    columns = [rows_at(near_annot_ref, near_places, size)]
    columns.append(jnp.zeros((shape[1] - groups * size, LANES), jnp.float32))
    spare_columns_ref[...] = jnp.concatenate(columns, axis=0).astype(jnp.bfloat16)


def near_score_kernel(groups, share, reach_ref, *refs):
    near_parts, refs = refs[:groups], refs[groups:]
    own_ref, mine_ref, rows_ref, columns_ref, spare_rows_ref, spare_columns_ref = refs[:6]
    near_annot_ref, annot_ref, masks_ref, spare_mask_ref, own_rows_ref = refs[6:11]
    out_ref, send_ref, near_out_ref, flipped, scores, other = refs[11:]
    snps = annot_ref.shape[0]
    wide = snps // groups
    size = wide // 2
    tiles = snps // LANES
    me = lax.axis_index("hap")
    block = lax.axis_index("snp")
    last = reach_ref.shape[0] - 1
    reach_here = reach_ref[block]
    reach_there = jnp.where(
        me < groups // 2, reach_ref[jnp.minimum(block + 1, last)], reach_ref[jnp.maximum(block - 1, 0)]
    )

    scores[...] = own_ref[...]
    near_sums = sum((part[...] for part in near_parts[1:]), near_parts[0][...])
    near_counts = from_tiles(near_sums[0 : tiles * share, :], share)
    start = tiles * share
    rest = near_sums[start + size : start + size + size // 2, :]
    rest = jnp.concatenate([rest, pltpu.roll(rest, HALF_LANES, 1)], axis=0)
    spare_fields = from_fields(jnp.concatenate([near_sums[start : start + size, :], rest], axis=1))
    extras = from_fields(near_sums[start + size + size // 2 :, :])
    near_stats, near_lines, spare_stats = [], [], []
    for pop in range(2):
        count = extras[pop][0:1, :]
        totals = jnp.concatenate([extras[pop][3:4, :], extras[pop][4:5, :]], axis=1)
        spare_stats.append(column_stats(totals, jnp.concatenate([count, count], axis=1)))
        near_stats.append(column_stats(extras[pop][1:2, :], extras[pop][0:1, :]))
        near_lines += [*near_stats[pop], extras[pop][2:3, :]]
    near_table = jnp.concatenate(near_lines, axis=0).T[0:wide, :]

    slots = [near_counts[:, 0:LANES]]
    for slot in range(1, groups):
        slots.append(pltpu.roll(near_counts, snps - slot * wide, 1)[:, 0:LANES])
    flipped[:, 0:size] = slots[0].T
    slots.append(pltpu.roll(flipped[0:size, :], size, 1))
    near_fields = from_fields(jnp.concatenate(slots, axis=0))
    product = 1.0
    for pop in range(2):
        row_stats = [rows_ref[3 * pop + k] for k in range(3)]
        product *= correlation(row_stats, near_stats[pop], near_fields[pop])
    near_here = jnp.where(masks_ref[0] > 0.0, product, 0.0)
    near_there = jnp.where(masks_ref[1] > 0.0, product, 0.0)
    slice_rows = pl.ds(pl.multiple_of(me * wide, 8), wide)
    direct = dot_rounded(near_here, columns_ref[...], 1)
    turned = pltpu.roll(direct, HALF_LANES, 1)
    left_places, right_places = owner_places(groups, size)
    other[...] = jnp.zeros_like(other)
    for ref, values, places in ((scores, direct, left_places[:-1]), (other, turned, right_places)):
        for slot, place in enumerate(places):
            ref[pl.ds(pl.multiple_of(place, 8), size), :] += values[slot * size : (slot + 1) * size, :]
    product = 1.0
    for pop in range(2):
        row_stats = [spare_rows_ref[3 * pop + k] for k in range(3)]
        product *= correlation(row_stats, spare_stats[pop], spare_fields[pop])
    spare_here = jnp.where(spare_mask_ref[...] > 0.0, product, 0.0)
    lane = iota(spare_here.shape, 1)
    spare_here = [
        jnp.where((lane >= slot * size) & (lane < (slot + 1) * size), spare_here, 0.0)
        for slot in range(groups)
    ]
    direct = dot_rounded(jnp.concatenate(spare_here, axis=0), spare_columns_ref[...], 1)
    for slot, place in enumerate(spare_places(groups, size)[0]):
        scores[pl.ds(pl.multiple_of(place, 8), size), :] += direct[slot * size : (slot + 1) * size, :]
    near_scores = dot_rounded(near_there, own_rows_ref[...], 0)
    near_scores = jnp.where(
        iota((size, LANES), 1) < HALF_LANES, near_scores[0:size], near_scores[size:wide]
    )

    mine_table = mine_ref[...]
    far_product = 1.0
    for pop in range(2):
        own_row = [mine_table[:, 4 * pop + k : 4 * pop + k + 1] for k in range(3)]
        near_row = [near_table[:, 4 * pop + k : 4 * pop + k + 1] for k in range(4)]
        far_product *= correlation(own_row, near_row, near_row[3])
    scores[slice_rows, :] += near_annot_ref[slice_rows, :] * jnp.where(reach_here >= snps, far_product, 0.0)
    far_scores = annot_ref[slice_rows, :] * jnp.where(reach_there >= snps, far_product, 0.0)
    near_out_ref[...] = (near_scores + pack_halves(far_scores)).astype(near_out_ref.dtype)

    def packed(step):
        group = partner(me, step, groups)
        rows = pl.ds(pl.multiple_of(group * wide, 8), wide)
        return pack_halves(scores[rows, :] + other[rows, :])

    out_ref[...] = packed(0)
    send_ref[...] = packed(1).astype(send_ref.dtype)


def column_finish_kernel(*refs):
    *parts, out_ref = refs
    packed = sum(part[...].astype(jnp.float32) for part in parts)
    out_ref[...] = unpack_halves(packed).T[0 : out_ref.shape[0], :]


def sum_kernel(*refs):
    *parts, own_ref, there_ref = refs
    total = sum((part[...].astype(jnp.float32) for part in parts[1:]), parts[0][...])
    own_ref[...] = total
    half = there_ref.shape[0]
    left = iota((half, LANES), 1) < HALF_LANES
    second = total[half:]
    if second.shape[0] < half:
        second = jnp.concatenate([second, jnp.zeros((half - second.shape[0], LANES))], axis=0)
    there_ref[...] = jnp.where(left, pltpu.roll(total[0:half], HALF_LANES, 1), second)


def finish_kernel(own_ref, there_ref, out_ref):
    annots, rows = out_ref.shape
    there = there_ref[...]
    there = jnp.concatenate([there, pltpu.roll(there, HALF_LANES, 1)], axis=0)
    out_ref[...] = (own_ref[...] + there[0:rows]).T[0:annots, :]


def around(value, groups, step):
    return lax.ppermute(
        value, "hap", [(source, partner(source, step, groups)) for source in range(groups)]
    )


def swapped(value, first):
    pairs = []
    for block in range(first, lax.axis_size("snp") - 1, 2):
        pairs += [(block, block + 1), (block + 1, block)]
    return lax.ppermute(value, "snp", pairs)


def per_device(haplotypes, labels, annotations, reach):
    rows, snps = haplotypes.shape
    half = snps // 2
    groups = lax.axis_size("hap")
    blocks = lax.axis_size("snp")
    share = round_up(-(-half // groups), 16)
    folded_rows = share * groups
    out_share = snps // groups
    padded = half + folded_rows
    annot_part = 32
    bf16, f32, i32 = jnp.bfloat16, jnp.float32, jnp.int32
    shape = jax.ShapeDtypeStruct

    packed = shape((rows // 2 + annot_part, snps), bf16)
    haplotypes = pltpu.with_memory_space_constraint(haplotypes, pltpu.HBM)
    annots_in = pltpu.with_memory_space_constraint(annotations, pltpu.HBM)
    alleles, far, close = call(
        prepare_kernel,
        [shape((rows, snps), bf16), packed, packed],
        [HBM, HBM],
        [
            pltpu.VMEM((rows, snps), i32),
            pltpu.VMEM(annotations.shape, i32),
            pltpu.SemaphoreType.DMA((2 * CHUNKS + 1,)),
        ],
        moved=rows * snps * 8,
    )(haplotypes, annots_in)
    from_far = swapped(far, 1)
    from_close = swapped(close, 0)

    by_column = groups == len(LEFT_BLOCKS)
    by_snp = shape((snps, LANES), f32)
    compact = shape((share * (snps // LANES) + 8, LANES), i32)
    own_share_counts = compact if by_column else shape((share, snps), i32)
    near_share_counts = shape((compact.shape[0] + share + share // 2, LANES), i32)
    tile = pltpu.VMEM((snps + 16, snps), f32)
    folded = pltpu.VMEM((folded_rows, snps), i32)
    weighted, totals, *own_parts = call(
        functools.partial(own_kernel, groups, share),
        [shape((snps + 16, rows), bf16), shape((8, snps), f32)] + [own_share_counts] * groups,
        [VMEM, VMEM],
        [tile, folded],
        flops=2 * rows * snps * snps,
        moved=rows * snps * 4,
    )(alleles, labels.reshape(1, rows))
    order = (2, 3, 1) if by_column else range(groups - 1, 0, -1)
    own_parts = [own_parts[0]] + [around(own_parts[k], groups, k) for k in order]

    near_shapes = [own_share_counts] + [near_share_counts if by_column else shape((share + 8, snps), i32)] * groups
    if by_column:
        work = dict(flops=4 * rows * snps * LANES, moved=rows * snps * 4)
        flipped = pltpu.VMEM((snps, LANES), f32)
        pair_rows = (groups + 1) * (out_share // 2)
        side_shapes = [((2 * share, snps), i32), ((2 * (share + 8), 2 * LANES), i32), ((8, snps), f32)]
        *close_counts, own_annots, masks, spare_mask, own_rows = call(
            functools.partial(close_kernel, groups),
            [shape(*args) for args in side_shapes]
            + [
                by_snp,
                shape((2, pair_rows, LANES), f32),
                shape((share, 2 * LANES), f32),
                shape((pair_rows, LANES), bf16),
            ],
            [SMEM] + [VMEM] * 3,
            [tile, flipped],
            **work,
        )(reach, weighted, from_close, annotations)
        near_parts = call(
            functools.partial(far_kernel, groups, share),
            near_shapes[1:],
            [VMEM] * 6,
            [pltpu.VMEM(*args) for args in side_shapes]
            + [tile, flipped, pltpu.VMEM((8 * groups, LANES), i32)],
            **work,
        )(weighted, from_far, *close_counts, totals)
    else:
        own_sum, *near_parts = call(
            functools.partial(near_kernel, groups, share),
            near_shapes,
            [VMEM] * (4 + groups),
            [pltpu.VMEM((rows, snps), bf16), tile, folded],
            flops=2 * rows * snps * snps,
            moved=rows * snps * 4,
        )(weighted, from_far, from_close, totals, *own_parts)
    order = range(groups - 1, 0, -1)
    near_parts = [near_parts[0]] + [around(near_parts[k], groups, k) for k in order]

    if not by_column:
        own_annots, near_annots = call(annots_kernel, [by_snp, by_snp], [VMEM] * 3, moved=1 << 20)(
            annotations, from_far[rows // 2 :], from_close[rows // 2 :]
        )
    pairs = []
    for block in range(blocks):
        for group in range(groups):
            target = block + 1 if group < groups // 2 else block - 1
            if 0 <= target < blocks:
                pairs.append((block * groups + group, target * groups + group))

    def to_neighbour(value):
        return lax.ppermute(value, ("snp", "hap"), pairs)

    result = shape((annotations.shape[0], out_share), f32)
    half_share = round_up(-(-out_share // 2), 8)
    own_share = shape((out_share, LANES), f32)
    packed_share = shape((half_share, LANES), f32)
    if by_column:
        sent = shape((half_share, LANES), bf16)
        *prepared, second, third = call(
            functools.partial(own_score_kernel, groups, share),
            [
                by_snp,
                shape((out_share, LANES), f32),
                shape((6, pair_rows, LANES), f32),
                shape((LANES, LANES), bf16),
                shape((6, share, 2 * LANES), f32),
                shape((2 * LANES, LANES), bf16),
                by_snp,
                sent,
                sent,
            ],
            [SMEM] + [VMEM] * (groups + 3),
            [pltpu.VMEM((snps, LANES), f32)],
            flops=1 << 33,
            moved=1 << 20,
        )(reach, *own_parts, own_annots, from_far[rows // 2 :], from_close[rows // 2 :])
        parts = [around(third, groups, 3), around(second, groups, 2)]
        own_scores, send, there = call(
            functools.partial(near_score_kernel, groups, share),
            [packed_share, sent, sent],
            [SMEM] + [VMEM] * (groups + 11),
            [pltpu.VMEM((LANES, LANES), i32)] + [pltpu.VMEM((snps, LANES), f32)] * 2,
            flops=1 << 26,
            moved=1 << 21,
        )(reach, *near_parts, *prepared, own_annots, masks, spare_mask, own_rows)
        parts += [around(send, groups, 1), to_neighbour(there)]
        return call(column_finish_kernel, result, [VMEM] * 5)(own_scores, *parts)

    tall = pltpu.VMEM((padded, LANES), f32)
    scores = call(
        functools.partial(score_kernel, groups, share),
        [own_share] + [shape((out_share, LANES), bf16)] * (groups - 1),
        [SMEM] + [VMEM] * (groups + 3),
        [tall, tall, tall, tall],
        flops=1 << 26,
        moved=1 << 21,
    )(reach, own_sum, *near_parts, own_annots, near_annots)
    scores = [scores[0]] + [around(scores[k], groups, k) for k in range(groups - 1, 0, -1)]
    own_scores, near_scores = call(sum_kernel, [own_share, packed_share], [VMEM] * groups)(*scores)
    return call(finish_kernel, result, [VMEM] * 2)(own_scores, to_neighbour(near_scores))


def solution(mesh):
    in_specs = (
        P("hap", ("parts", "snp")),
        P(("parts", "hap")),
        P(None, ("parts", "snp")),
        P("parts"),
    )
    out_specs = P(None, ("parts", "snp", "hap"))
    return jax.shard_map(
        per_device, mesh=mesh, in_specs=in_specs, out_specs=out_specs, check_vma=False
    )
```

```python
import functools

import jax
import jax.numpy as jnp
from jax import lax
from jax.experimental import pallas as pl
from jax.experimental.pallas import tpu as pltpu
from jax.sharding import PartitionSpec as P

VARIANCE_FLOOR = 0.01
BASE_BITS = 12
BASE = 1 << BASE_BITS
FIELD_BITS = 16
LANES = 128
HALF_LANES = LANES // 2
CHUNKS = (8, 5, 3)
VMEM = pl.BlockSpec(memory_space=pltpu.VMEM)
SMEM = pl.BlockSpec(memory_space=pltpu.SMEM)
HBM = pl.BlockSpec(memory_space=pltpu.HBM)
VMEM_LIMIT = 24 * 1024 * 1024


def iota(shape, axis):
    return lax.broadcasted_iota(jnp.int32, shape, axis)


def round_up(value, step):
    return -(-value // step) * step


def to_fields(values):
    whole = values.astype(jnp.int32)
    return whole + (whole >> BASE_BITS) * ((1 << FIELD_BITS) - BASE)


def from_fields(packed):
    first = packed & ((1 << FIELD_BITS) - 1)
    second = lax.shift_right_logical(packed, FIELD_BITS)
    return first.astype(jnp.float32), second.astype(jnp.float32)


def call(kernel, out_shape, in_specs, scratch_shapes=(), flops=0, moved=0):
    several = isinstance(out_shape, (list, tuple))
    return pl.pallas_call(
        kernel,
        out_shape=out_shape,
        in_specs=in_specs,
        out_specs=[VMEM] * len(out_shape) if several else VMEM,
        scratch_shapes=list(scratch_shapes),
        compiler_params=pltpu.CompilerParams(vmem_limit_bytes=VMEM_LIMIT),
        cost_estimate=pl.CostEstimate(flops=flops, bytes_accessed=moved, transcendentals=0),
    )


def odd_block():
    return lax.rem(lax.axis_index("snp"), 2) == 1


def store_packed(up_ref, down_ref, where, first, second):
    left = iota((first.shape[0], LANES), 1) < HALF_LANES
    middle = first[:, LANES : 2 * LANES]
    turned = pltpu.roll(second[:, LANES : 2 * LANES], HALF_LANES, 1)
    for ref, side, mixed in (
        (up_ref, slice(0, LANES), jnp.where(left, middle, turned)),
        (down_ref, slice(2 * LANES, 3 * LANES), jnp.where(left, turned, middle)),
    ):
        ref[where, 0:LANES] = first[:, side].astype(jnp.bfloat16)
        ref[where, LANES : 2 * LANES] = mixed.astype(jnp.bfloat16)
        ref[where, 2 * LANES : 3 * LANES] = second[:, side].astype(jnp.bfloat16)


def load_packed(up, down):
    left = iota((up.shape[0], LANES), 1) < HALF_LANES
    up_mixed, down_mixed = up[:, LANES : 2 * LANES], down[:, LANES : 2 * LANES]
    first = jnp.where(left, up_mixed, down_mixed)
    second = jnp.where(left, down_mixed, up_mixed)
    second = pltpu.roll(second.astype(jnp.float32), HALF_LANES, 1).astype(second.dtype)
    return (
        (up[:, :LANES], first, down[:, :LANES]),
        (up[:, 2 * LANES :], second, down[:, 2 * LANES :]),
    )


def prepare_kernel(hap_ref, annot_ref, alleles_ref, far_ref, close_ref, held, held_annots, sems):
    rows = hap_ref.shape[0]
    annot_rows = annot_ref.shape[0]
    sizes = [chunk * (rows // 32) for chunk in CHUNKS]
    places = [sum(sizes[:number]) for number in range(len(sizes))]
    pieces = [
        (side * (rows // 2) + place, size) for place, size in zip(places, sizes) for side in range(2)
    ]
    copies = [
        pltpu.make_async_copy(
            hap_ref.at[pl.ds(start, size)], held.at[pl.ds(start, size)], sems.at[number]
        )
        for number, (start, size) in enumerate(pieces)
    ]
    copies.append(pltpu.make_async_copy(annot_ref, held_annots, sems.at[len(pieces)]))
    for copy in copies:
        copy.start()
    part = far_ref.shape[0] - rows // 2
    odd = odd_block()

    def store(where, first, second):
        @pl.when(odd)
        def _():
            store_packed(close_ref, far_ref, where, first, second)

        @pl.when(jnp.logical_not(odd))
        def _():
            store_packed(far_ref, close_ref, where, first, second)

    for chunk, (place, size) in enumerate(zip(places, sizes)):
        pair = []
        for number in (2 * chunk, 2 * chunk + 1):
            copies[number].wait()
            where = slice(pieces[number][0], pieces[number][0] + size)
            values = held[where, :].astype(jnp.float32)
            alleles_ref[where, :] = values.astype(jnp.bfloat16)
            pair.append(values)
        store(slice(place, place + size), *pair)
    copies[-1].wait()
    annots = jnp.concatenate(
        [
            held_annots[...].astype(jnp.float32),
            jnp.zeros((2 * part - annot_rows, annot_ref.shape[1]), jnp.float32),
        ],
        axis=0,
    )
    store(slice(rows // 2, rows // 2 + part), annots[:part], annots[part:])


def partner(group, step, groups):
    if groups & (groups - 1) == 0:
        return group ^ step
    return (group + step) % groups


def send_shares(groups, source, share, targets):
    me = lax.axis_index("hap")
    for step, target in enumerate(targets):
        group = partner(me, step, groups)
        rows = source[pl.ds(pl.multiple_of(group * share, 8), share), :]
        target[0:share, :] = rows.astype(target.dtype)


def send_tiles(groups, source, share, targets):
    me = lax.axis_index("hap")
    for step, target in enumerate(targets):
        owner = partner(me, step, groups)
        counts = source[pl.ds(pl.multiple_of(owner * share, 8), share), :]
        for k in range(source.shape[1] // LANES):
            target[k * share : (k + 1) * share, :] = counts[:, k * LANES : (k + 1) * LANES]


def from_tiles(counts, share):
    tiles = counts.shape[0] // share
    return jnp.concatenate([counts[k * share : (k + 1) * share, :] for k in range(tiles)], axis=1)


def own_kernel(groups, share, alleles_ref, label_ref, *refs):
    weighted_ref, totals_ref, *targets = refs[: 2 + groups]
    tile, folded = refs[2 + groups :]
    rows, snps = alleles_ref.shape
    half = snps // 2
    weight = jnp.where(label_ref[...] > 0, float(BASE), 1.0)
    weighted_ref[0:snps, :] = alleles_ref[...].T * weight.astype(jnp.bfloat16)
    extra = weighted_ref.shape[0] - snps
    weighted_ref[snps:, :] = jnp.broadcast_to(weight, (extra, rows)).astype(jnp.bfloat16)
    tile[...] = jnp.dot(weighted_ref[...], alleles_ref[...], preferred_element_type=jnp.float32)
    count = jnp.sum(weight, axis=1, keepdims=True)
    totals_ref[...] = jnp.concatenate(
        [tile[snps : snps + 1, :], jnp.broadcast_to(count, (1, snps)), jnp.zeros((6, snps))], axis=0
    )
    row, col = iota((half, snps), 0), iota((half, snps), 1)
    moved = (col < half) | (col - half > row)
    turned = pltpu.roll(tile[0:half, :], half, 1)
    folded[0:half, :] = to_fields(jnp.where(moved, turned, tile[half:snps, :]))
    if folded.shape[0] > half:
        folded[half:, :] = jnp.zeros((folded.shape[0] - half, snps), jnp.int32)
    if groups != len(LEFT_BLOCKS):
        send_shares(groups, folded, share, targets)
        return
    tiles = snps // LANES
    shared = [totals_ref[0:1, k * LANES : (k + 1) * LANES] for k in range(tiles)]
    shared += [totals_ref[1:2, 0:LANES], jnp.zeros((7 - tiles, LANES))]
    extras = to_fields(jnp.concatenate(shared, axis=0))
    send_tiles(groups, folded, share, targets)
    for target in targets:
        target[tiles * share :, :] = extras


LEFT_BLOCKS = ((0, 1, 2, 3), (2, 3, 6, 7), (4, 0, 1, 2), (6, 0, 4, 5))
RIGHT_BLOCKS = ((2, 3, 6, 7), (4, 5, 6, 7), (0, 1, 2, 4), (0, 4, 5, 6))


SPARE_OWN = ((0, 0, 0, 0), (1, 1, 2, 2), (4, 5, 6, 7), (6, 6, 7, 7))
SPARE_NEAR = ((4, 5, 6, 7), (4, 5, 4, 5), (3, 3, 3, 3), (1, 2, 1, 2))


def fold_spare(tile, spare, first):
    owners = len(SPARE_OWN)
    snps = tile.shape[1]
    size = snps // (2 * owners)
    count = spare.shape[0] // 2
    totals = tile[snps : snps + count - size, :]
    lane = iota((count, snps), 1)
    for number, owner in enumerate(range(first, first + 2)):
        mixed = None
        for slot in range(owners):
            own, near = SPARE_OWN[owner][slot], SPARE_NEAR[owner][slot]
            before = (SPARE_OWN[owner][slot - 1], SPARE_NEAR[owner][slot - 1] + 1) if slot else None
            if before == (own, near):
                continue
            values = jnp.concatenate([tile[own * size : (own + 1) * size, :], totals], axis=0)
            shift = (slot - near) * size % snps
            values = pltpu.roll(values, shift, 1) if shift else values
            mixed = values if mixed is None else jnp.where(lane >= slot * size, values, mixed)
        spare[number * count : (number + 1) * count, :] = to_fields(mixed[:, 0 : spare.shape[1]])


def fold_by_column(tile, flipped, folded, first):
    groups = len(LEFT_BLOCKS)
    owners = range(first, first + groups // 2)
    snps = folded.shape[1]
    wide = snps // groups
    size = wide // 2
    shape = (size, snps)
    row, lane = iota(shape, 0), iota(shape, 1)

    def block(number):
        return tile[number * size : (number + 1) * size, :]

    diagonal, within = block(2 * first), lane - 2 * first * size
    for number in range(2 * first + 1, 2 * first + groups):
        diagonal = jnp.where(lane >= number * size, block(number), diagonal)
        within = jnp.where(lane >= number * size, lane - number * size, within)
    apart = jnp.sum(jnp.where(row == within, diagonal, 0.0), axis=0, keepdims=True)
    flipped[:, 0:size] = diagonal.T
    corner = diagonal
    for owner in owners:
        start = (2 * owner + 1) * size
        turned = jnp.concatenate(
            [flipped[start : start + size, :], jnp.zeros((size, snps - LANES), jnp.float32)], axis=1
        )
        if owner:
            turned = pltpu.roll(turned, owner * wide, 1)
        inside = lane - owner * wide
        other = (row <= inside) if first == 0 else (row >= inside)
        corner = jnp.where((inside >= 0) & (inside < size) & other, turned, corner)
    rolled = []
    for shift in range(groups):
        mixed = None
        for owner in owners:
            slot = (owner + shift) % groups
            left = block(LEFT_BLOCKS[owner][slot]) if slot else corner
            start = owner * wide
            mixed = left if mixed is None else jnp.where(lane >= start, left, mixed)
            mixed = jnp.where(lane >= start + size, block(RIGHT_BLOCKS[owner][slot]), mixed)
        rolled.append(pltpu.roll(mixed, shift * wide, 1) if shift else mixed)
    for number, owner in enumerate(owners):
        mixed = rolled[(0 - owner) % groups]
        for slot in range(1, groups):
            mixed = jnp.where(lane >= slot * wide, rolled[(slot - owner) % groups], mixed)
        folded[number * size : (number + 1) * size, :] = to_fields(mixed)
    return apart


def above(far):
    return odd_block() == far


def side_dot(weighted_ref, side_ref):
    rows = weighted_ref.shape[1]
    half = rows // 2

    def dot(which, columns):
        return jnp.dot(
            weighted_ref[:, which], side_ref[0:half, columns], preferred_element_type=jnp.float32
        )

    first = dot(slice(0, half), slice(0, 2 * LANES))
    second = dot(slice(half, rows), slice(LANES, 3 * LANES))
    whole = first[:, 0:LANES] + second[:, LANES:]
    return whole, first[:, LANES:] + pltpu.roll(second[:, 0:LANES], HALF_LANES, 1)


def fold_side(far, weighted_ref, side_ref, main, spare, lines, tile, flipped):
    snps = tile.shape[1]
    whole, shared = side_dot(weighted_ref, side_ref)
    tile[:, LANES : 2 * LANES] = shared

    def fold(first, start):
        tile[:, start : start + LANES] = whole
        apart = fold_by_column(tile, flipped, main, first)
        fold_spare(tile, spare, 2 - first)
        lines[0:1, :] = tile[snps : snps + 1, :]
        lines[1:2, :] = apart

    @pl.when(above(far))
    def _():
        fold(0, 0)

    @pl.when(jnp.logical_not(above(far)))
    def _():
        fold(2, 2 * LANES)


def close_kernel(groups, reach_ref, weighted_ref, side_ref, annot_ref, *refs):
    main_ref, spare_ref, lines_ref, annots, masks_ref, spare_mask_ref, own_rows_ref, tile, flipped = refs
    fold_side(False, weighted_ref, side_ref, main_ref, spare_ref, lines_ref, tile, flipped)
    snps = annot_ref.shape[1]
    half, wide = snps // 2, snps // groups
    size = wide // 2
    own = annot_ref[...].astype(jnp.float32)
    own = jnp.concatenate([own, jnp.zeros((LANES - own.shape[0], snps), jnp.float32)], axis=0)
    annots[...] = own.T

    me = lax.axis_index("hap")
    block = lax.axis_index("snp")
    last = reach_ref.shape[0] - 1
    upper = me < groups // 2
    reach_here = reach_ref[block]
    reach_there = jnp.where(
        upper, reach_ref[jnp.minimum(block + 1, last)], reach_ref[jnp.maximum(block - 1, 0)]
    )
    left_places, right_places = owner_places(groups, size)
    local, lane = iota((size, LANES), 0), iota((size, LANES), 1)
    own_row = jnp.concatenate(
        [local + jnp.where(lane < size, a, b) for a, b in zip(left_places, right_places)], axis=0
    )
    shape = own_row.shape
    lane = iota(shape, 1)
    apart = jnp.abs(own_row - (lane + me * wide))
    ahead = (own_row - (lane + me * wide)) * jnp.where(upper, 1, -1) > 0
    real = ahead & (lane < wide) & ((lane >= size) | (iota(shape, 0) < groups * size))
    inside = (own_row - half) * jnp.where(upper, 1, -1) < jnp.where(upper, 0, 1)
    masks_ref[0] = jnp.where(real & inside & (snps - apart <= reach_here), 1.0, 0.0)
    masks_ref[1] = jnp.where(real & (snps - apart <= reach_there), 1.0, 0.0)
    own_rows = rows_at(annots, left_places, size) + pltpu.roll(
        rows_at(annots, right_places, size), HALF_LANES, 1
    )
    own_rows_ref[...] = own_rows.astype(jnp.bfloat16)

    own_places, near_places = spare_places(groups, size)
    shape = spare_mask_ref.shape
    local, lane = iota(shape, 0), iota(shape, 1)
    own_row = by_slot([local + place for place in own_places], lane, size)
    near_col = by_slot(
        [lane + (place - slot * size) for slot, place in enumerate(near_places)], lane, size
    )
    close = snps - jnp.abs(own_row - near_col) <= reach_here
    spare_mask_ref[...] = jnp.where(close & (lane < groups * size), 1.0, 0.0)


def by_slot(values, lane, size):
    mixed = values[0]
    for slot in range(1, len(values)):
        mixed = jnp.where(lane >= slot * size, values[slot], mixed)
    return mixed


def far_kernel(groups, share, weighted_ref, side_ref, close_ref, close_spare_ref, close_lines_ref, totals_ref, *refs):
    targets, (main, spare, lines, tile, flipped, extras) = refs[:groups], refs[groups:]
    fold_side(True, weighted_ref, side_ref, main, spare, lines, tile, flipped)
    snps = tile.shape[1]
    half, size = snps // 2, share
    odd = odd_block()

    tiles = snps // LANES
    count = spare.shape[0] // 2
    from_far = (iota((8, snps), 1) < half) == odd
    by_column = jnp.concatenate(
        [totals_ref[1:2, :], jnp.where(from_far, lines[...], close_lines_ref[...])[0:2, :]], axis=0
    )
    by_column = jnp.concatenate([by_column, jnp.zeros((5, snps))], axis=0)
    for owner in range(groups):
        start = owner * (snps // groups)
        columns = pltpu.roll(by_column, snps - start, 1) if owner else by_column
        where = slice((owner & 1) * count + size, (owner & 1) * count + size + 1)
        second = odd if owner >= groups // 2 else jnp.logical_not(odd)
        spare_totals = jnp.where(second, spare[where, :], close_spare_ref[where, :])
        extras[8 * owner : 8 * (owner + 1), :] = jnp.concatenate(
            [
                to_fields(columns[0:3, 0:LANES]),
                spare_totals[:, 0:LANES],
                spare_totals[:, LANES:],
                jnp.zeros((3, LANES), jnp.int32),
            ],
            axis=0,
        )
    me = lax.axis_index("hap")
    left = iota((size // 2, LANES), 1) < HALF_LANES
    for step, target in enumerate(targets):
        owner = partner(me, step, groups)
        first = (owner < groups // 2) == odd
        where = pl.ds(pl.multiple_of((owner & 1) * size, 8), size)
        counts = jnp.where(first, main[where, :], close_ref[where, :])
        for k in range(tiles):
            target[k * size : (k + 1) * size, :] = counts[:, k * LANES : (k + 1) * LANES]
        where = pl.ds(pl.multiple_of((owner & 1) * count, 8), size)
        counts = jnp.where(first, close_spare_ref[where, :], spare[where, :])
        start = tiles * size
        target[start : start + size, :] = counts[:, 0:LANES]
        rest = counts[:, LANES:]
        target[start + size : start + size + size // 2, :] = jnp.where(
            left, rest[0 : size // 2], pltpu.roll(rest[size // 2 :], HALF_LANES, 1)
        )
        target[start + size + size // 2 :, :] = extras[pl.ds(pl.multiple_of(owner * 8, 8), 8), :]


def near_kernel(groups, share, weighted_ref, far_ref, close_ref, totals_ref, *refs):
    own_parts, own_sum_ref = refs[:groups], refs[groups]
    targets, (near, tile, folded) = refs[groups + 1 : 2 * groups + 1], refs[2 * groups + 1 :]
    rows, snps = near.shape
    half = snps // 2
    odd = odd_block()

    def unpack(up_ref, down_ref):
        pieces = load_packed(up_ref[0 : rows // 2, :], down_ref[0 : rows // 2, :])
        for side in range(2):
            where = slice(side * (rows // 2), (side + 1) * (rows // 2))
            for number in range(3):
                near[where, number * LANES : (number + 1) * LANES] = pieces[side][number]

    @pl.when(odd)
    def _():
        unpack(far_ref, close_ref)

    @pl.when(jnp.logical_not(odd))
    def _():
        unpack(close_ref, far_ref)

    tile[...] = jnp.dot(weighted_ref[...], near[...], preferred_element_type=jnp.float32)
    row, col = iota((half, snps), 0), iota((half, snps), 1)
    moved = (col >= half) & (col - half < row)
    turned = pltpu.roll(tile[0:half, :], half, 1)
    folded[0:half, :] = to_fields(jnp.where(moved, turned, tile[half:snps, :]))
    if folded.shape[0] > half:
        folded[half:, :] = jnp.zeros((folded.shape[0] - half, snps), jnp.int32)
    square = (snps, snps)
    far = jnp.sum(
        jnp.where(iota(square, 0) == iota(square, 1), tile[0:snps, :], 0.0), axis=0, keepdims=True
    )
    extras = to_fields(
        jnp.concatenate(
            [totals_ref[0:2, :], tile[snps : snps + 1, :], far, jnp.zeros((4, snps))], axis=0
        )
    )
    send_shares(groups, folded, share, targets)
    for target in targets:
        target[share:, :] = extras
    own_sum_ref[...] = sum((part[...] for part in own_parts[1:]), own_parts[0][...])


def annots_kernel(annot_ref, far_ref, close_ref, own_ref, near_ref):
    snps = annot_ref.shape[1]
    own = annot_ref[...].astype(jnp.float32)
    own = jnp.concatenate([own, jnp.zeros((LANES - own.shape[0], snps), jnp.float32)], axis=0)
    own_ref[...] = own.T
    near_ref[...] = near_annots_by_snp(far_ref, close_ref)


def near_annots_by_snp(far_ref, close_ref):
    part, snps = far_ref.shape
    wide = 2 * part
    odd = odd_block()
    far, close = far_ref[...].astype(jnp.float32), close_ref[...].astype(jnp.float32)
    first, second = load_packed(jnp.where(odd, far, close), jnp.where(odd, close, far))
    near = jnp.concatenate(
        [
            jnp.concatenate([piece.astype(jnp.float32) for piece in first], axis=1),
            jnp.concatenate([piece.astype(jnp.float32) for piece in second], axis=1),
            jnp.zeros((LANES - wide, snps), jnp.float32),
        ],
        axis=0,
    )
    return near.T


def column_stats(totals, count):
    size = jnp.maximum(count, 1.0)
    frequency = totals / size
    variance = jnp.maximum(frequency * (1.0 - frequency), VARIANCE_FLOOR)
    inverse = 1.0 / jnp.sqrt(size * variance)
    low = ((0.0 - frequency) * inverse).astype(jnp.bfloat16).astype(jnp.float32)
    high = ((1.0 - frequency) * inverse).astype(jnp.bfloat16).astype(jnp.float32)
    step = high - low
    root = 1.0 / jnp.sqrt(size)
    return step, step * totals * root, (low * count + step * totals) * root


def correlation(row, col, count):
    return row[0] * col[0] * count - row[1] * col[1] + row[2] * col[2]


def split(values):
    high = values.astype(jnp.bfloat16)
    return high, (values - high.astype(jnp.float32)).astype(jnp.bfloat16)


def dot_split(values, right, axis):
    dims = (((axis,), (0,)), ((), ()))
    return sum(
        lax.dot_general(part, right, dims, preferred_element_type=jnp.float32)
        for part in split(values)
    )


def score_kernel(groups, share, reach_ref, *refs):
    own_sum_ref, near_parts = refs[0], refs[1 : groups + 1]
    annot_ref, near_annot_ref = refs[groups + 1 : groups + 3]
    targets = refs[groups + 3 : 2 * groups + 3]
    table, annots, near_annots, scores = refs[2 * groups + 3 :]
    snps = annot_ref.shape[0]
    half = snps // 2
    out_share = snps // groups
    me = lax.axis_index("hap")
    block = lax.axis_index("snp")
    last = reach_ref.shape[0] - 1
    reach_here = reach_ref[block]
    reach_up = reach_ref[jnp.minimum(block + 1, last)]
    reach_down = reach_ref[jnp.maximum(block - 1, 0)]

    own_counts = own_sum_ref[...]
    near_sums = sum((part[...] for part in near_parts[1:]), near_parts[0][...])
    extras = from_fields(near_sums[share:, :])
    near_counts = near_sums[0:share, :]

    own_stats, near_stats, lines = [], [], []
    for pop in range(2):
        count = extras[pop][1:2, :]
        own_stats.append(column_stats(extras[pop][0:1, :], count))
        near_stats.append(column_stats(extras[pop][2:3, :], count))
        lines += [*own_stats[pop], *near_stats[pop], extras[pop][0:1, :], extras[pop][3:4, :]]
    by_row = jnp.concatenate(lines, axis=0).T
    table[0:snps, 0:16] = by_row
    if table.shape[0] > snps:
        table[snps:, 0:16] = jnp.zeros((table.shape[0] - snps, 16), jnp.float32)
    annots[0:snps, :] = annot_ref[...]
    near_annots[0:snps, :] = near_annot_ref[...]
    if annots.shape[0] > snps:
        annots[snps:, :] = jnp.zeros((annots.shape[0] - snps, LANES), jnp.float32)

    low_rows = pl.multiple_of(me * share, 8)
    high_rows = pl.multiple_of(half + me * share, 8)

    def both(ref):
        return jnp.concatenate([ref[pl.ds(low_rows, share), :], ref[pl.ds(high_rows, share), :]], axis=0)

    here = both(table)
    own_count = jnp.concatenate([pltpu.roll(own_counts, half, 1), own_counts], axis=0)
    near_count = jnp.concatenate([pltpu.roll(near_counts, half, 1), near_counts], axis=0)
    shape = (2 * share, snps)
    local, col = iota(shape, 0), iota(shape, 1)
    low = local < share
    place = jnp.where(low, local, local - share) + me * share
    row = jnp.where(low, place, place + half)
    own_fields, near_fields = from_fields(own_count), from_fields(near_count)
    own_product, near_product = 1.0, 1.0
    for pop in range(2):
        row_stats = [here[:, 8 * pop + k : 8 * pop + k + 1] for k in range(3)]
        own_product *= correlation(row_stats, own_stats[pop], own_fields[pop])
        near_product *= correlation(row_stats, near_stats[pop], near_fields[pop])
    real = place < half
    own_inside = real & ((low & (col > row)) | (~low & (col >= half) & (col < row)))
    own_inside &= jnp.abs(col - row) <= reach_here
    own_kept = jnp.where(own_inside, own_product, 0.0)
    in_upper = col < half
    near_inside = real & ((low & (col < row)) | (~low & (in_upper | (col > row))))
    distance = jnp.where(in_upper, snps + col - row, snps + row - col)
    near_here = jnp.where(near_inside & (distance <= reach_here), near_product, 0.0)
    reach_there = jnp.where(in_upper, reach_up, reach_down)
    near_there = jnp.where(near_inside & (distance <= reach_there), near_product, 0.0)

    rows_here = both(annots)
    rows_there = pltpu.roll(rows_here, HALF_LANES, 1)
    scores[0:snps, :] = dot_split(
        jnp.concatenate([own_kept, near_there], axis=0),
        jnp.concatenate([rows_here, rows_there], axis=0).astype(jnp.bfloat16),
        0,
    )
    direct = dot_split(
        jnp.concatenate([own_kept, near_here], axis=1),
        jnp.concatenate([annot_ref[...], near_annot_ref[...]], axis=0).astype(jnp.bfloat16),
        1,
    )
    scores[pl.ds(low_rows, share), :] += direct[0:share, :]
    scores[pl.ds(high_rows, share), :] += direct[share:, :]

    out_rows = pl.ds(pl.multiple_of(me * out_share, 8), out_share)
    mine = table[out_rows, :]
    self_product, far_product = 1.0, 1.0
    for pop in range(2):
        k = 8 * pop
        own_row = [mine[:, k + s : k + s + 1] for s in range(3)]
        near_row = [mine[:, k + 3 + s : k + 4 + s] for s in range(3)]
        self_product *= correlation(own_row, own_row, mine[:, k + 6 : k + 7])
        far_product *= correlation(own_row, near_row, mine[:, k + 7 : k + 8])
    mine_annots = annots[out_rows, :]
    far_reach = jnp.where(me < groups // 2, reach_up, reach_down)
    scores[out_rows, :] += (
        mine_annots * self_product
        + near_annots[out_rows, :] * jnp.where(reach_here >= snps, far_product, 0.0)
        + pltpu.roll(mine_annots, HALF_LANES, 1) * jnp.where(far_reach >= snps, far_product, 0.0)
    )
    send_shares(groups, scores, out_share, targets)


def pack_halves(values):
    half = values.shape[0] // 2
    left = iota((half, LANES), 1) < HALF_LANES
    return jnp.where(left, values[0:half], pltpu.roll(values[half:], HALF_LANES, 1))


def unpack_halves(packed):
    return jnp.concatenate([packed, pltpu.roll(packed, HALF_LANES, 1)], axis=0)


def dot_rounded(values, right, axis):
    dims = (((axis,), (0,)), ((), ()))
    return lax.dot_general(
        values.astype(jnp.bfloat16), right, dims, preferred_element_type=jnp.float32
    )


def owner_places(groups, size):
    me = lax.axis_index("hap")

    def mine(blocks, slot):
        value = blocks[0][slot]
        for group in range(1, groups):
            value = jnp.where(me == group, blocks[group][slot], value)
        return value * size

    left = [mine(LEFT_BLOCKS, slot) for slot in range(groups)]
    right = [mine(RIGHT_BLOCKS, slot) for slot in range(groups)]
    return left + left[0:1], right + [(2 * me + 1) * size]


def spare_places(groups, size):
    me = lax.axis_index("hap")

    def mine(blocks, slot):
        value = blocks[0][slot]
        for group in range(1, groups):
            value = jnp.where(me == group, blocks[group][slot], value)
        return value * size

    return [[mine(blocks, slot) for slot in range(groups)] for blocks in (SPARE_OWN, SPARE_NEAR)]


def rows_at(ref, places, size):
    return jnp.concatenate([ref[pl.ds(pl.multiple_of(place, 8), size), :] for place in places], axis=0)


def own_score_kernel(
    groups, share, reach_ref, *refs
):
    own_parts, refs = refs[:groups], refs[groups:]
    annot_ref, far_ref, close_ref, scores, mine_ref, rows_ref, columns_ref, *refs = refs
    spare_rows_ref, spare_columns_ref, near_annot_ref, *targets, table = refs
    near_annot_ref[...] = near_annots_by_snp(far_ref, close_ref)
    snps = annot_ref.shape[0]
    half = snps // 2
    wide = snps // groups
    tiles = snps // LANES
    me = lax.axis_index("hap")
    reach_here = reach_ref[lax.axis_index("snp")]
    own_sums = sum((part[...] for part in own_parts[1:]), own_parts[0][...])
    own_counts = from_tiles(own_sums[0 : tiles * share, :], share)
    extras = from_fields(own_sums[tiles * share :, :])

    own_stats, lines = [], []
    for pop in range(2):
        count = jnp.concatenate([extras[pop][tiles : tiles + 1, :]] * tiles, axis=1)
        totals = jnp.concatenate([extras[pop][k : k + 1, :] for k in range(tiles)], axis=1)
        own_stats.append(column_stats(totals, count))
        lines += [*own_stats[pop], totals]
    table[:, 0:8] = jnp.concatenate(lines, axis=0).T

    low_rows = pl.multiple_of(me * share, 8)
    high_rows = pl.multiple_of(half + me * share, 8)

    def both(ref):
        return jnp.concatenate([ref[pl.ds(low_rows, share), :], ref[pl.ds(high_rows, share), :]], axis=0)

    here = both(table)
    own_fields = from_fields(
        jnp.concatenate([pltpu.roll(own_counts, half, 1), own_counts], axis=0)
    )
    shape = (2 * share, snps)
    local, col = iota(shape, 0), iota(shape, 1)
    low = local < share
    row = jnp.where(low, local, local + half - share) + me * share
    product = 1.0
    for pop in range(2):
        row_stats = [here[:, 4 * pop + k : 4 * pop + k + 1] for k in range(3)]
        product *= correlation(row_stats, own_stats[pop], own_fields[pop])
    inside = (low & (col > row)) | (~low & (col >= half) & (col < row))
    own_kept = jnp.where(inside & (jnp.abs(col - row) <= reach_here), product, 0.0)
    rows_here = both(annot_ref).astype(jnp.bfloat16)
    scores[...] = dot_rounded(own_kept, rows_here, 0)
    direct = dot_rounded(own_kept, annot_ref[...].astype(jnp.bfloat16), 1)
    scores[pl.ds(low_rows, share), :] += direct[0:share, :]
    scores[pl.ds(high_rows, share), :] += direct[share:, :]

    slice_rows = pl.ds(pl.multiple_of(me * wide, 8), wide)
    mine = table[slice_rows, :]
    mine_ref[...] = mine
    product = 1.0
    for pop in range(2):
        own_row = [mine[:, 4 * pop + k : 4 * pop + k + 1] for k in range(4)]
        product *= correlation(own_row, own_row, own_row[3])
    scores[slice_rows, :] += annot_ref[slice_rows, :] * product
    for step, target in enumerate(targets, 2):
        group = partner(me, step, groups)
        rows = scores[pl.ds(pl.multiple_of(group * wide, 8), wide), :]
        target[...] = pack_halves(rows).astype(target.dtype)

    size = wide // 2
    left_places, right_places = owner_places(groups, size)
    left_table, right_table = rows_at(table, left_places, size), rows_at(table, right_places, size)
    is_left = iota(rows_ref.shape[1:], 1) < size
    for pop in range(2):
        for k in range(3):
            column = slice(4 * pop + k, 4 * pop + k + 1)
            rows_ref[3 * pop + k] = jnp.where(is_left, left_table[:, column], right_table[:, column])
    theirs = near_annot_ref[slice_rows, :]
    columns = [theirs[0:size], pltpu.roll(theirs[size:], HALF_LANES, 1), jnp.zeros((LANES - wide, LANES))]
    columns_ref[...] = jnp.concatenate(columns, axis=0).astype(jnp.bfloat16)

    own_places, near_places = spare_places(groups, size)
    shape = spare_rows_ref.shape[1:]
    lane = iota(shape, 1)
    tables = [table[pl.ds(pl.multiple_of(place, 8), size), :] for place in own_places]
    for pop in range(2):
        for k in range(3):
            column = slice(4 * pop + k, 4 * pop + k + 1)
            spare_rows_ref[3 * pop + k] = by_slot(
                [jnp.broadcast_to(values[:, column], shape) for values in tables], lane, size
            )
    columns = [rows_at(near_annot_ref, near_places, size)]
    columns.append(jnp.zeros((shape[1] - groups * size, LANES), jnp.float32))
    spare_columns_ref[...] = jnp.concatenate(columns, axis=0).astype(jnp.bfloat16)


def near_score_kernel(groups, share, reach_ref, *refs):
    near_parts, refs = refs[:groups], refs[groups:]
    own_ref, mine_ref, rows_ref, columns_ref, spare_rows_ref, spare_columns_ref = refs[:6]
    near_annot_ref, annot_ref, masks_ref, spare_mask_ref, own_rows_ref = refs[6:11]
    out_ref, send_ref, near_out_ref, flipped, scores, other = refs[11:]
    snps = annot_ref.shape[0]
    wide = snps // groups
    size = wide // 2
    tiles = snps // LANES
    me = lax.axis_index("hap")
    block = lax.axis_index("snp")
    last = reach_ref.shape[0] - 1
    reach_here = reach_ref[block]
    reach_there = jnp.where(
        me < groups // 2, reach_ref[jnp.minimum(block + 1, last)], reach_ref[jnp.maximum(block - 1, 0)]
    )

    scores[...] = own_ref[...]
    near_sums = sum((part[...] for part in near_parts[1:]), near_parts[0][...])
    near_counts = from_tiles(near_sums[0 : tiles * share, :], share)
    start = tiles * share
    rest = near_sums[start + size : start + size + size // 2, :]
    rest = jnp.concatenate([rest, pltpu.roll(rest, HALF_LANES, 1)], axis=0)
    spare_fields = from_fields(jnp.concatenate([near_sums[start : start + size, :], rest], axis=1))
    extras = from_fields(near_sums[start + size + size // 2 :, :])
    near_stats, near_lines, spare_stats = [], [], []
    for pop in range(2):
        count = extras[pop][0:1, :]
        totals = jnp.concatenate([extras[pop][3:4, :], extras[pop][4:5, :]], axis=1)
        spare_stats.append(column_stats(totals, jnp.concatenate([count, count], axis=1)))
        near_stats.append(column_stats(extras[pop][1:2, :], extras[pop][0:1, :]))
        near_lines += [*near_stats[pop], extras[pop][2:3, :]]
    near_table = jnp.concatenate(near_lines, axis=0).T[0:wide, :]

    slots = [near_counts[:, 0:LANES]]
    for slot in range(1, groups):
        slots.append(pltpu.roll(near_counts, snps - slot * wide, 1)[:, 0:LANES])
    flipped[:, 0:size] = slots[0].T
    slots.append(pltpu.roll(flipped[0:size, :], size, 1))
    near_fields = from_fields(jnp.concatenate(slots, axis=0))
    product = 1.0
    for pop in range(2):
        row_stats = [rows_ref[3 * pop + k] for k in range(3)]
        product *= correlation(row_stats, near_stats[pop], near_fields[pop])
    near_here = jnp.where(masks_ref[0] > 0.0, product, 0.0)
    near_there = jnp.where(masks_ref[1] > 0.0, product, 0.0)
    slice_rows = pl.ds(pl.multiple_of(me * wide, 8), wide)
    direct = dot_rounded(near_here, columns_ref[...], 1)
    turned = pltpu.roll(direct, HALF_LANES, 1)
    left_places, right_places = owner_places(groups, size)
    other[...] = jnp.zeros_like(other)
    for ref, values, places in ((scores, direct, left_places[:-1]), (other, turned, right_places)):
        for slot, place in enumerate(places):
            ref[pl.ds(pl.multiple_of(place, 8), size), :] += values[slot * size : (slot + 1) * size, :]
    product = 1.0
    for pop in range(2):
        row_stats = [spare_rows_ref[3 * pop + k] for k in range(3)]
        product *= correlation(row_stats, spare_stats[pop], spare_fields[pop])
    spare_here = jnp.where(spare_mask_ref[...] > 0.0, product, 0.0)
    lane = iota(spare_here.shape, 1)
    spare_here = [
        jnp.where((lane >= slot * size) & (lane < (slot + 1) * size), spare_here, 0.0)
        for slot in range(groups)
    ]
    direct = dot_rounded(jnp.concatenate(spare_here, axis=0), spare_columns_ref[...], 1)
    for slot, place in enumerate(spare_places(groups, size)[0]):
        scores[pl.ds(pl.multiple_of(place, 8), size), :] += direct[slot * size : (slot + 1) * size, :]
    near_scores = dot_rounded(near_there, own_rows_ref[...], 0)
    near_scores = jnp.where(
        iota((size, LANES), 1) < HALF_LANES, near_scores[0:size], near_scores[size:wide]
    )

    mine_table = mine_ref[...]
    far_product = 1.0
    for pop in range(2):
        own_row = [mine_table[:, 4 * pop + k : 4 * pop + k + 1] for k in range(3)]
        near_row = [near_table[:, 4 * pop + k : 4 * pop + k + 1] for k in range(4)]
        far_product *= correlation(own_row, near_row, near_row[3])
    scores[slice_rows, :] += near_annot_ref[slice_rows, :] * jnp.where(reach_here >= snps, far_product, 0.0)
    far_scores = annot_ref[slice_rows, :] * jnp.where(reach_there >= snps, far_product, 0.0)
    near_out_ref[...] = (near_scores + pack_halves(far_scores)).astype(near_out_ref.dtype)

    def packed(step):
        group = partner(me, step, groups)
        rows = pl.ds(pl.multiple_of(group * wide, 8), wide)
        return pack_halves(scores[rows, :] + other[rows, :])

    out_ref[...] = packed(0)
    send_ref[...] = packed(1).astype(send_ref.dtype)


def column_finish_kernel(*refs):
    *parts, out_ref = refs
    packed = sum(part[...].astype(jnp.float32) for part in parts)
    out_ref[...] = unpack_halves(packed).T[0 : out_ref.shape[0], :]


def sum_kernel(*refs):
    *parts, own_ref, there_ref = refs
    total = sum((part[...].astype(jnp.float32) for part in parts[1:]), parts[0][...])
    own_ref[...] = total
    half = there_ref.shape[0]
    left = iota((half, LANES), 1) < HALF_LANES
    second = total[half:]
    if second.shape[0] < half:
        second = jnp.concatenate([second, jnp.zeros((half - second.shape[0], LANES))], axis=0)
    there_ref[...] = jnp.where(left, pltpu.roll(total[0:half], HALF_LANES, 1), second)


def finish_kernel(own_ref, there_ref, out_ref):
    annots, rows = out_ref.shape
    there = there_ref[...]
    there = jnp.concatenate([there, pltpu.roll(there, HALF_LANES, 1)], axis=0)
    out_ref[...] = (own_ref[...] + there[0:rows]).T[0:annots, :]


def around(value, groups, step):
    return lax.ppermute(
        value, "hap", [(source, partner(source, step, groups)) for source in range(groups)]
    )


def swapped(value, first):
    pairs = []
    for block in range(first, lax.axis_size("snp") - 1, 2):
        pairs += [(block, block + 1), (block + 1, block)]
    return lax.ppermute(value, "snp", pairs)


def per_device(haplotypes, labels, annotations, reach):
    rows, snps = haplotypes.shape
    half = snps // 2
    groups = lax.axis_size("hap")
    blocks = lax.axis_size("snp")
    share = round_up(-(-half // groups), 16)
    folded_rows = share * groups
    out_share = snps // groups
    padded = half + folded_rows
    annot_part = 32
    bf16, f32, i32 = jnp.bfloat16, jnp.float32, jnp.int32
    shape = jax.ShapeDtypeStruct

    packed = shape((rows // 2 + annot_part, snps), bf16)
    haplotypes = pltpu.with_memory_space_constraint(haplotypes, pltpu.HBM)
    annots_in = pltpu.with_memory_space_constraint(annotations, pltpu.HBM)
    alleles, far, close = call(
        prepare_kernel,
        [shape((rows, snps), bf16), packed, packed],
        [HBM, HBM],
        [
            pltpu.VMEM((rows, snps), i32),
            pltpu.VMEM(annotations.shape, i32),
            pltpu.SemaphoreType.DMA((2 * len(CHUNKS) + 1,)),
        ],
        moved=rows * snps * 8,
    )(haplotypes, annots_in)
    from_far = swapped(far, 1)
    from_close = swapped(close, 0)

    by_column = groups == len(LEFT_BLOCKS)
    by_snp = shape((snps, LANES), f32)
    compact = shape((share * (snps // LANES) + 8, LANES), i32)
    own_share_counts = compact if by_column else shape((share, snps), i32)
    near_share_counts = shape((compact.shape[0] + share + share // 2, LANES), i32)
    tile = pltpu.VMEM((snps + 16, snps), f32)
    folded = pltpu.VMEM((folded_rows, snps), i32)
    weighted, totals, *own_parts = call(
        functools.partial(own_kernel, groups, share),
        [shape((snps + 16, rows), bf16), shape((8, snps), f32)] + [own_share_counts] * groups,
        [VMEM, VMEM],
        [tile, folded],
        flops=2 * rows * snps * snps,
        moved=rows * snps * 4,
    )(alleles, labels.reshape(1, rows))
    order = (2, 3, 1) if by_column else range(groups - 1, 0, -1)
    own_parts = [own_parts[0]] + [around(own_parts[k], groups, k) for k in order]

    near_shapes = [own_share_counts] + [near_share_counts if by_column else shape((share + 8, snps), i32)] * groups
    if by_column:
        work = dict(flops=4 * rows * snps * LANES, moved=rows * snps * 4)
        flipped = pltpu.VMEM((snps, LANES), f32)
        pair_rows = (groups + 1) * (out_share // 2)
        side_shapes = [((2 * share, snps), i32), ((2 * (share + 8), 2 * LANES), i32), ((8, snps), f32)]
        *close_counts, own_annots, masks, spare_mask, own_rows = call(
            functools.partial(close_kernel, groups),
            [shape(*args) for args in side_shapes]
            + [
                by_snp,
                shape((2, pair_rows, LANES), f32),
                shape((share, 2 * LANES), f32),
                shape((pair_rows, LANES), bf16),
            ],
            [SMEM] + [VMEM] * 3,
            [tile, flipped],
            **work,
        )(reach, weighted, from_close, annotations)
        near_parts = call(
            functools.partial(far_kernel, groups, share),
            near_shapes[1:],
            [VMEM] * 6,
            [pltpu.VMEM(*args) for args in side_shapes]
            + [tile, flipped, pltpu.VMEM((8 * groups, LANES), i32)],
            **work,
        )(weighted, from_far, *close_counts, totals)
    else:
        own_sum, *near_parts = call(
            functools.partial(near_kernel, groups, share),
            near_shapes,
            [VMEM] * (4 + groups),
            [pltpu.VMEM((rows, snps), bf16), tile, folded],
            flops=2 * rows * snps * snps,
            moved=rows * snps * 4,
        )(weighted, from_far, from_close, totals, *own_parts)
    near_parts = [near_parts[0]] + [around(near_parts[k], groups, k) for k in order]

    if not by_column:
        own_annots, near_annots = call(annots_kernel, [by_snp, by_snp], [VMEM] * 3, moved=1 << 20)(
            annotations, from_far[rows // 2 :], from_close[rows // 2 :]
        )
    pairs = []
    for block in range(blocks):
        for group in range(groups):
            target = block + 1 if group < groups // 2 else block - 1
            if 0 <= target < blocks:
                pairs.append((block * groups + group, target * groups + group))

    def to_neighbour(value):
        return lax.ppermute(value, ("snp", "hap"), pairs)

    result = shape((annotations.shape[0], out_share), f32)
    half_share = round_up(-(-out_share // 2), 8)
    own_share = shape((out_share, LANES), f32)
    packed_share = shape((half_share, LANES), f32)
    if by_column:
        sent = shape((half_share, LANES), bf16)
        *prepared, second, third = call(
            functools.partial(own_score_kernel, groups, share),
            [
                by_snp,
                shape((out_share, LANES), f32),
                shape((6, pair_rows, LANES), f32),
                shape((LANES, LANES), bf16),
                shape((6, share, 2 * LANES), f32),
                shape((2 * LANES, LANES), bf16),
                by_snp,
                sent,
                sent,
            ],
            [SMEM] + [VMEM] * (groups + 3),
            [pltpu.VMEM((snps, LANES), f32)],
            flops=1 << 33,
            moved=1 << 20,
        )(reach, *own_parts, own_annots, from_far[rows // 2 :], from_close[rows // 2 :])
        parts = [around(third, groups, 3), around(second, groups, 2)]
        own_scores, send, there = call(
            functools.partial(near_score_kernel, groups, share),
            [packed_share, sent, sent],
            [SMEM] + [VMEM] * (groups + 11),
            [pltpu.VMEM((LANES, LANES), i32)] + [pltpu.VMEM((snps, LANES), f32)] * 2,
            flops=1 << 26,
            moved=1 << 21,
        )(reach, *near_parts, *prepared, own_annots, masks, spare_mask, own_rows)
        parts += [around(send, groups, 1), to_neighbour(there)]
        return call(column_finish_kernel, result, [VMEM] * 5)(own_scores, *parts)

    tall = pltpu.VMEM((padded, LANES), f32)
    scores = call(
        functools.partial(score_kernel, groups, share),
        [own_share] + [shape((out_share, LANES), bf16)] * (groups - 1),
        [SMEM] + [VMEM] * (groups + 3),
        [tall, tall, tall, tall],
        flops=1 << 26,
        moved=1 << 21,
    )(reach, own_sum, *near_parts, own_annots, near_annots)
    scores = [scores[0]] + [around(scores[k], groups, k) for k in range(groups - 1, 0, -1)]
    own_scores, near_scores = call(sum_kernel, [own_share, packed_share], [VMEM] * groups)(*scores)
    return call(finish_kernel, result, [VMEM] * 2)(own_scores, to_neighbour(near_scores))


def solution(mesh):
    in_specs = (
        P("hap", ("parts", "snp")),
        P(("parts", "hap")),
        P(None, ("parts", "snp")),
        P("parts"),
    )
    out_specs = P(None, ("parts", "snp", "hap"))
    return jax.shard_map(
        per_device, mesh=mesh, in_specs=in_specs, out_specs=out_specs, check_vma=False
    )
```

```python
import functools

import jax
import jax.numpy as jnp
from jax import lax
from jax.experimental import pallas as pl
from jax.experimental.pallas import tpu as pltpu
from jax.sharding import PartitionSpec as P

VARIANCE_FLOOR = 0.01
BASE_BITS = 12
BASE = 1 << BASE_BITS
FIELD_BITS = 16
LANES = 128
HALF_LANES = LANES // 2
CHUNKS = (8, 5, 3)
VMEM = pl.BlockSpec(memory_space=pltpu.VMEM)
SMEM = pl.BlockSpec(memory_space=pltpu.SMEM)
HBM = pl.BlockSpec(memory_space=pltpu.HBM)
VMEM_LIMIT = 24 * 1024 * 1024


def iota(shape, axis):
    return lax.broadcasted_iota(jnp.int32, shape, axis)


def round_up(value, step):
    return -(-value // step) * step


def to_fields(values):
    whole = values.astype(jnp.int32)
    return whole + (whole >> BASE_BITS) * ((1 << FIELD_BITS) - BASE)


def from_fields(packed):
    first = packed & ((1 << FIELD_BITS) - 1)
    second = lax.shift_right_logical(packed, FIELD_BITS)
    return first.astype(jnp.float32), second.astype(jnp.float32)


def call(kernel, out_shape, in_specs, scratch_shapes=(), flops=0, moved=0):
    several = isinstance(out_shape, (list, tuple))
    return pl.pallas_call(
        kernel,
        out_shape=out_shape,
        in_specs=in_specs,
        out_specs=[VMEM] * len(out_shape) if several else VMEM,
        scratch_shapes=list(scratch_shapes),
        compiler_params=pltpu.CompilerParams(vmem_limit_bytes=VMEM_LIMIT),
        cost_estimate=pl.CostEstimate(flops=flops, bytes_accessed=moved, transcendentals=0),
    )


def odd_block():
    return lax.rem(lax.axis_index("snp"), 2) == 1


def store_packed(up_ref, down_ref, where, first, second):
    left = iota((first.shape[0], LANES), 1) < HALF_LANES
    middle = first[:, LANES : 2 * LANES]
    turned = pltpu.roll(second[:, LANES : 2 * LANES], HALF_LANES, 1)
    for ref, side, mixed in (
        (up_ref, slice(0, LANES), jnp.where(left, middle, turned)),
        (down_ref, slice(2 * LANES, 3 * LANES), jnp.where(left, turned, middle)),
    ):
        ref[where, 0:LANES] = first[:, side].astype(jnp.bfloat16)
        ref[where, LANES : 2 * LANES] = mixed.astype(jnp.bfloat16)
        ref[where, 2 * LANES : 3 * LANES] = second[:, side].astype(jnp.bfloat16)


def load_packed(up, down):
    left = iota((up.shape[0], LANES), 1) < HALF_LANES
    up_mixed, down_mixed = up[:, LANES : 2 * LANES], down[:, LANES : 2 * LANES]
    first = jnp.where(left, up_mixed, down_mixed)
    second = jnp.where(left, down_mixed, up_mixed)
    second = pltpu.roll(second.astype(jnp.float32), HALF_LANES, 1).astype(second.dtype)
    return (
        (up[:, :LANES], first, down[:, :LANES]),
        (up[:, 2 * LANES :], second, down[:, 2 * LANES :]),
    )


def prepare_kernel(hap_ref, annot_ref, alleles_ref, far_ref, close_ref, held, held_annots, sems):
    rows = hap_ref.shape[0]
    annot_rows = annot_ref.shape[0]
    sizes = [chunk * (rows // 32) for chunk in CHUNKS]
    places = [sum(sizes[:number]) for number in range(len(sizes))]
    pieces = [
        (side * (rows // 2) + place, size) for place, size in zip(places, sizes) for side in range(2)
    ]
    copies = [
        pltpu.make_async_copy(
            hap_ref.at[pl.ds(start, size)], held.at[pl.ds(start, size)], sems.at[number]
        )
        for number, (start, size) in enumerate(pieces)
    ]
    copies.append(pltpu.make_async_copy(annot_ref, held_annots, sems.at[len(pieces)]))
    for copy in copies:
        copy.start()
    part = far_ref.shape[0] - rows // 2
    odd = odd_block()

    def store(where, first, second):
        @pl.when(odd)
        def _():
            store_packed(close_ref, far_ref, where, first, second)

        @pl.when(jnp.logical_not(odd))
        def _():
            store_packed(far_ref, close_ref, where, first, second)

    for chunk, (place, size) in enumerate(zip(places, sizes)):
        pair = []
        for number in (2 * chunk, 2 * chunk + 1):
            copies[number].wait()
            where = slice(pieces[number][0], pieces[number][0] + size)
            values = held[where, :].astype(jnp.float32)
            alleles_ref[where, :] = values.astype(jnp.bfloat16)
            pair.append(values)
        store(slice(place, place + size), *pair)
    copies[-1].wait()
    annots = jnp.concatenate(
        [
            held_annots[...].astype(jnp.float32),
            jnp.zeros((2 * part - annot_rows, annot_ref.shape[1]), jnp.float32),
        ],
        axis=0,
    )
    store(slice(rows // 2, rows // 2 + part), annots[:part], annots[part:])


def partner(group, step, groups):
    if groups & (groups - 1) == 0:
        return group ^ step
    return (group + step) % groups


def send_shares(groups, source, share, targets):
    me = lax.axis_index("hap")
    for step, target in enumerate(targets):
        group = partner(me, step, groups)
        rows = source[pl.ds(pl.multiple_of(group * share, 8), share), :]
        target[0:share, :] = rows.astype(target.dtype)


def send_tiles(groups, source, share, targets):
    me = lax.axis_index("hap")
    for step, target in enumerate(targets):
        owner = partner(me, step, groups)
        counts = source[pl.ds(pl.multiple_of(owner * share, 8), share), :]
        for k in range(source.shape[1] // LANES):
            target[k * share : (k + 1) * share, :] = counts[:, k * LANES : (k + 1) * LANES]


def from_tiles(counts, share):
    tiles = counts.shape[0] // share
    return jnp.concatenate([counts[k * share : (k + 1) * share, :] for k in range(tiles)], axis=1)


def own_kernel(groups, share, alleles_ref, label_ref, *refs):
    weighted_ref, totals_ref, *targets = refs[: 2 + groups]
    tile, folded = refs[2 + groups :]
    rows, snps = alleles_ref.shape
    half = snps // 2
    weight = jnp.where(label_ref[...] > 0, float(BASE), 1.0)
    weighted_ref[0:snps, :] = alleles_ref[...].T * weight.astype(jnp.bfloat16)
    extra = weighted_ref.shape[0] - snps
    weighted_ref[snps:, :] = jnp.broadcast_to(weight, (extra, rows)).astype(jnp.bfloat16)
    tile[...] = jnp.dot(weighted_ref[...], alleles_ref[...], preferred_element_type=jnp.float32)
    count = jnp.sum(weight, axis=1, keepdims=True)
    totals_ref[...] = jnp.concatenate(
        [tile[snps : snps + 1, :], jnp.broadcast_to(count, (1, snps)), jnp.zeros((6, snps))], axis=0
    )
    row, col = iota((half, snps), 0), iota((half, snps), 1)
    moved = (col < half) | (col - half > row)
    turned = pltpu.roll(tile[0:half, :], half, 1)
    folded[0:half, :] = to_fields(jnp.where(moved, turned, tile[half:snps, :]))
    if folded.shape[0] > half:
        folded[half:, :] = jnp.zeros((folded.shape[0] - half, snps), jnp.int32)
    if groups != len(LEFT_BLOCKS):
        send_shares(groups, folded, share, targets)
        return
    tiles = snps // LANES
    shared = [totals_ref[0:1, k * LANES : (k + 1) * LANES] for k in range(tiles)]
    shared += [totals_ref[1:2, 0:LANES], jnp.zeros((7 - tiles, LANES))]
    extras = to_fields(jnp.concatenate(shared, axis=0))
    send_tiles(groups, folded, share, targets)
    for target in targets:
        target[tiles * share :, :] = extras


LEFT_BLOCKS = ((0, 1, 2, 3), (2, 3, 6, 7), (4, 0, 1, 2), (6, 0, 4, 5))
RIGHT_BLOCKS = ((2, 3, 6, 7), (4, 5, 6, 7), (0, 1, 2, 4), (0, 4, 5, 6))


SPARE_OWN = ((0, 0, 0, 0), (1, 1, 2, 2), (4, 5, 6, 7), (6, 6, 7, 7))
SPARE_NEAR = ((4, 5, 6, 7), (4, 5, 4, 5), (3, 3, 3, 3), (1, 2, 1, 2))


def fold_spare(tile, spare, first):
    owners = len(SPARE_OWN)
    snps = tile.shape[1]
    size = snps // (2 * owners)
    count = spare.shape[0] // 2
    totals = tile[snps : snps + count - size, :]
    lane = iota((count, snps), 1)
    for number, owner in enumerate(range(first, first + 2)):
        mixed = None
        for slot in range(owners):
            own, near = SPARE_OWN[owner][slot], SPARE_NEAR[owner][slot]
            before = (SPARE_OWN[owner][slot - 1], SPARE_NEAR[owner][slot - 1] + 1) if slot else None
            if before == (own, near):
                continue
            values = jnp.concatenate([tile[own * size : (own + 1) * size, :], totals], axis=0)
            shift = (slot - near) * size % snps
            values = pltpu.roll(values, shift, 1) if shift else values
            mixed = values if mixed is None else jnp.where(lane >= slot * size, values, mixed)
        spare[number * count : (number + 1) * count, :] = to_fields(mixed[:, 0 : spare.shape[1]])


def fold_by_column(tile, flipped, folded, first):
    groups = len(LEFT_BLOCKS)
    owners = range(first, first + groups // 2)
    snps = folded.shape[1]
    wide = snps // groups
    size = wide // 2
    shape = (size, snps)
    row, lane = iota(shape, 0), iota(shape, 1)

    def block(number):
        return tile[number * size : (number + 1) * size, :]

    diagonal, within = block(2 * first), lane - 2 * first * size
    for number in range(2 * first + 1, 2 * first + groups):
        diagonal = jnp.where(lane >= number * size, block(number), diagonal)
        within = jnp.where(lane >= number * size, lane - number * size, within)
    apart = jnp.sum(jnp.where(row == within, diagonal, 0.0), axis=0, keepdims=True)
    flipped[:, 0:size] = diagonal.T
    corner = diagonal
    for owner in owners:
        start = (2 * owner + 1) * size
        turned = jnp.concatenate(
            [flipped[start : start + size, :], jnp.zeros((size, snps - LANES), jnp.float32)], axis=1
        )
        if owner:
            turned = pltpu.roll(turned, owner * wide, 1)
        inside = lane - owner * wide
        other = (row <= inside) if first == 0 else (row >= inside)
        corner = jnp.where((inside >= 0) & (inside < size) & other, turned, corner)
    rolled = []
    for shift in range(groups):
        mixed = None
        for owner in owners:
            slot = (owner + shift) % groups
            left = block(LEFT_BLOCKS[owner][slot]) if slot else corner
            start = owner * wide
            mixed = left if mixed is None else jnp.where(lane >= start, left, mixed)
            mixed = jnp.where(lane >= start + size, block(RIGHT_BLOCKS[owner][slot]), mixed)
        rolled.append(pltpu.roll(mixed, shift * wide, 1) if shift else mixed)
    for number, owner in enumerate(owners):
        mixed = rolled[(0 - owner) % groups]
        for slot in range(1, groups):
            mixed = jnp.where(lane >= slot * wide, rolled[(slot - owner) % groups], mixed)
        folded[number * size : (number + 1) * size, :] = to_fields(mixed)
    return apart


def above(far):
    return odd_block() == far


def side_dot(weighted_ref, side_ref):
    rows = weighted_ref.shape[1]
    half = rows // 2

    def dot(which, columns):
        return jnp.dot(
            weighted_ref[:, which], side_ref[0:half, columns], preferred_element_type=jnp.float32
        )

    first = dot(slice(0, half), slice(0, 2 * LANES))
    second = dot(slice(half, rows), slice(LANES, 3 * LANES))
    whole = first[:, 0:LANES] + second[:, LANES:]
    return whole, first[:, LANES:] + pltpu.roll(second[:, 0:LANES], HALF_LANES, 1)


def fold_side(far, weighted_ref, side_ref, main, spare, lines, tile, flipped):
    snps = tile.shape[1]
    whole, shared = side_dot(weighted_ref, side_ref)
    tile[:, LANES : 2 * LANES] = shared

    def fold(first, start):
        tile[:, start : start + LANES] = whole
        apart = fold_by_column(tile, flipped, main, first)
        fold_spare(tile, spare, 2 - first)
        lines[0:1, :] = tile[snps : snps + 1, :]
        lines[1:2, :] = apart

    @pl.when(above(far))
    def _():
        fold(0, 0)

    @pl.when(jnp.logical_not(above(far)))
    def _():
        fold(2, 2 * LANES)


def close_kernel(groups, reach_ref, weighted_ref, side_ref, annot_ref, *refs):
    main_ref, spare_ref, lines_ref, annots, masks_ref, spare_mask_ref, own_rows_ref, tile, flipped = refs
    fold_side(False, weighted_ref, side_ref, main_ref, spare_ref, lines_ref, tile, flipped)
    snps = annot_ref.shape[1]
    half, wide = snps // 2, snps // groups
    size = wide // 2
    own = annot_ref[...].astype(jnp.float32)
    own = jnp.concatenate([own, jnp.zeros((LANES - own.shape[0], snps), jnp.float32)], axis=0)
    annots[...] = own.T

    me = lax.axis_index("hap")
    block = lax.axis_index("snp")
    last = reach_ref.shape[0] - 1
    upper = me < groups // 2
    reach_here = reach_ref[block]
    reach_there = jnp.where(
        upper, reach_ref[jnp.minimum(block + 1, last)], reach_ref[jnp.maximum(block - 1, 0)]
    )
    left_places, right_places = owner_places(groups, size)
    local, lane = iota((size, LANES), 0), iota((size, LANES), 1)
    own_row = jnp.concatenate(
        [local + jnp.where(lane < size, a, b) for a, b in zip(left_places, right_places)], axis=0
    )
    shape = own_row.shape
    lane = iota(shape, 1)
    apart = jnp.abs(own_row - (lane + me * wide))
    ahead = (own_row - (lane + me * wide)) * jnp.where(upper, 1, -1) > 0
    real = ahead & (lane < wide) & ((lane >= size) | (iota(shape, 0) < groups * size))
    inside = (own_row - half) * jnp.where(upper, 1, -1) < jnp.where(upper, 0, 1)
    masks_ref[0] = jnp.where(real & inside & (snps - apart <= reach_here), 1.0, 0.0)
    masks_ref[1] = jnp.where(real & (snps - apart <= reach_there), 1.0, 0.0)
    own_rows = rows_at(annots, left_places, size) + pltpu.roll(
        rows_at(annots, right_places, size), HALF_LANES, 1
    )
    own_rows_ref[...] = own_rows.astype(jnp.bfloat16)

    own_places, near_places = spare_places(groups, size)
    shape = spare_mask_ref.shape
    local, lane = iota(shape, 0), iota(shape, 1)
    own_row = by_slot([local + place for place in own_places], lane, size)
    near_col = by_slot(
        [lane + (place - slot * size) for slot, place in enumerate(near_places)], lane, size
    )
    close = snps - jnp.abs(own_row - near_col) <= reach_here
    spare_mask_ref[...] = jnp.where(close & (lane < groups * size), 1.0, 0.0)


def by_slot(values, lane, size):
    mixed = values[0]
    for slot in range(1, len(values)):
        mixed = jnp.where(lane >= slot * size, values[slot], mixed)
    return mixed


def far_kernel(groups, share, weighted_ref, side_ref, close_ref, close_spare_ref, close_lines_ref, totals_ref, *refs):
    targets, (main, spare, lines, tile, flipped, extras) = refs[:groups], refs[groups:]
    fold_side(True, weighted_ref, side_ref, main, spare, lines, tile, flipped)
    snps = tile.shape[1]
    half, size = snps // 2, share
    odd = odd_block()

    tiles = snps // LANES
    count = spare.shape[0] // 2
    from_far = (iota((8, snps), 1) < half) == odd
    by_column = jnp.concatenate(
        [totals_ref[1:2, :], jnp.where(from_far, lines[...], close_lines_ref[...])[0:2, :]], axis=0
    )
    by_column = jnp.concatenate([by_column, jnp.zeros((5, snps))], axis=0)
    for owner in range(groups):
        start = owner * (snps // groups)
        columns = pltpu.roll(by_column, snps - start, 1) if owner else by_column
        where = slice((owner & 1) * count + size, (owner & 1) * count + size + 1)
        second = odd if owner >= groups // 2 else jnp.logical_not(odd)
        spare_totals = jnp.where(second, spare[where, :], close_spare_ref[where, :])
        extras[8 * owner : 8 * (owner + 1), :] = jnp.concatenate(
            [
                to_fields(columns[0:3, 0:LANES]),
                spare_totals[:, 0:LANES],
                spare_totals[:, LANES:],
                jnp.zeros((3, LANES), jnp.int32),
            ],
            axis=0,
        )
    me = lax.axis_index("hap")
    left = iota((size // 2, LANES), 1) < HALF_LANES
    for step, target in enumerate(targets):
        owner = partner(me, step, groups)
        first = (owner < groups // 2) == odd
        where = pl.ds(pl.multiple_of((owner & 1) * size, 8), size)
        counts = jnp.where(first, main[where, :], close_ref[where, :])
        for k in range(tiles):
            target[k * size : (k + 1) * size, :] = counts[:, k * LANES : (k + 1) * LANES]
        where = pl.ds(pl.multiple_of((owner & 1) * count, 8), size)
        counts = jnp.where(first, close_spare_ref[where, :], spare[where, :])
        start = tiles * size
        target[start : start + size, :] = counts[:, 0:LANES]
        rest = counts[:, LANES:]
        target[start + size : start + size + size // 2, :] = jnp.where(
            left, rest[0 : size // 2], pltpu.roll(rest[size // 2 :], HALF_LANES, 1)
        )
        target[start + size + size // 2 :, :] = extras[pl.ds(pl.multiple_of(owner * 8, 8), 8), :]


def near_kernel(groups, share, weighted_ref, far_ref, close_ref, totals_ref, *refs):
    own_parts, own_sum_ref = refs[:groups], refs[groups]
    targets, (near, tile, folded) = refs[groups + 1 : 2 * groups + 1], refs[2 * groups + 1 :]
    rows, snps = near.shape
    half = snps // 2
    odd = odd_block()

    def unpack(up_ref, down_ref):
        pieces = load_packed(up_ref[0 : rows // 2, :], down_ref[0 : rows // 2, :])
        for side in range(2):
            where = slice(side * (rows // 2), (side + 1) * (rows // 2))
            for number in range(3):
                near[where, number * LANES : (number + 1) * LANES] = pieces[side][number]

    @pl.when(odd)
    def _():
        unpack(far_ref, close_ref)

    @pl.when(jnp.logical_not(odd))
    def _():
        unpack(close_ref, far_ref)

    tile[...] = jnp.dot(weighted_ref[...], near[...], preferred_element_type=jnp.float32)
    row, col = iota((half, snps), 0), iota((half, snps), 1)
    moved = (col >= half) & (col - half < row)
    turned = pltpu.roll(tile[0:half, :], half, 1)
    folded[0:half, :] = to_fields(jnp.where(moved, turned, tile[half:snps, :]))
    if folded.shape[0] > half:
        folded[half:, :] = jnp.zeros((folded.shape[0] - half, snps), jnp.int32)
    square = (snps, snps)
    far = jnp.sum(
        jnp.where(iota(square, 0) == iota(square, 1), tile[0:snps, :], 0.0), axis=0, keepdims=True
    )
    extras = to_fields(
        jnp.concatenate(
            [totals_ref[0:2, :], tile[snps : snps + 1, :], far, jnp.zeros((4, snps))], axis=0
        )
    )
    send_shares(groups, folded, share, targets)
    for target in targets:
        target[share:, :] = extras
    own_sum_ref[...] = sum((part[...] for part in own_parts[1:]), own_parts[0][...])


def annots_kernel(annot_ref, far_ref, close_ref, own_ref, near_ref):
    snps = annot_ref.shape[1]
    own = annot_ref[...].astype(jnp.float32)
    own = jnp.concatenate([own, jnp.zeros((LANES - own.shape[0], snps), jnp.float32)], axis=0)
    own_ref[...] = own.T
    near_ref[...] = near_annots_by_snp(far_ref, close_ref)


def near_annots_by_snp(far_ref, close_ref):
    part, snps = far_ref.shape
    wide = 2 * part
    odd = odd_block()
    far, close = far_ref[...].astype(jnp.float32), close_ref[...].astype(jnp.float32)
    first, second = load_packed(jnp.where(odd, far, close), jnp.where(odd, close, far))
    near = jnp.concatenate(
        [
            jnp.concatenate([piece.astype(jnp.float32) for piece in first], axis=1),
            jnp.concatenate([piece.astype(jnp.float32) for piece in second], axis=1),
            jnp.zeros((LANES - wide, snps), jnp.float32),
        ],
        axis=0,
    )
    return near.T


def column_stats(totals, count):
    size = jnp.maximum(count, 1.0)
    frequency = totals / size
    variance = jnp.maximum(frequency * (1.0 - frequency), VARIANCE_FLOOR)
    inverse = 1.0 / jnp.sqrt(size * variance)
    low = ((0.0 - frequency) * inverse).astype(jnp.bfloat16).astype(jnp.float32)
    high = ((1.0 - frequency) * inverse).astype(jnp.bfloat16).astype(jnp.float32)
    step = high - low
    root = 1.0 / jnp.sqrt(size)
    return step, step * totals * root, (low * count + step * totals) * root


def correlation(row, col, count):
    return row[0] * col[0] * count - row[1] * col[1] + row[2] * col[2]


def split(values):
    high = values.astype(jnp.bfloat16)
    return high, (values - high.astype(jnp.float32)).astype(jnp.bfloat16)


def dot_split(values, right, axis):
    dims = (((axis,), (0,)), ((), ()))
    return sum(
        lax.dot_general(part, right, dims, preferred_element_type=jnp.float32)
        for part in split(values)
    )


def score_kernel(groups, share, reach_ref, *refs):
    own_sum_ref, near_parts = refs[0], refs[1 : groups + 1]
    annot_ref, near_annot_ref = refs[groups + 1 : groups + 3]
    targets = refs[groups + 3 : 2 * groups + 3]
    table, annots, near_annots, scores = refs[2 * groups + 3 :]
    snps = annot_ref.shape[0]
    half = snps // 2
    out_share = snps // groups
    me = lax.axis_index("hap")
    block = lax.axis_index("snp")
    last = reach_ref.shape[0] - 1
    reach_here = reach_ref[block]
    reach_up = reach_ref[jnp.minimum(block + 1, last)]
    reach_down = reach_ref[jnp.maximum(block - 1, 0)]

    own_counts = own_sum_ref[...]
    near_sums = sum((part[...] for part in near_parts[1:]), near_parts[0][...])
    extras = from_fields(near_sums[share:, :])
    near_counts = near_sums[0:share, :]

    own_stats, near_stats, lines = [], [], []
    for pop in range(2):
        count = extras[pop][1:2, :]
        own_stats.append(column_stats(extras[pop][0:1, :], count))
        near_stats.append(column_stats(extras[pop][2:3, :], count))
        lines += [*own_stats[pop], *near_stats[pop], extras[pop][0:1, :], extras[pop][3:4, :]]
    by_row = jnp.concatenate(lines, axis=0).T
    table[0:snps, 0:16] = by_row
    if table.shape[0] > snps:
        table[snps:, 0:16] = jnp.zeros((table.shape[0] - snps, 16), jnp.float32)
    annots[0:snps, :] = annot_ref[...]
    near_annots[0:snps, :] = near_annot_ref[...]
    if annots.shape[0] > snps:
        annots[snps:, :] = jnp.zeros((annots.shape[0] - snps, LANES), jnp.float32)

    low_rows = pl.multiple_of(me * share, 8)
    high_rows = pl.multiple_of(half + me * share, 8)

    def both(ref):
        return jnp.concatenate([ref[pl.ds(low_rows, share), :], ref[pl.ds(high_rows, share), :]], axis=0)

    here = both(table)
    own_count = jnp.concatenate([pltpu.roll(own_counts, half, 1), own_counts], axis=0)
    near_count = jnp.concatenate([pltpu.roll(near_counts, half, 1), near_counts], axis=0)
    shape = (2 * share, snps)
    local, col = iota(shape, 0), iota(shape, 1)
    low = local < share
    place = jnp.where(low, local, local - share) + me * share
    row = jnp.where(low, place, place + half)
    own_fields, near_fields = from_fields(own_count), from_fields(near_count)
    own_product, near_product = 1.0, 1.0
    for pop in range(2):
        row_stats = [here[:, 8 * pop + k : 8 * pop + k + 1] for k in range(3)]
        own_product *= correlation(row_stats, own_stats[pop], own_fields[pop])
        near_product *= correlation(row_stats, near_stats[pop], near_fields[pop])
    real = place < half
    own_inside = real & ((low & (col > row)) | (~low & (col >= half) & (col < row)))
    own_inside &= jnp.abs(col - row) <= reach_here
    own_kept = jnp.where(own_inside, own_product, 0.0)
    in_upper = col < half
    near_inside = real & ((low & (col < row)) | (~low & (in_upper | (col > row))))
    distance = jnp.where(in_upper, snps + col - row, snps + row - col)
    near_here = jnp.where(near_inside & (distance <= reach_here), near_product, 0.0)
    reach_there = jnp.where(in_upper, reach_up, reach_down)
    near_there = jnp.where(near_inside & (distance <= reach_there), near_product, 0.0)

    rows_here = both(annots)
    rows_there = pltpu.roll(rows_here, HALF_LANES, 1)
    scores[0:snps, :] = dot_split(
        jnp.concatenate([own_kept, near_there], axis=0),
        jnp.concatenate([rows_here, rows_there], axis=0).astype(jnp.bfloat16),
        0,
    )
    direct = dot_split(
        jnp.concatenate([own_kept, near_here], axis=1),
        jnp.concatenate([annot_ref[...], near_annot_ref[...]], axis=0).astype(jnp.bfloat16),
        1,
    )
    scores[pl.ds(low_rows, share), :] += direct[0:share, :]
    scores[pl.ds(high_rows, share), :] += direct[share:, :]

    out_rows = pl.ds(pl.multiple_of(me * out_share, 8), out_share)
    mine = table[out_rows, :]
    self_product, far_product = 1.0, 1.0
    for pop in range(2):
        k = 8 * pop
        own_row = [mine[:, k + s : k + s + 1] for s in range(3)]
        near_row = [mine[:, k + 3 + s : k + 4 + s] for s in range(3)]
        self_product *= correlation(own_row, own_row, mine[:, k + 6 : k + 7])
        far_product *= correlation(own_row, near_row, mine[:, k + 7 : k + 8])
    mine_annots = annots[out_rows, :]
    far_reach = jnp.where(me < groups // 2, reach_up, reach_down)
    scores[out_rows, :] += (
        mine_annots * self_product
        + near_annots[out_rows, :] * jnp.where(reach_here >= snps, far_product, 0.0)
        + pltpu.roll(mine_annots, HALF_LANES, 1) * jnp.where(far_reach >= snps, far_product, 0.0)
    )
    send_shares(groups, scores, out_share, targets)


def pack_halves(values):
    half = values.shape[0] // 2
    left = iota((half, LANES), 1) < HALF_LANES
    return jnp.where(left, values[0:half], pltpu.roll(values[half:], HALF_LANES, 1))


def unpack_halves(packed):
    return jnp.concatenate([packed, pltpu.roll(packed, HALF_LANES, 1)], axis=0)


def dot_rounded(values, right, axis):
    dims = (((axis,), (0,)), ((), ()))
    return lax.dot_general(
        values.astype(jnp.bfloat16), right, dims, preferred_element_type=jnp.float32
    )


def owner_places(groups, size):
    me = lax.axis_index("hap")

    def mine(blocks, slot):
        value = blocks[0][slot]
        for group in range(1, groups):
            value = jnp.where(me == group, blocks[group][slot], value)
        return value * size

    left = [mine(LEFT_BLOCKS, slot) for slot in range(groups)]
    right = [mine(RIGHT_BLOCKS, slot) for slot in range(groups)]
    return left + left[0:1], right + [(2 * me + 1) * size]


def spare_places(groups, size):
    me = lax.axis_index("hap")

    def mine(blocks, slot):
        value = blocks[0][slot]
        for group in range(1, groups):
            value = jnp.where(me == group, blocks[group][slot], value)
        return value * size

    return [[mine(blocks, slot) for slot in range(groups)] for blocks in (SPARE_OWN, SPARE_NEAR)]


def rows_at(ref, places, size):
    return jnp.concatenate([ref[pl.ds(pl.multiple_of(place, 8), size), :] for place in places], axis=0)


def own_score_kernel(
    groups, share, reach_ref, *refs
):
    own_parts, refs = refs[:groups], refs[groups:]
    annot_ref, far_ref, close_ref, scores, mine_ref, rows_ref, columns_ref, *refs = refs
    spare_rows_ref, spare_columns_ref, near_annot_ref, *targets, table = refs
    near_annot_ref[...] = near_annots_by_snp(far_ref, close_ref)
    snps = annot_ref.shape[0]
    half = snps // 2
    wide = snps // groups
    tiles = snps // LANES
    me = lax.axis_index("hap")
    reach_here = reach_ref[lax.axis_index("snp")]
    own_sums = sum((part[...] for part in own_parts[1:]), own_parts[0][...])
    own_counts = from_tiles(own_sums[0 : tiles * share, :], share)
    extras = from_fields(own_sums[tiles * share :, :])

    own_stats, lines = [], []
    for pop in range(2):
        count = jnp.concatenate([extras[pop][tiles : tiles + 1, :]] * tiles, axis=1)
        totals = jnp.concatenate([extras[pop][k : k + 1, :] for k in range(tiles)], axis=1)
        own_stats.append(column_stats(totals, count))
        lines += [*own_stats[pop], totals]
    table[:, 0:8] = jnp.concatenate(lines, axis=0).T

    low_rows = pl.multiple_of(me * share, 8)
    high_rows = pl.multiple_of(half + me * share, 8)

    def both(ref):
        return jnp.concatenate([ref[pl.ds(low_rows, share), :], ref[pl.ds(high_rows, share), :]], axis=0)

    here = both(table)
    own_fields = from_fields(
        jnp.concatenate([pltpu.roll(own_counts, half, 1), own_counts], axis=0)
    )
    shape = (2 * share, snps)
    local, col = iota(shape, 0), iota(shape, 1)
    low = local < share
    row = jnp.where(low, local, local + half - share) + me * share
    product = 1.0
    for pop in range(2):
        row_stats = [here[:, 4 * pop + k : 4 * pop + k + 1] for k in range(3)]
        product *= correlation(row_stats, own_stats[pop], own_fields[pop])
    inside = (low & (col > row)) | (~low & (col >= half) & (col < row))
    own_kept = jnp.where(inside & (jnp.abs(col - row) <= reach_here), product, 0.0)
    rows_here = both(annot_ref).astype(jnp.bfloat16)
    scores[...] = dot_rounded(own_kept, rows_here, 0)
    direct = dot_rounded(own_kept, annot_ref[...].astype(jnp.bfloat16), 1)
    scores[pl.ds(low_rows, share), :] += direct[0:share, :]
    scores[pl.ds(high_rows, share), :] += direct[share:, :]

    slice_rows = pl.ds(pl.multiple_of(me * wide, 8), wide)
    mine = table[slice_rows, :]
    mine_ref[...] = mine
    product = 1.0
    for pop in range(2):
        own_row = [mine[:, 4 * pop + k : 4 * pop + k + 1] for k in range(4)]
        product *= correlation(own_row, own_row, own_row[3])
    scores[slice_rows, :] += annot_ref[slice_rows, :] * product
    for step, target in enumerate(targets, 2):
        group = partner(me, step, groups)
        rows = scores[pl.ds(pl.multiple_of(group * wide, 8), wide), :]
        target[...] = pack_halves(rows).astype(target.dtype)

    size = wide // 2
    left_places, right_places = owner_places(groups, size)
    left_table, right_table = rows_at(table, left_places, size), rows_at(table, right_places, size)
    is_left = iota(rows_ref.shape[1:], 1) < size
    for pop in range(2):
        for k in range(3):
            column = slice(4 * pop + k, 4 * pop + k + 1)
            rows_ref[3 * pop + k] = jnp.where(is_left, left_table[:, column], right_table[:, column])
    theirs = near_annot_ref[slice_rows, :]
    columns = [theirs[0:size], pltpu.roll(theirs[size:], HALF_LANES, 1), jnp.zeros((LANES - wide, LANES))]
    columns_ref[...] = jnp.concatenate(columns, axis=0).astype(jnp.bfloat16)

    own_places, near_places = spare_places(groups, size)
    shape = spare_rows_ref.shape[1:]
    lane = iota(shape, 1)
    tables = [table[pl.ds(pl.multiple_of(place, 8), size), :] for place in own_places]
    for pop in range(2):
        for k in range(3):
            column = slice(4 * pop + k, 4 * pop + k + 1)
            spare_rows_ref[3 * pop + k] = by_slot(
                [jnp.broadcast_to(values[:, column], shape) for values in tables], lane, size
            )
    columns = [rows_at(near_annot_ref, near_places, size)]
    columns.append(jnp.zeros((shape[1] - groups * size, LANES), jnp.float32))
    spare_columns_ref[...] = jnp.concatenate(columns, axis=0).astype(jnp.bfloat16)


def near_score_kernel(groups, share, reach_ref, *refs):
    near_parts, refs = refs[:groups], refs[groups:]
    own_ref, mine_ref, rows_ref, columns_ref, spare_rows_ref, spare_columns_ref = refs[:6]
    near_annot_ref, annot_ref, masks_ref, spare_mask_ref, own_rows_ref = refs[6:11]
    out_ref, send_ref, near_out_ref, flipped, scores, other = refs[11:]
    snps = annot_ref.shape[0]
    wide = snps // groups
    size = wide // 2
    tiles = snps // LANES
    me = lax.axis_index("hap")
    block = lax.axis_index("snp")
    last = reach_ref.shape[0] - 1
    reach_here = reach_ref[block]
    reach_there = jnp.where(
        me < groups // 2, reach_ref[jnp.minimum(block + 1, last)], reach_ref[jnp.maximum(block - 1, 0)]
    )

    scores[...] = own_ref[...]
    near_sums = sum((part[...] for part in near_parts[1:]), near_parts[0][...])
    near_counts = from_tiles(near_sums[0 : tiles * share, :], share)
    start = tiles * share
    rest = near_sums[start + size : start + size + size // 2, :]
    rest = jnp.concatenate([rest, pltpu.roll(rest, HALF_LANES, 1)], axis=0)
    spare_fields = from_fields(jnp.concatenate([near_sums[start : start + size, :], rest], axis=1))
    extras = from_fields(near_sums[start + size + size // 2 :, :])
    near_stats, near_lines, spare_stats = [], [], []
    for pop in range(2):
        count = extras[pop][0:1, :]
        totals = jnp.concatenate([extras[pop][3:4, :], extras[pop][4:5, :]], axis=1)
        spare_stats.append(column_stats(totals, jnp.concatenate([count, count], axis=1)))
        near_stats.append(column_stats(extras[pop][1:2, :], extras[pop][0:1, :]))
        near_lines += [*near_stats[pop], extras[pop][2:3, :]]
    near_table = jnp.concatenate(near_lines, axis=0).T[0:wide, :]

    slots = [near_counts[:, 0:LANES]]
    for slot in range(1, groups):
        slots.append(pltpu.roll(near_counts, snps - slot * wide, 1)[:, 0:LANES])
    flipped[:, 0:size] = slots[0].T
    slots.append(pltpu.roll(flipped[0:size, :], size, 1))
    near_fields = from_fields(jnp.concatenate(slots, axis=0))
    product = 1.0
    for pop in range(2):
        row_stats = [rows_ref[3 * pop + k] for k in range(3)]
        product *= correlation(row_stats, near_stats[pop], near_fields[pop])
    near_here = jnp.where(masks_ref[0] > 0.0, product, 0.0)
    near_there = jnp.where(masks_ref[1] > 0.0, product, 0.0)
    slice_rows = pl.ds(pl.multiple_of(me * wide, 8), wide)
    direct = dot_rounded(near_here, columns_ref[...], 1)
    turned = pltpu.roll(direct, HALF_LANES, 1)
    left_places, right_places = owner_places(groups, size)
    other[...] = jnp.zeros_like(other)
    for ref, values, places in ((scores, direct, left_places[:-1]), (other, turned, right_places)):
        for slot, place in enumerate(places):
            ref[pl.ds(pl.multiple_of(place, 8), size), :] += values[slot * size : (slot + 1) * size, :]
    product = 1.0
    for pop in range(2):
        row_stats = [spare_rows_ref[3 * pop + k] for k in range(3)]
        product *= correlation(row_stats, spare_stats[pop], spare_fields[pop])
    spare_here = jnp.where(spare_mask_ref[...] > 0.0, product, 0.0)
    lane = iota(spare_here.shape, 1)
    spare_here = [
        jnp.where((lane >= slot * size) & (lane < (slot + 1) * size), spare_here, 0.0)
        for slot in range(groups)
    ]
    direct = dot_rounded(jnp.concatenate(spare_here, axis=0), spare_columns_ref[...], 1)
    for slot, place in enumerate(spare_places(groups, size)[0]):
        scores[pl.ds(pl.multiple_of(place, 8), size), :] += direct[slot * size : (slot + 1) * size, :]
    near_scores = dot_rounded(near_there, own_rows_ref[...], 0)
    near_scores = jnp.where(
        iota((size, LANES), 1) < HALF_LANES, near_scores[0:size], near_scores[size:wide]
    )

    mine_table = mine_ref[...]
    far_product = 1.0
    for pop in range(2):
        own_row = [mine_table[:, 4 * pop + k : 4 * pop + k + 1] for k in range(3)]
        near_row = [near_table[:, 4 * pop + k : 4 * pop + k + 1] for k in range(4)]
        far_product *= correlation(own_row, near_row, near_row[3])
    scores[slice_rows, :] += near_annot_ref[slice_rows, :] * jnp.where(reach_here >= snps, far_product, 0.0)
    far_scores = annot_ref[slice_rows, :] * jnp.where(reach_there >= snps, far_product, 0.0)
    near_out_ref[...] = (near_scores + pack_halves(far_scores)).astype(near_out_ref.dtype)

    def packed(step):
        group = partner(me, step, groups)
        rows = pl.ds(pl.multiple_of(group * wide, 8), wide)
        return pack_halves(scores[rows, :] + other[rows, :])

    out_ref[...] = packed(0)
    send_ref[...] = packed(1).astype(send_ref.dtype)


def column_finish_kernel(*refs):
    *parts, out_ref = refs
    packed = sum(part[...].astype(jnp.float32) for part in parts)
    out_ref[...] = unpack_halves(packed).T[0 : out_ref.shape[0], :]


def sum_kernel(*refs):
    *parts, own_ref, there_ref = refs
    total = sum((part[...].astype(jnp.float32) for part in parts[1:]), parts[0][...])
    own_ref[...] = total
    half = there_ref.shape[0]
    left = iota((half, LANES), 1) < HALF_LANES
    second = total[half:]
    if second.shape[0] < half:
        second = jnp.concatenate([second, jnp.zeros((half - second.shape[0], LANES))], axis=0)
    there_ref[...] = jnp.where(left, pltpu.roll(total[0:half], HALF_LANES, 1), second)


def finish_kernel(own_ref, there_ref, out_ref):
    annots, rows = out_ref.shape
    there = there_ref[...]
    there = jnp.concatenate([there, pltpu.roll(there, HALF_LANES, 1)], axis=0)
    out_ref[...] = (own_ref[...] + there[0:rows]).T[0:annots, :]


def around(value, groups, step):
    return lax.ppermute(
        value, "hap", [(source, partner(source, step, groups)) for source in range(groups)]
    )


def swapped(value, first):
    pairs = []
    for block in range(first, lax.axis_size("snp") - 1, 2):
        pairs += [(block, block + 1), (block + 1, block)]
    return lax.ppermute(value, "snp", pairs)


def per_device(haplotypes, labels, annotations, reach):
    rows, snps = haplotypes.shape
    half = snps // 2
    groups = lax.axis_size("hap")
    blocks = lax.axis_size("snp")
    share = round_up(-(-half // groups), 16)
    folded_rows = share * groups
    out_share = snps // groups
    padded = half + folded_rows
    annot_part = 32
    bf16, f32, i32 = jnp.bfloat16, jnp.float32, jnp.int32
    shape = jax.ShapeDtypeStruct

    packed = shape((rows // 2 + annot_part, snps), bf16)
    haplotypes = pltpu.with_memory_space_constraint(haplotypes, pltpu.HBM)
    annots_in = pltpu.with_memory_space_constraint(annotations, pltpu.HBM)
    alleles, far, close = call(
        prepare_kernel,
        [shape((rows, snps), bf16), packed, packed],
        [HBM, HBM],
        [
            pltpu.VMEM((rows, snps), i32),
            pltpu.VMEM(annotations.shape, i32),
            pltpu.SemaphoreType.DMA((2 * len(CHUNKS) + 1,)),
        ],
        moved=rows * snps * 8,
    )(haplotypes, annots_in)
    from_far = swapped(far, 1)
    from_close = swapped(close, 0)

    by_column = groups == len(LEFT_BLOCKS)
    by_snp = shape((snps, LANES), f32)
    compact = shape((share * (snps // LANES) + 8, LANES), i32)
    own_share_counts = compact if by_column else shape((share, snps), i32)
    near_share_counts = shape((compact.shape[0] + share + share // 2, LANES), i32)
    tile = pltpu.VMEM((snps + 16, snps), f32)
    folded = pltpu.VMEM((folded_rows, snps), i32)
    weighted, totals, *own_parts = call(
        functools.partial(own_kernel, groups, share),
        [shape((snps + 16, rows), bf16), shape((8, snps), f32)] + [own_share_counts] * groups,
        [VMEM, VMEM],
        [tile, folded],
        flops=2 * rows * snps * snps,
        moved=rows * snps * 4,
    )(alleles, labels.reshape(1, rows))
    order = (2, 3, 1) if by_column else range(groups - 1, 0, -1)
    own_parts = [own_parts[0]] + [around(own_parts[k], groups, k) for k in range(groups - 1, 0, -1)]

    near_shapes = [own_share_counts] + [near_share_counts if by_column else shape((share + 8, snps), i32)] * groups
    if by_column:
        work = dict(flops=4 * rows * snps * LANES, moved=rows * snps * 4)
        flipped = pltpu.VMEM((snps, LANES), f32)
        pair_rows = (groups + 1) * (out_share // 2)
        side_shapes = [((2 * share, snps), i32), ((2 * (share + 8), 2 * LANES), i32), ((8, snps), f32)]
        *close_counts, own_annots, masks, spare_mask, own_rows = call(
            functools.partial(close_kernel, groups),
            [shape(*args) for args in side_shapes]
            + [
                by_snp,
                shape((2, pair_rows, LANES), f32),
                shape((share, 2 * LANES), f32),
                shape((pair_rows, LANES), bf16),
            ],
            [SMEM] + [VMEM] * 3,
            [tile, flipped],
            **work,
        )(reach, weighted, from_close, annotations)
        near_parts = call(
            functools.partial(far_kernel, groups, share),
            near_shapes[1:],
            [VMEM] * 6,
            [pltpu.VMEM(*args) for args in side_shapes]
            + [tile, flipped, pltpu.VMEM((8 * groups, LANES), i32)],
            **work,
        )(weighted, from_far, *close_counts, totals)
    else:
        own_sum, *near_parts = call(
            functools.partial(near_kernel, groups, share),
            near_shapes,
            [VMEM] * (4 + groups),
            [pltpu.VMEM((rows, snps), bf16), tile, folded],
            flops=2 * rows * snps * snps,
            moved=rows * snps * 4,
        )(weighted, from_far, from_close, totals, *own_parts)
    near_parts = [near_parts[0]] + [around(near_parts[k], groups, k) for k in order]

    if not by_column:
        own_annots, near_annots = call(annots_kernel, [by_snp, by_snp], [VMEM] * 3, moved=1 << 20)(
            annotations, from_far[rows // 2 :], from_close[rows // 2 :]
        )
    pairs = []
    for block in range(blocks):
        for group in range(groups):
            target = block + 1 if group < groups // 2 else block - 1
            if 0 <= target < blocks:
                pairs.append((block * groups + group, target * groups + group))

    def to_neighbour(value):
        return lax.ppermute(value, ("snp", "hap"), pairs)

    result = shape((annotations.shape[0], out_share), f32)
    half_share = round_up(-(-out_share // 2), 8)
    own_share = shape((out_share, LANES), f32)
    packed_share = shape((half_share, LANES), f32)
    if by_column:
        sent = shape((half_share, LANES), bf16)
        *prepared, second, third = call(
            functools.partial(own_score_kernel, groups, share),
            [
                by_snp,
                shape((out_share, LANES), f32),
                shape((6, pair_rows, LANES), f32),
                shape((LANES, LANES), bf16),
                shape((6, share, 2 * LANES), f32),
                shape((2 * LANES, LANES), bf16),
                by_snp,
                sent,
                sent,
            ],
            [SMEM] + [VMEM] * (groups + 3),
            [pltpu.VMEM((snps, LANES), f32)],
            flops=1 << 33,
            moved=1 << 20,
        )(reach, *own_parts, own_annots, from_far[rows // 2 :], from_close[rows // 2 :])
        parts = [around(third, groups, 3), around(second, groups, 2)]
        own_scores, send, there = call(
            functools.partial(near_score_kernel, groups, share),
            [packed_share, sent, sent],
            [SMEM] + [VMEM] * (groups + 11),
            [pltpu.VMEM((LANES, LANES), i32)] + [pltpu.VMEM((snps, LANES), f32)] * 2,
            flops=1 << 26,
            moved=1 << 21,
        )(reach, *near_parts, *prepared, own_annots, masks, spare_mask, own_rows)
        parts += [around(send, groups, 1), to_neighbour(there)]
        return call(column_finish_kernel, result, [VMEM] * 5)(own_scores, *parts)

    tall = pltpu.VMEM((padded, LANES), f32)
    scores = call(
        functools.partial(score_kernel, groups, share),
        [own_share] + [shape((out_share, LANES), bf16)] * (groups - 1),
        [SMEM] + [VMEM] * (groups + 3),
        [tall, tall, tall, tall],
        flops=1 << 26,
        moved=1 << 21,
    )(reach, own_sum, *near_parts, own_annots, near_annots)
    scores = [scores[0]] + [around(scores[k], groups, k) for k in range(groups - 1, 0, -1)]
    own_scores, near_scores = call(sum_kernel, [own_share, packed_share], [VMEM] * groups)(*scores)
    return call(finish_kernel, result, [VMEM] * 2)(own_scores, to_neighbour(near_scores))


def solution(mesh):
    in_specs = (
        P("hap", ("parts", "snp")),
        P(("parts", "hap")),
        P(None, ("parts", "snp")),
        P("parts"),
    )
    out_specs = P(None, ("parts", "snp", "hap"))
    return jax.shard_map(
        per_device, mesh=mesh, in_specs=in_specs, out_specs=out_specs, check_vma=False
    )
```

```python
import functools

import jax
import jax.numpy as jnp
from jax import lax
from jax.experimental import pallas as pl
from jax.experimental.pallas import tpu as pltpu
from jax.sharding import PartitionSpec as P

VARIANCE_FLOOR = 0.01
BASE_BITS = 12
BASE = 1 << BASE_BITS
FIELD_BITS = 16
LANES = 128
HALF_LANES = LANES // 2
CHUNKS = (8, 5, 3)
VMEM = pl.BlockSpec(memory_space=pltpu.VMEM)
SMEM = pl.BlockSpec(memory_space=pltpu.SMEM)
HBM = pl.BlockSpec(memory_space=pltpu.HBM)
VMEM_LIMIT = 24 * 1024 * 1024


def iota(shape, axis):
    return lax.broadcasted_iota(jnp.int32, shape, axis)


def round_up(value, step):
    return -(-value // step) * step


def to_fields(values):
    whole = values.astype(jnp.int32)
    return whole + (whole >> BASE_BITS) * ((1 << FIELD_BITS) - BASE)


def from_fields(packed):
    first = packed & ((1 << FIELD_BITS) - 1)
    second = lax.shift_right_logical(packed, FIELD_BITS)
    return first.astype(jnp.float32), second.astype(jnp.float32)


def call(kernel, out_shape, in_specs, scratch_shapes=(), flops=0, moved=0):
    several = isinstance(out_shape, (list, tuple))
    return pl.pallas_call(
        kernel,
        out_shape=out_shape,
        in_specs=in_specs,
        out_specs=[VMEM] * len(out_shape) if several else VMEM,
        scratch_shapes=list(scratch_shapes),
        compiler_params=pltpu.CompilerParams(vmem_limit_bytes=VMEM_LIMIT),
        cost_estimate=pl.CostEstimate(flops=flops, bytes_accessed=moved, transcendentals=0),
    )


def odd_block():
    return lax.rem(lax.axis_index("snp"), 2) == 1


def store_packed(up_ref, down_ref, where, first, second):
    left = iota((first.shape[0], LANES), 1) < HALF_LANES
    middle = first[:, LANES : 2 * LANES]
    turned = pltpu.roll(second[:, LANES : 2 * LANES], HALF_LANES, 1)
    for ref, side, mixed in (
        (up_ref, slice(0, LANES), jnp.where(left, middle, turned)),
        (down_ref, slice(2 * LANES, 3 * LANES), jnp.where(left, turned, middle)),
    ):
        ref[where, 0:LANES] = first[:, side].astype(jnp.bfloat16)
        ref[where, LANES : 2 * LANES] = mixed.astype(jnp.bfloat16)
        ref[where, 2 * LANES : 3 * LANES] = second[:, side].astype(jnp.bfloat16)


def load_packed(up, down):
    left = iota((up.shape[0], LANES), 1) < HALF_LANES
    up_mixed, down_mixed = up[:, LANES : 2 * LANES], down[:, LANES : 2 * LANES]
    first = jnp.where(left, up_mixed, down_mixed)
    second = jnp.where(left, down_mixed, up_mixed)
    second = pltpu.roll(second.astype(jnp.float32), HALF_LANES, 1).astype(second.dtype)
    return (
        (up[:, :LANES], first, down[:, :LANES]),
        (up[:, 2 * LANES :], second, down[:, 2 * LANES :]),
    )


def prepare_kernel(hap_ref, annot_ref, alleles_ref, far_ref, close_ref, held, held_annots, sems):
    rows = hap_ref.shape[0]
    annot_rows = annot_ref.shape[0]
    sizes = [chunk * (rows // 32) for chunk in CHUNKS]
    places = [sum(sizes[:number]) for number in range(len(sizes))]
    pieces = [
        (side * (rows // 2) + place, size) for place, size in zip(places, sizes) for side in range(2)
    ]
    copies = [
        pltpu.make_async_copy(
            hap_ref.at[pl.ds(start, size)], held.at[pl.ds(start, size)], sems.at[number]
        )
        for number, (start, size) in enumerate(pieces)
    ]
    copies.append(pltpu.make_async_copy(annot_ref, held_annots, sems.at[len(pieces)]))
    for copy in copies:
        copy.start()
    part = far_ref.shape[0] - rows // 2
    odd = odd_block()

    def store(where, first, second):
        @pl.when(odd)
        def _():
            store_packed(close_ref, far_ref, where, first, second)

        @pl.when(jnp.logical_not(odd))
        def _():
            store_packed(far_ref, close_ref, where, first, second)

    for chunk, (place, size) in enumerate(zip(places, sizes)):
        pair = []
        for number in (2 * chunk, 2 * chunk + 1):
            copies[number].wait()
            where = slice(pieces[number][0], pieces[number][0] + size)
            values = held[where, :].astype(jnp.float32)
            alleles_ref[where, :] = values.astype(jnp.bfloat16)
            pair.append(values)
        store(slice(place, place + size), *pair)
    copies[-1].wait()
    annots = jnp.concatenate(
        [
            held_annots[...].astype(jnp.float32),
            jnp.zeros((2 * part - annot_rows, annot_ref.shape[1]), jnp.float32),
        ],
        axis=0,
    )
    store(slice(rows // 2, rows // 2 + part), annots[:part], annots[part:])


def partner(group, step, groups):
    if groups & (groups - 1) == 0:
        return group ^ step
    return (group + step) % groups


def send_shares(groups, source, share, targets):
    me = lax.axis_index("hap")
    for step, target in enumerate(targets):
        group = partner(me, step, groups)
        rows = source[pl.ds(pl.multiple_of(group * share, 8), share), :]
        target[0:share, :] = rows.astype(target.dtype)


def send_tiles(groups, source, share, targets):
    me = lax.axis_index("hap")
    for step, target in enumerate(targets):
        owner = partner(me, step, groups)
        counts = source[pl.ds(pl.multiple_of(owner * share, 8), share), :]
        for k in range(source.shape[1] // LANES):
            target[k * share : (k + 1) * share, :] = counts[:, k * LANES : (k + 1) * LANES]


def from_tiles(counts, share):
    tiles = counts.shape[0] // share
    return jnp.concatenate([counts[k * share : (k + 1) * share, :] for k in range(tiles)], axis=1)


def own_kernel(groups, share, alleles_ref, label_ref, *refs):
    weighted_ref, totals_ref, *targets = refs[: 2 + groups]
    tile, folded = refs[2 + groups :]
    rows, snps = alleles_ref.shape
    half = snps // 2
    weight = jnp.where(label_ref[...] > 0, float(BASE), 1.0)
    weighted_ref[0:snps, :] = alleles_ref[...].T * weight.astype(jnp.bfloat16)
    extra = weighted_ref.shape[0] - snps
    weighted_ref[snps:, :] = jnp.broadcast_to(weight, (extra, rows)).astype(jnp.bfloat16)
    tile[...] = jnp.dot(weighted_ref[...], alleles_ref[...], preferred_element_type=jnp.float32)
    count = jnp.sum(weight, axis=1, keepdims=True)
    totals_ref[...] = jnp.concatenate(
        [tile[snps : snps + 1, :], jnp.broadcast_to(count, (1, snps)), jnp.zeros((6, snps))], axis=0
    )
    row, col = iota((half, snps), 0), iota((half, snps), 1)
    moved = (col < half) | (col - half > row)
    turned = pltpu.roll(tile[0:half, :], half, 1)
    folded[0:half, :] = to_fields(jnp.where(moved, turned, tile[half:snps, :]))
    if folded.shape[0] > half:
        folded[half:, :] = jnp.zeros((folded.shape[0] - half, snps), jnp.int32)
    if groups != len(LEFT_BLOCKS):
        send_shares(groups, folded, share, targets)
        return
    tiles = snps // LANES
    shared = [totals_ref[0:1, k * LANES : (k + 1) * LANES] for k in range(tiles)]
    shared += [totals_ref[1:2, 0:LANES], jnp.zeros((7 - tiles, LANES))]
    extras = to_fields(jnp.concatenate(shared, axis=0))
    send_tiles(groups, folded, share, targets)
    for target in targets:
        target[tiles * share :, :] = extras


LEFT_BLOCKS = ((0, 1, 2, 3), (2, 3, 6, 7), (4, 0, 1, 2), (6, 0, 4, 5))
RIGHT_BLOCKS = ((2, 3, 6, 7), (4, 5, 6, 7), (0, 1, 2, 4), (0, 4, 5, 6))


SPARE_OWN = ((0, 0, 0, 0), (1, 1, 2, 2), (4, 5, 6, 7), (6, 6, 7, 7))
SPARE_NEAR = ((4, 5, 6, 7), (4, 5, 4, 5), (3, 3, 3, 3), (1, 2, 1, 2))


def fold_spare(tile, spare, first):
    owners = len(SPARE_OWN)
    snps = tile.shape[1]
    size = snps // (2 * owners)
    count = spare.shape[0] // 2
    totals = tile[snps : snps + count - size, :]
    lane = iota((count, snps), 1)
    for number, owner in enumerate(range(first, first + 2)):
        mixed = None
        for slot in range(owners):
            own, near = SPARE_OWN[owner][slot], SPARE_NEAR[owner][slot]
            before = (SPARE_OWN[owner][slot - 1], SPARE_NEAR[owner][slot - 1] + 1) if slot else None
            if before == (own, near):
                continue
            values = jnp.concatenate([tile[own * size : (own + 1) * size, :], totals], axis=0)
            shift = (slot - near) * size % snps
            values = pltpu.roll(values, shift, 1) if shift else values
            mixed = values if mixed is None else jnp.where(lane >= slot * size, values, mixed)
        spare[number * count : (number + 1) * count, :] = to_fields(mixed[:, 0 : spare.shape[1]])


def fold_by_column(tile, flipped, folded, first):
    groups = len(LEFT_BLOCKS)
    owners = range(first, first + groups // 2)
    snps = folded.shape[1]
    wide = snps // groups
    size = wide // 2
    shape = (size, snps)
    row, lane = iota(shape, 0), iota(shape, 1)

    def block(number):
        return tile[number * size : (number + 1) * size, :]

    diagonal, within = block(2 * first), lane - 2 * first * size
    for number in range(2 * first + 1, 2 * first + groups):
        diagonal = jnp.where(lane >= number * size, block(number), diagonal)
        within = jnp.where(lane >= number * size, lane - number * size, within)
    apart = jnp.sum(jnp.where(row == within, diagonal, 0.0), axis=0, keepdims=True)
    flipped[:, 0:size] = diagonal.T
    corner = diagonal
    for owner in owners:
        start = (2 * owner + 1) * size
        turned = jnp.concatenate(
            [flipped[start : start + size, :], jnp.zeros((size, snps - LANES), jnp.float32)], axis=1
        )
        if owner:
            turned = pltpu.roll(turned, owner * wide, 1)
        inside = lane - owner * wide
        other = (row <= inside) if first == 0 else (row >= inside)
        corner = jnp.where((inside >= 0) & (inside < size) & other, turned, corner)
    rolled = []
    for shift in range(groups):
        mixed = None
        for owner in owners:
            slot = (owner + shift) % groups
            left = block(LEFT_BLOCKS[owner][slot]) if slot else corner
            start = owner * wide
            mixed = left if mixed is None else jnp.where(lane >= start, left, mixed)
            mixed = jnp.where(lane >= start + size, block(RIGHT_BLOCKS[owner][slot]), mixed)
        rolled.append(pltpu.roll(mixed, shift * wide, 1) if shift else mixed)
    for number, owner in enumerate(owners):
        mixed = rolled[(0 - owner) % groups]
        for slot in range(1, groups):
            mixed = jnp.where(lane >= slot * wide, rolled[(slot - owner) % groups], mixed)
        folded[number * size : (number + 1) * size, :] = to_fields(mixed)
    return apart


def above(far):
    return odd_block() == far


def side_dot(weighted_ref, side_ref):
    rows = weighted_ref.shape[1]
    half = rows // 2

    def dot(which, columns):
        return jnp.dot(
            weighted_ref[:, which], side_ref[0:half, columns], preferred_element_type=jnp.float32
        )

    first = dot(slice(0, half), slice(0, 2 * LANES))
    second = dot(slice(half, rows), slice(LANES, 3 * LANES))
    whole = first[:, 0:LANES] + second[:, LANES:]
    return whole, first[:, LANES:] + pltpu.roll(second[:, 0:LANES], HALF_LANES, 1)


def fold_side(far, weighted_ref, side_ref, main, spare, lines, tile, flipped):
    snps = tile.shape[1]
    whole, shared = side_dot(weighted_ref, side_ref)
    tile[:, LANES : 2 * LANES] = shared

    def fold(first, start):
        tile[:, start : start + LANES] = whole
        apart = fold_by_column(tile, flipped, main, first)
        fold_spare(tile, spare, 2 - first)
        lines[0:1, :] = tile[snps : snps + 1, :]
        lines[1:2, :] = apart

    @pl.when(above(far))
    def _():
        fold(0, 0)

    @pl.when(jnp.logical_not(above(far)))
    def _():
        fold(2, 2 * LANES)


def close_kernel(groups, reach_ref, weighted_ref, side_ref, annot_ref, *refs):
    main_ref, spare_ref, lines_ref, annots, masks_ref, spare_mask_ref, own_rows_ref, tile, flipped = refs
    fold_side(False, weighted_ref, side_ref, main_ref, spare_ref, lines_ref, tile, flipped)
    snps = annot_ref.shape[1]
    half, wide = snps // 2, snps // groups
    size = wide // 2
    own = annot_ref[...].astype(jnp.float32)
    own = jnp.concatenate([own, jnp.zeros((LANES - own.shape[0], snps), jnp.float32)], axis=0)
    annots[...] = own.T

    me = lax.axis_index("hap")
    block = lax.axis_index("snp")
    last = reach_ref.shape[0] - 1
    upper = me < groups // 2
    reach_here = reach_ref[block]
    reach_there = jnp.where(
        upper, reach_ref[jnp.minimum(block + 1, last)], reach_ref[jnp.maximum(block - 1, 0)]
    )
    left_places, right_places = owner_places(groups, size)
    local, lane = iota((size, LANES), 0), iota((size, LANES), 1)
    own_row = jnp.concatenate(
        [local + jnp.where(lane < size, a, b) for a, b in zip(left_places, right_places)], axis=0
    )
    shape = own_row.shape
    lane = iota(shape, 1)
    apart = jnp.abs(own_row - (lane + me * wide))
    ahead = (own_row - (lane + me * wide)) * jnp.where(upper, 1, -1) > 0
    real = ahead & (lane < wide) & ((lane >= size) | (iota(shape, 0) < groups * size))
    inside = (own_row - half) * jnp.where(upper, 1, -1) < jnp.where(upper, 0, 1)
    masks_ref[0] = jnp.where(real & inside & (snps - apart <= reach_here), 1.0, 0.0)
    masks_ref[1] = jnp.where(real & (snps - apart <= reach_there), 1.0, 0.0)
    own_rows = rows_at(annots, left_places, size) + pltpu.roll(
        rows_at(annots, right_places, size), HALF_LANES, 1
    )
    own_rows_ref[...] = own_rows.astype(jnp.bfloat16)

    own_places, near_places = spare_places(groups, size)
    shape = spare_mask_ref.shape
    local, lane = iota(shape, 0), iota(shape, 1)
    own_row = by_slot([local + place for place in own_places], lane, size)
    near_col = by_slot(
        [lane + (place - slot * size) for slot, place in enumerate(near_places)], lane, size
    )
    close = snps - jnp.abs(own_row - near_col) <= reach_here
    spare_mask_ref[...] = jnp.where(close & (lane < groups * size), 1.0, 0.0)


def by_slot(values, lane, size):
    mixed = values[0]
    for slot in range(1, len(values)):
        mixed = jnp.where(lane >= slot * size, values[slot], mixed)
    return mixed


def far_kernel(groups, share, weighted_ref, side_ref, close_ref, close_spare_ref, close_lines_ref, totals_ref, *refs):
    targets, (main, spare, lines, tile, flipped, extras) = refs[:groups], refs[groups:]
    fold_side(True, weighted_ref, side_ref, main, spare, lines, tile, flipped)
    snps = tile.shape[1]
    half, size = snps // 2, share
    odd = odd_block()

    tiles = snps // LANES
    count = spare.shape[0] // 2
    from_far = (iota((8, snps), 1) < half) == odd
    by_column = jnp.concatenate(
        [totals_ref[1:2, :], jnp.where(from_far, lines[...], close_lines_ref[...])[0:2, :]], axis=0
    )
    by_column = jnp.concatenate([by_column, jnp.zeros((5, snps))], axis=0)
    for owner in range(groups):
        start = owner * (snps // groups)
        columns = pltpu.roll(by_column, snps - start, 1) if owner else by_column
        where = slice((owner & 1) * count + size, (owner & 1) * count + size + 1)
        second = odd if owner >= groups // 2 else jnp.logical_not(odd)
        spare_totals = jnp.where(second, spare[where, :], close_spare_ref[where, :])
        extras[8 * owner : 8 * (owner + 1), :] = jnp.concatenate(
            [
                to_fields(columns[0:3, 0:LANES]),
                spare_totals[:, 0:LANES],
                spare_totals[:, LANES:],
                jnp.zeros((3, LANES), jnp.int32),
            ],
            axis=0,
        )
    me = lax.axis_index("hap")
    left = iota((size // 2, LANES), 1) < HALF_LANES
    for step, target in enumerate(targets):
        owner = partner(me, step, groups)
        first = (owner < groups // 2) == odd
        where = pl.ds(pl.multiple_of((owner & 1) * size, 8), size)
        counts = jnp.where(first, main[where, :], close_ref[where, :])
        for k in range(tiles):
            target[k * size : (k + 1) * size, :] = counts[:, k * LANES : (k + 1) * LANES]
        where = pl.ds(pl.multiple_of((owner & 1) * count, 8), size)
        counts = jnp.where(first, close_spare_ref[where, :], spare[where, :])
        start = tiles * size
        target[start : start + size, :] = counts[:, 0:LANES]
        rest = counts[:, LANES:]
        target[start + size : start + size + size // 2, :] = jnp.where(
            left, rest[0 : size // 2], pltpu.roll(rest[size // 2 :], HALF_LANES, 1)
        )
        target[start + size + size // 2 :, :] = extras[pl.ds(pl.multiple_of(owner * 8, 8), 8), :]


def near_kernel(groups, share, weighted_ref, far_ref, close_ref, totals_ref, *refs):
    own_parts, own_sum_ref = refs[:groups], refs[groups]
    targets, (near, tile, folded) = refs[groups + 1 : 2 * groups + 1], refs[2 * groups + 1 :]
    rows, snps = near.shape
    half = snps // 2
    odd = odd_block()

    def unpack(up_ref, down_ref):
        pieces = load_packed(up_ref[0 : rows // 2, :], down_ref[0 : rows // 2, :])
        for side in range(2):
            where = slice(side * (rows // 2), (side + 1) * (rows // 2))
            for number in range(3):
                near[where, number * LANES : (number + 1) * LANES] = pieces[side][number]

    @pl.when(odd)
    def _():
        unpack(far_ref, close_ref)

    @pl.when(jnp.logical_not(odd))
    def _():
        unpack(close_ref, far_ref)

    tile[...] = jnp.dot(weighted_ref[...], near[...], preferred_element_type=jnp.float32)
    row, col = iota((half, snps), 0), iota((half, snps), 1)
    moved = (col >= half) & (col - half < row)
    turned = pltpu.roll(tile[0:half, :], half, 1)
    folded[0:half, :] = to_fields(jnp.where(moved, turned, tile[half:snps, :]))
    if folded.shape[0] > half:
        folded[half:, :] = jnp.zeros((folded.shape[0] - half, snps), jnp.int32)
    square = (snps, snps)
    far = jnp.sum(
        jnp.where(iota(square, 0) == iota(square, 1), tile[0:snps, :], 0.0), axis=0, keepdims=True
    )
    extras = to_fields(
        jnp.concatenate(
            [totals_ref[0:2, :], tile[snps : snps + 1, :], far, jnp.zeros((4, snps))], axis=0
        )
    )
    send_shares(groups, folded, share, targets)
    for target in targets:
        target[share:, :] = extras
    own_sum_ref[...] = sum((part[...] for part in own_parts[1:]), own_parts[0][...])


def annots_kernel(annot_ref, far_ref, close_ref, own_ref, near_ref):
    snps = annot_ref.shape[1]
    own = annot_ref[...].astype(jnp.float32)
    own = jnp.concatenate([own, jnp.zeros((LANES - own.shape[0], snps), jnp.float32)], axis=0)
    own_ref[...] = own.T
    near_ref[...] = near_annots_by_snp(far_ref, close_ref)


def near_annots_by_snp(far_ref, close_ref):
    part, snps = far_ref.shape
    wide = 2 * part
    odd = odd_block()
    far, close = far_ref[...].astype(jnp.float32), close_ref[...].astype(jnp.float32)
    first, second = load_packed(jnp.where(odd, far, close), jnp.where(odd, close, far))
    near = jnp.concatenate(
        [
            jnp.concatenate([piece.astype(jnp.float32) for piece in first], axis=1),
            jnp.concatenate([piece.astype(jnp.float32) for piece in second], axis=1),
            jnp.zeros((LANES - wide, snps), jnp.float32),
        ],
        axis=0,
    )
    return near.T


def column_stats(totals, count):
    size = jnp.maximum(count, 1.0)
    frequency = totals / size
    variance = jnp.maximum(frequency * (1.0 - frequency), VARIANCE_FLOOR)
    inverse = 1.0 / jnp.sqrt(size * variance)
    low = ((0.0 - frequency) * inverse).astype(jnp.bfloat16).astype(jnp.float32)
    high = ((1.0 - frequency) * inverse).astype(jnp.bfloat16).astype(jnp.float32)
    step = high - low
    root = 1.0 / jnp.sqrt(size)
    return step, step * totals * root, (low * count + step * totals) * root


def correlation(row, col, count):
    return row[0] * col[0] * count - row[1] * col[1] + row[2] * col[2]


def split(values):
    high = values.astype(jnp.bfloat16)
    return high, (values - high.astype(jnp.float32)).astype(jnp.bfloat16)


def dot_split(values, right, axis):
    dims = (((axis,), (0,)), ((), ()))
    return sum(
        lax.dot_general(part, right, dims, preferred_element_type=jnp.float32)
        for part in split(values)
    )


def score_kernel(groups, share, reach_ref, *refs):
    own_sum_ref, near_parts = refs[0], refs[1 : groups + 1]
    annot_ref, near_annot_ref = refs[groups + 1 : groups + 3]
    targets = refs[groups + 3 : 2 * groups + 3]
    table, annots, near_annots, scores = refs[2 * groups + 3 :]
    snps = annot_ref.shape[0]
    half = snps // 2
    out_share = snps // groups
    me = lax.axis_index("hap")
    block = lax.axis_index("snp")
    last = reach_ref.shape[0] - 1
    reach_here = reach_ref[block]
    reach_up = reach_ref[jnp.minimum(block + 1, last)]
    reach_down = reach_ref[jnp.maximum(block - 1, 0)]

    own_counts = own_sum_ref[...]
    near_sums = sum((part[...] for part in near_parts[1:]), near_parts[0][...])
    extras = from_fields(near_sums[share:, :])
    near_counts = near_sums[0:share, :]

    own_stats, near_stats, lines = [], [], []
    for pop in range(2):
        count = extras[pop][1:2, :]
        own_stats.append(column_stats(extras[pop][0:1, :], count))
        near_stats.append(column_stats(extras[pop][2:3, :], count))
        lines += [*own_stats[pop], *near_stats[pop], extras[pop][0:1, :], extras[pop][3:4, :]]
    by_row = jnp.concatenate(lines, axis=0).T
    table[0:snps, 0:16] = by_row
    if table.shape[0] > snps:
        table[snps:, 0:16] = jnp.zeros((table.shape[0] - snps, 16), jnp.float32)
    annots[0:snps, :] = annot_ref[...]
    near_annots[0:snps, :] = near_annot_ref[...]
    if annots.shape[0] > snps:
        annots[snps:, :] = jnp.zeros((annots.shape[0] - snps, LANES), jnp.float32)

    low_rows = pl.multiple_of(me * share, 8)
    high_rows = pl.multiple_of(half + me * share, 8)

    def both(ref):
        return jnp.concatenate([ref[pl.ds(low_rows, share), :], ref[pl.ds(high_rows, share), :]], axis=0)

    here = both(table)
    own_count = jnp.concatenate([pltpu.roll(own_counts, half, 1), own_counts], axis=0)
    near_count = jnp.concatenate([pltpu.roll(near_counts, half, 1), near_counts], axis=0)
    shape = (2 * share, snps)
    local, col = iota(shape, 0), iota(shape, 1)
    low = local < share
    place = jnp.where(low, local, local - share) + me * share
    row = jnp.where(low, place, place + half)
    own_fields, near_fields = from_fields(own_count), from_fields(near_count)
    own_product, near_product = 1.0, 1.0
    for pop in range(2):
        row_stats = [here[:, 8 * pop + k : 8 * pop + k + 1] for k in range(3)]
        own_product *= correlation(row_stats, own_stats[pop], own_fields[pop])
        near_product *= correlation(row_stats, near_stats[pop], near_fields[pop])
    real = place < half
    own_inside = real & ((low & (col > row)) | (~low & (col >= half) & (col < row)))
    own_inside &= jnp.abs(col - row) <= reach_here
    own_kept = jnp.where(own_inside, own_product, 0.0)
    in_upper = col < half
    near_inside = real & ((low & (col < row)) | (~low & (in_upper | (col > row))))
    distance = jnp.where(in_upper, snps + col - row, snps + row - col)
    near_here = jnp.where(near_inside & (distance <= reach_here), near_product, 0.0)
    reach_there = jnp.where(in_upper, reach_up, reach_down)
    near_there = jnp.where(near_inside & (distance <= reach_there), near_product, 0.0)

    rows_here = both(annots)
    rows_there = pltpu.roll(rows_here, HALF_LANES, 1)
    scores[0:snps, :] = dot_split(
        jnp.concatenate([own_kept, near_there], axis=0),
        jnp.concatenate([rows_here, rows_there], axis=0).astype(jnp.bfloat16),
        0,
    )
    direct = dot_split(
        jnp.concatenate([own_kept, near_here], axis=1),
        jnp.concatenate([annot_ref[...], near_annot_ref[...]], axis=0).astype(jnp.bfloat16),
        1,
    )
    scores[pl.ds(low_rows, share), :] += direct[0:share, :]
    scores[pl.ds(high_rows, share), :] += direct[share:, :]

    out_rows = pl.ds(pl.multiple_of(me * out_share, 8), out_share)
    mine = table[out_rows, :]
    self_product, far_product = 1.0, 1.0
    for pop in range(2):
        k = 8 * pop
        own_row = [mine[:, k + s : k + s + 1] for s in range(3)]
        near_row = [mine[:, k + 3 + s : k + 4 + s] for s in range(3)]
        self_product *= correlation(own_row, own_row, mine[:, k + 6 : k + 7])
        far_product *= correlation(own_row, near_row, mine[:, k + 7 : k + 8])
    mine_annots = annots[out_rows, :]
    far_reach = jnp.where(me < groups // 2, reach_up, reach_down)
    scores[out_rows, :] += (
        mine_annots * self_product
        + near_annots[out_rows, :] * jnp.where(reach_here >= snps, far_product, 0.0)
        + pltpu.roll(mine_annots, HALF_LANES, 1) * jnp.where(far_reach >= snps, far_product, 0.0)
    )
    send_shares(groups, scores, out_share, targets)


def pack_halves(values):
    half = values.shape[0] // 2
    left = iota((half, LANES), 1) < HALF_LANES
    return jnp.where(left, values[0:half], pltpu.roll(values[half:], HALF_LANES, 1))


def unpack_halves(packed):
    return jnp.concatenate([packed, pltpu.roll(packed, HALF_LANES, 1)], axis=0)


def dot_rounded(values, right, axis):
    dims = (((axis,), (0,)), ((), ()))
    return lax.dot_general(
        values.astype(jnp.bfloat16), right, dims, preferred_element_type=jnp.float32
    )


def owner_places(groups, size):
    me = lax.axis_index("hap")

    def mine(blocks, slot):
        value = blocks[0][slot]
        for group in range(1, groups):
            value = jnp.where(me == group, blocks[group][slot], value)
        return value * size

    left = [mine(LEFT_BLOCKS, slot) for slot in range(groups)]
    right = [mine(RIGHT_BLOCKS, slot) for slot in range(groups)]
    return left + left[0:1], right + [(2 * me + 1) * size]


def spare_places(groups, size):
    me = lax.axis_index("hap")

    def mine(blocks, slot):
        value = blocks[0][slot]
        for group in range(1, groups):
            value = jnp.where(me == group, blocks[group][slot], value)
        return value * size

    return [[mine(blocks, slot) for slot in range(groups)] for blocks in (SPARE_OWN, SPARE_NEAR)]


def rows_at(ref, places, size):
    return jnp.concatenate([ref[pl.ds(pl.multiple_of(place, 8), size), :] for place in places], axis=0)


def own_score_kernel(
    groups, share, reach_ref, *refs
):
    own_parts, refs = refs[:groups], refs[groups:]
    annot_ref, far_ref, close_ref, scores, mine_ref, rows_ref, columns_ref, *refs = refs
    spare_rows_ref, spare_columns_ref, near_annot_ref, *targets, table = refs
    near_annot_ref[...] = near_annots_by_snp(far_ref, close_ref)
    snps = annot_ref.shape[0]
    half = snps // 2
    wide = snps // groups
    tiles = snps // LANES
    me = lax.axis_index("hap")
    reach_here = reach_ref[lax.axis_index("snp")]
    own_sums = sum((part[...] for part in own_parts[1:]), own_parts[0][...])
    own_counts = from_tiles(own_sums[0 : tiles * share, :], share)
    extras = from_fields(own_sums[tiles * share :, :])

    own_stats, lines = [], []
    for pop in range(2):
        count = jnp.concatenate([extras[pop][tiles : tiles + 1, :]] * tiles, axis=1)
        totals = jnp.concatenate([extras[pop][k : k + 1, :] for k in range(tiles)], axis=1)
        own_stats.append(column_stats(totals, count))
        lines += [*own_stats[pop], totals]
    table[:, 0:8] = jnp.concatenate(lines, axis=0).T

    low_rows = pl.multiple_of(me * share, 8)
    high_rows = pl.multiple_of(half + me * share, 8)

    def both(ref):
        return jnp.concatenate([ref[pl.ds(low_rows, share), :], ref[pl.ds(high_rows, share), :]], axis=0)

    here = both(table)
    own_fields = from_fields(
        jnp.concatenate([pltpu.roll(own_counts, half, 1), own_counts], axis=0)
    )
    shape = (2 * share, snps)
    local, col = iota(shape, 0), iota(shape, 1)
    low = local < share
    row = jnp.where(low, local, local + half - share) + me * share
    product = 1.0
    for pop in range(2):
        row_stats = [here[:, 4 * pop + k : 4 * pop + k + 1] for k in range(3)]
        product *= correlation(row_stats, own_stats[pop], own_fields[pop])
    inside = (low & (col > row)) | (~low & (col >= half) & (col < row))
    own_kept = jnp.where(inside & (jnp.abs(col - row) <= reach_here), product, 0.0)
    rows_here = both(annot_ref).astype(jnp.bfloat16)
    scores[...] = dot_rounded(own_kept, rows_here, 0)
    direct = dot_rounded(own_kept, annot_ref[...].astype(jnp.bfloat16), 1)
    scores[pl.ds(low_rows, share), :] += direct[0:share, :]
    scores[pl.ds(high_rows, share), :] += direct[share:, :]

    slice_rows = pl.ds(pl.multiple_of(me * wide, 8), wide)
    mine = table[slice_rows, :]
    mine_ref[...] = mine
    product = 1.0
    for pop in range(2):
        own_row = [mine[:, 4 * pop + k : 4 * pop + k + 1] for k in range(4)]
        product *= correlation(own_row, own_row, own_row[3])
    scores[slice_rows, :] += annot_ref[slice_rows, :] * product
    for step, target in enumerate(targets, 2):
        group = partner(me, step, groups)
        rows = scores[pl.ds(pl.multiple_of(group * wide, 8), wide), :]
        target[...] = pack_halves(rows).astype(target.dtype)

    size = wide // 2
    left_places, right_places = owner_places(groups, size)
    left_table, right_table = rows_at(table, left_places, size), rows_at(table, right_places, size)
    is_left = iota(rows_ref.shape[1:], 1) < size
    for pop in range(2):
        for k in range(3):
            column = slice(4 * pop + k, 4 * pop + k + 1)
            rows_ref[3 * pop + k] = jnp.where(is_left, left_table[:, column], right_table[:, column])
    theirs = near_annot_ref[slice_rows, :]
    columns = [theirs[0:size], pltpu.roll(theirs[size:], HALF_LANES, 1), jnp.zeros((LANES - wide, LANES))]
    columns_ref[...] = jnp.concatenate(columns, axis=0).astype(jnp.bfloat16)

    own_places, near_places = spare_places(groups, size)
    shape = spare_rows_ref.shape[1:]
    lane = iota(shape, 1)
    tables = [table[pl.ds(pl.multiple_of(place, 8), size), :] for place in own_places]
    for pop in range(2):
        for k in range(3):
            column = slice(4 * pop + k, 4 * pop + k + 1)
            spare_rows_ref[3 * pop + k] = by_slot(
                [jnp.broadcast_to(values[:, column], shape) for values in tables], lane, size
            )
    columns = [rows_at(near_annot_ref, near_places, size)]
    columns.append(jnp.zeros((shape[1] - groups * size, LANES), jnp.float32))
    spare_columns_ref[...] = jnp.concatenate(columns, axis=0).astype(jnp.bfloat16)


def near_score_kernel(groups, share, reach_ref, *refs):
    near_parts, refs = refs[:groups], refs[groups:]
    own_ref, mine_ref, rows_ref, columns_ref, spare_rows_ref, spare_columns_ref = refs[:6]
    near_annot_ref, annot_ref, masks_ref, spare_mask_ref, own_rows_ref = refs[6:11]
    out_ref, send_ref, near_out_ref, flipped, scores, other = refs[11:]
    snps = annot_ref.shape[0]
    wide = snps // groups
    size = wide // 2
    tiles = snps // LANES
    me = lax.axis_index("hap")
    block = lax.axis_index("snp")
    last = reach_ref.shape[0] - 1
    reach_here = reach_ref[block]
    reach_there = jnp.where(
        me < groups // 2, reach_ref[jnp.minimum(block + 1, last)], reach_ref[jnp.maximum(block - 1, 0)]
    )

    scores[...] = own_ref[...]
    near_sums = sum((part[...] for part in near_parts[1:]), near_parts[0][...])
    near_counts = from_tiles(near_sums[0 : tiles * share, :], share)
    start = tiles * share
    rest = near_sums[start + size : start + size + size // 2, :]
    rest = jnp.concatenate([rest, pltpu.roll(rest, HALF_LANES, 1)], axis=0)
    spare_fields = from_fields(jnp.concatenate([near_sums[start : start + size, :], rest], axis=1))
    extras = from_fields(near_sums[start + size + size // 2 :, :])
    near_stats, near_lines, spare_stats = [], [], []
    for pop in range(2):
        count = extras[pop][0:1, :]
        totals = jnp.concatenate([extras[pop][3:4, :], extras[pop][4:5, :]], axis=1)
        spare_stats.append(column_stats(totals, jnp.concatenate([count, count], axis=1)))
        near_stats.append(column_stats(extras[pop][1:2, :], extras[pop][0:1, :]))
        near_lines += [*near_stats[pop], extras[pop][2:3, :]]
    near_table = jnp.concatenate(near_lines, axis=0).T[0:wide, :]

    slots = [near_counts[:, 0:LANES]]
    for slot in range(1, groups):
        slots.append(pltpu.roll(near_counts, snps - slot * wide, 1)[:, 0:LANES])
    flipped[:, 0:size] = slots[0].T
    slots.append(pltpu.roll(flipped[0:size, :], size, 1))
    near_fields = from_fields(jnp.concatenate(slots, axis=0))
    product = 1.0
    for pop in range(2):
        row_stats = [rows_ref[3 * pop + k] for k in range(3)]
        product *= correlation(row_stats, near_stats[pop], near_fields[pop])
    near_here = jnp.where(masks_ref[0] > 0.0, product, 0.0)
    near_there = jnp.where(masks_ref[1] > 0.0, product, 0.0)
    slice_rows = pl.ds(pl.multiple_of(me * wide, 8), wide)
    direct = dot_rounded(near_here, columns_ref[...], 1)
    turned = pltpu.roll(direct, HALF_LANES, 1)
    left_places, right_places = owner_places(groups, size)
    other[...] = jnp.zeros_like(other)
    for ref, values, places in ((scores, direct, left_places[:-1]), (other, turned, right_places)):
        for slot, place in enumerate(places):
            ref[pl.ds(pl.multiple_of(place, 8), size), :] += values[slot * size : (slot + 1) * size, :]
    product = 1.0
    for pop in range(2):
        row_stats = [spare_rows_ref[3 * pop + k] for k in range(3)]
        product *= correlation(row_stats, spare_stats[pop], spare_fields[pop])
    spare_here = jnp.where(spare_mask_ref[...] > 0.0, product, 0.0)
    lane = iota(spare_here.shape, 1)
    spare_here = [
        jnp.where((lane >= slot * size) & (lane < (slot + 1) * size), spare_here, 0.0)
        for slot in range(groups)
    ]
    direct = dot_rounded(jnp.concatenate(spare_here, axis=0), spare_columns_ref[...], 1)
    for slot, place in enumerate(spare_places(groups, size)[0]):
        scores[pl.ds(pl.multiple_of(place, 8), size), :] += direct[slot * size : (slot + 1) * size, :]
    near_scores = dot_rounded(near_there, own_rows_ref[...], 0)
    near_scores = jnp.where(
        iota((size, LANES), 1) < HALF_LANES, near_scores[0:size], near_scores[size:wide]
    )

    mine_table = mine_ref[...]
    far_product = 1.0
    for pop in range(2):
        own_row = [mine_table[:, 4 * pop + k : 4 * pop + k + 1] for k in range(3)]
        near_row = [near_table[:, 4 * pop + k : 4 * pop + k + 1] for k in range(4)]
        far_product *= correlation(own_row, near_row, near_row[3])
    scores[slice_rows, :] += near_annot_ref[slice_rows, :] * jnp.where(reach_here >= snps, far_product, 0.0)
    far_scores = annot_ref[slice_rows, :] * jnp.where(reach_there >= snps, far_product, 0.0)
    near_out_ref[...] = (near_scores + pack_halves(far_scores)).astype(near_out_ref.dtype)

    def packed(step):
        group = partner(me, step, groups)
        rows = pl.ds(pl.multiple_of(group * wide, 8), wide)
        return pack_halves(scores[rows, :] + other[rows, :])

    out_ref[...] = packed(0)
    send_ref[...] = packed(1).astype(send_ref.dtype)


def column_finish_kernel(*refs):
    *parts, out_ref = refs
    packed = sum(part[...].astype(jnp.float32) for part in parts)
    out_ref[...] = unpack_halves(packed).T[0 : out_ref.shape[0], :]


def sum_kernel(*refs):
    *parts, own_ref, there_ref = refs
    total = sum((part[...].astype(jnp.float32) for part in parts[1:]), parts[0][...])
    own_ref[...] = total
    half = there_ref.shape[0]
    left = iota((half, LANES), 1) < HALF_LANES
    second = total[half:]
    if second.shape[0] < half:
        second = jnp.concatenate([second, jnp.zeros((half - second.shape[0], LANES))], axis=0)
    there_ref[...] = jnp.where(left, pltpu.roll(total[0:half], HALF_LANES, 1), second)


def finish_kernel(own_ref, there_ref, out_ref):
    annots, rows = out_ref.shape
    there = there_ref[...]
    there = jnp.concatenate([there, pltpu.roll(there, HALF_LANES, 1)], axis=0)
    out_ref[...] = (own_ref[...] + there[0:rows]).T[0:annots, :]


def around(value, groups, step):
    return lax.ppermute(
        value, "hap", [(source, partner(source, step, groups)) for source in range(groups)]
    )


def swapped(value, first):
    pairs = []
    for block in range(first, lax.axis_size("snp") - 1, 2):
        pairs += [(block, block + 1), (block + 1, block)]
    return lax.ppermute(value, "snp", pairs)


def per_device(haplotypes, labels, annotations, reach):
    rows, snps = haplotypes.shape
    half = snps // 2
    groups = lax.axis_size("hap")
    blocks = lax.axis_size("snp")
    share = round_up(-(-half // groups), 16)
    folded_rows = share * groups
    out_share = snps // groups
    padded = half + folded_rows
    annot_part = 32
    bf16, f32, i32 = jnp.bfloat16, jnp.float32, jnp.int32
    shape = jax.ShapeDtypeStruct

    packed = shape((rows // 2 + annot_part, snps), bf16)
    haplotypes = pltpu.with_memory_space_constraint(haplotypes, pltpu.HBM)
    annots_in = pltpu.with_memory_space_constraint(annotations, pltpu.HBM)
    alleles, far, close = call(
        prepare_kernel,
        [shape((rows, snps), bf16), packed, packed],
        [HBM, HBM],
        [
            pltpu.VMEM((rows, snps), i32),
            pltpu.VMEM(annotations.shape, i32),
            pltpu.SemaphoreType.DMA((2 * len(CHUNKS) + 1,)),
        ],
        moved=rows * snps * 8,
    )(haplotypes, annots_in)
    from_far = swapped(far, 1)
    from_close = swapped(close, 0)

    by_column = groups == len(LEFT_BLOCKS)
    by_snp = shape((snps, LANES), f32)
    compact = shape((share * (snps // LANES) + 8, LANES), i32)
    own_share_counts = compact if by_column else shape((share, snps), i32)
    near_share_counts = shape((compact.shape[0] + share + share // 2, LANES), i32)
    tile = pltpu.VMEM((snps + 16, snps), f32)
    folded = pltpu.VMEM((folded_rows, snps), i32)
    weighted, totals, *own_parts = call(
        functools.partial(own_kernel, groups, share),
        [shape((snps + 16, rows), bf16), shape((8, snps), f32)] + [own_share_counts] * groups,
        [VMEM, VMEM],
        [tile, folded],
        flops=2 * rows * snps * snps,
        moved=rows * snps * 4,
    )(alleles, labels.reshape(1, rows))
    order = (2, 3, 1) if by_column else range(groups - 1, 0, -1)
    own_parts = [own_parts[0]] + [around(own_parts[k], groups, k) for k in range(groups - 1, 0, -1)]

    near_shapes = [own_share_counts] + [near_share_counts if by_column else shape((share + 8, snps), i32)] * groups
    if by_column:
        work = dict(flops=4 * rows * snps * LANES, moved=rows * snps * 4)
        flipped = pltpu.VMEM((snps, LANES), f32)
        pair_rows = (groups + 1) * (out_share // 2)
        side_shapes = [((2 * share, snps), i32), ((2 * (share + 8), 2 * LANES), i32), ((8, snps), f32)]
        *close_counts, own_annots, masks, spare_mask, own_rows = call(
            functools.partial(close_kernel, groups),
            [shape(*args) for args in side_shapes]
            + [
                by_snp,
                shape((2, pair_rows, LANES), f32),
                shape((share, 2 * LANES), f32),
                shape((pair_rows, LANES), bf16),
            ],
            [SMEM] + [VMEM] * 3,
            [tile, flipped],
            **work,
        )(reach, weighted, from_close, annotations)
        near_parts = call(
            functools.partial(far_kernel, groups, share),
            near_shapes[1:],
            [VMEM] * 6,
            [pltpu.VMEM(*args) for args in side_shapes]
            + [tile, flipped, pltpu.VMEM((8 * groups, LANES), i32)],
            **work,
        )(weighted, from_far, *close_counts, totals)
    else:
        own_sum, *near_parts = call(
            functools.partial(near_kernel, groups, share),
            near_shapes,
            [VMEM] * (4 + groups),
            [pltpu.VMEM((rows, snps), bf16), tile, folded],
            flops=2 * rows * snps * snps,
            moved=rows * snps * 4,
        )(weighted, from_far, from_close, totals, *own_parts)
    near_parts = [near_parts[0]] + [around(near_parts[k], groups, k) for k in order]

    if not by_column:
        own_annots, near_annots = call(annots_kernel, [by_snp, by_snp], [VMEM] * 3, moved=1 << 20)(
            annotations, from_far[rows // 2 :], from_close[rows // 2 :]
        )
    pairs = []
    for block in range(blocks):
        for group in range(groups):
            target = block + 1 if group < groups // 2 else block - 1
            if 0 <= target < blocks:
                pairs.append((block * groups + group, target * groups + group))

    def to_neighbour(value):
        return lax.ppermute(value, ("snp", "hap"), pairs)

    result = shape((annotations.shape[0], out_share), f32)
    half_share = round_up(-(-out_share // 2), 8)
    own_share = shape((out_share, LANES), f32)
    packed_share = shape((half_share, LANES), f32)
    if by_column:
        sent = shape((half_share, LANES), bf16)
        *prepared, second, third = call(
            functools.partial(own_score_kernel, groups, share),
            [
                by_snp,
                shape((out_share, LANES), f32),
                shape((6, pair_rows, LANES), f32),
                shape((LANES, LANES), bf16),
                shape((6, share, 2 * LANES), f32),
                shape((2 * LANES, LANES), bf16),
                by_snp,
                sent,
                sent,
            ],
            [SMEM] + [VMEM] * (groups + 3),
            [pltpu.VMEM((snps, LANES), f32)],
            flops=1 << 33,
            moved=1 << 20,
        )(reach, *own_parts, own_annots, from_far[rows // 2 :], from_close[rows // 2 :])
        parts = [around(second, groups, 2), around(third, groups, 3)]
        own_scores, send, there = call(
            functools.partial(near_score_kernel, groups, share),
            [packed_share, sent, sent],
            [SMEM] + [VMEM] * (groups + 11),
            [pltpu.VMEM((LANES, LANES), i32)] + [pltpu.VMEM((snps, LANES), f32)] * 2,
            flops=1 << 26,
            moved=1 << 21,
        )(reach, *near_parts, *prepared, own_annots, masks, spare_mask, own_rows)
        parts += [around(send, groups, 1), to_neighbour(there)]
        return call(column_finish_kernel, result, [VMEM] * 5)(own_scores, *parts)

    tall = pltpu.VMEM((padded, LANES), f32)
    scores = call(
        functools.partial(score_kernel, groups, share),
        [own_share] + [shape((out_share, LANES), bf16)] * (groups - 1),
        [SMEM] + [VMEM] * (groups + 3),
        [tall, tall, tall, tall],
        flops=1 << 26,
        moved=1 << 21,
    )(reach, own_sum, *near_parts, own_annots, near_annots)
    scores = [scores[0]] + [around(scores[k], groups, k) for k in range(groups - 1, 0, -1)]
    own_scores, near_scores = call(sum_kernel, [own_share, packed_share], [VMEM] * groups)(*scores)
    return call(finish_kernel, result, [VMEM] * 2)(own_scores, to_neighbour(near_scores))


def solution(mesh):
    in_specs = (
        P("hap", ("parts", "snp")),
        P(("parts", "hap")),
        P(None, ("parts", "snp")),
        P("parts"),
    )
    out_specs = P(None, ("parts", "snp", "hap"))
    return jax.shard_map(
        per_device, mesh=mesh, in_specs=in_specs, out_specs=out_specs, check_vma=False
    )
```
